32 devices in a mesh: row: 4 (over y, x), col: 8 (over z, core).
Axes of the slice: x: 2, y: 2, z: 4, core: 2. Of those that a mesh axis runs over, the one named last changes fastest.
Arguments:
- inputs: bfloat16 [1536, 8192], P('col', 'row'), may hold values from -6 to 6
- segments: int32 [8192], P('row'), may hold values from 0 to 47, never falling along the last dimension, each value on 1 to 512 neighbouring positions
- mix_gain: float32 [1536], P('col'), may hold values from 0.5 to 1.5
- branch_weight: bfloat16 [1536, 2048], P('row', 'col'), may hold values from -0.15625 to 0.15625
- recur_weight: bfloat16 [1536, 2048], P('row', 'col'), may hold values from -0.15625 to 0.15625
- kernel: float32 [4, 2048], P(None, 'col'), may hold values from -3 to 3
- offsets: float32 [2048], P('col'), may hold values from -3 to 3
- retain_weight: float32 [32, 64, 64], P('col'), may hold values from -0.75 to 0.75
- retain_bias: float32 [2048], P('col'), may hold values from -4 to 4
- admit_weight: float32 [32, 64, 64], P('col'), may hold values from -0.75 to 0.75
- admit_bias: float32 [2048], P('col'), may hold values from -4 to 4
- lambdas: float32 [2048], P('col'), may hold values from 2.3 to 7.4, as said below
- merge_weight: bfloat16 [2048, 1536], P('col', 'row'), may hold values from -0.375 to 0.375
- feed_gain: float32 [1536], P('col'), may hold values from 0.5 to 1.5
- gate_weight: bfloat16 [1536, 4608], P('row', 'col'), may hold values from -0.15625 to 0.15625
- up_weight: bfloat16 [1536, 4608], P('row', 'col'), may hold values from -0.15625 to 0.15625
- down_weight: bfloat16 [4608, 1536], P('col', 'row'), may hold values from -0.125 to 0.125
- cotangent: bfloat16 [1536, 8192], P('col', 'row'), may hold values from -6 to 6
Outputs:
- result: bfloat16 [1536, 8192], P('col', 'row')
- input_grad: float32 [1536, 8192], P('col', 'row')
- grad_mix: float32 [1536], P('col')
- grad_branch: float32 [1536, 2048], P('row', 'col')
- grad_recur: float32 [1536, 2048], P('row', 'col')
- grad_kernel: float32 [4, 2048], P(None, 'col')
- grad_offsets: float32 [2048], P('col')
- grad_retain: float32 [32, 64, 64], P('col')
- bias_retain: float32 [2048], P('col')
- grad_admit: float32 [32, 64, 64], P('col')
- bias_admit: float32 [2048], P('col')
- grad_lambdas: float32 [2048], P('col')
- grad_merge: float32 [2048, 1536], P('col', 'row')
- grad_feed: float32 [1536], P('col')
- grad_gate: float32 [1536, 4608], P('row', 'col')
- grad_up: float32 [1536, 4608], P('row', 'col')
- grad_down: float32 [4608, 1536], P('col', 'row')
The draws below stay inside these ranges and needn't reach their ends.
Inputs may be any that keep to these rules, and one draw needn't show every extreme that they name: `segments`: segment numbers never fall along the tokens; a document has 1 to 512 tokens and one has exactly 512. 8 * softplus(-lambdas) lies between 0.005 and 0.7.
All inputs are finite; a program needn't handle non-finite values.
Results may differ from the reference program's by a relative error of at most 0.0091.
Values may be sent and summed in bfloat16 or wider, within the bound.
A program may use at most 192 MiB of HBM per device.

```python
import math
import jax
import jax.numpy as jnp
import numpy as np
from jax import lax

D = 1536
LRU = 2048
FF = 4608
CONV = 4
BLOCK = 64
SEQ = 1024
DOC_MOST = 512
HEADS = 32
TOKENS = 8192
DOCS = 48


def draw_lambdas(key, part):
    key = jax.random.fold_in(key, 11)
    rates = jnp.exp(jax.random.uniform(key, (LRU,), jnp.float32, jnp.log(0.02), jnp.log(0.7)))
    return -jnp.log(jnp.expm1(rates / 8.0))


def levels(key, dims, pieces, least, high):
    def one(axis_at, blocks):
        draws = jax.random.uniform(jax.random.fold_in(jax.random.fold_in(key, 6), axis_at), (blocks,), jnp.float32, least / len(pieces), high / len(pieces))
        return jnp.repeat(jnp.exp(draws), dims[axis_at] // blocks).reshape((-1,) + (1,) * (len(dims) - axis_at - 1))

    level = one(*pieces[0])
    for cut in pieces[1:]:
        level = level * one(*cut)
    return level


def split_up(count, total, limit, lean):
    portions = [(1 << 20) // math.isqrt(rank ** lean) + 1 for rank in range(2, count + 1)]
    spare, counts = total - limit - (count - 1), [1] * (count - 1)
    while spare > 0:
        candidates = [i for i in range(count - 1) if counts[i] < limit]
        mass, left = sum([portions[i] for i in candidates]), spare
        for i in candidates:
            addition = min(limit - counts[i], max(1, left * portions[i] // mass), spare)
            counts[i] = counts[i] + addition
            spare = spare - addition
    return np.array([limit] + counts)


def uneven(rng, amount, total, limit, slope):
    if amount == 2:
        one = jax.random.randint(rng, (), max(1, total - limit), min(limit, total - 1) + 1)
        return jnp.stack([one, total - one])
    sizes = jnp.asarray(split_up(amount, total, limit, slope), jnp.int32)
    twos = (amount - 1) // 2
    source_of, taker = sizes[1:1 + 2 * twos:2], sizes[2:2 + 2 * twos:2]
    room = jnp.minimum(source_of - 1, limit - taker)
    moved = jax.random.randint(jax.random.fold_in(rng, 1), (twos,), 0, 1 << 20) % (room + 1)
    sizes = sizes.at[1:1 + 2 * twos:2].set(source_of - moved).at[2:2 + 2 * twos:2].set(taker + moved)
    return sizes[jax.random.permutation(jax.random.fold_in(rng, 2), amount)]


def centred(rng, extent, deviation, limit, split=(), kind=jnp.bfloat16):
    entries = deviation * jax.random.normal(rng, extent, jnp.float32)
    if split:
        entries = entries * levels(rng, extent, split, -0.22, 0.18)
    return jnp.clip(entries, -limit, limit).astype(kind)


def setup_inputs(seed: int = 0) -> dict:
    keys = jax.random.split(jax.random.key(seed), 19)
    return {
        "inputs": centred(keys[0], (D, TOKENS), 1.0, 6.0, ((0, 8), (1, 4))),
        "segments": jnp.searchsorted(jnp.cumsum(uneven(keys[1], DOCS, TOKENS, DOC_MOST, 0)), jnp.arange(TOKENS), side="right").astype(jnp.int32),
        "mix_gain": jnp.clip(1.0 + 0.1 * jax.random.normal(keys[2], (D,), jnp.float32), 0.5, 1.5),
        "branch_weight": centred(keys[3], (D, LRU), D ** -0.5, 0.15625, ((0, 4), (1, 8))),
        "recur_weight": centred(keys[4], (D, LRU), D ** -0.5, 0.15625, ((0, 4), (1, 8))),
        "kernel": centred(keys[5], (CONV, LRU), CONV ** -0.5, 3.0, ((1, 8),), jnp.float32),
        "offsets": centred(keys[6], (LRU,), 0.5, 3.0, ((0, 8),), jnp.float32),
        "retain_weight": centred(keys[7], (HEADS, BLOCK, BLOCK), BLOCK ** -0.5, 0.75, ((0, 8),), jnp.float32),
        "retain_bias": centred(keys[8], (LRU,), 1.0, 4.0, ((0, 8),), jnp.float32),
        "admit_weight": centred(keys[9], (HEADS, BLOCK, BLOCK), BLOCK ** -0.5, 0.75, ((0, 8),), jnp.float32),
        "admit_bias": centred(keys[10], (LRU,), 1.0, 4.0, ((0, 8),), jnp.float32),
        "lambdas": draw_lambdas(jax.random.fold_in(keys[18], 71), 0),
        "merge_weight": centred(keys[12], (LRU, D), (LRU // 8) ** -0.5, 0.375, ((0, 8), (1, 4))),
        "feed_gain": jnp.clip(1.0 + 0.1 * jax.random.normal(keys[13], (D,), jnp.float32), 0.5, 1.5),
        "gate_weight": centred(keys[14], (D, FF), D ** -0.5, 0.15625, ((0, 4), (1, 8))),
        "up_weight": centred(keys[15], (D, FF), D ** -0.5, 0.15625, ((0, 4), (1, 8))),
        "down_weight": centred(keys[16], (FF, D), (FF // 2) ** -0.5, 0.125, ((0, 8), (1, 4))),
        "cotangent": centred(keys[17], (D, TOKENS), 1.0, 6.0, ((0, 8), (1, 4))),
    }


HIGH = lax.Precision.HIGHEST
EPS = 1e-06
POWER = 8.0
FLOOR = 0.01

@jax.custom_vjp
def low(v):
    return lax.optimization_barrier(v.astype(jnp.bfloat16)).astype(jnp.float32)

@jax.custom_vjp
def low_back(v):
    return v

def low_keep(v):
    return (low(v), None)

def low_pass(kept, grad):
    return (grad,)

def back_keep(v):
    return (v, None)

def back_low(kept, grad):
    return (low(grad),)
low.defvjp(low_keep, low_pass)
low_back.defvjp(back_keep, back_low)

def combine(earlier, later):
    first_a, first_b = earlier
    second_a, second_b = later
    return (first_a * second_a, second_a * first_b + second_b)

def rms_norm(resid, gain):
    scale = lax.rsqrt(lax.optimization_barrier(jnp.mean(resid * resid, axis=-1, keepdims=True)) + EPS)
    return resid * scale * gain

def mixer(branch_pre, lru_pre, segs, kernel, offsets, retain_weight, retain_bias, admit_weight, admit_bias, lambdas):
    length = lru_pre.shape[0]
    channels = lru_pre.shape[1]
    conv = offsets + kernel[0] * lru_pre
    for lag in range(1, kernel.shape[0]):
        shifted = jnp.concatenate([jnp.zeros((lag, channels), lru_pre.dtype), lru_pre[:-lag]], axis=0)
        prior = jnp.concatenate([jnp.full((lag,), -1, jnp.int32), segs[:-lag].astype(jnp.int32)])
        keep = (prior == segs.astype(jnp.int32)).astype(lru_pre.dtype)
        conv = conv + kernel[lag] * shifted * keep[:, None]
    heads = retain_weight.shape[0]
    blocks = conv.reshape(length, heads, channels // heads)
    retain = jax.nn.sigmoid(jnp.einsum('thi,hij->thj', blocks, retain_weight, precision=HIGH).reshape(length, channels) + retain_bias)
    admit = jax.nn.sigmoid(jnp.einsum('thi,hij->thj', blocks, admit_weight, precision=HIGH).reshape(length, channels) + admit_bias)
    decay = jnp.exp(-POWER * retain * jax.nn.softplus(-lambdas))
    factor = jnp.sqrt(1.0 - decay * decay + FLOOR)
    starts = jnp.concatenate([jnp.ones((1,), bool), segs[1:] != segs[:-1]])
    decay = jnp.where(starts[:, None], 0.0, decay)
    factor = jnp.where(starts[:, None], 1.0, factor)
    _, state = lax.associative_scan(combine, (decay, factor * admit * conv), axis=0)
    return jax.nn.gelu(branch_pre) * state

def layer(segs, resid, mix_gain, branch_weight, recur_weight, kernel, offsets, retain_weight, retain_bias, admit_weight, admit_bias, lambdas, merge_weight, feed_gain, gate_weight, up_weight, down_weight):
    normed = low(rms_norm(resid, mix_gain))
    branch_pre = low_back(jnp.dot(normed, branch_weight, precision=HIGH))
    lru_pre = low_back(jnp.dot(normed, recur_weight, precision=HIGH))
    mixed = low(mixer(branch_pre, lru_pre, segs, kernel, offsets, retain_weight, retain_bias, admit_weight, admit_bias, lambdas))
    middle = resid + low_back(jnp.dot(mixed, merge_weight, precision=HIGH))
    normed_two = low(rms_norm(middle, feed_gain))
    gate = low_back(jnp.dot(normed_two, gate_weight, precision=HIGH))
    upper = low_back(jnp.dot(normed_two, up_weight, precision=HIGH))
    hidden = low(jax.nn.gelu(gate) * upper)
    return middle + low_back(jnp.dot(hidden, down_weight, precision=HIGH))

def reference(inputs, segments, mix_gain, branch_weight, recur_weight, kernel, offsets, retain_weight, retain_bias, admit_weight, admit_bias, lambdas, merge_weight, feed_gain, gate_weight, up_weight, down_weight, cotangent):
    params = tuple((p.astype(jnp.float32) for p in (mix_gain, branch_weight, recur_weight, kernel, offsets, retain_weight, retain_bias, admit_weight, admit_bias, lambdas, merge_weight, feed_gain, gate_weight, up_weight, down_weight)))
    width = inputs.shape[0]
    total_tokens = inputs.shape[1]
    count = total_tokens // SEQ
    resids = inputs.astype(jnp.float32).T.reshape(count, SEQ, width)
    grads = cotangent.astype(jnp.float32).T.reshape(count, SEQ, width)
    segs = segments.reshape(count, SEQ)

    def step(totals, item):
        resid, grad, seg_row = item

        def forward(value, *weights):
            return layer(seg_row, value, *weights)
        output, pull = jax.vjp(forward, resid, *params)
        pulled = pull(grad)
        totals = tuple((t + w for t, w in zip(totals, pulled[1:])))
        return (totals, (output.astype(jnp.bfloat16), pulled[0]))
    zeros = tuple((jnp.zeros_like(p) for p in params))
    totals, (outputs, input_grads) = lax.scan(step, zeros, (resids, grads, segs))
    result = outputs.reshape(total_tokens, width).T
    input_grad = input_grads.reshape(total_tokens, width).T
    return (result, input_grad, totals[0], totals[1], totals[2], totals[3], totals[4], totals[5], totals[6], totals[7], totals[8], totals[9], totals[10], totals[11], totals[12], totals[13], totals[14])
```

```python
import jax
import jax.numpy as jnp
from jax import lax
from jax.sharding import PartitionSpec as P

D = 1536
SEQ = 1024
MICRO = 2


HIGH = lax.Precision.HIGHEST
EPS = 1e-06
POWER = 8.0
FLOOR = 0.01


def combine(earlier, later):
    first_a, first_b = earlier
    second_a, second_b = later
    return (first_a * second_a, second_a * first_b + second_b)


def mixer(
    branch_pre,
    lru_pre,
    segs,
    kernel,
    offsets,
    retain_weight,
    retain_bias,
    admit_weight,
    admit_bias,
    lambdas,
):
    length = lru_pre.shape[0]
    channels = lru_pre.shape[1]
    conv = offsets + kernel[0] * lru_pre
    for lag in range(1, kernel.shape[0]):
        shifted = jnp.concatenate(
            [jnp.zeros((lag, channels), lru_pre.dtype), lru_pre[:-lag]], axis=0
        )
        prior = jnp.concatenate([jnp.full((lag,), -1, jnp.int32), segs[:-lag]])
        keep = (prior == segs).astype(lru_pre.dtype)
        conv = conv + kernel[lag] * shifted * keep[:, None]
    heads = retain_weight.shape[0]
    blocks = conv.reshape(length, heads, channels // heads)
    retain = jax.nn.sigmoid(
        jnp.einsum("thi,hij->thj", blocks, retain_weight, precision=HIGH).reshape(length, channels)
        + retain_bias
    )
    admit = jax.nn.sigmoid(
        jnp.einsum("thi,hij->thj", blocks, admit_weight, precision=HIGH).reshape(length, channels)
        + admit_bias
    )
    decay = jnp.exp(-POWER * retain * jax.nn.softplus(-lambdas))
    factor = jnp.sqrt(1.0 - decay * decay + FLOOR)
    starts = jnp.concatenate([jnp.ones((1,), bool), segs[1:] != segs[:-1]])
    decay = jnp.where(starts[:, None], 0.0, decay)
    factor = jnp.where(starts[:, None], 1.0, factor)
    _, state = lax.associative_scan(combine, (decay, factor * admit * conv), axis=0)
    return jax.nn.gelu(branch_pre) * state


def geglu(gate, upper):
    return jax.nn.gelu(gate) * upper


def contract_rows(left, right):
    return lax.dot_general(
        left, right, (((0,), (0,)), ((), ())), preferred_element_type=jnp.float32
    )


def contract_cols(left, right):
    return lax.dot_general(
        left, right, (((1,), (1,)), ((), ())), preferred_element_type=jnp.float32
    )


def contract_cross(left, right):
    return lax.dot_general(
        left, right, (((0,), (1,)), ((), ())), preferred_element_type=jnp.float32
    )


def norm_forward(resid, gain):
    total = lax.psum(jnp.sum(resid * resid, axis=0), "col")
    scale = lax.rsqrt(total / D + EPS)[None, :]
    return (scale, (resid * scale * gain[:, None]).astype(jnp.bfloat16))


def norm_backward(resid, scale, gain, grad_normed):
    weighted = grad_normed * gain[:, None]
    total = lax.psum(jnp.sum(weighted * resid, axis=0), "col")
    grad_resid = scale * weighted - resid * (scale * scale * scale) * (total / D)[None, :]
    grad_gain = jnp.sum(grad_normed * resid * scale, axis=1)
    return (grad_resid, grad_gain)


def gather_features(normed):
    return lax.all_gather(normed, "col", axis=0, tiled=True)


def gather_cotangent(grad):
    return lax.all_gather(grad, "col", axis=0, tiled=True)


def spread_sum(term):
    return lax.psum_scatter(
        term.astype(jnp.bfloat16), "col", scatter_dimension=0, tiled=True
    ).astype(jnp.float32)


def back_sum(term):
    return spread_sum(term)


def merge_term(whole_merge, mixed_low):
    return spread_sum(contract_cross(whole_merge, mixed_low))


def weight_grads(normed, grad_joined):
    return jnp.dot(
        normed,
        grad_joined,
        preferred_element_type=jnp.float32,
    )


def row_sum(total, axis):
    return lax.psum_scatter(
        total.astype(jnp.bfloat16), "row", scatter_dimension=axis, tiled=True
    ).astype(jnp.float32)


def body(
    inputs,
    segments,
    mix_gain,
    branch_weight,
    recur_weight,
    kernel,
    offsets,
    retain_weight,
    retain_bias,
    admit_weight,
    admit_bias,
    lambdas,
    merge_weight,
    feed_gain,
    gate_weight,
    up_weight,
    down_weight,
    cotangent,
):
    lru_cols = branch_weight.shape[1]
    feed_cols = gate_weight.shape[1]
    mixer_params = (kernel, offsets, retain_weight, retain_bias, admit_weight, admit_bias, lambdas)
    acc_branch = jnp.zeros((D, lru_cols), jnp.float32)
    acc_recur = jnp.zeros((D, lru_cols), jnp.float32)
    acc_gate = jnp.zeros((D, feed_cols), jnp.float32)
    acc_up = jnp.zeros((D, feed_cols), jnp.float32)
    acc_merge = jnp.zeros((lru_cols, D), jnp.float32)
    acc_down = jnp.zeros((feed_cols, D), jnp.float32)
    acc_small = tuple((jnp.zeros_like(p) for p in mixer_params))
    acc_mix = jnp.zeros_like(mix_gain)
    acc_feed = jnp.zeros_like(feed_gain)
    outputs = []
    in_grads = []
    for batch in range(MICRO):
        lower = batch * SEQ
        resid_in = inputs[:, lower : lower + SEQ].astype(jnp.float32)
        grad_out = cotangent[:, lower : lower + SEQ].astype(jnp.float32)
        segs = segments[lower : lower + SEQ]
        whole_branch, whole_recur, whole_gate, whole_up = (
            lax.all_gather(branch_weight, "row", axis=0, tiled=True),
            lax.all_gather(recur_weight, "row", axis=0, tiled=True),
            lax.all_gather(gate_weight, "row", axis=0, tiled=True),
            lax.all_gather(up_weight, "row", axis=0, tiled=True),
        )
        whole_merge, whole_down = (
            lax.all_gather(merge_weight, "row", axis=1, tiled=True),
            lax.all_gather(down_weight, "row", axis=1, tiled=True),
        )
        scale_one, normed_one = norm_forward(resid_in, mix_gain)
        full_one = gather_features(normed_one)
        branch_pre = contract_rows(full_one, whole_branch)
        lru_pre = contract_rows(full_one, whole_recur)

        def local_mixer(bpre, lpre, kern, offs, rweight, rbias, aweight, abias, lams):
            return mixer(bpre, lpre, segs, kern, offs, rweight, rbias, aweight, abias, lams)

        mixed, mixer_pull = jax.vjp(local_mixer, branch_pre, lru_pre, *mixer_params)
        mixed_low = mixed.astype(jnp.bfloat16)
        resid_mid = resid_in + merge_term(whole_merge, mixed_low)
        scale_two, normed_two = norm_forward(resid_mid, feed_gain)
        full_two = gather_features(normed_two)
        gate = contract_rows(full_two, whole_gate)
        upper = contract_rows(full_two, whole_up)
        hidden, geglu_pull = jax.vjp(geglu, gate, upper)
        hidden_low = hidden.astype(jnp.bfloat16)
        result = resid_mid + spread_sum(contract_cross(whole_down, hidden_low))
        outputs.append(result.astype(jnp.bfloat16))
        grad_full = gather_cotangent(grad_out.astype(jnp.bfloat16))
        acc_down = acc_down + contract_cross(hidden_low, grad_full)
        grad_gate, grad_upper = geglu_pull(contract_cross(grad_full, whole_down))
        grad_gate = grad_gate.astype(jnp.bfloat16)
        grad_upper = grad_upper.astype(jnp.bfloat16)
        feed_joined = weight_grads(full_two, jnp.concatenate([grad_gate, grad_upper], axis=1))
        acc_gate = acc_gate + feed_joined[:, :feed_cols]
        acc_up = acc_up + feed_joined[:, feed_cols:]
        grad_normed_two = back_sum(
            contract_cols(whole_gate, grad_gate) + contract_cols(whole_up, grad_upper)
        )
        grad_mid_norm, feed_part = norm_backward(resid_mid, scale_two, feed_gain, grad_normed_two)
        acc_feed = acc_feed + feed_part
        grad_mid = grad_out + grad_mid_norm
        grad_mid_full = gather_cotangent(grad_mid.astype(jnp.bfloat16))
        acc_merge = acc_merge + contract_cross(mixed_low, grad_mid_full)
        pulled = mixer_pull(contract_cross(grad_mid_full, whole_merge))
        grad_branch = pulled[0].astype(jnp.bfloat16)
        grad_lru = pulled[1].astype(jnp.bfloat16)
        acc_small = tuple((total + part for total, part in zip(acc_small, pulled[2:])))
        branch_joined = weight_grads(full_one, jnp.concatenate([grad_branch, grad_lru], axis=1))
        acc_branch = acc_branch + branch_joined[:, :lru_cols]
        acc_recur = acc_recur + branch_joined[:, lru_cols:]
        grad_normed_one = back_sum(
            contract_cols(whole_branch, grad_branch) + contract_cols(whole_recur, grad_lru)
        )
        grad_in_norm, mix_part = norm_backward(resid_in, scale_one, mix_gain, grad_normed_one)
        acc_mix = acc_mix + mix_part
        in_grads.append(grad_mid + grad_in_norm)
    sum_branch, sum_recur, sum_gate, sum_up = (
        row_sum(acc_branch, 0),
        row_sum(acc_recur, 0),
        row_sum(acc_gate, 0),
        row_sum(acc_up, 0),
    )
    sum_merge, sum_down = (
        row_sum(acc_merge, 1),
        row_sum(acc_down, 1),
    )
    summed = lax.psum(
        (
            acc_mix,
            acc_feed,
            acc_small[0],
            acc_small[1],
            acc_small[2],
            acc_small[3],
            acc_small[4],
            acc_small[5],
            acc_small[6],
        ),
        "row",
    )
    result_all = jnp.concatenate(outputs, axis=1)
    input_grad = jnp.concatenate(in_grads, axis=1)
    return (
        result_all,
        input_grad,
        summed[0],
        sum_branch,
        sum_recur,
        summed[2],
        summed[3],
        summed[4],
        summed[5],
        summed[6],
        summed[7],
        summed[8],
        sum_merge,
        summed[1],
        sum_gate,
        sum_up,
        sum_down,
    )


def solution(mesh):
    in_specs = (
        P("col", "row"),
        P("row"),
        P("col"),
        P("row", "col"),
        P("row", "col"),
        P(None, "col"),
        P("col"),
        P("col", None, None),
        P("col"),
        P("col", None, None),
        P("col"),
        P("col"),
        P("col", "row"),
        P("col"),
        P("row", "col"),
        P("row", "col"),
        P("col", "row"),
        P("col", "row"),
    )
    out_specs = (
        P("col", "row"),
        P("col", "row"),
        P("col"),
        P("row", "col"),
        P("row", "col"),
        P(None, "col"),
        P("col"),
        P("col", None, None),
        P("col"),
        P("col", None, None),
        P("col"),
        P("col"),
        P("col", "row"),
        P("col"),
        P("row", "col"),
        P("row", "col"),
        P("col", "row"),
    )
    return jax.shard_map(body, mesh=mesh, in_specs=in_specs, out_specs=out_specs, check_vma=False)
```

```python
import functools

import jax
import jax.numpy as jnp
from jax import lax
from jax.experimental import pallas as pl
from jax.experimental.pallas import tpu as pltpu
from jax.sharding import PartitionSpec as P

D = 1536
SEQ = 1024
MICRO = 2


HIGH = lax.Precision.HIGHEST
EPS = 1e-06
POWER = 8.0
FLOOR = 0.01


def combine(earlier, later):
    first_a, first_b = earlier
    second_a, second_b = later
    return (first_a * second_a, second_a * first_b + second_b)


def mixer(
    branch_pre,
    lru_pre,
    segs,
    kernel,
    offsets,
    retain_weight,
    retain_bias,
    admit_weight,
    admit_bias,
    lambdas,
):
    length = lru_pre.shape[0]
    channels = lru_pre.shape[1]
    conv = offsets + kernel[0] * lru_pre
    for lag in range(1, kernel.shape[0]):
        shifted = jnp.concatenate(
            [jnp.zeros((lag, channels), lru_pre.dtype), lru_pre[:-lag]], axis=0
        )
        prior = jnp.concatenate([jnp.full((lag,), -1, jnp.int32), segs[:-lag]])
        keep = (prior == segs).astype(lru_pre.dtype)
        conv = conv + kernel[lag] * shifted * keep[:, None]
    heads = retain_weight.shape[0]
    blocks = conv.reshape(length, heads, channels // heads)
    retain = jax.nn.sigmoid(
        jnp.einsum("thi,hij->thj", blocks, retain_weight, precision=HIGH).reshape(length, channels)
        + retain_bias
    )
    admit = jax.nn.sigmoid(
        jnp.einsum("thi,hij->thj", blocks, admit_weight, precision=HIGH).reshape(length, channels)
        + admit_bias
    )
    decay = jnp.exp(-POWER * retain * jax.nn.softplus(-lambdas))
    factor = jnp.sqrt(1.0 - decay * decay + FLOOR)
    starts = jnp.concatenate([jnp.ones((1,), bool), segs[1:] != segs[:-1]])
    decay = jnp.where(starts[:, None], 0.0, decay)
    factor = jnp.where(starts[:, None], 1.0, factor)
    _, state = lax.associative_scan(combine, (decay, factor * admit * conv), axis=0)
    return jax.nn.gelu(branch_pre) * state


def geglu(gate, upper):
    return jax.nn.gelu(gate) * upper


def contract_rows(left, right):
    return lax.dot_general(
        left, right, (((0,), (0,)), ((), ())), preferred_element_type=jnp.float32
    )


def contract_cols(left, right):
    return lax.dot_general(
        left, right, (((1,), (1,)), ((), ())), preferred_element_type=jnp.float32
    )


def contract_cross(left, right):
    return lax.dot_general(
        left, right, (((0,), (1,)), ((), ())), preferred_element_type=jnp.float32
    )


def norm_forward(resid, gain):
    total = lax.psum(jnp.sum(resid * resid, axis=0), "col")
    scale = lax.rsqrt(total / D + EPS)[None, :]
    return (scale, (resid * scale * gain[:, None]).astype(jnp.bfloat16))


def norm_backward(resid, scale, gain, grad_normed):
    weighted = grad_normed * gain[:, None]
    total = lax.psum(jnp.sum(weighted * resid, axis=0), "col")
    grad_resid = scale * weighted - resid * (scale * scale * scale) * (total / D)[None, :]
    grad_gain = jnp.sum(grad_normed * resid * scale, axis=1)
    return (grad_resid, grad_gain)


def gather_features(normed):
    return lax.all_gather(normed, "col", axis=0, tiled=True)


def gather_cotangent(grad):
    return lax.all_gather(grad, "col", axis=0, tiled=True)


def spread_sum(term):
    return lax.psum_scatter(
        term.astype(jnp.bfloat16), "col", scatter_dimension=0, tiled=True
    ).astype(jnp.float32)


def back_sum(term):
    return spread_sum(term)


def merge_term(whole_merge, mixed_low):
    return spread_sum(contract_cross(whole_merge, mixed_low))


def weight_grads(normed, grad_joined):
    return jnp.dot(
        normed,
        grad_joined,
        preferred_element_type=jnp.float32,
    )


def row_sum(total, axis):
    return lax.psum_scatter(
        total.astype(jnp.bfloat16), "row", scatter_dimension=axis, tiled=True
    ).astype(jnp.float32)


def body(
    inputs,
    segments,
    mix_gain,
    branch_weight,
    recur_weight,
    kernel,
    offsets,
    retain_weight,
    retain_bias,
    admit_weight,
    admit_bias,
    lambdas,
    merge_weight,
    feed_gain,
    gate_weight,
    up_weight,
    down_weight,
    cotangent,
):
    lru_cols = branch_weight.shape[1]
    feed_cols = gate_weight.shape[1]
    mixer_params = (kernel, offsets, retain_weight, retain_bias, admit_weight, admit_bias, lambdas)
    acc_branch = jnp.zeros((D, lru_cols), jnp.float32)
    acc_recur = jnp.zeros((D, lru_cols), jnp.float32)
    acc_gate = jnp.zeros((D, feed_cols), jnp.float32)
    acc_up = jnp.zeros((D, feed_cols), jnp.float32)
    acc_merge = jnp.zeros((lru_cols, D), jnp.float32)
    acc_down = jnp.zeros((feed_cols, D), jnp.float32)
    acc_small = tuple((jnp.zeros_like(p) for p in mixer_params))
    acc_mix = jnp.zeros_like(mix_gain)
    acc_feed = jnp.zeros_like(feed_gain)
    outputs = []
    in_grads = []
    for batch in range(MICRO):
        lower = batch * SEQ
        resid_in = inputs[:, lower : lower + SEQ].astype(jnp.float32)
        grad_out = cotangent[:, lower : lower + SEQ].astype(jnp.float32)
        segs = segments[lower : lower + SEQ]
        whole_branch, whole_recur, whole_gate, whole_up = (
            lax.all_gather(branch_weight, "row", axis=0, tiled=True),
            lax.all_gather(recur_weight, "row", axis=0, tiled=True),
            lax.all_gather(gate_weight, "row", axis=0, tiled=True),
            lax.all_gather(up_weight, "row", axis=0, tiled=True),
        )
        whole_merge, whole_down = (
            lax.all_gather(merge_weight, "row", axis=1, tiled=True),
            lax.all_gather(down_weight, "row", axis=1, tiled=True),
        )
        scale_one, normed_one = norm_forward(resid_in, mix_gain)
        full_one = gather_features(normed_one)
        branch_pre = contract_rows(full_one, whole_branch)
        lru_pre = contract_rows(full_one, whole_recur)

        def local_mixer(bpre, lpre, kern, offs, rweight, rbias, aweight, abias, lams):
            return mixer(bpre, lpre, segs, kern, offs, rweight, rbias, aweight, abias, lams)

        mixed, mixer_pull = jax.vjp(local_mixer, branch_pre, lru_pre, *mixer_params)
        mixed_low = mixed.astype(jnp.bfloat16)
        resid_mid = resid_in + merge_term(whole_merge, mixed_low)
        scale_two, normed_two = norm_forward(resid_mid, feed_gain)
        full_two = gather_features(normed_two)
        gate = contract_rows(full_two, whole_gate)
        upper = contract_rows(full_two, whole_up)
        hidden, geglu_pull = jax.vjp(geglu, gate, upper)
        hidden_low = hidden.astype(jnp.bfloat16)
        result = resid_mid + spread_sum(contract_cross(whole_down, hidden_low))
        outputs.append(result.astype(jnp.bfloat16))
        grad_full = gather_cotangent(grad_out.astype(jnp.bfloat16))
        acc_down = acc_down + contract_cross(hidden_low, grad_full)
        grad_gate, grad_upper = geglu_pull(contract_cross(grad_full, whole_down))
        grad_gate = grad_gate.astype(jnp.bfloat16)
        grad_upper = grad_upper.astype(jnp.bfloat16)
        feed_joined = weight_grads(full_two, jnp.concatenate([grad_gate, grad_upper], axis=1))
        acc_gate = acc_gate + feed_joined[:, :feed_cols]
        acc_up = acc_up + feed_joined[:, feed_cols:]
        grad_normed_two = back_sum(
            contract_cols(whole_gate, grad_gate) + contract_cols(whole_up, grad_upper)
        )
        grad_mid_norm, feed_part = norm_backward(resid_mid, scale_two, feed_gain, grad_normed_two)
        acc_feed = acc_feed + feed_part
        grad_mid = grad_out + grad_mid_norm
        grad_mid_full = gather_cotangent(grad_mid.astype(jnp.bfloat16))
        acc_merge = acc_merge + contract_cross(mixed_low, grad_mid_full)
        pulled = mixer_pull(contract_cross(grad_mid_full, whole_merge))
        grad_branch = pulled[0].astype(jnp.bfloat16)
        grad_lru = pulled[1].astype(jnp.bfloat16)
        acc_small = tuple((total + part for total, part in zip(acc_small, pulled[2:])))
        branch_joined = weight_grads(full_one, jnp.concatenate([grad_branch, grad_lru], axis=1))
        acc_branch = acc_branch + branch_joined[:, :lru_cols]
        acc_recur = acc_recur + branch_joined[:, lru_cols:]
        grad_normed_one = back_sum(
            contract_cols(whole_branch, grad_branch) + contract_cols(whole_recur, grad_lru)
        )
        grad_in_norm, mix_part = norm_backward(resid_in, scale_one, mix_gain, grad_normed_one)
        acc_mix = acc_mix + mix_part
        in_grads.append(grad_mid + grad_in_norm)
    sum_branch, sum_recur, sum_gate, sum_up = (
        row_sum(acc_branch, 0),
        row_sum(acc_recur, 0),
        row_sum(acc_gate, 0),
        row_sum(acc_up, 0),
    )
    sum_merge, sum_down = (
        row_sum(acc_merge, 1),
        row_sum(acc_down, 1),
    )
    summed = lax.psum(
        (
            acc_mix,
            acc_feed,
            acc_small[0],
            acc_small[1],
            acc_small[2],
            acc_small[3],
            acc_small[4],
            acc_small[5],
            acc_small[6],
        ),
        "row",
    )
    result_all = jnp.concatenate(outputs, axis=1)
    input_grad = jnp.concatenate(in_grads, axis=1)
    return (
        result_all,
        input_grad,
        summed[0],
        sum_branch,
        sum_recur,
        summed[2],
        summed[3],
        summed[4],
        summed[5],
        summed[6],
        summed[7],
        summed[8],
        sum_merge,
        summed[1],
        sum_gate,
        sum_up,
        sum_down,
    )


MESH = pl.DeviceIdType.MESH
F32 = jnp.float32
BF16 = jnp.bfloat16
LINE = 4
PART = 256
PARTS = 4
GELU_A = 0.7978845608028654
GELU_B = 0.044715


def place():
    row, col = lax.axis_index("row"), lax.axis_index("col")
    return row, col // 2, col % 2


def at_line(z, core):
    return {"col": 2 * z + core}


def lanes(part):
    return pl.ds(pl.multiple_of(part * PART, PART), PART)


def rows_of(index, size):
    return pl.ds(pl.multiple_of(index * size, 16), size)


def dot(a, b):
    return lax.dot_general(a, b, (((1,), (0,)), ((), ())), preferred_element_type=F32)


def dot_nt(a, b):
    return lax.dot_general(a, b, (((1,), (1,)), ((), ())), preferred_element_type=F32)


def greet(row, z, core, rows, line):
    barrier = pltpu.get_barrier_semaphore()
    peers = [{"col": 2 * z + (1 - core)}]
    if rows:
        peers += [{"row": row ^ d} for d in (1, 2, 3)]
    if line:
        peers += [at_line(z ^ d, core) for d in (1, 2, 3)]
    for peer in peers:
        pl.semaphore_signal(barrier, inc=1, device_id=peer, device_id_type=MESH)
    pl.semaphore_wait(barrier, len(peers))


def remote(src, dst, send, recv, peer):
    return pltpu.make_async_remote_copy(
        src_ref=src, dst_ref=dst, send_sem=send, recv_sem=recv, device_id=peer, device_id_type=MESH
    )


class Gather:
    def __init__(self, ref, send, recv, z, core, block, back=False):
        self.ref, self.sems, self.z, self.core = ref, (send, recv), z, core
        self.block, self.back = block, back

    def copy(self, way, hop, step, owner, incoming=False):
        part = PARTS - 1 - step if self.back else step
        piece = self.ref.at[rows_of(owner, self.block), lanes(part)]
        peer = at_line(self.z + (1 if (way == 0) != incoming else -1), self.core)
        return remote(piece, piece, self.sems[0].at[way, hop, step], self.sems[1].at[way, hop, step], peer)

    def each(self, hop, act, incoming):
        z = self.z
        if incoming:
            cases = ((0, z - 1 - hop >= 0, z - 1 - hop), (1, z + 1 + hop < LINE, z + 1 + hop))
        else:
            cases = (
                (0, (z >= hop) & (z < LINE - 1), z - hop),
                (1, (z + hop < LINE) & (z >= 1), z + hop),
            )
        for way, here, owner in cases:
            pl.when(here)(functools.partial(act, way, owner))

    def send(self, hop, step):
        self.each(hop, lambda way, owner: self.copy(way, hop, step, owner).start(), False)

    def arrive(self, hop, step):
        self.each(hop, lambda way, owner: self.copy(way, hop, step, owner, True).wait_recv(), True)

    def forward(self, hop, step):
        self.arrive(hop - 1, step)
        self.send(hop, step)

    def sent(self):
        def one(step, carry):
            for hop in range(LINE - 1):
                self.each(hop, lambda way, owner: self.copy(way, hop, step, owner).wait_send(), False)
            return carry

        lax.fori_loop(0, PARTS, one, 0)

    def open(self):
        self.send(0, 0)
        self.forward(1, 0)
        self.send(0, 1)

    def serve(self, step):
        self.forward(2, step)

        @pl.when(step + 1 < PARTS)
        def _():
            self.forward(1, step + 1)

        @pl.when(step + 2 < PARTS)
        def _():
            self.send(0, step + 2)

        self.arrive(2, step)


class Spread:
    def __init__(self, own, held, send, recv, z, core):
        self.own, self.held, self.sems, self.z, self.core = own, held, (send, recv), z, core

    def copy(self, way, step, hop):
        slot = hop if way == 0 else LINE - hop
        there = slot - 1 if way == 0 else slot + 1
        peer = at_line(self.z + (1 if way == 0 else -1), self.core)
        return remote(
            self.held.at[step, slot],
            self.held.at[step, there],
            self.sems[0].at[way, step, hop],
            self.sems[1].at[way, step, hop - 1],
            peer,
        )

    def landed(self, way, step, hop):
        slot = hop if way == 0 else LINE - hop
        piece = self.held.at[step, slot]
        peer = at_line(self.z + (-1 if way == 0 else 1), self.core)
        remote(piece, piece, self.sems[0].at[way, step, hop], self.sems[1].at[way, step, hop], peer).wait_recv()

    def push(self, way, step):
        z = self.z
        first = z == 0 if way == 0 else z == LINE - 1

        def one(i, carry):
            hop = LINE - 1 - i
            owner = z + hop if way == 0 else z - hop
            slot = hop if way == 0 else LINE - hop

            @pl.when((owner >= 0) & (owner < LINE))
            def _():
                @pl.when(first)
                def _():
                    self.held[step, slot] = self.own[step, owner].astype(BF16)

                @pl.when(jnp.logical_not(first))
                def _():
                    self.landed(way, step, hop)
                    total = self.own[step, owner].astype(F32) + self.held[step, slot].astype(F32)
                    self.held[step, slot] = total.astype(BF16)

                self.copy(way, step, hop).start()

            return carry

        lax.fori_loop(0, LINE - 1, one, 0)

    def serve(self, t, finish):
        z = self.z
        for way, late in ((0, z), (1, LINE - 1 - z)):
            step = t - late
            pl.when((step >= 0) & (step < PARTS))(functools.partial(self.push, way, step))
        step = t - (LINE - 1)

        @pl.when((step >= 0) & (step < PARTS))
        def _():
            @pl.when(z == 0)
            def _():
                self.landed(1, step, 0)
                finish(step, lambda a, n: self.mine(step, a, n) + self.got(step, LINE, a, n))

            @pl.when(z == LINE - 1)
            def _():
                self.landed(0, step, 0)
                finish(step, lambda a, n: self.mine(step, a, n) + self.got(step, 0, a, n))

            @pl.when((z > 0) & (z < LINE - 1))
            def _():
                self.landed(0, step, 0)
                self.landed(1, step, 0)
                finish(
                    step,
                    lambda a, n: self.mine(step, a, n) + (self.got(step, 0, a, n) + self.got(step, LINE, a, n)),
                )

    def mine(self, step, start, size):
        return self.own[step, self.z, pl.ds(start, size)].astype(F32)

    def got(self, step, slot, start, size):
        return self.held[step, slot, pl.ds(start, size)].astype(F32)

    def sent(self):
        z = self.z

        def one(step, carry):
            for way in (0, 1):
                for hop in range(1, LINE):
                    owner = z + hop if way == 0 else z - hop

                    @pl.when((owner >= 0) & (owner < LINE))
                    def _():
                        self.copy(way, step, hop).wait_send()

            return carry

        lax.fori_loop(0, PARTS, one, 0)


def share_line(ref, send, recv, z, core):
    copies = [
        remote(ref.at[z], ref.at[z], send.at[d - 1], recv.at[d - 1], at_line(z ^ d, core)) for d in (1, 2, 3)
    ]
    for copy in copies:
        copy.start()
    for d in (1, 2, 3):
        piece = ref.at[z ^ d]
        remote(piece, piece, send.at[d - 1], recv.at[d - 1], at_line(z ^ d, core)).wait_recv()
    for copy in copies:
        copy.wait_send()


class Weights:
    def __init__(self, src, dst, send, recv, own, row, z, core, turned):
        self.src, self.dst, self.send, self.recv, self.own = src, dst, send, recv, own
        self.row, self.core, self.turned = row, core, turned
        self.sibling = {"col": 2 * z + (1 - core)}

    def spot(self, row, core):
        down, right = (row, core) if self.turned else (core, row)
        rows, cols = self.src.shape
        return self.dst.at[rows_of(down, rows), pl.ds(pl.multiple_of(right * cols, 128), cols)]

    def to_row(self, d):
        return remote(
            self.src, self.spot(self.row, self.core), self.send.at[d], self.recv.at[d], {"row": self.row ^ d}
        )

    def to_sibling(self, d):
        if d == 0:
            return remote(
                self.src, self.spot(self.row, self.core), self.send.at[0], self.recv.at[0], self.sibling
            )
        piece = self.spot(self.row ^ d, self.core)
        return remote(piece, piece, self.send.at[3 + d], self.recv.at[3 + d], self.sibling)

    def local(self):
        return pltpu.make_async_copy(self.src, self.spot(self.row, self.core), self.own)

    def start(self):
        for d in (1, 2, 3):
            self.to_row(d).start()
        self.to_sibling(0).start()
        self.local().start()

    def forward(self):
        for d in (1, 2, 3):
            piece = self.spot(self.row ^ d, self.core)
            remote(piece, piece, self.send.at[d], self.recv.at[d], {"row": self.row ^ d}).wait_recv()
            self.to_sibling(d).start()

    def finish(self):
        self.local().wait()
        for d in (0, 1, 2, 3):
            piece = self.spot(self.row ^ d, 1 - self.core)
            sem = 0 if d == 0 else 3 + d
            remote(piece, piece, self.send.at[sem], self.recv.at[sem], self.sibling).wait_recv()

    def sent(self):
        for d in (1, 2, 3):
            self.to_row(d).wait_send()
            self.to_sibling(d).wait_send()
        self.to_sibling(0).wait_send()


def gelu_parts(b):
    t = jnp.tanh(GELU_A * (b + GELU_B * (b * b * b)))
    half = 0.5 + 0.5 * t
    slope = half + (0.5 * b) * (1.0 - t * t) * (GELU_A + (3.0 * GELU_A * GELU_B) * (b * b))
    return b * half, slope


def blocks(count, body):
    def one(i, carry):
        body(i)
        return carry

    lax.fori_loop(0, count, one, 0)


def scale_of(ref, eps, width):
    total = jnp.sum(jnp.sum(ref[...], axis=0), axis=0, keepdims=True)
    return lax.rsqrt(total / width + eps)


def mix_kernel(
    width, eps,
    x_in, gain, masks, par, gates_hi, gates_lo, br_s, m_s, gu_s, d_s,
    y, normed, q, x_own, scale, br, mt, b_out, p_out, u_out, r_out, i_out, h_out, gu, down,
    sums, b_s, p_s, u_s, r_s, i_s, h_s, uh, ul, own, held,
    x_send, x_recv, l_send, l_recv, g_send, g_recv, s_send, s_recv, w_send, w_recv, w_own, o_sem,
):
    row, z, core = place()
    block, seq = y.shape
    half = x_in.shape[0]
    chan = q.shape[0]
    greet(row, z, core, True, True)
    weights = [
        Weights(src, dst, w_send.at[n], w_recv.at[n], w_own.at[n], row, z, core, n == 1)
        for n, (src, dst) in enumerate(((br_s, br), (m_s, mt), (gu_s, gu), (d_s, down)))
    ]
    mine = pl.ds(pl.multiple_of(core * seq, seq), seq)
    other = pl.ds(pl.multiple_of((1 - core) * seq, seq), seq)
    swap = remote(
        x_in.at[:, other], x_own.at[rows_of(core, half), :], x_send, x_recv, {"col": 2 * z + (1 - core)}
    )
    swap.start()
    for w in weights:
        w.start()
    x_own[rows_of(core, half), :] = x_in[:, mine]
    swap.wait()

    sums[z] = jnp.zeros(sums.shape[1:], F32)

    def squares(i):
        v = x_own[rows_of(i, 16), :].astype(F32)
        v = v * v
        sums[z] += v[:8] + v[8:]

    blocks(block // 16, squares)
    share_line(sums, l_send, l_recv, z, core)
    s1 = scale_of(sums, eps, width)
    scale[...] = jnp.broadcast_to(s1, scale.shape)

    def norm(i):
        v = x_own[rows_of(i, 16), :].astype(F32) * scale[0:1, :] * gain[rows_of(i, 16), :]
        normed[pl.ds(pl.multiple_of(z * block + i * 16, 16), 16), :] = v.astype(BF16)

    blocks(block // 16, norm)
    gather = Gather(normed, g_send, g_recv, z, core, block)
    spread = Spread(own, held, s_send, s_recv, z, core)
    gather.open()
    p_s[:, 0:128] = jnp.zeros((chan, 128), F32)
    h_s[:, 0:128] = jnp.zeros((chan, 128), F32)
    for w in weights[:2]:
        w.forward()
    for w in weights[:2]:
        w.finish()

    hc = chan // 2
    kept = (b_s, p_s, u_s, r_s, i_s, h_s)
    outs = (b_out, p_out, u_out, r_out, i_out, h_out)

    def keep(n, part):
        lead = 128 if kept[n] is p_s or kept[n] is h_s else 0
        at = pl.ds(pl.multiple_of(lead + part * PART, 128), PART)
        return pltpu.make_async_copy(kept[n].at[:, at], outs[n].at[:, lanes(part)], o_sem.at[n, part])

    def work(k):
        here = lanes(k)
        ahead = pl.ds(pl.multiple_of(128 + k * PART, 128), PART)
        wide = pl.ds(pl.multiple_of(k * PART, 128), PART + 128)
        n1 = normed[:, here]
        for c in (0, 1):
            b_s[c * hc : (c + 1) * hc, here] = dot(br[c * 2 * hc : c * 2 * hc + hc, :], n1)
            p_s[c * hc : (c + 1) * hc, ahead] = dot(br[c * 2 * hc + hc : (c + 1) * 2 * hc, :], n1)

        def conv(i):
            ch = rows_of(i, 32)
            window = p_s[ch, wide]
            pr = par[ch, :]
            u = pr[:, 4:5] + pr[:, 0:1] * window[:, 128:]
            for lag in (1, 2, 3):
                u = u + pr[:, lag : lag + 1] * (pltpu.roll(window, lag, 1)[:, 128:] * masks[lag : lag + 1, here])
            u_s[ch, here] = u
            high = u.astype(BF16)
            uh[ch, :] = high
            ul[ch, :] = (u - high.astype(F32)).astype(BF16)

        blocks(chan // 32, conv)
        for g in range(chan // 256):
            at = slice(g * 256, (g + 1) * 256)
            pre = dot(gates_hi[g], uh[at, :]) + dot(gates_hi[g], ul[at, :]) + dot(gates_lo[g], uh[at, :])
            r_s[at, here] = pre[:256]
            i_s[at, here] = pre[256:]
        first = lax.broadcasted_iota(jnp.int32, (32, PART), 1) == 0

        def recur(i):
            ch = rows_of(i, 32)
            pr = par[ch, :]
            start = masks[0:1, here] > 0.5
            r = jax.nn.sigmoid(r_s[ch, here] + pr[:, 5:6])
            gate = jax.nn.sigmoid(i_s[ch, here] + pr[:, 6:7])
            r_s[ch, here] = r
            i_s[ch, here] = gate
            a = jnp.exp(-(r * pr[:, 7:8]))
            m = jnp.sqrt(1.0 - a * a + FLOOR)
            a = jnp.where(start, 0.0, a)
            m = jnp.where(start, 1.0, m)
            h = m * gate * u_s[ch, here]
            last = h_s[ch, pl.ds(pl.multiple_of(k * PART, 128), 128)][:, 127:128]
            h = h + jnp.where(first, a * last, 0.0)
            a = jnp.where(first, 0.0, a)
            shift = 1
            while shift < PART:
                h = h + a * pltpu.roll(h, shift, 1)
                if shift * 2 < PART:
                    a = a * pltpu.roll(a, shift, 1)
                shift *= 2
            h_s[ch, ahead] = h
            b = b_s[ch, here]
            t = jnp.tanh(GELU_A * (b + GELU_B * (b * b * b)))
            q[ch, here] = (b * (0.5 + 0.5 * t) * h).astype(BF16)

        blocks(chan // 32, recur)
        qk = q[:, here]
        for s in range(LINE):
            own[k, s] = dot(mt[s * block : (s + 1) * block, :], qk)
        for n in range(len(kept)):
            keep(n, k).start()

    def finish(k, total):
        def add(i):
            at = pl.multiple_of(i * 16, 16)
            y[pl.ds(at, 16), lanes(k)] = x_own[pl.ds(at, 16), lanes(k)].astype(F32) + total(at, 16)

        blocks(block // 16, add)

    def step(t, carry):
        @pl.when(t < PARTS)
        def _():
            gather.serve(t)
            work(t)

        @pl.when(t == PARTS + 1)
        def _():
            weights[2].forward()

        spread.serve(t, finish)
        return carry

    lax.fori_loop(0, PARTS + LINE - 1, step, 0)
    weights[3].forward()
    for w in weights[2:]:
        w.finish()
    for w in weights:
        w.sent()
    gather.sent()
    spread.sent()
    for n in range(len(kept)):
        blocks(PARTS, lambda part: keep(n, part).wait())


def feed_kernel(
    width, eps,
    y, gain, g_in, gu_h, gun_h, d_h, dt_h,
    result, normed, go, scale, dn2, z_out, dev_out,
    sums, gu, gun, down, dt, ev, dz, zs, dev, res, own_o, own_n, held_o, held_n,
    c_sem, x_send, x_recv, l_send, l_recv, g_send, g_recv, e_send, e_recv, s_send, s_recv, t_send, t_recv, r_send, r_recv, o_sem,
):
    row, z, core = place()
    block, seq = y.shape
    half = g_in.shape[0]
    sibling = {"col": 2 * z + (1 - core)}
    greet(row, z, core, False, True)
    loads = [
        pltpu.make_async_copy(src, dst, c_sem.at[n])
        for n, (src, dst) in enumerate(((gu_h, gu), (d_h, down), (dt_h, dt), (gun_h, gun)))
    ]
    for load in loads:
        load.start()
    mine = pl.ds(pl.multiple_of(core * seq, seq), seq)
    other = pl.ds(pl.multiple_of((1 - core) * seq, seq), seq)
    inner = pl.ds(pl.multiple_of(z * block + core * half, 16), half)
    swap = remote(g_in.at[:, other], go.at[inner, :], x_send, x_recv, sibling)
    swap.start()
    go[inner, :] = g_in[:, mine]

    sums[z] = jnp.zeros(sums.shape[1:], F32)

    def squares(i):
        v = y[rows_of(i, 16), :]
        v = v * v
        sums[z] += v[:8] + v[8:]

    blocks(block // 16, squares)
    share_line(sums, l_send, l_recv, z, core)
    s2 = scale_of(sums, eps, width)
    scale[...] = jnp.broadcast_to(s2, scale.shape)

    def norm(i):
        v = y[rows_of(i, 16), :] * scale[0:1, :] * gain[rows_of(i, 16), :]
        normed[pl.ds(pl.multiple_of(z * block + i * 16, 16), 16), :] = v.astype(BF16)

    blocks(block // 16, norm)
    swap.wait()
    gather = Gather(normed, g_send, g_recv, z, core, block)
    gather_go = Gather(go, e_send, e_recv, z, core, block)
    spread_o = Spread(own_o, held_o, s_send, s_recv, z, core)
    spread_n = Spread(own_n, held_n, t_send, t_recv, z, core)
    gather.open()
    gather_go.open()
    for load in loads:
        load.wait()
    hid = zs.shape[1]
    hh = hid // 2

    def store(n, k):
        slot = k % 2
        src, dst = ((zs, z_out), (dev, dev_out))[n]
        return pltpu.make_async_copy(src.at[slot], dst.at[:, lanes(k)], o_sem.at[n, slot])

    def work(k):
        here = lanes(k)
        slot = k % 2
        n2 = normed[:, here]
        for c in range(4):
            ev[c * hh : (c + 1) * hh, :] = dot(gu[c * hh : (c + 1) * hh, :], n2)
        gk = go[:, here]
        for c in range(2):
            dz[c * hh : (c + 1) * hh, :] = dot(down[c * hh : (c + 1) * hh, :], gk)

        @pl.when(k >= 2)
        def _():
            store(0, k - 2).wait()
            store(1, k - 2).wait()

        for c in range(2):

            def one(i):
                off = pl.multiple_of(i * 32, 32)
                e = ev[pl.ds(c * 2 * hh + off, 32), :]
                v = ev[pl.ds(c * 2 * hh + hh + off, 32), :]
                d = dz[pl.ds(c * hh + off, 32), :]
                act, slope = gelu_parts(e)
                zs[slot, pl.ds(c * hh + off, 32), :] = (act * v).astype(BF16)
                dev[slot, pl.ds(c * 2 * hh + off, 32), :] = (d * v * slope).astype(BF16)
                dev[slot, pl.ds(c * 2 * hh + hh + off, 32), :] = (d * act).astype(BF16)

            blocks(hh // 32, one)
        zk = zs[slot]
        for s in range(LINE):
            own_o[k, s] = dot(dt[s * block : (s + 1) * block, :], zk).astype(own_o.dtype)
        dk = dev[slot]
        for s in range(LINE):
            own_n[k, s] = dot(gun[s * block : (s + 1) * block, :], dk)
        store(0, k).start()
        store(1, k).start()

    def finish_o(k, total):
        def add(i):
            at = pl.multiple_of(i * 16, 16)
            res[pl.ds(at, 16), lanes(k)] = (y[pl.ds(at, 16), lanes(k)] + total(at, 16)).astype(BF16)

        blocks(block // 16, add)

    def finish_n(k, total):
        def add(i):
            at = pl.multiple_of(i * 16, 16)
            dn2[pl.ds(at, 16), lanes(k)] = total(at, 16)

        blocks(block // 16, add)

    def step(t, carry):
        @pl.when(t < PARTS)
        def _():
            gather.serve(t)
            gather_go.serve(t)
            work(t)

        spread_n.serve(t, finish_n)
        spread_o.serve(t, finish_o)
        return carry

    lax.fori_loop(0, PARTS + LINE - 1, step, 0)
    back = remote(
        res.at[rows_of(1 - core, half), :], result.at[:, mine], r_send, r_recv, sibling
    )
    back.start()
    result[:, mine] = res[rows_of(core, half), :]
    gather.sent()
    gather_go.sent()
    spread_o.sent()
    spread_n.sent()
    for k in (PARTS - 2, PARTS - 1):
        store(0, k).wait()
        store(1, k).wait()
    back.wait()


def back_kernel(
    width,
    y, dn2, go_h, x_own, scale_two, scale_one, gain_two, gain_one, masks, par, gates_t, m_h, br_h,
    b_h, p_h, u_h, r_h, i_h, h_h,
    input_grad, dyf, dbp, feed_part, mix_part, small, gate_grad,
    sums, sums2, coef, m_n, br_n, b_s, p_s, u_s, r_s, i_s, h_s, g_s, dy, dn1, ig, dq, du, dri, carry_s, own, held,
    c_sem, k_sem, l_send, l_recv, l2_send, l2_recv, g_send, g_recv, s_send, s_recv, r_send, r_recv,
):
    row, z, core = place()
    block, seq = y.shape
    half = block // 2
    chan = b_s.shape[0]
    hc = chan // 2
    sibling = {"col": 2 * z + (1 - core)}
    greet(row, z, core, False, True)
    load_g = pltpu.make_async_copy(go_h.at[rows_of(z, block), :], g_s, c_sem.at[0])
    load_g.start()
    load_m = pltpu.make_async_copy(m_h, m_n, c_sem.at[1])
    load_m.start()
    load_b = pltpu.make_async_copy(br_h, br_n, c_sem.at[2])
    load_b.start()
    kept = (b_s, p_s, u_s, r_s, i_s, h_s)
    srcs = (b_h, p_h, u_h, r_h, i_h, h_h)

    def fetch(n, part):
        lead = 128 if kept[n] is p_s or kept[n] is h_s else 0
        at = pl.ds(pl.multiple_of(lead + part * PART, 128), PART)
        return pltpu.make_async_copy(srcs[n].at[:, lanes(part)], kept[n].at[:, at], k_sem.at[n, part])

    for part in range(PARTS - 1, -1, -1):
        for n in range(len(kept)):
            fetch(n, part).start()
    early, late = (1, 5), (0, 2, 3, 4)
    p_s[:, 0:128] = jnp.zeros((chan, 128), F32)
    h_s[:, 0:128] = jnp.zeros((chan, 128), F32)
    du[:, seq : seq + 128] = jnp.zeros((chan, 128), F32)
    carry_s[...] = jnp.zeros(carry_s.shape, F32)
    small[...] = jnp.zeros(small.shape, F32)
    gate_grad[...] = jnp.zeros(gate_grad.shape, F32)

    sums[z] = jnp.zeros(sums.shape[1:], F32)

    def inner(i):
        at = rows_of(i, 16)
        d, v = dn2[at, :], y[at, :]
        w = d * v
        c = w * gain_two[at, :]
        sums[z] += c[:8] + c[8:]
        w = w * scale_two[0:1, :]
        fold = w[:, 0:128]
        for j in range(1, seq // 128):
            fold = fold + w[:, j * 128 : (j + 1) * 128]
        feed_part[at, :] = fold

    blocks(block // 16, inner)
    share_line(sums, l_send, l_recv, z, core)
    load_g.wait()
    total = jnp.sum(jnp.sum(sums[...], axis=0), axis=0, keepdims=True)
    s2 = scale_two[0:1, :]
    coef[0:1, :] = s2 * s2 * s2 * (total / width)

    def outer(i):
        at = rows_of(i, 16)
        v = g_s[at, :].astype(F32) + (scale_two[0:1, :] * (gain_two[at, :] * dn2[at, :]) - y[at, :] * coef[0:1, :])
        dy[at, :] = v
        dyf[pl.ds(pl.multiple_of(z * block + i * 16, 16), 16), :] = v.astype(BF16)

    blocks(block // 16, outer)
    gather = Gather(dyf, g_send, g_recv, z, core, block, back=True)
    spread = Spread(own, held, s_send, s_recv, z, core)
    gather.open()
    load_m.wait()
    load_b.wait()
    for n in early:
        blocks(PARTS, lambda part: fetch(n, part).wait())
    final = lax.broadcasted_iota(jnp.int32, (32, PART), 1) == PART - 1

    def fold2(v):
        return v[:, 0:128] + v[:, 128:256]

    def work(t):
        k = PARTS - 1 - t
        here = lanes(k)
        wide = pl.ds(pl.multiple_of(k * PART, 128), PART + 128)
        for n in late:
            fetch(n, k).wait()

        dq[...] = dot(m_n[...], dyf[:, here])

        def recur(i):
            ch = rows_of(i, 32)
            c = i // (hc // 32)
            low = pl.ds(pl.multiple_of(c * hc + i * 32, 32), 32)
            pr = par[ch, :]
            start = masks[0:1, here] > 0.5
            b, d = b_s[ch, here], dq[ch, :]
            window = h_s[ch, wide]
            h = window[:, 128:]
            before = pltpu.roll(window, 1, 1)[:, 128:]
            act, slope = gelu_parts(b)
            dbp[low, here] = (d * h * slope).astype(BF16)
            lam = d * act
            r, gate, u = r_s[ch, here], i_s[ch, here], u_s[ch, here]
            a0 = jnp.exp(-(r * pr[:, 7:8]))
            m0 = jnp.sqrt(1.0 - a0 * a0 + FLOOR)
            a = jnp.where(start, 0.0, a0)
            m = jnp.where(start, 1.0, m0)
            lam = lam + jnp.where(final, carry_s[ch, :][:, 0:1], 0.0)
            w = jnp.where(final, 0.0, pltpu.roll(a, PART - 1, 1))
            shift = 1
            while shift < PART:
                lam = lam + w * pltpu.roll(lam, PART - shift, 1)
                if shift * 2 < PART:
                    w = w * pltpu.roll(w, PART - shift, 1)
                shift *= 2
            carry_s[ch, :] = jnp.broadcast_to((a * lam)[:, 0:1], (32, 128))
            lm = lam * m
            lu = lam * u
            du[ch, here] = lm * gate
            da = jnp.where(start, 0.0, lam * before - (lu * gate) * (a0 / m0)) * a0
            dr = da * (-pr[:, 7:8]) * (r * (1.0 - r))
            di = lu * m * (gate * (1.0 - gate))
            g, o = i // 8, (i % 8) * 32
            dri[pl.ds(pl.multiple_of(g * 512 + o, 32), 32), :] = dr.astype(BF16)
            dri[pl.ds(pl.multiple_of(g * 512 + 256 + o, 32), 32), :] = di.astype(BF16)
            small[5, ch, :] += fold2(dr)
            small[6, ch, :] += fold2(di)
            small[7, ch, :] += fold2(da * r)

        blocks(chan // 32, recur)
        for g in range(chan // 256):
            at = slice(g * 256, (g + 1) * 256)
            dd = dri[g * 512 : (g + 1) * 512, :]
            du[at, here] += dot(gates_t[g], dd)
            gate_grad[g] += dot_nt(u_s[at, here].astype(BF16), dd)

        def conv(i):
            ch = rows_of(i, 32)
            c = i // (hc // 32)
            low = pl.ds(pl.multiple_of((c + 1) * hc + i * 32, 32), 32)
            pr = par[ch, :]
            after = du[ch, wide]
            window = p_s[ch, wide]
            d = after[:, :PART]
            dp = pr[:, 0:1] * d
            small[4, ch, :] += fold2(d)
            small[0, ch, :] += fold2(d * window[:, 128:])
            for lag in (1, 2, 3):
                kd = after * masks[lag : lag + 1, wide]
                dp = dp + pr[:, lag : lag + 1] * pltpu.roll(kd, PART + 128 - lag, 1)[:, :PART]
                small[lag, ch, :] += fold2(kd[:, :PART] * pltpu.roll(window, lag, 1)[:, 128:])
            dbp[low, here] = dp.astype(BF16)

        blocks(chan // 32, conv)
        dk = dbp[:, here]
        for s in range(LINE):
            own[t, s] = dot(br_n[s * block : (s + 1) * block, :], dk)

    def finish(t, total):
        k = PARTS - 1 - t

        def add(i):
            at = pl.multiple_of(i * 16, 16)
            dn1[pl.ds(at, 16), lanes(k)] = total(at, 16)

        blocks(block // 16, add)

    def step(t, carry):
        @pl.when(t < PARTS)
        def _():
            gather.serve(t)
            work(t)

        spread.serve(t, finish)
        return carry

    lax.fori_loop(0, PARTS + LINE - 1, step, 0)

    sums2[z] = jnp.zeros(sums2.shape[1:], F32)

    def inner_one(i):
        at = rows_of(i, 16)
        w = dn1[at, :] * x_own[at, :].astype(F32)
        c = w * gain_one[at, :]
        sums2[z] += c[:8] + c[8:]
        w = w * scale_one[0:1, :]
        fold = w[:, 0:128]
        for j in range(1, seq // 128):
            fold = fold + w[:, j * 128 : (j + 1) * 128]
        mix_part[at, :] = fold

    blocks(block // 16, inner_one)
    share_line(sums2, l2_send, l2_recv, z, core)
    total = jnp.sum(jnp.sum(sums2[...], axis=0), axis=0, keepdims=True)
    s1 = scale_one[0:1, :]
    coef[0:1, :] = s1 * s1 * s1 * (total / width)

    def last(i):
        at = rows_of(i, 16)
        v = dy[at, :] + (
            scale_one[0:1, :] * (gain_one[at, :] * dn1[at, :]) - x_own[at, :].astype(F32) * coef[0:1, :]
        )
        ig[at, :] = v

    blocks(block // 16, last)
    mine = pl.ds(pl.multiple_of(core * seq, seq), seq)
    back = remote(ig.at[rows_of(1 - core, half), :], input_grad.at[:, mine], r_send, r_recv, sibling)
    back.start()
    input_grad[:, mine] = ig[rows_of(core, half), :]
    gather.sent()
    spread.sent()
    back.wait()


def sum_kernel(count, *refs):
    n = count
    grads, tiny = refs[:n], refs[n]
    outs, tiny_out = refs[n + 1 : 2 * n + 1], refs[2 * n + 1]
    rest = refs[2 * n + 2 :]
    fulls, gots, lands, fronts = rest[:n], rest[n : 2 * n], rest[2 * n : 3 * n], rest[3 * n : 4 * n]
    tiny_in, tiny_all = rest[4 * n], rest[4 * n + 1]
    a_send, a_recv, b_send, b_recv, c_sem = rest[4 * n + 2 :]
    row, z, core = place()
    sibling = {"col": 2 * z + (1 - core)}
    greet(row, z, core, True, False)

    def to_sibling(j):
        if j == n:
            return remote(tiny.at[1 - core], tiny_in, a_send.at[j], a_recv.at[j], sibling)
        return remote(grads[j].at[1 - core], gots[j], a_send.at[j], a_recv.at[j], sibling)

    def load(j):
        return pltpu.make_async_copy(grads[j].at[core], fulls[j], c_sem.at[j])

    def cols(r):
        return pl.ds(pl.multiple_of(r * 384, 384), 384)

    def to_row(j, d):
        if j == n:
            return remote(tiny_all.at[0], tiny_all.at[d], b_send.at[j, d - 1], b_recv.at[j, d - 1], {"row": row ^ d})
        return remote(
            fronts[j].at[d - 1], lands[j].at[d - 1], b_send.at[j, d - 1], b_recv.at[j, d - 1], {"row": row ^ d}
        )

    for j in range(n + 1):
        to_sibling(j).start()
    for j in range(n):
        load(j).start()
    for j in range(n):
        load(j).wait()
        to_sibling(j).wait_recv()
        full, got, front, out = fulls[j], gots[j], fronts[j], outs[j]

        for d in (1, 2, 3):

            def add(i):
                at = rows_of(i, 32)
                v = full[at, cols(row ^ d)].astype(F32) + got[at, cols(row ^ d)].astype(F32)
                front[d - 1, at, :] = v.astype(BF16)

            blocks(full.shape[0] // 32, add)
            to_row(j, d).start()

        def first(i):
            at = rows_of(i, 32)
            out[at, :] = full[at, cols(row)].astype(F32) + got[at, cols(row)].astype(F32)

        blocks(full.shape[0] // 32, first)
    to_sibling(n).wait_recv()
    tiny_all[0] = tiny[core] + tiny_in[...]
    for d in (1, 2, 3):
        to_row(n, d).start()
    for j in range(n):
        for d in (1, 2, 3):
            to_row(j, d).wait_recv()
        out, land = outs[j], lands[j]

        def second(i):
            at = rows_of(i, 32)
            out[at, :] += land[0, at, :].astype(F32) + (land[1, at, :].astype(F32) + land[2, at, :].astype(F32))

        blocks(out.shape[0] // 32, second)
    for d in (1, 2, 3):
        to_row(n, d).wait_recv()
    left, right = tiny_all[row % 2], tiny_all[1 - row % 2]
    up, down = tiny_all[2 + row % 2], tiny_all[3 - row % 2]
    tiny_out[...] = (left + right) + (up + down)
    for j in range(n + 1):
        to_sibling(j).wait_send()
        for d in (1, 2, 3):
            to_row(j, d).wait_send()


ANY = pl.BlockSpec(memory_space=pl.ANY)
VM = pl.BlockSpec(memory_space=pltpu.VMEM)
DMA = pltpu.SemaphoreType.DMA
ROOM = 60 * 1024 * 1024


def shape(dims, kind):
    return jax.ShapeDtypeStruct(dims, kind)


def call(kernel, ins, outs, scratch, ident, name, flops):
    return pl.pallas_call(
        kernel,
        out_shape=[o[0] for o in outs],
        in_specs=ins,
        out_specs=[o[1] for o in outs],
        scratch_shapes=scratch,
        name=name,
        compiler_params=pltpu.CompilerParams(
            collective_id=ident, has_side_effects=True, vmem_limit_bytes=ROOM
        ),
        cost_estimate=pl.CostEstimate(flops=flops, bytes_accessed=40000000, transcendentals=0),
    )


PAIRS = [[0, 1], [2, 3], [4, 5], [6, 7]]


def diagonal(w, size):
    per = size // w.shape[1]
    w = w.reshape(-1, per, w.shape[1], w.shape[2])
    eye = jnp.eye(per, dtype=w.dtype)
    full = w[:, :, :, None, :] * eye[None, :, None, :, None]
    return full.reshape(-1, size, size)


def fast_body(
    inputs, segments, mix_gain, branch_weight, recur_weight, kernel, offsets, retain_weight, retain_bias,
    admit_weight, admit_bias, lambdas, merge_weight, feed_gain, gate_weight, up_weight, down_weight, cotangent,
):
    half, tokens = inputs.shape
    block, seq, width = 2 * half, tokens // 2, D
    lru, heads = branch_weight.shape[1], retain_weight.shape[0]
    chan = 2 * lru
    ff = gate_weight.shape[1]
    hid = 2 * ff
    rows = branch_weight.shape[0]
    cols = merge_weight.shape[1]
    core = lax.axis_index("col") % 2

    parts = (mix_gain, feed_gain, kernel[0], kernel[1], kernel[2], kernel[3], offsets, retain_bias, admit_bias, lambdas)
    parts = parts + (retain_weight.reshape(-1), admit_weight.reshape(-1))
    both = lax.all_gather(jnp.concatenate(parts), "col", axis=0, axis_index_groups=PAIRS)
    whole, at = [], 0
    for part in parts:
        whole.append(both[:, at : at + part.shape[0]].reshape(-1))
        at += part.shape[0]
    gain_one, gain_two = whole[0][:, None], whole[1][:, None]
    lam = whole[9]
    rate = 8.0 * jax.nn.softplus(-lam)
    par = jnp.stack(whole[2:6] + whole[6:9] + [rate] + [jnp.zeros_like(lam)] * 8, axis=1)
    retain = diagonal(whole[10].reshape(-1, 64, 64), 256)
    admit = diagonal(whole[11].reshape(-1, 64, 64), 256)
    gates = jnp.concatenate([retain, admit], axis=2)
    gates_hi = gates.astype(BF16)
    gates_lo = (gates - gates_hi.astype(F32)).astype(BF16)
    flip = lambda w: jnp.swapaxes(w, 1, 2)

    segs = lax.dynamic_slice(segments, (core * seq,), (seq,))
    masks = [jnp.concatenate([jnp.ones((1,), bool), segs[1:] != segs[:-1]])]
    for lag in (1, 2, 3):
        masks.append(jnp.concatenate([jnp.zeros((lag,), bool), segs[lag:] == segs[:-lag]]))
    masks = jnp.pad(jnp.stack(masks).astype(F32), ((0, 4), (0, 128)))

    br_s = jnp.concatenate([branch_weight, recur_weight], axis=1).T
    m_s = merge_weight.T
    gu_s = jnp.concatenate([gate_weight, up_weight], axis=1).T

    f_tok = lambda n, kind=F32: shape((n, seq), kind)
    state = [(f_tok(chan), ANY)] * 6
    line = [DMA((3,)), DMA((3,))]
    steps = [DMA((2, 3, PARTS)), DMA((2, 3, PARTS))]
    sums = [DMA((2, PARTS, LINE)), DMA((2, PARTS, LINE))]
    held = pltpu.VMEM((PARTS, LINE + 1, block, PART), BF16)
    own = pltpu.VMEM((PARTS, LINE, block, PART), F32)
    tok = lambda n, kind=F32, lead=0: pltpu.VMEM((n, lead + seq), kind)

    y, n1, q, x_own, scale_one, br, mt, b, p, u, r, i, h, gu, down = call(
        functools.partial(mix_kernel, width, EPS),
        [VM] * 6 + [ANY] * 4,
        [(f_tok(block), VM), (f_tok(width, BF16), VM), (f_tok(chan, BF16), VM), (f_tok(block, BF16), VM), (f_tok(8), VM),
         (shape((2 * chan, width), BF16), VM), (shape((width, chan), BF16), VM)] + state
        + [(shape((2 * hid, width), BF16), ANY), (shape((hid, width), BF16), ANY)],
        [pltpu.VMEM((LINE, 8, seq), F32), tok(chan), tok(chan, F32, 128), tok(chan), tok(chan), tok(chan), tok(chan, F32, 128),
         pltpu.VMEM((chan, PART), BF16), pltpu.VMEM((chan, PART), BF16), own, held, DMA, DMA]
        + line + steps + sums + [DMA((4, 7)), DMA((4, 7)), DMA((4,)), DMA((6, PARTS))],
        0, "mix_forward", 5 * 10**9,
    )(inputs, gain_one, masks, par, flip(gates_hi), flip(gates_lo), br_s, m_s, gu_s, down_weight)

    result, n2, go, scale_two, dn2, hidden, grads_hidden = call(
        functools.partial(feed_kernel, width, EPS),
        [VM] * 3 + [ANY] * 4,
        [(shape((half, tokens), BF16), VM), (f_tok(width, BF16), VM), (f_tok(width, BF16), VM), (f_tok(8), VM), (f_tok(block), VM),
         (f_tok(hid, BF16), ANY), (f_tok(2 * hid, BF16), ANY)],
        [pltpu.VMEM((LINE, 8, seq), F32), pltpu.VMEM((2 * hid, width), BF16), pltpu.VMEM((width, 2 * hid), BF16),
         pltpu.VMEM((hid, width), BF16), pltpu.VMEM((width, hid), BF16), pltpu.VMEM((2 * hid, PART), F32),
         pltpu.VMEM((hid, PART), F32), pltpu.VMEM((2, hid, PART), BF16), pltpu.VMEM((2, 2 * hid, PART), BF16),
         tok(block, BF16), own, own, held, held, DMA((4,)), DMA, DMA]
        + line + steps + steps + sums + sums + [DMA, DMA, DMA((2, 2))],
        1, "feed", 33 * 10**9,
    )(y, gain_two, cotangent, gu, gu.T, down, down.T)

    nt = lambda a, c: lax.dot_general(a, c, (((1,), (1,)), ((), ())), preferred_element_type=F32).astype(BF16)
    g_gu = nt(grads_hidden, n2).reshape(2, hid, width)
    g_down = nt(hidden, go).reshape(2, ff, width)

    input_grad, dy, dbp, feed_part, mix_part, small, gate_grad = call(
        functools.partial(back_kernel, width),
        [VM] * 2 + [ANY] + [VM] * 8 + [ANY] * 8,
        [(shape((half, tokens), F32), VM), (f_tok(width, BF16), VM), (f_tok(2 * chan, BF16), VM), (shape((block, 128), F32), VM),
         (shape((block, 128), F32), VM), (shape((8, chan, 128), F32), VM), (shape((chan // 256, 256, 512), F32), VM)],
        [pltpu.VMEM((LINE, 8, seq), F32), pltpu.VMEM((LINE, 8, seq), F32), pltpu.VMEM((8, seq), F32),
         pltpu.VMEM((chan, width), BF16), pltpu.VMEM((width, 2 * chan), BF16),
         tok(chan), tok(chan, F32, 128), tok(chan), tok(chan), tok(chan), tok(chan, F32, 128), tok(block, BF16), tok(block), tok(block), tok(block),
         pltpu.VMEM((chan, PART), F32), tok(chan, F32, 128), pltpu.VMEM((2 * chan, PART), BF16), pltpu.VMEM((chan, 128), F32), own, held,
         DMA((3,)), DMA((6, PARTS))] + line + line + steps + sums + [DMA, DMA],
        2, "mix_backward", 5 * 10**9,
    )(y, dn2, go, x_own, scale_two, scale_one, gain_two, gain_one, masks, par, gates_hi, mt.T, br.T, b, p, u, r, i, h)

    g_br = nt(dbp, n1).reshape(2, chan, width)
    g_m = nt(q, dy).reshape(2, lru, width)

    small = jnp.sum(small, axis=2)
    small = jnp.concatenate([small[:7], small[7:] * (8.0 * jax.nn.sigmoid(-lam))[None]])
    gains = jnp.stack([jnp.sum(mix_part, axis=1), jnp.sum(feed_part, axis=1)])
    blocked = gate_grad.reshape(-1, 4, 64, 2, 4, 64)
    gate_blocks = jnp.stack([blocked[:, e, :, :, e, :] for e in range(4)], axis=1)
    tiny = jnp.concatenate(
        [
            jnp.swapaxes(small.reshape(8, 2, lru), 0, 1).reshape(2, -1),
            jnp.swapaxes(gains.reshape(2, 2, half), 0, 1).reshape(2, -1),
            gate_blocks.reshape(2, -1),
        ],
        axis=1,
    )
    size = tiny.shape[1]
    deep = -(-size // 1024) * 8
    tiny = jnp.pad(tiny, ((0, 0), (0, deep * 128 - size))).reshape(2, deep, 128)

    grads = (g_gu, g_down, g_br, g_m)
    count = len(grads)
    heights = [g.shape[1] for g in grads]
    outs = call(
        functools.partial(sum_kernel, count),
        [ANY] * count + [VM],
        [(shape((n, cols), F32), VM) for n in heights] + [(shape((deep, 128), F32), VM)],
        [pltpu.VMEM((n, width), BF16) for n in heights] * 2 + [pltpu.VMEM((3, n, cols), BF16) for n in heights] * 2
        + [pltpu.VMEM((deep, 128), F32), pltpu.VMEM((4, deep, 128), F32), DMA((count + 1,)), DMA((count + 1,)),
           DMA((count + 1, 3)), DMA((count + 1, 3)), DMA((count,))],
        3, "gradient_sums", 10**8,
    )(*grads, tiny)
    s_gu, s_down, s_br, s_m, tiny = outs
    tiny = tiny.reshape(-1)
    small = tiny[: 8 * lru].reshape(8, lru)
    gains = tiny[8 * lru : 8 * lru + 2 * half].reshape(2, half)
    gate_blocks = tiny[8 * lru + 2 * half : size].reshape(heads, 64, 2, 64)
    return (
        result,
        input_grad,
        gains[0],
        s_br[:lru].T,
        s_br[lru:].T,
        small[0:4],
        small[4],
        gate_blocks[:, :, 0],
        small[5],
        gate_blocks[:, :, 1],
        small[6],
        small[7],
        s_m,
        gains[1],
        s_gu[:ff].T,
        s_gu[ff:].T,
        s_down,
    )


def suits(mesh, args):
    return (
        dict(mesh.shape) == {"row": 4, "col": 8}
        and args[0].shape == (D, 8 * SEQ)
        and args[3].shape == (D, 2048)
        and args[14].shape == (D, 4608)
        and args[7].shape == (32, 64, 64)
    )


def solution(mesh):
    in_specs = (
        P("col", "row"),
        P("row"),
        P("col"),
        P("row", "col"),
        P("row", "col"),
        P(None, "col"),
        P("col"),
        P("col", None, None),
        P("col"),
        P("col", None, None),
        P("col"),
        P("col"),
        P("col", "row"),
        P("col"),
        P("row", "col"),
        P("row", "col"),
        P("col", "row"),
        P("col", "row"),
    )
    out_specs = (
        P("col", "row"),
        P("col", "row"),
        P("col"),
        P("row", "col"),
        P("row", "col"),
        P(None, "col"),
        P("col"),
        P("col", None, None),
        P("col"),
        P("col", None, None),
        P("col"),
        P("col"),
        P("col", "row"),
        P("col"),
        P("row", "col"),
        P("row", "col"),
        P("col", "row"),
    )
    def run(*args):
        chosen = fast_body if suits(mesh, args) else body
        return jax.shard_map(
            chosen, mesh=mesh, in_specs=in_specs, out_specs=out_specs, check_vma=False
        )(*args)

    return run
```

```python
import functools

import jax
import jax.numpy as jnp
from jax import lax
from jax.experimental import pallas as pl
from jax.experimental.pallas import tpu as pltpu
from jax.sharding import PartitionSpec as P

D = 1536
SEQ = 1024
MICRO = 2


HIGH = lax.Precision.HIGHEST
EPS = 1e-06
POWER = 8.0
FLOOR = 0.01


def combine(earlier, later):
    first_a, first_b = earlier
    second_a, second_b = later
    return (first_a * second_a, second_a * first_b + second_b)


def mixer(
    branch_pre,
    lru_pre,
    segs,
    kernel,
    offsets,
    retain_weight,
    retain_bias,
    admit_weight,
    admit_bias,
    lambdas,
):
    length = lru_pre.shape[0]
    channels = lru_pre.shape[1]
    conv = offsets + kernel[0] * lru_pre
    for lag in range(1, kernel.shape[0]):
        shifted = jnp.concatenate(
            [jnp.zeros((lag, channels), lru_pre.dtype), lru_pre[:-lag]], axis=0
        )
        prior = jnp.concatenate([jnp.full((lag,), -1, jnp.int32), segs[:-lag]])
        keep = (prior == segs).astype(lru_pre.dtype)
        conv = conv + kernel[lag] * shifted * keep[:, None]
    heads = retain_weight.shape[0]
    blocks = conv.reshape(length, heads, channels // heads)
    retain = jax.nn.sigmoid(
        jnp.einsum("thi,hij->thj", blocks, retain_weight, precision=HIGH).reshape(length, channels)
        + retain_bias
    )
    admit = jax.nn.sigmoid(
        jnp.einsum("thi,hij->thj", blocks, admit_weight, precision=HIGH).reshape(length, channels)
        + admit_bias
    )
    decay = jnp.exp(-POWER * retain * jax.nn.softplus(-lambdas))
    factor = jnp.sqrt(1.0 - decay * decay + FLOOR)
    starts = jnp.concatenate([jnp.ones((1,), bool), segs[1:] != segs[:-1]])
    decay = jnp.where(starts[:, None], 0.0, decay)
    factor = jnp.where(starts[:, None], 1.0, factor)
    _, state = lax.associative_scan(combine, (decay, factor * admit * conv), axis=0)
    return jax.nn.gelu(branch_pre) * state


def geglu(gate, upper):
    return jax.nn.gelu(gate) * upper


def contract_rows(left, right):
    return lax.dot_general(
        left, right, (((0,), (0,)), ((), ())), preferred_element_type=jnp.float32
    )


def contract_cols(left, right):
    return lax.dot_general(
        left, right, (((1,), (1,)), ((), ())), preferred_element_type=jnp.float32
    )


def contract_cross(left, right):
    return lax.dot_general(
        left, right, (((0,), (1,)), ((), ())), preferred_element_type=jnp.float32
    )


def norm_forward(resid, gain):
    total = lax.psum(jnp.sum(resid * resid, axis=0), "col")
    scale = lax.rsqrt(total / D + EPS)[None, :]
    return (scale, (resid * scale * gain[:, None]).astype(jnp.bfloat16))


def norm_backward(resid, scale, gain, grad_normed):
    weighted = grad_normed * gain[:, None]
    total = lax.psum(jnp.sum(weighted * resid, axis=0), "col")
    grad_resid = scale * weighted - resid * (scale * scale * scale) * (total / D)[None, :]
    grad_gain = jnp.sum(grad_normed * resid * scale, axis=1)
    return (grad_resid, grad_gain)


def gather_features(normed):
    return lax.all_gather(normed, "col", axis=0, tiled=True)


def gather_cotangent(grad):
    return lax.all_gather(grad, "col", axis=0, tiled=True)


def spread_sum(term):
    return lax.psum_scatter(
        term.astype(jnp.bfloat16), "col", scatter_dimension=0, tiled=True
    ).astype(jnp.float32)


def back_sum(term):
    return spread_sum(term)


def merge_term(whole_merge, mixed_low):
    return spread_sum(contract_cross(whole_merge, mixed_low))


def weight_grads(normed, grad_joined):
    return jnp.dot(
        normed,
        grad_joined,
        preferred_element_type=jnp.float32,
    )


def row_sum(total, axis):
    return lax.psum_scatter(
        total.astype(jnp.bfloat16), "row", scatter_dimension=axis, tiled=True
    ).astype(jnp.float32)


def body(
    inputs,
    segments,
    mix_gain,
    branch_weight,
    recur_weight,
    kernel,
    offsets,
    retain_weight,
    retain_bias,
    admit_weight,
    admit_bias,
    lambdas,
    merge_weight,
    feed_gain,
    gate_weight,
    up_weight,
    down_weight,
    cotangent,
):
    lru_cols = branch_weight.shape[1]
    feed_cols = gate_weight.shape[1]
    mixer_params = (kernel, offsets, retain_weight, retain_bias, admit_weight, admit_bias, lambdas)
    acc_branch = jnp.zeros((D, lru_cols), jnp.float32)
    acc_recur = jnp.zeros((D, lru_cols), jnp.float32)
    acc_gate = jnp.zeros((D, feed_cols), jnp.float32)
    acc_up = jnp.zeros((D, feed_cols), jnp.float32)
    acc_merge = jnp.zeros((lru_cols, D), jnp.float32)
    acc_down = jnp.zeros((feed_cols, D), jnp.float32)
    acc_small = tuple((jnp.zeros_like(p) for p in mixer_params))
    acc_mix = jnp.zeros_like(mix_gain)
    acc_feed = jnp.zeros_like(feed_gain)
    outputs = []
    in_grads = []
    for batch in range(MICRO):
        lower = batch * SEQ
        resid_in = inputs[:, lower : lower + SEQ].astype(jnp.float32)
        grad_out = cotangent[:, lower : lower + SEQ].astype(jnp.float32)
        segs = segments[lower : lower + SEQ]
        whole_branch, whole_recur, whole_gate, whole_up = (
            lax.all_gather(branch_weight, "row", axis=0, tiled=True),
            lax.all_gather(recur_weight, "row", axis=0, tiled=True),
            lax.all_gather(gate_weight, "row", axis=0, tiled=True),
            lax.all_gather(up_weight, "row", axis=0, tiled=True),
        )
        whole_merge, whole_down = (
            lax.all_gather(merge_weight, "row", axis=1, tiled=True),
            lax.all_gather(down_weight, "row", axis=1, tiled=True),
        )
        scale_one, normed_one = norm_forward(resid_in, mix_gain)
        full_one = gather_features(normed_one)
        branch_pre = contract_rows(full_one, whole_branch)
        lru_pre = contract_rows(full_one, whole_recur)

        def local_mixer(bpre, lpre, kern, offs, rweight, rbias, aweight, abias, lams):
            return mixer(bpre, lpre, segs, kern, offs, rweight, rbias, aweight, abias, lams)

        mixed, mixer_pull = jax.vjp(local_mixer, branch_pre, lru_pre, *mixer_params)
        mixed_low = mixed.astype(jnp.bfloat16)
        resid_mid = resid_in + merge_term(whole_merge, mixed_low)
        scale_two, normed_two = norm_forward(resid_mid, feed_gain)
        full_two = gather_features(normed_two)
        gate = contract_rows(full_two, whole_gate)
        upper = contract_rows(full_two, whole_up)
        hidden, geglu_pull = jax.vjp(geglu, gate, upper)
        hidden_low = hidden.astype(jnp.bfloat16)
        result = resid_mid + spread_sum(contract_cross(whole_down, hidden_low))
        outputs.append(result.astype(jnp.bfloat16))
        grad_full = gather_cotangent(grad_out.astype(jnp.bfloat16))
        acc_down = acc_down + contract_cross(hidden_low, grad_full)
        grad_gate, grad_upper = geglu_pull(contract_cross(grad_full, whole_down))
        grad_gate = grad_gate.astype(jnp.bfloat16)
        grad_upper = grad_upper.astype(jnp.bfloat16)
        feed_joined = weight_grads(full_two, jnp.concatenate([grad_gate, grad_upper], axis=1))
        acc_gate = acc_gate + feed_joined[:, :feed_cols]
        acc_up = acc_up + feed_joined[:, feed_cols:]
        grad_normed_two = back_sum(
            contract_cols(whole_gate, grad_gate) + contract_cols(whole_up, grad_upper)
        )
        grad_mid_norm, feed_part = norm_backward(resid_mid, scale_two, feed_gain, grad_normed_two)
        acc_feed = acc_feed + feed_part
        grad_mid = grad_out + grad_mid_norm
        grad_mid_full = gather_cotangent(grad_mid.astype(jnp.bfloat16))
        acc_merge = acc_merge + contract_cross(mixed_low, grad_mid_full)
        pulled = mixer_pull(contract_cross(grad_mid_full, whole_merge))
        grad_branch = pulled[0].astype(jnp.bfloat16)
        grad_lru = pulled[1].astype(jnp.bfloat16)
        acc_small = tuple((total + part for total, part in zip(acc_small, pulled[2:])))
        branch_joined = weight_grads(full_one, jnp.concatenate([grad_branch, grad_lru], axis=1))
        acc_branch = acc_branch + branch_joined[:, :lru_cols]
        acc_recur = acc_recur + branch_joined[:, lru_cols:]
        grad_normed_one = back_sum(
            contract_cols(whole_branch, grad_branch) + contract_cols(whole_recur, grad_lru)
        )
        grad_in_norm, mix_part = norm_backward(resid_in, scale_one, mix_gain, grad_normed_one)
        acc_mix = acc_mix + mix_part
        in_grads.append(grad_mid + grad_in_norm)
    sum_branch, sum_recur, sum_gate, sum_up = (
        row_sum(acc_branch, 0),
        row_sum(acc_recur, 0),
        row_sum(acc_gate, 0),
        row_sum(acc_up, 0),
    )
    sum_merge, sum_down = (
        row_sum(acc_merge, 1),
        row_sum(acc_down, 1),
    )
    summed = lax.psum(
        (
            acc_mix,
            acc_feed,
            acc_small[0],
            acc_small[1],
            acc_small[2],
            acc_small[3],
            acc_small[4],
            acc_small[5],
            acc_small[6],
        ),
        "row",
    )
    result_all = jnp.concatenate(outputs, axis=1)
    input_grad = jnp.concatenate(in_grads, axis=1)
    return (
        result_all,
        input_grad,
        summed[0],
        sum_branch,
        sum_recur,
        summed[2],
        summed[3],
        summed[4],
        summed[5],
        summed[6],
        summed[7],
        summed[8],
        sum_merge,
        summed[1],
        sum_gate,
        sum_up,
        sum_down,
    )


MESH = pl.DeviceIdType.MESH
F32 = jnp.float32
BF16 = jnp.bfloat16
LINE = 4
PART = 256
PARTS = 4
GELU_A = 0.7978845608028654
GELU_B = 0.044715


def place():
    row, col = lax.axis_index("row"), lax.axis_index("col")
    return row, col // 2, col % 2


def at_line(z, core):
    return {"col": 2 * z + core}


def lanes(part):
    return pl.ds(pl.multiple_of(part * PART, PART), PART)


def rows_of(index, size):
    return pl.ds(pl.multiple_of(index * size, 16), size)


def dot(a, b):
    return lax.dot_general(a, b, (((1,), (0,)), ((), ())), preferred_element_type=F32)


def dot_nt(a, b):
    return lax.dot_general(a, b, (((1,), (1,)), ((), ())), preferred_element_type=F32)


def greet(row, z, core, rows, line):
    barrier = pltpu.get_barrier_semaphore()
    peers = [{"col": 2 * z + (1 - core)}]
    if rows:
        peers += [{"row": row ^ d} for d in (1, 2, 3)]
    if line:
        peers += [at_line(z ^ d, core) for d in (1, 2, 3)]
    for peer in peers:
        pl.semaphore_signal(barrier, inc=1, device_id=peer, device_id_type=MESH)
    pl.semaphore_wait(barrier, len(peers))


def remote(src, dst, send, recv, peer):
    return pltpu.make_async_remote_copy(
        src_ref=src, dst_ref=dst, send_sem=send, recv_sem=recv, device_id=peer, device_id_type=MESH
    )


class Gather:
    def __init__(self, ref, send, recv, z, core, block, back=False):
        self.ref, self.sems, self.z, self.core = ref, (send, recv), z, core
        self.block, self.back = block, back

    def copy(self, way, hop, step, owner, incoming=False):
        part = PARTS - 1 - step if self.back else step
        piece = self.ref.at[rows_of(owner, self.block), lanes(part)]
        peer = at_line(self.z + (1 if (way == 0) != incoming else -1), self.core)
        return remote(piece, piece, self.sems[0].at[way, hop, step], self.sems[1].at[way, hop, step], peer)

    def each(self, hop, act, incoming):
        z = self.z
        if incoming:
            cases = ((0, z - 1 - hop >= 0, z - 1 - hop), (1, z + 1 + hop < LINE, z + 1 + hop))
        else:
            cases = (
                (0, (z >= hop) & (z < LINE - 1), z - hop),
                (1, (z + hop < LINE) & (z >= 1), z + hop),
            )
        for way, here, owner in cases:
            pl.when(here)(functools.partial(act, way, owner))

    def send(self, hop, step):
        self.each(hop, lambda way, owner: self.copy(way, hop, step, owner).start(), False)

    def arrive(self, hop, step):
        self.each(hop, lambda way, owner: self.copy(way, hop, step, owner, True).wait_recv(), True)

    def forward(self, hop, step):
        self.arrive(hop - 1, step)
        self.send(hop, step)

    def sent(self):
        def one(step, carry):
            for hop in range(LINE - 1):
                self.each(hop, lambda way, owner: self.copy(way, hop, step, owner).wait_send(), False)
            return carry

        lax.fori_loop(0, PARTS, one, 0)

    def open(self):
        self.send(0, 0)
        self.forward(1, 0)
        self.send(0, 1)
        self.forward(2, 0)

    def middle(self, step):
        @pl.when(step + 1 < PARTS)
        def _():
            self.forward(1, step + 1)

        @pl.when(step + 2 < PARTS)
        def _():
            self.send(0, step + 2)

    def later(self, step):
        @pl.when(step + 1 < PARTS)
        def _():
            self.forward(2, step + 1)


class Spread:
    def __init__(self, own, held, send, recv, z, core):
        self.own, self.held, self.sems, self.z, self.core = own, held, (send, recv), z, core

    def copy(self, way, step, hop):
        slot = hop if way == 0 else LINE - hop
        there = slot - 1 if way == 0 else slot + 1
        peer = at_line(self.z + (1 if way == 0 else -1), self.core)
        return remote(
            self.held.at[step, slot],
            self.held.at[step, there],
            self.sems[0].at[way, step, hop],
            self.sems[1].at[way, step, hop - 1],
            peer,
        )

    def landed(self, way, step, hop):
        slot = hop if way == 0 else LINE - hop
        piece = self.held.at[step, slot]
        peer = at_line(self.z + (-1 if way == 0 else 1), self.core)
        remote(piece, piece, self.sems[0].at[way, step, hop], self.sems[1].at[way, step, hop], peer).wait_recv()

    def push(self, way, step):
        z = self.z
        first = z == 0 if way == 0 else z == LINE - 1

        def one(i, carry):
            hop = LINE - 1 - i
            owner = z + hop if way == 0 else z - hop
            slot = hop if way == 0 else LINE - hop

            @pl.when((owner >= 0) & (owner < LINE))
            def _():
                @pl.when(first)
                def _():
                    self.held[step, slot] = self.own[step, owner].astype(BF16)

                @pl.when(jnp.logical_not(first))
                def _():
                    self.landed(way, step, hop)
                    total = self.own[step, owner].astype(F32) + self.held[step, slot].astype(F32)
                    self.held[step, slot] = total.astype(BF16)

                self.copy(way, step, hop).start()

            return carry

        lax.fori_loop(0, LINE - 1, one, 0)

    def serve(self, t, finish):
        z = self.z
        for way, late in ((0, z), (1, LINE - 1 - z)):
            step = t - late
            pl.when((step >= 0) & (step < PARTS))(functools.partial(self.push, way, step))
        step = t - (LINE - 1)

        @pl.when((step >= 0) & (step < PARTS))
        def _():
            @pl.when(z == 0)
            def _():
                self.landed(1, step, 0)
                finish(step, lambda a, n: self.mine(step, a, n) + self.got(step, LINE, a, n))

            @pl.when(z == LINE - 1)
            def _():
                self.landed(0, step, 0)
                finish(step, lambda a, n: self.mine(step, a, n) + self.got(step, 0, a, n))

            @pl.when((z > 0) & (z < LINE - 1))
            def _():
                self.landed(0, step, 0)
                self.landed(1, step, 0)
                finish(
                    step,
                    lambda a, n: self.mine(step, a, n) + (self.got(step, 0, a, n) + self.got(step, LINE, a, n)),
                )

    def mine(self, step, start, size):
        return self.own[step, self.z, pl.ds(start, size)].astype(F32)

    def got(self, step, slot, start, size):
        return self.held[step, slot, pl.ds(start, size)].astype(F32)

    def sent(self):
        z = self.z

        def one(step, carry):
            for way in (0, 1):
                for hop in range(1, LINE):
                    owner = z + hop if way == 0 else z - hop

                    @pl.when((owner >= 0) & (owner < LINE))
                    def _():
                        self.copy(way, step, hop).wait_send()

            return carry

        lax.fori_loop(0, PARTS, one, 0)


def share_line(ref, send, recv, z, core):
    copies = [
        remote(ref.at[z], ref.at[z], send.at[d - 1], recv.at[d - 1], at_line(z ^ d, core)) for d in (1, 2, 3)
    ]
    for copy in copies:
        copy.start()
    for d in (1, 2, 3):
        piece = ref.at[z ^ d]
        remote(piece, piece, send.at[d - 1], recv.at[d - 1], at_line(z ^ d, core)).wait_recv()
    for copy in copies:
        copy.wait_send()


class Weights:
    def __init__(self, src, dst, send, recv, own, row, z, core, turned):
        self.src, self.dst, self.send, self.recv, self.own = src, dst, send, recv, own
        self.row, self.core, self.turned = row, core, turned
        self.sibling = {"col": 2 * z + (1 - core)}

    def spot(self, row, core):
        down, right = (row, core) if self.turned else (core, row)
        rows, cols = self.src.shape
        return self.dst.at[rows_of(down, rows), pl.ds(pl.multiple_of(right * cols, 128), cols)]

    def to_row(self, d):
        return remote(
            self.src, self.spot(self.row, self.core), self.send.at[d], self.recv.at[d], {"row": self.row ^ d}
        )

    def to_sibling(self, d):
        if d == 0:
            return remote(
                self.src, self.spot(self.row, self.core), self.send.at[0], self.recv.at[0], self.sibling
            )
        piece = self.spot(self.row ^ d, self.core)
        return remote(piece, piece, self.send.at[3 + d], self.recv.at[3 + d], self.sibling)

    def local(self):
        return pltpu.make_async_copy(self.src, self.spot(self.row, self.core), self.own)

    def start(self):
        for d in (1, 2, 3):
            self.to_row(d).start()
        self.to_sibling(0).start()
        self.local().start()

    def forward(self):
        for d in (1, 2, 3):
            piece = self.spot(self.row ^ d, self.core)
            remote(piece, piece, self.send.at[d], self.recv.at[d], {"row": self.row ^ d}).wait_recv()
            self.to_sibling(d).start()

    def finish(self):
        self.local().wait()
        for d in (0, 1, 2, 3):
            piece = self.spot(self.row ^ d, 1 - self.core)
            sem = 0 if d == 0 else 3 + d
            remote(piece, piece, self.send.at[sem], self.recv.at[sem], self.sibling).wait_recv()

    def sent(self):
        for d in (1, 2, 3):
            self.to_row(d).wait_send()
            self.to_sibling(d).wait_send()
        self.to_sibling(0).wait_send()


def gelu_parts(b):
    t = jnp.tanh(GELU_A * (b + GELU_B * (b * b * b)))
    half = 0.5 + 0.5 * t
    slope = half + (0.5 * b) * (1.0 - t * t) * (GELU_A + (3.0 * GELU_A * GELU_B) * (b * b))
    return b * half, slope


def blocks(count, body):
    def one(i, carry):
        body(i)
        return carry

    lax.fori_loop(0, count, one, 0)


def scale_of(ref, eps, width):
    total = jnp.sum(jnp.sum(ref[...], axis=0), axis=0, keepdims=True)
    return lax.rsqrt(total / width + eps)


def mix_kernel(
    width, eps,
    x_in, gain, masks, par, gates_hi, gates_lo, br_s, m_s, gu_s, d_s,
    y, normed, q, x_own, scale, br, mt, b_out, p_out, u_out, r_out, i_out, h_out, gu, down,
    sums, b_s, p_s, u_s, r_s, i_s, h_s, a_c, uh, ul, own, held,
    x_send, x_recv, l_send, l_recv, g_send, g_recv, s_send, s_recv, w_send, w_recv, w_own, o_sem,
):
    row, z, core = place()
    block, seq = y.shape
    half = x_in.shape[0]
    chan = q.shape[0]
    greet(row, z, core, True, True)
    weights = [
        Weights(src, dst, w_send.at[n], w_recv.at[n], w_own.at[n], row, z, core, n == 1)
        for n, (src, dst) in enumerate(((br_s, br), (m_s, mt), (gu_s, gu), (d_s, down)))
    ]
    mine = pl.ds(pl.multiple_of(core * seq, seq), seq)
    other = pl.ds(pl.multiple_of((1 - core) * seq, seq), seq)
    swap = remote(
        x_in.at[:, other], x_own.at[rows_of(core, half), :], x_send, x_recv, {"col": 2 * z + (1 - core)}
    )
    swap.start()
    for w in weights[:2]:
        w.start()
    x_own[rows_of(core, half), :] = x_in[:, mine]
    swap.wait()

    sums[z] = jnp.zeros(sums.shape[1:], F32)

    def squares(i):
        v = x_own[rows_of(i, 16), :].astype(F32)
        v = v * v
        sums[z] += v[:8] + v[8:]

    blocks(block // 16, squares)
    share_line(sums, l_send, l_recv, z, core)
    s1 = scale_of(sums, eps, width)
    scale[...] = jnp.broadcast_to(s1, scale.shape)

    def norm(i):
        v = x_own[rows_of(i, 16), :].astype(F32) * scale[0:1, :] * gain[rows_of(i, 16), :]
        normed[pl.ds(pl.multiple_of(z * block + i * 16, 16), 16), :] = v.astype(BF16)

    blocks(block // 16, norm)
    gather = Gather(normed, g_send, g_recv, z, core, block)
    spread = Spread(own, held, s_send, s_recv, z, core)
    gather.open()
    p_s[:, 0:128] = jnp.zeros((chan, 128), F32)
    h_s[:, 0:128] = jnp.zeros((chan, 128), F32)
    for w in weights[:2]:
        w.forward()
    for w in weights[:2]:
        w.finish()
    for w in weights[2:]:
        w.start()

    hc = chan // 2
    kept = (b_s, p_s, u_s, r_s, i_s, h_s)
    outs = (b_out, p_out, u_out, r_out, i_out, h_out)

    def keep(n, part):
        lead = 128 if kept[n] is p_s or kept[n] is h_s else 0
        at = pl.ds(pl.multiple_of(lead + part * PART, 128), PART)
        to = at if lead else lanes(part)
        return pltpu.make_async_copy(kept[n].at[:, at], outs[n].at[:, to], o_sem.at[n, part])

    def pad(n):
        side = pl.ds(0, 128)
        return pltpu.make_async_copy(kept[n].at[:, side], outs[n].at[:, side], o_sem.at[n, PARTS])

    pad(1).start()
    pad(5).start()

    def work(k):
        here = lanes(k)
        ahead = pl.ds(pl.multiple_of(128 + k * PART, 128), PART)
        wide = pl.ds(pl.multiple_of(k * PART, 128), PART + 128)
        n1 = normed[:, here]
        for c in (0, 1):
            b_s[c * hc : (c + 1) * hc, here] = dot(br[c * 2 * hc : c * 2 * hc + hc, :], n1)
            p_s[c * hc : (c + 1) * hc, ahead] = dot(br[c * 2 * hc + hc : (c + 1) * 2 * hc, :], n1)

        def conv(i):
            ch = rows_of(i, 32)
            window = p_s[ch, wide]
            pr = par[ch, :]
            u = pr[:, 4:5] + pr[:, 0:1] * window[:, 128:]
            for lag in (1, 2, 3):
                u = u + pr[:, lag : lag + 1] * (pltpu.roll(window, lag, 1)[:, 128:] * masks[lag : lag + 1, here])
            u_s[ch, here] = u
            high = u.astype(BF16)
            uh[ch, :] = high
            ul[ch, :] = (u - high.astype(F32)).astype(BF16)

        blocks(chan // 32, conv)
        gather.middle(k)
        for g in range(chan // 256):
            at = slice(g * 256, (g + 1) * 256)
            pre = dot(gates_hi[g], uh[at, :]) + dot(gates_hi[g], ul[at, :]) + dot(gates_lo[g], uh[at, :])
            r_s[at, here] = pre[:256]
            i_s[at, here] = pre[256:]

        def decay(i):
            ch = rows_of(i, 64)
            pr = par[ch, :]
            start = masks[0:1, here] > 0.5
            r = jax.nn.sigmoid(r_s[ch, here] + pr[:, 5:6])
            gate = jax.nn.sigmoid(i_s[ch, here] + pr[:, 6:7])
            r_s[ch, here] = r
            i_s[ch, here] = gate
            a = jnp.exp(-(r * pr[:, 7:8]))
            m = jnp.where(start, 1.0, jnp.sqrt(1.0 - a * a + FLOOR))
            a_c[ch, :] = jnp.where(start, 0.0, a)
            h_s[ch, ahead] = m * gate * u_s[ch, here]

        blocks(chan // 64, decay)
        first = lax.broadcasted_iota(jnp.int32, (64, PART), 1) == 0

        def recur(i):
            ch = rows_of(i, 64)
            a, h = a_c[ch, :], h_s[ch, ahead]
            last = h_s[ch, pl.ds(pl.multiple_of(k * PART, 128), 128)][:, 127:128]
            h = h + jnp.where(first, a * last, 0.0)
            a = jnp.where(first, 0.0, a)
            shift = 1
            while shift < PART:
                h = h + a * pltpu.roll(h, shift, 1)
                if shift * 2 < PART:
                    a = a * pltpu.roll(a, shift, 1)
                shift *= 2
            h_s[ch, ahead] = h

        blocks(chan // 64, recur)
        gather.later(k)

        def mixed(i):
            ch = rows_of(i, 64)
            b = b_s[ch, here]
            t = jnp.tanh(GELU_A * (b + GELU_B * (b * b * b)))
            q[ch, here] = (b * (0.5 + 0.5 * t) * h_s[ch, ahead]).astype(BF16)

        blocks(chan // 64, mixed)
        qk = q[:, here]
        for s in range(LINE):
            own[k, s] = dot(mt[s * block : (s + 1) * block, :], qk)
        for n in range(len(kept)):
            keep(n, k).start()

    def finish(k, total):
        def add(i):
            at = pl.multiple_of(i * 16, 16)
            y[pl.ds(at, 16), lanes(k)] = x_own[pl.ds(at, 16), lanes(k)].astype(F32) + total(at, 16)

        blocks(block // 16, add)

    def step(t, carry):
        @pl.when(t < PARTS)
        def _():
            gather.arrive(2, t)
            work(t)

        for n in (2, 3):
            pl.when(t == PARTS + n - 2)(weights[n].forward)
        spread.serve(t, finish)
        return carry

    lax.fori_loop(0, PARTS + LINE - 1, step, 0)
    for w in weights[2:]:
        w.finish()
    for w in weights:
        w.sent()
    gather.sent()
    spread.sent()
    for n in range(len(kept)):
        blocks(PARTS, lambda part: keep(n, part).wait())
    pad(1).wait()
    pad(5).wait()


def feed_kernel(
    width, eps,
    y, gain, g_in, gu_h, d_h, br_s, m_s,
    result, normed, go, scale, dn2, g_own, g_got, gd_own, gd_got, br_n, m_n,
    sums, gu, gun, down, dt, ev, dz, zs, dev, res, own_o, own_n, held_o, held_n,
    c_sem, x_send, x_recv, l_send, l_recv, g_send, g_recv, e_send, e_recv, s_send, s_recv, t_send, t_recv,
    r_send, r_recv, w_send, w_recv, w_own, d_send, d_recv, d_own,
):
    row, z, core = place()
    block, seq = y.shape
    half = g_in.shape[0]
    sibling = {"col": 2 * z + (1 - core)}
    greet(row, z, core, True, True)
    loads = [
        pltpu.make_async_copy(src, dst, c_sem.at[n]) for n, (src, dst) in enumerate(((gu_h, gu), (d_h, down)))
    ]
    for load in loads:
        load.start()
    mine = pl.ds(pl.multiple_of(core * seq, seq), seq)
    other = pl.ds(pl.multiple_of((1 - core) * seq, seq), seq)
    inner = pl.ds(pl.multiple_of(z * block + core * half, 16), half)
    swap = remote(g_in.at[:, other], go.at[inner, :], x_send, x_recv, sibling)
    swap.start()
    go[inner, :] = g_in[:, mine]

    sums[z] = jnp.zeros(sums.shape[1:], F32)

    def squares(i):
        v = y[rows_of(i, 16), :]
        v = v * v
        sums[z] += v[:8] + v[8:]

    blocks(block // 16, squares)
    share_line(sums, l_send, l_recv, z, core)
    s2 = scale_of(sums, eps, width)
    scale[...] = jnp.broadcast_to(s2, scale.shape)

    def norm(i):
        v = y[rows_of(i, 16), :] * scale[0:1, :] * gain[rows_of(i, 16), :]
        normed[pl.ds(pl.multiple_of(z * block + i * 16, 16), 16), :] = v.astype(BF16)

    blocks(block // 16, norm)
    swap.wait()
    gather = Gather(normed, g_send, g_recv, z, core, block)
    gather_go = Gather(go, e_send, e_recv, z, core, block)
    spread_o = Spread(own_o, held_o, s_send, s_recv, z, core)
    spread_n = Spread(own_n, held_n, t_send, t_recv, z, core)
    hid = zs.shape[0]
    hh = hid // 2
    gather.send(0, 0)
    gather_go.send(0, 0)
    weights = [
        Weights(src, dst, w_send.at[n], w_recv.at[n], w_own.at[n], row, z, core, n == 0)
        for n, (src, dst) in enumerate(((br_s, br_n), (m_s, m_n)))
    ]
    for w in weights:
        w.start()
    loads[1].wait()

    def turn_down(i):
        at = pl.ds(pl.multiple_of(i * 128, 128), 128)
        dt[:, at] = down[at, :].T

    blocks(hid // 128, turn_down)
    gather.forward(1, 0)
    gather_go.forward(1, 0)
    gather.send(0, 1)
    gather_go.send(0, 1)
    loads[0].wait()

    def turn_up(i):
        at = pl.ds(pl.multiple_of(i * 128, 128), 128)
        gun[:, at] = gu[at, :].T

    blocks(hid // 128, turn_up)
    gather.forward(2, 0)
    gather_go.forward(2, 0)
    blocks(hid // 128, lambda i: turn_up(i + hid // 128))

    def work(k):
        here = lanes(k)
        n2 = normed[:, here]
        for c in range(2):
            for e in range(2):
                ev[e * hh : (e + 1) * hh, :] = dot(gu[(2 * c + e) * hh : (2 * c + e + 1) * hh, :], n2)
            if c == 0:
                gather.middle(k)
                gather_go.middle(k)
                gather_go.arrive(2, k)
            dz[...] = dot(down[c * hh : (c + 1) * hh, :], go[:, here])

            def one(i):
                off = pl.multiple_of(i * 64, 64)
                e = ev[pl.ds(off, 64), :]
                v = ev[pl.ds(hh + off, 64), :]
                d = dz[pl.ds(off, 64), :]
                act, slope = gelu_parts(e)
                zs[pl.ds(c * hh + off, 64), here] = (act * v).astype(BF16)
                dev[pl.ds(c * 2 * hh + off, 64), here] = (d * v * slope).astype(BF16)
                dev[pl.ds(c * 2 * hh + hh + off, 64), here] = (d * act).astype(BF16)

            blocks(hh // 64, one)
        gather.later(k)
        gather_go.later(k)
        dk = dev[:, here]
        for s in range(LINE):
            own_n[k, s] = dot(gun[s * block : (s + 1) * block, :], dk)
        spread_n.serve(k, finish_n)
        zk = zs[:, here]
        for s in range(LINE):
            own_o[k, s] = dot(dt[s * block : (s + 1) * block, :], zk).astype(own_o.dtype)
        spread_o.serve(k, finish_o)

    def columns(start):
        return pl.ds(pl.multiple_of(start, 128), block)

    def place_up(j):
        side = jnp.where(j >= 3, core, 1 - core)
        return side * hid + (j % 3) * block, columns((j % 3) * block)

    def send_up(j):
        at, to = place_up(j)
        return remote(gun.at[:, columns(at)], g_got.at[:, to], d_send.at[j], d_recv.at[j], sibling)

    def keep_up(j):
        at, to = place_up(j)
        return pltpu.make_async_copy(gun.at[:, columns(at)], g_own.at[:, to], d_own.at[j - 3])

    def send_down():
        return remote(down.at[rows_of(1 - core, hh), :], gd_got, d_send.at[3], d_recv.at[3], sibling)

    def keep_down():
        return pltpu.make_async_copy(down.at[rows_of(core, hh), :], gd_own, d_own.at[3])

    def grad_up(j):
        at = place_up(j)[0]
        right = pl.ds(pl.multiple_of(at, 16), block)
        for low in (0, width // 2):
            piece = slice(low, low + width // 2)
            gun[piece, columns(at)] = dot_nt(normed[piece, :], dev[right, :]).astype(BF16)

        @pl.when(j < 3)
        def _():
            send_up(j).start()

        @pl.when(j >= 3)
        def _():
            keep_up(j).start()

    def grad_down(side):
        at = rows_of(side, hh)
        down[at, :] = dot_nt(zs[at, :], go[...]).astype(BF16)

    def finish_o(k, total):
        def add(i):
            at = pl.multiple_of(i * 16, 16)
            res[pl.ds(at, 16), lanes(k)] = (y[pl.ds(at, 16), lanes(k)] + total(at, 16)).astype(BF16)

        blocks(block // 16, add)

    def finish_n(k, total):
        def add(i):
            at = pl.multiple_of(i * 16, 16)
            dn2[pl.ds(at, 16), lanes(k)] = total(at, 16)

        blocks(block // 16, add)

    def step(t, carry):
        gather.arrive(2, t)
        work(t)
        pl.when(t == 2)(weights[0].forward)
        pl.when(t == 3)(weights[1].forward)
        return carry

    lax.fori_loop(0, PARTS, step, 0)

    def drain(i, carry):
        t = PARTS + i
        blocks(2, lambda j: grad_up(2 * i + j))
        spread_n.serve(t, finish_n)
        spread_o.serve(t, finish_o)

        @pl.when(i < 2)
        def _():
            grad_down(jnp.where(i == 0, 1 - core, core))

        pl.when(i == 0)(lambda: send_down().start())
        pl.when(i == 1)(lambda: keep_down().start())
        return carry

    lax.fori_loop(0, LINE - 1, drain, 0)
    back = remote(
        res.at[rows_of(1 - core, half), :], result.at[:, mine], r_send, r_recv, sibling
    )
    back.start()
    result[:, mine] = res[rows_of(core, half), :]
    for w in weights:
        w.finish()
        w.sent()
    gather.sent()
    gather_go.sent()
    spread_o.sent()
    spread_n.sent()
    for j in range(3):
        keep_up(j + 3).wait()
        send_up(j).wait()
    keep_down().wait()
    send_down().wait()
    back.wait()


def back_kernel(
    width,
    y, dn2_h, go_h, x_own, scale_two, scale_one, gain_two, gain_one, masks, par, gates_t, m_h, br_h,
    b_h, p_h, u_h, r_h, i_h, h_h, q_h, n1_h, f_own, f_got, fd_own, fd_got,
    input_grad, feed_part, mix_part, small, gate_grad, f_sum, f_land, fd_sum, fd_land, g_own, g_got, gm_own, gm_got,
    sums, sums2, coef, m_n, br_n, b_s, p_s, u_s, r_s, i_s, h_s, g_s, dyf, dbp, dy, dn1, dq, du, dri, a_c, l_c, carry_s, own, held,
    qv, n1, f_a, f_b, fd_a, fd_b,
    c_sem, k_sem, l_send, l_recv, l2_send, l2_recv, g_send, g_recv, s_send, s_recv, r_send, r_recv,
    f_sem, f_send, f_recv, d_send, d_recv, d_own,
):
    row, z, core = place()
    block, seq = y.shape
    half = block // 2
    chan = b_s.shape[1]
    hc = chan // 2
    sibling = {"col": 2 * z + (1 - core)}
    greet(row, z, core, True, True)
    load_g = pltpu.make_async_copy(go_h.at[rows_of(z, block), :], g_s, c_sem.at[0])
    load_g.start()
    dn2 = dn1
    load_d = pltpu.make_async_copy(dn2_h, dn2, c_sem.at[5])
    load_d.start()
    load_m = pltpu.make_async_copy(m_h, m_n, c_sem.at[1])
    load_m.start()
    load_b = pltpu.make_async_copy(br_h, br_n, c_sem.at[2])
    load_b.start()
    load_q = pltpu.make_async_copy(q_h, qv, c_sem.at[3])
    load_n = pltpu.make_async_copy(n1_h, n1, c_sem.at[4])
    kept = (b_s, p_s, u_s, r_s, i_s, h_s)
    srcs = (b_h, p_h, u_h, r_h, i_h, h_h)

    def fetch(n, part):
        if kept[n] is p_s or kept[n] is h_s:
            at = pl.ds(pl.multiple_of(part * PART, 128), PART + 128)
        else:
            at = lanes(part)
        return pltpu.make_async_copy(srcs[n].at[:, at], kept[n].at[part % 2], k_sem.at[n, part % 2])

    def fetch_all(part):
        for n in range(len(kept)):
            fetch(n, part).start()

    fetch_all(PARTS - 1)
    load_q.start()
    load_n.start()
    du[:, seq : seq + 128] = jnp.zeros((chan, 128), F32)
    carry_s[...] = jnp.zeros(carry_s.shape, F32)
    small[...] = jnp.zeros(small.shape, F32)
    gate_grad[...] = jnp.zeros(gate_grad.shape, F32)

    sums[z] = jnp.zeros(sums.shape[1:], F32)

    load_d.wait()

    def inner(i):
        at = rows_of(i, 16)
        d, v = dn2[at, :], y[at, :]
        w = d * v
        c = w * gain_two[at, :]
        sums[z] += c[:8] + c[8:]
        w = w * scale_two[0:1, :]
        fold = w[:, 0:128]
        for j in range(1, seq // 128):
            fold = fold + w[:, j * 128 : (j + 1) * 128]
        feed_part[at, :] = fold

    blocks(block // 16, inner)
    share_line(sums, l_send, l_recv, z, core)
    load_g.wait()
    total = jnp.sum(jnp.sum(sums[...], axis=0), axis=0, keepdims=True)
    s2 = scale_two[0:1, :]
    coef[0:1, :] = s2 * s2 * s2 * (total / width)

    def outer(i):
        at = rows_of(i, 16)
        v = g_s[at, :].astype(F32) + (scale_two[0:1, :] * (gain_two[at, :] * dn2[at, :]) - y[at, :] * coef[0:1, :])
        dy[at, :] = v
        dyf[pl.ds(pl.multiple_of(z * block + i * 16, 16), 16), :] = v.astype(BF16)

    blocks(block // 16, outer)
    gather = Gather(dyf, g_send, g_recv, z, core, block, back=True)
    spread = Spread(own, held, s_send, s_recv, z, core)
    gather.open()
    load_m.wait()
    load_b.wait()
    final = lax.broadcasted_iota(jnp.int32, (64, PART), 1) == PART - 1

    f_arrays = ((f_own, f_got, f_a, f_b, f_sum, f_land), (fd_own, fd_got, fd_a, fd_b, fd_sum, fd_land))

    def f_loads(d):
        pulls = []
        for n, (ours, theirs, a, b, _, _) in enumerate(f_arrays):
            if n == 0:
                piece = (rows_of(row ^ d, block), slice(None))
            else:
                piece = (slice(None), pl.ds(pl.multiple_of((row ^ d) * block, 128), block))
            pulls.append(pltpu.make_async_copy(ours.at[piece], a.at[d], f_sem.at[n, 0]))
            pulls.append(pltpu.make_async_copy(theirs.at[piece], b, f_sem.at[n, 1]))
        return pulls

    def f_out(d):
        outs = []
        for n, (_, _, a, _, kept_at, land) in enumerate(f_arrays):
            if d == 0:
                outs.append(pltpu.make_async_copy(a.at[0], kept_at, f_send.at[n, 0]))
            else:
                outs.append(
                    remote(a.at[d], land.at[d - 1], f_send.at[n, d], f_recv.at[n, d], {"row": row ^ d})
                )
        return outs

    def f_part(d):
        for pull in f_loads(d):
            pull.wait()
        for _, _, a, b, _, _ in f_arrays:

            def add(i):
                at = rows_of(i, 16)
                a[d, at, :] = (a[d, at, :].astype(F32) + b[at, :].astype(F32)).astype(BF16)

            blocks(b.shape[0] // 16, add)
        for out in f_out(d):
            out.start()
        if d > 0:
            for pull in f_loads(d - 1):
                pull.start()

    def f_step(t):
        for d in range(PARTS):
            pl.when(t == PARTS - 1 - d)(functools.partial(f_part, d))

    for pull in f_loads(PARTS - 1):
        pull.start()

    def fold2(v):
        return v[:, 0:128] + v[:, 128:256]

    def work(t):
        k = PARTS - 1 - t
        here = lanes(k)
        wide = pl.ds(pl.multiple_of(k * PART, 128), PART + 128)
        slot = k % 2
        for n in range(len(kept)):
            fetch(n, k).wait()

        @pl.when(k > 0)
        def _():
            fetch_all(k - 1)

        dq[...] = dot(m_n[...], dyf[:, here])

        def before(i):
            ch = rows_of(i, 64)
            c = i // (hc // 64)
            low = pl.ds(pl.multiple_of(c * hc + i * 64, 64), 64)
            pr = par[ch, :]
            d = dq[ch, :]
            act, slope = gelu_parts(b_s[slot, ch, :])
            dbp[low, here] = (d * h_s[slot, ch, :][:, 128:] * slope).astype(BF16)
            l_c[ch, :] = d * act
            a_c[ch, :] = jnp.exp(-(r_s[slot, ch, :] * pr[:, 7:8]))

        blocks(chan // 64, before)
        gather.middle(t)

        def recur(i):
            ch = rows_of(i, 64)
            start = masks[0:1, here] > 0.5
            a, lam = jnp.where(start, 0.0, a_c[ch, :]), l_c[ch, :]
            lam = lam + jnp.where(final, carry_s[ch, :][:, 0:1], 0.0)
            w = jnp.where(final, 0.0, pltpu.roll(a, PART - 1, 1))
            shift = 1
            while shift < PART:
                lam = lam + w * pltpu.roll(lam, PART - shift, 1)
                if shift * 2 < PART:
                    w = w * pltpu.roll(w, PART - shift, 1)
                shift *= 2
            carry_s[ch, :] = jnp.broadcast_to((a * lam)[:, 0:1], (64, 128))
            l_c[ch, :] = lam

        blocks(chan // 64, recur)
        f_step(t)
        gather.later(t)

        def after(i):
            ch = rows_of(i, 32)
            pr = par[ch, :]
            start = masks[0:1, here] > 0.5
            lam, a0 = l_c[ch, :], a_c[ch, :]
            earlier = pltpu.roll(h_s[slot, ch, :], 1, 1)[:, 128:]
            r, gate, u = r_s[slot, ch, :], i_s[slot, ch, :], u_s[slot, ch, :]
            m0 = jnp.sqrt(1.0 - a0 * a0 + FLOOR)
            m = jnp.where(start, 1.0, m0)
            lm = lam * m
            lu = lam * u
            du[ch, here] = lm * gate
            da = jnp.where(start, 0.0, lam * earlier - (lu * gate) * (a0 / m0)) * a0
            dr = da * (-pr[:, 7:8]) * (r * (1.0 - r))
            di = lu * m * (gate * (1.0 - gate))
            g, o = i // 8, (i % 8) * 32
            dri[pl.ds(pl.multiple_of(g * 512 + o, 32), 32), :] = dr.astype(BF16)
            dri[pl.ds(pl.multiple_of(g * 512 + 256 + o, 32), 32), :] = di.astype(BF16)
            small[5, ch, :] += fold2(dr)
            small[6, ch, :] += fold2(di)
            small[7, ch, :] += fold2(da * r)

        blocks(chan // 32, after)
        for g in range(chan // 256):
            at = slice(g * 256, (g + 1) * 256)
            dd = dri[g * 512 : (g + 1) * 512, :]
            du[at, here] += dot(gates_t[g], dd)
            gate_grad[g] += dot_nt(u_s[slot, at, :].astype(BF16), dd)

        def conv(i):
            ch = rows_of(i, 32)
            c = i // (hc // 32)
            low = pl.ds(pl.multiple_of((c + 1) * hc + i * 32, 32), 32)
            pr = par[ch, :]
            follow = du[ch, wide]
            window = p_s[slot, ch, :]
            d = follow[:, :PART]
            dp = pr[:, 0:1] * d
            small[4, ch, :] += fold2(d)
            small[0, ch, :] += fold2(d * window[:, 128:])
            for lag in (1, 2, 3):
                kd = follow * masks[lag : lag + 1, wide]
                dp = dp + pr[:, lag : lag + 1] * pltpu.roll(kd, PART + 128 - lag, 1)[:, :PART]
                small[lag, ch, :] += fold2(kd[:, :PART] * pltpu.roll(window, lag, 1)[:, 128:])
            dbp[low, here] = dp.astype(BF16)

        blocks(chan // 32, conv)
        dk = dbp[:, here]
        for s in range(LINE):
            own[t, s] = dot(br_n[s * block : (s + 1) * block, :], dk)

    def finish(t, total):
        k = PARTS - 1 - t

        def add(i):
            at = pl.multiple_of(i * 16, 16)
            dn1[pl.ds(at, 16), lanes(k)] = total(at, 16)

        blocks(block // 16, add)

    def step(t, carry):
        gather.arrive(2, t)
        work(t)
        spread.serve(t, finish)
        return carry

    lax.fori_loop(0, PARTS, step, 0)
    load_q.wait()
    load_n.wait()

    lru = hc

    def cols_of(side):
        return pl.ds(pl.multiple_of(side * 2 * lru, 128), 2 * lru)

    def send_br():
        return remote(br_n.at[:, cols_of(1 - core)], g_got, d_send.at[0], d_recv.at[0], sibling)

    def keep_br():
        return pltpu.make_async_copy(br_n.at[:, cols_of(core)], g_own, d_own.at[0])

    def send_m():
        return remote(m_n.at[rows_of(1 - core, lru), :], gm_got, d_send.at[1], d_recv.at[1], sibling)

    def keep_m():
        return pltpu.make_async_copy(m_n.at[rows_of(core, lru), :], gm_own, d_own.at[1])

    def grad_br(side):
        br_n[:, cols_of(side)] = dot_nt(n1[...], dbp[rows_of(side, 2 * lru), :]).astype(BF16)

    def drain(i, carry):
        t = PARTS + i

        @pl.when(i == 0)
        def _():
            grad_br(1 - core)
            send_br().start()

        @pl.when(i == 1)
        def _():
            grad_br(core)
            keep_br().start()

        @pl.when(i == 2)
        def _():
            m_n[...] = dot_nt(qv[...], dyf[...]).astype(BF16)
            send_m().start()
            keep_m().start()

        spread.serve(t, finish)
        return carry

    lax.fori_loop(0, LINE - 1, drain, 0)

    sums2[z] = jnp.zeros(sums2.shape[1:], F32)

    def inner_one(i):
        at = rows_of(i, 16)
        w = dn1[at, :] * x_own[at, :].astype(F32)
        c = w * gain_one[at, :]
        sums2[z] += c[:8] + c[8:]
        w = w * scale_one[0:1, :]
        fold = w[:, 0:128]
        for j in range(1, seq // 128):
            fold = fold + w[:, j * 128 : (j + 1) * 128]
        mix_part[at, :] = fold

    blocks(block // 16, inner_one)
    share_line(sums2, l2_send, l2_recv, z, core)
    total = jnp.sum(jnp.sum(sums2[...], axis=0), axis=0, keepdims=True)
    s1 = scale_one[0:1, :]
    coef[0:1, :] = s1 * s1 * s1 * (total / width)

    def last(i):
        at = rows_of(i, 16)
        v = dy[at, :] + (
            scale_one[0:1, :] * (gain_one[at, :] * dn1[at, :]) - x_own[at, :].astype(F32) * coef[0:1, :]
        )
        dy[at, :] = v

    blocks(block // 16, last)
    mine = pl.ds(pl.multiple_of(core * seq, seq), seq)
    back = remote(dy.at[rows_of(1 - core, half), :], input_grad.at[:, mine], r_send, r_recv, sibling)
    back.start()
    input_grad[:, mine] = dy[rows_of(core, half), :]
    gather.sent()
    spread.sent()

    for d in range(PARTS):
        for out in f_out(d):
            out.wait()
    keep_br().wait()
    keep_m().wait()
    send_br().wait()
    send_m().wait()
    back.wait()


def sum_kernel(
    g_own, g_got, gm_own, gm_got, f_sum, f_land, fd_sum, fd_land, tiny,
    s_b, s_r, s_m, s_g, s_u, s_d, tiny_out,
    own, land, m_own, m_land, tiny_in, tiny_all,
    t_send, t_recv, a_send, a_recv, m_send, m_recv, b_send, b_recv,
):
    row, z, core = place()
    sibling = {"col": 2 * z + (1 - core)}
    lru, block = s_m.shape
    ff = s_d.shape[0]
    greet(row, z, core, True, False)
    swap = remote(tiny.at[1 - core], tiny_in, t_send, t_recv, sibling)
    swap.start()
    far = (1, 2, 3)

    def add(i):
        at = rows_of(i, 32)
        own[at, :] = (g_own[at, :].astype(F32) + g_got[at, :].astype(F32)).astype(BF16)

    blocks(own.shape[0] // 32, add)
    to_row = [
        remote(own.at[rows_of(row ^ d, block), :], land.at[d - 1], a_send.at[d - 1], a_recv.at[d - 1], {"row": row ^ d})
        for d in far
    ]
    for copy in to_row:
        copy.start()

    def add_m(i):
        at = rows_of(i, 32)
        m_own[at, :] = (gm_own[at, :].astype(F32) + gm_got[at, :].astype(F32)).astype(BF16)

    blocks(lru // 32, add_m)

    def spot(r):
        return pl.ds(pl.multiple_of(r * block, 128), block)

    m_row = [
        remote(m_own.at[:, spot(row ^ d)], m_land.at[d - 1], m_send.at[d - 1], m_recv.at[d - 1], {"row": row ^ d})
        for d in far
    ]
    for copy in m_row:
        copy.start()
    swap.wait()
    tiny_all[0] = tiny[core] + tiny_in[...]
    tiny_row = [
        remote(tiny_all.at[0], tiny_all.at[d], b_send.at[d - 1], b_recv.at[d - 1], {"row": row ^ d})
        for d in far
    ]
    for copy in tiny_row:
        copy.start()

    def four(first, others, at):
        return first[at, :].astype(F32) + others[0, at, :].astype(F32) + (
            others[1, at, :].astype(F32) + others[2, at, :].astype(F32)
        )

    def put_gu(i):
        at = rows_of(i, 32)
        v = four(f_sum, f_land, at)
        s_g[at, :] = v[:, :ff]
        s_u[at, :] = v[:, ff:]

    blocks(block // 32, put_gu)

    def put_d(i):
        at = rows_of(i, 32)
        s_d[at, :] = four(fd_sum, fd_land, at)

    blocks(ff // 32, put_d)
    for copy in tiny_row:
        copy.wait()
    left, right = tiny_all[row % 2], tiny_all[1 - row % 2]
    up, down = tiny_all[2 + row % 2], tiny_all[3 - row % 2]
    tiny_out[...] = (left + right) + (up + down)
    for copy in to_row:
        copy.wait()
    mine = own.at[rows_of(row, block), :]

    def put_br(i):
        at = rows_of(i, 32)
        v = four(mine, land, at)
        s_b[at, :] = v[:, :lru]
        s_r[at, :] = v[:, lru:]

    blocks(block // 32, put_br)
    for copy in m_row:
        copy.wait()
    mine_m = m_own.at[:, spot(row)]

    def put_m(i):
        at = rows_of(i, 32)
        s_m[at, :] = four(mine_m, m_land, at)

    blocks(lru // 32, put_m)


ANY = pl.BlockSpec(memory_space=pl.ANY)
VM = pl.BlockSpec(memory_space=pltpu.VMEM)
DMA = pltpu.SemaphoreType.DMA
ROOM = 62 * 1024 * 1024


def shape(dims, kind):
    return jax.ShapeDtypeStruct(dims, kind)


def call(kernel, ins, outs, scratch, ident, name, flops):
    return pl.pallas_call(
        kernel,
        out_shape=[o[0] for o in outs],
        in_specs=ins,
        out_specs=[o[1] for o in outs],
        scratch_shapes=scratch,
        name=name,
        compiler_params=pltpu.CompilerParams(
            collective_id=ident, has_side_effects=True, vmem_limit_bytes=ROOM
        ),
        cost_estimate=pl.CostEstimate(flops=flops, bytes_accessed=40000000, transcendentals=0),
    )


PAIRS = [[0, 1], [2, 3], [4, 5], [6, 7]]


def diagonal(w, size):
    per = size // w.shape[1]
    w = w.reshape(-1, per, w.shape[1], w.shape[2])
    eye = jnp.eye(per, dtype=w.dtype)
    full = w[:, :, :, None, :] * eye[None, :, None, :, None]
    return full.reshape(-1, size, size)


def fast_body(
    inputs, segments, mix_gain, branch_weight, recur_weight, kernel, offsets, retain_weight, retain_bias,
    admit_weight, admit_bias, lambdas, merge_weight, feed_gain, gate_weight, up_weight, down_weight, cotangent,
):
    half, tokens = inputs.shape
    block, seq, width = 2 * half, tokens // 2, D
    lru, heads = branch_weight.shape[1], retain_weight.shape[0]
    chan = 2 * lru
    ff = gate_weight.shape[1]
    hid = 2 * ff
    rows = branch_weight.shape[0]
    cols = merge_weight.shape[1]
    core = lax.axis_index("col") % 2

    parts = (mix_gain, feed_gain, kernel[0], kernel[1], kernel[2], kernel[3], offsets, retain_bias, admit_bias, lambdas)
    parts = parts + (retain_weight.reshape(-1), admit_weight.reshape(-1))
    both = lax.all_gather(jnp.concatenate(parts), "col", axis=0, axis_index_groups=PAIRS)
    whole, at = [], 0
    for part in parts:
        whole.append(both[:, at : at + part.shape[0]].reshape(-1))
        at += part.shape[0]
    gain_one, gain_two = whole[0][:, None], whole[1][:, None]
    lam = whole[9]
    rate = 8.0 * jax.nn.softplus(-lam)
    par = jnp.stack(whole[2:6] + whole[6:9] + [rate] + [jnp.zeros_like(lam)] * 8, axis=1)
    retain = diagonal(whole[10].reshape(-1, 64, 64), 256)
    admit = diagonal(whole[11].reshape(-1, 64, 64), 256)
    gates = jnp.concatenate([retain, admit], axis=2)
    gates_hi = gates.astype(BF16)
    gates_lo = (gates - gates_hi.astype(F32)).astype(BF16)
    flip = lambda w: jnp.swapaxes(w, 1, 2)

    segs = lax.dynamic_slice(segments, (core * seq,), (seq,))
    masks = [jnp.concatenate([jnp.ones((1,), bool), segs[1:] != segs[:-1]])]
    for lag in (1, 2, 3):
        masks.append(jnp.concatenate([jnp.zeros((lag,), bool), segs[lag:] == segs[:-lag]]))
    masks = jnp.pad(jnp.stack(masks).astype(F32), ((0, 4), (0, 128)))

    br_s = jnp.concatenate([branch_weight, recur_weight], axis=1).T
    m_s = merge_weight.T
    gu_s = jnp.concatenate([gate_weight, up_weight], axis=1).T

    f_tok = lambda n, kind=F32: shape((n, seq), kind)
    padded = (shape((chan, 128 + seq), F32), ANY)
    state = [(f_tok(chan), ANY), padded, *[(f_tok(chan), ANY)] * 3, padded]
    line = [DMA((3,)), DMA((3,))]
    steps = [DMA((2, 3, PARTS)), DMA((2, 3, PARTS))]
    sums = [DMA((2, PARTS, LINE)), DMA((2, PARTS, LINE))]
    held = pltpu.VMEM((PARTS, LINE + 1, block, PART), BF16)
    own = pltpu.VMEM((PARTS, LINE, block, PART), F32)
    tok = lambda n, kind=F32, lead=0: pltpu.VMEM((n, lead + seq), kind)

    y, n1, q, x_own, scale_one, _, _, b, p, u, r, i, h, gu, down = call(
        functools.partial(mix_kernel, width, EPS),
        [VM] * 6 + [ANY] * 4,
        [(f_tok(block), VM), (f_tok(width, BF16), VM), (f_tok(chan, BF16), VM), (f_tok(block, BF16), VM), (f_tok(8), VM),
         (shape((2 * chan, width), BF16), VM), (shape((width, chan), BF16), VM)] + state
        + [(shape((2 * hid, width), BF16), ANY), (shape((hid, width), BF16), ANY)],
        [pltpu.VMEM((LINE, 8, seq), F32), tok(chan), tok(chan, F32, 128), tok(chan), tok(chan), tok(chan), tok(chan, F32, 128),
         pltpu.VMEM((chan, PART), F32), pltpu.VMEM((chan, PART), BF16), pltpu.VMEM((chan, PART), BF16), own, held, DMA, DMA]
        + line + steps + sums + [DMA((4, 7)), DMA((4, 7)), DMA((4,)), DMA((6, PARTS + 1))],
        0, "mix_forward", 5 * 10**9,
    )(inputs, gain_one, masks, par, flip(gates_hi), flip(gates_lo), br_s, m_s, gu_s, down_weight)

    br_t = jnp.concatenate([branch_weight, recur_weight], axis=1)
    grad_gu, grad_d = (shape((width, 2 * ff), BF16), ANY), (shape((ff, width), BF16), ANY)
    grad_br, grad_m = (shape((width, 2 * lru), BF16), ANY), (shape((lru, width), BF16), ANY)
    own_low = pltpu.VMEM((PARTS, LINE, block, PART), BF16)
    result, n2, go, scale_two, dn2, f_own, f_got, fd_own, fd_got, br_n, m_n = call(
        functools.partial(feed_kernel, width, EPS),
        [VM] * 3 + [ANY] * 4,
        [(shape((half, tokens), BF16), VM), (f_tok(width, BF16), VM), (f_tok(width, BF16), VM), (f_tok(8), VM), (f_tok(block), VM),
         grad_gu, grad_gu, grad_d, grad_d, (shape((width, 2 * chan), BF16), ANY), (shape((chan, width), BF16), ANY)],
        [pltpu.VMEM((LINE, 8, seq), F32), pltpu.VMEM((2 * hid, width), BF16), pltpu.VMEM((width, 2 * hid), BF16),
         pltpu.VMEM((hid, width), BF16), pltpu.VMEM((width, hid), BF16), pltpu.VMEM((hid, PART), F32),
         pltpu.VMEM((ff, PART), F32), tok(hid, BF16), tok(2 * hid, BF16),
         tok(block, BF16), own_low, own, held, held, DMA((2,)), DMA, DMA]
        + line + steps + steps + sums + sums + [DMA, DMA, DMA((2, 7)), DMA((2, 7)), DMA((2,)), DMA((4,)), DMA((4,)), DMA((4,))],
        1, "feed", 44 * 10**9,
    )(y, gain_two, cotangent, gu, down, br_t, merge_weight)

    pair = lambda lead=0: pltpu.VMEM((2, chan, lead + PART), F32)
    input_grad, feed_part, mix_part, small, gate_grad, f_sum, f_land, fd_sum, fd_land, g_own, g_got, gm_own, gm_got = call(
        functools.partial(back_kernel, width),
        [VM] + [ANY] * 2 + [VM] * 8 + [ANY] * 14,
        [(shape((half, tokens), F32), VM), (shape((block, 128), F32), VM),
         (shape((block, 128), F32), VM), (shape((8, chan, 128), F32), VM), (shape((chan // 256, 256, 512), F32), VM),
         (shape((cols, 2 * ff), BF16), ANY), (shape((3, cols, 2 * ff), BF16), ANY), (shape((ff, cols), BF16), ANY),
         (shape((3, ff, cols), BF16), ANY), grad_br, grad_br, grad_m, grad_m],
        [pltpu.VMEM((LINE, 8, seq), F32), pltpu.VMEM((LINE, 8, seq), F32), pltpu.VMEM((8, seq), F32),
         pltpu.VMEM((chan, width), BF16), pltpu.VMEM((width, 2 * chan), BF16),
         pair(), pair(128), pair(), pair(), pair(), pair(128), tok(block, BF16), tok(width, BF16), tok(2 * chan, BF16),
         tok(block), tok(block), pltpu.VMEM((chan, PART), F32), tok(chan, F32, 128), pltpu.VMEM((2 * chan, PART), BF16),
         pltpu.VMEM((chan, PART), F32), pltpu.VMEM((chan, PART), F32), pltpu.VMEM((chan, 128), F32), own, held,
         tok(chan, BF16), tok(width, BF16), pltpu.VMEM((4, cols, 2 * ff), BF16), pltpu.VMEM((cols, 2 * ff), BF16),
         pltpu.VMEM((4, ff, cols), BF16), pltpu.VMEM((ff, cols), BF16),
         DMA((6,)), DMA((6, 2))] + line + line + steps + sums
        + [DMA, DMA, DMA((2, 2)), DMA((2, PARTS)), DMA((2, PARTS)), DMA((2,)), DMA((2,)), DMA((2,))],
        2, "mix_backward", 10 * 10**9,
    )(y, dn2, go, x_own, scale_two, scale_one, gain_two, gain_one, masks, par, gates_hi, m_n, br_n, b, p, u, r, i, h,
      q, n1, f_own, f_got, fd_own, fd_got)

    small = jnp.sum(small, axis=2)
    small = jnp.concatenate([small[:7], small[7:] * (8.0 * jax.nn.sigmoid(-lam))[None]])
    gains = jnp.stack([jnp.sum(mix_part, axis=1), jnp.sum(feed_part, axis=1)])
    blocked = gate_grad.reshape(-1, 4, 64, 2, 4, 64)
    gate_blocks = jnp.stack([blocked[:, e, :, :, e, :] for e in range(4)], axis=1)
    tiny = jnp.concatenate(
        [
            jnp.swapaxes(small.reshape(8, 2, lru), 0, 1).reshape(2, -1),
            jnp.swapaxes(gains.reshape(2, 2, half), 0, 1).reshape(2, -1),
            gate_blocks.reshape(2, -1),
        ],
        axis=1,
    )
    size = tiny.shape[1]
    deep = -(-size // 1024) * 8
    tiny = jnp.pad(tiny, ((0, 0), (0, deep * 128 - size))).reshape(2, deep, 128)

    s_b, s_r, s_m, s_g, s_u, s_d, tiny = call(
        sum_kernel,
        [VM] * 9,
        [(shape((cols, lru), F32), VM)] * 2 + [(shape((lru, cols), F32), VM)] + [(shape((cols, ff), F32), VM)] * 2
        + [(shape((ff, cols), F32), VM)] + [(shape((deep, 128), F32), VM)],
        [pltpu.VMEM((width, 2 * lru), BF16), pltpu.VMEM((3, cols, 2 * lru), BF16), pltpu.VMEM((lru, width), BF16),
         pltpu.VMEM((3, lru, cols), BF16), pltpu.VMEM((deep, 128), F32), pltpu.VMEM((4, deep, 128), F32), DMA, DMA] + line * 3,
        3, "gradient_sums", 10**8,
    )(g_own, g_got, gm_own, gm_got, f_sum, f_land, fd_sum, fd_land, tiny)
    tiny = tiny.reshape(-1)
    small = tiny[: 8 * lru].reshape(8, lru)
    gains = tiny[8 * lru : 8 * lru + 2 * half].reshape(2, half)
    gate_blocks = tiny[8 * lru + 2 * half : size].reshape(heads, 64, 2, 64)
    return (
        result,
        input_grad,
        gains[0],
        s_b,
        s_r,
        small[0:4],
        small[4],
        gate_blocks[:, :, 0],
        small[5],
        gate_blocks[:, :, 1],
        small[6],
        small[7],
        s_m,
        gains[1],
        s_g,
        s_u,
        s_d,
    )


def suits(mesh, args):
    return (
        dict(mesh.shape) == {"row": 4, "col": 8}
        and args[0].shape == (D, 8 * SEQ)
        and args[3].shape == (D, 2048)
        and args[14].shape == (D, 4608)
        and args[7].shape == (32, 64, 64)
    )


def solution(mesh):
    in_specs = (
        P("col", "row"),
        P("row"),
        P("col"),
        P("row", "col"),
        P("row", "col"),
        P(None, "col"),
        P("col"),
        P("col", None, None),
        P("col"),
        P("col", None, None),
        P("col"),
        P("col"),
        P("col", "row"),
        P("col"),
        P("row", "col"),
        P("row", "col"),
        P("col", "row"),
        P("col", "row"),
    )
    out_specs = (
        P("col", "row"),
        P("col", "row"),
        P("col"),
        P("row", "col"),
        P("row", "col"),
        P(None, "col"),
        P("col"),
        P("col", None, None),
        P("col"),
        P("col", None, None),
        P("col"),
        P("col"),
        P("col", "row"),
        P("col"),
        P("row", "col"),
        P("row", "col"),
        P("col", "row"),
    )
    def run(*args):
        chosen = fast_body if suits(mesh, args) else body
        return jax.shard_map(
            chosen, mesh=mesh, in_specs=in_specs, out_specs=out_specs, check_vma=False
        )(*args)

    return run
```

```python
import functools

import jax
import jax.numpy as jnp
from jax import lax
from jax.experimental import pallas as pl
from jax.experimental.pallas import tpu as pltpu
from jax.sharding import PartitionSpec as P

D = 1536
SEQ = 1024
MICRO = 2


HIGH = lax.Precision.HIGHEST
EPS = 1e-06
POWER = 8.0
FLOOR = 0.01


def combine(earlier, later):
    first_a, first_b = earlier
    second_a, second_b = later
    return (first_a * second_a, second_a * first_b + second_b)


def mixer(
    branch_pre,
    lru_pre,
    segs,
    kernel,
    offsets,
    retain_weight,
    retain_bias,
    admit_weight,
    admit_bias,
    lambdas,
):
    length = lru_pre.shape[0]
    channels = lru_pre.shape[1]
    conv = offsets + kernel[0] * lru_pre
    for lag in range(1, kernel.shape[0]):
        shifted = jnp.concatenate(
            [jnp.zeros((lag, channels), lru_pre.dtype), lru_pre[:-lag]], axis=0
        )
        prior = jnp.concatenate([jnp.full((lag,), -1, jnp.int32), segs[:-lag]])
        keep = (prior == segs).astype(lru_pre.dtype)
        conv = conv + kernel[lag] * shifted * keep[:, None]
    heads = retain_weight.shape[0]
    blocks = conv.reshape(length, heads, channels // heads)
    retain = jax.nn.sigmoid(
        jnp.einsum("thi,hij->thj", blocks, retain_weight, precision=HIGH).reshape(length, channels)
        + retain_bias
    )
    admit = jax.nn.sigmoid(
        jnp.einsum("thi,hij->thj", blocks, admit_weight, precision=HIGH).reshape(length, channels)
        + admit_bias
    )
    decay = jnp.exp(-POWER * retain * jax.nn.softplus(-lambdas))
    factor = jnp.sqrt(1.0 - decay * decay + FLOOR)
    starts = jnp.concatenate([jnp.ones((1,), bool), segs[1:] != segs[:-1]])
    decay = jnp.where(starts[:, None], 0.0, decay)
    factor = jnp.where(starts[:, None], 1.0, factor)
    _, state = lax.associative_scan(combine, (decay, factor * admit * conv), axis=0)
    return jax.nn.gelu(branch_pre) * state


def geglu(gate, upper):
    return jax.nn.gelu(gate) * upper


def contract_rows(left, right):
    return lax.dot_general(
        left, right, (((0,), (0,)), ((), ())), preferred_element_type=jnp.float32
    )


def contract_cols(left, right):
    return lax.dot_general(
        left, right, (((1,), (1,)), ((), ())), preferred_element_type=jnp.float32
    )


def contract_cross(left, right):
    return lax.dot_general(
        left, right, (((0,), (1,)), ((), ())), preferred_element_type=jnp.float32
    )


def norm_forward(resid, gain):
    total = lax.psum(jnp.sum(resid * resid, axis=0), "col")
    scale = lax.rsqrt(total / D + EPS)[None, :]
    return (scale, (resid * scale * gain[:, None]).astype(jnp.bfloat16))


def norm_backward(resid, scale, gain, grad_normed):
    weighted = grad_normed * gain[:, None]
    total = lax.psum(jnp.sum(weighted * resid, axis=0), "col")
    grad_resid = scale * weighted - resid * (scale * scale * scale) * (total / D)[None, :]
    grad_gain = jnp.sum(grad_normed * resid * scale, axis=1)
    return (grad_resid, grad_gain)


def gather_features(normed):
    return lax.all_gather(normed, "col", axis=0, tiled=True)


def gather_cotangent(grad):
    return lax.all_gather(grad, "col", axis=0, tiled=True)


def spread_sum(term):
    return lax.psum_scatter(
        term.astype(jnp.bfloat16), "col", scatter_dimension=0, tiled=True
    ).astype(jnp.float32)


def back_sum(term):
    return spread_sum(term)


def merge_term(whole_merge, mixed_low):
    return spread_sum(contract_cross(whole_merge, mixed_low))


def weight_grads(normed, grad_joined):
    return jnp.dot(
        normed,
        grad_joined,
        preferred_element_type=jnp.float32,
    )


def row_sum(total, axis):
    return lax.psum_scatter(
        total.astype(jnp.bfloat16), "row", scatter_dimension=axis, tiled=True
    ).astype(jnp.float32)


def body(
    inputs,
    segments,
    mix_gain,
    branch_weight,
    recur_weight,
    kernel,
    offsets,
    retain_weight,
    retain_bias,
    admit_weight,
    admit_bias,
    lambdas,
    merge_weight,
    feed_gain,
    gate_weight,
    up_weight,
    down_weight,
    cotangent,
):
    lru_cols = branch_weight.shape[1]
    feed_cols = gate_weight.shape[1]
    mixer_params = (kernel, offsets, retain_weight, retain_bias, admit_weight, admit_bias, lambdas)
    acc_branch = jnp.zeros((D, lru_cols), jnp.float32)
    acc_recur = jnp.zeros((D, lru_cols), jnp.float32)
    acc_gate = jnp.zeros((D, feed_cols), jnp.float32)
    acc_up = jnp.zeros((D, feed_cols), jnp.float32)
    acc_merge = jnp.zeros((lru_cols, D), jnp.float32)
    acc_down = jnp.zeros((feed_cols, D), jnp.float32)
    acc_small = tuple((jnp.zeros_like(p) for p in mixer_params))
    acc_mix = jnp.zeros_like(mix_gain)
    acc_feed = jnp.zeros_like(feed_gain)
    outputs = []
    in_grads = []
    for batch in range(MICRO):
        lower = batch * SEQ
        resid_in = inputs[:, lower : lower + SEQ].astype(jnp.float32)
        grad_out = cotangent[:, lower : lower + SEQ].astype(jnp.float32)
        segs = segments[lower : lower + SEQ]
        whole_branch, whole_recur, whole_gate, whole_up = (
            lax.all_gather(branch_weight, "row", axis=0, tiled=True),
            lax.all_gather(recur_weight, "row", axis=0, tiled=True),
            lax.all_gather(gate_weight, "row", axis=0, tiled=True),
            lax.all_gather(up_weight, "row", axis=0, tiled=True),
        )
        whole_merge, whole_down = (
            lax.all_gather(merge_weight, "row", axis=1, tiled=True),
            lax.all_gather(down_weight, "row", axis=1, tiled=True),
        )
        scale_one, normed_one = norm_forward(resid_in, mix_gain)
        full_one = gather_features(normed_one)
        branch_pre = contract_rows(full_one, whole_branch)
        lru_pre = contract_rows(full_one, whole_recur)

        def local_mixer(bpre, lpre, kern, offs, rweight, rbias, aweight, abias, lams):
            return mixer(bpre, lpre, segs, kern, offs, rweight, rbias, aweight, abias, lams)

        mixed, mixer_pull = jax.vjp(local_mixer, branch_pre, lru_pre, *mixer_params)
        mixed_low = mixed.astype(jnp.bfloat16)
        resid_mid = resid_in + merge_term(whole_merge, mixed_low)
        scale_two, normed_two = norm_forward(resid_mid, feed_gain)
        full_two = gather_features(normed_two)
        gate = contract_rows(full_two, whole_gate)
        upper = contract_rows(full_two, whole_up)
        hidden, geglu_pull = jax.vjp(geglu, gate, upper)
        hidden_low = hidden.astype(jnp.bfloat16)
        result = resid_mid + spread_sum(contract_cross(whole_down, hidden_low))
        outputs.append(result.astype(jnp.bfloat16))
        grad_full = gather_cotangent(grad_out.astype(jnp.bfloat16))
        acc_down = acc_down + contract_cross(hidden_low, grad_full)
        grad_gate, grad_upper = geglu_pull(contract_cross(grad_full, whole_down))
        grad_gate = grad_gate.astype(jnp.bfloat16)
        grad_upper = grad_upper.astype(jnp.bfloat16)
        feed_joined = weight_grads(full_two, jnp.concatenate([grad_gate, grad_upper], axis=1))
        acc_gate = acc_gate + feed_joined[:, :feed_cols]
        acc_up = acc_up + feed_joined[:, feed_cols:]
        grad_normed_two = back_sum(
            contract_cols(whole_gate, grad_gate) + contract_cols(whole_up, grad_upper)
        )
        grad_mid_norm, feed_part = norm_backward(resid_mid, scale_two, feed_gain, grad_normed_two)
        acc_feed = acc_feed + feed_part
        grad_mid = grad_out + grad_mid_norm
        grad_mid_full = gather_cotangent(grad_mid.astype(jnp.bfloat16))
        acc_merge = acc_merge + contract_cross(mixed_low, grad_mid_full)
        pulled = mixer_pull(contract_cross(grad_mid_full, whole_merge))
        grad_branch = pulled[0].astype(jnp.bfloat16)
        grad_lru = pulled[1].astype(jnp.bfloat16)
        acc_small = tuple((total + part for total, part in zip(acc_small, pulled[2:])))
        branch_joined = weight_grads(full_one, jnp.concatenate([grad_branch, grad_lru], axis=1))
        acc_branch = acc_branch + branch_joined[:, :lru_cols]
        acc_recur = acc_recur + branch_joined[:, lru_cols:]
        grad_normed_one = back_sum(
            contract_cols(whole_branch, grad_branch) + contract_cols(whole_recur, grad_lru)
        )
        grad_in_norm, mix_part = norm_backward(resid_in, scale_one, mix_gain, grad_normed_one)
        acc_mix = acc_mix + mix_part
        in_grads.append(grad_mid + grad_in_norm)
    sum_branch, sum_recur, sum_gate, sum_up = (
        row_sum(acc_branch, 0),
        row_sum(acc_recur, 0),
        row_sum(acc_gate, 0),
        row_sum(acc_up, 0),
    )
    sum_merge, sum_down = (
        row_sum(acc_merge, 1),
        row_sum(acc_down, 1),
    )
    summed = lax.psum(
        (
            acc_mix,
            acc_feed,
            acc_small[0],
            acc_small[1],
            acc_small[2],
            acc_small[3],
            acc_small[4],
            acc_small[5],
            acc_small[6],
        ),
        "row",
    )
    result_all = jnp.concatenate(outputs, axis=1)
    input_grad = jnp.concatenate(in_grads, axis=1)
    return (
        result_all,
        input_grad,
        summed[0],
        sum_branch,
        sum_recur,
        summed[2],
        summed[3],
        summed[4],
        summed[5],
        summed[6],
        summed[7],
        summed[8],
        sum_merge,
        summed[1],
        sum_gate,
        sum_up,
        sum_down,
    )


MESH = pl.DeviceIdType.MESH
F32 = jnp.float32
BF16 = jnp.bfloat16
LINE = 4
PART = 256
PARTS = 4
GELU_A = 0.7978845608028654
GELU_B = 0.044715


def place():
    row, col = lax.axis_index("row"), lax.axis_index("col")
    return row, col // 2, col % 2


def at_line(z, core):
    return {"col": 2 * z + core}


def lanes(part):
    return pl.ds(pl.multiple_of(part * PART, PART), PART)


def rows_of(index, size):
    return pl.ds(pl.multiple_of(index * size, 16), size)


def dot(a, b):
    return lax.dot_general(a, b, (((1,), (0,)), ((), ())), preferred_element_type=F32)


def dot_nt(a, b):
    return lax.dot_general(a, b, (((1,), (1,)), ((), ())), preferred_element_type=F32)


def greet(row, z, core, rows, line):
    barrier = pltpu.get_barrier_semaphore()
    peers = [{"col": 2 * z + (1 - core)}]
    if rows:
        peers += [{"row": row ^ d} for d in (1, 2, 3)]
    if line:
        peers += [at_line(z ^ d, core) for d in (1, 2, 3)]
    for peer in peers:
        pl.semaphore_signal(barrier, inc=1, device_id=peer, device_id_type=MESH)
    pl.semaphore_wait(barrier, len(peers))


def remote(src, dst, send, recv, peer):
    return pltpu.make_async_remote_copy(
        src_ref=src, dst_ref=dst, send_sem=send, recv_sem=recv, device_id=peer, device_id_type=MESH
    )


class Gather:
    def __init__(self, ref, send, recv, z, core, block, back=False):
        self.ref, self.sems, self.z, self.core = ref, (send, recv), z, core
        self.block, self.back = block, back

    def copy(self, way, hop, step, owner, incoming=False):
        part = PARTS - 1 - step if self.back else step
        piece = self.ref.at[rows_of(owner, self.block), lanes(part)]
        peer = at_line(self.z + (1 if (way == 0) != incoming else -1), self.core)
        return remote(piece, piece, self.sems[0].at[way, hop, step], self.sems[1].at[way, hop, step], peer)

    def each(self, hop, act, incoming):
        z = self.z
        if incoming:
            cases = ((0, z - 1 - hop >= 0, z - 1 - hop), (1, z + 1 + hop < LINE, z + 1 + hop))
        else:
            cases = (
                (0, (z >= hop) & (z < LINE - 1), z - hop),
                (1, (z + hop < LINE) & (z >= 1), z + hop),
            )
        for way, here, owner in cases:
            pl.when(here)(functools.partial(act, way, owner))

    def send(self, hop, step):
        self.each(hop, lambda way, owner: self.copy(way, hop, step, owner).start(), False)

    def arrive(self, hop, step):
        self.each(hop, lambda way, owner: self.copy(way, hop, step, owner, True).wait_recv(), True)

    def forward(self, hop, step):
        self.arrive(hop - 1, step)
        self.send(hop, step)

    def sent(self):
        def one(step, carry):
            for hop in range(LINE - 1):
                self.each(hop, lambda way, owner: self.copy(way, hop, step, owner).wait_send(), False)
            return carry

        lax.fori_loop(0, PARTS, one, 0)

    def open(self):
        self.send(0, 0)
        self.forward(1, 0)
        self.send(0, 1)
        self.forward(2, 0)

    def middle(self, step):
        @pl.when(step + 1 < PARTS)
        def _():
            self.forward(1, step + 1)

        @pl.when(step + 2 < PARTS)
        def _():
            self.send(0, step + 2)

    def later(self, step):
        @pl.when(step + 1 < PARTS)
        def _():
            self.forward(2, step + 1)


class Spread:
    def __init__(self, own, held, send, recv, z, core):
        self.own, self.held, self.sems, self.z, self.core = own, held, (send, recv), z, core

    def copy(self, way, step, hop):
        slot = hop if way == 0 else LINE - hop
        there = slot - 1 if way == 0 else slot + 1
        peer = at_line(self.z + (1 if way == 0 else -1), self.core)
        return remote(
            self.held.at[step, slot],
            self.held.at[step, there],
            self.sems[0].at[way, step, hop],
            self.sems[1].at[way, step, hop - 1],
            peer,
        )

    def landed(self, way, step, hop):
        slot = hop if way == 0 else LINE - hop
        piece = self.held.at[step, slot]
        peer = at_line(self.z + (-1 if way == 0 else 1), self.core)
        remote(piece, piece, self.sems[0].at[way, step, hop], self.sems[1].at[way, step, hop], peer).wait_recv()

    def push(self, way, step):
        z = self.z
        first = z == 0 if way == 0 else z == LINE - 1

        def one(i, carry):
            hop = LINE - 1 - i
            owner = z + hop if way == 0 else z - hop
            slot = hop if way == 0 else LINE - hop

            @pl.when((owner >= 0) & (owner < LINE))
            def _():
                @pl.when(first)
                def _():
                    self.held[step, slot] = self.own[step, owner].astype(BF16)

                @pl.when(jnp.logical_not(first))
                def _():
                    self.landed(way, step, hop)
                    total = self.own[step, owner].astype(F32) + self.held[step, slot].astype(F32)
                    self.held[step, slot] = total.astype(BF16)

                self.copy(way, step, hop).start()

            return carry

        lax.fori_loop(0, LINE - 1, one, 0)

    def serve(self, t, finish):
        z = self.z
        for way, late in ((0, z), (1, LINE - 1 - z)):
            step = t - late
            pl.when((step >= 0) & (step < PARTS))(functools.partial(self.push, way, step))
        step = t - (LINE - 1)

        @pl.when((step >= 0) & (step < PARTS))
        def _():
            @pl.when(z == 0)
            def _():
                self.landed(1, step, 0)
                finish(step, lambda a, n: self.mine(step, a, n) + self.got(step, LINE, a, n))

            @pl.when(z == LINE - 1)
            def _():
                self.landed(0, step, 0)
                finish(step, lambda a, n: self.mine(step, a, n) + self.got(step, 0, a, n))

            @pl.when((z > 0) & (z < LINE - 1))
            def _():
                self.landed(0, step, 0)
                self.landed(1, step, 0)
                finish(
                    step,
                    lambda a, n: self.mine(step, a, n) + (self.got(step, 0, a, n) + self.got(step, LINE, a, n)),
                )

    def mine(self, step, start, size):
        return self.own[step, self.z, pl.ds(start, size)].astype(F32)

    def got(self, step, slot, start, size):
        return self.held[step, slot, pl.ds(start, size)].astype(F32)

    def sent(self):
        z = self.z

        def one(step, carry):
            for way in (0, 1):
                for hop in range(1, LINE):
                    owner = z + hop if way == 0 else z - hop

                    @pl.when((owner >= 0) & (owner < LINE))
                    def _():
                        self.copy(way, step, hop).wait_send()

            return carry

        lax.fori_loop(0, PARTS, one, 0)


def share_line(ref, send, recv, z, core):
    copies = [
        remote(ref.at[z], ref.at[z], send.at[d - 1], recv.at[d - 1], at_line(z ^ d, core)) for d in (1, 2, 3)
    ]
    for copy in copies:
        copy.start()
    for d in (1, 2, 3):
        piece = ref.at[z ^ d]
        remote(piece, piece, send.at[d - 1], recv.at[d - 1], at_line(z ^ d, core)).wait_recv()
    for copy in copies:
        copy.wait_send()


class Weights:
    def __init__(self, src, dst, send, recv, own, row, z, core, turned):
        self.src, self.dst, self.send, self.recv, self.own = src, dst, send, recv, own
        self.row, self.core, self.turned = row, core, turned
        self.sibling = {"col": 2 * z + (1 - core)}

    def spot(self, row, core):
        down, right = (row, core) if self.turned else (core, row)
        rows, cols = self.src.shape
        return self.dst.at[rows_of(down, rows), pl.ds(pl.multiple_of(right * cols, 128), cols)]

    def to_row(self, d):
        return remote(
            self.src, self.spot(self.row, self.core), self.send.at[d], self.recv.at[d], {"row": self.row ^ d}
        )

    def to_sibling(self, d):
        if d == 0:
            return remote(
                self.src, self.spot(self.row, self.core), self.send.at[0], self.recv.at[0], self.sibling
            )
        piece = self.spot(self.row ^ d, self.core)
        return remote(piece, piece, self.send.at[3 + d], self.recv.at[3 + d], self.sibling)

    def local(self):
        return pltpu.make_async_copy(self.src, self.spot(self.row, self.core), self.own)

    def start(self):
        for d in (1, 2, 3):
            self.to_row(d).start()
        self.to_sibling(0).start()
        self.local().start()

    def forward(self):
        for d in (1, 2, 3):
            piece = self.spot(self.row ^ d, self.core)
            remote(piece, piece, self.send.at[d], self.recv.at[d], {"row": self.row ^ d}).wait_recv()
            self.to_sibling(d).start()

    def finish(self):
        self.local().wait()
        for d in (0, 1, 2, 3):
            piece = self.spot(self.row ^ d, 1 - self.core)
            sem = 0 if d == 0 else 3 + d
            remote(piece, piece, self.send.at[sem], self.recv.at[sem], self.sibling).wait_recv()

    def sent(self):
        for d in (1, 2, 3):
            self.to_row(d).wait_send()
            self.to_sibling(d).wait_send()
        self.to_sibling(0).wait_send()


def gelu_parts(b):
    t = jnp.tanh(GELU_A * (b + GELU_B * (b * b * b)))
    half = 0.5 + 0.5 * t
    slope = half + (0.5 * b) * (1.0 - t * t) * (GELU_A + (3.0 * GELU_A * GELU_B) * (b * b))
    return b * half, slope


def blocks(count, body):
    def one(i, carry):
        body(i)
        return carry

    lax.fori_loop(0, count, one, 0)


def scale_of(ref, eps, width):
    total = jnp.sum(jnp.sum(ref[...], axis=0), axis=0, keepdims=True)
    return lax.rsqrt(total / width + eps)


def mix_kernel(
    width, eps,
    x_in, g_in, gain, masks, par, gates_hi, gates_lo, br_s, m_s, gu_s, d_s,
    y, normed, q, x_own, go, scale, br, mt, b_out, p_out, u_out, r_out, i_out, h_out, gu, down,
    sums, b_s, p_s, u_s, r_s, i_s, h_s, a_c, uh, ul, own, held,
    x_send, x_recv, y_send, y_recv, l_send, l_recv, g_send, g_recv, e_send, e_recv, s_send, s_recv, w_send, w_recv, w_own, o_sem,
):
    row, z, core = place()
    block, seq = y.shape
    half = x_in.shape[0]
    chan = q.shape[0]
    greet(row, z, core, True, True)
    weights = [
        Weights(src, dst, w_send.at[n], w_recv.at[n], w_own.at[n], row, z, core, n == 1)
        for n, (src, dst) in enumerate(((br_s, br), (m_s, mt), (gu_s, gu), (d_s, down)))
    ]
    mine = pl.ds(pl.multiple_of(core * seq, seq), seq)
    other = pl.ds(pl.multiple_of((1 - core) * seq, seq), seq)
    sibling = {"col": 2 * z + (1 - core)}
    swap = remote(x_in.at[:, other], x_own.at[rows_of(core, half), :], x_send, x_recv, sibling)
    swap.start()
    inner = pl.ds(pl.multiple_of(z * block + core * half, 16), half)
    swap_go = remote(g_in.at[:, other], go.at[inner, :], y_send, y_recv, sibling)
    swap_go.start()
    for w in weights[:2]:
        w.start()
    x_own[rows_of(core, half), :] = x_in[:, mine]
    go[inner, :] = g_in[:, mine]
    swap.wait()
    swap_go.wait()
    gather_go = Gather(go, e_send, e_recv, z, core, block)
    gather_go.send(0, 0)

    sums[z] = jnp.zeros(sums.shape[1:], F32)

    def squares(i):
        v = x_own[rows_of(i, 16), :].astype(F32)
        v = v * v
        sums[z] += v[:8] + v[8:]

    blocks(block // 16, squares)
    share_line(sums, l_send, l_recv, z, core)
    s1 = scale_of(sums, eps, width)
    scale[...] = jnp.broadcast_to(s1, scale.shape)

    def norm(i):
        v = x_own[rows_of(i, 16), :].astype(F32) * scale[0:1, :] * gain[rows_of(i, 16), :]
        normed[pl.ds(pl.multiple_of(z * block + i * 16, 16), 16), :] = v.astype(BF16)

    blocks(block // 16, norm)
    gather = Gather(normed, g_send, g_recv, z, core, block)
    spread = Spread(own, held, s_send, s_recv, z, core)
    gather.send(0, 0)
    gather_go.forward(1, 0)
    gather.forward(1, 0)
    gather.send(0, 1)
    gather.forward(2, 0)
    gather_go.forward(2, 0)
    gather_go.send(0, 1)
    p_s[:, 0:128] = jnp.zeros((chan, 128), F32)
    h_s[:, 0:128] = jnp.zeros((chan, 128), F32)
    weights[0].forward()
    gather_go.forward(1, 1)
    weights[0].finish()

    hc = chan // 2
    kept = (b_s, p_s, u_s, r_s, i_s, h_s)
    outs = (b_out, p_out, u_out, r_out, i_out, h_out)

    def keep(n, part):
        lead = 128 if kept[n] is p_s or kept[n] is h_s else 0
        at = pl.ds(pl.multiple_of(lead + part * PART, 128), PART)
        to = at if lead else lanes(part)
        return pltpu.make_async_copy(kept[n].at[:, at], outs[n].at[:, to], o_sem.at[n, part])

    def pad(n):
        side = pl.ds(0, 128)
        return pltpu.make_async_copy(kept[n].at[:, side], outs[n].at[:, side], o_sem.at[n, PARTS])

    pad(1).start()
    pad(5).start()

    def work(k):
        here = lanes(k)
        ahead = pl.ds(pl.multiple_of(128 + k * PART, 128), PART)
        wide = pl.ds(pl.multiple_of(k * PART, 128), PART + 128)
        n1 = normed[:, here]
        for c in (0, 1):
            b_s[c * hc : (c + 1) * hc, here] = dot(br[c * 2 * hc : c * 2 * hc + hc, :], n1)
            p_s[c * hc : (c + 1) * hc, ahead] = dot(br[c * 2 * hc + hc : (c + 1) * 2 * hc, :], n1)

        def conv(i):
            ch = rows_of(i, 32)
            window = p_s[ch, wide]
            pr = par[ch, :]
            u = pr[:, 4:5] + pr[:, 0:1] * window[:, 128:]
            for lag in (1, 2, 3):
                u = u + pr[:, lag : lag + 1] * (pltpu.roll(window, lag, 1)[:, 128:] * masks[lag : lag + 1, here])
            u_s[ch, here] = u
            high = u.astype(BF16)
            uh[ch, :] = high
            ul[ch, :] = (u - high.astype(F32)).astype(BF16)

        blocks(chan // 32, conv)
        gather.middle(k)
        for g in range(chan // 256):
            at = slice(g * 256, (g + 1) * 256)
            pre = dot(gates_hi[g], uh[at, :]) + dot(gates_hi[g], ul[at, :]) + dot(gates_lo[g], uh[at, :])
            r_s[at, here] = pre[:256]
            i_s[at, here] = pre[256:]

        def decay(i):
            ch = rows_of(i, 64)
            pr = par[ch, :]
            start = masks[0:1, here] > 0.5
            r = jax.nn.sigmoid(r_s[ch, here] + pr[:, 5:6])
            gate = jax.nn.sigmoid(i_s[ch, here] + pr[:, 6:7])
            r_s[ch, here] = r
            i_s[ch, here] = gate
            a = jnp.exp(-(r * pr[:, 7:8]))
            m = jnp.where(start, 1.0, jnp.sqrt(1.0 - a * a + FLOOR))
            a_c[ch, :] = jnp.where(start, 0.0, a)
            h_s[ch, ahead] = m * gate * u_s[ch, here]

        blocks(chan // 64, decay)
        first = lax.broadcasted_iota(jnp.int32, (64, PART), 1) == 0

        def recur(i):
            ch = rows_of(i, 64)
            a, h = a_c[ch, :], h_s[ch, ahead]
            last = h_s[ch, pl.ds(pl.multiple_of(k * PART, 128), 128)][:, 127:128]
            h = h + jnp.where(first, a * last, 0.0)
            a = jnp.where(first, 0.0, a)
            shift = 1
            while shift < PART:
                h = h + a * pltpu.roll(h, shift, 1)
                if shift * 2 < PART:
                    a = a * pltpu.roll(a, shift, 1)
                shift *= 2
            h_s[ch, ahead] = h

        blocks(chan // 64, recur)
        gather.later(k)

        @pl.when(k == 0)
        def _():
            gather_go.forward(2, 1)
            weights[1].forward()
            for w in weights[2:]:
                w.start()
            weights[1].finish()

        def mixed(i):
            ch = rows_of(i, 64)
            b = b_s[ch, here]
            t = jnp.tanh(GELU_A * (b + GELU_B * (b * b * b)))
            q[ch, here] = (b * (0.5 + 0.5 * t) * h_s[ch, ahead]).astype(BF16)

        blocks(chan // 64, mixed)
        qk = q[:, here]
        for s in range(LINE):
            own[k, s] = dot(mt[s * block : (s + 1) * block, :], qk)
        for n in range(len(kept)):
            keep(n, k).start()

    def finish(k, total):
        def add(i):
            at = pl.multiple_of(i * 16, 16)
            y[pl.ds(at, 16), lanes(k)] = x_own[pl.ds(at, 16), lanes(k)].astype(F32) + total(at, 16)

        blocks(block // 16, add)

    def step(t, carry):
        @pl.when(t < PARTS)
        def _():
            gather.arrive(2, t)
            work(t)

        @pl.when(t == PARTS - 1)
        def _():
            gather_go.send(0, 2)
            gather_go.send(0, 3)

        spread.serve(t, finish)

        @pl.when(t == PARTS)
        def _():
            gather_go.forward(1, 2)
            gather_go.forward(1, 3)

        @pl.when(t == PARTS + 1)
        def _():
            gather_go.forward(2, 2)
            gather_go.forward(2, 3)
            weights[2].forward()

        pl.when(t == PARTS + 2)(weights[3].forward)
        return carry

    lax.fori_loop(0, PARTS + LINE - 1, step, 0)
    for w in weights[2:]:
        w.finish()
    for w in weights:
        w.sent()
    blocks(PARTS, lambda part: gather_go.arrive(2, part))
    gather_go.sent()
    gather.sent()
    spread.sent()
    for n in range(len(kept)):
        blocks(PARTS, lambda part: keep(n, part).wait())
    pad(1).wait()
    pad(5).wait()


def feed_kernel(
    width, eps,
    y, gain, go_h, gu_h, d_h, br_s, m_s,
    normed, scale, dn2, o_out, g_own, g_got, gd_own, gd_got, br_n, m_n,
    sums, gu, gun, down, dt, go, ev, dz, zs, dev, own_o, own_n, held_n,
    c_sem, o_sem, l_send, l_recv, g_send, g_recv, t_send, t_recv, w_send, w_recv, w_own, d_send, d_recv, d_own,
):
    row, z, core = place()
    block, seq = y.shape
    sibling = {"col": 2 * z + (1 - core)}
    greet(row, z, core, True, True)
    loads = [
        pltpu.make_async_copy(src, dst, c_sem.at[n]) for n, (src, dst) in enumerate(((gu_h, gu), (d_h, down), (go_h, go)))
    ]
    for load in loads:
        load.start()
    sums[z] = jnp.zeros(sums.shape[1:], F32)

    def squares(i):
        v = y[rows_of(i, 16), :]
        v = v * v
        sums[z] += v[:8] + v[8:]

    blocks(block // 16, squares)
    share_line(sums, l_send, l_recv, z, core)
    s2 = scale_of(sums, eps, width)
    scale[...] = jnp.broadcast_to(s2, scale.shape)

    def norm(i):
        v = y[rows_of(i, 16), :] * scale[0:1, :] * gain[rows_of(i, 16), :]
        normed[pl.ds(pl.multiple_of(z * block + i * 16, 16), 16), :] = v.astype(BF16)

    blocks(block // 16, norm)
    gather = Gather(normed, g_send, g_recv, z, core, block)
    spread_n = Spread(own_n, held_n, t_send, t_recv, z, core)
    hid = zs.shape[0]
    hh = hid // 2
    gather.send(0, 0)
    weights = [
        Weights(src, dst, w_send.at[n], w_recv.at[n], w_own.at[n], row, z, core, n == 0)
        for n, (src, dst) in enumerate(((br_s, br_n), (m_s, m_n)))
    ]
    for w in weights:
        w.start()
    loads[1].wait()

    def turn_down(i):
        at = pl.ds(pl.multiple_of(i * 128, 128), 128)
        dt[:, at] = down[at, :].T

    blocks(hid // 128, turn_down)
    gather.forward(1, 0)
    gather.send(0, 1)
    loads[0].wait()

    def turn_up(i):
        at = pl.ds(pl.multiple_of(i * 128, 128), 128)
        gun[:, at] = gu[at, :].T

    blocks(hid // 128, turn_up)
    gather.forward(2, 0)
    blocks(hid // 128, lambda i: turn_up(i + hid // 128))
    loads[2].wait()

    def keep_o(k):
        return pltpu.make_async_copy(own_o.at[k], o_out.at[k], o_sem.at[k])

    def work(k):
        here = lanes(k)
        n2 = normed[:, here]
        for c in range(2):
            for e in range(2):
                ev[e * hh : (e + 1) * hh, :] = dot(gu[(2 * c + e) * hh : (2 * c + e + 1) * hh, :], n2)
            if c == 0:
                gather.middle(k)
            dz[...] = dot(down[c * hh : (c + 1) * hh, :], go[:, here])

            def one(i):
                off = pl.multiple_of(i * 64, 64)
                e = ev[pl.ds(off, 64), :]
                v = ev[pl.ds(hh + off, 64), :]
                d = dz[pl.ds(off, 64), :]
                act, slope = gelu_parts(e)
                zs[pl.ds(c * hh + off, 64), here] = (act * v).astype(BF16)
                dev[pl.ds(c * 2 * hh + off, 64), here] = (d * v * slope).astype(BF16)
                dev[pl.ds(c * 2 * hh + hh + off, 64), here] = (d * act).astype(BF16)

            blocks(hh // 64, one)
        gather.later(k)
        dk = dev[:, here]
        for s in range(LINE):
            own_n[k, s] = dot(gun[s * block : (s + 1) * block, :], dk)
        spread_n.serve(k, finish_n)
        zk = zs[:, here]
        for s in range(LINE):
            own_o[k, s] = dot(dt[s * block : (s + 1) * block, :], zk).astype(own_o.dtype)
        keep_o(k).start()

    def columns(start):
        return pl.ds(pl.multiple_of(start, 128), block)

    def place_up(j):
        side = jnp.where(j >= 3, core, 1 - core)
        return side * hid + (j % 3) * block, columns((j % 3) * block)

    def send_up(j):
        at, to = place_up(j)
        return remote(gun.at[:, columns(at)], g_got.at[:, to], d_send.at[j], d_recv.at[j], sibling)

    def keep_up(j):
        at, to = place_up(j)
        return pltpu.make_async_copy(gun.at[:, columns(at)], g_own.at[:, to], d_own.at[j - 3])

    def send_down():
        return remote(down.at[rows_of(1 - core, hh), :], gd_got, d_send.at[3], d_recv.at[3], sibling)

    def keep_down():
        return pltpu.make_async_copy(down.at[rows_of(core, hh), :], gd_own, d_own.at[3])

    def grad_up(j):
        at = place_up(j)[0]
        right = pl.ds(pl.multiple_of(at, 16), block)
        for low in (0, width // 2):
            piece = slice(low, low + width // 2)
            gun[piece, columns(at)] = dot_nt(normed[piece, :], dev[right, :]).astype(BF16)

        @pl.when(j < 3)
        def _():
            send_up(j).start()

        @pl.when(j >= 3)
        def _():
            keep_up(j).start()

    def grad_down(side):
        at = rows_of(side, hh)
        down[at, :] = dot_nt(zs[at, :], go[...]).astype(BF16)

    def finish_n(k, total):
        def add(i):
            at = pl.multiple_of(i * 16, 16)
            dn2[pl.ds(at, 16), lanes(k)] = total(at, 16)

        blocks(block // 16, add)

    def step(t, carry):
        gather.arrive(2, t)
        work(t)
        pl.when(t == 2)(weights[0].forward)
        pl.when(t == 3)(weights[1].forward)
        return carry

    lax.fori_loop(0, PARTS, step, 0)

    def drain(i, carry):
        t = PARTS + i
        blocks(2, lambda j: grad_up(2 * i + j))
        spread_n.serve(t, finish_n)

        @pl.when(i < 2)
        def _():
            grad_down(jnp.where(i == 0, 1 - core, core))

        pl.when(i == 0)(lambda: send_down().start())
        pl.when(i == 1)(lambda: keep_down().start())
        return carry

    lax.fori_loop(0, LINE - 1, drain, 0)
    for w in weights:
        w.finish()
        w.sent()
    gather.sent()
    spread_n.sent()
    blocks(PARTS, lambda k: keep_o(k).wait())
    for j in range(3):
        keep_up(j + 3).wait()
        send_up(j).wait()
    keep_down().wait()
    send_down().wait()


def back_kernel(
    width,
    y, dn2_h, go_h, x_own, scale_two, scale_one, gain_two, gain_one, masks, par, gates_t, m_h, br_h,
    b_h, p_h, u_h, r_h, i_h, h_h, q_h, n1_h, f_own, f_got, fd_own, fd_got, o_h,
    result, input_grad, tiny_v, tiny_g, f_sum, f_land, fd_sum, fd_land, g_sum, g_land, gm_sum, gm_land,
    sums, sums2, coef, m_n, br_n, b_s, p_s, u_s, r_s, i_s, h_s, dyf, dbp, dy, dn1, dq, du, dri, a_c, l_c, carry_s, own, held,
    qv, f_a, f_b, fd_a, fd_b, feed_part, mix_part, small, gate_grad, own_o, held_o, res, g_got, gm_got,
    vec, vec_in, vec_all, gd, gd_in, gd_all,
    c_sem, k_sem, l_send, l_recv, l2_send, l2_recv, g_send, g_recv, s_send, s_recv, r_send, r_recv,
    f_sem, f_send, f_recv, d_send, d_recv, d_own, o_send, o_recv, y_send, y_recv, q_send, q_recv, n_send, n_recv, v_send, v_recv,
):
    row, z, core = place()
    block, seq = y.shape
    half = block // 2
    chan = b_s.shape[1]
    hc = chan // 2
    sibling = {"col": 2 * z + (1 - core)}
    greet(row, z, core, True, True)
    g_s = res
    load_g = pltpu.make_async_copy(go_h.at[rows_of(z, block), :], g_s, c_sem.at[0])
    load_g.start()
    dn2 = dn1
    load_d = pltpu.make_async_copy(dn2_h, dn2, c_sem.at[5])
    load_d.start()
    load_o = pltpu.make_async_copy(o_h, own_o, c_sem.at[6])
    load_o.start()
    load_m = pltpu.make_async_copy(m_h, m_n, c_sem.at[1])
    load_m.start()
    load_b = pltpu.make_async_copy(br_h, br_n, c_sem.at[2])
    load_b.start()
    load_q = pltpu.make_async_copy(q_h, qv, c_sem.at[3])
    n1 = dyf
    load_n = pltpu.make_async_copy(n1_h, n1, c_sem.at[4])
    kept = (b_s, p_s, u_s, r_s, i_s, h_s)
    srcs = (b_h, p_h, u_h, r_h, i_h, h_h)

    def fetch(n, part):
        if kept[n] is p_s or kept[n] is h_s:
            at = pl.ds(pl.multiple_of(part * PART, 128), PART + 128)
        else:
            at = lanes(part)
        return pltpu.make_async_copy(srcs[n].at[:, at], kept[n].at[part % 2], k_sem.at[n, part % 2])

    def fetch_all(part):
        for n in range(len(kept)):
            fetch(n, part).start()

    fetch_all(PARTS - 1)
    load_q.start()
    du[:, 0:128] = jnp.zeros((chan, 128), F32)
    carry_s[...] = jnp.zeros(carry_s.shape, F32)
    small[...] = jnp.zeros(small.shape, F32)
    gate_grad[...] = jnp.zeros(gate_grad.shape, F32)

    sums[z] = jnp.zeros(sums.shape[1:], F32)

    load_d.wait()

    def inner(i):
        at = rows_of(i, 16)
        d, v = dn2[at, :], y[at, :]
        w = d * v
        c = w * gain_two[at, :]
        sums[z] += c[:8] + c[8:]
        w = w * scale_two[0:1, :]
        fold = w[:, 0:128]
        for j in range(1, seq // 128):
            fold = fold + w[:, j * 128 : (j + 1) * 128]
        feed_part[at, :] = fold

    blocks(block // 16, inner)
    share_line(sums, l_send, l_recv, z, core)
    spread_o = Spread(own_o, held_o, o_send, o_recv, z, core)

    def finish_o(k, total):
        def add(i):
            at = pl.multiple_of(i * 16, 16)
            res[pl.ds(at, 16), lanes(k)] = (y[pl.ds(at, 16), lanes(k)] + total(at, 16)).astype(BF16)

        blocks(block // 16, add)

    load_o.wait()
    spread_o.serve(0, finish_o)
    load_g.wait()
    total = jnp.sum(jnp.sum(sums[...], axis=0), axis=0, keepdims=True)
    s2 = scale_two[0:1, :]
    coef[0:1, :] = s2 * s2 * s2 * (total / width)

    def outer(i):
        at = rows_of(i, 16)
        v = g_s[at, :].astype(F32) + (scale_two[0:1, :] * (gain_two[at, :] * dn2[at, :]) - y[at, :] * coef[0:1, :])
        dy[at, :] = v
        dyf[pl.ds(pl.multiple_of(z * block + i * 16, 16), 16), :] = v.astype(BF16)

    blocks(block // 16, outer)
    gather = Gather(dyf, g_send, g_recv, z, core, block, back=True)
    spread = Spread(own, held, s_send, s_recv, z, core)
    gather.open()
    spread_o.serve(1, finish_o)
    load_m.wait()
    load_b.wait()
    final = lax.broadcasted_iota(jnp.int32, (64, PART), 1) == PART - 1

    f_arrays = ((f_own, f_got, f_a, f_b, f_sum, f_land), (fd_own, fd_got, fd_a, fd_b, fd_sum, fd_land))

    def f_loads(d):
        pulls = []
        for n, (ours, theirs, a, b, _, _) in enumerate(f_arrays):
            if n == 0:
                piece = (rows_of(row ^ d, block), slice(None))
            else:
                piece = (slice(None), pl.ds(pl.multiple_of((row ^ d) * block, 128), block))
            pulls.append(pltpu.make_async_copy(ours.at[piece], a.at[d], f_sem.at[n, 0]))
            pulls.append(pltpu.make_async_copy(theirs.at[piece], b, f_sem.at[n, 1]))
        return pulls

    def f_out(d):
        outs = []
        for n, (_, _, a, _, kept_at, land) in enumerate(f_arrays):
            if d == 0:
                outs.append(pltpu.make_async_copy(a.at[0], kept_at, f_send.at[n, 0]))
            else:
                outs.append(
                    remote(a.at[d], land.at[d - 1], f_send.at[n, d], f_recv.at[n, d], {"row": row ^ d})
                )
        return outs

    def f_part(d):
        for pull in f_loads(d):
            pull.wait()
        for _, _, a, b, _, _ in f_arrays:

            def add(i):
                at = rows_of(i, 16)
                a[d, at, :] = (a[d, at, :].astype(F32) + b[at, :].astype(F32)).astype(BF16)

            blocks(b.shape[0] // 16, add)
        for out in f_out(d):
            out.start()
        if d > 0:
            for pull in f_loads(d - 1):
                pull.start()

    def f_step(t):
        for d in range(PARTS):
            pl.when(t == PARTS - 1 - d)(functools.partial(f_part, d))

    for pull in f_loads(PARTS - 1):
        pull.start()

    def fold2(v):
        return v[:, 0:128] + v[:, 128:256]

    def work(t):
        k = PARTS - 1 - t
        here = lanes(k)
        wide = pl.ds(pl.multiple_of(k * PART, 128), PART + 128)
        slot = k % 2
        for n in range(len(kept)):
            fetch(n, k).wait()

        @pl.when(k > 0)
        def _():
            fetch_all(k - 1)

        dq[...] = dot(m_n[...], dyf[:, here])

        def before(i):
            ch = rows_of(i, 64)
            c = i // (hc // 64)
            low = pl.ds(pl.multiple_of(c * hc + i * 64, 64), 64)
            pr = par[ch, :]
            d = dq[ch, :]
            act, slope = gelu_parts(b_s[slot, ch, :])
            dbp[low, here] = (d * h_s[slot, ch, :][:, 128:] * slope).astype(BF16)
            l_c[ch, :] = d * act
            a_c[ch, :] = jnp.exp(-(r_s[slot, ch, :] * pr[:, 7:8]))

        blocks(chan // 64, before)
        gather.middle(t)

        def recur(i):
            ch = rows_of(i, 64)
            start = masks[0:1, here] > 0.5
            a, lam = jnp.where(start, 0.0, a_c[ch, :]), l_c[ch, :]
            lam = lam + jnp.where(final, carry_s[ch, :][:, 0:1], 0.0)
            w = jnp.where(final, 0.0, pltpu.roll(a, PART - 1, 1))
            shift = 1
            while shift < PART:
                lam = lam + w * pltpu.roll(lam, PART - shift, 1)
                if shift * 2 < PART:
                    w = w * pltpu.roll(w, PART - shift, 1)
                shift *= 2
            carry_s[ch, :] = jnp.broadcast_to((a * lam)[:, 0:1], (64, 128))
            l_c[ch, :] = lam

        blocks(chan // 64, recur)
        f_step(t)
        gather.later(t)

        def after(i):
            ch = rows_of(i, 32)
            du[ch, PART:] = du[ch, 0:128]
            pr = par[ch, :]
            start = masks[0:1, here] > 0.5
            lam, a0 = l_c[ch, :], a_c[ch, :]
            earlier = pltpu.roll(h_s[slot, ch, :], 1, 1)[:, 128:]
            r, gate, u = r_s[slot, ch, :], i_s[slot, ch, :], u_s[slot, ch, :]
            m0 = jnp.sqrt(1.0 - a0 * a0 + FLOOR)
            m = jnp.where(start, 1.0, m0)
            lm = lam * m
            lu = lam * u
            du[ch, 0:PART] = lm * gate
            da = jnp.where(start, 0.0, lam * earlier - (lu * gate) * (a0 / m0)) * a0
            dr = da * (-pr[:, 7:8]) * (r * (1.0 - r))
            di = lu * m * (gate * (1.0 - gate))
            g, o = i // 8, (i % 8) * 32
            dri[pl.ds(pl.multiple_of(g * 512 + o, 32), 32), :] = dr.astype(BF16)
            dri[pl.ds(pl.multiple_of(g * 512 + 256 + o, 32), 32), :] = di.astype(BF16)
            small[5, ch, :] += fold2(dr)
            small[6, ch, :] += fold2(di)
            small[7, ch, :] += fold2(da * r)

        blocks(chan // 32, after)
        for g in range(chan // 256):
            at = slice(g * 256, (g + 1) * 256)
            dd = dri[g * 512 : (g + 1) * 512, :]
            du[at, 0:PART] += dot(gates_t[g], dd)
            gate_grad[g] += dot_nt(u_s[slot, at, :].astype(BF16), dd)

        def conv(i):
            ch = rows_of(i, 32)
            c = i // (hc // 32)
            low = pl.ds(pl.multiple_of((c + 1) * hc + i * 32, 32), 32)
            pr = par[ch, :]
            follow = du[ch, :]
            window = p_s[slot, ch, :]
            d = follow[:, :PART]
            dp = pr[:, 0:1] * d
            small[4, ch, :] += fold2(d)
            small[0, ch, :] += fold2(d * window[:, 128:])
            for lag in (1, 2, 3):
                kd = follow * masks[lag : lag + 1, wide]
                dp = dp + pr[:, lag : lag + 1] * pltpu.roll(kd, PART + 128 - lag, 1)[:, :PART]
                small[lag, ch, :] += fold2(kd[:, :PART] * pltpu.roll(window, lag, 1)[:, 128:])
            dbp[low, here] = dp.astype(BF16)

        blocks(chan // 32, conv)
        dk = dbp[:, here]
        for s in range(LINE):
            own[t, s] = dot(br_n[s * block : (s + 1) * block, :], dk).astype(own.dtype)

    def finish(t, total):
        k = PARTS - 1 - t

        def add(i):
            at = pl.multiple_of(i * 16, 16)
            dn1[pl.ds(at, 16), lanes(k)] = total(at, 16)

        blocks(block // 16, add)

    def step(t, carry):
        gather.arrive(2, t)
        work(t)
        spread.serve(t, finish)

        @pl.when(t >= 2)
        def _():
            spread_o.serve(t, finish_o)

        return carry

    lax.fori_loop(0, PARTS, step, 0)
    load_q.wait()

    lru = hc

    def cols_of(side):
        return pl.ds(pl.multiple_of(side * 2 * lru, 128), 2 * lru)

    def send_br():
        return remote(br_n.at[:, cols_of(1 - core)], g_got, d_send.at[0], d_recv.at[0], sibling)

    def send_m():
        return remote(m_n.at[rows_of(1 - core, lru), :], gm_got, d_send.at[1], d_recv.at[1], sibling)

    def grad_br(side):
        br_n[:, cols_of(side)] = dot_nt(n1[...], dbp[rows_of(side, 2 * lru), :]).astype(BF16)

    def out_br(d):
        piece = br_n.at[rows_of(row ^ d, block), cols_of(core)]
        if d == 0:
            return pltpu.make_async_copy(piece, g_sum, d_own.at[0])
        return remote(piece, g_land.at[d - 1], q_send.at[0, d - 1], q_recv.at[0, d - 1], {"row": row ^ d})

    def out_m(d):
        piece = m_n.at[rows_of(core, lru), pl.ds(pl.multiple_of((row ^ d) * block, 128), block)]
        if d == 0:
            return pltpu.make_async_copy(piece, gm_sum, d_own.at[1])
        return remote(piece, gm_land.at[d - 1], q_send.at[1, d - 1], q_recv.at[1, d - 1], {"row": row ^ d})

    def drain(i, carry):
        t = PARTS + i

        @pl.when(i == 0)
        def _():
            m_n[...] = dot_nt(qv[...], dyf[...]).astype(BF16)
            send_m().start()
            gather.sent()
            load_n.start()
            load_n.wait()
            grad_br(1 - core)
            send_br().start()

        @pl.when(i == 1)
        def _():
            grad_br(core)
            send_m().wait_recv()

            def add(j):
                at = rows_of(j, 32)
                to = pl.ds(pl.multiple_of(core * lru + j * 32, 32), 32)
                m_n[to, :] = (m_n[to, :].astype(F32) + gm_got[at, :].astype(F32)).astype(BF16)

            blocks(lru // 32, add)
            for d in (3, 2, 1, 0):
                out_m(d).start()

        @pl.when(i == 2)
        def _():
            send_br().wait_recv()

            def add(j):
                at = rows_of(j, 32)
                br_n[at, cols_of(core)] = (br_n[at, cols_of(core)].astype(F32) + g_got[at, :].astype(F32)).astype(BF16)

            blocks(width // 32, add)
            for d in (3, 2, 1, 0):
                out_br(d).start()

        spread.serve(t, finish)
        spread_o.serve(t, finish_o)
        return carry

    lax.fori_loop(0, LINE - 1, drain, 0)
    mine = pl.ds(pl.multiple_of(core * seq, seq), seq)
    for side in (0, 1):
        for e in range(4):
            at = slice(e * 64, (e + 1) * 64)
            gd[side, at, 0:64] = gate_grad[side, at, e * 64 : (e + 1) * 64]
            gd[side, at, 64:128] = gate_grad[side, at, 256 + e * 64 : 256 + (e + 1) * 64]
    swap_gd = remote(gd.at[1 - core], gd_in, v_send.at[0], v_recv.at[0], sibling)
    swap_gd.start()
    back_o = remote(res.at[rows_of(1 - core, half), :], result.at[:, mine], y_send, y_recv, sibling)
    back_o.start()
    keep_res = pltpu.make_async_copy(res.at[rows_of(core, half), :], result.at[:, mine], d_own.at[2])
    keep_res.start()
    lane = lax.broadcasted_iota(jnp.int32, (64, 128), 1)

    def columns(parts, at):
        total = jnp.zeros((64, 128), F32)
        for n, part in enumerate(parts):
            total = total + jnp.where(lane == n, jnp.sum(part(at), axis=1, keepdims=True), 0.0)
        return total

    vec[...] = jnp.zeros(vec.shape, F32)
    for j in range(chan // 64):
        at = slice(j * 64, (j + 1) * 64)
        v = columns([lambda at, n=n: small[n, at, :] for n in range(8)], at)
        vec[0, :, at] = v.T[0:8, :]

    sums2[z] = jnp.zeros(sums2.shape[1:], F32)

    def inner_one(i):
        at = rows_of(i, 16)
        w = dn1[at, :] * x_own[at, :].astype(F32)
        c = w * gain_one[at, :]
        sums2[z] += c[:8] + c[8:]
        w = w * scale_one[0:1, :]
        fold = w[:, 0:128]
        for j in range(1, seq // 128):
            fold = fold + w[:, j * 128 : (j + 1) * 128]
        mix_part[at, :] = fold

    blocks(block // 16, inner_one)
    share_line(sums2, l2_send, l2_recv, z, core)
    total = jnp.sum(jnp.sum(sums2[...], axis=0), axis=0, keepdims=True)
    s1 = scale_one[0:1, :]
    coef[0:1, :] = s1 * s1 * s1 * (total / width)

    def last(i):
        at = rows_of(i, 16)
        v = dy[at, :] + (
            scale_one[0:1, :] * (gain_one[at, :] * dn1[at, :]) - x_own[at, :].astype(F32) * coef[0:1, :]
        )
        dy[at, :] = v

    blocks(block // 16, last)
    back = remote(dy.at[rows_of(1 - core, half), :], input_grad.at[:, mine], r_send, r_recv, sibling)
    back.start()
    keep_in = pltpu.make_async_copy(dy.at[rows_of(core, half), :], input_grad.at[:, mine], d_own.at[3])
    keep_in.start()
    for j in range(block // 64):
        at = slice(j * 64, (j + 1) * 64)
        v = columns([lambda at: mix_part[at, :], lambda at: feed_part[at, :]], at)
        vec[1, :, at] = v.T[0:8, :]
    swap_vec = remote(vec, vec_in, v_send.at[1], v_recv.at[1], sibling)
    swap_vec.start()
    swap_gd.wait()
    gd_all[0] = gd[core] + gd_in[...]
    rows_gd = [
        remote(gd_all.at[0], gd_all.at[d], n_send.at[0, d - 1], n_recv.at[0, d - 1], {"row": row ^ d}) for d in (1, 2, 3)
    ]
    for copy in rows_gd:
        copy.start()
    swap_vec.wait()
    vec_all[0] = vec[...] + vec_in[...]
    rows_vec = [
        remote(vec_all.at[0], vec_all.at[d], n_send.at[1, d - 1], n_recv.at[1, d - 1], {"row": row ^ d}) for d in (1, 2, 3)
    ]
    for copy in rows_vec:
        copy.start()
    spread.sent()
    spread_o.sent()
    for copy in rows_gd + rows_vec:
        copy.wait()
    for every, out in ((gd_all, tiny_g), (vec_all, tiny_v)):
        first, second = every[row % 2], every[1 - row % 2]
        third, fourth = every[2 + row % 2], every[3 - row % 2]
        out[...] = (first + second) + (third + fourth)
    for d in range(PARTS):
        for out in f_out(d):
            out.wait()
    send_br().wait_send()
    send_m().wait_send()
    for d in (0, 1, 2, 3):
        out_br(d).wait()
        out_m(d).wait()
    for copy in (keep_res, keep_in, back_o, back):
        copy.wait()


def last_kernel(
    f_sum, f_land, fd_sum, fd_land, g_sum, g_land, gm_sum, gm_land, tiny_v, tiny_g, lambdas,
    s_b, s_r, s_m, s_g, s_u, s_d, taps, offs, bias_r, bias_a, decay, mix, feed, retain, admit,
):
    core = place()[2]
    lru, block = s_m.shape
    ff, half = s_d.shape[0], mix.shape[1]

    def four(first, others, at):
        return first[at, :].astype(F32) + others[0, at, :].astype(F32) + (
            others[1, at, :].astype(F32) + others[2, at, :].astype(F32)
        )

    def put_gu(i):
        at = rows_of(i, 32)
        v = four(f_sum, f_land, at)
        s_g[at, :] = v[:, :ff]
        s_u[at, :] = v[:, ff:]
        v = four(g_sum, g_land, at)
        s_b[at, :] = v[:, :lru]
        s_r[at, :] = v[:, lru:]

    blocks(block // 32, put_gu)

    def put_d(i):
        at = rows_of(i, 32)
        s_d[at, :] = four(fd_sum, fd_land, at)

    blocks(ff // 32, put_d)

    def put_m(i):
        at = rows_of(i, 32)
        s_m[at, :] = four(gm_sum, gm_land, at)

    blocks(lru // 32, put_m)
    small = tiny_v[0, :, pl.ds(pl.multiple_of(core * lru, 128), lru)]
    taps[...] = small[0:4]
    offs[...] = small[4:5]
    bias_r[...] = small[5:6]
    bias_a[...] = small[6:7]
    decay[...] = small[7:8] * (8.0 * jax.nn.sigmoid(-lambdas[...]))
    gains = jnp.where(core == 0, tiny_v[1, :, 0:half], tiny_v[1, :, half : 2 * half])
    mix[...] = gains[0:1]
    feed[...] = gains[1:2]
    for e in range(retain.shape[0]):
        at = slice(e * 64, (e + 1) * 64)
        retain[e] = tiny_g[at, 0:64]
        admit[e] = tiny_g[at, 64:128]


ANY = pl.BlockSpec(memory_space=pl.ANY)
VM = pl.BlockSpec(memory_space=pltpu.VMEM)
DMA = pltpu.SemaphoreType.DMA
ROOM = 62 * 1024 * 1024


def shape(dims, kind):
    return jax.ShapeDtypeStruct(dims, kind)


def call(kernel, ins, outs, scratch, ident, name, flops):
    return pl.pallas_call(
        kernel,
        out_shape=[o[0] for o in outs],
        in_specs=ins,
        out_specs=[o[1] for o in outs],
        scratch_shapes=scratch,
        name=name,
        compiler_params=pltpu.CompilerParams(
            collective_id=ident, has_side_effects=True, vmem_limit_bytes=ROOM
        ),
        cost_estimate=pl.CostEstimate(flops=flops, bytes_accessed=40000000, transcendentals=0),
    )


PAIRS = [[0, 1], [2, 3], [4, 5], [6, 7]]


def diagonal(w, size):
    per = size // w.shape[1]
    w = w.reshape(-1, per, w.shape[1], w.shape[2])
    eye = jnp.eye(per, dtype=w.dtype)
    full = w[:, :, :, None, :] * eye[None, :, None, :, None]
    return full.reshape(-1, size, size)


def fast_body(
    inputs, segments, mix_gain, branch_weight, recur_weight, kernel, offsets, retain_weight, retain_bias,
    admit_weight, admit_bias, lambdas, merge_weight, feed_gain, gate_weight, up_weight, down_weight, cotangent,
):
    half, tokens = inputs.shape
    block, seq, width = 2 * half, tokens // 2, D
    lru, heads = branch_weight.shape[1], retain_weight.shape[0]
    chan = 2 * lru
    ff = gate_weight.shape[1]
    hid = 2 * ff
    rows = branch_weight.shape[0]
    cols = merge_weight.shape[1]
    core = lax.axis_index("col") % 2

    parts = (mix_gain, feed_gain, kernel[0], kernel[1], kernel[2], kernel[3], offsets, retain_bias, admit_bias, lambdas)
    parts = parts + (retain_weight.reshape(-1), admit_weight.reshape(-1))
    both = lax.all_gather(jnp.concatenate(parts), "col", axis=0, axis_index_groups=PAIRS)
    whole, at = [], 0
    for part in parts:
        whole.append(both[:, at : at + part.shape[0]].reshape(-1))
        at += part.shape[0]
    gain_one, gain_two = whole[0][:, None], whole[1][:, None]
    lam = whole[9]
    rate = 8.0 * jax.nn.softplus(-lam)
    par = jnp.stack(whole[2:6] + whole[6:9] + [rate] + [jnp.zeros_like(lam)] * 8, axis=1)
    retain = diagonal(whole[10].reshape(-1, 64, 64), 256)
    admit = diagonal(whole[11].reshape(-1, 64, 64), 256)
    gates = jnp.concatenate([retain, admit], axis=2)
    gates_hi = gates.astype(BF16)
    gates_lo = (gates - gates_hi.astype(F32)).astype(BF16)
    flip = lambda w: jnp.swapaxes(w, 1, 2)

    segs = lax.dynamic_slice(segments, (core * seq,), (seq,))
    masks = [jnp.concatenate([jnp.ones((1,), bool), segs[1:] != segs[:-1]])]
    for lag in (1, 2, 3):
        masks.append(jnp.concatenate([jnp.zeros((lag,), bool), segs[lag:] == segs[:-lag]]))
    masks = jnp.pad(jnp.stack(masks).astype(F32), ((0, 4), (0, 128)))

    br_s = jnp.concatenate([branch_weight, recur_weight], axis=1).T
    m_s = merge_weight.T
    gu_s = jnp.concatenate([gate_weight, up_weight], axis=1).T

    f_tok = lambda n, kind=F32: shape((n, seq), kind)
    padded = (shape((chan, 128 + seq), F32), ANY)
    state = [(f_tok(chan), ANY), padded, *[(f_tok(chan), ANY)] * 3, padded]
    line = [DMA((3,)), DMA((3,))]
    steps = [DMA((2, 3, PARTS)), DMA((2, 3, PARTS))]
    sums = [DMA((2, PARTS, LINE)), DMA((2, PARTS, LINE))]
    held = pltpu.VMEM((PARTS, LINE + 1, block, PART), BF16)
    own = pltpu.VMEM((PARTS, LINE, block, PART), F32)
    tok = lambda n, kind=F32, lead=0: pltpu.VMEM((n, lead + seq), kind)

    y, n1, q, x_own, go, scale_one, _, _, b, p, u, r, i, h, gu, down = call(
        functools.partial(mix_kernel, width, EPS),
        [VM] * 7 + [ANY] * 4,
        [(f_tok(block), VM), (f_tok(width, BF16), VM), (f_tok(chan, BF16), VM), (f_tok(block, BF16), VM),
         (f_tok(width, BF16), VM), (f_tok(8), VM),
         (shape((2 * chan, width), BF16), VM), (shape((width, chan), BF16), VM)] + state
        + [(shape((2 * hid, width), BF16), ANY), (shape((hid, width), BF16), ANY)],
        [pltpu.VMEM((LINE, 8, seq), F32), tok(chan), tok(chan, F32, 128), tok(chan), tok(chan), tok(chan), tok(chan, F32, 128),
         pltpu.VMEM((chan, PART), F32), pltpu.VMEM((chan, PART), BF16), pltpu.VMEM((chan, PART), BF16), own, held, DMA, DMA, DMA, DMA]
        + line + steps + steps + sums + [DMA((4, 7)), DMA((4, 7)), DMA((4,)), DMA((6, PARTS + 1))],
        0, "mix_forward", 5 * 10**9,
    )(inputs, cotangent, gain_one, masks, par, flip(gates_hi), flip(gates_lo), br_s, m_s, gu_s, down_weight)

    br_t = jnp.concatenate([branch_weight, recur_weight], axis=1)
    grad_gu, grad_d = (shape((width, 2 * ff), BF16), ANY), (shape((ff, width), BF16), ANY)
    grad_br, grad_m = (shape((width, 2 * lru), BF16), ANY), (shape((lru, width), BF16), ANY)
    own_low = pltpu.VMEM((PARTS, LINE, block, PART), BF16)
    parts_o = (PARTS, LINE, block, PART)
    n2, scale_two, dn2, o, f_own, f_got, fd_own, fd_got, br_n, m_n = call(
        functools.partial(feed_kernel, width, EPS),
        [VM] * 2 + [ANY] * 5,
        [(f_tok(width, BF16), VM), (f_tok(8), VM), (f_tok(block), VM), (shape(parts_o, BF16), ANY),
         grad_gu, grad_gu, grad_d, grad_d, (shape((width, 2 * chan), BF16), ANY), (shape((chan, width), BF16), ANY)],
        [pltpu.VMEM((LINE, 8, seq), F32), pltpu.VMEM((2 * hid, width), BF16), pltpu.VMEM((width, 2 * hid), BF16),
         pltpu.VMEM((hid, width), BF16), pltpu.VMEM((width, hid), BF16), tok(width, BF16), pltpu.VMEM((hid, PART), F32),
         pltpu.VMEM((ff, PART), F32), tok(hid, BF16), tok(2 * hid, BF16), own_low, own, held, DMA((3,)), DMA((PARTS,))]
        + line + steps + sums + [DMA((2, 7)), DMA((2, 7)), DMA((2,)), DMA((4,)), DMA((4,)), DMA((4,))],
        1, "feed", 44 * 10**9,
    )(y, gain_two, go, gu, down, br_t, merge_weight)

    pair = lambda lead=0: pltpu.VMEM((2, chan, lead + PART), F32)
    land = lambda n, m: ((shape((n, m), BF16), ANY), (shape((3, n, m), BF16), ANY))
    result, input_grad, tiny_v, tiny_g, *sums_of = call(
        functools.partial(back_kernel, width),
        [VM] + [ANY] * 2 + [VM] * 8 + [ANY] * 15,
        [(shape((half, tokens), BF16), ANY), (shape((half, tokens), F32), ANY), (shape((2, 8, chan), F32), VM),
         (shape((lru, 128), F32), VM), *land(cols, 2 * ff), *land(ff, cols), *land(cols, 2 * lru), *land(lru, cols)],
        [pltpu.VMEM((LINE, 8, seq), F32), pltpu.VMEM((LINE, 8, seq), F32), pltpu.VMEM((8, seq), F32),
         pltpu.VMEM((chan, width), BF16), pltpu.VMEM((width, 2 * chan), BF16),
         pair(), pair(128), pair(), pair(), pair(), pair(128), tok(width, BF16), tok(2 * chan, BF16),
         tok(block), tok(block), pltpu.VMEM((chan, PART), F32), pltpu.VMEM((chan, PART + 128), F32), pltpu.VMEM((2 * chan, PART), BF16),
         pltpu.VMEM((chan, PART), F32), pltpu.VMEM((chan, PART), F32), pltpu.VMEM((chan, 128), F32), own_low, held,
         tok(chan, BF16), pltpu.VMEM((4, cols, 2 * ff), BF16), pltpu.VMEM((cols, 2 * ff), BF16),
         pltpu.VMEM((4, ff, cols), BF16), pltpu.VMEM((ff, cols), BF16),
         pltpu.VMEM((block, 128), F32), pltpu.VMEM((block, 128), F32), pltpu.VMEM((8, chan, 128), F32),
         pltpu.VMEM((2, lru, 2 * lru), F32), own_low, held, tok(block, BF16), pltpu.VMEM((width, 2 * lru), BF16),
         pltpu.VMEM((lru, width), BF16), pltpu.VMEM((2, 8, chan), F32), pltpu.VMEM((2, 8, chan), F32),
         pltpu.VMEM((4, 2, 8, chan), F32), pltpu.VMEM((2, lru, 128), F32), pltpu.VMEM((lru, 128), F32),
         pltpu.VMEM((4, lru, 128), F32), DMA((7,)), DMA((6, 2))] + line + line + steps + sums
        + [DMA, DMA, DMA((2, 2)), DMA((2, PARTS)), DMA((2, PARTS)), DMA((2,)), DMA((2,)), DMA((4,))] + sums
        + [DMA, DMA, DMA((2, 3)), DMA((2, 3)), DMA((2, 3)), DMA((2, 3)), DMA((2,)), DMA((2,))],
        2, "mix_backward", 10 * 10**9,
    )(y, dn2, go, x_own, scale_two, scale_one, gain_two, gain_one, masks, par, gates_hi, m_n, br_n, b, p, u, r, i, h,
      q, n1, f_own, f_got, fd_own, fd_got, o)

    line_of = shape((1, lru), F32)
    s_b, s_r, s_m, s_g, s_u, s_d, taps, offs, bias_r, bias_a, decay, mix, feed, retain, admit = pl.pallas_call(
        last_kernel,
        out_shape=[shape((cols, lru), F32)] * 2 + [shape((lru, cols), F32)] + [shape((cols, ff), F32)] * 2
        + [shape((ff, cols), F32), shape((4, lru), F32)] + [line_of] * 4 + [shape((1, half), F32)] * 2
        + [shape((heads, 64, 64), F32)] * 2,
        in_specs=[VM] * 11,
        out_specs=[VM] * 15,
        name="last_sums",
        compiler_params=pltpu.CompilerParams(vmem_limit_bytes=ROOM),
    )(*sums_of, tiny_v, tiny_g, lambdas[None, :])
    return (
        result,
        input_grad,
        mix[0],
        s_b,
        s_r,
        taps,
        offs[0],
        retain,
        bias_r[0],
        admit,
        bias_a[0],
        decay[0],
        s_m,
        feed[0],
        s_g,
        s_u,
        s_d,
    )


def suits(mesh, args):
    return (
        dict(mesh.shape) == {"row": 4, "col": 8}
        and args[0].shape == (D, 8 * SEQ)
        and args[3].shape == (D, 2048)
        and args[14].shape == (D, 4608)
        and args[7].shape == (32, 64, 64)
    )


def solution(mesh):
    in_specs = (
        P("col", "row"),
        P("row"),
        P("col"),
        P("row", "col"),
        P("row", "col"),
        P(None, "col"),
        P("col"),
        P("col", None, None),
        P("col"),
        P("col", None, None),
        P("col"),
        P("col"),
        P("col", "row"),
        P("col"),
        P("row", "col"),
        P("row", "col"),
        P("col", "row"),
        P("col", "row"),
    )
    out_specs = (
        P("col", "row"),
        P("col", "row"),
        P("col"),
        P("row", "col"),
        P("row", "col"),
        P(None, "col"),
        P("col"),
        P("col", None, None),
        P("col"),
        P("col", None, None),
        P("col"),
        P("col"),
        P("col", "row"),
        P("col"),
        P("row", "col"),
        P("row", "col"),
        P("col", "row"),
    )
    def run(*args):
        chosen = fast_body if suits(mesh, args) else body
        return jax.shard_map(
            chosen, mesh=mesh, in_specs=in_specs, out_specs=out_specs, check_vma=False
        )(*args)

    return run
```

```python
import functools

import jax
import jax.numpy as jnp
from jax import lax
from jax.experimental import pallas as pl
from jax.experimental.pallas import tpu as pltpu
from jax.sharding import PartitionSpec as P

D = 1536
SEQ = 1024
MICRO = 2


HIGH = lax.Precision.HIGHEST
EPS = 1e-06
POWER = 8.0
FLOOR = 0.01


def combine(earlier, later):
    first_a, first_b = earlier
    second_a, second_b = later
    return (first_a * second_a, second_a * first_b + second_b)


def mixer(
    branch_pre,
    lru_pre,
    segs,
    kernel,
    offsets,
    retain_weight,
    retain_bias,
    admit_weight,
    admit_bias,
    lambdas,
):
    length = lru_pre.shape[0]
    channels = lru_pre.shape[1]
    conv = offsets + kernel[0] * lru_pre
    for lag in range(1, kernel.shape[0]):
        shifted = jnp.concatenate(
            [jnp.zeros((lag, channels), lru_pre.dtype), lru_pre[:-lag]], axis=0
        )
        prior = jnp.concatenate([jnp.full((lag,), -1, jnp.int32), segs[:-lag]])
        keep = (prior == segs).astype(lru_pre.dtype)
        conv = conv + kernel[lag] * shifted * keep[:, None]
    heads = retain_weight.shape[0]
    blocks = conv.reshape(length, heads, channels // heads)
    retain = jax.nn.sigmoid(
        jnp.einsum("thi,hij->thj", blocks, retain_weight, precision=HIGH).reshape(length, channels)
        + retain_bias
    )
    admit = jax.nn.sigmoid(
        jnp.einsum("thi,hij->thj", blocks, admit_weight, precision=HIGH).reshape(length, channels)
        + admit_bias
    )
    decay = jnp.exp(-POWER * retain * jax.nn.softplus(-lambdas))
    factor = jnp.sqrt(1.0 - decay * decay + FLOOR)
    starts = jnp.concatenate([jnp.ones((1,), bool), segs[1:] != segs[:-1]])
    decay = jnp.where(starts[:, None], 0.0, decay)
    factor = jnp.where(starts[:, None], 1.0, factor)
    _, state = lax.associative_scan(combine, (decay, factor * admit * conv), axis=0)
    return jax.nn.gelu(branch_pre) * state


def geglu(gate, upper):
    return jax.nn.gelu(gate) * upper


def contract_rows(left, right):
    return lax.dot_general(
        left, right, (((0,), (0,)), ((), ())), preferred_element_type=jnp.float32
    )


def contract_cols(left, right):
    return lax.dot_general(
        left, right, (((1,), (1,)), ((), ())), preferred_element_type=jnp.float32
    )


def contract_cross(left, right):
    return lax.dot_general(
        left, right, (((0,), (1,)), ((), ())), preferred_element_type=jnp.float32
    )


def norm_forward(resid, gain):
    total = lax.psum(jnp.sum(resid * resid, axis=0), "col")
    scale = lax.rsqrt(total / D + EPS)[None, :]
    return (scale, (resid * scale * gain[:, None]).astype(jnp.bfloat16))


def norm_backward(resid, scale, gain, grad_normed):
    weighted = grad_normed * gain[:, None]
    total = lax.psum(jnp.sum(weighted * resid, axis=0), "col")
    grad_resid = scale * weighted - resid * (scale * scale * scale) * (total / D)[None, :]
    grad_gain = jnp.sum(grad_normed * resid * scale, axis=1)
    return (grad_resid, grad_gain)


def gather_features(normed):
    return lax.all_gather(normed, "col", axis=0, tiled=True)


def gather_cotangent(grad):
    return lax.all_gather(grad, "col", axis=0, tiled=True)


def spread_sum(term):
    return lax.psum_scatter(
        term.astype(jnp.bfloat16), "col", scatter_dimension=0, tiled=True
    ).astype(jnp.float32)


def back_sum(term):
    return spread_sum(term)


def merge_term(whole_merge, mixed_low):
    return spread_sum(contract_cross(whole_merge, mixed_low))


def weight_grads(normed, grad_joined):
    return jnp.dot(
        normed,
        grad_joined,
        preferred_element_type=jnp.float32,
    )


def row_sum(total, axis):
    return lax.psum_scatter(
        total.astype(jnp.bfloat16), "row", scatter_dimension=axis, tiled=True
    ).astype(jnp.float32)


def body(
    inputs,
    segments,
    mix_gain,
    branch_weight,
    recur_weight,
    kernel,
    offsets,
    retain_weight,
    retain_bias,
    admit_weight,
    admit_bias,
    lambdas,
    merge_weight,
    feed_gain,
    gate_weight,
    up_weight,
    down_weight,
    cotangent,
):
    lru_cols = branch_weight.shape[1]
    feed_cols = gate_weight.shape[1]
    mixer_params = (kernel, offsets, retain_weight, retain_bias, admit_weight, admit_bias, lambdas)
    acc_branch = jnp.zeros((D, lru_cols), jnp.float32)
    acc_recur = jnp.zeros((D, lru_cols), jnp.float32)
    acc_gate = jnp.zeros((D, feed_cols), jnp.float32)
    acc_up = jnp.zeros((D, feed_cols), jnp.float32)
    acc_merge = jnp.zeros((lru_cols, D), jnp.float32)
    acc_down = jnp.zeros((feed_cols, D), jnp.float32)
    acc_small = tuple((jnp.zeros_like(p) for p in mixer_params))
    acc_mix = jnp.zeros_like(mix_gain)
    acc_feed = jnp.zeros_like(feed_gain)
    outputs = []
    in_grads = []
    for batch in range(MICRO):
        lower = batch * SEQ
        resid_in = inputs[:, lower : lower + SEQ].astype(jnp.float32)
        grad_out = cotangent[:, lower : lower + SEQ].astype(jnp.float32)
        segs = segments[lower : lower + SEQ]
        whole_branch, whole_recur, whole_gate, whole_up = (
            lax.all_gather(branch_weight, "row", axis=0, tiled=True),
            lax.all_gather(recur_weight, "row", axis=0, tiled=True),
            lax.all_gather(gate_weight, "row", axis=0, tiled=True),
            lax.all_gather(up_weight, "row", axis=0, tiled=True),
        )
        whole_merge, whole_down = (
            lax.all_gather(merge_weight, "row", axis=1, tiled=True),
            lax.all_gather(down_weight, "row", axis=1, tiled=True),
        )
        scale_one, normed_one = norm_forward(resid_in, mix_gain)
        full_one = gather_features(normed_one)
        branch_pre = contract_rows(full_one, whole_branch)
        lru_pre = contract_rows(full_one, whole_recur)

        def local_mixer(bpre, lpre, kern, offs, rweight, rbias, aweight, abias, lams):
            return mixer(bpre, lpre, segs, kern, offs, rweight, rbias, aweight, abias, lams)

        mixed, mixer_pull = jax.vjp(local_mixer, branch_pre, lru_pre, *mixer_params)
        mixed_low = mixed.astype(jnp.bfloat16)
        resid_mid = resid_in + merge_term(whole_merge, mixed_low)
        scale_two, normed_two = norm_forward(resid_mid, feed_gain)
        full_two = gather_features(normed_two)
        gate = contract_rows(full_two, whole_gate)
        upper = contract_rows(full_two, whole_up)
        hidden, geglu_pull = jax.vjp(geglu, gate, upper)
        hidden_low = hidden.astype(jnp.bfloat16)
        result = resid_mid + spread_sum(contract_cross(whole_down, hidden_low))
        outputs.append(result.astype(jnp.bfloat16))
        grad_full = gather_cotangent(grad_out.astype(jnp.bfloat16))
        acc_down = acc_down + contract_cross(hidden_low, grad_full)
        grad_gate, grad_upper = geglu_pull(contract_cross(grad_full, whole_down))
        grad_gate = grad_gate.astype(jnp.bfloat16)
        grad_upper = grad_upper.astype(jnp.bfloat16)
        feed_joined = weight_grads(full_two, jnp.concatenate([grad_gate, grad_upper], axis=1))
        acc_gate = acc_gate + feed_joined[:, :feed_cols]
        acc_up = acc_up + feed_joined[:, feed_cols:]
        grad_normed_two = back_sum(
            contract_cols(whole_gate, grad_gate) + contract_cols(whole_up, grad_upper)
        )
        grad_mid_norm, feed_part = norm_backward(resid_mid, scale_two, feed_gain, grad_normed_two)
        acc_feed = acc_feed + feed_part
        grad_mid = grad_out + grad_mid_norm
        grad_mid_full = gather_cotangent(grad_mid.astype(jnp.bfloat16))
        acc_merge = acc_merge + contract_cross(mixed_low, grad_mid_full)
        pulled = mixer_pull(contract_cross(grad_mid_full, whole_merge))
        grad_branch = pulled[0].astype(jnp.bfloat16)
        grad_lru = pulled[1].astype(jnp.bfloat16)
        acc_small = tuple((total + part for total, part in zip(acc_small, pulled[2:])))
        branch_joined = weight_grads(full_one, jnp.concatenate([grad_branch, grad_lru], axis=1))
        acc_branch = acc_branch + branch_joined[:, :lru_cols]
        acc_recur = acc_recur + branch_joined[:, lru_cols:]
        grad_normed_one = back_sum(
            contract_cols(whole_branch, grad_branch) + contract_cols(whole_recur, grad_lru)
        )
        grad_in_norm, mix_part = norm_backward(resid_in, scale_one, mix_gain, grad_normed_one)
        acc_mix = acc_mix + mix_part
        in_grads.append(grad_mid + grad_in_norm)
    sum_branch, sum_recur, sum_gate, sum_up = (
        row_sum(acc_branch, 0),
        row_sum(acc_recur, 0),
        row_sum(acc_gate, 0),
        row_sum(acc_up, 0),
    )
    sum_merge, sum_down = (
        row_sum(acc_merge, 1),
        row_sum(acc_down, 1),
    )
    summed = lax.psum(
        (
            acc_mix,
            acc_feed,
            acc_small[0],
            acc_small[1],
            acc_small[2],
            acc_small[3],
            acc_small[4],
            acc_small[5],
            acc_small[6],
        ),
        "row",
    )
    result_all = jnp.concatenate(outputs, axis=1)
    input_grad = jnp.concatenate(in_grads, axis=1)
    return (
        result_all,
        input_grad,
        summed[0],
        sum_branch,
        sum_recur,
        summed[2],
        summed[3],
        summed[4],
        summed[5],
        summed[6],
        summed[7],
        summed[8],
        sum_merge,
        summed[1],
        sum_gate,
        sum_up,
        sum_down,
    )


MESH = pl.DeviceIdType.MESH
F32 = jnp.float32
BF16 = jnp.bfloat16
LINE = 4
PART = 256
PARTS = 4
GELU_A = 0.7978845608028654
GELU_B = 0.044715


def place():
    row, col = lax.axis_index("row"), lax.axis_index("col")
    return row, col // 2, col % 2


def at_line(z, core):
    return {"col": 2 * z + core}


def lanes(part):
    return pl.ds(pl.multiple_of(part * PART, PART), PART)


def rows_of(index, size):
    return pl.ds(pl.multiple_of(index * size, 16), size)


def dot(a, b):
    return lax.dot_general(a, b, (((1,), (0,)), ((), ())), preferred_element_type=F32)


def dot_nt(a, b):
    return lax.dot_general(a, b, (((1,), (1,)), ((), ())), preferred_element_type=F32)


def greet(row, z, core, rows, line):
    barrier = pltpu.get_barrier_semaphore()
    peers = [{"col": 2 * z + (1 - core)}]
    if rows:
        peers += [{"row": row ^ d} for d in (1, 2, 3)]
    if line:
        peers += [at_line(z ^ d, core) for d in (1, 2, 3)]
    for peer in peers:
        pl.semaphore_signal(barrier, inc=1, device_id=peer, device_id_type=MESH)
    pl.semaphore_wait(barrier, len(peers))


def remote(src, dst, send, recv, peer):
    return pltpu.make_async_remote_copy(
        src_ref=src, dst_ref=dst, send_sem=send, recv_sem=recv, device_id=peer, device_id_type=MESH
    )


class Gather:
    def __init__(self, ref, send, recv, z, core, block, back=False):
        self.ref, self.sems, self.z, self.core = ref, (send, recv), z, core
        self.block, self.back = block, back

    def copy(self, way, hop, step, owner, incoming=False):
        part = PARTS - 1 - step if self.back else step
        piece = self.ref.at[rows_of(owner, self.block), lanes(part)]
        peer = at_line(self.z + (1 if (way == 0) != incoming else -1), self.core)
        return remote(piece, piece, self.sems[0].at[way, hop, step], self.sems[1].at[way, hop, step], peer)

    def each(self, hop, act, incoming):
        z = self.z
        if incoming:
            cases = ((0, z - 1 - hop >= 0, z - 1 - hop), (1, z + 1 + hop < LINE, z + 1 + hop))
        else:
            cases = (
                (0, (z >= hop) & (z < LINE - 1), z - hop),
                (1, (z + hop < LINE) & (z >= 1), z + hop),
            )
        for way, here, owner in cases:
            pl.when(here)(functools.partial(act, way, owner))

    def send(self, hop, step):
        self.each(hop, lambda way, owner: self.copy(way, hop, step, owner).start(), False)

    def arrive(self, hop, step):
        self.each(hop, lambda way, owner: self.copy(way, hop, step, owner, True).wait_recv(), True)

    def forward(self, hop, step):
        self.arrive(hop - 1, step)
        self.send(hop, step)

    def sent(self):
        def one(step, carry):
            for hop in range(LINE - 1):
                self.each(hop, lambda way, owner: self.copy(way, hop, step, owner).wait_send(), False)
            return carry

        lax.fori_loop(0, PARTS, one, 0)

    def open(self):
        self.send(0, 0)
        self.forward(1, 0)
        self.send(0, 1)
        self.forward(2, 0)

    def middle(self, step):
        @pl.when(step + 1 < PARTS)
        def _():
            self.forward(1, step + 1)

        @pl.when(step + 2 < PARTS)
        def _():
            self.send(0, step + 2)

    def later(self, step):
        @pl.when(step + 1 < PARTS)
        def _():
            self.forward(2, step + 1)


class Spread:
    def __init__(self, own, held, send, recv, z, core):
        self.own, self.held, self.sems, self.z, self.core = own, held, (send, recv), z, core

    def copy(self, way, step, hop):
        slot = hop if way == 0 else LINE - hop
        there = slot - 1 if way == 0 else slot + 1
        peer = at_line(self.z + (1 if way == 0 else -1), self.core)
        return remote(
            self.held.at[step, slot],
            self.held.at[step, there],
            self.sems[0].at[way, step, hop],
            self.sems[1].at[way, step, hop - 1],
            peer,
        )

    def landed(self, way, step, hop):
        slot = hop if way == 0 else LINE - hop
        piece = self.held.at[step, slot]
        peer = at_line(self.z + (-1 if way == 0 else 1), self.core)
        remote(piece, piece, self.sems[0].at[way, step, hop], self.sems[1].at[way, step, hop], peer).wait_recv()

    def push(self, way, step, first):
        z = self.z

        def one(i, carry):
            hop = LINE - 1 - i
            owner = z + hop if way == 0 else z - hop
            slot = hop if way == 0 else LINE - hop

            @pl.when((owner >= 0) & (owner < LINE))
            def _():
                @pl.when(first)
                def _():
                    self.held[step, slot] = self.own(step, owner)[...].astype(BF16)

                @pl.when(jnp.logical_not(first))
                def _():
                    self.landed(way, step, hop)
                    total = self.own(step, owner)[...].astype(F32) + self.held[step, slot].astype(F32)
                    self.held[step, slot] = total.astype(BF16)

                self.copy(way, step, hop).start()

            return carry

        lax.fori_loop(0, LINE - 1, one, 0)

    def serve(self, t, finish):
        z = self.z
        step = t - (LINE - 1)

        @pl.when((step >= 0) & (step < PARTS))
        def _():
            @pl.when(z == 0)
            def _():
                self.landed(1, step, 0)
                finish(step, lambda a, n: self.mine(step, a, n) + self.got(step, LINE, a, n))

            @pl.when(z == LINE - 1)
            def _():
                self.landed(0, step, 0)
                finish(step, lambda a, n: self.mine(step, a, n) + self.got(step, 0, a, n))

            @pl.when((z > 0) & (z < LINE - 1))
            def _():
                self.landed(0, step, 0)
                self.landed(1, step, 0)
                finish(
                    step,
                    lambda a, n: self.mine(step, a, n) + (self.got(step, 0, a, n) + self.got(step, LINE, a, n)),
                )

        for way, late, turn in ((1, LINE - 1 - z, z < 2), (0, z, z >= 0), (1, LINE - 1 - z, z >= 2)):
            step = t - late
            pl.when((step >= 0) & (step < PARTS) & turn)(functools.partial(self.push, way, step, late == 0))

    def mine(self, step, start, size):
        return self.own(step, self.z)[pl.ds(start, size), :].astype(F32)

    def got(self, step, slot, start, size):
        return self.held[step, slot, pl.ds(start, size)].astype(F32)

    def sent(self):
        z = self.z

        def one(step, carry):
            for way in (0, 1):
                for hop in range(1, LINE):
                    owner = z + hop if way == 0 else z - hop

                    @pl.when((owner >= 0) & (owner < LINE))
                    def _():
                        self.copy(way, step, hop).wait_send()

            return carry

        lax.fori_loop(0, PARTS, one, 0)


def share_line(ref, send, recv, z, core):
    copies = [
        remote(ref.at[z], ref.at[z], send.at[d - 1], recv.at[d - 1], at_line(z ^ d, core)) for d in (1, 2, 3)
    ]
    for copy in copies:
        copy.start()
    for d in (1, 2, 3):
        piece = ref.at[z ^ d]
        remote(piece, piece, send.at[d - 1], recv.at[d - 1], at_line(z ^ d, core)).wait_recv()
    for copy in copies:
        copy.wait_send()


class Weights:
    def __init__(self, src, dst, send, recv, own, row, z, core, turned):
        self.src, self.dst, self.send, self.recv, self.own = src, dst, send, recv, own
        self.row, self.core, self.turned = row, core, turned
        self.sibling = {"col": 2 * z + (1 - core)}

    def spot(self, row, core):
        down, right = (row, core) if self.turned else (core, row)
        rows, cols = self.src.shape
        return self.dst.at[rows_of(down, rows), pl.ds(pl.multiple_of(right * cols, 128), cols)]

    def to_row(self, d):
        return remote(
            self.src, self.spot(self.row, self.core), self.send.at[d], self.recv.at[d], {"row": self.row ^ d}
        )

    def to_sibling(self, d):
        if d == 0:
            return remote(
                self.src, self.spot(self.row, self.core), self.send.at[0], self.recv.at[0], self.sibling
            )
        piece = self.spot(self.row ^ d, self.core)
        return remote(piece, piece, self.send.at[3 + d], self.recv.at[3 + d], self.sibling)

    def local(self):
        return pltpu.make_async_copy(self.src, self.spot(self.row, self.core), self.own)

    def start(self):
        for d in (1, 2, 3):
            self.to_row(d).start()
        self.to_sibling(0).start()
        self.local().start()

    def forward(self):
        for d in (1, 2, 3):
            piece = self.spot(self.row ^ d, self.core)
            remote(piece, piece, self.send.at[d], self.recv.at[d], {"row": self.row ^ d}).wait_recv()
            self.to_sibling(d).start()

    def finish(self):
        self.local().wait()
        for d in (0, 1, 2, 3):
            piece = self.spot(self.row ^ d, 1 - self.core)
            sem = 0 if d == 0 else 3 + d
            remote(piece, piece, self.send.at[sem], self.recv.at[sem], self.sibling).wait_recv()

    def sent(self):
        for d in (1, 2, 3):
            self.to_row(d).wait_send()
            self.to_sibling(d).wait_send()
        self.to_sibling(0).wait_send()


def gelu_parts(b):
    t = jnp.tanh(GELU_A * (b + GELU_B * (b * b * b)))
    half = 0.5 + 0.5 * t
    slope = half + (0.5 * b) * (1.0 - t * t) * (GELU_A + (3.0 * GELU_A * GELU_B) * (b * b))
    return b * half, slope


def blocks(count, body):
    def one(i, carry):
        body(i)
        return carry

    lax.fori_loop(0, count, one, 0)


def scale_of(ref, eps, width):
    total = jnp.sum(jnp.sum(ref[...], axis=0), axis=0, keepdims=True)
    return lax.rsqrt(total / width + eps)


def forward_kernel(
    width, eps,
    x_in, g_in, gain, gain_two, masks, par, gates_hi, gates_lo, br_s, m_s, gu_s, d_s, brn_s, mn_s,
    scale, scale_two, y_out, n1_out, q_out, x_out, g_out, b_out, p_out, u_out, r_out, i_out, h_out,
    result, dn2_out, dev_h, z_h, g_own, g_got, gd_own, gd_got, br_n, m_n,
    sums, sums2, normed, normed2, go, x_own, y, dn2, q_c, p_s, h_s, room, uh, ul,
    own, held, held_n, held_o, gu, gun, down, dt, zs, dev,
    x_send, x_recv, x_loc, l_send, l_recv, n_send, n_recv, g_send, g_recv, e_send, e_recv, f_send, f_recv,
    s_send, s_recv, t_send, t_recv, o_send, o_recv, w_send, w_recv, w_own, k_sem, v_sem, d_send, d_recv, d_own,
):
    row, z, core = place()
    block, seq = y.shape
    half = x_in.shape[0]
    chan = p_s.shape[0]
    hid = zs.shape[0]
    b_s, u_s, r_s, i_s, a_c = [room.at[n * chan : (n + 1) * chan, :] for n in range(5)]
    ev, dz = room.at[0:hid, :], room.at[hid : hid + hid // 2, :]
    hh = hid // 2
    hc = chan // 2
    sibling = {"col": 2 * z + (1 - core)}
    greet(row, z, core, True, True)
    br, mt = gun.at[0 : 2 * chan, 0:width], dt.at[:, 0:chan]
    weights = [
        Weights(src, dst, w_send.at[n], w_recv.at[n], w_own.at[n], row, z, core, n in (1, 4))
        for n, (src, dst) in enumerate(((br_s, br), (m_s, mt), (gu_s, gu), (d_s, down), (brn_s, br_n), (mn_s, m_n)))
    ]
    mine = pl.ds(pl.multiple_of(core * seq, seq), seq)
    other = pl.ds(pl.multiple_of((1 - core) * seq, seq), seq)
    inner = pl.ds(pl.multiple_of(z * block + core * half, 16), half)
    outer = rows_of(core, half)
    swaps = [
        remote(x_in.at[:, other], x_own.at[outer, :], x_send.at[0], x_recv.at[0], sibling),
        remote(g_in.at[:, other], go.at[inner, :], x_send.at[1], x_recv.at[1], sibling),
        pltpu.make_async_copy(x_in.at[:, mine], x_own.at[outer, :], x_loc.at[0]),
        pltpu.make_async_copy(g_in.at[:, mine], go.at[inner, :], x_loc.at[1]),
    ]
    for swap in swaps:
        swap.start()
    for w in weights[:2]:
        w.start()
    for swap in swaps:
        swap.wait()
    flushes = [
        pltpu.make_async_copy(x_own, x_out, v_sem.at[0]),
        pltpu.make_async_copy(go.at[rows_of(z, block), :], g_out, v_sem.at[1]),
    ]
    for flush in flushes:
        flush.start()
    gather = Gather(normed, g_send, g_recv, z, core, block)
    gather_go = Gather(go, e_send, e_recv, z, core, block)
    gather_two = Gather(normed2, f_send, f_recv, z, core, block)
    shares = lambda k, s: own.at[k, s]
    shares_o = lambda k, s: normed.at[rows_of(s, block), lanes(k)]
    spread = Spread(shares, held, s_send, s_recv, z, core)
    spread_n = Spread(shares, held_n, t_send, t_recv, z, core)
    spread_o = Spread(shares_o, held_o, o_send, o_recv, z, core)
    res = x_own
    gather_go.send(0, 0)

    sums[z] = jnp.zeros(sums.shape[1:], F32)

    def squares(i):
        v = x_own[rows_of(i, 16), :].astype(F32)
        v = v * v
        sums[z] += v[:8] + v[8:]

    blocks(block // 16, squares)
    share_line(sums, l_send, l_recv, z, core)
    scale[...] = jnp.broadcast_to(scale_of(sums, eps, width), scale.shape)

    def norm(i):
        v = x_own[rows_of(i, 16), :].astype(F32) * scale[0:1, :] * gain[rows_of(i, 16), :]
        normed[pl.ds(pl.multiple_of(z * block + i * 16, 16), 16), :] = v.astype(BF16)

    blocks(block // 16, norm)
    gather.send(0, 0)
    gather_go.forward(1, 0)
    gather.forward(1, 0)
    gather.send(0, 1)
    gather.forward(2, 0)
    gather_go.forward(2, 0)
    gather_go.send(0, 1)
    p_s[:, PART:] = jnp.zeros((chan, 128), F32)
    h_s[:, PART:] = jnp.zeros((chan, 128), F32)
    pads = [
        pltpu.make_async_copy(src.at[:, PART:], out.at[:, 0:128], v_sem.at[2 + n])
        for n, (src, out) in enumerate(((p_s, p_out), (h_s, h_out)))
    ]
    for pad in pads:
        pad.start()
    weights[0].forward()
    gather_go.forward(1, 1)
    weights[0].finish()
    for pad in pads:
        pad.wait()

    kept = (b_s, p_s, u_s, r_s, i_s, h_s, q_c)
    outs = (b_out, p_out, u_out, r_out, i_out, h_out, q_out)

    def keep(n, part):
        if n in (1, 5):
            at = pl.ds(pl.multiple_of(128 + part * PART, 128), PART)
            return pltpu.make_async_copy(kept[n].at[:, 128:], outs[n].at[:, at], k_sem.at[n])
        return pltpu.make_async_copy(kept[n], outs[n].at[:, lanes(part)], k_sem.at[n])

    def work(k):
        here = lanes(k)

        @pl.when(k > 0)
        def _():
            for n in range(len(kept)):
                keep(n, k - 1).wait()

        p_s[:, 0:128] = p_s[:, PART:]
        h_s[:, 0:128] = h_s[:, PART:]
        n1 = normed[:, here]
        for c in (0, 1):
            b_s[c * hc : (c + 1) * hc, :] = dot(br[c * 2 * hc : c * 2 * hc + hc, :], n1)
            p_s[c * hc : (c + 1) * hc, 128:] = dot(br[c * 2 * hc + hc : (c + 1) * 2 * hc, :], n1)

        def conv(i):
            ch = rows_of(i, 32)
            window = p_s[ch, :]
            pr = par[ch, :]
            u = pr[:, 4:5] + pr[:, 0:1] * window[:, 128:]
            for lag in (1, 2, 3):
                u = u + pr[:, lag : lag + 1] * (pltpu.roll(window, lag, 1)[:, 128:] * masks[lag : lag + 1, here])
            u_s[ch, :] = u
            high = u.astype(BF16)
            uh[ch, :] = high
            ul[ch, :] = (u - high.astype(F32)).astype(BF16)

        blocks(chan // 32, conv)
        gather.middle(k)
        for g in range(chan // 256):
            at = slice(g * 256, (g + 1) * 256)
            pre = dot(gates_hi[g], uh[at, :]) + dot(gates_hi[g], ul[at, :]) + dot(gates_lo[g], uh[at, :])
            r_s[at, :] = pre[:256]
            i_s[at, :] = pre[256:]

        def decay(i):
            ch = rows_of(i, 64)
            pr = par[ch, :]
            start = masks[0:1, here] > 0.5
            r = jax.nn.sigmoid(r_s[ch, :] + pr[:, 5:6])
            gate = jax.nn.sigmoid(i_s[ch, :] + pr[:, 6:7])
            r_s[ch, :] = r
            i_s[ch, :] = gate
            a = jnp.exp(-(r * pr[:, 7:8]))
            m = jnp.where(start, 1.0, jnp.sqrt(1.0 - a * a + FLOOR))
            a_c[ch, :] = jnp.where(start, 0.0, a)
            h_s[ch, 128:] = m * gate * u_s[ch, :]

        blocks(chan // 64, decay)
        first = lax.broadcasted_iota(jnp.int32, (64, PART), 1) == 0

        def recur(i):
            ch = rows_of(i, 64)
            a, h = a_c[ch, :], h_s[ch, 128:]
            h = h + jnp.where(first, a * h_s[ch, 0:128][:, 127:128], 0.0)
            a = jnp.where(first, 0.0, a)
            shift = 1
            while shift < PART:
                h = h + a * pltpu.roll(h, shift, 1)
                if shift * 2 < PART:
                    a = a * pltpu.roll(a, shift, 1)
                shift *= 2
            h_s[ch, 128:] = h

        blocks(chan // 64, recur)
        gather.later(k)

        @pl.when(k == 0)
        def _():
            gather_go.forward(2, 1)
            weights[1].forward()
            for w in weights[2:4]:
                w.start()
            weights[1].finish()

        def mixed(i):
            ch = rows_of(i, 64)
            b = b_s[ch, :]
            t = jnp.tanh(GELU_A * (b + GELU_B * (b * b * b)))
            q_c[ch, :] = (b * (0.5 + 0.5 * t) * h_s[ch, 128:]).astype(BF16)

        blocks(chan // 64, mixed)
        qk = q_c[...]
        for s in range(LINE):
            own[k, s] = dot(mt[s * block : (s + 1) * block, :], qk).astype(own.dtype)
        for n in range(len(kept)):
            keep(n, k).start()

    def finish(k, total):
        def add(i):
            at = pl.multiple_of(i * 16, 16)
            y[pl.ds(at, 16), lanes(k)] = x_own[pl.ds(at, 16), lanes(k)].astype(F32) + total(at, 16)

        blocks(block // 16, add)

    def step(t, carry):
        gather.arrive(2, t)
        work(t)
        spread.serve(t, finish)
        return carry

    lax.fori_loop(0, PARTS, step, 0)

    def square(k):
        sums2[k, z] = jnp.zeros(sums2.shape[2:], F32)

        def one(i):
            v = y[rows_of(i, 16), lanes(k)]
            v = v * v
            sums2[k, z] += v[:8] + v[8:]

        blocks(block // 16, one)
        for d in (1, 2, 3):
            share(k, d).start()

    def share(k, d):
        return remote(
            sums2.at[k, z], sums2.at[k, z], n_send.at[k, d - 1], n_recv.at[k, d - 1], at_line(z ^ d, core)
        )

    def norm_two(k):
        for d in (1, 2, 3):
            piece = sums2.at[k, z ^ d]
            remote(piece, piece, n_send.at[k, d - 1], n_recv.at[k, d - 1], at_line(z ^ d, core)).wait_recv()
        s2 = scale_of(sums2.at[k], eps, width)
        scale_two[:, lanes(k)] = jnp.broadcast_to(s2, (8, PART))

        def one(i):
            at = rows_of(i, 16)
            v = y[at, lanes(k)] * scale_two[0:1, lanes(k)] * gain_two[at, :]
            normed2[pl.ds(pl.multiple_of(z * block + i * 16, 16), 16), lanes(k)] = v.astype(BF16)

        blocks(block // 16, one)

    square(0)
    for w in weights[:2]:
        w.sent()
    for w in weights[4:]:
        w.start()
    for n in range(len(kept)):
        keep(n, PARTS - 1).wait()
    flush_n = pltpu.make_async_copy(normed, n1_out, v_sem.at[4])
    flush_n.start()
    gather_go.send(0, 2)
    spread.serve(PARTS, finish)
    norm_two(0)
    gather_two.send(0, 0)
    square(1)
    gather_go.forward(1, 2)
    for w in weights[2:4]:
        w.forward()
    spread.serve(PARTS + 1, finish)
    norm_two(1)
    gather_two.forward(1, 0)
    gather_two.send(0, 1)
    square(2)
    weights[3].finish()

    def turn_down(i):
        at = pl.ds(pl.multiple_of(i * 128, 128), 128)
        dt[:, at] = down[at, :].T

    blocks(hid // 128, turn_down)
    spread.serve(PARTS + 2, finish)
    gather.sent()
    for flush in flushes + [flush_n]:
        flush.wait()
    gather_two.forward(2, 0)
    gather_go.forward(2, 2)
    norm_two(2)
    square(3)
    weights[2].finish()

    def turn_up(i):
        at = pl.ds(pl.multiple_of(i * 128, 128), 128)
        gun[:, at] = gu[at, :].T

    blocks(2 * hid // 128, turn_up)
    norm_two(3)
    gather_go.send(0, 3)

    def keep_dev(k):
        return pltpu.make_async_copy(dev, dev_h.at[:, lanes(k)], v_sem.at[5])

    def keep_z(k):
        return pltpu.make_async_copy(zs, z_h.at[:, lanes(k)], v_sem.at[6])

    def feed(k):
        here = lanes(k)
        n2 = normed2[:, here]

        @pl.when(k > 0)
        def _():
            keep_dev(k - 1).wait()
            keep_z(k - 1).wait()

        for c in range(2):
            for e in range(2):
                ev[e * hh : (e + 1) * hh, :] = dot(gu[(2 * c + e) * hh : (2 * c + e + 1) * hh, :], n2)
            if c == 0:
                gather_two.middle(k)
                pl.when(k == 0)(lambda: gather_go.forward(1, 3))
                gather_go.arrive(2, k)
            dz[...] = dot(down[c * hh : (c + 1) * hh, :], go[:, here])

            def one(i):
                off = pl.multiple_of(i * 64, 64)
                e = ev[pl.ds(off, 64), :]
                v = ev[pl.ds(hh + off, 64), :]
                d = dz[pl.ds(off, 64), :]
                act, slope = gelu_parts(e)
                zs[pl.ds(c * hh + off, 64), :] = (act * v).astype(BF16)
                dev[pl.ds(c * 2 * hh + off, 64), :] = (d * v * slope).astype(BF16)
                dev[pl.ds(c * 2 * hh + hh + off, 64), :] = (d * act).astype(BF16)

            blocks(hh // 64, one)
        gather_two.later(k)
        pl.when(k == 0)(lambda: gather_go.forward(2, 3))
        dk = dev[...]
        for s in range(LINE):
            own[k, s] = dot(gun[s * block : (s + 1) * block, :], dk).astype(own.dtype)
        spread_n.serve(k, finish_n)
        zk = zs[...]
        for s in range(LINE):
            normed[s * block : (s + 1) * block, here] = dot(dt[s * block : (s + 1) * block, :], zk).astype(BF16)
        spread_o.serve(k, finish_o)
        keep_dev(k).start()
        keep_z(k).start()

    def finish_o(k, total):
        def add(i):
            at = pl.multiple_of(i * 16, 16)
            res[pl.ds(at, 16), lanes(k)] = (y[pl.ds(at, 16), lanes(k)] + total(at, 16)).astype(BF16)

        blocks(block // 16, add)

    def keep_n(k):
        return pltpu.make_async_copy(dn2, dn2_out.at[:, lanes(k)], v_sem.at[3])

    def finish_n(k, total):
        @pl.when(k > 0)
        def _():
            keep_n(k - 1).wait()

        def add(i):
            at = pl.multiple_of(i * 16, 16)
            dn2[pl.ds(at, 16), :] = total(at, 16)

        blocks(block // 16, add)
        keep_n(k).start()

    def feed_step(t, carry):
        gather_two.arrive(2, t)
        feed(t)
        pl.when(t == 2)(weights[4].forward)
        pl.when(t == 3)(weights[5].forward)
        return carry

    lax.fori_loop(0, PARTS, feed_step, 0)
    for w in weights[2:4]:
        w.sent()
    keep_dev(PARTS - 1).wait()
    keep_z(PARTS - 1).wait()
    dev_all, z_all = gu.at[:, 0:seq], dt.at[0:hid, 0:seq]
    loads = [pltpu.make_async_copy(dev_h, dev_all, v_sem.at[5]), pltpu.make_async_copy(z_h, z_all, v_sem.at[6])]
    for load in loads:
        load.start()
    for load in loads:
        load.wait()

    def columns(start):
        return pl.ds(pl.multiple_of(start, 128), block)

    def place_up(j):
        side = jnp.where(j >= 3, core, 1 - core)
        return side * hid + (j % 3) * block, columns((j % 3) * block)

    def send_up(j):
        at, to = place_up(j)
        return remote(gun.at[:, columns(at)], g_got.at[:, to], d_send.at[j], d_recv.at[j], sibling)

    def keep_up(j):
        at, to = place_up(j)
        return pltpu.make_async_copy(gun.at[:, columns(at)], g_own.at[:, to], d_own.at[j - 3])

    def send_down():
        return remote(down.at[rows_of(1 - core, hh), :], gd_got, d_send.at[3], d_recv.at[3], sibling)

    def keep_down():
        return pltpu.make_async_copy(down.at[rows_of(core, hh), :], gd_own, d_own.at[3])

    def grad_up(j):
        at = place_up(j)[0]
        right = pl.ds(pl.multiple_of(at, 16), block)
        for low in (0, width // 2):
            piece = slice(low, low + width // 2)
            gun[piece, columns(at)] = dot_nt(normed2[piece, :], dev_all[right, :]).astype(BF16)

        @pl.when(j < 3)
        def _():
            send_up(j).start()

        @pl.when(j >= 3)
        def _():
            keep_up(j).start()

    def grad_down(side):
        at = rows_of(side, hh)
        down[at, :] = dot_nt(z_all[at, :], go[...]).astype(BF16)

    def drain(i, carry):
        t = PARTS + i
        blocks(2, lambda j: grad_up(2 * i + j))
        spread_n.serve(t, finish_n)
        spread_o.serve(t, finish_o)

        @pl.when(i < 2)
        def _():
            grad_down(jnp.where(i == 0, 1 - core, core))

        pl.when(i == 0)(lambda: send_down().start())
        pl.when(i == 1)(lambda: keep_down().start())
        return carry

    lax.fori_loop(0, LINE - 1, drain, 0)
    last = [
        remote(res.at[rows_of(1 - core, half), :], result.at[:, mine], x_send.at[0], x_recv.at[0], sibling),
        pltpu.make_async_copy(res.at[rows_of(core, half), :], result.at[:, mine], x_loc.at[0]),
        pltpu.make_async_copy(y, y_out, v_sem.at[2]),
        keep_n(PARTS - 1),
    ]
    for copy in last[:3]:
        copy.start()
    for w in weights[4:]:
        w.finish()
        w.sent()
    for one in (gather_go, gather_two, spread, spread_n, spread_o):
        one.sent()
    for k in range(PARTS):
        for d in (1, 2, 3):
            share(k, d).wait_send()
    for j in range(3):
        keep_up(j + 3).wait()
        send_up(j).wait()
    keep_down().wait()
    send_down().wait()
    for copy in last:
        copy.wait()


def back_kernel(
    width,
    y, dn2_h, g_h, x_own, scale_two, scale_one, gain_two, gain_one, masks, par, gates_t, m_h, br_h,
    b_h, p_h, u_h, r_h, i_h, h_h, q_h, n1_h, f_own, f_got, fd_own, fd_got,
    input_grad, tiny_v, tiny_g, f_sum, f_land, fd_sum, fd_land, g_sum, g_land, gm_sum, gm_land,
    sums, sums2, coef, m_n, br_n, b_s, p_s, u_s, r_s, i_s, h_s, dyf, dbp, dy, dn1, dq, du, dri, a_c, l_c, carry_s, own, held,
    qv, f_a, f_b, fd_a, fd_b, feed_part, mix_part, small, gate_grad, g_s, g_got, gm_got,
    vec, vec_in, vec_all, gd, gd_in, gd_all,
    c_sem, k_sem, l_send, l_recv, l2_send, l2_recv, g_send, g_recv, s_send, s_recv, r_send, r_recv,
    f_sem, f_send, f_recv, d_send, d_recv, d_own, q_send, q_recv, n_send, n_recv, v_send, v_recv,
):
    row, z, core = place()
    block, seq = y.shape
    half = block // 2
    chan = b_s.shape[1]
    hc = chan // 2
    sibling = {"col": 2 * z + (1 - core)}
    greet(row, z, core, True, True)
    load_g = pltpu.make_async_copy(g_h, g_s, c_sem.at[0])
    load_g.start()
    dn2 = dn1
    load_d = pltpu.make_async_copy(dn2_h, dn2, c_sem.at[5])
    load_d.start()
    load_m = pltpu.make_async_copy(m_h, m_n, c_sem.at[1])
    load_m.start()
    load_b = pltpu.make_async_copy(br_h, br_n, c_sem.at[2])
    load_b.start()
    load_q = pltpu.make_async_copy(q_h, qv, c_sem.at[3])
    n1 = dyf
    load_n = pltpu.make_async_copy(n1_h, n1, c_sem.at[4])
    kept = (b_s, p_s, u_s, r_s, i_s, h_s)
    srcs = (b_h, p_h, u_h, r_h, i_h, h_h)

    def fetch(n, part):
        if kept[n] is p_s or kept[n] is h_s:
            at = pl.ds(pl.multiple_of(part * PART, 128), PART + 128)
        else:
            at = lanes(part)
        return pltpu.make_async_copy(srcs[n].at[:, at], kept[n].at[part % 2], k_sem.at[n, part % 2])

    def fetch_all(part):
        for n in range(len(kept)):
            fetch(n, part).start()

    fetch_all(PARTS - 1)
    load_q.start()
    du[:, 0:128] = jnp.zeros((chan, 128), F32)
    carry_s[...] = jnp.zeros(carry_s.shape, F32)
    small[...] = jnp.zeros(small.shape, F32)
    gate_grad[...] = jnp.zeros(gate_grad.shape, F32)

    sums[z] = jnp.zeros(sums.shape[1:], F32)

    load_d.wait()

    def inner(i):
        at = rows_of(i, 16)
        d, v = dn2[at, :], y[at, :]
        w = d * v
        c = w * gain_two[at, :]
        sums[z] += c[:8] + c[8:]
        w = w * scale_two[0:1, :]
        fold = w[:, 0:128]
        for j in range(1, seq // 128):
            fold = fold + w[:, j * 128 : (j + 1) * 128]
        feed_part[at, :] = fold

    blocks(block // 16, inner)
    share_line(sums, l_send, l_recv, z, core)
    load_g.wait()
    total = jnp.sum(jnp.sum(sums[...], axis=0), axis=0, keepdims=True)
    s2 = scale_two[0:1, :]
    coef[0:1, :] = s2 * s2 * s2 * (total / width)

    def outer(i):
        at = rows_of(i, 16)
        v = g_s[at, :].astype(F32) + (scale_two[0:1, :] * (gain_two[at, :] * dn2[at, :]) - y[at, :] * coef[0:1, :])
        dy[at, :] = v
        dyf[pl.ds(pl.multiple_of(z * block + i * 16, 16), 16), :] = v.astype(BF16)

    blocks(block // 16, outer)
    gather = Gather(dyf, g_send, g_recv, z, core, block, back=True)
    spread = Spread(lambda k, s: own.at[k, s], held, s_send, s_recv, z, core)
    gather.open()
    load_m.wait()
    load_b.wait()
    final = lax.broadcasted_iota(jnp.int32, (64, PART), 1) == PART - 1

    f_arrays = ((f_own, f_got, f_a, f_b, f_sum, f_land), (fd_own, fd_got, fd_a, fd_b, fd_sum, fd_land))

    def f_loads(d):
        pulls = []
        for n, (ours, theirs, a, b, _, _) in enumerate(f_arrays):
            if n == 0:
                piece = (rows_of(row ^ d, block), slice(None))
            else:
                piece = (slice(None), pl.ds(pl.multiple_of((row ^ d) * block, 128), block))
            pulls.append(pltpu.make_async_copy(ours.at[piece], a.at[d], f_sem.at[n, 0]))
            pulls.append(pltpu.make_async_copy(theirs.at[piece], b, f_sem.at[n, 1]))
        return pulls

    def f_out(d):
        outs = []
        for n, (_, _, a, _, kept_at, land) in enumerate(f_arrays):
            if d == 0:
                outs.append(pltpu.make_async_copy(a.at[0], kept_at, f_send.at[n, 0]))
            else:
                outs.append(
                    remote(a.at[d], land.at[d - 1], f_send.at[n, d], f_recv.at[n, d], {"row": row ^ d})
                )
        return outs

    def f_part(d):
        for pull in f_loads(d):
            pull.wait()
        for _, _, a, b, _, _ in f_arrays:

            def add(i):
                at = rows_of(i, 16)
                a[d, at, :] = (a[d, at, :].astype(F32) + b[at, :].astype(F32)).astype(BF16)

            blocks(b.shape[0] // 16, add)
        for out in f_out(d):
            out.start()
        if d > 0:
            for pull in f_loads(d - 1):
                pull.start()

    def f_step(t):
        for d in range(PARTS):
            pl.when(t == PARTS - 1 - d)(functools.partial(f_part, d))

    for pull in f_loads(PARTS - 1):
        pull.start()

    def fold2(v):
        return v[:, 0:128] + v[:, 128:256]

    def work(t):
        k = PARTS - 1 - t
        here = lanes(k)
        wide = pl.ds(pl.multiple_of(k * PART, 128), PART + 128)
        slot = k % 2
        for n in range(len(kept)):
            fetch(n, k).wait()

        @pl.when(k > 0)
        def _():
            fetch_all(k - 1)

        dq[...] = dot(m_n[...], dyf[:, here])

        def before(i):
            ch = rows_of(i, 64)
            c = i // (hc // 64)
            low = pl.ds(pl.multiple_of(c * hc + i * 64, 64), 64)
            pr = par[ch, :]
            d = dq[ch, :]
            act, slope = gelu_parts(b_s[slot, ch, :])
            dbp[low, here] = (d * h_s[slot, ch, :][:, 128:] * slope).astype(BF16)
            l_c[ch, :] = d * act
            a_c[ch, :] = jnp.exp(-(r_s[slot, ch, :] * pr[:, 7:8]))

        blocks(chan // 64, before)
        gather.middle(t)

        def recur(i):
            ch = rows_of(i, 64)
            start = masks[0:1, here] > 0.5
            a, lam = jnp.where(start, 0.0, a_c[ch, :]), l_c[ch, :]
            lam = lam + jnp.where(final, carry_s[ch, :][:, 0:1], 0.0)
            w = jnp.where(final, 0.0, pltpu.roll(a, PART - 1, 1))
            shift = 1
            while shift < PART:
                lam = lam + w * pltpu.roll(lam, PART - shift, 1)
                if shift * 2 < PART:
                    w = w * pltpu.roll(w, PART - shift, 1)
                shift *= 2
            carry_s[ch, :] = jnp.broadcast_to((a * lam)[:, 0:1], (64, 128))
            l_c[ch, :] = lam

        blocks(chan // 64, recur)
        f_step(t)
        gather.later(t)

        def after(i):
            ch = rows_of(i, 32)
            du[ch, PART:] = du[ch, 0:128]
            pr = par[ch, :]
            start = masks[0:1, here] > 0.5
            lam, a0 = l_c[ch, :], a_c[ch, :]
            earlier = pltpu.roll(h_s[slot, ch, :], 1, 1)[:, 128:]
            r, gate, u = r_s[slot, ch, :], i_s[slot, ch, :], u_s[slot, ch, :]
            m0 = jnp.sqrt(1.0 - a0 * a0 + FLOOR)
            m = jnp.where(start, 1.0, m0)
            lm = lam * m
            lu = lam * u
            du[ch, 0:PART] = lm * gate
            da = jnp.where(start, 0.0, lam * earlier - (lu * gate) * (a0 / m0)) * a0
            dr = da * (-pr[:, 7:8]) * (r * (1.0 - r))
            di = lu * m * (gate * (1.0 - gate))
            g, o = i // 8, (i % 8) * 32
            dri[pl.ds(pl.multiple_of(g * 512 + o, 32), 32), :] = dr.astype(BF16)
            dri[pl.ds(pl.multiple_of(g * 512 + 256 + o, 32), 32), :] = di.astype(BF16)
            small[5, ch, :] += fold2(dr)
            small[6, ch, :] += fold2(di)
            small[7, ch, :] += fold2(da * r)

        blocks(chan // 32, after)
        for g in range(chan // 256):
            at = slice(g * 256, (g + 1) * 256)
            dd = dri[g * 512 : (g + 1) * 512, :]
            du[at, 0:PART] += dot(gates_t[g], dd)
            gate_grad[g] += dot_nt(u_s[slot, at, :].astype(BF16), dd)

        def conv(i):
            ch = rows_of(i, 32)
            c = i // (hc // 32)
            low = pl.ds(pl.multiple_of((c + 1) * hc + i * 32, 32), 32)
            pr = par[ch, :]
            follow = du[ch, :]
            window = p_s[slot, ch, :]
            d = follow[:, :PART]
            dp = pr[:, 0:1] * d
            small[4, ch, :] += fold2(d)
            small[0, ch, :] += fold2(d * window[:, 128:])
            for lag in (1, 2, 3):
                kd = follow * masks[lag : lag + 1, wide]
                dp = dp + pr[:, lag : lag + 1] * pltpu.roll(kd, PART + 128 - lag, 1)[:, :PART]
                small[lag, ch, :] += fold2(kd[:, :PART] * pltpu.roll(window, lag, 1)[:, 128:])
            dbp[low, here] = dp.astype(BF16)

        blocks(chan // 32, conv)
        dk = dbp[:, here]
        for s in range(LINE):
            own[t, s] = dot(br_n[s * block : (s + 1) * block, :], dk).astype(own.dtype)

    def finish(t, total):
        k = PARTS - 1 - t

        def add(i):
            at = pl.multiple_of(i * 16, 16)
            dn1[pl.ds(at, 16), lanes(k)] = total(at, 16)

        blocks(block // 16, add)

    def step(t, carry):
        gather.arrive(2, t)
        work(t)
        spread.serve(t, finish)
        return carry

    lax.fori_loop(0, PARTS, step, 0)
    load_q.wait()

    lru = hc

    def cols_of(side):
        return pl.ds(pl.multiple_of(side * 2 * lru, 128), 2 * lru)

    def send_br():
        return remote(br_n.at[:, cols_of(1 - core)], g_got, d_send.at[0], d_recv.at[0], sibling)

    def send_m():
        return remote(m_n.at[rows_of(1 - core, lru), :], gm_got, d_send.at[1], d_recv.at[1], sibling)

    def grad_br(side):
        br_n[:, cols_of(side)] = dot_nt(n1[...], dbp[rows_of(side, 2 * lru), :]).astype(BF16)

    def out_br(d):
        piece = br_n.at[rows_of(row ^ d, block), cols_of(core)]
        if d == 0:
            return pltpu.make_async_copy(piece, g_sum, d_own.at[0])
        return remote(piece, g_land.at[d - 1], q_send.at[0, d - 1], q_recv.at[0, d - 1], {"row": row ^ d})

    def out_m(d):
        piece = m_n.at[rows_of(core, lru), pl.ds(pl.multiple_of((row ^ d) * block, 128), block)]
        if d == 0:
            return pltpu.make_async_copy(piece, gm_sum, d_own.at[1])
        return remote(piece, gm_land.at[d - 1], q_send.at[1, d - 1], q_recv.at[1, d - 1], {"row": row ^ d})

    def drain(i, carry):
        t = PARTS + i

        @pl.when(i == 0)
        def _():
            m_n[...] = dot_nt(qv[...], dyf[...]).astype(BF16)
            send_m().start()
            gather.sent()
            load_n.start()
            load_n.wait()
            grad_br(1 - core)
            send_br().start()

        @pl.when(i == 1)
        def _():
            grad_br(core)
            send_m().wait_recv()

            def add(j):
                at = rows_of(j, 32)
                to = pl.ds(pl.multiple_of(core * lru + j * 32, 32), 32)
                m_n[to, :] = (m_n[to, :].astype(F32) + gm_got[at, :].astype(F32)).astype(BF16)

            blocks(lru // 32, add)
            for d in (3, 2, 1, 0):
                out_m(d).start()

        @pl.when(i == 2)
        def _():
            send_br().wait_recv()

            def add(j):
                at = rows_of(j, 32)
                br_n[at, cols_of(core)] = (br_n[at, cols_of(core)].astype(F32) + g_got[at, :].astype(F32)).astype(BF16)

            blocks(width // 32, add)
            for d in (3, 2, 1, 0):
                out_br(d).start()

        spread.serve(t, finish)
        return carry

    lax.fori_loop(0, LINE - 1, drain, 0)
    mine = pl.ds(pl.multiple_of(core * seq, seq), seq)
    for side in (0, 1):
        for e in range(4):
            at = slice(e * 64, (e + 1) * 64)
            gd[side, at, 0:64] = gate_grad[side, at, e * 64 : (e + 1) * 64]
            gd[side, at, 64:128] = gate_grad[side, at, 256 + e * 64 : 256 + (e + 1) * 64]
    swap_gd = remote(gd.at[1 - core], gd_in, v_send.at[0], v_recv.at[0], sibling)
    swap_gd.start()
    lane = lax.broadcasted_iota(jnp.int32, (64, 128), 1)

    def columns(parts, at):
        total = jnp.zeros((64, 128), F32)
        for n, part in enumerate(parts):
            total = total + jnp.where(lane == n, jnp.sum(part(at), axis=1, keepdims=True), 0.0)
        return total

    vec[...] = jnp.zeros(vec.shape, F32)
    for j in range(chan // 64):
        at = slice(j * 64, (j + 1) * 64)
        v = columns([lambda at, n=n: small[n, at, :] for n in range(8)], at)
        vec[0, :, at] = v.T[0:8, :]

    sums2[z] = jnp.zeros(sums2.shape[1:], F32)

    def inner_one(i):
        at = rows_of(i, 16)
        w = dn1[at, :] * x_own[at, :].astype(F32)
        c = w * gain_one[at, :]
        sums2[z] += c[:8] + c[8:]
        w = w * scale_one[0:1, :]
        fold = w[:, 0:128]
        for j in range(1, seq // 128):
            fold = fold + w[:, j * 128 : (j + 1) * 128]
        mix_part[at, :] = fold

    blocks(block // 16, inner_one)
    share_line(sums2, l2_send, l2_recv, z, core)
    total = jnp.sum(jnp.sum(sums2[...], axis=0), axis=0, keepdims=True)
    s1 = scale_one[0:1, :]
    coef[0:1, :] = s1 * s1 * s1 * (total / width)

    def last(i):
        at = rows_of(i, 16)
        v = dy[at, :] + (
            scale_one[0:1, :] * (gain_one[at, :] * dn1[at, :]) - x_own[at, :].astype(F32) * coef[0:1, :]
        )
        dy[at, :] = v

    blocks(block // 16, last)
    back = remote(dy.at[rows_of(1 - core, half), :], input_grad.at[:, mine], r_send, r_recv, sibling)
    back.start()
    keep_in = pltpu.make_async_copy(dy.at[rows_of(core, half), :], input_grad.at[:, mine], d_own.at[3])
    keep_in.start()
    for j in range(block // 64):
        at = slice(j * 64, (j + 1) * 64)
        v = columns([lambda at: mix_part[at, :], lambda at: feed_part[at, :]], at)
        vec[1, :, at] = v.T[0:8, :]
    swap_vec = remote(vec, vec_in, v_send.at[1], v_recv.at[1], sibling)
    swap_vec.start()
    swap_gd.wait()
    gd_all[0] = gd[core] + gd_in[...]
    rows_gd = [
        remote(gd_all.at[0], gd_all.at[d], n_send.at[0, d - 1], n_recv.at[0, d - 1], {"row": row ^ d}) for d in (1, 2, 3)
    ]
    for copy in rows_gd:
        copy.start()
    swap_vec.wait()
    vec_all[0] = vec[...] + vec_in[...]
    rows_vec = [
        remote(vec_all.at[0], vec_all.at[d], n_send.at[1, d - 1], n_recv.at[1, d - 1], {"row": row ^ d}) for d in (1, 2, 3)
    ]
    for copy in rows_vec:
        copy.start()
    spread.sent()
    for copy in rows_gd + rows_vec:
        copy.wait()
    for every, out in ((gd_all, tiny_g), (vec_all, tiny_v)):
        first, second = every[row % 2], every[1 - row % 2]
        third, fourth = every[2 + row % 2], every[3 - row % 2]
        out[...] = (first + second) + (third + fourth)
    for d in range(PARTS):
        for out in f_out(d):
            out.wait()
    send_br().wait_send()
    send_m().wait_send()
    for d in (0, 1, 2, 3):
        out_br(d).wait()
        out_m(d).wait()
    for copy in (keep_in, back):
        copy.wait()


def last_kernel(
    f_sum, f_land, fd_sum, fd_land, g_sum, g_land, gm_sum, gm_land, tiny_v, tiny_g, lambdas,
    s_b, s_r, s_m, s_g, s_u, s_d, taps, offs, bias_r, bias_a, decay, mix, feed, retain, admit,
):
    core = place()[2]
    lru, block = s_m.shape
    ff, half = s_d.shape[0], mix.shape[1]

    def four(first, others, at):
        return first[at, :].astype(F32) + others[0, at, :].astype(F32) + (
            others[1, at, :].astype(F32) + others[2, at, :].astype(F32)
        )

    def put_gu(i):
        at = rows_of(i, 32)
        v = four(f_sum, f_land, at)
        s_g[at, :] = v[:, :ff]
        s_u[at, :] = v[:, ff:]
        v = four(g_sum, g_land, at)
        s_b[at, :] = v[:, :lru]
        s_r[at, :] = v[:, lru:]

    blocks(block // 32, put_gu)

    def put_d(i):
        at = rows_of(i, 32)
        s_d[at, :] = four(fd_sum, fd_land, at)

    blocks(ff // 32, put_d)

    def put_m(i):
        at = rows_of(i, 32)
        s_m[at, :] = four(gm_sum, gm_land, at)

    blocks(lru // 32, put_m)
    small = tiny_v[0, :, pl.ds(pl.multiple_of(core * lru, 128), lru)]
    taps[...] = small[0:4]
    offs[...] = small[4:5]
    bias_r[...] = small[5:6]
    bias_a[...] = small[6:7]
    decay[...] = small[7:8] * (8.0 * jax.nn.sigmoid(-lambdas[...]))
    gains = jnp.where(core == 0, tiny_v[1, :, 0:half], tiny_v[1, :, half : 2 * half])
    mix[...] = gains[0:1]
    feed[...] = gains[1:2]
    for e in range(retain.shape[0]):
        at = slice(e * 64, (e + 1) * 64)
        retain[e] = tiny_g[at, 0:64]
        admit[e] = tiny_g[at, 64:128]


ANY = pl.BlockSpec(memory_space=pl.ANY)
VM = pl.BlockSpec(memory_space=pltpu.VMEM)
DMA = pltpu.SemaphoreType.DMA
ROOM = 62 * 1024 * 1024


def shape(dims, kind):
    return jax.ShapeDtypeStruct(dims, kind)


def call(kernel, ins, outs, scratch, ident, name, flops):
    return pl.pallas_call(
        kernel,
        out_shape=[o[0] for o in outs],
        in_specs=ins,
        out_specs=[o[1] for o in outs],
        scratch_shapes=scratch,
        name=name,
        compiler_params=pltpu.CompilerParams(
            collective_id=ident, has_side_effects=True, vmem_limit_bytes=ROOM
        ),
        cost_estimate=pl.CostEstimate(flops=flops, bytes_accessed=40000000, transcendentals=0),
    )


PAIRS = [[0, 1], [2, 3], [4, 5], [6, 7]]


def diagonal(w, size):
    per = size // w.shape[1]
    w = w.reshape(-1, per, w.shape[1], w.shape[2])
    eye = jnp.eye(per, dtype=w.dtype)
    full = w[:, :, :, None, :] * eye[None, :, None, :, None]
    return full.reshape(-1, size, size)


def fast_body(
    inputs, segments, mix_gain, branch_weight, recur_weight, kernel, offsets, retain_weight, retain_bias,
    admit_weight, admit_bias, lambdas, merge_weight, feed_gain, gate_weight, up_weight, down_weight, cotangent,
):
    half, tokens = inputs.shape
    block, seq, width = 2 * half, tokens // 2, D
    lru, heads = branch_weight.shape[1], retain_weight.shape[0]
    chan = 2 * lru
    ff = gate_weight.shape[1]
    hid = 2 * ff
    rows = branch_weight.shape[0]
    cols = merge_weight.shape[1]
    core = lax.axis_index("col") % 2

    parts = (mix_gain, feed_gain, kernel[0], kernel[1], kernel[2], kernel[3], offsets, retain_bias, admit_bias, lambdas)
    parts = parts + (retain_weight.reshape(-1), admit_weight.reshape(-1))
    both = lax.all_gather(jnp.concatenate(parts), "col", axis=0, axis_index_groups=PAIRS)
    whole, at = [], 0
    for part in parts:
        whole.append(both[:, at : at + part.shape[0]].reshape(-1))
        at += part.shape[0]
    gain_one, gain_two = whole[0][:, None], whole[1][:, None]
    lam = whole[9]
    rate = 8.0 * jax.nn.softplus(-lam)
    par = jnp.stack(whole[2:6] + whole[6:9] + [rate] + [jnp.zeros_like(lam)] * 8, axis=1)
    retain = diagonal(whole[10].reshape(-1, 64, 64), 256)
    admit = diagonal(whole[11].reshape(-1, 64, 64), 256)
    gates = jnp.concatenate([retain, admit], axis=2)
    gates_hi = gates.astype(BF16)
    gates_lo = (gates - gates_hi.astype(F32)).astype(BF16)
    flip = lambda w: jnp.swapaxes(w, 1, 2)

    segs = lax.dynamic_slice(segments, (core * seq,), (seq,))
    masks = [jnp.concatenate([jnp.ones((1,), bool), segs[1:] != segs[:-1]])]
    for lag in (1, 2, 3):
        masks.append(jnp.concatenate([jnp.zeros((lag,), bool), segs[lag:] == segs[:-lag]]))
    masks = jnp.pad(jnp.stack(masks).astype(F32), ((0, 4), (0, 128)))

    br_s = jnp.concatenate([branch_weight, recur_weight], axis=1).T
    m_s = merge_weight.T
    gu_s = jnp.concatenate([gate_weight, up_weight], axis=1).T

    f_tok = lambda n, kind=F32: shape((n, seq), kind)
    padded = (shape((chan, 128 + seq), F32), ANY)
    state = [(f_tok(chan), ANY), padded, *[(f_tok(chan), ANY)] * 3, padded]
    line = [DMA((3,)), DMA((3,))]
    steps = [DMA((2, 3, PARTS)), DMA((2, 3, PARTS))]
    sums = [DMA((2, PARTS, LINE)), DMA((2, PARTS, LINE))]
    held = pltpu.VMEM((PARTS, LINE + 1, block, PART), BF16)
    own_low = pltpu.VMEM((PARTS, LINE, block, PART), BF16)
    tok = lambda n, kind=F32, lead=0: pltpu.VMEM((n, lead + seq), kind)
    one = lambda n, kind=F32, lead=0: pltpu.VMEM((n, lead + PART), kind)
    br_t = jnp.concatenate([branch_weight, recur_weight], axis=1)
    grad_gu, grad_d = (shape((width, 2 * ff), BF16), ANY), (shape((ff, width), BF16), ANY)
    low = lambda n, m: (shape((n, m), BF16), ANY)

    (scale_one, scale_two, y, n1, q, x_own, g, b, p, u, r, i, h, result, dn2, _, _, f_own, f_got, fd_own, fd_got,
     br_n, m_n) = call(
        functools.partial(forward_kernel, width, EPS),
        [ANY] * 2 + [VM] * 6 + [ANY] * 6,
        [(f_tok(8), VM), (f_tok(8), VM), (f_tok(block), ANY), low(width, seq), low(chan, seq), low(block, seq), low(block, seq)]
        + state + [low(half, tokens), (f_tok(block), ANY), low(2 * hid, seq), low(hid, seq), grad_gu, grad_gu, grad_d, grad_d,
                   low(width, 2 * chan), low(chan, width)],
        [pltpu.VMEM((LINE, 8, seq), F32), pltpu.VMEM((PARTS, LINE, 8, PART), F32), tok(width, BF16), tok(width, BF16),
         tok(width, BF16), tok(block, BF16), tok(block), one(block), one(chan, BF16),
         one(chan, F32, 128), one(chan, F32, 128), one(5 * chan), one(chan, BF16), one(chan, BF16),
         own_low, held, held, held, pltpu.VMEM((2 * hid, width), BF16), pltpu.VMEM((width, 2 * hid), BF16),
         pltpu.VMEM((hid, width), BF16), pltpu.VMEM((width, hid), BF16), one(hid, BF16), one(2 * hid, BF16),
         DMA((2,)), DMA((2,)), DMA((2,))] + line + [DMA((PARTS, 3)), DMA((PARTS, 3))] + steps * 3 + sums * 3
        + [DMA((6, 7)), DMA((6, 7)), DMA((6,)), DMA((7,)), DMA((7,)), DMA((4,)), DMA((4,)), DMA((4,))],
        0, "forward", 50 * 10**9,
    )(inputs, cotangent, gain_one, gain_two, masks, par, flip(gates_hi), flip(gates_lo), br_s, m_s, gu_s, down_weight,
      br_t, merge_weight)

    pair = lambda lead=0: pltpu.VMEM((2, chan, lead + PART), F32)
    land = lambda n, m: ((shape((n, m), BF16), ANY), (shape((3, n, m), BF16), ANY))
    input_grad, tiny_v, tiny_g, *sums_of = call(
        functools.partial(back_kernel, width),
        [VM] + [ANY] * 2 + [VM] * 8 + [ANY] * 14,
        [(shape((half, tokens), F32), ANY), (shape((2, 8, chan), F32), VM),
         (shape((lru, 128), F32), VM), *land(cols, 2 * ff), *land(ff, cols), *land(cols, 2 * lru), *land(lru, cols)],
        [pltpu.VMEM((LINE, 8, seq), F32), pltpu.VMEM((LINE, 8, seq), F32), pltpu.VMEM((8, seq), F32),
         pltpu.VMEM((chan, width), BF16), pltpu.VMEM((width, 2 * chan), BF16),
         pair(), pair(128), pair(), pair(), pair(), pair(128), tok(width, BF16), tok(2 * chan, BF16),
         tok(block), tok(block), pltpu.VMEM((chan, PART), F32), pltpu.VMEM((chan, PART + 128), F32), pltpu.VMEM((2 * chan, PART), BF16),
         pltpu.VMEM((chan, PART), F32), pltpu.VMEM((chan, PART), F32), pltpu.VMEM((chan, 128), F32), own_low, held,
         tok(chan, BF16), pltpu.VMEM((4, cols, 2 * ff), BF16), pltpu.VMEM((cols, 2 * ff), BF16),
         pltpu.VMEM((4, ff, cols), BF16), pltpu.VMEM((ff, cols), BF16),
         pltpu.VMEM((block, 128), F32), pltpu.VMEM((block, 128), F32), pltpu.VMEM((8, chan, 128), F32),
         pltpu.VMEM((2, lru, 2 * lru), F32), tok(block, BF16), pltpu.VMEM((width, 2 * lru), BF16),
         pltpu.VMEM((lru, width), BF16), pltpu.VMEM((2, 8, chan), F32), pltpu.VMEM((2, 8, chan), F32),
         pltpu.VMEM((4, 2, 8, chan), F32), pltpu.VMEM((2, lru, 128), F32), pltpu.VMEM((lru, 128), F32),
         pltpu.VMEM((4, lru, 128), F32), DMA((7,)), DMA((6, 2))] + line + line + steps + sums
        + [DMA, DMA, DMA((2, 2)), DMA((2, PARTS)), DMA((2, PARTS)), DMA((2,)), DMA((2,)), DMA((4,))]
        + [DMA((2, 3)), DMA((2, 3)), DMA((2, 3)), DMA((2, 3)), DMA((2,)), DMA((2,))],
        2, "mix_backward", 10 * 10**9,
    )(y, dn2, g, x_own, scale_two, scale_one, gain_two, gain_one, masks, par, gates_hi, m_n, br_n, b, p, u, r, i, h,
      q, n1, f_own, f_got, fd_own, fd_got)

    line_of = shape((1, lru), F32)
    s_b, s_r, s_m, s_g, s_u, s_d, taps, offs, bias_r, bias_a, decay, mix, feed, retain, admit = pl.pallas_call(
        last_kernel,
        out_shape=[shape((cols, lru), F32)] * 2 + [shape((lru, cols), F32)] + [shape((cols, ff), F32)] * 2
        + [shape((ff, cols), F32), shape((4, lru), F32)] + [line_of] * 4 + [shape((1, half), F32)] * 2
        + [shape((heads, 64, 64), F32)] * 2,
        in_specs=[VM] * 11,
        out_specs=[VM] * 15,
        name="last_sums",
        compiler_params=pltpu.CompilerParams(vmem_limit_bytes=ROOM),
    )(*sums_of, tiny_v, tiny_g, lambdas[None, :])
    return (
        result,
        input_grad,
        mix[0],
        s_b,
        s_r,
        taps,
        offs[0],
        retain,
        bias_r[0],
        admit,
        bias_a[0],
        decay[0],
        s_m,
        feed[0],
        s_g,
        s_u,
        s_d,
    )


def suits(mesh, args):
    return (
        dict(mesh.shape) == {"row": 4, "col": 8}
        and args[0].shape == (D, 8 * SEQ)
        and args[3].shape == (D, 2048)
        and args[14].shape == (D, 4608)
        and args[7].shape == (32, 64, 64)
    )


def solution(mesh):
    in_specs = (
        P("col", "row"),
        P("row"),
        P("col"),
        P("row", "col"),
        P("row", "col"),
        P(None, "col"),
        P("col"),
        P("col", None, None),
        P("col"),
        P("col", None, None),
        P("col"),
        P("col"),
        P("col", "row"),
        P("col"),
        P("row", "col"),
        P("row", "col"),
        P("col", "row"),
        P("col", "row"),
    )
    out_specs = (
        P("col", "row"),
        P("col", "row"),
        P("col"),
        P("row", "col"),
        P("row", "col"),
        P(None, "col"),
        P("col"),
        P("col", None, None),
        P("col"),
        P("col", None, None),
        P("col"),
        P("col"),
        P("col", "row"),
        P("col"),
        P("row", "col"),
        P("row", "col"),
        P("col", "row"),
    )
    def run(*args):
        chosen = fast_body if suits(mesh, args) else body
        return jax.shard_map(
            chosen, mesh=mesh, in_specs=in_specs, out_specs=out_specs, check_vma=False
        )(*args)

    return run
```

```python
import functools

import jax
import jax.numpy as jnp
from jax import lax
from jax.experimental import pallas as pl
from jax.experimental.pallas import tpu as pltpu
from jax.sharding import PartitionSpec as P

D = 1536
SEQ = 1024
MICRO = 2


HIGH = lax.Precision.HIGHEST
EPS = 1e-06
POWER = 8.0
FLOOR = 0.01


def combine(earlier, later):
    first_a, first_b = earlier
    second_a, second_b = later
    return (first_a * second_a, second_a * first_b + second_b)


def mixer(
    branch_pre,
    lru_pre,
    segs,
    kernel,
    offsets,
    retain_weight,
    retain_bias,
    admit_weight,
    admit_bias,
    lambdas,
):
    length = lru_pre.shape[0]
    channels = lru_pre.shape[1]
    conv = offsets + kernel[0] * lru_pre
    for lag in range(1, kernel.shape[0]):
        shifted = jnp.concatenate(
            [jnp.zeros((lag, channels), lru_pre.dtype), lru_pre[:-lag]], axis=0
        )
        prior = jnp.concatenate([jnp.full((lag,), -1, jnp.int32), segs[:-lag]])
        keep = (prior == segs).astype(lru_pre.dtype)
        conv = conv + kernel[lag] * shifted * keep[:, None]
    heads = retain_weight.shape[0]
    blocks = conv.reshape(length, heads, channels // heads)
    retain = jax.nn.sigmoid(
        jnp.einsum("thi,hij->thj", blocks, retain_weight, precision=HIGH).reshape(length, channels)
        + retain_bias
    )
    admit = jax.nn.sigmoid(
        jnp.einsum("thi,hij->thj", blocks, admit_weight, precision=HIGH).reshape(length, channels)
        + admit_bias
    )
    decay = jnp.exp(-POWER * retain * jax.nn.softplus(-lambdas))
    factor = jnp.sqrt(1.0 - decay * decay + FLOOR)
    starts = jnp.concatenate([jnp.ones((1,), bool), segs[1:] != segs[:-1]])
    decay = jnp.where(starts[:, None], 0.0, decay)
    factor = jnp.where(starts[:, None], 1.0, factor)
    _, state = lax.associative_scan(combine, (decay, factor * admit * conv), axis=0)
    return jax.nn.gelu(branch_pre) * state


def geglu(gate, upper):
    return jax.nn.gelu(gate) * upper


def contract_rows(left, right):
    return lax.dot_general(
        left, right, (((0,), (0,)), ((), ())), preferred_element_type=jnp.float32
    )


def contract_cols(left, right):
    return lax.dot_general(
        left, right, (((1,), (1,)), ((), ())), preferred_element_type=jnp.float32
    )


def contract_cross(left, right):
    return lax.dot_general(
        left, right, (((0,), (1,)), ((), ())), preferred_element_type=jnp.float32
    )


def norm_forward(resid, gain):
    total = lax.psum(jnp.sum(resid * resid, axis=0), "col")
    scale = lax.rsqrt(total / D + EPS)[None, :]
    return (scale, (resid * scale * gain[:, None]).astype(jnp.bfloat16))


def norm_backward(resid, scale, gain, grad_normed):
    weighted = grad_normed * gain[:, None]
    total = lax.psum(jnp.sum(weighted * resid, axis=0), "col")
    grad_resid = scale * weighted - resid * (scale * scale * scale) * (total / D)[None, :]
    grad_gain = jnp.sum(grad_normed * resid * scale, axis=1)
    return (grad_resid, grad_gain)


def gather_features(normed):
    return lax.all_gather(normed, "col", axis=0, tiled=True)


def gather_cotangent(grad):
    return lax.all_gather(grad, "col", axis=0, tiled=True)


def spread_sum(term):
    return lax.psum_scatter(
        term.astype(jnp.bfloat16), "col", scatter_dimension=0, tiled=True
    ).astype(jnp.float32)


def back_sum(term):
    return spread_sum(term)


def merge_term(whole_merge, mixed_low):
    return spread_sum(contract_cross(whole_merge, mixed_low))


def weight_grads(normed, grad_joined):
    return jnp.dot(
        normed,
        grad_joined,
        preferred_element_type=jnp.float32,
    )


def row_sum(total, axis):
    return lax.psum_scatter(
        total.astype(jnp.bfloat16), "row", scatter_dimension=axis, tiled=True
    ).astype(jnp.float32)


def body(
    inputs,
    segments,
    mix_gain,
    branch_weight,
    recur_weight,
    kernel,
    offsets,
    retain_weight,
    retain_bias,
    admit_weight,
    admit_bias,
    lambdas,
    merge_weight,
    feed_gain,
    gate_weight,
    up_weight,
    down_weight,
    cotangent,
):
    lru_cols = branch_weight.shape[1]
    feed_cols = gate_weight.shape[1]
    mixer_params = (kernel, offsets, retain_weight, retain_bias, admit_weight, admit_bias, lambdas)
    acc_branch = jnp.zeros((D, lru_cols), jnp.float32)
    acc_recur = jnp.zeros((D, lru_cols), jnp.float32)
    acc_gate = jnp.zeros((D, feed_cols), jnp.float32)
    acc_up = jnp.zeros((D, feed_cols), jnp.float32)
    acc_merge = jnp.zeros((lru_cols, D), jnp.float32)
    acc_down = jnp.zeros((feed_cols, D), jnp.float32)
    acc_small = tuple((jnp.zeros_like(p) for p in mixer_params))
    acc_mix = jnp.zeros_like(mix_gain)
    acc_feed = jnp.zeros_like(feed_gain)
    outputs = []
    in_grads = []
    for batch in range(MICRO):
        lower = batch * SEQ
        resid_in = inputs[:, lower : lower + SEQ].astype(jnp.float32)
        grad_out = cotangent[:, lower : lower + SEQ].astype(jnp.float32)
        segs = segments[lower : lower + SEQ]
        whole_branch, whole_recur, whole_gate, whole_up = (
            lax.all_gather(branch_weight, "row", axis=0, tiled=True),
            lax.all_gather(recur_weight, "row", axis=0, tiled=True),
            lax.all_gather(gate_weight, "row", axis=0, tiled=True),
            lax.all_gather(up_weight, "row", axis=0, tiled=True),
        )
        whole_merge, whole_down = (
            lax.all_gather(merge_weight, "row", axis=1, tiled=True),
            lax.all_gather(down_weight, "row", axis=1, tiled=True),
        )
        scale_one, normed_one = norm_forward(resid_in, mix_gain)
        full_one = gather_features(normed_one)
        branch_pre = contract_rows(full_one, whole_branch)
        lru_pre = contract_rows(full_one, whole_recur)

        def local_mixer(bpre, lpre, kern, offs, rweight, rbias, aweight, abias, lams):
            return mixer(bpre, lpre, segs, kern, offs, rweight, rbias, aweight, abias, lams)

        mixed, mixer_pull = jax.vjp(local_mixer, branch_pre, lru_pre, *mixer_params)
        mixed_low = mixed.astype(jnp.bfloat16)
        resid_mid = resid_in + merge_term(whole_merge, mixed_low)
        scale_two, normed_two = norm_forward(resid_mid, feed_gain)
        full_two = gather_features(normed_two)
        gate = contract_rows(full_two, whole_gate)
        upper = contract_rows(full_two, whole_up)
        hidden, geglu_pull = jax.vjp(geglu, gate, upper)
        hidden_low = hidden.astype(jnp.bfloat16)
        result = resid_mid + spread_sum(contract_cross(whole_down, hidden_low))
        outputs.append(result.astype(jnp.bfloat16))
        grad_full = gather_cotangent(grad_out.astype(jnp.bfloat16))
        acc_down = acc_down + contract_cross(hidden_low, grad_full)
        grad_gate, grad_upper = geglu_pull(contract_cross(grad_full, whole_down))
        grad_gate = grad_gate.astype(jnp.bfloat16)
        grad_upper = grad_upper.astype(jnp.bfloat16)
        feed_joined = weight_grads(full_two, jnp.concatenate([grad_gate, grad_upper], axis=1))
        acc_gate = acc_gate + feed_joined[:, :feed_cols]
        acc_up = acc_up + feed_joined[:, feed_cols:]
        grad_normed_two = back_sum(
            contract_cols(whole_gate, grad_gate) + contract_cols(whole_up, grad_upper)
        )
        grad_mid_norm, feed_part = norm_backward(resid_mid, scale_two, feed_gain, grad_normed_two)
        acc_feed = acc_feed + feed_part
        grad_mid = grad_out + grad_mid_norm
        grad_mid_full = gather_cotangent(grad_mid.astype(jnp.bfloat16))
        acc_merge = acc_merge + contract_cross(mixed_low, grad_mid_full)
        pulled = mixer_pull(contract_cross(grad_mid_full, whole_merge))
        grad_branch = pulled[0].astype(jnp.bfloat16)
        grad_lru = pulled[1].astype(jnp.bfloat16)
        acc_small = tuple((total + part for total, part in zip(acc_small, pulled[2:])))
        branch_joined = weight_grads(full_one, jnp.concatenate([grad_branch, grad_lru], axis=1))
        acc_branch = acc_branch + branch_joined[:, :lru_cols]
        acc_recur = acc_recur + branch_joined[:, lru_cols:]
        grad_normed_one = back_sum(
            contract_cols(whole_branch, grad_branch) + contract_cols(whole_recur, grad_lru)
        )
        grad_in_norm, mix_part = norm_backward(resid_in, scale_one, mix_gain, grad_normed_one)
        acc_mix = acc_mix + mix_part
        in_grads.append(grad_mid + grad_in_norm)
    sum_branch, sum_recur, sum_gate, sum_up = (
        row_sum(acc_branch, 0),
        row_sum(acc_recur, 0),
        row_sum(acc_gate, 0),
        row_sum(acc_up, 0),
    )
    sum_merge, sum_down = (
        row_sum(acc_merge, 1),
        row_sum(acc_down, 1),
    )
    summed = lax.psum(
        (
            acc_mix,
            acc_feed,
            acc_small[0],
            acc_small[1],
            acc_small[2],
            acc_small[3],
            acc_small[4],
            acc_small[5],
            acc_small[6],
        ),
        "row",
    )
    result_all = jnp.concatenate(outputs, axis=1)
    input_grad = jnp.concatenate(in_grads, axis=1)
    return (
        result_all,
        input_grad,
        summed[0],
        sum_branch,
        sum_recur,
        summed[2],
        summed[3],
        summed[4],
        summed[5],
        summed[6],
        summed[7],
        summed[8],
        sum_merge,
        summed[1],
        sum_gate,
        sum_up,
        sum_down,
    )


MESH = pl.DeviceIdType.MESH
F32 = jnp.float32
BF16 = jnp.bfloat16
LINE = 4
PART = 256
PARTS = 4
GELU_A = 0.7978845608028654
GELU_B = 0.044715


def place():
    row, col = lax.axis_index("row"), lax.axis_index("col")
    return row, col // 2, col % 2


def at_line(z, core):
    return {"col": 2 * z + core}


def lanes(part):
    return pl.ds(pl.multiple_of(part * PART, PART), PART)


def rows_of(index, size):
    return pl.ds(pl.multiple_of(index * size, 16), size)


def dot(a, b):
    return lax.dot_general(a, b, (((1,), (0,)), ((), ())), preferred_element_type=F32)


def dot_nt(a, b):
    return lax.dot_general(a, b, (((1,), (1,)), ((), ())), preferred_element_type=F32)


def greet(row, z, core, rows, line):
    barrier = pltpu.get_barrier_semaphore()
    peers = [{"col": 2 * z + (1 - core)}]
    if rows:
        peers += [{"row": row ^ d} for d in (1, 2, 3)]
    if line:
        peers += [at_line(z ^ d, core) for d in (1, 2, 3)]
    for peer in peers:
        pl.semaphore_signal(barrier, inc=1, device_id=peer, device_id_type=MESH)
    pl.semaphore_wait(barrier, len(peers))


def remote(src, dst, send, recv, peer):
    return pltpu.make_async_remote_copy(
        src_ref=src, dst_ref=dst, send_sem=send, recv_sem=recv, device_id=peer, device_id_type=MESH
    )


class Gather:
    def __init__(self, ref, send, recv, z, core, block, back=False):
        self.ref, self.sems, self.z, self.core = ref, (send, recv), z, core
        self.block, self.back = block, back

    def copy(self, way, hop, step, owner, incoming=False):
        part = PARTS - 1 - step if self.back else step
        piece = self.ref.at[rows_of(owner, self.block), lanes(part)]
        peer = at_line(self.z + (1 if (way == 0) != incoming else -1), self.core)
        return remote(piece, piece, self.sems[0].at[way, hop, step], self.sems[1].at[way, hop, step], peer)

    def each(self, hop, act, incoming):
        z = self.z
        if incoming:
            cases = ((0, z - 1 - hop >= 0, z - 1 - hop), (1, z + 1 + hop < LINE, z + 1 + hop))
        else:
            cases = (
                (0, (z >= hop) & (z < LINE - 1), z - hop),
                (1, (z + hop < LINE) & (z >= 1), z + hop),
            )
        for way, here, owner in cases:
            pl.when(here)(functools.partial(act, way, owner))

    def send(self, hop, step):
        self.each(hop, lambda way, owner: self.copy(way, hop, step, owner).start(), False)

    def arrive(self, hop, step):
        self.each(hop, lambda way, owner: self.copy(way, hop, step, owner, True).wait_recv(), True)

    def forward(self, hop, step):
        self.arrive(hop - 1, step)
        self.send(hop, step)

    def sent(self):
        def one(step, carry):
            for hop in range(LINE - 1):
                self.each(hop, lambda way, owner: self.copy(way, hop, step, owner).wait_send(), False)
            return carry

        lax.fori_loop(0, PARTS, one, 0)

    def open(self):
        self.send(0, 0)
        self.forward(1, 0)
        self.send(0, 1)
        self.forward(2, 0)

    def middle(self, step):
        @pl.when(step + 1 < PARTS)
        def _():
            self.forward(1, step + 1)

        @pl.when(step + 2 < PARTS)
        def _():
            self.send(0, step + 2)

    def later(self, step):
        @pl.when(step + 1 < PARTS)
        def _():
            self.forward(2, step + 1)


class Spread:
    def __init__(self, own, held, send, recv, z, core):
        self.own, self.held, self.sems, self.z, self.core = own, held, (send, recv), z, core

    def copy(self, way, step, hop):
        slot = hop if way == 0 else LINE - hop
        there = slot - 1 if way == 0 else slot + 1
        peer = at_line(self.z + (1 if way == 0 else -1), self.core)
        return remote(
            self.held.at[step, slot],
            self.held.at[step, there],
            self.sems[0].at[way, step, hop],
            self.sems[1].at[way, step, hop - 1],
            peer,
        )

    def landed(self, way, step, hop):
        slot = hop if way == 0 else LINE - hop
        piece = self.held.at[step, slot]
        peer = at_line(self.z + (-1 if way == 0 else 1), self.core)
        remote(piece, piece, self.sems[0].at[way, step, hop], self.sems[1].at[way, step, hop], peer).wait_recv()

    def push(self, way, step, first):
        z = self.z

        def one(i, carry):
            hop = LINE - 1 - i
            owner = z + hop if way == 0 else z - hop
            slot = hop if way == 0 else LINE - hop

            @pl.when((owner >= 0) & (owner < LINE))
            def _():
                @pl.when(first)
                def _():
                    self.held[step, slot] = self.own(step, owner)[...].astype(BF16)

                @pl.when(jnp.logical_not(first))
                def _():
                    self.landed(way, step, hop)
                    total = self.own(step, owner)[...].astype(F32) + self.held[step, slot].astype(F32)
                    self.held[step, slot] = total.astype(BF16)

                self.copy(way, step, hop).start()

            return carry

        lax.fori_loop(0, LINE - 1, one, 0)

    def serve(self, t, finish):
        z = self.z
        step = t - (LINE - 1)

        @pl.when((step >= 0) & (step < PARTS))
        def _():
            @pl.when(z == 0)
            def _():
                self.landed(1, step, 0)
                finish(step, lambda a, n: self.mine(step, a, n) + self.got(step, LINE, a, n))

            @pl.when(z == LINE - 1)
            def _():
                self.landed(0, step, 0)
                finish(step, lambda a, n: self.mine(step, a, n) + self.got(step, 0, a, n))

            @pl.when((z > 0) & (z < LINE - 1))
            def _():
                self.landed(0, step, 0)
                self.landed(1, step, 0)
                finish(
                    step,
                    lambda a, n: self.mine(step, a, n) + (self.got(step, 0, a, n) + self.got(step, LINE, a, n)),
                )

        for way, late, turn in ((1, LINE - 1 - z, z < 2), (0, z, z >= 0), (1, LINE - 1 - z, z >= 2)):
            step = t - late
            pl.when((step >= 0) & (step < PARTS) & turn)(functools.partial(self.push, way, step, late == 0))

    def mine(self, step, start, size):
        return self.own(step, self.z)[pl.ds(start, size), :].astype(F32)

    def got(self, step, slot, start, size):
        return self.held[step, slot, pl.ds(start, size)].astype(F32)

    def sent(self):
        z = self.z

        def one(step, carry):
            for way in (0, 1):
                for hop in range(1, LINE):
                    owner = z + hop if way == 0 else z - hop

                    @pl.when((owner >= 0) & (owner < LINE))
                    def _():
                        self.copy(way, step, hop).wait_send()

            return carry

        lax.fori_loop(0, PARTS, one, 0)


def share_line(ref, send, recv, z, core):
    copies = [
        remote(ref.at[z], ref.at[z], send.at[d - 1], recv.at[d - 1], at_line(z ^ d, core)) for d in (1, 2, 3)
    ]
    for copy in copies:
        copy.start()
    for d in (1, 2, 3):
        piece = ref.at[z ^ d]
        remote(piece, piece, send.at[d - 1], recv.at[d - 1], at_line(z ^ d, core)).wait_recv()
    for copy in copies:
        copy.wait_send()


class Weights:
    def __init__(self, src, dst, send, recv, own, row, z, core, turned, stride=0, start=0):
        self.src, self.dst, self.send, self.recv, self.own = src, dst, send, recv, own
        self.row, self.core, self.turned = row, core, turned
        self.stride, self.first = stride or src.shape[0], start
        self.sibling = {"col": 2 * z + (1 - core)}

    def spot(self, row, core):
        down, right = (row, core) if self.turned else (core, row)
        rows, cols = self.src.shape
        at = pl.ds(pl.multiple_of(down * self.stride + self.first, 16), rows)
        return self.dst.at[at, pl.ds(pl.multiple_of(right * cols, 128), cols)]

    def to_row(self, d):
        return remote(
            self.src, self.spot(self.row, self.core), self.send.at[d], self.recv.at[d], {"row": self.row ^ d}
        )

    def to_sibling(self, d):
        if d == 0:
            return remote(
                self.src, self.spot(self.row, self.core), self.send.at[0], self.recv.at[0], self.sibling
            )
        piece = self.spot(self.row ^ d, self.core)
        return remote(piece, piece, self.send.at[3 + d], self.recv.at[3 + d], self.sibling)

    def local(self):
        return pltpu.make_async_copy(self.src, self.spot(self.row, self.core), self.own)

    def start(self):
        for d in (1, 2, 3):
            self.to_row(d).start()
        self.to_sibling(0).start()
        self.local().start()

    def forward(self):
        for d in (1, 2, 3):
            piece = self.spot(self.row ^ d, self.core)
            remote(piece, piece, self.send.at[d], self.recv.at[d], {"row": self.row ^ d}).wait_recv()
            self.to_sibling(d).start()

    def finish(self):
        self.local().wait()
        for d in (0, 1, 2, 3):
            piece = self.spot(self.row ^ d, 1 - self.core)
            sem = 0 if d == 0 else 3 + d
            remote(piece, piece, self.send.at[sem], self.recv.at[sem], self.sibling).wait_recv()

    def sent(self):
        for d in (1, 2, 3):
            self.to_row(d).wait_send()
            self.to_sibling(d).wait_send()
        self.to_sibling(0).wait_send()


def gelu_parts(b):
    t = jnp.tanh(GELU_A * (b + GELU_B * (b * b * b)))
    half = 0.5 + 0.5 * t
    slope = half + (0.5 * b) * (1.0 - t * t) * (GELU_A + (3.0 * GELU_A * GELU_B) * (b * b))
    return b * half, slope


def blocks(count, body):
    def one(i, carry):
        body(i)
        return carry

    lax.fori_loop(0, count, one, 0)


def scale_of(ref, eps, width):
    total = jnp.sum(jnp.sum(ref[...], axis=0), axis=0, keepdims=True)
    return lax.rsqrt(total / width + eps)


def forward_kernel(
    width, eps,
    x_in, g_in, segs, vec, retain, admit, br_s, m_s, gu_s, d_s, brn_s, mn_s,
    masks, par, gains, gates, coef, scale, scale_two, y_out, n1_out, q_out, x_out, g_out, b_out, p_out, u_out, r_out, i_out, h_out,
    result, dn2_out, dev_h, z_h, g_own, g_got, gd_own, gd_got, br_n, m_n,
    sums, sums2, sums3, vec_all, block_all, gates_hi, gates_lo, normed, normed2, go, x_own, y, dn2, q_c, p_s, h_s, room, uh, ul,
    own, held, held_n, held_o, gu, gun, down, dt, zs, dev,
    x_send, x_recv, x_loc, l_send, l_recv, n_send, n_recv, c_send, c_recv, g_send, g_recv, e_send, e_recv, f_send, f_recv,
    s_send, s_recv, t_send, t_recv, o_send, o_recv, w_send, w_recv, w_own, k_sem, v_sem, d_send, d_recv, d_own,
):
    row, z, core = place()
    block, seq = y.shape
    half = x_in.shape[0]
    chan = p_s.shape[0]
    hid = zs.shape[0]
    b_s, u_s, r_s, i_s, a_c = [room.at[n * chan : (n + 1) * chan, :] for n in range(5)]
    ev, dz = room.at[0:hid, :], room.at[hid : hid + hid // 2, :]
    hh = hid // 2
    hc = chan // 2
    sibling = {"col": 2 * z + (1 - core)}
    greet(row, z, core, True, True)
    br, mt = gun.at[0 : 2 * chan, 0:width], dt.at[:, 0:chan]
    wide = br_s.shape[0]
    recur_s, branch_s = br_s.at[wide // 2 :, :], br_s.at[0 : wide // 2, :]
    weights = [
        Weights(src, dst, w_send.at[n], w_recv.at[n], w_own.at[n], row, z, core, n in (2, 5), stride, start)
        for n, (src, dst, stride, start) in enumerate(
            (
                (recur_s, br, wide, wide // 2),
                (branch_s, br, wide, 0),
                (m_s, mt, 0, 0),
                (gu_s, gu, 0, 0),
                (d_s, down, 0, 0),
                (brn_s, br_n, 0, 0),
                (mn_s, m_n, 0, 0),
            )
        )
    ]
    mine = pl.ds(pl.multiple_of(core * seq, seq), seq)
    other = pl.ds(pl.multiple_of((1 - core) * seq, seq), seq)
    inner = pl.ds(pl.multiple_of(z * block + core * half, 16), half)
    outer = rows_of(core, half)
    swaps = [
        remote(x_in.at[:, other], x_own.at[outer, :], x_send.at[0], x_recv.at[0], sibling),
        remote(g_in.at[:, other], go.at[inner, :], x_send.at[1], x_recv.at[1], sibling),
        pltpu.make_async_copy(x_in.at[:, mine], x_own.at[outer, :], x_loc.at[0]),
        pltpu.make_async_copy(g_in.at[:, mine], go.at[inner, :], x_loc.at[1]),
    ]
    trades = []
    for n, (src, dst) in enumerate(
        ((vec, vec_all.at[core]), (retain, block_all.at[core, 0]), (admit, block_all.at[core, 1]))
    ):
        trades.append(remote(src, dst, x_send.at[2 + n], x_recv.at[2 + n], sibling))
        trades.append(pltpu.make_async_copy(src, dst, x_loc.at[2 + n]))
    for swap in swaps + trades:
        swap.start()
    for w in weights[:3]:
        w.start()
    for swap in swaps + trades:
        swap.wait()
    flushes = [
        pltpu.make_async_copy(x_own, x_out, v_sem.at[0]),
        pltpu.make_async_copy(go.at[rows_of(z, block), :], g_out, v_sem.at[1]),
    ]
    for flush in flushes:
        flush.start()
    gather = Gather(normed, g_send, g_recv, z, core, block)
    gather_go = Gather(go, e_send, e_recv, z, core, block)
    gather_two = Gather(normed2, f_send, f_recv, z, core, block)
    shares = lambda k, s: own.at[k, s]
    shares_o = lambda k, s: normed.at[rows_of(s, block), lanes(k)]
    spread = Spread(shares, held, s_send, s_recv, z, core)
    spread_n = Spread(shares, held_n, t_send, t_recv, z, core)
    spread_o = Spread(shares_o, held_o, o_send, o_recv, z, core)
    res = x_own
    gather_go.send(0, 0)
    for c in (0, 1):
        at = slice(c * hc, (c + 1) * hc)
        par[at, :] = vec_all[c].T
        gains[c * half : (c + 1) * half, :] = par[c * hc : c * hc + half, :]

    sums[z] = jnp.zeros(sums.shape[1:], F32)

    def squares(i):
        v = x_own[rows_of(i, 16), :].astype(F32)
        v = v * v
        sums[z] += v[:8] + v[8:]

    blocks(block // 16, squares)
    share_line(sums, l_send, l_recv, z, core)
    scale[...] = jnp.broadcast_to(scale_of(sums, eps, width), scale.shape)

    def norm(i):
        v = x_own[rows_of(i, 16), :].astype(F32) * scale[0:1, :] * gains[rows_of(i, 16), 8:9]
        normed[pl.ds(pl.multiple_of(z * block + i * 16, 16), 16), :] = v.astype(BF16)

    blocks(block // 16, norm)
    gather.send(0, 0)
    gather_go.forward(1, 0)
    gather.forward(1, 0)
    gather.send(0, 1)
    gather.forward(2, 0)
    gather_go.forward(2, 0)
    gather_go.send(0, 1)
    p_s[:, PART:] = jnp.zeros((chan, 128), F32)
    h_s[:, PART:] = jnp.zeros((chan, 128), F32)
    pads = [
        pltpu.make_async_copy(src.at[:, PART:], out.at[:, 0:128], v_sem.at[2 + n])
        for n, (src, out) in enumerate(((p_s, p_out), (h_s, h_out)))
    ]
    for pad in pads:
        pad.start()
    weights[0].forward()
    gather_go.forward(1, 1)

    gates[...] = jnp.zeros(gates.shape, BF16)
    gates_hi[...] = jnp.zeros(gates_hi.shape, BF16)
    gates_lo[...] = jnp.zeros(gates_lo.shape, BF16)
    per = retain.shape[0]
    tap = retain.shape[1]
    for c in (0, 1):
        for n in (0, 1):
            for e in range(per):
                w = block_all[c, n, e]
                at, far = slice(e * tap, (e + 1) * tap), slice(n * hc + e * tap, n * hc + (e + 1) * tap)
                gates[c, at, far] = w.astype(BF16)
                w = w.T
                high = w.astype(BF16)
                gates_hi[c, far, at] = high
                gates_lo[c, far, at] = (w - high.astype(F32)).astype(BF16)
    masks[...] = jnp.zeros(masks.shape, F32)
    here = jnp.broadcast_to(segs[:, mine], (8, seq))
    spot = lax.broadcasted_iota(jnp.int32, (8, seq), 1)
    for lag in (1, 2, 3):
        same = jnp.where((pltpu.roll(here, lag, 1) == here) & (spot >= lag), 1.0, 0.0)
        masks[lag : lag + 1, 0:seq] = same[0:1]
        if lag == 1:
            masks[0:1, 0:seq] = 1.0 - same[0:1]
    weights[1].forward()
    for w in weights[3:5]:
        w.start()
    weights[0].finish()
    for pad in pads:
        pad.wait()

    kept = (b_s, p_s, u_s, r_s, i_s, h_s, q_c)
    outs = (b_out, p_out, u_out, r_out, i_out, h_out, q_out)

    def keep(n, part):
        if n in (1, 5):
            at = pl.ds(pl.multiple_of(128 + part * PART, 128), PART)
            return pltpu.make_async_copy(kept[n].at[:, 128:], outs[n].at[:, at], k_sem.at[n])
        return pltpu.make_async_copy(kept[n], outs[n].at[:, lanes(part)], k_sem.at[n])

    def work(k):
        here = lanes(k)

        @pl.when(k > 0)
        def _():
            for n in range(len(kept)):
                keep(n, k - 1).wait()

        p_s[:, 0:128] = p_s[:, PART:]
        h_s[:, 0:128] = h_s[:, PART:]
        n1 = normed[:, here]
        for c in (0, 1):
            p_s[c * hc : (c + 1) * hc, 128:] = dot(br[c * 2 * hc + hc : (c + 1) * 2 * hc, :], n1)

        def conv(i):
            ch = rows_of(i, 32)
            window = p_s[ch, :]
            pr = par[ch, :]
            u = pr[:, 4:5] + pr[:, 0:1] * window[:, 128:]
            for lag in (1, 2, 3):
                u = u + pr[:, lag : lag + 1] * (pltpu.roll(window, lag, 1)[:, 128:] * masks[lag : lag + 1, here])
            u_s[ch, :] = u
            high = u.astype(BF16)
            uh[ch, :] = high
            ul[ch, :] = (u - high.astype(F32)).astype(BF16)

        blocks(chan // 32, conv)
        gather.middle(k)
        for g in range(chan // 256):
            at = slice(g * 256, (g + 1) * 256)
            pre = dot(gates_hi[g], uh[at, :]) + dot(gates_hi[g], ul[at, :]) + dot(gates_lo[g], uh[at, :])
            r_s[at, :] = pre[:256]
            i_s[at, :] = pre[256:]

        def decay(i):
            ch = rows_of(i, 64)
            pr = par[ch, :]
            start = masks[0:1, here] > 0.5
            r = jax.nn.sigmoid(r_s[ch, :] + pr[:, 5:6])
            gate = jax.nn.sigmoid(i_s[ch, :] + pr[:, 6:7])
            r_s[ch, :] = r
            i_s[ch, :] = gate
            a = jnp.exp(-(r * pr[:, 7:8]))
            m = jnp.where(start, 1.0, jnp.sqrt(1.0 - a * a + FLOOR))
            a_c[ch, :] = jnp.where(start, 0.0, a)
            h_s[ch, 128:] = m * gate * u_s[ch, :]

        blocks(chan // 64, decay)
        first = lax.broadcasted_iota(jnp.int32, (64, PART), 1) == 0

        def recur(i):
            ch = rows_of(i, 64)
            a, h = a_c[ch, :], h_s[ch, 128:]
            h = h + jnp.where(first, a * h_s[ch, 0:128][:, 127:128], 0.0)
            a = jnp.where(first, 0.0, a)
            shift = 1
            while shift < PART:
                h = h + a * pltpu.roll(h, shift, 1)
                if shift * 2 < PART:
                    a = a * pltpu.roll(a, shift, 1)
                shift *= 2
            h_s[ch, 128:] = h

        blocks(chan // 64, recur)
        gather.later(k)

        @pl.when(k == 0)
        def _():
            gather_go.forward(2, 1)
            weights[2].forward()
            weights[1].finish()

        for c in (0, 1):
            b_s[c * hc : (c + 1) * hc, :] = dot(br[c * 2 * hc : c * 2 * hc + hc, :], normed[:, here])

        def mixed(i):
            ch = rows_of(i, 64)
            b = b_s[ch, :]
            t = jnp.tanh(GELU_A * (b + GELU_B * (b * b * b)))
            q_c[ch, :] = (b * (0.5 + 0.5 * t) * h_s[ch, 128:]).astype(BF16)

        blocks(chan // 64, mixed)
        pl.when(k == 0)(weights[2].finish)
        qk = q_c[...]
        for s in range(LINE):
            own[k, s] = dot(mt[s * block : (s + 1) * block, :], qk).astype(own.dtype)
        for n in range(len(kept)):
            keep(n, k).start()

    def finish(k, total):
        def add(i):
            at = pl.multiple_of(i * 16, 16)
            y[pl.ds(at, 16), lanes(k)] = x_own[pl.ds(at, 16), lanes(k)].astype(F32) + total(at, 16)

        blocks(block // 16, add)

    def step(t, carry):
        gather.arrive(2, t)
        work(t)
        spread.serve(t, finish)
        pl.when(t == PARTS - 1)(weights[3].forward)
        return carry

    lax.fori_loop(0, PARTS, step, 0)

    def square(k):
        sums2[k, z] = jnp.zeros(sums2.shape[2:], F32)

        def one(i):
            v = y[rows_of(i, 16), lanes(k)]
            v = v * v
            sums2[k, z] += v[:8] + v[8:]

        blocks(block // 16, one)
        for d in (1, 2, 3):
            share(k, d).start()

    def share(k, d):
        return remote(
            sums2.at[k, z], sums2.at[k, z], n_send.at[k, d - 1], n_recv.at[k, d - 1], at_line(z ^ d, core)
        )

    def norm_two(k):
        for d in (1, 2, 3):
            piece = sums2.at[k, z ^ d]
            remote(piece, piece, n_send.at[k, d - 1], n_recv.at[k, d - 1], at_line(z ^ d, core)).wait_recv()
        s2 = scale_of(sums2.at[k], eps, width)
        scale_two[:, lanes(k)] = jnp.broadcast_to(s2, (8, PART))

        def one(i):
            at = rows_of(i, 16)
            v = y[at, lanes(k)] * scale_two[0:1, lanes(k)] * gains[at, 9:10]
            normed2[pl.ds(pl.multiple_of(z * block + i * 16, 16), 16), lanes(k)] = v.astype(BF16)

        blocks(block // 16, one)

    square(0)
    for w in weights[:3]:
        w.sent()
    for w in weights[5:]:
        w.start()
    for n in range(len(kept)):
        keep(n, PARTS - 1).wait()
    flush_n = pltpu.make_async_copy(normed, n1_out, v_sem.at[4])
    flush_n.start()
    gather_go.send(0, 2)
    spread.serve(PARTS, finish)
    norm_two(0)
    gather_two.send(0, 0)
    square(1)
    gather_go.forward(1, 2)
    weights[4].forward()
    spread.serve(PARTS + 1, finish)
    norm_two(1)
    gather_two.forward(1, 0)
    gather_two.send(0, 1)
    square(2)
    weights[4].finish()

    def turn_down(i):
        at = pl.ds(pl.multiple_of(i * 128, 128), 128)
        dt[:, at] = down[at, :].T

    blocks(hid // 128, turn_down)
    spread.serve(PARTS + 2, finish)
    gather.sent()
    for flush in flushes + [flush_n]:
        flush.wait()
    gather_two.forward(2, 0)
    gather_go.forward(2, 2)
    norm_two(2)
    square(3)
    weights[3].finish()

    def turn_up(i):
        at = pl.ds(pl.multiple_of(i * 128, 128), 128)
        gun[:, at] = gu[at, :].T

    blocks(2 * hid // 128, turn_up)
    norm_two(3)
    gather_go.send(0, 3)

    def keep_dev(k):
        return pltpu.make_async_copy(dev, dev_h.at[:, lanes(k)], v_sem.at[5])

    def keep_z(k):
        return pltpu.make_async_copy(zs, z_h.at[:, lanes(k)], v_sem.at[6])

    def feed(k):
        here = lanes(k)
        n2 = normed2[:, here]

        @pl.when(k > 0)
        def _():
            keep_dev(k - 1).wait()
            keep_z(k - 1).wait()

        for c in range(2):
            for e in range(2):
                ev[e * hh : (e + 1) * hh, :] = dot(gu[(2 * c + e) * hh : (2 * c + e + 1) * hh, :], n2)
            if c == 0:
                gather_two.middle(k)
                pl.when(k == 0)(lambda: gather_go.forward(1, 3))
                gather_go.arrive(2, k)
            dz[...] = dot(down[c * hh : (c + 1) * hh, :], go[:, here])

            def one(i):
                off = pl.multiple_of(i * 64, 64)
                e = ev[pl.ds(off, 64), :]
                v = ev[pl.ds(hh + off, 64), :]
                d = dz[pl.ds(off, 64), :]
                act, slope = gelu_parts(e)
                zs[pl.ds(c * hh + off, 64), :] = (act * v).astype(BF16)
                dev[pl.ds(c * 2 * hh + off, 64), :] = (d * v * slope).astype(BF16)
                dev[pl.ds(c * 2 * hh + hh + off, 64), :] = (d * act).astype(BF16)

            blocks(hh // 64, one)
        gather_two.later(k)
        pl.when(k == 0)(lambda: gather_go.forward(2, 3))
        dk = dev[...]
        for s in range(LINE):
            own[k, s] = dot(gun[s * block : (s + 1) * block, :], dk).astype(own.dtype)
        spread_n.serve(k, finish_n)
        zk = zs[...]
        for s in range(LINE):
            normed[s * block : (s + 1) * block, here] = dot(dt[s * block : (s + 1) * block, :], zk).astype(BF16)
        spread_o.serve(k, finish_o)
        keep_dev(k).start()
        keep_z(k).start()

    def finish_o(k, total):
        def add(i):
            at = pl.multiple_of(i * 16, 16)
            res[pl.ds(at, 16), lanes(k)] = (y[pl.ds(at, 16), lanes(k)] + total(at, 16)).astype(BF16)

        blocks(block // 16, add)

    def keep_n(k):
        return pltpu.make_async_copy(dn2, dn2_out.at[:, lanes(k)], v_sem.at[3])

    def finish_n(k, total):
        @pl.when(k > 0)
        def _():
            keep_n(k - 1).wait()

        sums3[k, z] = jnp.zeros(sums3.shape[2:], F32)

        def add(i):
            at = pl.multiple_of(i * 16, 16)
            d = total(at, 16)
            dn2[pl.ds(at, 16), :] = d
            c = d * y[pl.ds(at, 16), lanes(k)] * gains[pl.ds(at, 16), 9:10]
            sums3[k, z] += c[:8] + c[8:]

        blocks(block // 16, add)
        keep_n(k).start()
        for d in (1, 2, 3):
            share_c(k, d).start()

    def share_c(k, d):
        return remote(
            sums3.at[k, z], sums3.at[k, z], c_send.at[k, d - 1], c_recv.at[k, d - 1], at_line(z ^ d, core)
        )

    def feed_step(t, carry):
        gather_two.arrive(2, t)
        feed(t)
        pl.when(t == 2)(weights[5].forward)
        pl.when(t == 3)(weights[6].forward)
        return carry

    lax.fori_loop(0, PARTS, feed_step, 0)
    for w in weights[3:5]:
        w.sent()
    keep_dev(PARTS - 1).wait()
    keep_z(PARTS - 1).wait()
    dev_all, z_all = gu.at[:, 0:seq], dt.at[0:hid, 0:seq]
    loads = [pltpu.make_async_copy(dev_h, dev_all, v_sem.at[5]), pltpu.make_async_copy(z_h, z_all, v_sem.at[6])]
    for load in loads:
        load.start()
    for load in loads:
        load.wait()

    def columns(start):
        return pl.ds(pl.multiple_of(start, 128), block)

    def place_up(j):
        side = jnp.where(j >= 3, core, 1 - core)
        return side * hid + (j % 3) * block, columns((j % 3) * block)

    def send_up(j):
        at, to = place_up(j)
        return remote(gun.at[:, columns(at)], g_got.at[:, to], d_send.at[j], d_recv.at[j], sibling)

    def keep_up(j):
        at, to = place_up(j)
        return pltpu.make_async_copy(gun.at[:, columns(at)], g_own.at[:, to], d_own.at[j - 3])

    def send_down():
        return remote(down.at[rows_of(1 - core, hh), :], gd_got, d_send.at[3], d_recv.at[3], sibling)

    def keep_down():
        return pltpu.make_async_copy(down.at[rows_of(core, hh), :], gd_own, d_own.at[3])

    def grad_up(j):
        at = place_up(j)[0]
        right = pl.ds(pl.multiple_of(at, 16), block)
        for low in (0, width // 2):
            piece = slice(low, low + width // 2)
            gun[piece, columns(at)] = dot_nt(normed2[piece, :], dev_all[right, :]).astype(BF16)

        @pl.when(j < 3)
        def _():
            send_up(j).start()

        @pl.when(j >= 3)
        def _():
            keep_up(j).start()

    def grad_down(side):
        at = rows_of(side, hh)
        down[at, :] = dot_nt(z_all[at, :], go[...]).astype(BF16)

    def drain(i, carry):
        t = PARTS + i
        blocks(2, lambda j: grad_up(2 * i + j))
        spread_n.serve(t, finish_n)
        spread_o.serve(t, finish_o)

        @pl.when(i < 2)
        def _():
            grad_down(jnp.where(i == 0, 1 - core, core))

        pl.when(i == 0)(lambda: send_down().start())
        pl.when(i == 1)(lambda: keep_down().start())
        return carry

    lax.fori_loop(0, LINE - 1, drain, 0)
    last = [
        remote(res.at[rows_of(1 - core, half), :], result.at[:, mine], x_send.at[0], x_recv.at[0], sibling),
        pltpu.make_async_copy(res.at[rows_of(core, half), :], result.at[:, mine], x_loc.at[0]),
        pltpu.make_async_copy(y, y_out, v_sem.at[2]),
        keep_n(PARTS - 1),
    ]
    for copy in last[:3]:
        copy.start()
    for w in weights[5:]:
        w.finish()
        w.sent()
    for one in (gather_go, gather_two, spread, spread_n, spread_o):
        one.sent()
    for k in range(PARTS):
        for d in (1, 2, 3):
            share(k, d).wait_send()
            share_c(k, d).wait_send()
            piece = sums3.at[k, z ^ d]
            remote(piece, piece, c_send.at[k, d - 1], c_recv.at[k, d - 1], at_line(z ^ d, core)).wait_recv()
        total = jnp.sum(jnp.sum(sums3[k], axis=0), axis=0, keepdims=True)
        at = slice(k * PART, (k + 1) * PART)
        s2 = scale_two[:, at]
        coef[:, at] = s2 * s2 * s2 * (total / width)
    for j in range(3):
        keep_up(j + 3).wait()
        send_up(j).wait()
    keep_down().wait()
    send_down().wait()
    for copy in last:
        copy.wait()


def back_kernel(
    width,
    y, dn2_h, g_h, x_own, scale_two, scale_one, coef_two, gains, masks, par, gates_t, m_h, br_h,
    b_h, p_h, u_h, r_h, i_h, h_h, q_h, n1_h, f_own, f_got, fd_own, fd_got,
    input_grad, tiny_v, tiny_g, f_sum, f_land, fd_sum, fd_land, g_sum, g_land, gm_sum, gm_land,
    sums, coef, m_n, br_n, b_s, p_s, u_s, r_s, i_s, h_s, dyf, dbp, dy, dn1, dq, du, dri, a_c, l_c, carry_s, own, held,
    qv, f_a, f_b, fd_a, fd_b, feed_part, mix_part, small, gate_grad, g_s, g_got, gm_got,
    vec, vec_in, vec_all, gd, gd_in, gd_all,
    c_sem, k_sem, l_send, l_recv, g_send, g_recv, s_send, s_recv, r_send, r_recv,
    f_sem, f_send, f_recv, d_send, d_recv, d_own, q_send, q_recv, n_send, n_recv, v_send, v_recv,
):
    row, z, core = place()
    block, seq = y.shape
    half = block // 2
    chan = b_s.shape[1]
    hc = chan // 2
    sibling = {"col": 2 * z + (1 - core)}
    greet(row, z, core, True, True)
    load_g = pltpu.make_async_copy(g_h, g_s, c_sem.at[0])
    load_g.start()
    dn2 = dn1
    load_d = pltpu.make_async_copy(dn2_h, dn2, c_sem.at[5])
    load_d.start()
    load_m = pltpu.make_async_copy(m_h, m_n, c_sem.at[1])
    load_m.start()
    load_b = pltpu.make_async_copy(br_h, br_n, c_sem.at[2])
    load_b.start()
    load_q = pltpu.make_async_copy(q_h, qv, c_sem.at[3])
    n1 = dyf
    load_n = pltpu.make_async_copy(n1_h, n1, c_sem.at[4])
    kept = (b_s, p_s, u_s, r_s, i_s, h_s)
    srcs = (b_h, p_h, u_h, r_h, i_h, h_h)

    def fetch(n, part):
        if kept[n] is p_s or kept[n] is h_s:
            at = pl.ds(pl.multiple_of(part * PART, 128), PART + 128)
        else:
            at = lanes(part)
        return pltpu.make_async_copy(srcs[n].at[:, at], kept[n].at[part % 2], k_sem.at[n, part % 2])

    def fetch_all(part):
        for n in range(len(kept)):
            fetch(n, part).start()

    fetch_all(PARTS - 1)
    load_q.start()
    du[:, 0:128] = jnp.zeros((chan, 128), F32)
    carry_s[...] = jnp.zeros(carry_s.shape, F32)
    small[...] = jnp.zeros(small.shape, F32)
    gate_grad[...] = jnp.zeros(gate_grad.shape, F32)

    load_d.wait()
    load_g.wait()
    gather = Gather(dyf, g_send, g_recv, z, core, block, back=True)

    def outer(part):
        here = slice(part * PART, (part + 1) * PART)

        def one(i):
            at = rows_of(i, 16)
            s2 = scale_two[0:1, here]
            d, v = dn2[at, here], y[at, here]
            w = d * v * s2
            w = w[:, 0:128] + w[:, 128:256]
            feed_part[at, :] = w if part == PARTS - 1 else feed_part[at, :] + w
            v = g_s[at, here].astype(F32) + (s2 * (gains[at, 9:10] * d) - v * coef_two[0:1, here])
            dy[at, here] = v
            dyf[pl.ds(pl.multiple_of(z * block + i * 16, 16), 16), here] = v.astype(BF16)

        blocks(block // 16, one)

    outer(PARTS - 1)
    gather.send(0, 0)
    outer(PARTS - 2)
    spread = Spread(lambda k, s: own.at[k, s], held, s_send, s_recv, z, core)
    gather.forward(1, 0)
    gather.send(0, 1)
    for part in range(PARTS - 2):
        outer(part)
    gather.forward(2, 0)
    load_m.wait()
    load_b.wait()
    final = lax.broadcasted_iota(jnp.int32, (64, PART), 1) == PART - 1

    f_arrays = ((f_own, f_got, f_a, f_b, f_sum, f_land), (fd_own, fd_got, fd_a, fd_b, fd_sum, fd_land))

    def f_loads(d):
        pulls = []
        for n, (ours, theirs, a, b, _, _) in enumerate(f_arrays):
            if n == 0:
                piece = (rows_of(row ^ d, block), slice(None))
            else:
                piece = (slice(None), pl.ds(pl.multiple_of((row ^ d) * block, 128), block))
            pulls.append(pltpu.make_async_copy(ours.at[piece], a.at[d], f_sem.at[n, 0]))
            pulls.append(pltpu.make_async_copy(theirs.at[piece], b, f_sem.at[n, 1]))
        return pulls

    def f_out(d):
        outs = []
        for n, (_, _, a, _, kept_at, land) in enumerate(f_arrays):
            if d == 0:
                outs.append(pltpu.make_async_copy(a.at[0], kept_at, f_send.at[n, 0]))
            else:
                outs.append(
                    remote(a.at[d], land.at[d - 1], f_send.at[n, d], f_recv.at[n, d], {"row": row ^ d})
                )
        return outs

    def f_part(d):
        for pull in f_loads(d):
            pull.wait()
        for _, _, a, b, _, _ in f_arrays:

            def add(i):
                at = rows_of(i, 16)
                a[d, at, :] = (a[d, at, :].astype(F32) + b[at, :].astype(F32)).astype(BF16)

            blocks(b.shape[0] // 16, add)
        for out in f_out(d):
            out.start()
        if d > 0:
            for pull in f_loads(d - 1):
                pull.start()

    def f_step(t):
        for d in range(PARTS):
            pl.when(t == PARTS - 1 - d)(functools.partial(f_part, d))

    for pull in f_loads(PARTS - 1):
        pull.start()

    def fold2(v):
        return v[:, 0:128] + v[:, 128:256]

    def work(t):
        k = PARTS - 1 - t
        here = lanes(k)
        wide = pl.ds(pl.multiple_of(k * PART, 128), PART + 128)
        slot = k % 2
        for n in range(len(kept)):
            fetch(n, k).wait()

        @pl.when(k > 0)
        def _():
            fetch_all(k - 1)

        dq[...] = dot(m_n[...], dyf[:, here])

        def before(i):
            ch = rows_of(i, 64)
            c = i // (hc // 64)
            low = pl.ds(pl.multiple_of(c * hc + i * 64, 64), 64)
            pr = par[ch, :]
            d = dq[ch, :]
            act, slope = gelu_parts(b_s[slot, ch, :])
            dbp[low, here] = (d * h_s[slot, ch, :][:, 128:] * slope).astype(BF16)
            l_c[ch, :] = d * act
            a_c[ch, :] = jnp.exp(-(r_s[slot, ch, :] * pr[:, 7:8]))

        blocks(chan // 64, before)
        gather.middle(t)

        def recur(i):
            ch = rows_of(i, 64)
            start = masks[0:1, here] > 0.5
            a, lam = jnp.where(start, 0.0, a_c[ch, :]), l_c[ch, :]
            lam = lam + jnp.where(final, carry_s[ch, :][:, 0:1], 0.0)
            w = jnp.where(final, 0.0, pltpu.roll(a, PART - 1, 1))
            shift = 1
            while shift < PART:
                lam = lam + w * pltpu.roll(lam, PART - shift, 1)
                if shift * 2 < PART:
                    w = w * pltpu.roll(w, PART - shift, 1)
                shift *= 2
            carry_s[ch, :] = jnp.broadcast_to((a * lam)[:, 0:1], (64, 128))
            l_c[ch, :] = lam

        blocks(chan // 64, recur)
        f_step(t)
        gather.later(t)

        def after(i):
            ch = rows_of(i, 32)
            du[ch, PART:] = du[ch, 0:128]
            pr = par[ch, :]
            start = masks[0:1, here] > 0.5
            lam, a0 = l_c[ch, :], a_c[ch, :]
            earlier = pltpu.roll(h_s[slot, ch, :], 1, 1)[:, 128:]
            r, gate, u = r_s[slot, ch, :], i_s[slot, ch, :], u_s[slot, ch, :]
            m0 = jnp.sqrt(1.0 - a0 * a0 + FLOOR)
            m = jnp.where(start, 1.0, m0)
            lm = lam * m
            lu = lam * u
            du[ch, 0:PART] = lm * gate
            da = jnp.where(start, 0.0, lam * earlier - (lu * gate) * (a0 / m0)) * a0
            dr = da * (-pr[:, 7:8]) * (r * (1.0 - r))
            di = lu * m * (gate * (1.0 - gate))
            g, o = i // 8, (i % 8) * 32
            dri[pl.ds(pl.multiple_of(g * 512 + o, 32), 32), :] = dr.astype(BF16)
            dri[pl.ds(pl.multiple_of(g * 512 + 256 + o, 32), 32), :] = di.astype(BF16)
            small[5, ch, :] += fold2(dr)
            small[6, ch, :] += fold2(di)
            small[7, ch, :] += fold2(da * r)

        blocks(chan // 32, after)
        for g in range(chan // 256):
            at = slice(g * 256, (g + 1) * 256)
            dd = dri[g * 512 : (g + 1) * 512, :]
            du[at, 0:PART] += dot(gates_t[g], dd)
            gate_grad[g] += dot_nt(u_s[slot, at, :].astype(BF16), dd)

        def conv(i):
            ch = rows_of(i, 32)
            c = i // (hc // 32)
            low = pl.ds(pl.multiple_of((c + 1) * hc + i * 32, 32), 32)
            pr = par[ch, :]
            follow = du[ch, :]
            window = p_s[slot, ch, :]
            d = follow[:, :PART]
            dp = pr[:, 0:1] * d
            small[4, ch, :] += fold2(d)
            small[0, ch, :] += fold2(d * window[:, 128:])
            for lag in (1, 2, 3):
                kd = follow * masks[lag : lag + 1, wide]
                dp = dp + pr[:, lag : lag + 1] * pltpu.roll(kd, PART + 128 - lag, 1)[:, :PART]
                small[lag, ch, :] += fold2(kd[:, :PART] * pltpu.roll(window, lag, 1)[:, 128:])
            dbp[low, here] = dp.astype(BF16)

        blocks(chan // 32, conv)
        dk = dbp[:, here]
        for s in range(LINE):
            own[t, s] = dot(br_n[s * block : (s + 1) * block, :], dk).astype(own.dtype)

    def finish(t, total):
        k = PARTS - 1 - t

        sums[k, z] = jnp.zeros(sums.shape[2:], F32)

        @pl.when(t == 0)
        def _():
            mix_part[...] = jnp.zeros(mix_part.shape, F32)

        def add(i):
            at = pl.ds(pl.multiple_of(i * 16, 16), 16)
            d = total(pl.multiple_of(i * 16, 16), 16)
            dn1[at, lanes(k)] = d
            w = d * x_own[at, lanes(k)].astype(F32)
            c = w * gains[at, 8:9]
            sums[k, z] += c[:8] + c[8:]
            w = w * scale_one[0:1, lanes(k)]
            mix_part[at, :] += w[:, 0:128] + w[:, 128:256]

        blocks(block // 16, add)
        for d in (1, 2, 3):
            share(k, d).start()

    def share(k, d):
        return remote(sums.at[k, z], sums.at[k, z], l_send.at[k, d - 1], l_recv.at[k, d - 1], at_line(z ^ d, core))

    def step(t, carry):
        gather.arrive(2, t)
        work(t)
        spread.serve(t, finish)
        return carry

    lax.fori_loop(0, PARTS, step, 0)
    load_q.wait()

    lru = hc

    def cols_of(side):
        return pl.ds(pl.multiple_of(side * 2 * lru, 128), 2 * lru)

    def send_br():
        return remote(br_n.at[:, cols_of(1 - core)], g_got, d_send.at[0], d_recv.at[0], sibling)

    def send_m():
        return remote(m_n.at[rows_of(1 - core, lru), :], gm_got, d_send.at[1], d_recv.at[1], sibling)

    def grad_br(side):
        br_n[:, cols_of(side)] = dot_nt(n1[...], dbp[rows_of(side, 2 * lru), :]).astype(BF16)

    def out_br(d):
        piece = br_n.at[rows_of(row ^ d, block), cols_of(core)]
        if d == 0:
            return pltpu.make_async_copy(piece, g_sum, d_own.at[0])
        return remote(piece, g_land.at[d - 1], q_send.at[0, d - 1], q_recv.at[0, d - 1], {"row": row ^ d})

    def out_m(d):
        piece = m_n.at[rows_of(core, lru), pl.ds(pl.multiple_of((row ^ d) * block, 128), block)]
        if d == 0:
            return pltpu.make_async_copy(piece, gm_sum, d_own.at[1])
        return remote(piece, gm_land.at[d - 1], q_send.at[1, d - 1], q_recv.at[1, d - 1], {"row": row ^ d})

    def drain(i, carry):
        t = PARTS + i

        @pl.when(i == 0)
        def _():
            m_n[...] = dot_nt(qv[...], dyf[...]).astype(BF16)
            send_m().start()
            gather.sent()
            load_n.start()
            load_n.wait()
            grad_br(1 - core)
            send_br().start()

        @pl.when(i == 1)
        def _():
            grad_br(core)
            send_m().wait_recv()

            def add(j):
                at = rows_of(j, 32)
                to = pl.ds(pl.multiple_of(core * lru + j * 32, 32), 32)
                m_n[to, :] = (m_n[to, :].astype(F32) + gm_got[at, :].astype(F32)).astype(BF16)

            blocks(lru // 32, add)
            for d in (3, 2, 1, 0):
                out_m(d).start()

        @pl.when(i == 2)
        def _():
            send_br().wait_recv()

            def add(j):
                at = rows_of(j, 32)
                br_n[at, cols_of(core)] = (br_n[at, cols_of(core)].astype(F32) + g_got[at, :].astype(F32)).astype(BF16)

            blocks(width // 32, add)
            for d in (3, 2, 1, 0):
                out_br(d).start()

        spread.serve(t, finish)
        return carry

    lax.fori_loop(0, LINE - 1, drain, 0)
    mine = pl.ds(pl.multiple_of(core * seq, seq), seq)
    for side in (0, 1):
        for e in range(4):
            at = slice(e * 64, (e + 1) * 64)
            gd[side, at, 0:64] = gate_grad[side, at, e * 64 : (e + 1) * 64]
            gd[side, at, 64:128] = gate_grad[side, at, 256 + e * 64 : 256 + (e + 1) * 64]
    swap_gd = remote(gd.at[1 - core], gd_in, v_send.at[0], v_recv.at[0], sibling)
    swap_gd.start()
    lane = lax.broadcasted_iota(jnp.int32, (64, 128), 1)

    def columns(parts, at):
        total = jnp.zeros((64, 128), F32)
        for n, part in enumerate(parts):
            total = total + jnp.where(lane == n, jnp.sum(part(at), axis=1, keepdims=True), 0.0)
        return total

    vec[...] = jnp.zeros(vec.shape, F32)
    for j in range(chan // 64):
        at = slice(j * 64, (j + 1) * 64)
        v = columns([lambda at, n=n: small[n, at, :] for n in range(8)], at)
        vec[0, :, at] = v.T[0:8, :]

    for k in range(PARTS):
        for d in (1, 2, 3):
            share(k, d).wait_send()
            piece = sums.at[k, z ^ d]
            remote(piece, piece, l_send.at[k, d - 1], l_recv.at[k, d - 1], at_line(z ^ d, core)).wait_recv()
        total = jnp.sum(jnp.sum(sums[k], axis=0), axis=0, keepdims=True)
        at = slice(k * PART, (k + 1) * PART)
        s1 = scale_one[:, at]
        coef[:, at] = s1 * s1 * s1 * (total / width)

    def last(i):
        at = rows_of(i, 16)
        v = dy[at, :] + (
            scale_one[0:1, :] * (gains[at, 8:9] * dn1[at, :]) - x_own[at, :].astype(F32) * coef[0:1, :]
        )
        dy[at, :] = v

    blocks(block // 16, last)
    back = remote(dy.at[rows_of(1 - core, half), :], input_grad.at[:, mine], r_send, r_recv, sibling)
    back.start()
    keep_in = pltpu.make_async_copy(dy.at[rows_of(core, half), :], input_grad.at[:, mine], d_own.at[3])
    keep_in.start()
    for j in range(block // 64):
        at = slice(j * 64, (j + 1) * 64)
        v = columns([lambda at: mix_part[at, :], lambda at: feed_part[at, :]], at)
        vec[1, :, at] = v.T[0:8, :]
    swap_vec = remote(vec, vec_in, v_send.at[1], v_recv.at[1], sibling)
    swap_vec.start()
    swap_gd.wait()
    gd_all[0] = gd[core] + gd_in[...]
    rows_gd = [
        remote(gd_all.at[0], gd_all.at[d], n_send.at[0, d - 1], n_recv.at[0, d - 1], {"row": row ^ d}) for d in (1, 2, 3)
    ]
    for copy in rows_gd:
        copy.start()
    swap_vec.wait()
    vec_all[0] = vec[...] + vec_in[...]
    rows_vec = [
        remote(vec_all.at[0], vec_all.at[d], n_send.at[1, d - 1], n_recv.at[1, d - 1], {"row": row ^ d}) for d in (1, 2, 3)
    ]
    for copy in rows_vec:
        copy.start()
    spread.sent()
    for copy in rows_gd + rows_vec:
        copy.wait()
    for every, out in ((gd_all, tiny_g), (vec_all, tiny_v)):
        first, second = every[row % 2], every[1 - row % 2]
        third, fourth = every[2 + row % 2], every[3 - row % 2]
        out[...] = (first + second) + (third + fourth)
    for d in range(PARTS):
        for out in f_out(d):
            out.wait()
    send_br().wait_send()
    send_m().wait_send()
    for d in (0, 1, 2, 3):
        out_br(d).wait()
        out_m(d).wait()
    for copy in (keep_in, back):
        copy.wait()


def last_kernel(
    f_sum, f_land, fd_sum, fd_land, g_sum, g_land, gm_sum, gm_land, tiny_v, tiny_g, lambdas,
    s_b, s_r, s_m, s_g, s_u, s_d, taps, offs, bias_r, bias_a, decay, mix, feed, retain, admit,
):
    core = place()[2]
    lru, block = s_m.shape
    ff, half = s_d.shape[0], mix.shape[1]

    def four(first, others, at):
        return first[at, :].astype(F32) + others[0, at, :].astype(F32) + (
            others[1, at, :].astype(F32) + others[2, at, :].astype(F32)
        )

    def put_gu(i):
        at = rows_of(i, 32)
        v = four(f_sum, f_land, at)
        s_g[at, :] = v[:, :ff]
        s_u[at, :] = v[:, ff:]
        v = four(g_sum, g_land, at)
        s_b[at, :] = v[:, :lru]
        s_r[at, :] = v[:, lru:]

    blocks(block // 32, put_gu)

    def put_d(i):
        at = rows_of(i, 32)
        s_d[at, :] = four(fd_sum, fd_land, at)

    blocks(ff // 32, put_d)

    def put_m(i):
        at = rows_of(i, 32)
        s_m[at, :] = four(gm_sum, gm_land, at)

    blocks(lru // 32, put_m)
    small = tiny_v[0, :, pl.ds(pl.multiple_of(core * lru, 128), lru)]
    taps[...] = small[0:4]
    offs[...] = small[4:5]
    bias_r[...] = small[5:6]
    bias_a[...] = small[6:7]
    decay[...] = small[7:8] * (8.0 * jax.nn.sigmoid(-lambdas[...]))
    gains = jnp.where(core == 0, tiny_v[1, :, 0:half], tiny_v[1, :, half : 2 * half])
    mix[...] = gains[0:1]
    feed[...] = gains[1:2]
    for e in range(retain.shape[0]):
        at = slice(e * 64, (e + 1) * 64)
        retain[e] = tiny_g[at, 0:64]
        admit[e] = tiny_g[at, 64:128]


ANY = pl.BlockSpec(memory_space=pl.ANY)
VM = pl.BlockSpec(memory_space=pltpu.VMEM)
DMA = pltpu.SemaphoreType.DMA
ROOM = 62 * 1024 * 1024


def shape(dims, kind):
    return jax.ShapeDtypeStruct(dims, kind)


def call(kernel, ins, outs, scratch, ident, name, flops):
    return pl.pallas_call(
        kernel,
        out_shape=[o[0] for o in outs],
        in_specs=ins,
        out_specs=[o[1] for o in outs],
        scratch_shapes=scratch,
        name=name,
        compiler_params=pltpu.CompilerParams(
            collective_id=ident, has_side_effects=True, vmem_limit_bytes=ROOM
        ),
        cost_estimate=pl.CostEstimate(flops=flops, bytes_accessed=40000000, transcendentals=0),
    )


def fast_body(
    inputs, segments, mix_gain, branch_weight, recur_weight, kernel, offsets, retain_weight, retain_bias,
    admit_weight, admit_bias, lambdas, merge_weight, feed_gain, gate_weight, up_weight, down_weight, cotangent,
):
    half, tokens = inputs.shape
    block, seq, width = 2 * half, tokens // 2, D
    lru, heads = branch_weight.shape[1], retain_weight.shape[0]
    chan = 2 * lru
    ff = gate_weight.shape[1]
    hid = 2 * ff
    rows = branch_weight.shape[0]
    cols = merge_weight.shape[1]
    rate = 8.0 * jax.nn.softplus(-lambdas)
    vec = [kernel] + [v[None, :] for v in (offsets, retain_bias, admit_bias, rate)]
    vec += [jnp.pad(v[None, :], ((0, 0), (0, lru - half))) for v in (mix_gain, feed_gain)]
    vec = jnp.concatenate(vec + [jnp.zeros((6, lru), F32)])
    br_s = jnp.concatenate([branch_weight, recur_weight], axis=1).T
    m_s = merge_weight.T
    gu_s = jnp.concatenate([gate_weight, up_weight], axis=1).T

    f_tok = lambda n, kind=F32: shape((n, seq), kind)
    padded = (shape((chan, 128 + seq), F32), ANY)
    state = [(f_tok(chan), ANY), padded, *[(f_tok(chan), ANY)] * 3, padded]
    line = [DMA((3,)), DMA((3,))]
    steps = [DMA((2, 3, PARTS)), DMA((2, 3, PARTS))]
    sums = [DMA((2, PARTS, LINE)), DMA((2, PARTS, LINE))]
    held = pltpu.VMEM((PARTS, LINE + 1, block, PART), BF16)
    own_low = pltpu.VMEM((PARTS, LINE, block, PART), BF16)
    tok = lambda n, kind=F32, lead=0: pltpu.VMEM((n, lead + seq), kind)
    one = lambda n, kind=F32, lead=0: pltpu.VMEM((n, lead + PART), kind)
    br_t = jnp.concatenate([branch_weight, recur_weight], axis=1)
    grad_gu, grad_d = (shape((width, 2 * ff), BF16), ANY), (shape((ff, width), BF16), ANY)
    low = lambda n, m: (shape((n, m), BF16), ANY)

    (masks, par, gains, gates, coef, scale_one, scale_two, y, n1, q, x_own, g, b, p, u, r, i, h, result, dn2, _, _, f_own, f_got, fd_own, fd_got,
     br_n, m_n) = call(
        functools.partial(forward_kernel, width, EPS),
        [ANY] * 2 + [VM] * 4 + [ANY] * 6,
        [(shape((8, seq + 128), F32), VM), (shape((chan, 16), F32), VM), (shape((block, 16), F32), VM), (shape((2, lru, 2 * lru), BF16), VM),
         (f_tok(8), VM), (f_tok(8), VM), (f_tok(8), VM), (f_tok(block), ANY), low(width, seq), low(chan, seq), low(block, seq), low(block, seq)]
        + state + [low(half, tokens), (f_tok(block), ANY), low(2 * hid, seq), low(hid, seq), grad_gu, grad_gu, grad_d, grad_d,
                   low(width, 2 * chan), low(chan, width)],
        [pltpu.VMEM((LINE, 8, seq), F32), pltpu.VMEM((PARTS, LINE, 8, PART), F32), pltpu.VMEM((PARTS, LINE, 8, PART), F32),
         pltpu.VMEM((2, 16, lru), F32), pltpu.VMEM((2, 2) + retain_weight.shape, F32), pltpu.VMEM((2, 2 * lru, lru), BF16),
         pltpu.VMEM((2, 2 * lru, lru), BF16), tok(width, BF16), tok(width, BF16),
         tok(width, BF16), tok(block, BF16), tok(block), one(block), one(chan, BF16),
         one(chan, F32, 128), one(chan, F32, 128), one(5 * chan), one(chan, BF16), one(chan, BF16),
         own_low, held, held, held, pltpu.VMEM((2 * hid, width), BF16), pltpu.VMEM((width, 2 * hid), BF16),
         pltpu.VMEM((hid, width), BF16), pltpu.VMEM((width, hid), BF16), one(hid, BF16), one(2 * hid, BF16),
         DMA((5,)), DMA((5,)), DMA((5,))] + line + [DMA((PARTS, 3)), DMA((PARTS, 3))] * 2 + steps * 3 + sums * 3
        + [DMA((7, 7)), DMA((7, 7)), DMA((7,)), DMA((7,)), DMA((7,)), DMA((4,)), DMA((4,)), DMA((4,))],
        0, "forward", 50 * 10**9,
    )(inputs, cotangent, segments[None, :], vec, retain_weight, admit_weight, br_s, m_s, gu_s, down_weight,
      br_t, merge_weight)

    pair = lambda lead=0: pltpu.VMEM((2, chan, lead + PART), F32)
    land = lambda n, m: ((shape((n, m), BF16), ANY), (shape((3, n, m), BF16), ANY))
    input_grad, tiny_v, tiny_g, *sums_of = call(
        functools.partial(back_kernel, width),
        [VM] + [ANY] * 2 + [VM] * 8 + [ANY] * 14,
        [(shape((half, tokens), F32), ANY), (shape((2, 8, chan), F32), VM),
         (shape((lru, 128), F32), VM), *land(cols, 2 * ff), *land(ff, cols), *land(cols, 2 * lru), *land(lru, cols)],
        [pltpu.VMEM((PARTS, LINE, 8, PART), F32), pltpu.VMEM((8, seq), F32),
         pltpu.VMEM((chan, width), BF16), pltpu.VMEM((width, 2 * chan), BF16),
         pair(), pair(128), pair(), pair(), pair(), pair(128), tok(width, BF16), tok(2 * chan, BF16),
         tok(block), tok(block), pltpu.VMEM((chan, PART), F32), pltpu.VMEM((chan, PART + 128), F32), pltpu.VMEM((2 * chan, PART), BF16),
         pltpu.VMEM((chan, PART), F32), pltpu.VMEM((chan, PART), F32), pltpu.VMEM((chan, 128), F32), own_low, held,
         tok(chan, BF16), pltpu.VMEM((4, cols, 2 * ff), BF16), pltpu.VMEM((cols, 2 * ff), BF16),
         pltpu.VMEM((4, ff, cols), BF16), pltpu.VMEM((ff, cols), BF16),
         pltpu.VMEM((block, 128), F32), pltpu.VMEM((block, 128), F32), pltpu.VMEM((8, chan, 128), F32),
         pltpu.VMEM((2, lru, 2 * lru), F32), tok(block, BF16), pltpu.VMEM((width, 2 * lru), BF16),
         pltpu.VMEM((lru, width), BF16), pltpu.VMEM((2, 8, chan), F32), pltpu.VMEM((2, 8, chan), F32),
         pltpu.VMEM((4, 2, 8, chan), F32), pltpu.VMEM((2, lru, 128), F32), pltpu.VMEM((lru, 128), F32),
         pltpu.VMEM((4, lru, 128), F32), DMA((7,)), DMA((6, 2))] + [DMA((PARTS, 3)), DMA((PARTS, 3))] + steps + sums
        + [DMA, DMA, DMA((2, 2)), DMA((2, PARTS)), DMA((2, PARTS)), DMA((2,)), DMA((2,)), DMA((4,))]
        + [DMA((2, 3)), DMA((2, 3)), DMA((2, 3)), DMA((2, 3)), DMA((2,)), DMA((2,))],
        2, "mix_backward", 10 * 10**9,
    )(y, dn2, g, x_own, scale_two, scale_one, coef, gains, masks, par, gates, m_n, br_n, b, p, u, r, i, h,
      q, n1, f_own, f_got, fd_own, fd_got)

    line_of = shape((1, lru), F32)
    s_b, s_r, s_m, s_g, s_u, s_d, taps, offs, bias_r, bias_a, decay, mix, feed, retain, admit = pl.pallas_call(
        last_kernel,
        out_shape=[shape((cols, lru), F32)] * 2 + [shape((lru, cols), F32)] + [shape((cols, ff), F32)] * 2
        + [shape((ff, cols), F32), shape((4, lru), F32)] + [line_of] * 4 + [shape((1, half), F32)] * 2
        + [shape((heads, 64, 64), F32)] * 2,
        in_specs=[VM] * 11,
        out_specs=[VM] * 15,
        name="last_sums",
        compiler_params=pltpu.CompilerParams(vmem_limit_bytes=ROOM),
    )(*sums_of, tiny_v, tiny_g, lambdas[None, :])
    return (
        result,
        input_grad,
        mix[0],
        s_b,
        s_r,
        taps,
        offs[0],
        retain,
        bias_r[0],
        admit,
        bias_a[0],
        decay[0],
        s_m,
        feed[0],
        s_g,
        s_u,
        s_d,
    )


def suits(mesh, args):
    return (
        dict(mesh.shape) == {"row": 4, "col": 8}
        and args[0].shape == (D, 8 * SEQ)
        and args[3].shape == (D, 2048)
        and args[14].shape == (D, 4608)
        and args[7].shape == (32, 64, 64)
    )


def solution(mesh):
    in_specs = (
        P("col", "row"),
        P("row"),
        P("col"),
        P("row", "col"),
        P("row", "col"),
        P(None, "col"),
        P("col"),
        P("col", None, None),
        P("col"),
        P("col", None, None),
        P("col"),
        P("col"),
        P("col", "row"),
        P("col"),
        P("row", "col"),
        P("row", "col"),
        P("col", "row"),
        P("col", "row"),
    )
    out_specs = (
        P("col", "row"),
        P("col", "row"),
        P("col"),
        P("row", "col"),
        P("row", "col"),
        P(None, "col"),
        P("col"),
        P("col", None, None),
        P("col"),
        P("col", None, None),
        P("col"),
        P("col"),
        P("col", "row"),
        P("col"),
        P("row", "col"),
        P("row", "col"),
        P("col", "row"),
    )
    def run(*args):
        chosen = fast_body if suits(mesh, args) else body
        return jax.shard_map(
            chosen, mesh=mesh, in_specs=in_specs, out_specs=out_specs, check_vma=False
        )(*args)

    return run
```

```python
import functools

import jax
import jax.numpy as jnp
from jax import lax
from jax.experimental import pallas as pl
from jax.experimental.pallas import tpu as pltpu
from jax.sharding import PartitionSpec as P

D = 1536
SEQ = 1024
MICRO = 2


HIGH = lax.Precision.HIGHEST
EPS = 1e-06
POWER = 8.0
FLOOR = 0.01


def combine(earlier, later):
    first_a, first_b = earlier
    second_a, second_b = later
    return (first_a * second_a, second_a * first_b + second_b)


def mixer(
    branch_pre,
    lru_pre,
    segs,
    kernel,
    offsets,
    retain_weight,
    retain_bias,
    admit_weight,
    admit_bias,
    lambdas,
):
    length = lru_pre.shape[0]
    channels = lru_pre.shape[1]
    conv = offsets + kernel[0] * lru_pre
    for lag in range(1, kernel.shape[0]):
        shifted = jnp.concatenate(
            [jnp.zeros((lag, channels), lru_pre.dtype), lru_pre[:-lag]], axis=0
        )
        prior = jnp.concatenate([jnp.full((lag,), -1, jnp.int32), segs[:-lag]])
        keep = (prior == segs).astype(lru_pre.dtype)
        conv = conv + kernel[lag] * shifted * keep[:, None]
    heads = retain_weight.shape[0]
    blocks = conv.reshape(length, heads, channels // heads)
    retain = jax.nn.sigmoid(
        jnp.einsum("thi,hij->thj", blocks, retain_weight, precision=HIGH).reshape(length, channels)
        + retain_bias
    )
    admit = jax.nn.sigmoid(
        jnp.einsum("thi,hij->thj", blocks, admit_weight, precision=HIGH).reshape(length, channels)
        + admit_bias
    )
    decay = jnp.exp(-POWER * retain * jax.nn.softplus(-lambdas))
    factor = jnp.sqrt(1.0 - decay * decay + FLOOR)
    starts = jnp.concatenate([jnp.ones((1,), bool), segs[1:] != segs[:-1]])
    decay = jnp.where(starts[:, None], 0.0, decay)
    factor = jnp.where(starts[:, None], 1.0, factor)
    _, state = lax.associative_scan(combine, (decay, factor * admit * conv), axis=0)
    return jax.nn.gelu(branch_pre) * state


def geglu(gate, upper):
    return jax.nn.gelu(gate) * upper


def contract_rows(left, right):
    return lax.dot_general(
        left, right, (((0,), (0,)), ((), ())), preferred_element_type=jnp.float32
    )


def contract_cols(left, right):
    return lax.dot_general(
        left, right, (((1,), (1,)), ((), ())), preferred_element_type=jnp.float32
    )


def contract_cross(left, right):
    return lax.dot_general(
        left, right, (((0,), (1,)), ((), ())), preferred_element_type=jnp.float32
    )


def norm_forward(resid, gain):
    total = lax.psum(jnp.sum(resid * resid, axis=0), "col")
    scale = lax.rsqrt(total / D + EPS)[None, :]
    return (scale, (resid * scale * gain[:, None]).astype(jnp.bfloat16))


def norm_backward(resid, scale, gain, grad_normed):
    weighted = grad_normed * gain[:, None]
    total = lax.psum(jnp.sum(weighted * resid, axis=0), "col")
    grad_resid = scale * weighted - resid * (scale * scale * scale) * (total / D)[None, :]
    grad_gain = jnp.sum(grad_normed * resid * scale, axis=1)
    return (grad_resid, grad_gain)


def gather_features(normed):
    return lax.all_gather(normed, "col", axis=0, tiled=True)


def gather_cotangent(grad):
    return lax.all_gather(grad, "col", axis=0, tiled=True)


def spread_sum(term):
    return lax.psum_scatter(
        term.astype(jnp.bfloat16), "col", scatter_dimension=0, tiled=True
    ).astype(jnp.float32)


def back_sum(term):
    return spread_sum(term)


def merge_term(whole_merge, mixed_low):
    return spread_sum(contract_cross(whole_merge, mixed_low))


def weight_grads(normed, grad_joined):
    return jnp.dot(
        normed,
        grad_joined,
        preferred_element_type=jnp.float32,
    )


def row_sum(total, axis):
    return lax.psum_scatter(
        total.astype(jnp.bfloat16), "row", scatter_dimension=axis, tiled=True
    ).astype(jnp.float32)


def body(
    inputs,
    segments,
    mix_gain,
    branch_weight,
    recur_weight,
    kernel,
    offsets,
    retain_weight,
    retain_bias,
    admit_weight,
    admit_bias,
    lambdas,
    merge_weight,
    feed_gain,
    gate_weight,
    up_weight,
    down_weight,
    cotangent,
):
    lru_cols = branch_weight.shape[1]
    feed_cols = gate_weight.shape[1]
    mixer_params = (kernel, offsets, retain_weight, retain_bias, admit_weight, admit_bias, lambdas)
    acc_branch = jnp.zeros((D, lru_cols), jnp.float32)
    acc_recur = jnp.zeros((D, lru_cols), jnp.float32)
    acc_gate = jnp.zeros((D, feed_cols), jnp.float32)
    acc_up = jnp.zeros((D, feed_cols), jnp.float32)
    acc_merge = jnp.zeros((lru_cols, D), jnp.float32)
    acc_down = jnp.zeros((feed_cols, D), jnp.float32)
    acc_small = tuple((jnp.zeros_like(p) for p in mixer_params))
    acc_mix = jnp.zeros_like(mix_gain)
    acc_feed = jnp.zeros_like(feed_gain)
    outputs = []
    in_grads = []
    for batch in range(MICRO):
        lower = batch * SEQ
        resid_in = inputs[:, lower : lower + SEQ].astype(jnp.float32)
        grad_out = cotangent[:, lower : lower + SEQ].astype(jnp.float32)
        segs = segments[lower : lower + SEQ]
        whole_branch, whole_recur, whole_gate, whole_up = (
            lax.all_gather(branch_weight, "row", axis=0, tiled=True),
            lax.all_gather(recur_weight, "row", axis=0, tiled=True),
            lax.all_gather(gate_weight, "row", axis=0, tiled=True),
            lax.all_gather(up_weight, "row", axis=0, tiled=True),
        )
        whole_merge, whole_down = (
            lax.all_gather(merge_weight, "row", axis=1, tiled=True),
            lax.all_gather(down_weight, "row", axis=1, tiled=True),
        )
        scale_one, normed_one = norm_forward(resid_in, mix_gain)
        full_one = gather_features(normed_one)
        branch_pre = contract_rows(full_one, whole_branch)
        lru_pre = contract_rows(full_one, whole_recur)

        def local_mixer(bpre, lpre, kern, offs, rweight, rbias, aweight, abias, lams):
            return mixer(bpre, lpre, segs, kern, offs, rweight, rbias, aweight, abias, lams)

        mixed, mixer_pull = jax.vjp(local_mixer, branch_pre, lru_pre, *mixer_params)
        mixed_low = mixed.astype(jnp.bfloat16)
        resid_mid = resid_in + merge_term(whole_merge, mixed_low)
        scale_two, normed_two = norm_forward(resid_mid, feed_gain)
        full_two = gather_features(normed_two)
        gate = contract_rows(full_two, whole_gate)
        upper = contract_rows(full_two, whole_up)
        hidden, geglu_pull = jax.vjp(geglu, gate, upper)
        hidden_low = hidden.astype(jnp.bfloat16)
        result = resid_mid + spread_sum(contract_cross(whole_down, hidden_low))
        outputs.append(result.astype(jnp.bfloat16))
        grad_full = gather_cotangent(grad_out.astype(jnp.bfloat16))
        acc_down = acc_down + contract_cross(hidden_low, grad_full)
        grad_gate, grad_upper = geglu_pull(contract_cross(grad_full, whole_down))
        grad_gate = grad_gate.astype(jnp.bfloat16)
        grad_upper = grad_upper.astype(jnp.bfloat16)
        feed_joined = weight_grads(full_two, jnp.concatenate([grad_gate, grad_upper], axis=1))
        acc_gate = acc_gate + feed_joined[:, :feed_cols]
        acc_up = acc_up + feed_joined[:, feed_cols:]
        grad_normed_two = back_sum(
            contract_cols(whole_gate, grad_gate) + contract_cols(whole_up, grad_upper)
        )
        grad_mid_norm, feed_part = norm_backward(resid_mid, scale_two, feed_gain, grad_normed_two)
        acc_feed = acc_feed + feed_part
        grad_mid = grad_out + grad_mid_norm
        grad_mid_full = gather_cotangent(grad_mid.astype(jnp.bfloat16))
        acc_merge = acc_merge + contract_cross(mixed_low, grad_mid_full)
        pulled = mixer_pull(contract_cross(grad_mid_full, whole_merge))
        grad_branch = pulled[0].astype(jnp.bfloat16)
        grad_lru = pulled[1].astype(jnp.bfloat16)
        acc_small = tuple((total + part for total, part in zip(acc_small, pulled[2:])))
        branch_joined = weight_grads(full_one, jnp.concatenate([grad_branch, grad_lru], axis=1))
        acc_branch = acc_branch + branch_joined[:, :lru_cols]
        acc_recur = acc_recur + branch_joined[:, lru_cols:]
        grad_normed_one = back_sum(
            contract_cols(whole_branch, grad_branch) + contract_cols(whole_recur, grad_lru)
        )
        grad_in_norm, mix_part = norm_backward(resid_in, scale_one, mix_gain, grad_normed_one)
        acc_mix = acc_mix + mix_part
        in_grads.append(grad_mid + grad_in_norm)
    sum_branch, sum_recur, sum_gate, sum_up = (
        row_sum(acc_branch, 0),
        row_sum(acc_recur, 0),
        row_sum(acc_gate, 0),
        row_sum(acc_up, 0),
    )
    sum_merge, sum_down = (
        row_sum(acc_merge, 1),
        row_sum(acc_down, 1),
    )
    summed = lax.psum(
        (
            acc_mix,
            acc_feed,
            acc_small[0],
            acc_small[1],
            acc_small[2],
            acc_small[3],
            acc_small[4],
            acc_small[5],
            acc_small[6],
        ),
        "row",
    )
    result_all = jnp.concatenate(outputs, axis=1)
    input_grad = jnp.concatenate(in_grads, axis=1)
    return (
        result_all,
        input_grad,
        summed[0],
        sum_branch,
        sum_recur,
        summed[2],
        summed[3],
        summed[4],
        summed[5],
        summed[6],
        summed[7],
        summed[8],
        sum_merge,
        summed[1],
        sum_gate,
        sum_up,
        sum_down,
    )


MESH = pl.DeviceIdType.MESH
F32 = jnp.float32
BF16 = jnp.bfloat16
LINE = 4
PART = 256
PARTS = 4
GELU_A = 0.7978845608028654
GELU_B = 0.044715


def place():
    row, col = lax.axis_index("row"), lax.axis_index("col")
    return row, col // 2, col % 2


def at_line(z, core):
    return {"col": 2 * z + core}


def lanes(part):
    return pl.ds(pl.multiple_of(part * PART, PART), PART)


def rows_of(index, size):
    return pl.ds(pl.multiple_of(index * size, 16), size)


def dot(a, b):
    return lax.dot_general(a, b, (((1,), (0,)), ((), ())), preferred_element_type=F32)


def dot_nt(a, b):
    return lax.dot_general(a, b, (((1,), (1,)), ((), ())), preferred_element_type=F32)


def greet(row, z, core, rows, line):
    barrier = pltpu.get_barrier_semaphore()
    peers = [{"col": 2 * z + (1 - core)}]
    if rows:
        peers += [{"row": row ^ d} for d in (1, 2, 3)]
    if line:
        peers += [at_line(z ^ d, core) for d in (1, 2, 3)]
    for peer in peers:
        pl.semaphore_signal(barrier, inc=1, device_id=peer, device_id_type=MESH)
    pl.semaphore_wait(barrier, len(peers))


def remote(src, dst, send, recv, peer):
    return pltpu.make_async_remote_copy(
        src_ref=src, dst_ref=dst, send_sem=send, recv_sem=recv, device_id=peer, device_id_type=MESH
    )


class Gather:
    def __init__(self, ref, send, recv, z, core, block, back=False):
        self.ref, self.sems, self.z, self.core = ref, (send, recv), z, core
        self.block, self.back = block, back

    def copy(self, way, hop, step, owner, incoming=False):
        part = PARTS - 1 - step if self.back else step
        piece = self.ref.at[rows_of(owner, self.block), lanes(part)]
        peer = at_line(self.z + (1 if (way == 0) != incoming else -1), self.core)
        return remote(piece, piece, self.sems[0].at[way, hop, step], self.sems[1].at[way, hop, step], peer)

    def each(self, hop, act, incoming):
        z = self.z
        if incoming:
            cases = ((0, z - 1 - hop >= 0, z - 1 - hop), (1, z + 1 + hop < LINE, z + 1 + hop))
        else:
            cases = (
                (0, (z >= hop) & (z < LINE - 1), z - hop),
                (1, (z + hop < LINE) & (z >= 1), z + hop),
            )
        for way, here, owner in cases:
            pl.when(here)(functools.partial(act, way, owner))

    def send(self, hop, step):
        self.each(hop, lambda way, owner: self.copy(way, hop, step, owner).start(), False)

    def arrive(self, hop, step):
        self.each(hop, lambda way, owner: self.copy(way, hop, step, owner, True).wait_recv(), True)

    def forward(self, hop, step):
        self.arrive(hop - 1, step)
        self.send(hop, step)

    def sent(self):
        def one(step, carry):
            for hop in range(LINE - 1):
                self.each(hop, lambda way, owner: self.copy(way, hop, step, owner).wait_send(), False)
            return carry

        lax.fori_loop(0, PARTS, one, 0)

    def open(self):
        self.send(0, 0)
        self.forward(1, 0)
        self.send(0, 1)
        self.forward(2, 0)

    def middle(self, step):
        @pl.when(step + 1 < PARTS)
        def _():
            self.forward(1, step + 1)

        @pl.when(step + 2 < PARTS)
        def _():
            self.send(0, step + 2)

    def later(self, step):
        @pl.when(step + 1 < PARTS)
        def _():
            self.forward(2, step + 1)


class Spread:
    def __init__(self, own, held, send, recv, z, core):
        self.own, self.held, self.sems, self.z, self.core = own, held, (send, recv), z, core

    def copy(self, way, step, hop):
        slot = hop if way == 0 else LINE - hop
        there = slot - 1 if way == 0 else slot + 1
        peer = at_line(self.z + (1 if way == 0 else -1), self.core)
        return remote(
            self.held.at[step, slot],
            self.held.at[step, there],
            self.sems[0].at[way, step, hop],
            self.sems[1].at[way, step, hop - 1],
            peer,
        )

    def landed(self, way, step, hop):
        slot = hop if way == 0 else LINE - hop
        piece = self.held.at[step, slot]
        peer = at_line(self.z + (-1 if way == 0 else 1), self.core)
        remote(piece, piece, self.sems[0].at[way, step, hop], self.sems[1].at[way, step, hop], peer).wait_recv()

    def push(self, way, step, first):
        z = self.z

        def one(i, carry):
            hop = LINE - 1 - i
            owner = z + hop if way == 0 else z - hop
            slot = hop if way == 0 else LINE - hop

            @pl.when((owner >= 0) & (owner < LINE))
            def _():
                @pl.when(first)
                def _():
                    self.held[step, slot] = self.own(step, owner)[...].astype(BF16)

                @pl.when(jnp.logical_not(first))
                def _():
                    self.landed(way, step, hop)
                    total = self.own(step, owner)[...].astype(F32) + self.held[step, slot].astype(F32)
                    self.held[step, slot] = total.astype(BF16)

                self.copy(way, step, hop).start()

            return carry

        lax.fori_loop(0, LINE - 1, one, 0)

    def serve(self, t, finish):
        z = self.z
        step = t - (LINE - 1)

        @pl.when((step >= 0) & (step < PARTS))
        def _():
            @pl.when(z == 0)
            def _():
                self.landed(1, step, 0)
                finish(step, lambda a, n: self.mine(step, a, n) + self.got(step, LINE, a, n))

            @pl.when(z == LINE - 1)
            def _():
                self.landed(0, step, 0)
                finish(step, lambda a, n: self.mine(step, a, n) + self.got(step, 0, a, n))

            @pl.when((z > 0) & (z < LINE - 1))
            def _():
                self.landed(0, step, 0)
                self.landed(1, step, 0)
                finish(
                    step,
                    lambda a, n: self.mine(step, a, n) + (self.got(step, 0, a, n) + self.got(step, LINE, a, n)),
                )

        for way, late, turn in ((1, LINE - 1 - z, z < 2), (0, z, z >= 0), (1, LINE - 1 - z, z >= 2)):
            step = t - late
            pl.when((step >= 0) & (step < PARTS) & turn)(functools.partial(self.push, way, step, late == 0))

    def mine(self, step, start, size):
        return self.own(step, self.z)[pl.ds(start, size), :].astype(F32)

    def got(self, step, slot, start, size):
        return self.held[step, slot, pl.ds(start, size)].astype(F32)

    def sent(self):
        z = self.z

        def one(step, carry):
            for way in (0, 1):
                for hop in range(1, LINE):
                    owner = z + hop if way == 0 else z - hop

                    @pl.when((owner >= 0) & (owner < LINE))
                    def _():
                        self.copy(way, step, hop).wait_send()

            return carry

        lax.fori_loop(0, PARTS, one, 0)


def share_line(ref, send, recv, z, core):
    copies = [
        remote(ref.at[z], ref.at[z], send.at[d - 1], recv.at[d - 1], at_line(z ^ d, core)) for d in (1, 2, 3)
    ]
    for copy in copies:
        copy.start()
    for d in (1, 2, 3):
        piece = ref.at[z ^ d]
        remote(piece, piece, send.at[d - 1], recv.at[d - 1], at_line(z ^ d, core)).wait_recv()
    for copy in copies:
        copy.wait_send()


class Weights:
    def __init__(self, src, dst, send, recv, own, row, z, core, turned, stride=0, start=0):
        self.src, self.dst, self.send, self.recv, self.own = src, dst, send, recv, own
        self.row, self.core, self.turned = row, core, turned
        self.stride, self.first = stride or src.shape[0], start
        self.sibling = {"col": 2 * z + (1 - core)}

    def spot(self, row, core):
        down, right = (row, core) if self.turned else (core, row)
        rows, cols = self.src.shape
        at = pl.ds(pl.multiple_of(down * self.stride + self.first, 16), rows)
        return self.dst.at[at, pl.ds(pl.multiple_of(right * cols, 128), cols)]

    def to_row(self, d):
        return remote(
            self.src, self.spot(self.row, self.core), self.send.at[d], self.recv.at[d], {"row": self.row ^ d}
        )

    def to_sibling(self, d):
        if d == 0:
            return remote(
                self.src, self.spot(self.row, self.core), self.send.at[0], self.recv.at[0], self.sibling
            )
        piece = self.spot(self.row ^ d, self.core)
        return remote(piece, piece, self.send.at[3 + d], self.recv.at[3 + d], self.sibling)

    def local(self):
        return pltpu.make_async_copy(self.src, self.spot(self.row, self.core), self.own)

    def start(self):
        for d in (1, 2, 3):
            self.to_row(d).start()
        self.to_sibling(0).start()
        self.local().start()

    def forward(self):
        for d in (1, 2, 3):
            piece = self.spot(self.row ^ d, self.core)
            remote(piece, piece, self.send.at[d], self.recv.at[d], {"row": self.row ^ d}).wait_recv()
            self.to_sibling(d).start()

    def finish(self):
        self.local().wait()
        for d in (0, 1, 2, 3):
            piece = self.spot(self.row ^ d, 1 - self.core)
            sem = 0 if d == 0 else 3 + d
            remote(piece, piece, self.send.at[sem], self.recv.at[sem], self.sibling).wait_recv()

    def sent(self):
        for d in (1, 2, 3):
            self.to_row(d).wait_send()
            self.to_sibling(d).wait_send()
        self.to_sibling(0).wait_send()


def gelu_parts(b):
    t = jnp.tanh(GELU_A * (b + GELU_B * (b * b * b)))
    half = 0.5 + 0.5 * t
    slope = half + (0.5 * b) * (1.0 - t * t) * (GELU_A + (3.0 * GELU_A * GELU_B) * (b * b))
    return b * half, slope


def eight(v):
    return jnp.sum(v.reshape(v.shape[0] // 8, 8, v.shape[1]), axis=0)


def blocks(count, body):
    def one(i, carry):
        body(i)
        return carry

    lax.fori_loop(0, count, one, 0)


def scale_of(ref, eps, width):
    total = jnp.sum(jnp.sum(ref[...], axis=0), axis=0, keepdims=True)
    return lax.rsqrt(total / width + eps)


def forward_kernel(
    width, eps,
    x_in, g_in, segs, vec, retain, admit, br_s, m_s, gu_s, d_s, brn_s, mn_s,
    masks, par, gains, gates, coef, scale, scale_two, y_out, n1_out, q_out, x_out, g_out, b_out, p_out, u_out, r_out, i_out, h_out,
    result, dn2_out, dev_h, z_h, g_own, g_got, gd_own, gd_got, br_n, m_n,
    sums, sums2, sums3, vec_all, block_all, gates_hi, gates_lo, normed, normed2, go, x_own, y, dn2, q_c, p_s, h_s, room, uh, ul,
    own, held, held_n, held_o, gu, gun, down, dt, zs, dev,
    x_send, x_recv, x_loc, l_send, l_recv, n_send, n_recv, c_send, c_recv, g_send, g_recv, e_send, e_recv, f_send, f_recv,
    s_send, s_recv, t_send, t_recv, o_send, o_recv, w_send, w_recv, w_own, k_sem, v_sem, d_send, d_recv, d_own,
):
    row, z, core = place()
    block, seq = y.shape
    half = x_in.shape[0]
    chan = p_s.shape[0]
    hid = zs.shape[0]
    b_s, u_s, r_s, i_s, a_c = [room.at[n * chan : (n + 1) * chan, :] for n in range(5)]
    ev, dz = room.at[0 : 2 * hid, :], room.at[2 * hid : 3 * hid, :]
    hh = hid // 2
    hc = chan // 2
    sibling = {"col": 2 * z + (1 - core)}
    greet(row, z, core, True, True)
    br, mt = gun.at[0 : 2 * chan, 0:width], dt.at[:, 0:chan]
    wide = br_s.shape[0]
    recur_s, branch_s = br_s.at[wide // 2 :, :], br_s.at[0 : wide // 2, :]
    weights = [
        Weights(src, dst, w_send.at[n], w_recv.at[n], w_own.at[n], row, z, core, n in (2, 5), stride, start)
        for n, (src, dst, stride, start) in enumerate(
            (
                (recur_s, br, hc, 0),
                (branch_s, br, hc, chan),
                (m_s, mt, 0, 0),
                (gu_s, gu, 0, 0),
                (d_s, down, 0, 0),
                (brn_s, br_n, 0, 0),
                (mn_s, m_n, 0, 0),
            )
        )
    ]
    mine = pl.ds(pl.multiple_of(core * seq, seq), seq)
    other = pl.ds(pl.multiple_of((1 - core) * seq, seq), seq)
    inner = pl.ds(pl.multiple_of(z * block + core * half, 16), half)
    outer = rows_of(core, half)
    swaps = [
        remote(x_in.at[:, other], x_own.at[outer, :], x_send.at[0], x_recv.at[0], sibling),
        remote(g_in.at[:, other], go.at[inner, :], x_send.at[1], x_recv.at[1], sibling),
        pltpu.make_async_copy(x_in.at[:, mine], x_own.at[outer, :], x_loc.at[0]),
        pltpu.make_async_copy(g_in.at[:, mine], go.at[inner, :], x_loc.at[1]),
    ]
    trades = []
    for n, (src, dst) in enumerate(
        ((vec, vec_all.at[core]), (retain, block_all.at[core, 0]), (admit, block_all.at[core, 1]))
    ):
        trades.append(remote(src, dst, x_send.at[2 + n], x_recv.at[2 + n], sibling))
        trades.append(pltpu.make_async_copy(src, dst, x_loc.at[2 + n]))
    for swap in swaps + trades:
        swap.start()
    for w in weights[:3]:
        w.start()
    for swap in swaps + trades:
        swap.wait()
    flushes = [
        pltpu.make_async_copy(x_own, x_out, v_sem.at[0]),
        pltpu.make_async_copy(go.at[rows_of(z, block), :], g_out, v_sem.at[1]),
    ]
    for flush in flushes:
        flush.start()
    gather = Gather(normed, g_send, g_recv, z, core, block)
    gather_go = Gather(go, e_send, e_recv, z, core, block)
    gather_two = Gather(normed2, f_send, f_recv, z, core, block)
    shares = lambda k, s: own.at[k, s]
    shares_o = lambda k, s: normed.at[rows_of(s, block), lanes(k)]
    spread = Spread(shares, held, s_send, s_recv, z, core)
    spread_n = Spread(shares, held_n, t_send, t_recv, z, core)
    spread_o = Spread(shares_o, held_o, o_send, o_recv, z, core)
    res = x_own
    gather_go.send(0, 0)
    for c in (0, 1):
        at = slice(c * hc, (c + 1) * hc)
        par[at, :] = vec_all[c].T
        gains[c * half : (c + 1) * half, :] = par[c * hc : c * hc + half, :]

    sums[z] = jnp.zeros(sums.shape[1:], F32)

    def squares(i):
        v = x_own[rows_of(i, 16), :].astype(F32)
        v = v * v
        sums[z] += v[:8] + v[8:]

    blocks(block // 16, squares)
    share_line(sums, l_send, l_recv, z, core)
    scale[...] = jnp.broadcast_to(scale_of(sums, eps, width), scale.shape)

    def norm(i):
        v = x_own[rows_of(i, 16), :].astype(F32) * scale[0:1, :] * gains[rows_of(i, 16), 8:9]
        normed[pl.ds(pl.multiple_of(z * block + i * 16, 16), 16), :] = v.astype(BF16)

    blocks(block // 16, norm)
    gather.send(0, 0)
    p_s[:, PART:] = jnp.zeros((chan, 128), F32)
    h_s[:, PART:] = jnp.zeros((chan, 128), F32)
    pads = [
        pltpu.make_async_copy(src.at[:, PART:], out.at[:, 0:128], v_sem.at[2 + n])
        for n, (src, out) in enumerate(((p_s, p_out), (h_s, h_out)))
    ]
    for pad in pads:
        pad.start()
    gates[...] = jnp.zeros(gates.shape, BF16)
    gates_hi[...] = jnp.zeros(gates_hi.shape, BF16)
    gates_lo[...] = jnp.zeros(gates_lo.shape, BF16)
    per = retain.shape[0]
    tap = retain.shape[1]
    for c in (0, 1):
        for n in (0, 1):
            for e in range(per):
                w = block_all[c, n, e]
                at, far = slice(e * tap, (e + 1) * tap), slice(n * hc + e * tap, n * hc + (e + 1) * tap)
                gates[c, at, far] = w.astype(BF16)
                w = w.T
                high = w.astype(BF16)
                gates_hi[c, far, at] = high
                gates_lo[c, far, at] = (w - high.astype(F32)).astype(BF16)
    masks[...] = jnp.zeros(masks.shape, F32)
    here = jnp.broadcast_to(segs[:, mine], (8, seq))
    spot = lax.broadcasted_iota(jnp.int32, (8, seq), 1)
    for lag in (1, 2, 3):
        same = jnp.where((pltpu.roll(here, lag, 1) == here) & (spot >= lag), 1.0, 0.0)
        masks[lag : lag + 1, 0:seq] = same[0:1]
        if lag == 1:
            masks[0:1, 0:seq] = 1.0 - same[0:1]
    gather.forward(1, 0)
    gather_go.forward(1, 0)
    gather.send(0, 1)
    weights[0].forward()
    gather.forward(2, 0)
    weights[1].forward()
    for w in weights[3:5]:
        w.start()
    gather_go.forward(2, 0)
    gather_go.send(0, 1)
    weights[0].finish()
    for pad in pads:
        pad.wait()

    kept = (b_s, p_s, u_s, r_s, i_s, h_s, q_c)
    outs = (b_out, p_out, u_out, r_out, i_out, h_out, q_out)

    def keep(n, part):
        if n in (1, 5):
            at = pl.ds(pl.multiple_of(128 + part * PART, 128), PART)
            return pltpu.make_async_copy(kept[n].at[:, 128:], outs[n].at[:, at], k_sem.at[n])
        return pltpu.make_async_copy(kept[n], outs[n].at[:, lanes(part)], k_sem.at[n])

    def put_shares(k, whole):
        for s in range(LINE):
            own[k, s] = whole[s * block : (s + 1) * block, :].astype(own.dtype)

    def work(k):
        here = lanes(k)

        @pl.when(k > 0)
        def _():
            for n in range(len(kept)):
                keep(n, k - 1).wait()

        p_s[:, 0:128] = p_s[:, PART:]
        h_s[:, 0:128] = h_s[:, PART:]
        n1 = normed[:, here]
        p_s[:, 128:] = dot(br[0:chan, :], n1)

        def conv(i):
            ch = rows_of(i, 64)
            window = p_s[ch, :]
            pr = par[ch, :]
            u = pr[:, 4:5] + pr[:, 0:1] * window[:, 128:]
            for lag in (1, 2, 3):
                u = u + pr[:, lag : lag + 1] * (pltpu.roll(window, lag, 1)[:, 128:] * masks[lag : lag + 1, here])
            u_s[ch, :] = u
            high = u.astype(BF16)
            uh[ch, :] = high
            ul[ch, :] = (u - high.astype(F32)).astype(BF16)

        blocks(chan // 64, conv)
        gather.middle(k)
        pl.when(k == 0)(lambda: gather_go.forward(1, 1))
        for g in range(chan // 256):
            at = slice(g * 256, (g + 1) * 256)
            pre = dot(gates_hi[g], uh[at, :]) + dot(gates_hi[g], ul[at, :]) + dot(gates_lo[g], uh[at, :])
            r_s[at, :] = pre[:256]
            i_s[at, :] = pre[256:]

        def decay(i):
            ch = rows_of(i, 64)
            pr = par[ch, :]
            start = masks[0:1, here] > 0.5
            r = jax.nn.sigmoid(r_s[ch, :] + pr[:, 5:6])
            gate = jax.nn.sigmoid(i_s[ch, :] + pr[:, 6:7])
            r_s[ch, :] = r
            i_s[ch, :] = gate
            a = jnp.exp(-(r * pr[:, 7:8]))
            m = jnp.where(start, 1.0, jnp.sqrt(1.0 - a * a + FLOOR))
            a_c[ch, :] = jnp.where(start, 0.0, a)
            h_s[ch, 128:] = m * gate * u_s[ch, :]

        blocks(chan // 64, decay)
        first = lax.broadcasted_iota(jnp.int32, (128, PART), 1) == 0

        def recur(i):
            ch = rows_of(i, 128)
            a, h = a_c[ch, :], h_s[ch, 128:]
            h = h + jnp.where(first, a * h_s[ch, 0:128][:, 127:128], 0.0)
            a = jnp.where(first, 0.0, a)
            shift = 1
            while shift < PART:
                h = h + a * pltpu.roll(h, shift, 1)
                if shift * 2 < PART:
                    a = a * pltpu.roll(a, shift, 1)
                shift *= 2
            h_s[ch, 128:] = h

        blocks(chan // 128, recur)
        gather.later(k)

        @pl.when(k == 0)
        def _():
            gather_go.forward(2, 1)
            weights[2].forward()
            weights[1].finish()

        b_s[...] = dot(br[chan : 2 * chan, :], normed[:, here])

        def mixed(i):
            ch = rows_of(i, 64)
            b = b_s[ch, :]
            t = jnp.tanh(GELU_A * (b + GELU_B * (b * b * b)))
            q_c[ch, :] = (b * (0.5 + 0.5 * t) * h_s[ch, 128:]).astype(BF16)

        blocks(chan // 64, mixed)
        pl.when(k == 0)(weights[2].finish)
        put_shares(k, dot(mt[...], q_c[...]))
        for n in range(len(kept)):
            keep(n, k).start()

    def finish(k, total):
        def add(i):
            at = pl.multiple_of(i * 64, 64)
            y[pl.ds(at, 64), lanes(k)] = x_own[pl.ds(at, 64), lanes(k)].astype(F32) + total(at, 64)

        blocks(block // 64, add)

    def step(t, carry):
        gather.arrive(2, t)
        work(t)
        spread.serve(t, finish)
        pl.when(t == PARTS - 1)(weights[3].forward)
        return carry

    lax.fori_loop(0, PARTS, step, 0)

    def square(k):
        sums2[k, z] = jnp.zeros(sums2.shape[2:], F32)

        def one(i):
            v = y[rows_of(i, 64), lanes(k)]
            sums2[k, z] += eight(v * v)

        blocks(block // 64, one)
        for d in (1, 2, 3):
            share(k, d).start()

    def share(k, d):
        return remote(
            sums2.at[k, z], sums2.at[k, z], n_send.at[k, d - 1], n_recv.at[k, d - 1], at_line(z ^ d, core)
        )

    def norm_two(k):
        for d in (1, 2, 3):
            piece = sums2.at[k, z ^ d]
            remote(piece, piece, n_send.at[k, d - 1], n_recv.at[k, d - 1], at_line(z ^ d, core)).wait_recv()
        s2 = scale_of(sums2.at[k], eps, width)
        scale_two[:, lanes(k)] = jnp.broadcast_to(s2, (8, PART))

        def one(i):
            at = rows_of(i, 64)
            v = y[at, lanes(k)] * scale_two[0:1, lanes(k)] * gains[at, 9:10]
            normed2[pl.ds(pl.multiple_of(z * block + i * 64, 64), 64), lanes(k)] = v.astype(BF16)

        blocks(block // 64, one)

    square(0)
    for w in weights[:3]:
        w.sent()
    for w in weights[5:]:
        w.start()
    for n in range(len(kept)):
        keep(n, PARTS - 1).wait()
    flush_n = pltpu.make_async_copy(normed, n1_out, v_sem.at[4])
    flush_n.start()
    gather_go.send(0, 2)
    spread.serve(PARTS, finish)
    norm_two(0)
    gather_two.send(0, 0)
    square(1)
    gather_go.forward(1, 2)
    weights[4].forward()
    spread.serve(PARTS + 1, finish)
    norm_two(1)
    gather_two.forward(1, 0)
    gather_two.send(0, 1)
    square(2)
    weights[4].finish()

    def turn_down(i):
        at = pl.ds(pl.multiple_of(i * 128, 128), 128)
        dt[:, at] = down[at, :].T

    blocks(hid // 128, turn_down)
    spread.serve(PARTS + 2, finish)
    gather.sent()
    for flush in flushes + [flush_n]:
        flush.wait()
    gather_two.forward(2, 0)
    gather_go.forward(2, 2)
    norm_two(2)
    square(3)
    weights[3].finish()

    def turn_up(i):
        at = pl.ds(pl.multiple_of(i * 128, 128), 128)
        gun[:, at] = gu[at, :].T

    blocks(2 * hid // 128, turn_up)
    norm_two(3)
    gather_go.send(0, 3)

    def keep_dev(k):
        return pltpu.make_async_copy(dev, dev_h.at[:, lanes(k)], v_sem.at[5])

    def keep_z(k):
        return pltpu.make_async_copy(zs, z_h.at[:, lanes(k)], v_sem.at[6])

    def feed(k):
        here = lanes(k)
        n2 = normed2[:, here]

        @pl.when(k > 0)
        def _():
            keep_dev(k - 1).wait()
            keep_z(k - 1).wait()

        ev[...] = dot(gu[...], n2)
        gather_two.middle(k)
        pl.when(k == 0)(lambda: gather_go.forward(1, 3))
        gather_go.arrive(2, k)
        dz[...] = dot(down[...], go[:, here])
        for c in range(2):

            def one(i):
                off = pl.multiple_of(i * 64, 64)
                e = ev[pl.ds(c * 2 * hh + off, 64), :]
                v = ev[pl.ds(c * 2 * hh + hh + off, 64), :]
                d = dz[pl.ds(c * hh + off, 64), :]
                act, slope = gelu_parts(e)
                zs[pl.ds(c * hh + off, 64), :] = (act * v).astype(BF16)
                dev[pl.ds(c * 2 * hh + off, 64), :] = (d * v * slope).astype(BF16)
                dev[pl.ds(c * 2 * hh + hh + off, 64), :] = (d * act).astype(BF16)

            blocks(hh // 64, one)
        gather_two.later(k)
        pl.when(k == 0)(lambda: gather_go.forward(2, 3))
        put_shares(k, dot(gun[...], dev[...]))
        spread_n.serve(k, finish_n)
        normed[:, here] = dot(dt[...], zs[...]).astype(BF16)
        spread_o.serve(k, finish_o)
        keep_dev(k).start()
        keep_z(k).start()

    def finish_o(k, total):
        def add(i):
            at = pl.multiple_of(i * 64, 64)
            res[pl.ds(at, 64), lanes(k)] = (y[pl.ds(at, 64), lanes(k)] + total(at, 64)).astype(BF16)

        blocks(block // 64, add)

    def keep_n(k):
        return pltpu.make_async_copy(dn2, dn2_out.at[:, lanes(k)], v_sem.at[3])

    def finish_n(k, total):
        @pl.when(k > 0)
        def _():
            keep_n(k - 1).wait()

        sums3[k, z] = jnp.zeros(sums3.shape[2:], F32)

        def add(i):
            at = pl.multiple_of(i * 64, 64)
            d = total(at, 64)
            dn2[pl.ds(at, 64), :] = d
            sums3[k, z] += eight(d * y[pl.ds(at, 64), lanes(k)] * gains[pl.ds(at, 64), 9:10])

        blocks(block // 64, add)
        keep_n(k).start()
        for d in (1, 2, 3):
            share_c(k, d).start()

    def share_c(k, d):
        return remote(
            sums3.at[k, z], sums3.at[k, z], c_send.at[k, d - 1], c_recv.at[k, d - 1], at_line(z ^ d, core)
        )

    def feed_step(t, carry):
        gather_two.arrive(2, t)
        feed(t)
        pl.when(t == 2)(weights[5].forward)
        pl.when(t == 3)(weights[6].forward)
        return carry

    lax.fori_loop(0, PARTS, feed_step, 0)
    for w in weights[3:5]:
        w.sent()
    keep_dev(PARTS - 1).wait()
    keep_z(PARTS - 1).wait()
    dev_all, z_all = gu.at[:, 0:seq], dt.at[0:hid, 0:seq]
    loads = [pltpu.make_async_copy(dev_h, dev_all, v_sem.at[5]), pltpu.make_async_copy(z_h, z_all, v_sem.at[6])]
    for load in loads:
        load.start()
    for load in loads:
        load.wait()

    def columns(start):
        return pl.ds(pl.multiple_of(start, 128), block)

    def place_up(j):
        side = jnp.where(j >= 3, core, 1 - core)
        return side * hid + (j % 3) * block, columns((j % 3) * block)

    def send_up(j):
        at, to = place_up(j)
        return remote(gun.at[:, columns(at)], g_got.at[:, to], d_send.at[j], d_recv.at[j], sibling)

    def keep_up(j):
        at, to = place_up(j)
        return pltpu.make_async_copy(gun.at[:, columns(at)], g_own.at[:, to], d_own.at[j - 3])

    def send_down():
        return remote(down.at[rows_of(1 - core, hh), :], gd_got, d_send.at[3], d_recv.at[3], sibling)

    def keep_down():
        return pltpu.make_async_copy(down.at[rows_of(core, hh), :], gd_own, d_own.at[3])

    def grad_up(j):
        at = place_up(j)[0]
        right = pl.ds(pl.multiple_of(at, 16), block)
        for low in (0, width // 2):
            piece = slice(low, low + width // 2)
            gun[piece, columns(at)] = dot_nt(normed2[piece, :], dev_all[right, :]).astype(BF16)

        @pl.when(j < 3)
        def _():
            send_up(j).start()

        @pl.when(j >= 3)
        def _():
            keep_up(j).start()

    def grad_down(side):
        at = rows_of(side, hh)
        down[at, :] = dot_nt(z_all[at, :], go[...]).astype(BF16)

    def drain(i, carry):
        t = PARTS + i
        blocks(2, lambda j: grad_up(2 * i + j))
        spread_n.serve(t, finish_n)
        spread_o.serve(t, finish_o)

        @pl.when(i < 2)
        def _():
            grad_down(jnp.where(i == 0, 1 - core, core))

        pl.when(i == 0)(lambda: send_down().start())
        pl.when(i == 1)(lambda: keep_down().start())
        return carry

    lax.fori_loop(0, LINE - 1, drain, 0)
    last = [
        remote(res.at[rows_of(1 - core, half), :], result.at[:, mine], x_send.at[0], x_recv.at[0], sibling),
        pltpu.make_async_copy(res.at[rows_of(core, half), :], result.at[:, mine], x_loc.at[0]),
        pltpu.make_async_copy(y, y_out, v_sem.at[2]),
        keep_n(PARTS - 1),
    ]
    for copy in last[:3]:
        copy.start()
    for w in weights[5:]:
        w.finish()
        w.sent()
    for one in (gather_go, gather_two, spread, spread_n, spread_o):
        one.sent()
    for k in range(PARTS):
        for d in (1, 2, 3):
            share(k, d).wait_send()
            share_c(k, d).wait_send()
            piece = sums3.at[k, z ^ d]
            remote(piece, piece, c_send.at[k, d - 1], c_recv.at[k, d - 1], at_line(z ^ d, core)).wait_recv()
        total = jnp.sum(jnp.sum(sums3[k], axis=0), axis=0, keepdims=True)
        at = slice(k * PART, (k + 1) * PART)
        s2 = scale_two[:, at]
        coef[:, at] = s2 * s2 * s2 * (total / width)
    for j in range(3):
        keep_up(j + 3).wait()
        send_up(j).wait()
    keep_down().wait()
    send_down().wait()
    for copy in last:
        copy.wait()


def back_kernel(
    width,
    y, dn2_h, g_h, x_own, scale_two, scale_one, coef_two, gains, masks, par, gates_t, m_h, br_h,
    b_h, p_h, u_h, r_h, i_h, h_h, q_h, n1_h, f_own, f_got, fd_own, fd_got,
    input_grad, tiny_v, tiny_g, f_sum, f_land, fd_sum, fd_land, g_sum, g_land, gm_sum, gm_land,
    sums, coef, m_n, br_n, b_s, p_s, u_s, r_s, i_s, h_s, dyf, dbp, dy, dn1, dq, du, dri, a_c, l_c, carry_s, own, held,
    qv, f_a, f_b, fd_a, fd_b, feed_part, mix_part, small, gate_grad, g_s, g_got, gm_got,
    vec, vec_in, vec_all, gd, gd_in, gd_all,
    c_sem, k_sem, l_send, l_recv, g_send, g_recv, s_send, s_recv, r_send, r_recv,
    f_sem, f_send, f_recv, d_send, d_recv, d_own, q_send, q_recv, n_send, n_recv, v_send, v_recv,
):
    row, z, core = place()
    block, seq = y.shape
    half = block // 2
    chan = b_s.shape[1]
    hc = chan // 2
    sibling = {"col": 2 * z + (1 - core)}
    greet(row, z, core, True, True)
    load_g = pltpu.make_async_copy(g_h, g_s, c_sem.at[0])
    load_g.start()
    dn2 = dn1
    load_d = pltpu.make_async_copy(dn2_h, dn2, c_sem.at[5])
    load_d.start()
    load_m = pltpu.make_async_copy(m_h, m_n, c_sem.at[1])
    load_m.start()
    load_b = pltpu.make_async_copy(br_h, br_n, c_sem.at[2])
    load_b.start()
    load_q = pltpu.make_async_copy(q_h, qv, c_sem.at[3])
    n1 = dyf
    load_n = pltpu.make_async_copy(n1_h, n1, c_sem.at[4])
    kept = (b_s, p_s, u_s, r_s, i_s, h_s)
    srcs = (b_h, p_h, u_h, r_h, i_h, h_h)

    def fetch(n, part):
        if kept[n] is p_s or kept[n] is h_s:
            at = pl.ds(pl.multiple_of(part * PART, 128), PART + 128)
        else:
            at = lanes(part)
        return pltpu.make_async_copy(srcs[n].at[:, at], kept[n].at[part % 2], k_sem.at[n, part % 2])

    def fetch_all(part):
        for n in range(len(kept)):
            fetch(n, part).start()

    fetch_all(PARTS - 1)
    load_q.start()
    du[:, 0:128] = jnp.zeros((chan, 128), F32)
    carry_s[...] = jnp.zeros(carry_s.shape, F32)
    small[...] = jnp.zeros(small.shape, F32)
    gate_grad[...] = jnp.zeros(gate_grad.shape, F32)

    load_d.wait()
    load_g.wait()
    gather = Gather(dyf, g_send, g_recv, z, core, block, back=True)

    def outer(part):
        here = slice(part * PART, (part + 1) * PART)

        def one(i):
            at = rows_of(i, 64)
            s2 = scale_two[0:1, here]
            d, v = dn2[at, here], y[at, here]
            w = d * v * s2
            w = w[:, 0:128] + w[:, 128:256]
            feed_part[at, :] = w if part == PARTS - 1 else feed_part[at, :] + w
            v = g_s[at, here].astype(F32) + (s2 * (gains[at, 9:10] * d) - v * coef_two[0:1, here])
            dy[at, here] = v
            dyf[pl.ds(pl.multiple_of(z * block + i * 64, 64), 64), here] = v.astype(BF16)

        blocks(block // 64, one)

    outer(PARTS - 1)
    gather.send(0, 0)
    outer(PARTS - 2)
    spread = Spread(lambda k, s: own.at[k, s], held, s_send, s_recv, z, core)
    gather.forward(1, 0)
    gather.send(0, 1)
    for part in range(PARTS - 2):
        outer(part)
    gather.forward(2, 0)
    load_m.wait()
    load_b.wait()
    final = lax.broadcasted_iota(jnp.int32, (128, PART), 1) == PART - 1

    f_arrays = ((f_own, f_got, f_a, f_b, f_sum, f_land), (fd_own, fd_got, fd_a, fd_b, fd_sum, fd_land))

    def f_loads(d):
        pulls = []
        for n, (ours, theirs, a, b, _, _) in enumerate(f_arrays):
            if n == 0:
                piece = (rows_of(row ^ d, block), slice(None))
            else:
                piece = (slice(None), pl.ds(pl.multiple_of((row ^ d) * block, 128), block))
            pulls.append(pltpu.make_async_copy(ours.at[piece], a.at[d], f_sem.at[n, 0]))
            pulls.append(pltpu.make_async_copy(theirs.at[piece], b, f_sem.at[n, 1]))
        return pulls

    def f_out(d):
        outs = []
        for n, (_, _, a, _, kept_at, land) in enumerate(f_arrays):
            if d == 0:
                outs.append(pltpu.make_async_copy(a.at[0], kept_at, f_send.at[n, 0]))
            else:
                outs.append(
                    remote(a.at[d], land.at[d - 1], f_send.at[n, d], f_recv.at[n, d], {"row": row ^ d})
                )
        return outs

    def f_part(d):
        for pull in f_loads(d):
            pull.wait()
        for _, _, a, b, _, _ in f_arrays:

            def add(i):
                at = rows_of(i, 64)
                a[d, at, :] = (a[d, at, :].astype(F32) + b[at, :].astype(F32)).astype(BF16)

            blocks(b.shape[0] // 64, add)
        for out in f_out(d):
            out.start()
        if d > 0:
            for pull in f_loads(d - 1):
                pull.start()

    def f_step(t):
        for d in range(PARTS):
            pl.when(t == PARTS - 1 - d)(functools.partial(f_part, d))

    for pull in f_loads(PARTS - 1):
        pull.start()

    def fold2(v):
        return v[:, 0:128] + v[:, 128:256]

    def work(t):
        k = PARTS - 1 - t
        here = lanes(k)
        wide = pl.ds(pl.multiple_of(k * PART, 128), PART + 128)
        slot = k % 2
        for n in range(len(kept)):
            fetch(n, k).wait()

        @pl.when(k > 0)
        def _():
            fetch_all(k - 1)

        dq[...] = dot(m_n[...], dyf[:, here])

        def before(i):
            ch = rows_of(i, 64)
            c = i // (hc // 64)
            low = pl.ds(pl.multiple_of(c * hc + i * 64, 64), 64)
            pr = par[ch, :]
            d = dq[ch, :]
            act, slope = gelu_parts(b_s[slot, ch, :])
            dbp[low, here] = (d * h_s[slot, ch, :][:, 128:] * slope).astype(BF16)
            l_c[ch, :] = d * act
            a_c[ch, :] = jnp.exp(-(r_s[slot, ch, :] * pr[:, 7:8]))

        blocks(chan // 64, before)
        gather.middle(t)

        def recur(i):
            ch = rows_of(i, 128)
            start = masks[0:1, here] > 0.5
            a, lam = jnp.where(start, 0.0, a_c[ch, :]), l_c[ch, :]
            lam = lam + jnp.where(final, carry_s[ch, :][:, 0:1], 0.0)
            w = jnp.where(final, 0.0, pltpu.roll(a, PART - 1, 1))
            shift = 1
            while shift < PART:
                lam = lam + w * pltpu.roll(lam, PART - shift, 1)
                if shift * 2 < PART:
                    w = w * pltpu.roll(w, PART - shift, 1)
                shift *= 2
            carry_s[ch, :] = jnp.broadcast_to((a * lam)[:, 0:1], (128, 128))
            l_c[ch, :] = lam

        blocks(chan // 128, recur)
        f_step(t)
        gather.later(t)

        def after(i):
            ch = rows_of(i, 64)
            du[ch, PART:] = du[ch, 0:128]
            pr = par[ch, :]
            start = masks[0:1, here] > 0.5
            lam, a0 = l_c[ch, :], a_c[ch, :]
            earlier = pltpu.roll(h_s[slot, ch, :], 1, 1)[:, 128:]
            r, gate, u = r_s[slot, ch, :], i_s[slot, ch, :], u_s[slot, ch, :]
            m0 = jnp.sqrt(1.0 - a0 * a0 + FLOOR)
            m = jnp.where(start, 1.0, m0)
            lm = lam * m
            lu = lam * u
            du[ch, 0:PART] = lm * gate
            da = jnp.where(start, 0.0, lam * earlier - (lu * gate) * (a0 / m0)) * a0
            dr = da * (-pr[:, 7:8]) * (r * (1.0 - r))
            di = lu * m * (gate * (1.0 - gate))
            g, o = i // 4, (i % 4) * 64
            dri[pl.ds(pl.multiple_of(g * 512 + o, 64), 64), :] = dr.astype(BF16)
            dri[pl.ds(pl.multiple_of(g * 512 + 256 + o, 64), 64), :] = di.astype(BF16)
            small[5, ch, :] += fold2(dr)
            small[6, ch, :] += fold2(di)
            small[7, ch, :] += fold2(da * r)

        blocks(chan // 64, after)
        for g in range(chan // 256):
            at = slice(g * 256, (g + 1) * 256)
            dd = dri[g * 512 : (g + 1) * 512, :]
            du[at, 0:PART] += dot(gates_t[g], dd)
            gate_grad[g] += dot_nt(u_s[slot, at, :].astype(BF16), dd)

        def conv(i):
            ch = rows_of(i, 64)
            c = i // (hc // 64)
            low = pl.ds(pl.multiple_of((c + 1) * hc + i * 64, 64), 64)
            pr = par[ch, :]
            follow = du[ch, :]
            window = p_s[slot, ch, :]
            d = follow[:, :PART]
            dp = pr[:, 0:1] * d
            small[4, ch, :] += fold2(d)
            small[0, ch, :] += fold2(d * window[:, 128:])
            for lag in (1, 2, 3):
                kd = follow * masks[lag : lag + 1, wide]
                dp = dp + pr[:, lag : lag + 1] * pltpu.roll(kd, PART + 128 - lag, 1)[:, :PART]
                small[lag, ch, :] += fold2(kd[:, :PART] * pltpu.roll(window, lag, 1)[:, 128:])
            dbp[low, here] = dp.astype(BF16)

        blocks(chan // 64, conv)
        whole = dot(br_n[...], dbp[:, here])
        for s in range(LINE):
            own[t, s] = whole[s * block : (s + 1) * block, :].astype(own.dtype)

    def finish(t, total):
        k = PARTS - 1 - t

        sums[k, z] = jnp.zeros(sums.shape[2:], F32)

        @pl.when(t == 0)
        def _():
            mix_part[...] = jnp.zeros(mix_part.shape, F32)

        def add(i):
            at = pl.ds(pl.multiple_of(i * 64, 64), 64)
            d = total(pl.multiple_of(i * 64, 64), 64)
            dn1[at, lanes(k)] = d
            w = d * x_own[at, lanes(k)].astype(F32)
            sums[k, z] += eight(w * gains[at, 8:9])
            w = w * scale_one[0:1, lanes(k)]
            mix_part[at, :] += w[:, 0:128] + w[:, 128:256]

        blocks(block // 64, add)
        for d in (1, 2, 3):
            share(k, d).start()

    def share(k, d):
        return remote(sums.at[k, z], sums.at[k, z], l_send.at[k, d - 1], l_recv.at[k, d - 1], at_line(z ^ d, core))

    def step(t, carry):
        gather.arrive(2, t)
        work(t)
        spread.serve(t, finish)
        return carry

    lax.fori_loop(0, PARTS, step, 0)
    load_q.wait()

    lru = hc

    def cols_of(side):
        return pl.ds(pl.multiple_of(side * 2 * lru, 128), 2 * lru)

    def send_br():
        return remote(br_n.at[:, cols_of(1 - core)], g_got, d_send.at[0], d_recv.at[0], sibling)

    def send_m():
        return remote(m_n.at[rows_of(1 - core, lru), :], gm_got, d_send.at[1], d_recv.at[1], sibling)

    def grad_br(side):
        br_n[:, cols_of(side)] = dot_nt(n1[...], dbp[rows_of(side, 2 * lru), :]).astype(BF16)

    def out_br(d):
        piece = br_n.at[rows_of(row ^ d, block), cols_of(core)]
        if d == 0:
            return pltpu.make_async_copy(piece, g_sum, d_own.at[0])
        return remote(piece, g_land.at[d - 1], q_send.at[0, d - 1], q_recv.at[0, d - 1], {"row": row ^ d})

    def out_m(d):
        piece = m_n.at[rows_of(core, lru), pl.ds(pl.multiple_of((row ^ d) * block, 128), block)]
        if d == 0:
            return pltpu.make_async_copy(piece, gm_sum, d_own.at[1])
        return remote(piece, gm_land.at[d - 1], q_send.at[1, d - 1], q_recv.at[1, d - 1], {"row": row ^ d})

    def drain(i, carry):
        t = PARTS + i

        @pl.when(i == 0)
        def _():
            m_n[...] = dot_nt(qv[...], dyf[...]).astype(BF16)
            send_m().start()
            gather.sent()
            load_n.start()
            load_n.wait()
            grad_br(1 - core)
            send_br().start()

        @pl.when(i == 1)
        def _():
            grad_br(core)
            send_m().wait_recv()

            def add(j):
                at = rows_of(j, 32)
                to = pl.ds(pl.multiple_of(core * lru + j * 32, 32), 32)
                m_n[to, :] = (m_n[to, :].astype(F32) + gm_got[at, :].astype(F32)).astype(BF16)

            blocks(lru // 32, add)
            for d in (3, 2, 1, 0):
                out_m(d).start()

        @pl.when(i == 2)
        def _():
            send_br().wait_recv()

            def add(j):
                at = rows_of(j, 32)
                br_n[at, cols_of(core)] = (br_n[at, cols_of(core)].astype(F32) + g_got[at, :].astype(F32)).astype(BF16)

            blocks(width // 32, add)
            for d in (3, 2, 1, 0):
                out_br(d).start()

        spread.serve(t, finish)
        return carry

    lax.fori_loop(0, LINE - 1, drain, 0)
    mine = pl.ds(pl.multiple_of(core * seq, seq), seq)
    for side in (0, 1):
        for e in range(4):
            at = slice(e * 64, (e + 1) * 64)
            gd[side, at, 0:64] = gate_grad[side, at, e * 64 : (e + 1) * 64]
            gd[side, at, 64:128] = gate_grad[side, at, 256 + e * 64 : 256 + (e + 1) * 64]
    swap_gd = remote(gd.at[1 - core], gd_in, v_send.at[0], v_recv.at[0], sibling)
    swap_gd.start()
    lane = lax.broadcasted_iota(jnp.int32, (64, 128), 1)

    def columns(parts, at):
        total = jnp.zeros((64, 128), F32)
        for n, part in enumerate(parts):
            total = total + jnp.where(lane == n, jnp.sum(part(at), axis=1, keepdims=True), 0.0)
        return total

    vec[...] = jnp.zeros(vec.shape, F32)
    for j in range(chan // 64):
        at = slice(j * 64, (j + 1) * 64)
        v = columns([lambda at, n=n: small[n, at, :] for n in range(8)], at)
        vec[0, :, at] = v.T[0:8, :]

    for k in range(PARTS):
        for d in (1, 2, 3):
            share(k, d).wait_send()
            piece = sums.at[k, z ^ d]
            remote(piece, piece, l_send.at[k, d - 1], l_recv.at[k, d - 1], at_line(z ^ d, core)).wait_recv()
        total = jnp.sum(jnp.sum(sums[k], axis=0), axis=0, keepdims=True)
        at = slice(k * PART, (k + 1) * PART)
        s1 = scale_one[:, at]
        coef[:, at] = s1 * s1 * s1 * (total / width)

    def last(i):
        at = rows_of(i, 16)
        v = dy[at, :] + (
            scale_one[0:1, :] * (gains[at, 8:9] * dn1[at, :]) - x_own[at, :].astype(F32) * coef[0:1, :]
        )
        dy[at, :] = v

    blocks(block // 16, last)
    back = remote(dy.at[rows_of(1 - core, half), :], input_grad.at[:, mine], r_send, r_recv, sibling)
    back.start()
    keep_in = pltpu.make_async_copy(dy.at[rows_of(core, half), :], input_grad.at[:, mine], d_own.at[3])
    keep_in.start()
    for j in range(block // 64):
        at = slice(j * 64, (j + 1) * 64)
        v = columns([lambda at: mix_part[at, :], lambda at: feed_part[at, :]], at)
        vec[1, :, at] = v.T[0:8, :]
    swap_vec = remote(vec, vec_in, v_send.at[1], v_recv.at[1], sibling)
    swap_vec.start()
    swap_gd.wait()
    gd_all[0] = gd[core] + gd_in[...]
    rows_gd = [
        remote(gd_all.at[0], gd_all.at[d], n_send.at[0, d - 1], n_recv.at[0, d - 1], {"row": row ^ d}) for d in (1, 2, 3)
    ]
    for copy in rows_gd:
        copy.start()
    swap_vec.wait()
    vec_all[0] = vec[...] + vec_in[...]
    rows_vec = [
        remote(vec_all.at[0], vec_all.at[d], n_send.at[1, d - 1], n_recv.at[1, d - 1], {"row": row ^ d}) for d in (1, 2, 3)
    ]
    for copy in rows_vec:
        copy.start()
    spread.sent()
    for copy in rows_gd + rows_vec:
        copy.wait()
    for every, out in ((gd_all, tiny_g), (vec_all, tiny_v)):
        first, second = every[row % 2], every[1 - row % 2]
        third, fourth = every[2 + row % 2], every[3 - row % 2]
        out[...] = (first + second) + (third + fourth)
    for d in range(PARTS):
        for out in f_out(d):
            out.wait()
    send_br().wait_send()
    send_m().wait_send()
    for d in (0, 1, 2, 3):
        out_br(d).wait()
        out_m(d).wait()
    for copy in (keep_in, back):
        copy.wait()


def last_kernel(
    f_sum, f_land, fd_sum, fd_land, g_sum, g_land, gm_sum, gm_land, tiny_v, tiny_g, lambdas,
    s_b, s_r, s_m, s_g, s_u, s_d, taps, offs, bias_r, bias_a, decay, mix, feed, retain, admit,
):
    core = place()[2]
    lru, block = s_m.shape
    ff, half = s_d.shape[0], mix.shape[1]

    def four(first, others, at):
        return first[at, :].astype(F32) + others[0, at, :].astype(F32) + (
            others[1, at, :].astype(F32) + others[2, at, :].astype(F32)
        )

    def put_gu(i):
        at = rows_of(i, 32)
        v = four(f_sum, f_land, at)
        s_g[at, :] = v[:, :ff]
        s_u[at, :] = v[:, ff:]
        v = four(g_sum, g_land, at)
        s_b[at, :] = v[:, :lru]
        s_r[at, :] = v[:, lru:]

    blocks(block // 32, put_gu)

    def put_d(i):
        at = rows_of(i, 32)
        s_d[at, :] = four(fd_sum, fd_land, at)

    blocks(ff // 32, put_d)

    def put_m(i):
        at = rows_of(i, 32)
        s_m[at, :] = four(gm_sum, gm_land, at)

    blocks(lru // 32, put_m)
    small = tiny_v[0, :, pl.ds(pl.multiple_of(core * lru, 128), lru)]
    taps[...] = small[0:4]
    offs[...] = small[4:5]
    bias_r[...] = small[5:6]
    bias_a[...] = small[6:7]
    decay[...] = small[7:8] * (8.0 * jax.nn.sigmoid(-lambdas[...]))
    gains = jnp.where(core == 0, tiny_v[1, :, 0:half], tiny_v[1, :, half : 2 * half])
    mix[...] = gains[0:1]
    feed[...] = gains[1:2]
    for e in range(retain.shape[0]):
        at = slice(e * 64, (e + 1) * 64)
        retain[e] = tiny_g[at, 0:64]
        admit[e] = tiny_g[at, 64:128]


ANY = pl.BlockSpec(memory_space=pl.ANY)
VM = pl.BlockSpec(memory_space=pltpu.VMEM)
DMA = pltpu.SemaphoreType.DMA
ROOM = 62 * 1024 * 1024


def shape(dims, kind):
    return jax.ShapeDtypeStruct(dims, kind)


def call(kernel, ins, outs, scratch, ident, name, flops):
    return pl.pallas_call(
        kernel,
        out_shape=[o[0] for o in outs],
        in_specs=ins,
        out_specs=[o[1] for o in outs],
        scratch_shapes=scratch,
        name=name,
        compiler_params=pltpu.CompilerParams(
            collective_id=ident, has_side_effects=True, vmem_limit_bytes=ROOM
        ),
        cost_estimate=pl.CostEstimate(flops=flops, bytes_accessed=40000000, transcendentals=0),
    )


def fast_body(
    inputs, segments, mix_gain, branch_weight, recur_weight, kernel, offsets, retain_weight, retain_bias,
    admit_weight, admit_bias, lambdas, merge_weight, feed_gain, gate_weight, up_weight, down_weight, cotangent,
):
    half, tokens = inputs.shape
    block, seq, width = 2 * half, tokens // 2, D
    lru, heads = branch_weight.shape[1], retain_weight.shape[0]
    chan = 2 * lru
    ff = gate_weight.shape[1]
    hid = 2 * ff
    rows = branch_weight.shape[0]
    cols = merge_weight.shape[1]
    rate = 8.0 * jax.nn.softplus(-lambdas)
    vec = [kernel] + [v[None, :] for v in (offsets, retain_bias, admit_bias, rate)]
    vec += [jnp.pad(v[None, :], ((0, 0), (0, lru - half))) for v in (mix_gain, feed_gain)]
    vec = jnp.concatenate(vec + [jnp.zeros((6, lru), F32)])
    br_s = jnp.concatenate([branch_weight, recur_weight], axis=1).T
    m_s = merge_weight.T
    gu_s = jnp.concatenate([gate_weight, up_weight], axis=1).T

    f_tok = lambda n, kind=F32: shape((n, seq), kind)
    padded = (shape((chan, 128 + seq), F32), ANY)
    state = [(f_tok(chan), ANY), padded, *[(f_tok(chan), ANY)] * 3, padded]
    line = [DMA((3,)), DMA((3,))]
    steps = [DMA((2, 3, PARTS)), DMA((2, 3, PARTS))]
    sums = [DMA((2, PARTS, LINE)), DMA((2, PARTS, LINE))]
    held = pltpu.VMEM((PARTS, LINE + 1, block, PART), BF16)
    own_low = pltpu.VMEM((PARTS, LINE, block, PART), BF16)
    tok = lambda n, kind=F32, lead=0: pltpu.VMEM((n, lead + seq), kind)
    one = lambda n, kind=F32, lead=0: pltpu.VMEM((n, lead + PART), kind)
    br_t = jnp.concatenate([branch_weight, recur_weight], axis=1)
    grad_gu, grad_d = (shape((width, 2 * ff), BF16), ANY), (shape((ff, width), BF16), ANY)
    low = lambda n, m: (shape((n, m), BF16), ANY)

    (masks, par, gains, gates, coef, scale_one, scale_two, y, n1, q, x_own, g, b, p, u, r, i, h, result, dn2, _, _, f_own, f_got, fd_own, fd_got,
     br_n, m_n) = call(
        functools.partial(forward_kernel, width, EPS),
        [ANY] * 2 + [VM] * 4 + [ANY] * 6,
        [(shape((8, seq + 128), F32), VM), (shape((chan, 16), F32), VM), (shape((block, 16), F32), VM), (shape((2, lru, 2 * lru), BF16), VM),
         (f_tok(8), VM), (f_tok(8), VM), (f_tok(8), VM), (f_tok(block), ANY), low(width, seq), low(chan, seq), low(block, seq), low(block, seq)]
        + state + [low(half, tokens), (f_tok(block), ANY), low(2 * hid, seq), low(hid, seq), grad_gu, grad_gu, grad_d, grad_d,
                   low(width, 2 * chan), low(chan, width)],
        [pltpu.VMEM((LINE, 8, seq), F32), pltpu.VMEM((PARTS, LINE, 8, PART), F32), pltpu.VMEM((PARTS, LINE, 8, PART), F32),
         pltpu.VMEM((2, 16, lru), F32), pltpu.VMEM((2, 2) + retain_weight.shape, F32), pltpu.VMEM((2, 2 * lru, lru), BF16),
         pltpu.VMEM((2, 2 * lru, lru), BF16), tok(width, BF16), tok(width, BF16),
         tok(width, BF16), tok(block, BF16), tok(block), one(block), one(chan, BF16),
         one(chan, F32, 128), one(chan, F32, 128), one(max(5 * chan, 3 * hid)), one(chan, BF16), one(chan, BF16),
         own_low, held, held, held, pltpu.VMEM((2 * hid, width), BF16), pltpu.VMEM((width, 2 * hid), BF16),
         pltpu.VMEM((hid, width), BF16), pltpu.VMEM((width, hid), BF16), one(hid, BF16), one(2 * hid, BF16),
         DMA((5,)), DMA((5,)), DMA((5,))] + line + [DMA((PARTS, 3)), DMA((PARTS, 3))] * 2 + steps * 3 + sums * 3
        + [DMA((7, 7)), DMA((7, 7)), DMA((7,)), DMA((7,)), DMA((7,)), DMA((4,)), DMA((4,)), DMA((4,))],
        0, "forward", 50 * 10**9,
    )(inputs, cotangent, segments[None, :], vec, retain_weight, admit_weight, br_s, m_s, gu_s, down_weight,
      br_t, merge_weight)

    pair = lambda lead=0: pltpu.VMEM((2, chan, lead + PART), F32)
    land = lambda n, m: ((shape((n, m), BF16), ANY), (shape((3, n, m), BF16), ANY))
    input_grad, tiny_v, tiny_g, *sums_of = call(
        functools.partial(back_kernel, width),
        [VM] + [ANY] * 2 + [VM] * 8 + [ANY] * 14,
        [(shape((half, tokens), F32), ANY), (shape((2, 8, chan), F32), VM),
         (shape((lru, 128), F32), VM), *land(cols, 2 * ff), *land(ff, cols), *land(cols, 2 * lru), *land(lru, cols)],
        [pltpu.VMEM((PARTS, LINE, 8, PART), F32), pltpu.VMEM((8, seq), F32),
         pltpu.VMEM((chan, width), BF16), pltpu.VMEM((width, 2 * chan), BF16),
         pair(), pair(128), pair(), pair(), pair(), pair(128), tok(width, BF16), tok(2 * chan, BF16),
         tok(block), tok(block), pltpu.VMEM((chan, PART), F32), pltpu.VMEM((chan, PART + 128), F32), pltpu.VMEM((2 * chan, PART), BF16),
         pltpu.VMEM((chan, PART), F32), pltpu.VMEM((chan, PART), F32), pltpu.VMEM((chan, 128), F32), own_low, held,
         tok(chan, BF16), pltpu.VMEM((4, cols, 2 * ff), BF16), pltpu.VMEM((cols, 2 * ff), BF16),
         pltpu.VMEM((4, ff, cols), BF16), pltpu.VMEM((ff, cols), BF16),
         pltpu.VMEM((block, 128), F32), pltpu.VMEM((block, 128), F32), pltpu.VMEM((8, chan, 128), F32),
         pltpu.VMEM((2, lru, 2 * lru), F32), tok(block, BF16), pltpu.VMEM((width, 2 * lru), BF16),
         pltpu.VMEM((lru, width), BF16), pltpu.VMEM((2, 8, chan), F32), pltpu.VMEM((2, 8, chan), F32),
         pltpu.VMEM((4, 2, 8, chan), F32), pltpu.VMEM((2, lru, 128), F32), pltpu.VMEM((lru, 128), F32),
         pltpu.VMEM((4, lru, 128), F32), DMA((7,)), DMA((6, 2))] + [DMA((PARTS, 3)), DMA((PARTS, 3))] + steps + sums
        + [DMA, DMA, DMA((2, 2)), DMA((2, PARTS)), DMA((2, PARTS)), DMA((2,)), DMA((2,)), DMA((4,))]
        + [DMA((2, 3)), DMA((2, 3)), DMA((2, 3)), DMA((2, 3)), DMA((2,)), DMA((2,))],
        2, "mix_backward", 10 * 10**9,
    )(y, dn2, g, x_own, scale_two, scale_one, coef, gains, masks, par, gates, m_n, br_n, b, p, u, r, i, h,
      q, n1, f_own, f_got, fd_own, fd_got)

    line_of = shape((1, lru), F32)
    s_b, s_r, s_m, s_g, s_u, s_d, taps, offs, bias_r, bias_a, decay, mix, feed, retain, admit = pl.pallas_call(
        last_kernel,
        out_shape=[shape((cols, lru), F32)] * 2 + [shape((lru, cols), F32)] + [shape((cols, ff), F32)] * 2
        + [shape((ff, cols), F32), shape((4, lru), F32)] + [line_of] * 4 + [shape((1, half), F32)] * 2
        + [shape((heads, 64, 64), F32)] * 2,
        in_specs=[VM] * 11,
        out_specs=[VM] * 15,
        name="last_sums",
        compiler_params=pltpu.CompilerParams(vmem_limit_bytes=ROOM),
    )(*sums_of, tiny_v, tiny_g, lambdas[None, :])
    return (
        result,
        input_grad,
        mix[0],
        s_b,
        s_r,
        taps,
        offs[0],
        retain,
        bias_r[0],
        admit,
        bias_a[0],
        decay[0],
        s_m,
        feed[0],
        s_g,
        s_u,
        s_d,
    )


def suits(mesh, args):
    return (
        dict(mesh.shape) == {"row": 4, "col": 8}
        and args[0].shape == (D, 8 * SEQ)
        and args[3].shape == (D, 2048)
        and args[14].shape == (D, 4608)
        and args[7].shape == (32, 64, 64)
    )


def solution(mesh):
    in_specs = (
        P("col", "row"),
        P("row"),
        P("col"),
        P("row", "col"),
        P("row", "col"),
        P(None, "col"),
        P("col"),
        P("col", None, None),
        P("col"),
        P("col", None, None),
        P("col"),
        P("col"),
        P("col", "row"),
        P("col"),
        P("row", "col"),
        P("row", "col"),
        P("col", "row"),
        P("col", "row"),
    )
    out_specs = (
        P("col", "row"),
        P("col", "row"),
        P("col"),
        P("row", "col"),
        P("row", "col"),
        P(None, "col"),
        P("col"),
        P("col", None, None),
        P("col"),
        P("col", None, None),
        P("col"),
        P("col"),
        P("col", "row"),
        P("col"),
        P("row", "col"),
        P("row", "col"),
        P("col", "row"),
    )
    def run(*args):
        chosen = fast_body if suits(mesh, args) else body
        return jax.shard_map(
            chosen, mesh=mesh, in_specs=in_specs, out_specs=out_specs, check_vma=False
        )(*args)

    return run
```

```python
import functools

import jax
import jax.numpy as jnp
from jax import lax
from jax.experimental import pallas as pl
from jax.experimental.pallas import tpu as pltpu
from jax.sharding import PartitionSpec as P

D = 1536
SEQ = 1024
MICRO = 2


HIGH = lax.Precision.HIGHEST
EPS = 1e-06
POWER = 8.0
FLOOR = 0.01


def combine(earlier, later):
    first_a, first_b = earlier
    second_a, second_b = later
    return (first_a * second_a, second_a * first_b + second_b)


def mixer(
    branch_pre,
    lru_pre,
    segs,
    kernel,
    offsets,
    retain_weight,
    retain_bias,
    admit_weight,
    admit_bias,
    lambdas,
):
    length = lru_pre.shape[0]
    channels = lru_pre.shape[1]
    conv = offsets + kernel[0] * lru_pre
    for lag in range(1, kernel.shape[0]):
        shifted = jnp.concatenate(
            [jnp.zeros((lag, channels), lru_pre.dtype), lru_pre[:-lag]], axis=0
        )
        prior = jnp.concatenate([jnp.full((lag,), -1, jnp.int32), segs[:-lag]])
        keep = (prior == segs).astype(lru_pre.dtype)
        conv = conv + kernel[lag] * shifted * keep[:, None]
    heads = retain_weight.shape[0]
    blocks = conv.reshape(length, heads, channels // heads)
    retain = jax.nn.sigmoid(
        jnp.einsum("thi,hij->thj", blocks, retain_weight, precision=HIGH).reshape(length, channels)
        + retain_bias
    )
    admit = jax.nn.sigmoid(
        jnp.einsum("thi,hij->thj", blocks, admit_weight, precision=HIGH).reshape(length, channels)
        + admit_bias
    )
    decay = jnp.exp(-POWER * retain * jax.nn.softplus(-lambdas))
    factor = jnp.sqrt(1.0 - decay * decay + FLOOR)
    starts = jnp.concatenate([jnp.ones((1,), bool), segs[1:] != segs[:-1]])
    decay = jnp.where(starts[:, None], 0.0, decay)
    factor = jnp.where(starts[:, None], 1.0, factor)
    _, state = lax.associative_scan(combine, (decay, factor * admit * conv), axis=0)
    return jax.nn.gelu(branch_pre) * state


def geglu(gate, upper):
    return jax.nn.gelu(gate) * upper


def contract_rows(left, right):
    return lax.dot_general(
        left, right, (((0,), (0,)), ((), ())), preferred_element_type=jnp.float32
    )


def contract_cols(left, right):
    return lax.dot_general(
        left, right, (((1,), (1,)), ((), ())), preferred_element_type=jnp.float32
    )


def contract_cross(left, right):
    return lax.dot_general(
        left, right, (((0,), (1,)), ((), ())), preferred_element_type=jnp.float32
    )


def norm_forward(resid, gain):
    total = lax.psum(jnp.sum(resid * resid, axis=0), "col")
    scale = lax.rsqrt(total / D + EPS)[None, :]
    return (scale, (resid * scale * gain[:, None]).astype(jnp.bfloat16))


def norm_backward(resid, scale, gain, grad_normed):
    weighted = grad_normed * gain[:, None]
    total = lax.psum(jnp.sum(weighted * resid, axis=0), "col")
    grad_resid = scale * weighted - resid * (scale * scale * scale) * (total / D)[None, :]
    grad_gain = jnp.sum(grad_normed * resid * scale, axis=1)
    return (grad_resid, grad_gain)


def gather_features(normed):
    return lax.all_gather(normed, "col", axis=0, tiled=True)


def gather_cotangent(grad):
    return lax.all_gather(grad, "col", axis=0, tiled=True)


def spread_sum(term):
    return lax.psum_scatter(
        term.astype(jnp.bfloat16), "col", scatter_dimension=0, tiled=True
    ).astype(jnp.float32)


def back_sum(term):
    return spread_sum(term)


def merge_term(whole_merge, mixed_low):
    return spread_sum(contract_cross(whole_merge, mixed_low))


def weight_grads(normed, grad_joined):
    return jnp.dot(
        normed,
        grad_joined,
        preferred_element_type=jnp.float32,
    )


def row_sum(total, axis):
    return lax.psum_scatter(
        total.astype(jnp.bfloat16), "row", scatter_dimension=axis, tiled=True
    ).astype(jnp.float32)


def body(
    inputs,
    segments,
    mix_gain,
    branch_weight,
    recur_weight,
    kernel,
    offsets,
    retain_weight,
    retain_bias,
    admit_weight,
    admit_bias,
    lambdas,
    merge_weight,
    feed_gain,
    gate_weight,
    up_weight,
    down_weight,
    cotangent,
):
    lru_cols = branch_weight.shape[1]
    feed_cols = gate_weight.shape[1]
    mixer_params = (kernel, offsets, retain_weight, retain_bias, admit_weight, admit_bias, lambdas)
    acc_branch = jnp.zeros((D, lru_cols), jnp.float32)
    acc_recur = jnp.zeros((D, lru_cols), jnp.float32)
    acc_gate = jnp.zeros((D, feed_cols), jnp.float32)
    acc_up = jnp.zeros((D, feed_cols), jnp.float32)
    acc_merge = jnp.zeros((lru_cols, D), jnp.float32)
    acc_down = jnp.zeros((feed_cols, D), jnp.float32)
    acc_small = tuple((jnp.zeros_like(p) for p in mixer_params))
    acc_mix = jnp.zeros_like(mix_gain)
    acc_feed = jnp.zeros_like(feed_gain)
    outputs = []
    in_grads = []
    for batch in range(MICRO):
        lower = batch * SEQ
        resid_in = inputs[:, lower : lower + SEQ].astype(jnp.float32)
        grad_out = cotangent[:, lower : lower + SEQ].astype(jnp.float32)
        segs = segments[lower : lower + SEQ]
        whole_branch, whole_recur, whole_gate, whole_up = (
            lax.all_gather(branch_weight, "row", axis=0, tiled=True),
            lax.all_gather(recur_weight, "row", axis=0, tiled=True),
            lax.all_gather(gate_weight, "row", axis=0, tiled=True),
            lax.all_gather(up_weight, "row", axis=0, tiled=True),
        )
        whole_merge, whole_down = (
            lax.all_gather(merge_weight, "row", axis=1, tiled=True),
            lax.all_gather(down_weight, "row", axis=1, tiled=True),
        )
        scale_one, normed_one = norm_forward(resid_in, mix_gain)
        full_one = gather_features(normed_one)
        branch_pre = contract_rows(full_one, whole_branch)
        lru_pre = contract_rows(full_one, whole_recur)

        def local_mixer(bpre, lpre, kern, offs, rweight, rbias, aweight, abias, lams):
            return mixer(bpre, lpre, segs, kern, offs, rweight, rbias, aweight, abias, lams)

        mixed, mixer_pull = jax.vjp(local_mixer, branch_pre, lru_pre, *mixer_params)
        mixed_low = mixed.astype(jnp.bfloat16)
        resid_mid = resid_in + merge_term(whole_merge, mixed_low)
        scale_two, normed_two = norm_forward(resid_mid, feed_gain)
        full_two = gather_features(normed_two)
        gate = contract_rows(full_two, whole_gate)
        upper = contract_rows(full_two, whole_up)
        hidden, geglu_pull = jax.vjp(geglu, gate, upper)
        hidden_low = hidden.astype(jnp.bfloat16)
        result = resid_mid + spread_sum(contract_cross(whole_down, hidden_low))
        outputs.append(result.astype(jnp.bfloat16))
        grad_full = gather_cotangent(grad_out.astype(jnp.bfloat16))
        acc_down = acc_down + contract_cross(hidden_low, grad_full)
        grad_gate, grad_upper = geglu_pull(contract_cross(grad_full, whole_down))
        grad_gate = grad_gate.astype(jnp.bfloat16)
        grad_upper = grad_upper.astype(jnp.bfloat16)
        feed_joined = weight_grads(full_two, jnp.concatenate([grad_gate, grad_upper], axis=1))
        acc_gate = acc_gate + feed_joined[:, :feed_cols]
        acc_up = acc_up + feed_joined[:, feed_cols:]
        grad_normed_two = back_sum(
            contract_cols(whole_gate, grad_gate) + contract_cols(whole_up, grad_upper)
        )
        grad_mid_norm, feed_part = norm_backward(resid_mid, scale_two, feed_gain, grad_normed_two)
        acc_feed = acc_feed + feed_part
        grad_mid = grad_out + grad_mid_norm
        grad_mid_full = gather_cotangent(grad_mid.astype(jnp.bfloat16))
        acc_merge = acc_merge + contract_cross(mixed_low, grad_mid_full)
        pulled = mixer_pull(contract_cross(grad_mid_full, whole_merge))
        grad_branch = pulled[0].astype(jnp.bfloat16)
        grad_lru = pulled[1].astype(jnp.bfloat16)
        acc_small = tuple((total + part for total, part in zip(acc_small, pulled[2:])))
        branch_joined = weight_grads(full_one, jnp.concatenate([grad_branch, grad_lru], axis=1))
        acc_branch = acc_branch + branch_joined[:, :lru_cols]
        acc_recur = acc_recur + branch_joined[:, lru_cols:]
        grad_normed_one = back_sum(
            contract_cols(whole_branch, grad_branch) + contract_cols(whole_recur, grad_lru)
        )
        grad_in_norm, mix_part = norm_backward(resid_in, scale_one, mix_gain, grad_normed_one)
        acc_mix = acc_mix + mix_part
        in_grads.append(grad_mid + grad_in_norm)
    sum_branch, sum_recur, sum_gate, sum_up = (
        row_sum(acc_branch, 0),
        row_sum(acc_recur, 0),
        row_sum(acc_gate, 0),
        row_sum(acc_up, 0),
    )
    sum_merge, sum_down = (
        row_sum(acc_merge, 1),
        row_sum(acc_down, 1),
    )
    summed = lax.psum(
        (
            acc_mix,
            acc_feed,
            acc_small[0],
            acc_small[1],
            acc_small[2],
            acc_small[3],
            acc_small[4],
            acc_small[5],
            acc_small[6],
        ),
        "row",
    )
    result_all = jnp.concatenate(outputs, axis=1)
    input_grad = jnp.concatenate(in_grads, axis=1)
    return (
        result_all,
        input_grad,
        summed[0],
        sum_branch,
        sum_recur,
        summed[2],
        summed[3],
        summed[4],
        summed[5],
        summed[6],
        summed[7],
        summed[8],
        sum_merge,
        summed[1],
        sum_gate,
        sum_up,
        sum_down,
    )


MESH = pl.DeviceIdType.MESH
F32 = jnp.float32
BF16 = jnp.bfloat16
LINE = 4
PART = 128
PARTS = 8
GELU_A = 0.7978845608028654
GELU_B = 0.044715


def place():
    row, col = lax.axis_index("row"), lax.axis_index("col")
    return row, col // 2, col % 2


def at_line(z, core):
    return {"col": 2 * z + core}


def lanes(part):
    return pl.ds(pl.multiple_of(part * PART, PART), PART)


def rows_of(index, size):
    return pl.ds(pl.multiple_of(index * size, 16), size)


def dot(a, b):
    return lax.dot_general(a, b, (((1,), (0,)), ((), ())), preferred_element_type=F32)


def dot_nt(a, b):
    return lax.dot_general(a, b, (((1,), (1,)), ((), ())), preferred_element_type=F32)


def greet(row, z, core, rows, line):
    barrier = pltpu.get_barrier_semaphore()
    peers = [{"col": 2 * z + (1 - core)}]
    if rows:
        peers += [{"row": row ^ d} for d in (1, 2, 3)]
    if line:
        peers += [at_line(z ^ d, core) for d in (1, 2, 3)]
    for peer in peers:
        pl.semaphore_signal(barrier, inc=1, device_id=peer, device_id_type=MESH)
    pl.semaphore_wait(barrier, len(peers))


def remote(src, dst, send, recv, peer):
    return pltpu.make_async_remote_copy(
        src_ref=src, dst_ref=dst, send_sem=send, recv_sem=recv, device_id=peer, device_id_type=MESH
    )


class Gather:
    def __init__(self, ref, send, recv, z, core, block, back=False):
        self.ref, self.sems, self.z, self.core = ref, (send, recv), z, core
        self.block, self.back = block, back

    def copy(self, way, hop, step, owner, incoming=False):
        part = PARTS - 1 - step if self.back else step
        piece = self.ref.at[part, rows_of(owner, self.block), :]
        peer = at_line(self.z + (1 if (way == 0) != incoming else -1), self.core)
        return remote(piece, piece, self.sems[0].at[way, hop, step], self.sems[1].at[way, hop, step], peer)

    def each(self, hop, act, incoming):
        z = self.z
        if incoming:
            cases = ((0, z - 1 - hop >= 0, z - 1 - hop), (1, z + 1 + hop < LINE, z + 1 + hop))
        else:
            cases = (
                (0, (z >= hop) & (z < LINE - 1), z - hop),
                (1, (z + hop < LINE) & (z >= 1), z + hop),
            )
        for way, here, owner in cases:
            pl.when(here)(functools.partial(act, way, owner))

    def send(self, hop, step):
        self.each(hop, lambda way, owner: self.copy(way, hop, step, owner).start(), False)

    def arrive(self, hop, step):
        self.each(hop, lambda way, owner: self.copy(way, hop, step, owner, True).wait_recv(), True)

    def forward(self, hop, step):
        self.arrive(hop - 1, step)
        self.send(hop, step)

    def sent(self):
        def one(step, carry):
            for hop in range(LINE - 1):
                self.each(hop, lambda way, owner: self.copy(way, hop, step, owner).wait_send(), False)
            return carry

        lax.fori_loop(0, PARTS, one, 0)

    def middle(self, step, ahead=1):
        for hop in (2, 1, 0):
            later = step + ahead + 2 - hop
            act = self.forward if hop else self.send
            pl.when(later < PARTS)(functools.partial(act, hop, later))


class Spread:
    def __init__(self, own, held, send, recv, z, core):
        self.own, self.held, self.sems, self.z, self.core = own, held, (send, recv), z, core

    def copy(self, way, step, hop):
        slot = hop if way == 0 else LINE - hop
        there = slot - 1 if way == 0 else slot + 1
        peer = at_line(self.z + (1 if way == 0 else -1), self.core)
        return remote(
            self.held.at[step, slot],
            self.held.at[step, there],
            self.sems[0].at[way, step, hop],
            self.sems[1].at[way, step, hop - 1],
            peer,
        )

    def landed(self, way, step, hop):
        slot = hop if way == 0 else LINE - hop
        piece = self.held.at[step, slot]
        peer = at_line(self.z + (-1 if way == 0 else 1), self.core)
        remote(piece, piece, self.sems[0].at[way, step, hop], self.sems[1].at[way, step, hop], peer).wait_recv()

    def push(self, way, step, first):
        z = self.z

        def one(i, carry):
            hop = LINE - 1 - i
            owner = z + hop if way == 0 else z - hop
            slot = hop if way == 0 else LINE - hop

            @pl.when((owner >= 0) & (owner < LINE))
            def _():
                @pl.when(first)
                def _():
                    self.held[step, slot] = self.own(step, owner)[...].astype(BF16)

                @pl.when(jnp.logical_not(first))
                def _():
                    self.landed(way, step, hop)
                    total = self.own(step, owner)[...].astype(F32) + self.held[step, slot].astype(F32)
                    self.held[step, slot] = total.astype(BF16)

                self.copy(way, step, hop).start()

            return carry

        lax.fori_loop(0, LINE - 1, one, 0)

    def serve(self, t, finish):
        z = self.z
        step = t - (LINE - 1)

        @pl.when((step >= 0) & (step < PARTS))
        def _():
            @pl.when(z == 0)
            def _():
                self.landed(1, step, 0)
                finish(step, lambda a, n: self.mine(step, a, n) + self.got(step, LINE, a, n))

            @pl.when(z == LINE - 1)
            def _():
                self.landed(0, step, 0)
                finish(step, lambda a, n: self.mine(step, a, n) + self.got(step, 0, a, n))

            @pl.when((z > 0) & (z < LINE - 1))
            def _():
                self.landed(0, step, 0)
                self.landed(1, step, 0)
                finish(
                    step,
                    lambda a, n: self.mine(step, a, n) + (self.got(step, 0, a, n) + self.got(step, LINE, a, n)),
                )

        for way, late, turn in ((1, LINE - 1 - z, z < 2), (0, z, z >= 0), (1, LINE - 1 - z, z >= 2)):
            step = t - late
            pl.when((step >= 0) & (step < PARTS) & turn)(functools.partial(self.push, way, step, late == 0))

    def mine(self, step, start, size):
        return self.own(step, self.z)[pl.ds(start, size), :].astype(F32)

    def got(self, step, slot, start, size):
        return self.held[step, slot, pl.ds(start, size)].astype(F32)

    def sent(self):
        z = self.z

        def one(step, carry):
            for way in (0, 1):
                for hop in range(1, LINE):
                    owner = z + hop if way == 0 else z - hop

                    @pl.when((owner >= 0) & (owner < LINE))
                    def _():
                        self.copy(way, step, hop).wait_send()

            return carry

        lax.fori_loop(0, PARTS, one, 0)


def share_line(ref, send, recv, z, core):
    copies = [
        remote(ref.at[z], ref.at[z], send.at[d - 1], recv.at[d - 1], at_line(z ^ d, core)) for d in (1, 2, 3)
    ]
    for copy in copies:
        copy.start()
    for d in (1, 2, 3):
        piece = ref.at[z ^ d]
        remote(piece, piece, send.at[d - 1], recv.at[d - 1], at_line(z ^ d, core)).wait_recv()
    for copy in copies:
        copy.wait_send()


class Weights:
    def __init__(self, src, dst, send, recv, own, row, z, core, turned, stride=0, start=0):
        self.src, self.dst, self.send, self.recv, self.own = src, dst, send, recv, own
        self.row, self.core, self.turned = row, core, turned
        self.stride, self.first = stride or src.shape[0], start
        self.sibling = {"col": 2 * z + (1 - core)}

    def spot(self, row, core):
        down, right = (row, core) if self.turned else (core, row)
        rows, cols = self.src.shape
        at = pl.ds(pl.multiple_of(down * self.stride + self.first, 16), rows)
        return self.dst.at[at, pl.ds(pl.multiple_of(right * cols, 128), cols)]

    def to_row(self, d):
        return remote(
            self.src, self.spot(self.row, self.core), self.send.at[d], self.recv.at[d], {"row": self.row ^ d}
        )

    def to_sibling(self, d):
        if d == 0:
            return remote(
                self.src, self.spot(self.row, self.core), self.send.at[0], self.recv.at[0], self.sibling
            )
        piece = self.spot(self.row ^ d, self.core)
        return remote(piece, piece, self.send.at[3 + d], self.recv.at[3 + d], self.sibling)

    def local(self):
        return pltpu.make_async_copy(self.src, self.spot(self.row, self.core), self.own)

    def start(self):
        for d in (1, 2, 3):
            self.to_row(d).start()
        self.to_sibling(0).start()
        self.local().start()

    def forward(self):
        for d in (1, 2, 3):
            piece = self.spot(self.row ^ d, self.core)
            remote(piece, piece, self.send.at[d], self.recv.at[d], {"row": self.row ^ d}).wait_recv()
            self.to_sibling(d).start()

    def finish(self):
        self.local().wait()
        for d in (0, 1, 2, 3):
            piece = self.spot(self.row ^ d, 1 - self.core)
            sem = 0 if d == 0 else 3 + d
            remote(piece, piece, self.send.at[sem], self.recv.at[sem], self.sibling).wait_recv()

    def sent(self):
        for d in (1, 2, 3):
            self.to_row(d).wait_send()
            self.to_sibling(d).wait_send()
        self.to_sibling(0).wait_send()


def gelu_parts(b):
    t = jnp.tanh(GELU_A * (b + GELU_B * (b * b * b)))
    half = 0.5 + 0.5 * t
    slope = half + (0.5 * b) * (1.0 - t * t) * (GELU_A + (3.0 * GELU_A * GELU_B) * (b * b))
    return b * half, slope


def eight(v):
    return jnp.sum(v.reshape(v.shape[0] // 8, 8, v.shape[1]), axis=0)


def fold(v):
    total = v[:, 0:128]
    for j in range(1, v.shape[1] // 128):
        total = total + v[:, j * 128 : (j + 1) * 128]
    return total


def tokens_of(ref, piece):
    return jnp.concatenate([ref[k, piece, :] for k in range(PARTS)], axis=1)


def blocks(count, body):
    def one(i, carry):
        body(i)
        return carry

    lax.fori_loop(0, count, one, 0)


def scale_of(ref, eps, width):
    total = jnp.sum(jnp.sum(ref[...], axis=0), axis=0, keepdims=True)
    return lax.rsqrt(total / width + eps)


def forward_kernel(
    width, eps,
    x_in, g_in, segs, vec, retain, admit, br_s, m_s, gu_s, d_s, brn_s, mn_s,
    masks, par, gains, gates, coef, scale, scale_two, y_out, n1_out, q_out, x_out, g_out, b_out, p_out, u_out, r_out, i_out, h_out,
    result, dn2_out, dev_h, z_h, g_own, g_got, gd_own, gd_got, br_n, m_n,
    sums, sums2, sums3, vec_all, block_all, gates_hi, gates_lo, normed, normed2, go, x_own, y, dn2, q_c, p_s, h_s, room, uh, ul,
    own, held, held_n, held_o, gu, gun, down, dt, zs, dev,
    x_send, x_recv, x_loc, i_send, i_recv, i_loc, l_send, l_recv, n_send, n_recv, c_send, c_recv, g_send, g_recv, e_send, e_recv, f_send, f_recv,
    s_send, s_recv, t_send, t_recv, o_send, o_recv, w_send, w_recv, w_own, k_sem, v_sem, d_send, d_recv, d_own,
):
    row, z, core = place()
    block, seq = y.shape
    half = x_in.shape[0]
    chan = p_s.shape[0]
    hid = zs.shape[0]
    b_s, u_s, r_s, i_s, a_c = [room.at[n * chan : (n + 1) * chan, :] for n in range(5)]
    ev, dz = room.at[0 : 2 * hid, :], room.at[2 * hid : 3 * hid, :]
    hh = hid // 2
    hc = chan // 2
    sibling = {"col": 2 * z + (1 - core)}
    greet(row, z, core, True, True)
    br, mt = gun.at[0 : 2 * chan, 0:width], dt.at[:, 0:chan]
    wide = br_s.shape[0]
    recur_s, branch_s = br_s.at[wide // 2 :, :], br_s.at[0 : wide // 2, :]
    weights = [
        Weights(src, dst, w_send.at[n], w_recv.at[n], w_own.at[n], row, z, core, n in (2, 5), stride, start)
        for n, (src, dst, stride, start) in enumerate(
            (
                (recur_s, br, hc, 0),
                (branch_s, br, hc, chan),
                (m_s, mt, 0, 0),
                (gu_s, gu, 0, 0),
                (d_s, down, 0, 0),
                (brn_s, br_n, 0, 0),
                (mn_s, m_n, 0, 0),
            )
        )
    ]
    mine = pl.ds(pl.multiple_of(core * seq, seq), seq)
    other = pl.ds(pl.multiple_of((1 - core) * seq, seq), seq)
    inner = pl.ds(pl.multiple_of(z * block + core * half, 16), half)
    outer = rows_of(core, half)
    swaps = [
        remote(x_in.at[:, other], x_own.at[outer, :], x_send.at[0], x_recv.at[0], sibling),
        pltpu.make_async_copy(x_in.at[:, mine], x_own.at[outer, :], x_loc.at[0]),
    ]
    for k in range(PARTS):
        theirs, ours = [pl.ds(pl.multiple_of(c * seq + k * PART, 128), PART) for c in (1 - core, core)]
        swaps.append(remote(g_in.at[:, theirs], go.at[k, inner, :], i_send.at[k], i_recv.at[k], sibling))
        swaps.append(pltpu.make_async_copy(g_in.at[:, ours], go.at[k, inner, :], i_loc.at[k]))
    trades = []
    for n, (src, dst) in enumerate(
        ((vec, vec_all.at[core]), (retain, block_all.at[core, 0]), (admit, block_all.at[core, 1]))
    ):
        trades.append(remote(src, dst, x_send.at[2 + n], x_recv.at[2 + n], sibling))
        trades.append(pltpu.make_async_copy(src, dst, x_loc.at[2 + n]))
    for swap in swaps + trades:
        swap.start()
    for w in weights[:3]:
        w.start()
    for swap in swaps + trades:
        swap.wait()
    flushes = [
        pltpu.make_async_copy(x_own, x_out, v_sem.at[0]),
        pltpu.make_async_copy(go.at[:, rows_of(z, block), :], g_out, v_sem.at[1]),
    ]
    for flush in flushes:
        flush.start()
    gather = Gather(normed, g_send, g_recv, z, core, block)
    gather_go = Gather(go, e_send, e_recv, z, core, block)
    gather_two = Gather(normed2, f_send, f_recv, z, core, block)
    shares = lambda k, s: own.at[k, s]
    shares_o = lambda k, s: normed.at[k, rows_of(s, block), :]
    spread = Spread(shares, held, s_send, s_recv, z, core)
    spread_n = Spread(shares, held_n, t_send, t_recv, z, core)
    spread_o = Spread(shares_o, held_o, o_send, o_recv, z, core)
    res = x_own
    gather_go.send(0, 0)
    gather_go.send(0, 1)
    for c in (0, 1):
        at = slice(c * hc, (c + 1) * hc)
        par[at, :] = vec_all[c].T
        gains[c * half : (c + 1) * half, :] = par[c * hc : c * hc + half, :]

    sums[z] = jnp.zeros(sums.shape[1:], F32)

    def squares(i):
        v = x_own[rows_of(i, 16), :].astype(F32)
        v = v * v
        sums[z] += v[:8] + v[8:]

    blocks(block // 16, squares)
    share_line(sums, l_send, l_recv, z, core)
    scale[...] = jnp.broadcast_to(scale_of(sums, eps, width), scale.shape)

    def norm(i):
        v = x_own[rows_of(i, 16), :].astype(F32) * scale[0:1, :] * gains[rows_of(i, 16), 8:9]
        v = v.astype(BF16)
        for k in range(PARTS):
            normed[k, pl.ds(pl.multiple_of(z * block + i * 16, 16), 16), :] = v[:, k * PART : (k + 1) * PART]

    blocks(block // 16, norm)
    gather.send(0, 0)
    gather.send(0, 1)
    p_s[:, PART:] = jnp.zeros((chan, 128), F32)
    h_s[:, PART:] = jnp.zeros((chan, 128), F32)
    pads = [
        pltpu.make_async_copy(src.at[:, PART:], out.at[:, 0:128], v_sem.at[2 + n])
        for n, (src, out) in enumerate(((p_s, p_out), (h_s, h_out)))
    ]
    for pad in pads:
        pad.start()
    gates[...] = jnp.zeros(gates.shape, BF16)
    gates_hi[...] = jnp.zeros(gates_hi.shape, BF16)
    gates_lo[...] = jnp.zeros(gates_lo.shape, BF16)
    per = retain.shape[0]
    tap = retain.shape[1]
    for c in (0, 1):
        for n in (0, 1):
            for e in range(per):
                w = block_all[c, n, e]
                at, far = slice(e * tap, (e + 1) * tap), slice(n * hc + e * tap, n * hc + (e + 1) * tap)
                gates[c, at, far] = w.astype(BF16)
                w = w.T
                high = w.astype(BF16)
                gates_hi[c, far, at] = high
                gates_lo[c, far, at] = (w - high.astype(F32)).astype(BF16)
    masks[...] = jnp.zeros(masks.shape, F32)
    here = jnp.broadcast_to(segs[:, mine], (8, seq))
    spot = lax.broadcasted_iota(jnp.int32, (8, seq), 1)
    for lag in (1, 2, 3):
        same = jnp.where((pltpu.roll(here, lag, 1) == here) & (spot >= lag), 1.0, 0.0)
        masks[lag : lag + 1, 0:seq] = same[0:1]
        if lag == 1:
            masks[0:1, 0:seq] = 1.0 - same[0:1]
    gather.forward(1, 0)
    gather.send(0, 2)
    gather_go.forward(1, 0)
    gather.forward(1, 1)
    gather.forward(2, 0)
    weights[0].forward()
    gather_go.forward(1, 1)
    gather_go.forward(2, 0)
    weights[1].forward()
    for w in weights[3:5]:
        w.start()
    gather_go.forward(2, 1)
    weights[0].finish()
    for pad in pads:
        pad.wait()

    kept = (b_s, p_s, u_s, r_s, i_s, h_s, q_c)
    outs = (b_out, p_out, u_out, r_out, i_out, h_out, q_out)

    def keep(n, part):
        if n in (1, 5):
            at = pl.ds(pl.multiple_of(128 + part * PART, 128), PART)
            return pltpu.make_async_copy(kept[n].at[:, 128:], outs[n].at[:, at], k_sem.at[n])
        return pltpu.make_async_copy(kept[n], outs[n].at[:, lanes(part)], k_sem.at[n])

    def put_shares(k, whole):
        for s in range(LINE):
            own[k, s] = whole[s * block : (s + 1) * block, :].astype(own.dtype)

    def work(k):
        here = lanes(k)

        @pl.when(k > 0)
        def _():
            for n in range(len(kept)):
                keep(n, k - 1).wait()

        p_s[:, 0:128] = p_s[:, PART:]
        h_s[:, 0:128] = h_s[:, PART:]
        p_s[:, 128:] = dot(br[0:chan, :], normed[k])

        def conv(i):
            ch = rows_of(i, 64)
            window = p_s[ch, :]
            pr = par[ch, :]
            u = pr[:, 4:5] + pr[:, 0:1] * window[:, 128:]
            for lag in (1, 2, 3):
                u = u + pr[:, lag : lag + 1] * (pltpu.roll(window, lag, 1)[:, 128:] * masks[lag : lag + 1, here])
            u_s[ch, :] = u
            high = u.astype(BF16)
            uh[ch, :] = high
            ul[ch, :] = (u - high.astype(F32)).astype(BF16)

        blocks(chan // 64, conv)
        gather.middle(k)
        for g in range(chan // 256):
            at = slice(g * 256, (g + 1) * 256)
            pre = dot(gates_hi[g], uh[at, :]) + dot(gates_hi[g], ul[at, :]) + dot(gates_lo[g], uh[at, :])
            r_s[at, :] = pre[:256]
            i_s[at, :] = pre[256:]

        def decay(i):
            ch = rows_of(i, 64)
            pr = par[ch, :]
            start = masks[0:1, here] > 0.5
            r = jax.nn.sigmoid(r_s[ch, :] + pr[:, 5:6])
            gate = jax.nn.sigmoid(i_s[ch, :] + pr[:, 6:7])
            r_s[ch, :] = r
            i_s[ch, :] = gate
            a = jnp.exp(-(r * pr[:, 7:8]))
            m = jnp.where(start, 1.0, jnp.sqrt(1.0 - a * a + FLOOR))
            a_c[ch, :] = jnp.where(start, 0.0, a)
            h_s[ch, 128:] = m * gate * u_s[ch, :]

        blocks(chan // 64, decay)
        first = lax.broadcasted_iota(jnp.int32, (128, PART), 1) == 0

        def recur(i):
            ch = rows_of(i, 128)
            a, h = a_c[ch, :], h_s[ch, 128:]
            h = h + jnp.where(first, a * h_s[ch, 0:128][:, 127:128], 0.0)
            a = jnp.where(first, 0.0, a)
            shift = 1
            while shift < PART:
                h = h + a * pltpu.roll(h, shift, 1)
                if shift * 2 < PART:
                    a = a * pltpu.roll(a, shift, 1)
                shift *= 2
            h_s[ch, 128:] = h

        blocks(chan // 128, recur)

        @pl.when(k == 0)
        def _():
            weights[2].forward()
            weights[1].finish()

        b_s[...] = dot(br[chan : 2 * chan, :], normed[k])

        def mixed(i):
            ch = rows_of(i, 64)
            b = b_s[ch, :]
            t = jnp.tanh(GELU_A * (b + GELU_B * (b * b * b)))
            q_c[ch, :] = (b * (0.5 + 0.5 * t) * h_s[ch, 128:]).astype(BF16)

        blocks(chan // 64, mixed)
        pl.when(k == 0)(weights[2].finish)
        put_shares(k, dot(mt[...], q_c[...]))
        for n in range(len(kept)):
            keep(n, k).start()

    def finish(k, total):
        def add(i):
            at = pl.multiple_of(i * 64, 64)
            y[pl.ds(at, 64), lanes(k)] = x_own[pl.ds(at, 64), lanes(k)].astype(F32) + total(at, 64)

        blocks(block // 64, add)

    def square(k):
        sums2[k, z] = jnp.zeros(sums2.shape[2:], F32)

        def one(i):
            v = y[rows_of(i, 64), lanes(k)]
            sums2[k, z] += eight(v * v)

        blocks(block // 64, one)
        for d in (1, 2, 3):
            share(k, d).start()

    def share(k, d):
        return remote(
            sums2.at[k, z], sums2.at[k, z], n_send.at[k, d - 1], n_recv.at[k, d - 1], at_line(z ^ d, core)
        )

    def norm_two(k):
        for d in (1, 2, 3):
            piece = sums2.at[k, z ^ d]
            remote(piece, piece, n_send.at[k, d - 1], n_recv.at[k, d - 1], at_line(z ^ d, core)).wait_recv()
        s2 = scale_of(sums2.at[k], eps, width)
        scale_two[:, lanes(k)] = jnp.broadcast_to(s2, (8, PART))

        def one(i):
            at = rows_of(i, 64)
            v = y[at, lanes(k)] * scale_two[0:1, lanes(k)] * gains[at, 9:10]
            normed2[k, pl.ds(pl.multiple_of(z * block + i * 64, 64), 64), :] = v.astype(BF16)

        blocks(block // 64, one)

    def turn_down(i):
        at = pl.ds(pl.multiple_of(i * 128, 128), 128)
        dt[:, at] = down[at, :].T

    def turn_up(i):
        at = pl.ds(pl.multiple_of(i * 128, 128), 128)
        gun[:, at] = gu[at, :].T

    def step(t, carry):
        gather.arrive(2, t)
        work(t)
        spread.serve(t, finish)
        pl.when(t >= 3)(lambda: square(t - 3))
        pl.when(t >= 4)(lambda: norm_two(t - 4))
        pl.when((t >= 4) & (t < 7))(lambda: gather_two.send(0, t - 4))
        pl.when((t >= 6) & (t < 8))(lambda: gather_two.forward(1, t - 6))
        pl.when(t == 5)(weights[3].forward)
        return carry

    lax.fori_loop(0, PARTS, step, 0)
    for w in weights[:3]:
        w.sent()
    for w in weights[5:]:
        w.start()
    for n in range(len(kept)):
        keep(n, PARTS - 1).wait()
    flush_n = pltpu.make_async_copy(normed, n1_out, v_sem.at[4])
    flush_n.start()
    gather_go.send(0, 2)
    gather_go.send(0, 3)
    spread.serve(PARTS, finish)
    square(PARTS - 3)
    norm_two(PARTS - 4)
    gather_two.forward(2, 0)
    weights[4].forward()
    spread.serve(PARTS + 1, finish)
    square(PARTS - 2)
    norm_two(PARTS - 3)
    gather_go.forward(1, 2)
    weights[4].finish()
    blocks(hid // 128, turn_down)
    spread.serve(PARTS + 2, finish)
    square(PARTS - 1)
    norm_two(PARTS - 2)
    gather.sent()
    for flush in flushes + [flush_n]:
        flush.wait()
    weights[3].finish()
    blocks(2 * hid // 128, turn_up)
    norm_two(PARTS - 1)

    def keep_dev(k):
        return pltpu.make_async_copy(dev, dev_h.at[:, lanes(k)], v_sem.at[5])

    def keep_z(k):
        return pltpu.make_async_copy(zs, z_h.at[:, lanes(k)], v_sem.at[6])

    def feed(k):

        @pl.when(k > 0)
        def _():
            keep_dev(k - 1).wait()
            keep_z(k - 1).wait()

        ev[...] = dot(gu[...], normed2[k])
        gather_two.middle(k)
        gather_go.middle(k, 2)
        gather_go.arrive(2, k)
        dz[...] = dot(down[...], go[k])
        for c in range(2):

            def one(i):
                off = pl.multiple_of(i * 64, 64)
                e = ev[pl.ds(c * 2 * hh + off, 64), :]
                v = ev[pl.ds(c * 2 * hh + hh + off, 64), :]
                d = dz[pl.ds(c * hh + off, 64), :]
                act, slope = gelu_parts(e)
                zs[pl.ds(c * hh + off, 64), :] = (act * v).astype(BF16)
                dev[pl.ds(c * 2 * hh + off, 64), :] = (d * v * slope).astype(BF16)
                dev[pl.ds(c * 2 * hh + hh + off, 64), :] = (d * act).astype(BF16)

            blocks(hh // 64, one)
        put_shares(k, dot(gun[...], dev[...]))
        spread_n.serve(k, finish_n)
        normed[k] = dot(dt[...], zs[...]).astype(BF16)
        spread_o.serve(k, finish_o)
        keep_dev(k).start()
        keep_z(k).start()

    def finish_o(k, total):
        def add(i):
            at = pl.multiple_of(i * 64, 64)
            res[pl.ds(at, 64), lanes(k)] = (y[pl.ds(at, 64), lanes(k)] + total(at, 64)).astype(BF16)

        blocks(block // 64, add)

    def keep_n(k):
        return pltpu.make_async_copy(dn2, dn2_out.at[:, lanes(k)], v_sem.at[3])

    def finish_n(k, total):
        @pl.when(k > 0)
        def _():
            keep_n(k - 1).wait()

        sums3[k, z] = jnp.zeros(sums3.shape[2:], F32)

        def add(i):
            at = pl.multiple_of(i * 64, 64)
            d = total(at, 64)
            dn2[pl.ds(at, 64), :] = d
            sums3[k, z] += eight(d * y[pl.ds(at, 64), lanes(k)] * gains[pl.ds(at, 64), 9:10])

        blocks(block // 64, add)
        keep_n(k).start()
        for d in (1, 2, 3):
            share_c(k, d).start()

    def share_c(k, d):
        return remote(
            sums3.at[k, z], sums3.at[k, z], c_send.at[k, d - 1], c_recv.at[k, d - 1], at_line(z ^ d, core)
        )

    def feed_step(t, carry):
        gather_two.arrive(2, t)
        feed(t)
        pl.when(t == 4)(weights[5].forward)
        pl.when(t == 6)(weights[6].forward)
        return carry

    lax.fori_loop(0, PARTS, feed_step, 0)
    for w in weights[3:5]:
        w.sent()
    keep_dev(PARTS - 1).wait()
    keep_z(PARTS - 1).wait()
    dev_all, z_all = gu.at[:, 0:seq], dt.at[0:hid, 0:seq]
    loads = [pltpu.make_async_copy(dev_h, dev_all, v_sem.at[5]), pltpu.make_async_copy(z_h, z_all, v_sem.at[6])]
    for load in loads:
        load.start()
    for load in loads:
        load.wait()

    def columns(start):
        return pl.ds(pl.multiple_of(start, 128), block)

    def place_up(j):
        side = jnp.where(j >= 3, core, 1 - core)
        return side * hid + (j % 3) * block, columns((j % 3) * block)

    def send_up(j):
        at, to = place_up(j)
        return remote(gun.at[:, columns(at)], g_got.at[:, to], d_send.at[j], d_recv.at[j], sibling)

    def keep_up(j):
        at, to = place_up(j)
        return pltpu.make_async_copy(gun.at[:, columns(at)], g_own.at[:, to], d_own.at[j - 3])

    def send_down():
        return remote(down.at[rows_of(1 - core, hh), :], gd_got, d_send.at[3], d_recv.at[3], sibling)

    def keep_down():
        return pltpu.make_async_copy(down.at[rows_of(core, hh), :], gd_own, d_own.at[3])

    def grad_up(j):
        at = place_up(j)[0]
        right = pl.ds(pl.multiple_of(at, 16), block)
        for low in (0, width // 2):
            piece = slice(low, low + width // 2)
            gun[piece, columns(at)] = dot_nt(tokens_of(normed2, piece), dev_all[right, :]).astype(BF16)

        @pl.when(j < 3)
        def _():
            send_up(j).start()

        @pl.when(j >= 3)
        def _():
            keep_up(j).start()

    def grad_down(side):
        at = rows_of(side, hh)
        for low in range(0, width, 2 * block):
            piece = slice(low, low + 2 * block)
            down[at, piece] = dot_nt(z_all[at, :], tokens_of(go, piece)).astype(BF16)

    def drain(i, carry):
        t = PARTS + i
        blocks(2, lambda j: grad_up(2 * i + j))
        spread_n.serve(t, finish_n)
        spread_o.serve(t, finish_o)

        @pl.when(i < 2)
        def _():
            grad_down(jnp.where(i == 0, 1 - core, core))

        pl.when(i == 0)(lambda: send_down().start())
        pl.when(i == 1)(lambda: keep_down().start())
        return carry

    lax.fori_loop(0, LINE - 1, drain, 0)
    last = [
        remote(res.at[rows_of(1 - core, half), :], result.at[:, mine], x_send.at[0], x_recv.at[0], sibling),
        pltpu.make_async_copy(res.at[rows_of(core, half), :], result.at[:, mine], x_loc.at[0]),
        pltpu.make_async_copy(y, y_out, v_sem.at[2]),
        keep_n(PARTS - 1),
    ]
    for copy in last[:3]:
        copy.start()
    for w in weights[5:]:
        w.finish()
        w.sent()
    for one in (gather_go, gather_two, spread, spread_n, spread_o):
        one.sent()
    for k in range(PARTS):
        for d in (1, 2, 3):
            share(k, d).wait_send()
            share_c(k, d).wait_send()
            piece = sums3.at[k, z ^ d]
            remote(piece, piece, c_send.at[k, d - 1], c_recv.at[k, d - 1], at_line(z ^ d, core)).wait_recv()
        total = jnp.sum(jnp.sum(sums3[k], axis=0), axis=0, keepdims=True)
        at = slice(k * PART, (k + 1) * PART)
        s2 = scale_two[:, at]
        coef[:, at] = s2 * s2 * s2 * (total / width)
    for j in range(3):
        keep_up(j + 3).wait()
        send_up(j).wait()
    keep_down().wait()
    send_down().wait()
    for copy in last:
        copy.wait()


def back_kernel(
    width,
    y, dn2_h, g_h, x_own, scale_two, scale_one, coef_two, gains, masks, par, gates_t, m_h, br_h,
    b_h, p_h, u_h, r_h, i_h, h_h, q_h, n1_h, f_own, f_got, fd_own, fd_got,
    input_grad, tiny_v, tiny_g, f_sum, f_land, fd_sum, fd_land, g_sum, g_land, gm_sum, gm_land,
    sums, coef, m_n, br_n, b_s, p_s, u_s, r_s, i_s, h_s, dyf, dbp, dy, dn1, dq, du, dri, a_c, l_c, carry_s, own, held,
    qv, f_a, f_b, fd_a, fd_b, feed_part, mix_part, small, gate_grad, g_s, g_got, gm_got,
    vec, vec_in, vec_all, gd, gd_in, gd_all,
    c_sem, k_sem, l_send, l_recv, g_send, g_recv, s_send, s_recv, r_send, r_recv,
    f_sem, f_send, f_recv, d_send, d_recv, d_own, q_send, q_recv, n_send, n_recv, v_send, v_recv,
):
    row, z, core = place()
    block, seq = y.shape
    half = block // 2
    chan = b_s.shape[1]
    hc = chan // 2
    sibling = {"col": 2 * z + (1 - core)}
    greet(row, z, core, True, True)
    load_g = pltpu.make_async_copy(g_h, g_s, c_sem.at[0])
    load_g.start()
    dn2 = dn1
    load_d = pltpu.make_async_copy(dn2_h, dn2, c_sem.at[5])
    load_d.start()
    load_m = pltpu.make_async_copy(m_h, m_n, c_sem.at[1])
    load_m.start()
    load_b = pltpu.make_async_copy(br_h, br_n, c_sem.at[2])
    load_b.start()
    load_q = pltpu.make_async_copy(q_h, qv, c_sem.at[3])
    n1 = dyf
    load_n = pltpu.make_async_copy(n1_h, n1, c_sem.at[4])
    kept = (b_s, p_s, u_s, r_s, i_s, h_s)
    srcs = (b_h, p_h, u_h, r_h, i_h, h_h)

    def fetch(n, part):
        if kept[n] is p_s or kept[n] is h_s:
            at = pl.ds(pl.multiple_of(part * PART, 128), PART + 128)
        else:
            at = lanes(part)
        return pltpu.make_async_copy(srcs[n].at[:, at], kept[n].at[part % 2], k_sem.at[n, part % 2])

    def fetch_all(part):
        for n in range(len(kept)):
            fetch(n, part).start()

    fetch_all(PARTS - 1)
    load_q.start()
    du[:, 0:128] = jnp.zeros((chan, 128), F32)
    carry_s[...] = jnp.zeros(carry_s.shape, F32)
    small[...] = jnp.zeros(small.shape, F32)
    gate_grad[...] = jnp.zeros(gate_grad.shape, F32)

    load_d.wait()
    load_g.wait()
    gather = Gather(dyf, g_send, g_recv, z, core, block, back=True)

    def outer(part):
        here = slice(part * PART, (part + 1) * PART)

        def one(i):
            at = rows_of(i, 64)
            s2 = scale_two[0:1, here]
            d, v = dn2[at, here], y[at, here]
            w = fold(d * v * s2)
            feed_part[at, :] = w if part == PARTS - 1 else feed_part[at, :] + w
            v = g_s[part, at, :].astype(F32) + (s2 * (gains[at, 9:10] * d) - v * coef_two[0:1, here])
            dy[at, here] = v
            dyf[part, pl.ds(pl.multiple_of(z * block + i * 64, 64), 64), :] = v.astype(BF16)

        blocks(block // 64, one)

    outer(PARTS - 1)
    gather.send(0, 0)
    outer(PARTS - 2)
    gather.send(0, 1)
    outer(PARTS - 3)
    gather.forward(1, 0)
    gather.send(0, 2)
    for part in range(PARTS - 3):
        outer(part)
    gather.forward(1, 1)
    gather.forward(2, 0)
    spread = Spread(lambda k, s: own.at[k, s], held, s_send, s_recv, z, core)
    load_m.wait()
    load_b.wait()
    final = lax.broadcasted_iota(jnp.int32, (128, PART), 1) == PART - 1

    f_arrays = ((f_own, f_got, f_a, f_b, f_sum, f_land), (fd_own, fd_got, fd_a, fd_b, fd_sum, fd_land))

    def f_loads(d):
        pulls = []
        for n, (ours, theirs, a, b, _, _) in enumerate(f_arrays):
            if n == 0:
                piece = (rows_of(row ^ d, block), slice(None))
            else:
                piece = (slice(None), pl.ds(pl.multiple_of((row ^ d) * block, 128), block))
            pulls.append(pltpu.make_async_copy(ours.at[piece], a.at[d], f_sem.at[n, 0]))
            pulls.append(pltpu.make_async_copy(theirs.at[piece], b, f_sem.at[n, 1]))
        return pulls

    def f_out(d):
        outs = []
        for n, (_, _, a, _, kept_at, land) in enumerate(f_arrays):
            if d == 0:
                outs.append(pltpu.make_async_copy(a.at[0], kept_at, f_send.at[n, 0]))
            else:
                outs.append(
                    remote(a.at[d], land.at[d - 1], f_send.at[n, d], f_recv.at[n, d], {"row": row ^ d})
                )
        return outs

    def f_part(d):
        for pull in f_loads(d):
            pull.wait()
        for _, _, a, b, _, _ in f_arrays:

            def add(i):
                at = rows_of(i, 64)
                a[d, at, :] = (a[d, at, :].astype(F32) + b[at, :].astype(F32)).astype(BF16)

            blocks(b.shape[0] // 64, add)
        for out in f_out(d):
            out.start()
        if d > 0:
            for pull in f_loads(d - 1):
                pull.start()

    def f_step(t):
        for d in range(LINE):
            pl.when(t == LINE - 1 - d)(functools.partial(f_part, d))

    for pull in f_loads(LINE - 1):
        pull.start()

    def work(t):
        k = PARTS - 1 - t
        here = lanes(k)
        wide = pl.ds(pl.multiple_of(k * PART, 128), PART + 128)
        slot = k % 2
        for n in range(len(kept)):
            fetch(n, k).wait()

        @pl.when(k > 0)
        def _():
            fetch_all(k - 1)

        dq[...] = dot(m_n[...], dyf[k])

        def before(i):
            ch = rows_of(i, 64)
            c = i // (hc // 64)
            low = pl.ds(pl.multiple_of(c * hc + i * 64, 64), 64)
            pr = par[ch, :]
            d = dq[ch, :]
            act, slope = gelu_parts(b_s[slot, ch, :])
            dbp[low, here] = (d * h_s[slot, ch, :][:, 128:] * slope).astype(BF16)
            l_c[ch, :] = d * act
            a_c[ch, :] = jnp.exp(-(r_s[slot, ch, :] * pr[:, 7:8]))

        blocks(chan // 64, before)
        gather.middle(t)

        def recur(i):
            ch = rows_of(i, 128)
            start = masks[0:1, here] > 0.5
            a, lam = jnp.where(start, 0.0, a_c[ch, :]), l_c[ch, :]
            lam = lam + jnp.where(final, carry_s[ch, :][:, 0:1], 0.0)
            w = jnp.where(final, 0.0, pltpu.roll(a, PART - 1, 1))
            shift = 1
            while shift < PART:
                lam = lam + w * pltpu.roll(lam, PART - shift, 1)
                if shift * 2 < PART:
                    w = w * pltpu.roll(w, PART - shift, 1)
                shift *= 2
            carry_s[ch, :] = jnp.broadcast_to((a * lam)[:, 0:1], (128, 128))
            l_c[ch, :] = lam

        blocks(chan // 128, recur)
        f_step(t)

        def after(i):
            ch = rows_of(i, 64)
            du[ch, PART:] = du[ch, 0:128]
            pr = par[ch, :]
            start = masks[0:1, here] > 0.5
            lam, a0 = l_c[ch, :], a_c[ch, :]
            earlier = pltpu.roll(h_s[slot, ch, :], 1, 1)[:, 128:]
            r, gate, u = r_s[slot, ch, :], i_s[slot, ch, :], u_s[slot, ch, :]
            m0 = jnp.sqrt(1.0 - a0 * a0 + FLOOR)
            m = jnp.where(start, 1.0, m0)
            lm = lam * m
            lu = lam * u
            du[ch, 0:PART] = lm * gate
            da = jnp.where(start, 0.0, lam * earlier - (lu * gate) * (a0 / m0)) * a0
            dr = da * (-pr[:, 7:8]) * (r * (1.0 - r))
            di = lu * m * (gate * (1.0 - gate))
            g, o = i // 4, (i % 4) * 64
            dri[pl.ds(pl.multiple_of(g * 512 + o, 64), 64), :] = dr.astype(BF16)
            dri[pl.ds(pl.multiple_of(g * 512 + 256 + o, 64), 64), :] = di.astype(BF16)
            small[5, ch, :] += fold(dr)
            small[6, ch, :] += fold(di)
            small[7, ch, :] += fold(da * r)

        blocks(chan // 64, after)
        for g in range(chan // 256):
            at = slice(g * 256, (g + 1) * 256)
            dd = dri[g * 512 : (g + 1) * 512, :]
            du[at, 0:PART] += dot(gates_t[g], dd)
            gate_grad[g] += dot_nt(u_s[slot, at, :].astype(BF16), dd)

        def conv(i):
            ch = rows_of(i, 64)
            c = i // (hc // 64)
            low = pl.ds(pl.multiple_of((c + 1) * hc + i * 64, 64), 64)
            pr = par[ch, :]
            follow = du[ch, :]
            window = p_s[slot, ch, :]
            d = follow[:, :PART]
            dp = pr[:, 0:1] * d
            small[4, ch, :] += fold(d)
            small[0, ch, :] += fold(d * window[:, 128:])
            for lag in (1, 2, 3):
                kd = follow * masks[lag : lag + 1, wide]
                dp = dp + pr[:, lag : lag + 1] * pltpu.roll(kd, PART + 128 - lag, 1)[:, :PART]
                small[lag, ch, :] += fold(kd[:, :PART] * pltpu.roll(window, lag, 1)[:, 128:])
            dbp[low, here] = dp.astype(BF16)

        blocks(chan // 64, conv)
        whole = dot(br_n[...], dbp[:, here])
        for s in range(LINE):
            own[t, s] = whole[s * block : (s + 1) * block, :].astype(own.dtype)

    def finish(t, total):
        k = PARTS - 1 - t

        sums[k, z] = jnp.zeros(sums.shape[2:], F32)

        @pl.when(t == 0)
        def _():
            mix_part[...] = jnp.zeros(mix_part.shape, F32)

        def add(i):
            at = pl.ds(pl.multiple_of(i * 64, 64), 64)
            d = total(pl.multiple_of(i * 64, 64), 64)
            dn1[at, lanes(k)] = d
            w = d * x_own[at, lanes(k)].astype(F32)
            sums[k, z] += eight(w * gains[at, 8:9])
            w = w * scale_one[0:1, lanes(k)]
            mix_part[at, :] += fold(w)

        blocks(block // 64, add)
        for d in (1, 2, 3):
            share(k, d).start()

    def share(k, d):
        return remote(sums.at[k, z], sums.at[k, z], l_send.at[k, d - 1], l_recv.at[k, d - 1], at_line(z ^ d, core))

    def step(t, carry):
        gather.arrive(2, t)
        work(t)
        spread.serve(t, finish)
        return carry

    lax.fori_loop(0, PARTS, step, 0)
    load_q.wait()

    lru = hc

    def cols_of(side):
        return pl.ds(pl.multiple_of(side * 2 * lru, 128), 2 * lru)

    def send_br():
        return remote(br_n.at[:, cols_of(1 - core)], g_got, d_send.at[0], d_recv.at[0], sibling)

    def send_m():
        return remote(m_n.at[rows_of(1 - core, lru), :], gm_got, d_send.at[1], d_recv.at[1], sibling)

    def grad_br(side):
        for low in range(0, width, 2 * block):
            piece = slice(low, low + 2 * block)
            br_n[piece, cols_of(side)] = dot_nt(tokens_of(n1, piece), dbp[rows_of(side, 2 * lru), :]).astype(BF16)

    def out_br(d):
        piece = br_n.at[rows_of(row ^ d, block), cols_of(core)]
        if d == 0:
            return pltpu.make_async_copy(piece, g_sum, d_own.at[0])
        return remote(piece, g_land.at[d - 1], q_send.at[0, d - 1], q_recv.at[0, d - 1], {"row": row ^ d})

    def out_m(d):
        piece = m_n.at[rows_of(core, lru), pl.ds(pl.multiple_of((row ^ d) * block, 128), block)]
        if d == 0:
            return pltpu.make_async_copy(piece, gm_sum, d_own.at[1])
        return remote(piece, gm_land.at[d - 1], q_send.at[1, d - 1], q_recv.at[1, d - 1], {"row": row ^ d})

    def drain(i, carry):
        t = PARTS + i

        @pl.when(i == 0)
        def _():
            for low in range(0, width, 2 * block):
                piece = slice(low, low + 2 * block)
                m_n[:, piece] = dot_nt(qv[...], tokens_of(dyf, piece)).astype(BF16)
            send_m().start()
            gather.sent()
            load_n.start()
            load_n.wait()
            grad_br(1 - core)
            send_br().start()

        @pl.when(i == 1)
        def _():
            grad_br(core)
            send_m().wait_recv()

            def add(j):
                at = rows_of(j, 32)
                to = pl.ds(pl.multiple_of(core * lru + j * 32, 32), 32)
                m_n[to, :] = (m_n[to, :].astype(F32) + gm_got[at, :].astype(F32)).astype(BF16)

            blocks(lru // 32, add)
            for d in (3, 2, 1, 0):
                out_m(d).start()

        @pl.when(i == 2)
        def _():
            send_br().wait_recv()

            def add(j):
                at = rows_of(j, 32)
                br_n[at, cols_of(core)] = (br_n[at, cols_of(core)].astype(F32) + g_got[at, :].astype(F32)).astype(BF16)

            blocks(width // 32, add)
            for d in (3, 2, 1, 0):
                out_br(d).start()

        spread.serve(t, finish)
        return carry

    lax.fori_loop(0, LINE - 1, drain, 0)
    mine = pl.ds(pl.multiple_of(core * seq, seq), seq)
    for side in (0, 1):
        for e in range(4):
            at = slice(e * 64, (e + 1) * 64)
            gd[side, at, 0:64] = gate_grad[side, at, e * 64 : (e + 1) * 64]
            gd[side, at, 64:128] = gate_grad[side, at, 256 + e * 64 : 256 + (e + 1) * 64]
    swap_gd = remote(gd.at[1 - core], gd_in, v_send.at[0], v_recv.at[0], sibling)
    swap_gd.start()
    lane = lax.broadcasted_iota(jnp.int32, (64, 128), 1)

    def columns(parts, at):
        total = jnp.zeros((64, 128), F32)
        for n, part in enumerate(parts):
            total = total + jnp.where(lane == n, jnp.sum(part(at), axis=1, keepdims=True), 0.0)
        return total

    vec[...] = jnp.zeros(vec.shape, F32)
    for j in range(chan // 64):
        at = slice(j * 64, (j + 1) * 64)
        v = columns([lambda at, n=n: small[n, at, :] for n in range(8)], at)
        vec[0, :, at] = v.T[0:8, :]

    for k in range(PARTS):
        for d in (1, 2, 3):
            share(k, d).wait_send()
            piece = sums.at[k, z ^ d]
            remote(piece, piece, l_send.at[k, d - 1], l_recv.at[k, d - 1], at_line(z ^ d, core)).wait_recv()
        total = jnp.sum(jnp.sum(sums[k], axis=0), axis=0, keepdims=True)
        at = slice(k * PART, (k + 1) * PART)
        s1 = scale_one[:, at]
        coef[:, at] = s1 * s1 * s1 * (total / width)

    def last(i):
        at = rows_of(i, 16)
        v = dy[at, :] + (
            scale_one[0:1, :] * (gains[at, 8:9] * dn1[at, :]) - x_own[at, :].astype(F32) * coef[0:1, :]
        )
        dy[at, :] = v

    blocks(block // 16, last)
    back = remote(dy.at[rows_of(1 - core, half), :], input_grad.at[:, mine], r_send, r_recv, sibling)
    back.start()
    keep_in = pltpu.make_async_copy(dy.at[rows_of(core, half), :], input_grad.at[:, mine], d_own.at[3])
    keep_in.start()
    for j in range(block // 64):
        at = slice(j * 64, (j + 1) * 64)
        v = columns([lambda at: mix_part[at, :], lambda at: feed_part[at, :]], at)
        vec[1, :, at] = v.T[0:8, :]
    swap_vec = remote(vec, vec_in, v_send.at[1], v_recv.at[1], sibling)
    swap_vec.start()
    swap_gd.wait()
    gd_all[0] = gd[core] + gd_in[...]
    rows_gd = [
        remote(gd_all.at[0], gd_all.at[d], n_send.at[0, d - 1], n_recv.at[0, d - 1], {"row": row ^ d}) for d in (1, 2, 3)
    ]
    for copy in rows_gd:
        copy.start()
    swap_vec.wait()
    vec_all[0] = vec[...] + vec_in[...]
    rows_vec = [
        remote(vec_all.at[0], vec_all.at[d], n_send.at[1, d - 1], n_recv.at[1, d - 1], {"row": row ^ d}) for d in (1, 2, 3)
    ]
    for copy in rows_vec:
        copy.start()
    spread.sent()
    for copy in rows_gd + rows_vec:
        copy.wait()
    for every, out in ((gd_all, tiny_g), (vec_all, tiny_v)):
        first, second = every[row % 2], every[1 - row % 2]
        third, fourth = every[2 + row % 2], every[3 - row % 2]
        out[...] = (first + second) + (third + fourth)
    for d in range(LINE):
        for out in f_out(d):
            out.wait()
    send_br().wait_send()
    send_m().wait_send()
    for d in (0, 1, 2, 3):
        out_br(d).wait()
        out_m(d).wait()
    for copy in (keep_in, back):
        copy.wait()


def last_kernel(
    f_sum, f_land, fd_sum, fd_land, g_sum, g_land, gm_sum, gm_land, tiny_v, tiny_g, lambdas,
    s_b, s_r, s_m, s_g, s_u, s_d, taps, offs, bias_r, bias_a, decay, mix, feed, retain, admit,
):
    core = place()[2]
    lru, block = s_m.shape
    ff, half = s_d.shape[0], mix.shape[1]

    def four(first, others, at):
        return first[at, :].astype(F32) + others[0, at, :].astype(F32) + (
            others[1, at, :].astype(F32) + others[2, at, :].astype(F32)
        )

    def put_gu(i):
        at = rows_of(i, 32)
        v = four(f_sum, f_land, at)
        s_g[at, :] = v[:, :ff]
        s_u[at, :] = v[:, ff:]
        v = four(g_sum, g_land, at)
        s_b[at, :] = v[:, :lru]
        s_r[at, :] = v[:, lru:]

    blocks(block // 32, put_gu)

    def put_d(i):
        at = rows_of(i, 32)
        s_d[at, :] = four(fd_sum, fd_land, at)

    blocks(ff // 32, put_d)

    def put_m(i):
        at = rows_of(i, 32)
        s_m[at, :] = four(gm_sum, gm_land, at)

    blocks(lru // 32, put_m)
    small = tiny_v[0, :, pl.ds(pl.multiple_of(core * lru, 128), lru)]
    taps[...] = small[0:4]
    offs[...] = small[4:5]
    bias_r[...] = small[5:6]
    bias_a[...] = small[6:7]
    decay[...] = small[7:8] * (8.0 * jax.nn.sigmoid(-lambdas[...]))
    gains = jnp.where(core == 0, tiny_v[1, :, 0:half], tiny_v[1, :, half : 2 * half])
    mix[...] = gains[0:1]
    feed[...] = gains[1:2]
    for e in range(retain.shape[0]):
        at = slice(e * 64, (e + 1) * 64)
        retain[e] = tiny_g[at, 0:64]
        admit[e] = tiny_g[at, 64:128]


ANY = pl.BlockSpec(memory_space=pl.ANY)
VM = pl.BlockSpec(memory_space=pltpu.VMEM)
DMA = pltpu.SemaphoreType.DMA
ROOM = 62 * 1024 * 1024


def shape(dims, kind):
    return jax.ShapeDtypeStruct(dims, kind)


def call(kernel, ins, outs, scratch, ident, name, flops):
    return pl.pallas_call(
        kernel,
        out_shape=[o[0] for o in outs],
        in_specs=ins,
        out_specs=[o[1] for o in outs],
        scratch_shapes=scratch,
        name=name,
        compiler_params=pltpu.CompilerParams(
            collective_id=ident, has_side_effects=True, vmem_limit_bytes=ROOM
        ),
        cost_estimate=pl.CostEstimate(flops=flops, bytes_accessed=40000000, transcendentals=0),
    )


def fast_body(
    inputs, segments, mix_gain, branch_weight, recur_weight, kernel, offsets, retain_weight, retain_bias,
    admit_weight, admit_bias, lambdas, merge_weight, feed_gain, gate_weight, up_weight, down_weight, cotangent,
):
    half, tokens = inputs.shape
    block, seq, width = 2 * half, tokens // 2, D
    lru, heads = branch_weight.shape[1], retain_weight.shape[0]
    chan = 2 * lru
    ff = gate_weight.shape[1]
    hid = 2 * ff
    rows = branch_weight.shape[0]
    cols = merge_weight.shape[1]
    rate = 8.0 * jax.nn.softplus(-lambdas)
    vec = [kernel] + [v[None, :] for v in (offsets, retain_bias, admit_bias, rate)]
    vec += [jnp.pad(v[None, :], ((0, 0), (0, lru - half))) for v in (mix_gain, feed_gain)]
    vec = jnp.concatenate(vec + [jnp.zeros((6, lru), F32)])
    br_s = jnp.concatenate([branch_weight, recur_weight], axis=1).T
    m_s = merge_weight.T
    gu_s = jnp.concatenate([gate_weight, up_weight], axis=1).T

    f_tok = lambda n, kind=F32: shape((n, seq), kind)
    padded = (shape((chan, 128 + seq), F32), ANY)
    state = [(f_tok(chan), ANY), padded, *[(f_tok(chan), ANY)] * 3, padded]
    line = [DMA((3,)), DMA((3,))]
    steps = [DMA((2, 3, PARTS)), DMA((2, 3, PARTS))]
    sums = [DMA((2, PARTS, LINE)), DMA((2, PARTS, LINE))]
    held = pltpu.VMEM((PARTS, LINE + 1, block, PART), BF16)
    own_low = pltpu.VMEM((PARTS, LINE, block, PART), BF16)
    tok = lambda n, kind=F32, lead=0: pltpu.VMEM((n, lead + seq), kind)
    one = lambda n, kind=F32, lead=0: pltpu.VMEM((n, lead + PART), kind)
    br_t = jnp.concatenate([branch_weight, recur_weight], axis=1)
    grad_gu, grad_d = (shape((width, 2 * ff), BF16), ANY), (shape((ff, width), BF16), ANY)
    low = lambda n, m: (shape((n, m), BF16), ANY)
    parted = lambda n: (shape((PARTS, n, PART), BF16), ANY)
    by_part = lambda n: pltpu.VMEM((PARTS, n, PART), BF16)

    (masks, par, gains, gates, coef, scale_one, scale_two, y, n1, q, x_own, g, b, p, u, r, i, h, result, dn2, _, _, f_own, f_got, fd_own, fd_got,
     br_n, m_n) = call(
        functools.partial(forward_kernel, width, EPS),
        [ANY] * 2 + [VM] * 4 + [ANY] * 6,
        [(shape((8, seq + 128), F32), VM), (shape((chan, 16), F32), VM), (shape((block, 16), F32), VM), (shape((2, lru, 2 * lru), BF16), VM),
         (f_tok(8), VM), (f_tok(8), VM), (f_tok(8), VM), (f_tok(block), ANY), parted(width), low(chan, seq), low(block, seq), parted(block)]
        + state + [low(half, tokens), (f_tok(block), ANY), low(2 * hid, seq), low(hid, seq), grad_gu, grad_gu, grad_d, grad_d,
                   low(width, 2 * chan), low(chan, width)],
        [pltpu.VMEM((LINE, 8, seq), F32), pltpu.VMEM((PARTS, LINE, 8, PART), F32), pltpu.VMEM((PARTS, LINE, 8, PART), F32),
         pltpu.VMEM((2, 16, lru), F32), pltpu.VMEM((2, 2) + retain_weight.shape, F32), pltpu.VMEM((2, 2 * lru, lru), BF16),
         pltpu.VMEM((2, 2 * lru, lru), BF16), by_part(width), by_part(width),
         by_part(width), tok(block, BF16), tok(block), one(block), one(chan, BF16),
         one(chan, F32, 128), one(chan, F32, 128), one(max(5 * chan, 3 * hid)), one(chan, BF16), one(chan, BF16),
         own_low, held, held, held, pltpu.VMEM((2 * hid, width), BF16), pltpu.VMEM((width, 2 * hid), BF16),
         pltpu.VMEM((hid, width), BF16), pltpu.VMEM((width, hid), BF16), one(hid, BF16), one(2 * hid, BF16),
         DMA((5,)), DMA((5,)), DMA((5,)), DMA((PARTS,)), DMA((PARTS,)), DMA((PARTS,))] + line + [DMA((PARTS, 3)), DMA((PARTS, 3))] * 2 + steps * 3 + sums * 3
        + [DMA((7, 7)), DMA((7, 7)), DMA((7,)), DMA((7,)), DMA((7,)), DMA((4,)), DMA((4,)), DMA((4,))],
        0, "forward", 50 * 10**9,
    )(inputs, cotangent, segments[None, :], vec, retain_weight, admit_weight, br_s, m_s, gu_s, down_weight,
      br_t, merge_weight)

    pair = lambda lead=0: pltpu.VMEM((2, chan, lead + PART), F32)
    land = lambda n, m: ((shape((n, m), BF16), ANY), (shape((3, n, m), BF16), ANY))
    input_grad, tiny_v, tiny_g, *sums_of = call(
        functools.partial(back_kernel, width),
        [VM] + [ANY] * 2 + [VM] * 8 + [ANY] * 14,
        [(shape((half, tokens), F32), ANY), (shape((2, 8, chan), F32), VM),
         (shape((lru, 128), F32), VM), *land(cols, 2 * ff), *land(ff, cols), *land(cols, 2 * lru), *land(lru, cols)],
        [pltpu.VMEM((PARTS, LINE, 8, PART), F32), pltpu.VMEM((8, seq), F32),
         pltpu.VMEM((chan, width), BF16), pltpu.VMEM((width, 2 * chan), BF16),
         pair(), pair(128), pair(), pair(), pair(), pair(128), by_part(width), tok(2 * chan, BF16),
         tok(block), tok(block), pltpu.VMEM((chan, PART), F32), pltpu.VMEM((chan, PART + 128), F32), pltpu.VMEM((2 * chan, PART), BF16),
         pltpu.VMEM((chan, PART), F32), pltpu.VMEM((chan, PART), F32), pltpu.VMEM((chan, 128), F32), own_low, held,
         tok(chan, BF16), pltpu.VMEM((4, cols, 2 * ff), BF16), pltpu.VMEM((cols, 2 * ff), BF16),
         pltpu.VMEM((4, ff, cols), BF16), pltpu.VMEM((ff, cols), BF16),
         pltpu.VMEM((block, 128), F32), pltpu.VMEM((block, 128), F32), pltpu.VMEM((8, chan, 128), F32),
         pltpu.VMEM((2, lru, 2 * lru), F32), by_part(block), pltpu.VMEM((width, 2 * lru), BF16),
         pltpu.VMEM((lru, width), BF16), pltpu.VMEM((2, 8, chan), F32), pltpu.VMEM((2, 8, chan), F32),
         pltpu.VMEM((4, 2, 8, chan), F32), pltpu.VMEM((2, lru, 128), F32), pltpu.VMEM((lru, 128), F32),
         pltpu.VMEM((4, lru, 128), F32), DMA((7,)), DMA((6, 2))] + [DMA((PARTS, 3)), DMA((PARTS, 3))] + steps + sums
        + [DMA, DMA, DMA((2, 2)), DMA((2, PARTS)), DMA((2, PARTS)), DMA((2,)), DMA((2,)), DMA((4,))]
        + [DMA((2, 3)), DMA((2, 3)), DMA((2, 3)), DMA((2, 3)), DMA((2,)), DMA((2,))],
        2, "mix_backward", 10 * 10**9,
    )(y, dn2, g, x_own, scale_two, scale_one, coef, gains, masks, par, gates, m_n, br_n, b, p, u, r, i, h,
      q, n1, f_own, f_got, fd_own, fd_got)

    line_of = shape((1, lru), F32)
    s_b, s_r, s_m, s_g, s_u, s_d, taps, offs, bias_r, bias_a, decay, mix, feed, retain, admit = pl.pallas_call(
        last_kernel,
        out_shape=[shape((cols, lru), F32)] * 2 + [shape((lru, cols), F32)] + [shape((cols, ff), F32)] * 2
        + [shape((ff, cols), F32), shape((4, lru), F32)] + [line_of] * 4 + [shape((1, half), F32)] * 2
        + [shape((heads, 64, 64), F32)] * 2,
        in_specs=[VM] * 11,
        out_specs=[VM] * 15,
        name="last_sums",
        compiler_params=pltpu.CompilerParams(vmem_limit_bytes=ROOM),
    )(*sums_of, tiny_v, tiny_g, lambdas[None, :])
    return (
        result,
        input_grad,
        mix[0],
        s_b,
        s_r,
        taps,
        offs[0],
        retain,
        bias_r[0],
        admit,
        bias_a[0],
        decay[0],
        s_m,
        feed[0],
        s_g,
        s_u,
        s_d,
    )


def suits(mesh, args):
    return (
        dict(mesh.shape) == {"row": 4, "col": 8}
        and args[0].shape == (D, 8 * SEQ)
        and args[3].shape == (D, 2048)
        and args[14].shape == (D, 4608)
        and args[7].shape == (32, 64, 64)
    )


def solution(mesh):
    in_specs = (
        P("col", "row"),
        P("row"),
        P("col"),
        P("row", "col"),
        P("row", "col"),
        P(None, "col"),
        P("col"),
        P("col", None, None),
        P("col"),
        P("col", None, None),
        P("col"),
        P("col"),
        P("col", "row"),
        P("col"),
        P("row", "col"),
        P("row", "col"),
        P("col", "row"),
        P("col", "row"),
    )
    out_specs = (
        P("col", "row"),
        P("col", "row"),
        P("col"),
        P("row", "col"),
        P("row", "col"),
        P(None, "col"),
        P("col"),
        P("col", None, None),
        P("col"),
        P("col", None, None),
        P("col"),
        P("col"),
        P("col", "row"),
        P("col"),
        P("row", "col"),
        P("row", "col"),
        P("col", "row"),
    )
    def run(*args):
        chosen = fast_body if suits(mesh, args) else body
        return jax.shard_map(
            chosen, mesh=mesh, in_specs=in_specs, out_specs=out_specs, check_vma=False
        )(*args)

    return run
```

```python
import functools

import jax
import jax.numpy as jnp
from jax import lax
from jax.experimental import pallas as pl
from jax.experimental.pallas import tpu as pltpu
from jax.sharding import PartitionSpec as P

D = 1536
SEQ = 1024
MICRO = 2


HIGH = lax.Precision.HIGHEST
EPS = 1e-06
POWER = 8.0
FLOOR = 0.01


def combine(earlier, later):
    first_a, first_b = earlier
    second_a, second_b = later
    return (first_a * second_a, second_a * first_b + second_b)


def mixer(
    branch_pre,
    lru_pre,
    segs,
    kernel,
    offsets,
    retain_weight,
    retain_bias,
    admit_weight,
    admit_bias,
    lambdas,
):
    length = lru_pre.shape[0]
    channels = lru_pre.shape[1]
    conv = offsets + kernel[0] * lru_pre
    for lag in range(1, kernel.shape[0]):
        shifted = jnp.concatenate(
            [jnp.zeros((lag, channels), lru_pre.dtype), lru_pre[:-lag]], axis=0
        )
        prior = jnp.concatenate([jnp.full((lag,), -1, jnp.int32), segs[:-lag]])
        keep = (prior == segs).astype(lru_pre.dtype)
        conv = conv + kernel[lag] * shifted * keep[:, None]
    heads = retain_weight.shape[0]
    blocks = conv.reshape(length, heads, channels // heads)
    retain = jax.nn.sigmoid(
        jnp.einsum("thi,hij->thj", blocks, retain_weight, precision=HIGH).reshape(length, channels)
        + retain_bias
    )
    admit = jax.nn.sigmoid(
        jnp.einsum("thi,hij->thj", blocks, admit_weight, precision=HIGH).reshape(length, channels)
        + admit_bias
    )
    decay = jnp.exp(-POWER * retain * jax.nn.softplus(-lambdas))
    factor = jnp.sqrt(1.0 - decay * decay + FLOOR)
    starts = jnp.concatenate([jnp.ones((1,), bool), segs[1:] != segs[:-1]])
    decay = jnp.where(starts[:, None], 0.0, decay)
    factor = jnp.where(starts[:, None], 1.0, factor)
    _, state = lax.associative_scan(combine, (decay, factor * admit * conv), axis=0)
    return jax.nn.gelu(branch_pre) * state


def geglu(gate, upper):
    return jax.nn.gelu(gate) * upper


def contract_rows(left, right):
    return lax.dot_general(
        left, right, (((0,), (0,)), ((), ())), preferred_element_type=jnp.float32
    )


def contract_cols(left, right):
    return lax.dot_general(
        left, right, (((1,), (1,)), ((), ())), preferred_element_type=jnp.float32
    )


def contract_cross(left, right):
    return lax.dot_general(
        left, right, (((0,), (1,)), ((), ())), preferred_element_type=jnp.float32
    )


def norm_forward(resid, gain):
    total = lax.psum(jnp.sum(resid * resid, axis=0), "col")
    scale = lax.rsqrt(total / D + EPS)[None, :]
    return (scale, (resid * scale * gain[:, None]).astype(jnp.bfloat16))


def norm_backward(resid, scale, gain, grad_normed):
    weighted = grad_normed * gain[:, None]
    total = lax.psum(jnp.sum(weighted * resid, axis=0), "col")
    grad_resid = scale * weighted - resid * (scale * scale * scale) * (total / D)[None, :]
    grad_gain = jnp.sum(grad_normed * resid * scale, axis=1)
    return (grad_resid, grad_gain)


def gather_features(normed):
    return lax.all_gather(normed, "col", axis=0, tiled=True)


def gather_cotangent(grad):
    return lax.all_gather(grad, "col", axis=0, tiled=True)


def spread_sum(term):
    return lax.psum_scatter(
        term.astype(jnp.bfloat16), "col", scatter_dimension=0, tiled=True
    ).astype(jnp.float32)


def back_sum(term):
    return spread_sum(term)


def merge_term(whole_merge, mixed_low):
    return spread_sum(contract_cross(whole_merge, mixed_low))


def weight_grads(normed, grad_joined):
    return jnp.dot(
        normed,
        grad_joined,
        preferred_element_type=jnp.float32,
    )


def row_sum(total, axis):
    return lax.psum_scatter(
        total.astype(jnp.bfloat16), "row", scatter_dimension=axis, tiled=True
    ).astype(jnp.float32)


def body(
    inputs,
    segments,
    mix_gain,
    branch_weight,
    recur_weight,
    kernel,
    offsets,
    retain_weight,
    retain_bias,
    admit_weight,
    admit_bias,
    lambdas,
    merge_weight,
    feed_gain,
    gate_weight,
    up_weight,
    down_weight,
    cotangent,
):
    lru_cols = branch_weight.shape[1]
    feed_cols = gate_weight.shape[1]
    mixer_params = (kernel, offsets, retain_weight, retain_bias, admit_weight, admit_bias, lambdas)
    acc_branch = jnp.zeros((D, lru_cols), jnp.float32)
    acc_recur = jnp.zeros((D, lru_cols), jnp.float32)
    acc_gate = jnp.zeros((D, feed_cols), jnp.float32)
    acc_up = jnp.zeros((D, feed_cols), jnp.float32)
    acc_merge = jnp.zeros((lru_cols, D), jnp.float32)
    acc_down = jnp.zeros((feed_cols, D), jnp.float32)
    acc_small = tuple((jnp.zeros_like(p) for p in mixer_params))
    acc_mix = jnp.zeros_like(mix_gain)
    acc_feed = jnp.zeros_like(feed_gain)
    outputs = []
    in_grads = []
    for batch in range(MICRO):
        lower = batch * SEQ
        resid_in = inputs[:, lower : lower + SEQ].astype(jnp.float32)
        grad_out = cotangent[:, lower : lower + SEQ].astype(jnp.float32)
        segs = segments[lower : lower + SEQ]
        whole_branch, whole_recur, whole_gate, whole_up = (
            lax.all_gather(branch_weight, "row", axis=0, tiled=True),
            lax.all_gather(recur_weight, "row", axis=0, tiled=True),
            lax.all_gather(gate_weight, "row", axis=0, tiled=True),
            lax.all_gather(up_weight, "row", axis=0, tiled=True),
        )
        whole_merge, whole_down = (
            lax.all_gather(merge_weight, "row", axis=1, tiled=True),
            lax.all_gather(down_weight, "row", axis=1, tiled=True),
        )
        scale_one, normed_one = norm_forward(resid_in, mix_gain)
        full_one = gather_features(normed_one)
        branch_pre = contract_rows(full_one, whole_branch)
        lru_pre = contract_rows(full_one, whole_recur)

        def local_mixer(bpre, lpre, kern, offs, rweight, rbias, aweight, abias, lams):
            return mixer(bpre, lpre, segs, kern, offs, rweight, rbias, aweight, abias, lams)

        mixed, mixer_pull = jax.vjp(local_mixer, branch_pre, lru_pre, *mixer_params)
        mixed_low = mixed.astype(jnp.bfloat16)
        resid_mid = resid_in + merge_term(whole_merge, mixed_low)
        scale_two, normed_two = norm_forward(resid_mid, feed_gain)
        full_two = gather_features(normed_two)
        gate = contract_rows(full_two, whole_gate)
        upper = contract_rows(full_two, whole_up)
        hidden, geglu_pull = jax.vjp(geglu, gate, upper)
        hidden_low = hidden.astype(jnp.bfloat16)
        result = resid_mid + spread_sum(contract_cross(whole_down, hidden_low))
        outputs.append(result.astype(jnp.bfloat16))
        grad_full = gather_cotangent(grad_out.astype(jnp.bfloat16))
        acc_down = acc_down + contract_cross(hidden_low, grad_full)
        grad_gate, grad_upper = geglu_pull(contract_cross(grad_full, whole_down))
        grad_gate = grad_gate.astype(jnp.bfloat16)
        grad_upper = grad_upper.astype(jnp.bfloat16)
        feed_joined = weight_grads(full_two, jnp.concatenate([grad_gate, grad_upper], axis=1))
        acc_gate = acc_gate + feed_joined[:, :feed_cols]
        acc_up = acc_up + feed_joined[:, feed_cols:]
        grad_normed_two = back_sum(
            contract_cols(whole_gate, grad_gate) + contract_cols(whole_up, grad_upper)
        )
        grad_mid_norm, feed_part = norm_backward(resid_mid, scale_two, feed_gain, grad_normed_two)
        acc_feed = acc_feed + feed_part
        grad_mid = grad_out + grad_mid_norm
        grad_mid_full = gather_cotangent(grad_mid.astype(jnp.bfloat16))
        acc_merge = acc_merge + contract_cross(mixed_low, grad_mid_full)
        pulled = mixer_pull(contract_cross(grad_mid_full, whole_merge))
        grad_branch = pulled[0].astype(jnp.bfloat16)
        grad_lru = pulled[1].astype(jnp.bfloat16)
        acc_small = tuple((total + part for total, part in zip(acc_small, pulled[2:])))
        branch_joined = weight_grads(full_one, jnp.concatenate([grad_branch, grad_lru], axis=1))
        acc_branch = acc_branch + branch_joined[:, :lru_cols]
        acc_recur = acc_recur + branch_joined[:, lru_cols:]
        grad_normed_one = back_sum(
            contract_cols(whole_branch, grad_branch) + contract_cols(whole_recur, grad_lru)
        )
        grad_in_norm, mix_part = norm_backward(resid_in, scale_one, mix_gain, grad_normed_one)
        acc_mix = acc_mix + mix_part
        in_grads.append(grad_mid + grad_in_norm)
    sum_branch, sum_recur, sum_gate, sum_up = (
        row_sum(acc_branch, 0),
        row_sum(acc_recur, 0),
        row_sum(acc_gate, 0),
        row_sum(acc_up, 0),
    )
    sum_merge, sum_down = (
        row_sum(acc_merge, 1),
        row_sum(acc_down, 1),
    )
    summed = lax.psum(
        (
            acc_mix,
            acc_feed,
            acc_small[0],
            acc_small[1],
            acc_small[2],
            acc_small[3],
            acc_small[4],
            acc_small[5],
            acc_small[6],
        ),
        "row",
    )
    result_all = jnp.concatenate(outputs, axis=1)
    input_grad = jnp.concatenate(in_grads, axis=1)
    return (
        result_all,
        input_grad,
        summed[0],
        sum_branch,
        sum_recur,
        summed[2],
        summed[3],
        summed[4],
        summed[5],
        summed[6],
        summed[7],
        summed[8],
        sum_merge,
        summed[1],
        sum_gate,
        sum_up,
        sum_down,
    )


MESH = pl.DeviceIdType.MESH
F32 = jnp.float32
BF16 = jnp.bfloat16
LINE = 4
PART = 128
PARTS = 8
LATE = 256
GELU_A = 0.7978845608028654
GELU_B = 0.044715


def place():
    row, col = lax.axis_index("row"), lax.axis_index("col")
    return row, col // 2, col % 2


def at_line(z, core):
    return {"col": 2 * z + core}


def lanes(part):
    return pl.ds(pl.multiple_of(part * PART, PART), PART)


def rows_of(index, size):
    return pl.ds(pl.multiple_of(index * size, 16), size)


def dot(a, b):
    return lax.dot_general(a, b, (((1,), (0,)), ((), ())), preferred_element_type=F32)


def dot_nt(a, b):
    return lax.dot_general(a, b, (((1,), (1,)), ((), ())), preferred_element_type=F32)


def greet(row, z, core, rows, line):
    barrier = pltpu.get_barrier_semaphore()
    peers = [{"col": 2 * z + (1 - core)}]
    if rows:
        peers += [{"row": row ^ d} for d in (1, 2, 3)]
    if line:
        peers += [at_line(z ^ d, core) for d in (1, 2, 3)]
    for peer in peers:
        pl.semaphore_signal(barrier, inc=1, device_id=peer, device_id_type=MESH)
    pl.semaphore_wait(barrier, len(peers))


def remote(src, dst, send, recv, peer):
    return pltpu.make_async_remote_copy(
        src_ref=src, dst_ref=dst, send_sem=send, recv_sem=recv, device_id=peer, device_id_type=MESH
    )


class Gather:
    def __init__(self, ref, send, recv, z, core, block, back=False):
        self.parts = ref.shape[0]
        self.ref, self.sems, self.z, self.core = ref, (send, recv), z, core
        self.block, self.back = block, back

    def copy(self, way, hop, step, owner, incoming=False):
        part = self.parts - 1 - step if self.back else step
        piece = self.ref.at[part, rows_of(owner, self.block), :]
        peer = at_line(self.z + (1 if (way == 0) != incoming else -1), self.core)
        return remote(piece, piece, self.sems[0].at[way, hop, step], self.sems[1].at[way, hop, step], peer)

    def each(self, hop, act, incoming):
        z = self.z
        if incoming:
            cases = ((0, z - 1 - hop >= 0, z - 1 - hop), (1, z + 1 + hop < LINE, z + 1 + hop))
        else:
            cases = (
                (0, (z >= hop) & (z < LINE - 1), z - hop),
                (1, (z + hop < LINE) & (z >= 1), z + hop),
            )
        for way, here, owner in cases:
            pl.when(here)(functools.partial(act, way, owner))

    def send(self, hop, step):
        self.each(hop, lambda way, owner: self.copy(way, hop, step, owner).start(), False)

    def arrive(self, hop, step):
        self.each(hop, lambda way, owner: self.copy(way, hop, step, owner, True).wait_recv(), True)

    def forward(self, hop, step):
        self.arrive(hop - 1, step)
        self.send(hop, step)

    def sent(self):
        def one(step, carry):
            for hop in range(LINE - 1):
                self.each(hop, lambda way, owner: self.copy(way, hop, step, owner).wait_send(), False)
            return carry

        lax.fori_loop(0, self.parts, one, 0)

    def middle(self, step, ahead=1):
        for hop in (2, 1, 0):
            later = step + ahead + 2 - hop
            act = self.forward if hop else self.send
            pl.when(later < self.parts)(functools.partial(act, hop, later))


class Spread:
    def __init__(self, own, held, send, recv, z, core):
        self.parts = held.shape[0]
        self.own, self.held, self.sems, self.z, self.core = own, held, (send, recv), z, core

    def copy(self, way, step, hop):
        slot = hop if way == 0 else LINE - hop
        there = slot - 1 if way == 0 else slot + 1
        peer = at_line(self.z + (1 if way == 0 else -1), self.core)
        return remote(
            self.held.at[step, slot],
            self.held.at[step, there],
            self.sems[0].at[way, step, hop],
            self.sems[1].at[way, step, hop - 1],
            peer,
        )

    def landed(self, way, step, hop):
        slot = hop if way == 0 else LINE - hop
        piece = self.held.at[step, slot]
        peer = at_line(self.z + (-1 if way == 0 else 1), self.core)
        remote(piece, piece, self.sems[0].at[way, step, hop], self.sems[1].at[way, step, hop], peer).wait_recv()

    def push(self, way, step, first):
        z = self.z

        def one(i, carry):
            hop = LINE - 1 - i
            owner = z + hop if way == 0 else z - hop
            slot = hop if way == 0 else LINE - hop

            @pl.when((owner >= 0) & (owner < LINE))
            def _():
                @pl.when(first)
                def _():
                    self.held[step, slot] = self.own(step, owner)[...].astype(BF16)

                @pl.when(jnp.logical_not(first))
                def _():
                    self.landed(way, step, hop)
                    total = self.own(step, owner)[...].astype(F32) + self.held[step, slot].astype(F32)
                    self.held[step, slot] = total.astype(BF16)

                self.copy(way, step, hop).start()

            return carry

        lax.fori_loop(0, LINE - 1, one, 0)

    def serve(self, t, finish):
        z = self.z
        step = t - (LINE - 1)

        @pl.when((step >= 0) & (step < self.parts))
        def _():
            @pl.when(z == 0)
            def _():
                self.landed(1, step, 0)
                finish(step, lambda a, n: self.mine(step, a, n) + self.got(step, LINE, a, n))

            @pl.when(z == LINE - 1)
            def _():
                self.landed(0, step, 0)
                finish(step, lambda a, n: self.mine(step, a, n) + self.got(step, 0, a, n))

            @pl.when((z > 0) & (z < LINE - 1))
            def _():
                self.landed(0, step, 0)
                self.landed(1, step, 0)
                finish(
                    step,
                    lambda a, n: self.mine(step, a, n) + (self.got(step, 0, a, n) + self.got(step, LINE, a, n)),
                )

        for way, late, turn in ((1, LINE - 1 - z, z < 2), (0, z, z >= 0), (1, LINE - 1 - z, z >= 2)):
            step = t - late
            pl.when((step >= 0) & (step < self.parts) & turn)(functools.partial(self.push, way, step, late == 0))

    def mine(self, step, start, size):
        return self.own(step, self.z)[pl.ds(start, size), :].astype(F32)

    def got(self, step, slot, start, size):
        return self.held[step, slot, pl.ds(start, size)].astype(F32)

    def sent(self):
        z = self.z

        def one(step, carry):
            for way in (0, 1):
                for hop in range(1, LINE):
                    owner = z + hop if way == 0 else z - hop

                    @pl.when((owner >= 0) & (owner < LINE))
                    def _():
                        self.copy(way, step, hop).wait_send()

            return carry

        lax.fori_loop(0, self.parts, one, 0)


def share_line(ref, send, recv, z, core):
    copies = [
        remote(ref.at[z], ref.at[z], send.at[d - 1], recv.at[d - 1], at_line(z ^ d, core)) for d in (1, 2, 3)
    ]
    for copy in copies:
        copy.start()
    for d in (1, 2, 3):
        piece = ref.at[z ^ d]
        remote(piece, piece, send.at[d - 1], recv.at[d - 1], at_line(z ^ d, core)).wait_recv()
    for copy in copies:
        copy.wait_send()


class Weights:
    def __init__(self, src, dst, send, recv, own, row, z, core, turned, stride=0, start=0):
        self.src, self.dst, self.send, self.recv, self.own = src, dst, send, recv, own
        self.row, self.core, self.turned = row, core, turned
        self.stride, self.first = stride or src.shape[0], start
        self.sibling = {"col": 2 * z + (1 - core)}

    def spot(self, row, core):
        down, right = (row, core) if self.turned else (core, row)
        rows, cols = self.src.shape
        at = pl.ds(pl.multiple_of(down * self.stride + self.first, 16), rows)
        return self.dst.at[at, pl.ds(pl.multiple_of(right * cols, 128), cols)]

    def to_row(self, d):
        return remote(
            self.src, self.spot(self.row, self.core), self.send.at[d], self.recv.at[d], {"row": self.row ^ d}
        )

    def to_sibling(self, d):
        if d == 0:
            return remote(
                self.src, self.spot(self.row, self.core), self.send.at[0], self.recv.at[0], self.sibling
            )
        piece = self.spot(self.row ^ d, self.core)
        return remote(piece, piece, self.send.at[3 + d], self.recv.at[3 + d], self.sibling)

    def local(self):
        return pltpu.make_async_copy(self.src, self.spot(self.row, self.core), self.own)

    def start(self):
        for d in (1, 2, 3):
            self.to_row(d).start()
        self.to_sibling(0).start()
        self.local().start()

    def forward(self):
        for d in (1, 2, 3):
            piece = self.spot(self.row ^ d, self.core)
            remote(piece, piece, self.send.at[d], self.recv.at[d], {"row": self.row ^ d}).wait_recv()
            self.to_sibling(d).start()

    def finish(self):
        self.local().wait()
        for d in (0, 1, 2, 3):
            piece = self.spot(self.row ^ d, 1 - self.core)
            sem = 0 if d == 0 else 3 + d
            remote(piece, piece, self.send.at[sem], self.recv.at[sem], self.sibling).wait_recv()

    def sent(self):
        for d in (1, 2, 3):
            self.to_row(d).wait_send()
            self.to_sibling(d).wait_send()
        self.to_sibling(0).wait_send()


def gelu_parts(b):
    t = jnp.tanh(GELU_A * (b + GELU_B * (b * b * b)))
    half = 0.5 + 0.5 * t
    slope = half + (0.5 * b) * (1.0 - t * t) * (GELU_A + (3.0 * GELU_A * GELU_B) * (b * b))
    return b * half, slope


def eight(v):
    return jnp.sum(v.reshape(v.shape[0] // 8, 8, v.shape[1]), axis=0)


def fold(v):
    total = v[:, 0:128]
    for j in range(1, v.shape[1] // 128):
        total = total + v[:, j * 128 : (j + 1) * 128]
    return total


def tokens_of(ref, piece):
    return jnp.concatenate([ref[k, piece, :] for k in range(ref.shape[0])], axis=1)


def blocks(count, body):
    def one(i, carry):
        body(i)
        return carry

    lax.fori_loop(0, count, one, 0)


def scale_of(ref, eps, width):
    total = jnp.sum(jnp.sum(ref[...], axis=0), axis=0, keepdims=True)
    return lax.rsqrt(total / width + eps)


def forward_kernel(
    width, eps,
    x_in, g_in, vec, retain, admit, br_s, m_s, gu_s, d_s, brn_s, mn_s,
    masks, par, gains, gates, coef, scale, scale_two, y_out, n1_out, q_out, x_out, g_out, b_out, p_out, u_out, r_out, i_out, h_out,
    result, dn2_out, dev_h, z_h, g_own, g_got, gd_own, gd_got, br_n, m_n,
    sums, sums2, sums3, vec_all, block_all, gates_hi, gates_lo, normed, normed2, go, x_own, y, dn2, q_c, p_s, h_s, room, uh, ul,
    own, held, held_n, held_o, gu, gun, down, dt, zs, dev,
    x_send, x_recv, x_loc, i_send, i_recv, i_loc, l_send, l_recv, n_send, n_recv, c_send, c_recv, g_send, g_recv, e_send, e_recv, f_send, f_recv,
    s_send, s_recv, t_send, t_recv, o_send, o_recv, w_send, w_recv, w_own, k_sem, v_sem, d_send, d_recv, d_own,
):
    row, z, core = place()
    block, seq = y.shape
    half = x_in.shape[0]
    chan = p_s.shape[0]
    hid = zs.shape[0]
    b_s, u_s, r_s, i_s, a_c = [room.at[n * chan : (n + 1) * chan, :] for n in range(5)]
    ev, dz = room.at[0 : 2 * hid, :], room.at[2 * hid : 3 * hid, :]
    hh = hid // 2
    hc = chan // 2
    sibling = {"col": 2 * z + (1 - core)}
    greet(row, z, core, True, True)
    br, mt = gun.at[0 : 2 * chan, 0:width], dt.at[:, 0:chan]
    wide = br_s.shape[0]
    recur_s, branch_s = br_s.at[wide // 2 :, :], br_s.at[0 : wide // 2, :]
    weights = [
        Weights(src, dst, w_send.at[n], w_recv.at[n], w_own.at[n], row, z, core, n in (2, 5), stride, start)
        for n, (src, dst, stride, start) in enumerate(
            (
                (recur_s, br, hc, 0),
                (branch_s, br, hc, chan),
                (m_s, mt, 0, 0),
                (gu_s, gu, 0, 0),
                (d_s, down, 0, 0),
                (brn_s, br_n, 0, 0),
                (mn_s, m_n, 0, 0),
            )
        )
    ]
    mine = pl.ds(pl.multiple_of(core * seq, seq), seq)
    other = pl.ds(pl.multiple_of((1 - core) * seq, seq), seq)
    inner = pl.ds(pl.multiple_of(z * block + core * half, 16), half)
    outer = rows_of(core, half)
    swaps = [
        remote(x_in.at[:, other], x_own.at[outer, :], x_send.at[0], x_recv.at[0], sibling),
        pltpu.make_async_copy(x_in.at[:, mine], x_own.at[outer, :], x_loc.at[0]),
    ]
    for k in range(PARTS):
        theirs, ours = [pl.ds(pl.multiple_of(c * seq + k * PART, 128), PART) for c in (1 - core, core)]
        swaps.append(remote(g_in.at[:, theirs], go.at[k, inner, :], i_send.at[k], i_recv.at[k], sibling))
        swaps.append(pltpu.make_async_copy(g_in.at[:, ours], go.at[k, inner, :], i_loc.at[k]))
    trades = []
    for n, (src, dst) in enumerate(
        ((vec.at[0:16, :], vec_all.at[core]), (retain, block_all.at[core, 0]), (admit, block_all.at[core, 1]))
    ):
        trades.append(remote(src, dst, x_send.at[2 + n], x_recv.at[2 + n], sibling))
        trades.append(pltpu.make_async_copy(src, dst, x_loc.at[2 + n]))
    for swap in swaps + trades:
        swap.start()
    for w in weights[:3]:
        w.start()
    for swap in swaps + trades:
        swap.wait()
    flushes = [
        pltpu.make_async_copy(x_own, x_out, v_sem.at[0]),
        pltpu.make_async_copy(go.at[:, rows_of(z, block), :], g_out, v_sem.at[1]),
    ]
    for flush in flushes:
        flush.start()
    gather = Gather(normed, g_send, g_recv, z, core, block)
    gather_go = Gather(go, e_send, e_recv, z, core, block)
    gather_two = Gather(normed2, f_send, f_recv, z, core, block)
    shares = lambda k, s: own.at[k, s]
    shares_o = lambda k, s: normed.at[k, rows_of(s, block), :]
    spread = Spread(shares, held, s_send, s_recv, z, core)
    spread_n = Spread(shares, held_n, t_send, t_recv, z, core)
    spread_o = Spread(shares_o, held_o, o_send, o_recv, z, core)
    res = x_own
    gather_go.send(0, 0)
    gather_go.send(0, 1)
    for c in (0, 1):
        at = slice(c * hc, (c + 1) * hc)
        rate = -vec_all[c, 7:8, :]
        vec_all[c, 7:8, :] = 8.0 * (jnp.maximum(rate, 0.0) + jnp.log1p(jnp.exp(-jnp.abs(rate))))
        par[at, :] = vec_all[c].T
        gains[c * half : (c + 1) * half, :] = par[c * hc : c * hc + half, :]

    sums[z] = jnp.zeros(sums.shape[1:], F32)

    def squares(i):
        v = x_own[rows_of(i, 16), :].astype(F32)
        v = v * v
        sums[z] += v[:8] + v[8:]

    blocks(block // 16, squares)
    share_line(sums, l_send, l_recv, z, core)
    scale[...] = jnp.broadcast_to(scale_of(sums, eps, width), scale.shape)

    def norm(i):
        v = x_own[rows_of(i, 16), :].astype(F32) * scale[0:1, :] * gains[rows_of(i, 16), 8:9]
        v = v.astype(BF16)
        for k in range(PARTS):
            normed[k, pl.ds(pl.multiple_of(z * block + i * 16, 16), 16), :] = v[:, k * PART : (k + 1) * PART]

    blocks(block // 16, norm)
    gather.send(0, 0)
    gather.send(0, 1)
    p_s[:, PART:] = jnp.zeros((chan, 128), F32)
    h_s[:, PART:] = jnp.zeros((chan, 128), F32)
    pads = [
        pltpu.make_async_copy(src.at[:, PART:], out.at[:, 0:128], v_sem.at[2 + n])
        for n, (src, out) in enumerate(((p_s, p_out), (h_s, h_out)))
    ]
    for pad in pads:
        pad.start()
    gates[...] = jnp.zeros(gates.shape, BF16)
    gates_hi[...] = jnp.zeros(gates_hi.shape, BF16)
    gates_lo[...] = jnp.zeros(gates_lo.shape, BF16)
    per = retain.shape[0]
    tap = retain.shape[1]
    for c in (0, 1):
        for n in (0, 1):
            for e in range(per):
                w = block_all[c, n, e]
                at, far = slice(e * tap, (e + 1) * tap), slice(n * hc + e * tap, n * hc + (e + 1) * tap)
                gates[c, at, far] = w.astype(BF16)
                w = w.T
                high = w.astype(BF16)
                gates_hi[c, far, at] = high
                gates_lo[c, far, at] = (w - high.astype(F32)).astype(BF16)
    masks[...] = jnp.zeros(masks.shape, F32)
    segs = [
        jnp.concatenate([vec[16 + c * 4 + j : 17 + c * 4 + j, :] for j in range(4)], axis=1) for c in (0, 1)
    ]
    here = jnp.broadcast_to(jnp.where(core == 0, segs[0], segs[1]), (8, seq))
    spot = lax.broadcasted_iota(jnp.int32, (8, seq), 1)
    for lag in (1, 2, 3):
        same = jnp.where((pltpu.roll(here, lag, 1) == here) & (spot >= lag), 1.0, 0.0)
        masks[lag : lag + 1, 0:seq] = same[0:1]
        if lag == 1:
            masks[0:1, 0:seq] = 1.0 - same[0:1]
    gather.forward(1, 0)
    gather.send(0, 2)
    gather_go.forward(1, 0)
    gather.forward(1, 1)
    gather.forward(2, 0)
    weights[0].forward()
    gather_go.forward(1, 1)
    gather_go.forward(2, 0)
    weights[1].forward()
    for w in weights[3:5]:
        w.start()
    gather_go.forward(2, 1)
    weights[0].finish()
    for pad in pads:
        pad.wait()

    kept = (b_s, p_s, u_s, r_s, i_s, h_s, q_c)
    outs = (b_out, p_out, u_out, r_out, i_out, h_out, q_out)

    def keep(n, part):
        if n in (1, 5):
            at = pl.ds(pl.multiple_of(128 + part * PART, 128), PART)
            return pltpu.make_async_copy(kept[n].at[:, 128:], outs[n].at[:, at], k_sem.at[n])
        return pltpu.make_async_copy(kept[n], outs[n].at[:, lanes(part)], k_sem.at[n])

    def put_shares(k, whole):
        for s in range(LINE):
            own[k, s] = whole[s * block : (s + 1) * block, :].astype(own.dtype)

    def work(k):
        here = lanes(k)

        @pl.when(k > 0)
        def _():
            for n in range(len(kept)):
                keep(n, k - 1).wait()

        p_s[:, 0:128] = p_s[:, PART:]
        h_s[:, 0:128] = h_s[:, PART:]
        p_s[:, 128:] = dot(br[0:chan, :], normed[k])

        def conv(i):
            ch = rows_of(i, 64)
            window = p_s[ch, :]
            pr = par[ch, :]
            u = pr[:, 4:5] + pr[:, 0:1] * window[:, 128:]
            for lag in (1, 2, 3):
                u = u + pr[:, lag : lag + 1] * (pltpu.roll(window, lag, 1)[:, 128:] * masks[lag : lag + 1, here])
            u_s[ch, :] = u
            high = u.astype(BF16)
            uh[ch, :] = high
            ul[ch, :] = (u - high.astype(F32)).astype(BF16)

        blocks(chan // 64, conv)
        gather.middle(k)
        for g in range(chan // 256):
            at = slice(g * 256, (g + 1) * 256)
            pre = dot(gates_hi[g], uh[at, :]) + dot(gates_hi[g], ul[at, :]) + dot(gates_lo[g], uh[at, :])
            r_s[at, :] = pre[:256]
            i_s[at, :] = pre[256:]

        def decay(i):
            ch = rows_of(i, 64)
            pr = par[ch, :]
            start = masks[0:1, here] > 0.5
            r = jax.nn.sigmoid(r_s[ch, :] + pr[:, 5:6])
            gate = jax.nn.sigmoid(i_s[ch, :] + pr[:, 6:7])
            r_s[ch, :] = r
            i_s[ch, :] = gate
            a = jnp.exp(-(r * pr[:, 7:8]))
            m = jnp.where(start, 1.0, jnp.sqrt(1.0 - a * a + FLOOR))
            a_c[ch, :] = jnp.where(start, 0.0, a)
            h_s[ch, 128:] = m * gate * u_s[ch, :]

        blocks(chan // 64, decay)
        first = lax.broadcasted_iota(jnp.int32, (128, PART), 1) == 0

        def recur(i):
            ch = rows_of(i, 128)
            a, h = a_c[ch, :], h_s[ch, 128:]
            h = h + jnp.where(first, a * h_s[ch, 0:128][:, 127:128], 0.0)
            a = jnp.where(first, 0.0, a)
            shift = 1
            while shift < PART:
                h = h + a * pltpu.roll(h, shift, 1)
                if shift * 2 < PART:
                    a = a * pltpu.roll(a, shift, 1)
                shift *= 2
            h_s[ch, 128:] = h

        blocks(chan // 128, recur)

        @pl.when(k == 0)
        def _():
            weights[2].forward()
            weights[1].finish()

        b_s[...] = dot(br[chan : 2 * chan, :], normed[k])

        def mixed(i):
            ch = rows_of(i, 64)
            b = b_s[ch, :]
            t = jnp.tanh(GELU_A * (b + GELU_B * (b * b * b)))
            q_c[ch, :] = (b * (0.5 + 0.5 * t) * h_s[ch, 128:]).astype(BF16)

        blocks(chan // 64, mixed)
        pl.when(k == 0)(weights[2].finish)
        put_shares(k, dot(mt[...], q_c[...]))
        for n in range(len(kept)):
            keep(n, k).start()

    def finish(k, total):
        def add(i):
            at = pl.multiple_of(i * 64, 64)
            y[pl.ds(at, 64), lanes(k)] = x_own[pl.ds(at, 64), lanes(k)].astype(F32) + total(at, 64)

        blocks(block // 64, add)

    def square(k):
        sums2[k, z] = jnp.zeros(sums2.shape[2:], F32)

        def one(i):
            v = y[rows_of(i, 64), lanes(k)]
            sums2[k, z] += eight(v * v)

        blocks(block // 64, one)
        for d in (1, 2, 3):
            share(k, d).start()

    def share(k, d):
        return remote(
            sums2.at[k, z], sums2.at[k, z], n_send.at[k, d - 1], n_recv.at[k, d - 1], at_line(z ^ d, core)
        )

    def norm_two(k):
        for d in (1, 2, 3):
            piece = sums2.at[k, z ^ d]
            remote(piece, piece, n_send.at[k, d - 1], n_recv.at[k, d - 1], at_line(z ^ d, core)).wait_recv()
        s2 = scale_of(sums2.at[k], eps, width)
        scale_two[:, lanes(k)] = jnp.broadcast_to(s2, (8, PART))

        def one(i):
            at = rows_of(i, 64)
            v = y[at, lanes(k)] * scale_two[0:1, lanes(k)] * gains[at, 9:10]
            normed2[k, pl.ds(pl.multiple_of(z * block + i * 64, 64), 64), :] = v.astype(BF16)

        blocks(block // 64, one)

    def turn_down(i):
        at = pl.ds(pl.multiple_of(i * 128, 128), 128)
        dt[:, at] = down[at, :].T

    def turn_up(i):
        at = pl.ds(pl.multiple_of(i * 128, 128), 128)
        gun[:, at] = gu[at, :].T

    def step(t, carry):
        gather.arrive(2, t)
        work(t)
        spread.serve(t, finish)
        pl.when(t >= 3)(lambda: square(t - 3))
        pl.when(t >= 4)(lambda: norm_two(t - 4))
        pl.when((t >= 4) & (t < 7))(lambda: gather_two.send(0, t - 4))
        pl.when((t >= 6) & (t < 8))(lambda: gather_two.forward(1, t - 6))
        pl.when(t == 5)(weights[3].forward)
        return carry

    lax.fori_loop(0, PARTS, step, 0)
    for w in weights[:3]:
        w.sent()
    for w in weights[5:]:
        w.start()
    for n in range(len(kept)):
        keep(n, PARTS - 1).wait()
    flush_n = pltpu.make_async_copy(normed, n1_out, v_sem.at[4])
    flush_n.start()
    gather_go.send(0, 2)
    gather_go.send(0, 3)
    spread.serve(PARTS, finish)
    square(PARTS - 3)
    norm_two(PARTS - 4)
    gather_two.forward(2, 0)
    weights[4].forward()
    spread.serve(PARTS + 1, finish)
    square(PARTS - 2)
    norm_two(PARTS - 3)
    gather_go.forward(1, 2)
    weights[4].finish()
    blocks(hid // 128, turn_down)
    spread.serve(PARTS + 2, finish)
    square(PARTS - 1)
    norm_two(PARTS - 2)
    gather.sent()
    for flush in flushes + [flush_n]:
        flush.wait()
    weights[3].finish()
    blocks(2 * hid // 128, turn_up)
    norm_two(PARTS - 1)

    def keep_dev(k):
        return pltpu.make_async_copy(dev, dev_h.at[:, lanes(k)], v_sem.at[5])

    def keep_z(k):
        return pltpu.make_async_copy(zs, z_h.at[:, lanes(k)], v_sem.at[6])

    def feed(k):

        @pl.when(k > 0)
        def _():
            keep_dev(k - 1).wait()
            keep_z(k - 1).wait()

        ev[...] = dot(gu[...], normed2[k])
        gather_two.middle(k)
        gather_go.middle(k, 2)
        gather_go.arrive(2, k)
        dz[...] = dot(down[...], go[k])
        for c in range(2):

            def one(i):
                off = pl.multiple_of(i * 64, 64)
                e = ev[pl.ds(c * 2 * hh + off, 64), :]
                v = ev[pl.ds(c * 2 * hh + hh + off, 64), :]
                d = dz[pl.ds(c * hh + off, 64), :]
                act, slope = gelu_parts(e)
                zs[pl.ds(c * hh + off, 64), :] = (act * v).astype(BF16)
                dev[pl.ds(c * 2 * hh + off, 64), :] = (d * v * slope).astype(BF16)
                dev[pl.ds(c * 2 * hh + hh + off, 64), :] = (d * act).astype(BF16)

            blocks(hh // 64, one)
        put_shares(k, dot(gun[...], dev[...]))
        spread_n.serve(k, finish_n)
        normed[k] = dot(dt[...], zs[...]).astype(BF16)
        spread_o.serve(k, finish_o)
        keep_dev(k).start()
        keep_z(k).start()

    def finish_o(k, total):
        def add(i):
            at = pl.multiple_of(i * 64, 64)
            res[pl.ds(at, 64), lanes(k)] = (y[pl.ds(at, 64), lanes(k)] + total(at, 64)).astype(BF16)

        blocks(block // 64, add)

    def keep_n(k):
        return pltpu.make_async_copy(dn2, dn2_out.at[:, lanes(k)], v_sem.at[3])

    def finish_n(k, total):
        @pl.when(k > 0)
        def _():
            keep_n(k - 1).wait()

        sums3[k, z] = jnp.zeros(sums3.shape[2:], F32)

        def add(i):
            at = pl.multiple_of(i * 64, 64)
            d = total(at, 64)
            dn2[pl.ds(at, 64), :] = d
            sums3[k, z] += eight(d * y[pl.ds(at, 64), lanes(k)] * gains[pl.ds(at, 64), 9:10])

        blocks(block // 64, add)
        keep_n(k).start()
        for d in (1, 2, 3):
            share_c(k, d).start()

    def share_c(k, d):
        return remote(
            sums3.at[k, z], sums3.at[k, z], c_send.at[k, d - 1], c_recv.at[k, d - 1], at_line(z ^ d, core)
        )

    def feed_step(t, carry):
        gather_two.arrive(2, t)
        feed(t)
        pl.when(t == 4)(weights[5].forward)
        pl.when(t == 6)(weights[6].forward)
        return carry

    lax.fori_loop(0, PARTS, feed_step, 0)
    for w in weights[3:5]:
        w.sent()
    keep_dev(PARTS - 1).wait()
    keep_z(PARTS - 1).wait()
    dev_all, z_all = gu.at[:, 0:seq], dt.at[0:hid, 0:seq]
    loads = [pltpu.make_async_copy(dev_h, dev_all, v_sem.at[5]), pltpu.make_async_copy(z_h, z_all, v_sem.at[6])]
    for load in loads:
        load.start()
    for load in loads:
        load.wait()

    def columns(start):
        return pl.ds(pl.multiple_of(start, 128), block)

    def place_up(j):
        side = jnp.where(j >= 3, core, 1 - core)
        return side * hid + (j % 3) * block, columns((j % 3) * block)

    def send_up(j):
        at, to = place_up(j)
        return remote(gun.at[:, columns(at)], g_got.at[:, to], d_send.at[j], d_recv.at[j], sibling)

    def keep_up(j):
        at, to = place_up(j)
        return pltpu.make_async_copy(gun.at[:, columns(at)], g_own.at[:, to], d_own.at[j - 3])

    def send_down():
        return remote(down.at[rows_of(1 - core, hh), :], gd_got, d_send.at[3], d_recv.at[3], sibling)

    def keep_down():
        return pltpu.make_async_copy(down.at[rows_of(core, hh), :], gd_own, d_own.at[3])

    def grad_up(j):
        at = place_up(j)[0]
        right = pl.ds(pl.multiple_of(at, 16), block)
        for low in (0, width // 2):
            piece = slice(low, low + width // 2)
            gun[piece, columns(at)] = dot_nt(tokens_of(normed2, piece), dev_all[right, :]).astype(BF16)

        @pl.when(j < 3)
        def _():
            send_up(j).start()

        @pl.when(j >= 3)
        def _():
            keep_up(j).start()

    def grad_down(side):
        at = rows_of(side, hh)
        for low in range(0, width, 2 * block):
            piece = slice(low, low + 2 * block)
            down[at, piece] = dot_nt(z_all[at, :], tokens_of(go, piece)).astype(BF16)

    def drain(i, carry):
        t = PARTS + i
        blocks(2, lambda j: grad_up(2 * i + j))
        spread_n.serve(t, finish_n)
        spread_o.serve(t, finish_o)

        @pl.when(i < 2)
        def _():
            grad_down(jnp.where(i == 0, 1 - core, core))

        pl.when(i == 0)(lambda: send_down().start())
        pl.when(i == 1)(lambda: keep_down().start())
        return carry

    lax.fori_loop(0, LINE - 1, drain, 0)
    last = [
        remote(res.at[rows_of(1 - core, half), :], result.at[:, mine], x_send.at[0], x_recv.at[0], sibling),
        pltpu.make_async_copy(res.at[rows_of(core, half), :], result.at[:, mine], x_loc.at[0]),
        pltpu.make_async_copy(y, y_out, v_sem.at[2]),
        keep_n(PARTS - 1),
    ]
    for copy in last[:3]:
        copy.start()
    for w in weights[5:]:
        w.finish()
        w.sent()
    for one in (gather_go, gather_two, spread, spread_n, spread_o):
        one.sent()
    for k in range(PARTS):
        for d in (1, 2, 3):
            share(k, d).wait_send()
            share_c(k, d).wait_send()
            piece = sums3.at[k, z ^ d]
            remote(piece, piece, c_send.at[k, d - 1], c_recv.at[k, d - 1], at_line(z ^ d, core)).wait_recv()
        total = jnp.sum(jnp.sum(sums3[k], axis=0), axis=0, keepdims=True)
        at = slice(k * PART, (k + 1) * PART)
        s2 = scale_two[:, at]
        coef[:, at] = s2 * s2 * s2 * (total / width)
    for j in range(3):
        keep_up(j + 3).wait()
        send_up(j).wait()
    keep_down().wait()
    send_down().wait()
    for copy in last:
        copy.wait()


def back_kernel(
    width,
    y, dn2_h, g_h, x_own, scale_two, scale_one, coef_two, gains, masks, par, gates_t, m_h, br_h,
    b_h, p_h, u_h, r_h, i_h, h_h, q_h, n1_h, f_own, f_got, fd_own, fd_got,
    input_grad, tiny_v, tiny_g, f_sum, f_land, fd_sum, fd_land, g_sum, g_land, gm_sum, gm_land,
    sums, coef, m_n, br_n, b_s, p_s, u_s, r_s, i_s, h_s, dyf, dbp, dy, dn1, dq, du, dri, a_c, l_c, carry_s, own, held,
    qv, n1, f_a, f_b, fd_a, fd_b, feed_part, mix_part, small, gate_grad, g_s, g_got, gm_got,
    vec, vec_in, vec_all, gd, gd_in, gd_all,
    c_sem, k_sem, l_send, l_recv, g_send, g_recv, s_send, s_recv, r_send, r_recv,
    f_sem, f_send, f_recv, d_send, d_recv, d_own, q_send, q_recv, n_send, n_recv, v_send, v_recv,
):
    row, z, core = place()
    block, seq = y.shape
    PART, PARTS = LATE, seq // LATE

    def lanes(part):
        return pl.ds(pl.multiple_of(part * PART, PART), PART)

    half = block // 2
    chan = b_s.shape[1]
    hc = chan // 2
    sibling = {"col": 2 * z + (1 - core)}
    greet(row, z, core, True, True)
    load_g = pltpu.make_async_copy(g_h, g_s, c_sem.at[0])
    load_g.start()
    dn2 = dn1
    load_d = pltpu.make_async_copy(dn2_h, dn2, c_sem.at[5])
    load_d.start()
    load_m = pltpu.make_async_copy(m_h, m_n, c_sem.at[1])
    load_m.start()
    load_b = pltpu.make_async_copy(br_h, br_n, c_sem.at[2])
    load_b.start()
    load_q = pltpu.make_async_copy(q_h, qv, c_sem.at[3])
    load_n = pltpu.make_async_copy(n1_h, n1, c_sem.at[4])
    kept = (b_s, p_s, u_s, r_s, i_s, h_s)
    srcs = (b_h, p_h, u_h, r_h, i_h, h_h)

    def fetch(n, part):
        if kept[n] is p_s or kept[n] is h_s:
            at = pl.ds(pl.multiple_of(part * PART, 128), PART + 128)
        else:
            at = lanes(part)
        return pltpu.make_async_copy(srcs[n].at[:, at], kept[n].at[part % 2], k_sem.at[n, part % 2])

    def fetch_all(part):
        for n in range(len(kept)):
            fetch(n, part).start()

    fetch_all(PARTS - 1)
    load_q.start()
    load_n.start()
    du[:, 0:128] = jnp.zeros((chan, 128), F32)
    carry_s[...] = jnp.zeros(carry_s.shape, F32)
    small[...] = jnp.zeros(small.shape, F32)
    gate_grad[...] = jnp.zeros(gate_grad.shape, F32)

    load_d.wait()
    load_g.wait()
    gather = Gather(dyf, g_send, g_recv, z, core, block, back=True)

    def outer(part):
        here = slice(part * PART, (part + 1) * PART)

        def one(i):
            at = rows_of(i, 64)
            s2 = scale_two[0:1, here]
            d, v = dn2[at, here], y[at, here]
            w = fold(d * v * s2)
            feed_part[at, :] = w if part == PARTS - 1 else feed_part[at, :] + w
            few = PART // g_s.shape[2]
            g = jnp.concatenate([g_s[part * few + j, at, :] for j in range(few)], axis=1)
            v = g.astype(F32) + (s2 * (gains[at, 9:10] * d) - v * coef_two[0:1, here])
            dy[at, here] = v
            dyf[part, pl.ds(pl.multiple_of(z * block + i * 64, 64), 64), :] = v.astype(BF16)

        blocks(block // 64, one)

    outer(PARTS - 1)
    gather.send(0, 0)
    outer(PARTS - 2)
    gather.send(0, 1)
    outer(PARTS - 3)
    gather.forward(1, 0)
    gather.send(0, 2)
    for part in range(PARTS - 3):
        outer(part)
    gather.forward(1, 1)
    gather.forward(2, 0)
    spread = Spread(lambda k, s: own.at[k, s], held, s_send, s_recv, z, core)
    load_m.wait()
    load_b.wait()
    final = lax.broadcasted_iota(jnp.int32, (128, PART), 1) == PART - 1

    f_arrays = ((f_own, f_got, f_a, f_b, f_sum, f_land), (fd_own, fd_got, fd_a, fd_b, fd_sum, fd_land))

    def f_loads(d):
        pulls = []
        for n, (ours, theirs, a, b, _, _) in enumerate(f_arrays):
            if n == 0:
                piece = (rows_of(row ^ d, block), slice(None))
            else:
                piece = (slice(None), pl.ds(pl.multiple_of((row ^ d) * block, 128), block))
            pulls.append(pltpu.make_async_copy(ours.at[piece], a.at[d], f_sem.at[n, 0]))
            pulls.append(pltpu.make_async_copy(theirs.at[piece], b, f_sem.at[n, 1]))
        return pulls

    def f_out(d):
        outs = []
        for n, (_, _, a, _, kept_at, land) in enumerate(f_arrays):
            if d == 0:
                outs.append(pltpu.make_async_copy(a.at[0], kept_at, f_send.at[n, 0]))
            else:
                outs.append(
                    remote(a.at[d], land.at[d - 1], f_send.at[n, d], f_recv.at[n, d], {"row": row ^ d})
                )
        return outs

    def f_part(d):
        for pull in f_loads(d):
            pull.wait()
        for _, _, a, b, _, _ in f_arrays:

            def add(i):
                at = rows_of(i, 64)
                a[d, at, :] = (a[d, at, :].astype(F32) + b[at, :].astype(F32)).astype(BF16)

            blocks(b.shape[0] // 64, add)
        for out in f_out(d):
            out.start()
        if d > 0:
            for pull in f_loads(d - 1):
                pull.start()

    def f_step(t):
        for d in range(LINE):
            pl.when(t == LINE - 1 - d)(functools.partial(f_part, d))

    for pull in f_loads(LINE - 1):
        pull.start()

    def work(t):
        k = PARTS - 1 - t
        here = lanes(k)
        wide = pl.ds(pl.multiple_of(k * PART, 128), PART + 128)
        slot = k % 2
        for n in range(len(kept)):
            fetch(n, k).wait()

        @pl.when(k > 0)
        def _():
            fetch_all(k - 1)

        dq[...] = dot(m_n[...], dyf[k])

        def before(i):
            ch = rows_of(i, 64)
            c = i // (hc // 64)
            low = pl.ds(pl.multiple_of(c * hc + i * 64, 64), 64)
            pr = par[ch, :]
            d = dq[ch, :]
            act, slope = gelu_parts(b_s[slot, ch, :])
            dbp[low, here] = (d * h_s[slot, ch, :][:, 128:] * slope).astype(BF16)
            l_c[ch, :] = d * act
            a_c[ch, :] = jnp.exp(-(r_s[slot, ch, :] * pr[:, 7:8]))

        blocks(chan // 64, before)
        gather.middle(t)

        def recur(i):
            ch = rows_of(i, 128)
            start = masks[0:1, here] > 0.5
            a, lam = jnp.where(start, 0.0, a_c[ch, :]), l_c[ch, :]
            lam = lam + jnp.where(final, carry_s[ch, :][:, 0:1], 0.0)
            w = jnp.where(final, 0.0, pltpu.roll(a, PART - 1, 1))
            shift = 1
            while shift < PART:
                lam = lam + w * pltpu.roll(lam, PART - shift, 1)
                if shift * 2 < PART:
                    w = w * pltpu.roll(w, PART - shift, 1)
                shift *= 2
            carry_s[ch, :] = jnp.broadcast_to((a * lam)[:, 0:1], (128, 128))
            l_c[ch, :] = lam

        blocks(chan // 128, recur)
        f_step(t)

        def after(i):
            ch = rows_of(i, 64)
            du[ch, PART:] = du[ch, 0:128]
            pr = par[ch, :]
            start = masks[0:1, here] > 0.5
            lam, a0 = l_c[ch, :], a_c[ch, :]
            earlier = pltpu.roll(h_s[slot, ch, :], 1, 1)[:, 128:]
            r, gate, u = r_s[slot, ch, :], i_s[slot, ch, :], u_s[slot, ch, :]
            m0 = jnp.sqrt(1.0 - a0 * a0 + FLOOR)
            m = jnp.where(start, 1.0, m0)
            lm = lam * m
            lu = lam * u
            du[ch, 0:PART] = lm * gate
            da = jnp.where(start, 0.0, lam * earlier - (lu * gate) * (a0 / m0)) * a0
            dr = da * (-pr[:, 7:8]) * (r * (1.0 - r))
            di = lu * m * (gate * (1.0 - gate))
            g, o = i // 4, (i % 4) * 64
            dri[pl.ds(pl.multiple_of(g * 512 + o, 64), 64), :] = dr.astype(BF16)
            dri[pl.ds(pl.multiple_of(g * 512 + 256 + o, 64), 64), :] = di.astype(BF16)
            small[5, ch, :] += fold(dr)
            small[6, ch, :] += fold(di)
            small[7, ch, :] += fold(da * r)

        blocks(chan // 64, after)
        for g in range(chan // 256):
            at = slice(g * 256, (g + 1) * 256)
            dd = dri[g * 512 : (g + 1) * 512, :]
            du[at, 0:PART] += dot(gates_t[g], dd)
            gate_grad[g] += dot_nt(u_s[slot, at, :].astype(BF16), dd)

        def conv(i):
            ch = rows_of(i, 64)
            c = i // (hc // 64)
            low = pl.ds(pl.multiple_of((c + 1) * hc + i * 64, 64), 64)
            pr = par[ch, :]
            follow = du[ch, :]
            window = p_s[slot, ch, :]
            d = follow[:, :PART]
            dp = pr[:, 0:1] * d
            small[4, ch, :] += fold(d)
            small[0, ch, :] += fold(d * window[:, 128:])
            for lag in (1, 2, 3):
                kd = follow * masks[lag : lag + 1, wide]
                dp = dp + pr[:, lag : lag + 1] * pltpu.roll(kd, PART + 128 - lag, 1)[:, :PART]
                small[lag, ch, :] += fold(kd[:, :PART] * pltpu.roll(window, lag, 1)[:, 128:])
            dbp[low, here] = dp.astype(BF16)

        blocks(chan // 64, conv)
        whole = dot(br_n[...], dbp[:, here])
        for s in range(LINE):
            own[t, s] = whole[s * block : (s + 1) * block, :].astype(own.dtype)

    def finish(t, total):
        k = PARTS - 1 - t

        sums[k, z] = jnp.zeros(sums.shape[2:], F32)

        @pl.when(t == 0)
        def _():
            mix_part[...] = jnp.zeros(mix_part.shape, F32)

        def add(i):
            at = pl.ds(pl.multiple_of(i * 64, 64), 64)
            d = total(pl.multiple_of(i * 64, 64), 64)
            dn1[at, lanes(k)] = d
            w = d * x_own[at, lanes(k)].astype(F32)
            sums[k, z] += eight(w * gains[at, 8:9])
            w = w * scale_one[0:1, lanes(k)]
            mix_part[at, :] += fold(w)

        blocks(block // 64, add)
        for d in (1, 2, 3):
            share(k, d).start()

    def share(k, d):
        return remote(sums.at[k, z], sums.at[k, z], l_send.at[k, d - 1], l_recv.at[k, d - 1], at_line(z ^ d, core))

    def step(t, carry):
        gather.arrive(2, t)
        work(t)
        spread.serve(t, finish)
        return carry

    lax.fori_loop(0, PARTS, step, 0)
    load_q.wait()
    load_n.wait()

    lru = hc

    def cols_of(side):
        return pl.ds(pl.multiple_of(side * 2 * lru, 128), 2 * lru)

    def send_br():
        return remote(br_n.at[:, cols_of(1 - core)], g_got, d_send.at[0], d_recv.at[0], sibling)

    def send_m():
        return remote(m_n.at[rows_of(1 - core, lru), :], gm_got, d_send.at[1], d_recv.at[1], sibling)

    def grad_br(side):
        for low in range(0, width, 2 * block):
            piece = slice(low, low + 2 * block)
            br_n[piece, cols_of(side)] = dot_nt(tokens_of(n1, piece), dbp[rows_of(side, 2 * lru), :]).astype(BF16)

    def out_br(d):
        piece = br_n.at[rows_of(row ^ d, block), cols_of(core)]
        if d == 0:
            return pltpu.make_async_copy(piece, g_sum, d_own.at[0])
        return remote(piece, g_land.at[d - 1], q_send.at[0, d - 1], q_recv.at[0, d - 1], {"row": row ^ d})

    def out_m(d):
        piece = m_n.at[rows_of(core, lru), pl.ds(pl.multiple_of((row ^ d) * block, 128), block)]
        if d == 0:
            return pltpu.make_async_copy(piece, gm_sum, d_own.at[1])
        return remote(piece, gm_land.at[d - 1], q_send.at[1, d - 1], q_recv.at[1, d - 1], {"row": row ^ d})

    def drain(i, carry):
        t = PARTS + i

        @pl.when(i == 0)
        def _():
            grad_br(1 - core)
            send_br().start()
            grad_br(core)

        @pl.when(i == 1)
        def _():
            send_br().wait_recv()

            def add(j):
                at = rows_of(j, 64)
                br_n[at, cols_of(core)] = (br_n[at, cols_of(core)].astype(F32) + g_got[at, :].astype(F32)).astype(BF16)

            blocks(width // 64, add)
            for d in (3, 2, 1, 0):
                out_br(d).start()
            for low in range(0, width, 2 * block):
                piece = slice(low, low + 2 * block)
                m_n[:, piece] = dot_nt(qv[...], tokens_of(dyf, piece)).astype(BF16)
            send_m().start()

        @pl.when(i == 2)
        def _():
            send_m().wait_recv()

            def add(j):
                at = rows_of(j, 64)
                to = pl.ds(pl.multiple_of(core * lru + j * 64, 64), 64)
                m_n[to, :] = (m_n[to, :].astype(F32) + gm_got[at, :].astype(F32)).astype(BF16)

            blocks(lru // 64, add)
            for d in (3, 2, 1, 0):
                out_m(d).start()

        spread.serve(t, finish)
        return carry

    lax.fori_loop(0, LINE - 1, drain, 0)
    mine = pl.ds(pl.multiple_of(core * seq, seq), seq)
    for side in (0, 1):
        for e in range(4):
            at = slice(e * 64, (e + 1) * 64)
            gd[side, at, 0:64] = gate_grad[side, at, e * 64 : (e + 1) * 64]
            gd[side, at, 64:128] = gate_grad[side, at, 256 + e * 64 : 256 + (e + 1) * 64]
    swap_gd = remote(gd.at[1 - core], gd_in, v_send.at[0], v_recv.at[0], sibling)
    swap_gd.start()
    lane = lax.broadcasted_iota(jnp.int32, (64, 128), 1)

    def columns(parts, at):
        total = jnp.zeros((64, 128), F32)
        for n, part in enumerate(parts):
            total = total + jnp.where(lane == n, jnp.sum(part(at), axis=1, keepdims=True), 0.0)
        return total

    vec[...] = jnp.zeros(vec.shape, F32)
    for j in range(chan // 64):
        at = slice(j * 64, (j + 1) * 64)
        v = columns([lambda at, n=n: small[n, at, :] for n in range(8)], at)
        vec[0, :, at] = v.T[0:8, :]

    for k in range(PARTS):
        for d in (1, 2, 3):
            share(k, d).wait_send()
            piece = sums.at[k, z ^ d]
            remote(piece, piece, l_send.at[k, d - 1], l_recv.at[k, d - 1], at_line(z ^ d, core)).wait_recv()
        total = jnp.sum(jnp.sum(sums[k], axis=0), axis=0, keepdims=True)
        at = slice(k * PART, (k + 1) * PART)
        s1 = scale_one[:, at]
        coef[:, at] = s1 * s1 * s1 * (total / width)

    def last(i):
        at = rows_of(i, 16)
        v = dy[at, :] + (
            scale_one[0:1, :] * (gains[at, 8:9] * dn1[at, :]) - x_own[at, :].astype(F32) * coef[0:1, :]
        )
        dy[at, :] = v

    blocks(block // 16, last)
    back = remote(dy.at[rows_of(1 - core, half), :], input_grad.at[:, mine], r_send, r_recv, sibling)
    back.start()
    keep_in = pltpu.make_async_copy(dy.at[rows_of(core, half), :], input_grad.at[:, mine], d_own.at[3])
    keep_in.start()
    for j in range(block // 64):
        at = slice(j * 64, (j + 1) * 64)
        v = columns([lambda at: mix_part[at, :], lambda at: feed_part[at, :]], at)
        vec[1, :, at] = v.T[0:8, :]
    swap_vec = remote(vec, vec_in, v_send.at[1], v_recv.at[1], sibling)
    swap_vec.start()
    swap_gd.wait()
    gd_all[0] = gd[core] + gd_in[...]
    rows_gd = [
        remote(gd_all.at[0], gd_all.at[d], n_send.at[0, d - 1], n_recv.at[0, d - 1], {"row": row ^ d}) for d in (1, 2, 3)
    ]
    for copy in rows_gd:
        copy.start()
    swap_vec.wait()
    vec_all[0] = vec[...] + vec_in[...]
    rows_vec = [
        remote(vec_all.at[0], vec_all.at[d], n_send.at[1, d - 1], n_recv.at[1, d - 1], {"row": row ^ d}) for d in (1, 2, 3)
    ]
    for copy in rows_vec:
        copy.start()
    spread.sent()
    gather.sent()
    for copy in rows_gd + rows_vec:
        copy.wait()
    for every, out in ((gd_all, tiny_g), (vec_all, tiny_v)):
        first, second = every[row % 2], every[1 - row % 2]
        third, fourth = every[2 + row % 2], every[3 - row % 2]
        out[...] = (first + second) + (third + fourth)
    for d in range(LINE):
        for out in f_out(d):
            out.wait()
    send_br().wait_send()
    send_m().wait_send()
    for d in (0, 1, 2, 3):
        out_br(d).wait()
        out_m(d).wait()
    for copy in (keep_in, back):
        copy.wait()


def last_kernel(
    f_sum, f_land, fd_sum, fd_land, g_sum, g_land, gm_sum, gm_land, result_in, grad_in, tiny_v, tiny_g, lambdas,
    s_b, s_r, s_m, s_g, s_u, s_d, result, input_grad, taps, offs, bias_r, bias_a, decay, mix, feed, retain, admit,
):
    lru, ff, half = s_b.shape[1], s_g.shape[1], mix.shape[1]

    def four(first, others):
        return first[...].astype(F32) + others[0].astype(F32) + (others[1].astype(F32) + others[2].astype(F32))

    v = four(f_sum, f_land)
    s_g[...] = v[:, :ff]
    s_u[...] = v[:, ff:]
    v = four(g_sum, g_land)
    s_b[...] = v[:, :lru]
    s_r[...] = v[:, lru:]
    s_d[...] = four(fd_sum, fd_land)
    s_m[...] = four(gm_sum, gm_land)
    result[...] = result_in[...]
    input_grad[...] = grad_in[...]

    @pl.when(pl.program_id(0) == 0)
    def _():
        core = place()[2]
        small = tiny_v[0, :, pl.ds(pl.multiple_of(core * lru, 128), lru)]
        taps[...] = small[0:4]
        offs[...] = small[4:5]
        bias_r[...] = small[5:6]
        bias_a[...] = small[6:7]
        decay[...] = small[7:8] * (8.0 * jax.nn.sigmoid(-lambdas[...]))
        gains = jnp.where(core == 0, tiny_v[1, :, 0:half], tiny_v[1, :, half : 2 * half])
        mix[...] = gains[0:1]
        feed[...] = gains[1:2]
        for e in range(retain.shape[0]):
            at = slice(e * 64, (e + 1) * 64)
            retain[e] = tiny_g[at, 0:64]
            admit[e] = tiny_g[at, 64:128]


ANY = pl.BlockSpec(memory_space=pl.ANY)
VM = pl.BlockSpec(memory_space=pltpu.VMEM)
DMA = pltpu.SemaphoreType.DMA
ROOM = 62 * 1024 * 1024


def shape(dims, kind):
    return jax.ShapeDtypeStruct(dims, kind)


def call(kernel, ins, outs, scratch, ident, name, flops):
    return pl.pallas_call(
        kernel,
        out_shape=[o[0] for o in outs],
        in_specs=ins,
        out_specs=[o[1] for o in outs],
        scratch_shapes=scratch,
        name=name,
        compiler_params=pltpu.CompilerParams(
            collective_id=ident, has_side_effects=True, vmem_limit_bytes=ROOM
        ),
        cost_estimate=pl.CostEstimate(flops=flops, bytes_accessed=40000000, transcendentals=0),
    )


def fast_body(
    inputs, segments, mix_gain, branch_weight, recur_weight, kernel, offsets, retain_weight, retain_bias,
    admit_weight, admit_bias, lambdas, merge_weight, feed_gain, gate_weight, up_weight, down_weight, cotangent,
):
    half, tokens = inputs.shape
    block, seq, width = 2 * half, tokens // 2, D
    lru, heads = branch_weight.shape[1], retain_weight.shape[0]
    chan = 2 * lru
    ff = gate_weight.shape[1]
    hid = 2 * ff
    rows = branch_weight.shape[0]
    cols = merge_weight.shape[1]
    blank = jnp.zeros((lru - half,), F32)
    vec = [kernel] + [v[None, :] for v in (offsets, retain_bias, admit_bias, lambdas)]
    vec.append(jnp.concatenate([mix_gain, blank, feed_gain, blank]).reshape(2, lru))
    vec = jnp.concatenate(vec + [jnp.zeros((6, lru), F32), segments.astype(F32).reshape(-1, lru)])
    br_s = jnp.concatenate([branch_weight, recur_weight], axis=1).T
    m_s = merge_weight.T
    gu_s = jnp.concatenate([gate_weight, up_weight], axis=1).T

    f_tok = lambda n, kind=F32: shape((n, seq), kind)
    padded = (shape((chan, 128 + seq), F32), ANY)
    state = [(f_tok(chan), ANY), padded, *[(f_tok(chan), ANY)] * 3, padded]
    line = [DMA((3,)), DMA((3,))]
    steps = [DMA((2, 3, PARTS)), DMA((2, 3, PARTS))]
    sums = [DMA((2, PARTS, LINE)), DMA((2, PARTS, LINE))]
    held = pltpu.VMEM((PARTS, LINE + 1, block, PART), BF16)
    own_low = pltpu.VMEM((PARTS, LINE, block, PART), BF16)
    tok = lambda n, kind=F32, lead=0: pltpu.VMEM((n, lead + seq), kind)
    one = lambda n, kind=F32, lead=0: pltpu.VMEM((n, lead + PART), kind)
    br_t = jnp.concatenate([branch_weight, recur_weight], axis=1)
    grad_gu, grad_d = (shape((width, 2 * ff), BF16), ANY), (shape((ff, width), BF16), ANY)
    low = lambda n, m: (shape((n, m), BF16), ANY)
    parted = lambda n: (shape((PARTS, n, PART), BF16), ANY)
    by_part = lambda n: pltpu.VMEM((PARTS, n, PART), BF16)

    (masks, par, gains, gates, coef, scale_one, scale_two, y, n1, q, x_own, g, b, p, u, r, i, h, result, dn2, _, _, f_own, f_got, fd_own, fd_got,
     br_n, m_n) = call(
        functools.partial(forward_kernel, width, EPS),
        [ANY] * 2 + [VM] * 3 + [ANY] * 6,
        [(shape((8, seq + 128), F32), VM), (shape((chan, 16), F32), VM), (shape((block, 16), F32), VM), (shape((2, lru, 2 * lru), BF16), VM),
         (f_tok(8), VM), (f_tok(8), VM), (f_tok(8), VM), (f_tok(block), ANY), parted(width), low(chan, seq), low(block, seq), parted(block)]
        + state + [low(half, tokens), (f_tok(block), ANY), low(2 * hid, seq), low(hid, seq), grad_gu, grad_gu, grad_d, grad_d,
                   low(width, 2 * chan), low(chan, width)],
        [pltpu.VMEM((LINE, 8, seq), F32), pltpu.VMEM((PARTS, LINE, 8, PART), F32), pltpu.VMEM((PARTS, LINE, 8, PART), F32),
         pltpu.VMEM((2, 16, lru), F32), pltpu.VMEM((2, 2) + retain_weight.shape, F32), pltpu.VMEM((2, 2 * lru, lru), BF16),
         pltpu.VMEM((2, 2 * lru, lru), BF16), by_part(width), by_part(width),
         by_part(width), tok(block, BF16), tok(block), one(block), one(chan, BF16),
         one(chan, F32, 128), one(chan, F32, 128), one(max(5 * chan, 3 * hid)), one(chan, BF16), one(chan, BF16),
         own_low, held, held, held, pltpu.VMEM((2 * hid, width), BF16), pltpu.VMEM((width, 2 * hid), BF16),
         pltpu.VMEM((hid, width), BF16), pltpu.VMEM((width, hid), BF16), one(hid, BF16), one(2 * hid, BF16),
         DMA((5,)), DMA((5,)), DMA((5,)), DMA((PARTS,)), DMA((PARTS,)), DMA((PARTS,))] + line + [DMA((PARTS, 3)), DMA((PARTS, 3))] * 2 + steps * 3 + sums * 3
        + [DMA((7, 7)), DMA((7, 7)), DMA((7,)), DMA((7,)), DMA((7,)), DMA((4,)), DMA((4,)), DMA((4,))],
        0, "forward", 50 * 10**9,
    )(inputs, cotangent, vec, retain_weight, admit_weight, br_s, m_s, gu_s, down_weight,
      br_t, merge_weight)

    late = seq // LATE
    pair = lambda lead=0: pltpu.VMEM((2, chan, lead + LATE), F32)
    one = lambda n, kind=F32, lead=0: pltpu.VMEM((n, lead + LATE), kind)
    steps = [DMA((2, 3, late)), DMA((2, 3, late))]
    sums = [DMA((2, late, LINE)), DMA((2, late, LINE))]
    held = pltpu.VMEM((late, LINE + 1, block, LATE), BF16)
    own_low = pltpu.VMEM((late, LINE, block, LATE), BF16)
    land = lambda n, m: ((shape((n, m), BF16), ANY), (shape((3, n, m), BF16), ANY))
    input_grad, tiny_v, tiny_g, *sums_of = call(
        functools.partial(back_kernel, width),
        [VM] + [ANY] * 2 + [VM] * 8 + [ANY] * 14,
        [(shape((half, tokens), F32), ANY), (shape((2, 8, chan), F32), VM),
         (shape((lru, 128), F32), VM), *land(cols, 2 * ff), *land(ff, cols), *land(cols, 2 * lru), *land(lru, cols)],
        [pltpu.VMEM((late, LINE, 8, LATE), F32), pltpu.VMEM((8, seq), F32),
         pltpu.VMEM((chan, width), BF16), pltpu.VMEM((width, 2 * chan), BF16),
         pair(), pair(128), pair(), pair(), pair(), pair(128), pltpu.VMEM((late, width, LATE), BF16), tok(2 * chan, BF16),
         tok(block), tok(block), one(chan), one(chan, F32, 128), one(2 * chan, BF16),
         one(chan), one(chan), pltpu.VMEM((chan, 128), F32), own_low, held,
         tok(chan, BF16), by_part(width), pltpu.VMEM((4, cols, 2 * ff), BF16), pltpu.VMEM((cols, 2 * ff), BF16),
         pltpu.VMEM((4, ff, cols), BF16), pltpu.VMEM((ff, cols), BF16),
         pltpu.VMEM((block, 128), F32), pltpu.VMEM((block, 128), F32), pltpu.VMEM((8, chan, 128), F32),
         pltpu.VMEM((2, lru, 2 * lru), F32), by_part(block), pltpu.VMEM((width, 2 * lru), BF16),
         pltpu.VMEM((lru, width), BF16), pltpu.VMEM((2, 8, chan), F32), pltpu.VMEM((2, 8, chan), F32),
         pltpu.VMEM((4, 2, 8, chan), F32), pltpu.VMEM((2, lru, 128), F32), pltpu.VMEM((lru, 128), F32),
         pltpu.VMEM((4, lru, 128), F32), DMA((7,)), DMA((6, 2))] + [DMA((late, 3)), DMA((late, 3))] + steps + sums
        + [DMA, DMA, DMA((2, 2)), DMA((2, LINE)), DMA((2, LINE)), DMA((2,)), DMA((2,)), DMA((4,))]
        + [DMA((2, 3)), DMA((2, 3)), DMA((2, 3)), DMA((2, 3)), DMA((2,)), DMA((2,))],
        2, "mix_backward", 10 * 10**9,
    )(y, dn2, g, x_own, scale_two, scale_one, coef, gains, masks, par, gates, m_n, br_n, b, p, u, r, i, h,
      q, n1, f_own, f_got, fd_own, fd_got)

    line_of = shape((1, lru), F32)
    cuts = 4
    rows_in = lambda *dims: pl.BlockSpec((dims[0] // cuts,) + dims[1:], lambda n: (n,) + (0,) * (len(dims) - 1))
    three = lambda *dims: pl.BlockSpec((3, dims[0] // cuts, dims[1]), lambda n: (0, n, 0))
    still = lambda *dims: pl.BlockSpec(dims, lambda n: (0,) * len(dims))
    sizes = ((cols, 2 * ff), (ff, cols), (cols, 2 * lru), (lru, cols))
    big = ((cols, lru), (cols, lru), (lru, cols), (cols, ff), (cols, ff), (ff, cols))
    flat = ((4, lru),) + ((1, lru),) * 4 + ((1, half),) * 2 + ((heads, 64, 64),) * 2
    s_b, s_r, s_m, s_g, s_u, s_d, result, input_grad, taps, offs, bias_r, bias_a, decay, mix, feed, retain, admit = pl.pallas_call(
        last_kernel,
        grid=(cuts,),
        out_shape=[shape(d, F32) for d in big] + [shape((half, tokens), BF16), shape((half, tokens), F32)]
        + [shape(d, F32) for d in flat],
        in_specs=[spec(*d) for d in sizes for spec in (rows_in, three)] + [rows_in(half, tokens)] * 2
        + [still(2, 8, chan), still(lru, 128), still(1, lru)],
        out_specs=[rows_in(*d) for d in big] + [rows_in(half, tokens)] * 2 + [still(*d) for d in flat],
        name="last_sums",
        compiler_params=pltpu.CompilerParams(vmem_limit_bytes=ROOM),
    )(*sums_of, result, input_grad, tiny_v, tiny_g, lambdas[None, :])
    return (
        result,
        input_grad,
        mix[0],
        s_b,
        s_r,
        taps,
        offs[0],
        retain,
        bias_r[0],
        admit,
        bias_a[0],
        decay[0],
        s_m,
        feed[0],
        s_g,
        s_u,
        s_d,
    )


def suits(mesh, args):
    return (
        dict(mesh.shape) == {"row": 4, "col": 8}
        and args[0].shape == (D, 8 * SEQ)
        and args[3].shape == (D, 2048)
        and args[14].shape == (D, 4608)
        and args[7].shape == (32, 64, 64)
    )


def solution(mesh):
    in_specs = (
        P("col", "row"),
        P("row"),
        P("col"),
        P("row", "col"),
        P("row", "col"),
        P(None, "col"),
        P("col"),
        P("col", None, None),
        P("col"),
        P("col", None, None),
        P("col"),
        P("col"),
        P("col", "row"),
        P("col"),
        P("row", "col"),
        P("row", "col"),
        P("col", "row"),
        P("col", "row"),
    )
    out_specs = (
        P("col", "row"),
        P("col", "row"),
        P("col"),
        P("row", "col"),
        P("row", "col"),
        P(None, "col"),
        P("col"),
        P("col", None, None),
        P("col"),
        P("col", None, None),
        P("col"),
        P("col"),
        P("col", "row"),
        P("col"),
        P("row", "col"),
        P("row", "col"),
        P("col", "row"),
    )
    def run(*args):
        chosen = fast_body if suits(mesh, args) else body
        return jax.shard_map(
            chosen, mesh=mesh, in_specs=in_specs, out_specs=out_specs, check_vma=False
        )(*args)

    return run
```

```python
import functools

import jax
import jax.numpy as jnp
from jax import lax
from jax.experimental import pallas as pl
from jax.experimental.pallas import tpu as pltpu
from jax.sharding import PartitionSpec as P

D = 1536
SEQ = 1024
MICRO = 2


HIGH = lax.Precision.HIGHEST
EPS = 1e-06
POWER = 8.0
FLOOR = 0.01


def combine(earlier, later):
    first_a, first_b = earlier
    second_a, second_b = later
    return (first_a * second_a, second_a * first_b + second_b)


def mixer(
    branch_pre,
    lru_pre,
    segs,
    kernel,
    offsets,
    retain_weight,
    retain_bias,
    admit_weight,
    admit_bias,
    lambdas,
):
    length = lru_pre.shape[0]
    channels = lru_pre.shape[1]
    conv = offsets + kernel[0] * lru_pre
    for lag in range(1, kernel.shape[0]):
        shifted = jnp.concatenate(
            [jnp.zeros((lag, channels), lru_pre.dtype), lru_pre[:-lag]], axis=0
        )
        prior = jnp.concatenate([jnp.full((lag,), -1, jnp.int32), segs[:-lag]])
        keep = (prior == segs).astype(lru_pre.dtype)
        conv = conv + kernel[lag] * shifted * keep[:, None]
    heads = retain_weight.shape[0]
    blocks = conv.reshape(length, heads, channels // heads)
    retain = jax.nn.sigmoid(
        jnp.einsum("thi,hij->thj", blocks, retain_weight, precision=HIGH).reshape(length, channels)
        + retain_bias
    )
    admit = jax.nn.sigmoid(
        jnp.einsum("thi,hij->thj", blocks, admit_weight, precision=HIGH).reshape(length, channels)
        + admit_bias
    )
    decay = jnp.exp(-POWER * retain * jax.nn.softplus(-lambdas))
    factor = jnp.sqrt(1.0 - decay * decay + FLOOR)
    starts = jnp.concatenate([jnp.ones((1,), bool), segs[1:] != segs[:-1]])
    decay = jnp.where(starts[:, None], 0.0, decay)
    factor = jnp.where(starts[:, None], 1.0, factor)
    _, state = lax.associative_scan(combine, (decay, factor * admit * conv), axis=0)
    return jax.nn.gelu(branch_pre) * state


def geglu(gate, upper):
    return jax.nn.gelu(gate) * upper


def contract_rows(left, right):
    return lax.dot_general(
        left, right, (((0,), (0,)), ((), ())), preferred_element_type=jnp.float32
    )


def contract_cols(left, right):
    return lax.dot_general(
        left, right, (((1,), (1,)), ((), ())), preferred_element_type=jnp.float32
    )


def contract_cross(left, right):
    return lax.dot_general(
        left, right, (((0,), (1,)), ((), ())), preferred_element_type=jnp.float32
    )


def norm_forward(resid, gain):
    total = lax.psum(jnp.sum(resid * resid, axis=0), "col")
    scale = lax.rsqrt(total / D + EPS)[None, :]
    return (scale, (resid * scale * gain[:, None]).astype(jnp.bfloat16))


def norm_backward(resid, scale, gain, grad_normed):
    weighted = grad_normed * gain[:, None]
    total = lax.psum(jnp.sum(weighted * resid, axis=0), "col")
    grad_resid = scale * weighted - resid * (scale * scale * scale) * (total / D)[None, :]
    grad_gain = jnp.sum(grad_normed * resid * scale, axis=1)
    return (grad_resid, grad_gain)


def gather_features(normed):
    return lax.all_gather(normed, "col", axis=0, tiled=True)


def gather_cotangent(grad):
    return lax.all_gather(grad, "col", axis=0, tiled=True)


def spread_sum(term):
    return lax.psum_scatter(
        term.astype(jnp.bfloat16), "col", scatter_dimension=0, tiled=True
    ).astype(jnp.float32)


def back_sum(term):
    return spread_sum(term)


def merge_term(whole_merge, mixed_low):
    return spread_sum(contract_cross(whole_merge, mixed_low))


def weight_grads(normed, grad_joined):
    return jnp.dot(
        normed,
        grad_joined,
        preferred_element_type=jnp.float32,
    )


def row_sum(total, axis):
    return lax.psum_scatter(
        total.astype(jnp.bfloat16), "row", scatter_dimension=axis, tiled=True
    ).astype(jnp.float32)


def body(
    inputs,
    segments,
    mix_gain,
    branch_weight,
    recur_weight,
    kernel,
    offsets,
    retain_weight,
    retain_bias,
    admit_weight,
    admit_bias,
    lambdas,
    merge_weight,
    feed_gain,
    gate_weight,
    up_weight,
    down_weight,
    cotangent,
):
    lru_cols = branch_weight.shape[1]
    feed_cols = gate_weight.shape[1]
    mixer_params = (kernel, offsets, retain_weight, retain_bias, admit_weight, admit_bias, lambdas)
    acc_branch = jnp.zeros((D, lru_cols), jnp.float32)
    acc_recur = jnp.zeros((D, lru_cols), jnp.float32)
    acc_gate = jnp.zeros((D, feed_cols), jnp.float32)
    acc_up = jnp.zeros((D, feed_cols), jnp.float32)
    acc_merge = jnp.zeros((lru_cols, D), jnp.float32)
    acc_down = jnp.zeros((feed_cols, D), jnp.float32)
    acc_small = tuple((jnp.zeros_like(p) for p in mixer_params))
    acc_mix = jnp.zeros_like(mix_gain)
    acc_feed = jnp.zeros_like(feed_gain)
    outputs = []
    in_grads = []
    for batch in range(MICRO):
        lower = batch * SEQ
        resid_in = inputs[:, lower : lower + SEQ].astype(jnp.float32)
        grad_out = cotangent[:, lower : lower + SEQ].astype(jnp.float32)
        segs = segments[lower : lower + SEQ]
        whole_branch, whole_recur, whole_gate, whole_up = (
            lax.all_gather(branch_weight, "row", axis=0, tiled=True),
            lax.all_gather(recur_weight, "row", axis=0, tiled=True),
            lax.all_gather(gate_weight, "row", axis=0, tiled=True),
            lax.all_gather(up_weight, "row", axis=0, tiled=True),
        )
        whole_merge, whole_down = (
            lax.all_gather(merge_weight, "row", axis=1, tiled=True),
            lax.all_gather(down_weight, "row", axis=1, tiled=True),
        )
        scale_one, normed_one = norm_forward(resid_in, mix_gain)
        full_one = gather_features(normed_one)
        branch_pre = contract_rows(full_one, whole_branch)
        lru_pre = contract_rows(full_one, whole_recur)

        def local_mixer(bpre, lpre, kern, offs, rweight, rbias, aweight, abias, lams):
            return mixer(bpre, lpre, segs, kern, offs, rweight, rbias, aweight, abias, lams)

        mixed, mixer_pull = jax.vjp(local_mixer, branch_pre, lru_pre, *mixer_params)
        mixed_low = mixed.astype(jnp.bfloat16)
        resid_mid = resid_in + merge_term(whole_merge, mixed_low)
        scale_two, normed_two = norm_forward(resid_mid, feed_gain)
        full_two = gather_features(normed_two)
        gate = contract_rows(full_two, whole_gate)
        upper = contract_rows(full_two, whole_up)
        hidden, geglu_pull = jax.vjp(geglu, gate, upper)
        hidden_low = hidden.astype(jnp.bfloat16)
        result = resid_mid + spread_sum(contract_cross(whole_down, hidden_low))
        outputs.append(result.astype(jnp.bfloat16))
        grad_full = gather_cotangent(grad_out.astype(jnp.bfloat16))
        acc_down = acc_down + contract_cross(hidden_low, grad_full)
        grad_gate, grad_upper = geglu_pull(contract_cross(grad_full, whole_down))
        grad_gate = grad_gate.astype(jnp.bfloat16)
        grad_upper = grad_upper.astype(jnp.bfloat16)
        feed_joined = weight_grads(full_two, jnp.concatenate([grad_gate, grad_upper], axis=1))
        acc_gate = acc_gate + feed_joined[:, :feed_cols]
        acc_up = acc_up + feed_joined[:, feed_cols:]
        grad_normed_two = back_sum(
            contract_cols(whole_gate, grad_gate) + contract_cols(whole_up, grad_upper)
        )
        grad_mid_norm, feed_part = norm_backward(resid_mid, scale_two, feed_gain, grad_normed_two)
        acc_feed = acc_feed + feed_part
        grad_mid = grad_out + grad_mid_norm
        grad_mid_full = gather_cotangent(grad_mid.astype(jnp.bfloat16))
        acc_merge = acc_merge + contract_cross(mixed_low, grad_mid_full)
        pulled = mixer_pull(contract_cross(grad_mid_full, whole_merge))
        grad_branch = pulled[0].astype(jnp.bfloat16)
        grad_lru = pulled[1].astype(jnp.bfloat16)
        acc_small = tuple((total + part for total, part in zip(acc_small, pulled[2:])))
        branch_joined = weight_grads(full_one, jnp.concatenate([grad_branch, grad_lru], axis=1))
        acc_branch = acc_branch + branch_joined[:, :lru_cols]
        acc_recur = acc_recur + branch_joined[:, lru_cols:]
        grad_normed_one = back_sum(
            contract_cols(whole_branch, grad_branch) + contract_cols(whole_recur, grad_lru)
        )
        grad_in_norm, mix_part = norm_backward(resid_in, scale_one, mix_gain, grad_normed_one)
        acc_mix = acc_mix + mix_part
        in_grads.append(grad_mid + grad_in_norm)
    sum_branch, sum_recur, sum_gate, sum_up = (
        row_sum(acc_branch, 0),
        row_sum(acc_recur, 0),
        row_sum(acc_gate, 0),
        row_sum(acc_up, 0),
    )
    sum_merge, sum_down = (
        row_sum(acc_merge, 1),
        row_sum(acc_down, 1),
    )
    summed = lax.psum(
        (
            acc_mix,
            acc_feed,
            acc_small[0],
            acc_small[1],
            acc_small[2],
            acc_small[3],
            acc_small[4],
            acc_small[5],
            acc_small[6],
        ),
        "row",
    )
    result_all = jnp.concatenate(outputs, axis=1)
    input_grad = jnp.concatenate(in_grads, axis=1)
    return (
        result_all,
        input_grad,
        summed[0],
        sum_branch,
        sum_recur,
        summed[2],
        summed[3],
        summed[4],
        summed[5],
        summed[6],
        summed[7],
        summed[8],
        sum_merge,
        summed[1],
        sum_gate,
        sum_up,
        sum_down,
    )


MESH = pl.DeviceIdType.MESH
F32 = jnp.float32
BF16 = jnp.bfloat16
LINE = 4
PART = 128
PARTS = 8
LATE = 256
GELU_A = 0.7978845608028654
GELU_B = 0.044715


def place():
    row, col = lax.axis_index("row"), lax.axis_index("col")
    return row, col // 2, col % 2


def at_line(z, core):
    return {"col": 2 * z + core}


def lanes(part):
    return pl.ds(pl.multiple_of(part * PART, PART), PART)


def rows_of(index, size):
    return pl.ds(pl.multiple_of(index * size, 16), size)


def dot(a, b):
    return lax.dot_general(a, b, (((1,), (0,)), ((), ())), preferred_element_type=F32)


def dot_nt(a, b):
    return lax.dot_general(a, b, (((1,), (1,)), ((), ())), preferred_element_type=F32)


def greet(row, z, core, rows, line):
    barrier = pltpu.get_barrier_semaphore()
    peers = [{"col": 2 * z + (1 - core)}]
    if rows:
        peers += [{"row": row ^ d} for d in (1, 2, 3)]
    if line:
        peers += [at_line(z ^ d, core) for d in (1, 2, 3)]
    for peer in peers:
        pl.semaphore_signal(barrier, inc=1, device_id=peer, device_id_type=MESH)
    return functools.partial(pl.semaphore_wait, barrier, len(peers))


def remote(src, dst, send, recv, peer):
    return pltpu.make_async_remote_copy(
        src_ref=src, dst_ref=dst, send_sem=send, recv_sem=recv, device_id=peer, device_id_type=MESH
    )


class Gather:
    def __init__(self, ref, send, recv, z, core, block, back=False):
        self.parts = ref.shape[0]
        self.ref, self.sems, self.z, self.core = ref, (send, recv), z, core
        self.block, self.back = block, back

    def copy(self, way, hop, step, owner, incoming=False):
        part = self.parts - 1 - step if self.back else step
        piece = self.ref.at[part, rows_of(owner, self.block), :]
        peer = at_line(self.z + (1 if (way == 0) != incoming else -1), self.core)
        return remote(piece, piece, self.sems[0].at[way, hop, step], self.sems[1].at[way, hop, step], peer)

    def each(self, hop, act, incoming):
        z = self.z
        if incoming:
            cases = ((0, z - 1 - hop >= 0, z - 1 - hop), (1, z + 1 + hop < LINE, z + 1 + hop))
        else:
            cases = (
                (0, (z >= hop) & (z < LINE - 1), z - hop),
                (1, (z + hop < LINE) & (z >= 1), z + hop),
            )
        for way, here, owner in cases:
            pl.when(here)(functools.partial(act, way, owner))

    def send(self, hop, step):
        self.each(hop, lambda way, owner: self.copy(way, hop, step, owner).start(), False)

    def arrive(self, hop, step):
        self.each(hop, lambda way, owner: self.copy(way, hop, step, owner, True).wait_recv(), True)

    def forward(self, hop, step):
        self.arrive(hop - 1, step)
        self.send(hop, step)

    def sent(self):
        def one(step, carry):
            for hop in range(LINE - 1):
                self.each(hop, lambda way, owner: self.copy(way, hop, step, owner).wait_send(), False)
            return carry

        lax.fori_loop(0, self.parts, one, 0)

    def middle(self, step, ahead=1):
        for hop in (2, 1, 0):
            later = step + ahead + 2 - hop
            act = self.forward if hop else self.send
            pl.when(later < self.parts)(functools.partial(act, hop, later))


class Spread:
    def __init__(self, own, held, send, recv, z, core):
        self.parts = held.shape[0]
        self.own, self.held, self.sems, self.z, self.core = own, held, (send, recv), z, core

    def copy(self, way, step, hop):
        slot = hop if way == 0 else LINE - hop
        there = slot - 1 if way == 0 else slot + 1
        peer = at_line(self.z + (1 if way == 0 else -1), self.core)
        return remote(
            self.held.at[step, slot],
            self.held.at[step, there],
            self.sems[0].at[way, step, hop],
            self.sems[1].at[way, step, hop - 1],
            peer,
        )

    def landed(self, way, step, hop):
        slot = hop if way == 0 else LINE - hop
        piece = self.held.at[step, slot]
        peer = at_line(self.z + (-1 if way == 0 else 1), self.core)
        remote(piece, piece, self.sems[0].at[way, step, hop], self.sems[1].at[way, step, hop], peer).wait_recv()

    def push(self, way, step, first):
        z = self.z

        def one(i, carry):
            hop = LINE - 1 - i
            owner = z + hop if way == 0 else z - hop
            slot = hop if way == 0 else LINE - hop

            @pl.when((owner >= 0) & (owner < LINE))
            def _():
                @pl.when(first)
                def _():
                    self.held[step, slot] = self.own(step, owner)[...].astype(BF16)

                @pl.when(jnp.logical_not(first))
                def _():
                    self.landed(way, step, hop)
                    total = self.own(step, owner)[...].astype(F32) + self.held[step, slot].astype(F32)
                    self.held[step, slot] = total.astype(BF16)

                self.copy(way, step, hop).start()

            return carry

        lax.fori_loop(0, LINE - 1, one, 0)

    def serve(self, t, finish):
        z = self.z
        step = t - (LINE - 1)

        @pl.when((step >= 0) & (step < self.parts))
        def _():
            @pl.when(z == 0)
            def _():
                self.landed(1, step, 0)
                finish(step, lambda a, n: self.mine(step, a, n) + self.got(step, LINE, a, n))

            @pl.when(z == LINE - 1)
            def _():
                self.landed(0, step, 0)
                finish(step, lambda a, n: self.mine(step, a, n) + self.got(step, 0, a, n))

            @pl.when((z > 0) & (z < LINE - 1))
            def _():
                self.landed(0, step, 0)
                self.landed(1, step, 0)
                finish(
                    step,
                    lambda a, n: self.mine(step, a, n) + (self.got(step, 0, a, n) + self.got(step, LINE, a, n)),
                )

        for way, late, turn in ((1, LINE - 1 - z, z < 2), (0, z, z >= 0), (1, LINE - 1 - z, z >= 2)):
            step = t - late
            pl.when((step >= 0) & (step < self.parts) & turn)(functools.partial(self.push, way, step, late == 0))

    def mine(self, step, start, size):
        return self.own(step, self.z)[pl.ds(start, size), :].astype(F32)

    def got(self, step, slot, start, size):
        return self.held[step, slot, pl.ds(start, size)].astype(F32)

    def sent(self):
        z = self.z

        def one(step, carry):
            for way in (0, 1):
                for hop in range(1, LINE):
                    owner = z + hop if way == 0 else z - hop

                    @pl.when((owner >= 0) & (owner < LINE))
                    def _():
                        self.copy(way, step, hop).wait_send()

            return carry

        lax.fori_loop(0, self.parts, one, 0)


def share_line(ref, send, recv, z, core):
    copies = [
        remote(ref.at[z], ref.at[z], send.at[d - 1], recv.at[d - 1], at_line(z ^ d, core)) for d in (1, 2, 3)
    ]
    for copy in copies:
        copy.start()
    for d in (1, 2, 3):
        piece = ref.at[z ^ d]
        remote(piece, piece, send.at[d - 1], recv.at[d - 1], at_line(z ^ d, core)).wait_recv()
    for copy in copies:
        copy.wait_send()


class Weights:
    def __init__(self, src, dst, send, recv, own, row, z, core, turned, stride=0, start=0):
        self.src, self.dst, self.send, self.recv, self.own = src, dst, send, recv, own
        self.row, self.core, self.turned = row, core, turned
        self.stride, self.first = stride or src.shape[0], start
        self.sibling = {"col": 2 * z + (1 - core)}

    def spot(self, row, core):
        down, right = (row, core) if self.turned else (core, row)
        rows, cols = self.src.shape
        at = pl.ds(pl.multiple_of(down * self.stride + self.first, 16), rows)
        return self.dst.at[at, pl.ds(pl.multiple_of(right * cols, 128), cols)]

    def to_row(self, d):
        return remote(
            self.src, self.spot(self.row, self.core), self.send.at[d], self.recv.at[d], {"row": self.row ^ d}
        )

    def to_sibling(self, d):
        if d == 0:
            return remote(
                self.src, self.spot(self.row, self.core), self.send.at[0], self.recv.at[0], self.sibling
            )
        piece = self.spot(self.row ^ d, self.core)
        return remote(piece, piece, self.send.at[3 + d], self.recv.at[3 + d], self.sibling)

    def local(self):
        return pltpu.make_async_copy(self.src, self.spot(self.row, self.core), self.own)

    def start(self):
        for d in (1, 2, 3):
            self.to_row(d).start()
        self.to_sibling(0).start()
        self.local().start()

    def forward(self):
        for d in (1, 2, 3):
            piece = self.spot(self.row ^ d, self.core)
            remote(piece, piece, self.send.at[d], self.recv.at[d], {"row": self.row ^ d}).wait_recv()
            self.to_sibling(d).start()

    def finish(self):
        self.local().wait()
        for d in (0, 1, 2, 3):
            piece = self.spot(self.row ^ d, 1 - self.core)
            sem = 0 if d == 0 else 3 + d
            remote(piece, piece, self.send.at[sem], self.recv.at[sem], self.sibling).wait_recv()

    def sent(self):
        for d in (1, 2, 3):
            self.to_row(d).wait_send()
            self.to_sibling(d).wait_send()
        self.to_sibling(0).wait_send()


def gelu_parts(b):
    t = jnp.tanh(GELU_A * (b + GELU_B * (b * b * b)))
    half = 0.5 + 0.5 * t
    slope = half + (0.5 * b) * (1.0 - t * t) * (GELU_A + (3.0 * GELU_A * GELU_B) * (b * b))
    return b * half, slope


def eight(v):
    return jnp.sum(v.reshape(v.shape[0] // 8, 8, v.shape[1]), axis=0)


def fold(v):
    total = v[:, 0:128]
    for j in range(1, v.shape[1] // 128):
        total = total + v[:, j * 128 : (j + 1) * 128]
    return total


def tokens_of(ref, piece):
    return jnp.concatenate([ref[k, piece, :] for k in range(ref.shape[0])], axis=1)


def blocks(count, body):
    def one(i, carry):
        body(i)
        return carry

    lax.fori_loop(0, count, one, 0)


def scale_of(ref, eps, width):
    total = jnp.sum(jnp.sum(ref[...], axis=0), axis=0, keepdims=True)
    return lax.rsqrt(total / width + eps)


def forward_kernel(
    width, eps,
    x_in, g_in, segs, taps, offs, bias_r, bias_a, decay, mix, late, retain, admit, branch, recur, mn_s, gu_s, d_s,
    masks, par, gains, gates, coef, scale, scale_two, y_out, n1_out, q_out, x_out, g_out, b_out, p_out, u_out, r_out, i_out, h_out,
    result, dn2_out, dev_h, z_h, g_own, g_got, gd_own, gd_got, br_n, m_n,
    sums, sums2, sums3, vec, br_s, brn_s, m_s, vec_all, block_all, gates_hi, gates_lo, normed, normed2, go, x_own, y, dn2, q_c, p_s, h_s, room, uh, ul,
    own, held, held_n, held_o, gu, gun, down, dt, zs, dev,
    x_send, x_recv, x_loc, i_send, i_recv, i_loc, l_send, l_recv, n_send, n_recv, c_send, c_recv, g_send, g_recv, e_send, e_recv, f_send, f_recv,
    s_send, s_recv, t_send, t_recv, o_send, o_recv, w_send, w_recv, w_own, k_sem, v_sem, d_send, d_recv, d_own,
):
    row, z, core = place()
    block, seq = y.shape
    half = x_in.shape[0]
    chan = p_s.shape[0]
    hid = zs.shape[0]
    b_s, u_s, r_s, i_s, a_c = [room.at[n * chan : (n + 1) * chan, :] for n in range(5)]
    ev, dz = room.at[0 : 2 * hid, :], room.at[2 * hid : 3 * hid, :]
    hh = hid // 2
    hc = chan // 2
    sibling = {"col": 2 * z + (1 - core)}
    met = greet(row, z, core, True, True)
    br_s[0:hc, :] = branch[...].T
    br_s[hc:, :] = recur[...].T
    m_s[...] = mn_s[...].T
    br, mt = gun.at[0 : 2 * chan, 0:width], dt.at[:, 0:chan]
    wide = br_s.shape[0]
    recur_s, branch_s = br_s.at[wide // 2 :, :], br_s.at[0 : wide // 2, :]
    weights = [
        Weights(src, dst, w_send.at[n], w_recv.at[n], w_own.at[n], row, z, core, n in (2, 5), stride, start)
        for n, (src, dst, stride, start) in enumerate(
            (
                (recur_s, br, hc, 0),
                (branch_s, br, hc, chan),
                (m_s, mt, 0, 0),
                (gu_s, gu, 0, 0),
                (d_s, down, 0, 0),
                (brn_s, br_n, 0, 0),
                (mn_s, m_n, 0, 0),
            )
        )
    ]
    mine = pl.ds(pl.multiple_of(core * seq, seq), seq)
    other = pl.ds(pl.multiple_of((1 - core) * seq, seq), seq)
    inner = pl.ds(pl.multiple_of(z * block + core * half, 16), half)
    outer = rows_of(core, half)
    swaps = [
        remote(x_in.at[:, other], x_own.at[outer, :], x_send.at[0], x_recv.at[0], sibling),
        pltpu.make_async_copy(x_in.at[:, mine], x_own.at[outer, :], x_loc.at[0]),
    ]
    for k in range(PARTS):
        theirs, ours = [pl.ds(pl.multiple_of(c * seq + k * PART, 128), PART) for c in (1 - core, core)]
        swaps.append(remote(g_in.at[:, theirs], go.at[k, inner, :], i_send.at[k], i_recv.at[k], sibling))
        swaps.append(pltpu.make_async_copy(g_in.at[:, ours], go.at[k, inner, :], i_loc.at[k]))
    vec[...] = jnp.zeros(vec.shape, F32)
    vec[0:4, :] = taps[...]
    for n, one_row in enumerate((offs, bias_r, bias_a)):
        vec[4 + n : 5 + n, :] = one_row[...]
    rate = -decay[...]
    vec[7:8, :] = 8.0 * (jnp.maximum(rate, 0.0) + jnp.log1p(jnp.exp(-jnp.abs(rate))))
    vec[8:9, 0:half] = mix[...]
    vec[9:10, 0:half] = late[...]
    brn_s[:, 0:hc] = branch[...]
    brn_s[:, hc:] = recur[...]
    met()
    for w in weights[:3]:
        w.start()
    for swap in swaps:
        swap.start()
    trades = []
    for n, (src, dst) in enumerate(
        ((vec, vec_all.at[core]), (retain, block_all.at[core, 0]), (admit, block_all.at[core, 1]))
    ):
        trades.append(remote(src, dst, x_send.at[2 + n], x_recv.at[2 + n], sibling))
        trades.append(pltpu.make_async_copy(src, dst, x_loc.at[2 + n]))
    for trade in trades:
        trade.start()
    for swap in swaps + trades:
        swap.wait()
    flushes = [
        pltpu.make_async_copy(x_own, x_out, v_sem.at[0]),
        pltpu.make_async_copy(go.at[:, rows_of(z, block), :], g_out, v_sem.at[1]),
    ]
    for flush in flushes:
        flush.start()
    gather = Gather(normed, g_send, g_recv, z, core, block)
    gather_go = Gather(go, e_send, e_recv, z, core, block)
    gather_two = Gather(normed2, f_send, f_recv, z, core, block)
    shares = lambda k, s: own.at[k, s]
    shares_o = lambda k, s: normed.at[k, rows_of(s, block), :]
    spread = Spread(shares, held, s_send, s_recv, z, core)
    spread_n = Spread(shares, held_n, t_send, t_recv, z, core)
    spread_o = Spread(shares_o, held_o, o_send, o_recv, z, core)
    res = x_own
    gather_go.send(0, 0)
    gather_go.send(0, 1)
    for c in (0, 1):
        at = slice(c * hc, (c + 1) * hc)
        par[at, :] = vec_all[c].T
        gains[c * half : (c + 1) * half, :] = par[c * hc : c * hc + half, :]

    sums[z] = jnp.zeros(sums.shape[1:], F32)

    def squares(i):
        v = x_own[rows_of(i, 16), :].astype(F32)
        v = v * v
        sums[z] += v[:8] + v[8:]

    blocks(block // 16, squares)
    share_line(sums, l_send, l_recv, z, core)
    scale[...] = jnp.broadcast_to(scale_of(sums, eps, width), scale.shape)

    def norm(i):
        v = x_own[rows_of(i, 16), :].astype(F32) * scale[0:1, :] * gains[rows_of(i, 16), 8:9]
        v = v.astype(BF16)
        for k in range(PARTS):
            normed[k, pl.ds(pl.multiple_of(z * block + i * 16, 16), 16), :] = v[:, k * PART : (k + 1) * PART]

    blocks(block // 16, norm)
    gather.send(0, 0)
    gather.send(0, 1)
    p_s[:, PART:] = jnp.zeros((chan, 128), F32)
    h_s[:, PART:] = jnp.zeros((chan, 128), F32)
    pads = [
        pltpu.make_async_copy(src.at[:, PART:], out.at[:, 0:128], v_sem.at[2 + n])
        for n, (src, out) in enumerate(((p_s, p_out), (h_s, h_out)))
    ]
    for pad in pads:
        pad.start()
    gates[...] = jnp.zeros(gates.shape, BF16)
    gates_hi[...] = jnp.zeros(gates_hi.shape, BF16)
    gates_lo[...] = jnp.zeros(gates_lo.shape, BF16)
    per = retain.shape[0]
    tap = retain.shape[1]
    for c in (0, 1):
        for n in (0, 1):
            for e in range(per):
                w = block_all[c, n, e]
                at, far = slice(e * tap, (e + 1) * tap), slice(n * hc + e * tap, n * hc + (e + 1) * tap)
                gates[c, at, far] = w.astype(BF16)
                w = w.T
                high = w.astype(BF16)
                gates_hi[c, far, at] = high
                gates_lo[c, far, at] = (w - high.astype(F32)).astype(BF16)
    masks[...] = jnp.zeros(masks.shape, F32)
    here = jnp.broadcast_to(segs[:, mine], (8, seq))
    spot = lax.broadcasted_iota(jnp.int32, (8, seq), 1)
    for lag in (1, 2, 3):
        same = jnp.where((pltpu.roll(here, lag, 1) == here) & (spot >= lag), 1.0, 0.0)
        masks[lag : lag + 1, 0:seq] = same[0:1]
        if lag == 1:
            masks[0:1, 0:seq] = 1.0 - same[0:1]
    gather.forward(1, 0)
    gather.send(0, 2)
    gather_go.forward(1, 0)
    gather.forward(1, 1)
    gather.forward(2, 0)
    weights[0].forward()
    gather_go.forward(1, 1)
    gather_go.forward(2, 0)
    weights[1].forward()
    for w in weights[3:5]:
        w.start()
    gather_go.forward(2, 1)
    weights[0].finish()
    for pad in pads:
        pad.wait()

    kept = (b_s, p_s, u_s, r_s, i_s, h_s, q_c)
    outs = (b_out, p_out, u_out, r_out, i_out, h_out, q_out)

    def keep(n, part):
        if n in (1, 5):
            at = pl.ds(pl.multiple_of(128 + part * PART, 128), PART)
            return pltpu.make_async_copy(kept[n].at[:, 128:], outs[n].at[:, at], k_sem.at[n])
        return pltpu.make_async_copy(kept[n], outs[n].at[:, lanes(part)], k_sem.at[n])

    def put_shares(k, whole):
        for s in range(LINE):
            own[k, s] = whole[s * block : (s + 1) * block, :].astype(own.dtype)

    def work(k):
        here = lanes(k)

        @pl.when(k > 0)
        def _():
            for n in range(len(kept)):
                keep(n, k - 1).wait()

        p_s[:, 0:128] = p_s[:, PART:]
        h_s[:, 0:128] = h_s[:, PART:]
        p_s[:, 128:] = dot(br[0:chan, :], normed[k])

        def conv(i):
            ch = rows_of(i, 64)
            window = p_s[ch, :]
            pr = par[ch, :]
            u = pr[:, 4:5] + pr[:, 0:1] * window[:, 128:]
            for lag in (1, 2, 3):
                u = u + pr[:, lag : lag + 1] * (pltpu.roll(window, lag, 1)[:, 128:] * masks[lag : lag + 1, here])
            u_s[ch, :] = u
            high = u.astype(BF16)
            uh[ch, :] = high
            ul[ch, :] = (u - high.astype(F32)).astype(BF16)

        blocks(chan // 64, conv)
        gather.middle(k)
        for g in range(chan // 256):
            at = slice(g * 256, (g + 1) * 256)
            pre = dot(gates_hi[g], uh[at, :]) + dot(gates_hi[g], ul[at, :]) + dot(gates_lo[g], uh[at, :])
            r_s[at, :] = pre[:256]
            i_s[at, :] = pre[256:]

        def gated(i):
            ch = rows_of(i, 64)
            pr = par[ch, :]
            start = masks[0:1, here] > 0.5
            r = jax.nn.sigmoid(r_s[ch, :] + pr[:, 5:6])
            gate = jax.nn.sigmoid(i_s[ch, :] + pr[:, 6:7])
            r_s[ch, :] = r
            i_s[ch, :] = gate
            a = jnp.exp(-(r * pr[:, 7:8]))
            m = jnp.where(start, 1.0, jnp.sqrt(1.0 - a * a + FLOOR))
            a_c[ch, :] = jnp.where(start, 0.0, a)
            h_s[ch, 128:] = m * gate * u_s[ch, :]

        blocks(chan // 64, gated)
        first = lax.broadcasted_iota(jnp.int32, (128, PART), 1) == 0

        def recur(i):
            ch = rows_of(i, 128)
            a, h = a_c[ch, :], h_s[ch, 128:]
            h = h + jnp.where(first, a * h_s[ch, 0:128][:, 127:128], 0.0)
            a = jnp.where(first, 0.0, a)
            shift = 1
            while shift < PART:
                h = h + a * pltpu.roll(h, shift, 1)
                if shift * 2 < PART:
                    a = a * pltpu.roll(a, shift, 1)
                shift *= 2
            h_s[ch, 128:] = h

        blocks(chan // 128, recur)

        @pl.when(k == 0)
        def _():
            weights[2].forward()
            weights[1].finish()

        b_s[...] = dot(br[chan : 2 * chan, :], normed[k])

        def mixed(i):
            ch = rows_of(i, 64)
            b = b_s[ch, :]
            t = jnp.tanh(GELU_A * (b + GELU_B * (b * b * b)))
            q_c[ch, :] = (b * (0.5 + 0.5 * t) * h_s[ch, 128:]).astype(BF16)

        blocks(chan // 64, mixed)
        pl.when(k == 0)(weights[2].finish)
        put_shares(k, dot(mt[...], q_c[...]))
        for n in range(len(kept)):
            keep(n, k).start()

    def finish(k, total):
        def add(i):
            at = pl.multiple_of(i * 64, 64)
            y[pl.ds(at, 64), lanes(k)] = x_own[pl.ds(at, 64), lanes(k)].astype(F32) + total(at, 64)

        blocks(block // 64, add)

    def square(k):
        sums2[k, z] = jnp.zeros(sums2.shape[2:], F32)

        def one(i):
            v = y[rows_of(i, 64), lanes(k)]
            sums2[k, z] += eight(v * v)

        blocks(block // 64, one)
        for d in (1, 2, 3):
            share(k, d).start()

    def share(k, d):
        return remote(
            sums2.at[k, z], sums2.at[k, z], n_send.at[k, d - 1], n_recv.at[k, d - 1], at_line(z ^ d, core)
        )

    def norm_two(k):
        for d in (1, 2, 3):
            piece = sums2.at[k, z ^ d]
            remote(piece, piece, n_send.at[k, d - 1], n_recv.at[k, d - 1], at_line(z ^ d, core)).wait_recv()
        s2 = scale_of(sums2.at[k], eps, width)
        scale_two[:, lanes(k)] = jnp.broadcast_to(s2, (8, PART))

        def one(i):
            at = rows_of(i, 64)
            v = y[at, lanes(k)] * scale_two[0:1, lanes(k)] * gains[at, 9:10]
            normed2[k, pl.ds(pl.multiple_of(z * block + i * 64, 64), 64), :] = v.astype(BF16)

        blocks(block // 64, one)

    def turn_down(i):
        at = pl.ds(pl.multiple_of(i * 128, 128), 128)
        dt[:, at] = down[at, :].T

    def turn_up(i):
        at = pl.ds(pl.multiple_of(i * 128, 128), 128)
        gun[:, at] = gu[at, :].T

    def step(t, carry):
        gather.arrive(2, t)
        work(t)
        spread.serve(t, finish)
        pl.when(t >= 3)(lambda: square(t - 3))
        pl.when(t >= 4)(lambda: norm_two(t - 4))
        pl.when((t >= 4) & (t < 7))(lambda: gather_two.send(0, t - 4))
        pl.when((t >= 6) & (t < 8))(lambda: gather_two.forward(1, t - 6))
        pl.when(t == 5)(weights[3].forward)
        return carry

    lax.fori_loop(0, PARTS, step, 0)
    for w in weights[:3]:
        w.sent()
    for w in weights[5:]:
        w.start()
    for n in range(len(kept)):
        keep(n, PARTS - 1).wait()
    flush_n = pltpu.make_async_copy(normed, n1_out, v_sem.at[4])
    flush_n.start()
    gather_go.send(0, 2)
    gather_go.send(0, 3)
    spread.serve(PARTS, finish)
    square(PARTS - 3)
    norm_two(PARTS - 4)
    gather_two.forward(2, 0)
    weights[4].forward()
    spread.serve(PARTS + 1, finish)
    square(PARTS - 2)
    norm_two(PARTS - 3)
    gather_go.forward(1, 2)
    weights[4].finish()
    blocks(hid // 128, turn_down)
    spread.serve(PARTS + 2, finish)
    square(PARTS - 1)
    norm_two(PARTS - 2)
    gather.sent()
    for flush in flushes + [flush_n]:
        flush.wait()
    weights[3].finish()
    blocks(2 * hid // 128, turn_up)
    norm_two(PARTS - 1)

    def keep_dev(k):
        return pltpu.make_async_copy(dev, dev_h.at[:, lanes(k)], v_sem.at[5])

    def keep_z(k):
        return pltpu.make_async_copy(zs, z_h.at[:, lanes(k)], v_sem.at[6])

    def feed(k):

        @pl.when(k > 0)
        def _():
            keep_dev(k - 1).wait()
            keep_z(k - 1).wait()

        ev[...] = dot(gu[...], normed2[k])
        gather_two.middle(k)
        gather_go.middle(k, 2)
        gather_go.arrive(2, k)
        dz[...] = dot(down[...], go[k])
        for c in range(2):

            def one(i):
                off = pl.multiple_of(i * 64, 64)
                e = ev[pl.ds(c * 2 * hh + off, 64), :]
                v = ev[pl.ds(c * 2 * hh + hh + off, 64), :]
                d = dz[pl.ds(c * hh + off, 64), :]
                act, slope = gelu_parts(e)
                zs[pl.ds(c * hh + off, 64), :] = (act * v).astype(BF16)
                dev[pl.ds(c * 2 * hh + off, 64), :] = (d * v * slope).astype(BF16)
                dev[pl.ds(c * 2 * hh + hh + off, 64), :] = (d * act).astype(BF16)

            blocks(hh // 64, one)
        put_shares(k, dot(gun[...], dev[...]))
        spread_n.serve(k, finish_n)
        normed[k] = dot(dt[...], zs[...]).astype(BF16)
        spread_o.serve(k, finish_o)
        keep_dev(k).start()
        keep_z(k).start()

    def finish_o(k, total):
        def add(i):
            at = pl.multiple_of(i * 64, 64)
            res[pl.ds(at, 64), lanes(k)] = (y[pl.ds(at, 64), lanes(k)] + total(at, 64)).astype(BF16)

        blocks(block // 64, add)

    def keep_n(k):
        return pltpu.make_async_copy(dn2, dn2_out.at[:, lanes(k)], v_sem.at[3])

    def finish_n(k, total):
        @pl.when(k > 0)
        def _():
            keep_n(k - 1).wait()

        sums3[k, z] = jnp.zeros(sums3.shape[2:], F32)

        def add(i):
            at = pl.multiple_of(i * 64, 64)
            d = total(at, 64)
            dn2[pl.ds(at, 64), :] = d
            sums3[k, z] += eight(d * y[pl.ds(at, 64), lanes(k)] * gains[pl.ds(at, 64), 9:10])

        blocks(block // 64, add)
        keep_n(k).start()
        for d in (1, 2, 3):
            share_c(k, d).start()

    def share_c(k, d):
        return remote(
            sums3.at[k, z], sums3.at[k, z], c_send.at[k, d - 1], c_recv.at[k, d - 1], at_line(z ^ d, core)
        )

    def feed_step(t, carry):
        gather_two.arrive(2, t)
        feed(t)
        pl.when(t == 4)(weights[5].forward)
        pl.when(t == 6)(weights[6].forward)
        return carry

    lax.fori_loop(0, PARTS, feed_step, 0)
    for w in weights[3:5]:
        w.sent()
    keep_dev(PARTS - 1).wait()
    keep_z(PARTS - 1).wait()
    dev_all, z_all = gu.at[:, 0:seq], dt.at[0:hid, 0:seq]
    loads = [pltpu.make_async_copy(dev_h, dev_all, v_sem.at[5]), pltpu.make_async_copy(z_h, z_all, v_sem.at[6])]
    for load in loads:
        load.start()
    for load in loads:
        load.wait()

    def columns(start):
        return pl.ds(pl.multiple_of(start, 128), block)

    def place_up(j):
        side = jnp.where(j >= 3, core, 1 - core)
        return side * hid + (j % 3) * block, columns((j % 3) * block)

    def send_up(j):
        at, to = place_up(j)
        return remote(gun.at[:, columns(at)], g_got.at[:, to], d_send.at[j], d_recv.at[j], sibling)

    def keep_up(j):
        at, to = place_up(j)
        return pltpu.make_async_copy(gun.at[:, columns(at)], g_own.at[:, to], d_own.at[j - 3])

    def send_down():
        return remote(down.at[rows_of(1 - core, hh), :], gd_got, d_send.at[3], d_recv.at[3], sibling)

    def keep_down():
        return pltpu.make_async_copy(down.at[rows_of(core, hh), :], gd_own, d_own.at[3])

    def grad_up(j):
        at = place_up(j)[0]
        right = pl.ds(pl.multiple_of(at, 16), block)
        for low in (0, width // 2):
            piece = slice(low, low + width // 2)
            gun[piece, columns(at)] = dot_nt(tokens_of(normed2, piece), dev_all[right, :]).astype(BF16)

        @pl.when(j < 3)
        def _():
            send_up(j).start()

        @pl.when(j >= 3)
        def _():
            keep_up(j).start()

    def grad_down(side):
        at = rows_of(side, hh)
        for low in range(0, width, 2 * block):
            piece = slice(low, low + 2 * block)
            down[at, piece] = dot_nt(z_all[at, :], tokens_of(go, piece)).astype(BF16)

    def drain(i, carry):
        t = PARTS + i
        blocks(2, lambda j: grad_up(2 * i + j))
        spread_n.serve(t, finish_n)
        spread_o.serve(t, finish_o)

        @pl.when(i < 2)
        def _():
            grad_down(jnp.where(i == 0, 1 - core, core))

        pl.when(i == 0)(lambda: send_down().start())
        pl.when(i == 1)(lambda: keep_down().start())
        return carry

    lax.fori_loop(0, LINE - 1, drain, 0)
    last = [
        remote(res.at[rows_of(1 - core, half), :], result.at[:, mine], x_send.at[0], x_recv.at[0], sibling),
        pltpu.make_async_copy(res.at[rows_of(core, half), :], result.at[:, mine], x_loc.at[0]),
        pltpu.make_async_copy(y, y_out, v_sem.at[2]),
        keep_n(PARTS - 1),
    ]
    for copy in last[:3]:
        copy.start()
    for w in weights[5:]:
        w.finish()
        w.sent()
    for one in (gather_go, gather_two, spread, spread_n, spread_o):
        one.sent()
    for k in range(PARTS):
        for d in (1, 2, 3):
            share(k, d).wait_send()
            share_c(k, d).wait_send()
            piece = sums3.at[k, z ^ d]
            remote(piece, piece, c_send.at[k, d - 1], c_recv.at[k, d - 1], at_line(z ^ d, core)).wait_recv()
        total = jnp.sum(jnp.sum(sums3[k], axis=0), axis=0, keepdims=True)
        at = slice(k * PART, (k + 1) * PART)
        s2 = scale_two[:, at]
        coef[:, at] = s2 * s2 * s2 * (total / width)
    for j in range(3):
        keep_up(j + 3).wait()
        send_up(j).wait()
    keep_down().wait()
    send_down().wait()
    for copy in last:
        copy.wait()


def back_kernel(
    width,
    y, dn2_h, g_h, x_own, scale_two, scale_one, coef_two, gains, masks, par, gates_t, m_h, br_h,
    b_h, p_h, u_h, r_h, i_h, h_h, q_h, n1_h, f_own, f_got, fd_own, fd_got,
    input_grad, tiny_v, tiny_g, f_sum, f_land, fd_sum, fd_land, g_sum, g_land, gm_sum, gm_land,
    sums, coef, m_n, br_n, b_s, p_s, u_s, r_s, i_s, h_s, dyf, dbp, dy, dn1, dq, du, dri, a_c, l_c, carry_s, own, held,
    qv, n1, f_a, f_b, fd_a, fd_b, feed_part, mix_part, small, gate_grad, g_s, g_got, gm_got,
    vec, vec_in, vec_all, gd, gd_in, gd_all,
    c_sem, k_sem, l_send, l_recv, g_send, g_recv, s_send, s_recv, r_send, r_recv,
    f_sem, f_send, f_recv, d_send, d_recv, d_own, q_send, q_recv, n_send, n_recv, v_send, v_recv,
):
    row, z, core = place()
    block, seq = y.shape
    PART, PARTS = LATE, seq // LATE

    def lanes(part):
        return pl.ds(pl.multiple_of(part * PART, PART), PART)

    half = block // 2
    chan = b_s.shape[1]
    hc = chan // 2
    sibling = {"col": 2 * z + (1 - core)}
    met = greet(row, z, core, True, True)
    load_g = pltpu.make_async_copy(g_h, g_s, c_sem.at[0])
    load_g.start()
    dn2 = dn1
    load_d = pltpu.make_async_copy(dn2_h, dn2, c_sem.at[5])
    load_d.start()
    load_m = pltpu.make_async_copy(m_h, m_n, c_sem.at[1])
    load_m.start()
    load_b = pltpu.make_async_copy(br_h, br_n, c_sem.at[2])
    load_b.start()
    load_q = pltpu.make_async_copy(q_h, qv, c_sem.at[3])
    load_n = pltpu.make_async_copy(n1_h, n1, c_sem.at[4])
    kept = (b_s, p_s, u_s, r_s, i_s, h_s)
    srcs = (b_h, p_h, u_h, r_h, i_h, h_h)

    def fetch(n, part):
        if kept[n] is p_s or kept[n] is h_s:
            at = pl.ds(pl.multiple_of(part * PART, 128), PART + 128)
        else:
            at = lanes(part)
        return pltpu.make_async_copy(srcs[n].at[:, at], kept[n].at[part % 2], k_sem.at[n, part % 2])

    def fetch_all(part):
        for n in range(len(kept)):
            fetch(n, part).start()

    fetch_all(PARTS - 1)
    load_q.start()
    load_n.start()
    du[:, 0:128] = jnp.zeros((chan, 128), F32)
    carry_s[...] = jnp.zeros(carry_s.shape, F32)
    small[...] = jnp.zeros(small.shape, F32)
    gate_grad[...] = jnp.zeros(gate_grad.shape, F32)

    load_d.wait()
    load_g.wait()
    gather = Gather(dyf, g_send, g_recv, z, core, block, back=True)

    def outer(part):
        here = slice(part * PART, (part + 1) * PART)

        def one(i):
            at = rows_of(i, 64)
            s2 = scale_two[0:1, here]
            d, v = dn2[at, here], y[at, here]
            w = fold(d * v * s2)
            feed_part[at, :] = w if part == PARTS - 1 else feed_part[at, :] + w
            few = PART // g_s.shape[2]
            g = jnp.concatenate([g_s[part * few + j, at, :] for j in range(few)], axis=1)
            v = g.astype(F32) + (s2 * (gains[at, 9:10] * d) - v * coef_two[0:1, here])
            dy[at, here] = v
            dyf[part, pl.ds(pl.multiple_of(z * block + i * 64, 64), 64), :] = v.astype(BF16)

        blocks(block // 64, one)

    outer(PARTS - 1)
    met()
    gather.send(0, 0)
    outer(PARTS - 2)
    gather.send(0, 1)
    outer(PARTS - 3)
    gather.forward(1, 0)
    gather.send(0, 2)
    for part in range(PARTS - 3):
        outer(part)
    gather.forward(1, 1)
    gather.forward(2, 0)
    spread = Spread(lambda k, s: own.at[k, s], held, s_send, s_recv, z, core)
    load_m.wait()
    load_b.wait()
    final = lax.broadcasted_iota(jnp.int32, (128, PART), 1) == PART - 1

    f_arrays = ((f_own, f_got, f_a, f_b, f_sum, f_land), (fd_own, fd_got, fd_a, fd_b, fd_sum, fd_land))

    def f_loads(d):
        pulls = []
        for n, (ours, theirs, a, b, _, _) in enumerate(f_arrays):
            if n == 0:
                piece = (rows_of(row ^ d, block), slice(None))
            else:
                piece = (slice(None), pl.ds(pl.multiple_of((row ^ d) * block, 128), block))
            pulls.append(pltpu.make_async_copy(ours.at[piece], a.at[d], f_sem.at[n, 0]))
            pulls.append(pltpu.make_async_copy(theirs.at[piece], b, f_sem.at[n, 1]))
        return pulls

    def f_out(d):
        outs = []
        for n, (_, _, a, _, kept_at, land) in enumerate(f_arrays):
            if d == 0:
                outs.append(pltpu.make_async_copy(a.at[0], kept_at, f_send.at[n, 0]))
            else:
                outs.append(
                    remote(a.at[d], land.at[d - 1], f_send.at[n, d], f_recv.at[n, d], {"row": row ^ d})
                )
        return outs

    def f_part(d):
        for pull in f_loads(d):
            pull.wait()
        for _, _, a, b, _, _ in f_arrays:

            def add(i):
                at = rows_of(i, 64)
                a[d, at, :] = (a[d, at, :].astype(F32) + b[at, :].astype(F32)).astype(BF16)

            blocks(b.shape[0] // 64, add)
        for out in f_out(d):
            out.start()
        if d > 0:
            for pull in f_loads(d - 1):
                pull.start()

    def f_step(t):
        for d in range(LINE):
            pl.when(t == LINE - 1 - d)(functools.partial(f_part, d))

    for pull in f_loads(LINE - 1):
        pull.start()

    lru = hc

    def send_m():
        return remote(m_n.at[rows_of(1 - core, lru), :], gm_got, d_send.at[1], d_recv.at[1], sibling)

    def work(t):
        k = PARTS - 1 - t
        here = lanes(k)
        wide = pl.ds(pl.multiple_of(k * PART, 128), PART + 128)
        slot = k % 2
        for n in range(len(kept)):
            fetch(n, k).wait()

        @pl.when(k > 0)
        def _():
            fetch_all(k - 1)

        dq[...] = dot(m_n[...], dyf[k])

        @pl.when(t == PARTS - 1)
        def _():
            load_q.wait()
            for low in range(0, width, 2 * block):
                piece = slice(low, low + 2 * block)
                m_n[:, piece] = dot_nt(qv[...], tokens_of(dyf, piece)).astype(BF16)
            send_m().start()

        def before(i):
            ch = rows_of(i, 64)
            c = i // (hc // 64)
            low = pl.ds(pl.multiple_of(c * hc + i * 64, 64), 64)
            pr = par[ch, :]
            d = dq[ch, :]
            act, slope = gelu_parts(b_s[slot, ch, :])
            dbp[low, here] = (d * h_s[slot, ch, :][:, 128:] * slope).astype(BF16)
            l_c[ch, :] = d * act
            a_c[ch, :] = jnp.exp(-(r_s[slot, ch, :] * pr[:, 7:8]))

        blocks(chan // 64, before)
        gather.middle(t)

        def recur(i):
            ch = rows_of(i, 128)
            start = masks[0:1, here] > 0.5
            a, lam = jnp.where(start, 0.0, a_c[ch, :]), l_c[ch, :]
            lam = lam + jnp.where(final, carry_s[ch, :][:, 0:1], 0.0)
            w = jnp.where(final, 0.0, pltpu.roll(a, PART - 1, 1))
            shift = 1
            while shift < PART:
                lam = lam + w * pltpu.roll(lam, PART - shift, 1)
                if shift * 2 < PART:
                    w = w * pltpu.roll(w, PART - shift, 1)
                shift *= 2
            carry_s[ch, :] = jnp.broadcast_to((a * lam)[:, 0:1], (128, 128))
            l_c[ch, :] = lam

        blocks(chan // 128, recur)
        f_step(t)

        def after(i):
            ch = rows_of(i, 64)
            du[ch, PART:] = du[ch, 0:128]
            pr = par[ch, :]
            start = masks[0:1, here] > 0.5
            lam, a0 = l_c[ch, :], a_c[ch, :]
            earlier = pltpu.roll(h_s[slot, ch, :], 1, 1)[:, 128:]
            r, gate, u = r_s[slot, ch, :], i_s[slot, ch, :], u_s[slot, ch, :]
            m0 = jnp.sqrt(1.0 - a0 * a0 + FLOOR)
            m = jnp.where(start, 1.0, m0)
            lm = lam * m
            lu = lam * u
            du[ch, 0:PART] = lm * gate
            da = jnp.where(start, 0.0, lam * earlier - (lu * gate) * (a0 / m0)) * a0
            dr = da * (-pr[:, 7:8]) * (r * (1.0 - r))
            di = lu * m * (gate * (1.0 - gate))
            g, o = i // 4, (i % 4) * 64
            dri[pl.ds(pl.multiple_of(g * 512 + o, 64), 64), :] = dr.astype(BF16)
            dri[pl.ds(pl.multiple_of(g * 512 + 256 + o, 64), 64), :] = di.astype(BF16)
            small[5, ch, :] += fold(dr)
            small[6, ch, :] += fold(di)
            small[7, ch, :] += fold(da * r)

        blocks(chan // 64, after)
        for g in range(chan // 256):
            at = slice(g * 256, (g + 1) * 256)
            dd = dri[g * 512 : (g + 1) * 512, :]
            du[at, 0:PART] += dot(gates_t[g], dd)
            gate_grad[g] += dot_nt(u_s[slot, at, :].astype(BF16), dd)

        def conv(i):
            ch = rows_of(i, 64)
            c = i // (hc // 64)
            low = pl.ds(pl.multiple_of((c + 1) * hc + i * 64, 64), 64)
            pr = par[ch, :]
            follow = du[ch, :]
            window = p_s[slot, ch, :]
            d = follow[:, :PART]
            dp = pr[:, 0:1] * d
            small[4, ch, :] += fold(d)
            small[0, ch, :] += fold(d * window[:, 128:])
            for lag in (1, 2, 3):
                kd = follow * masks[lag : lag + 1, wide]
                dp = dp + pr[:, lag : lag + 1] * pltpu.roll(kd, PART + 128 - lag, 1)[:, :PART]
                small[lag, ch, :] += fold(kd[:, :PART] * pltpu.roll(window, lag, 1)[:, 128:])
            dbp[low, here] = dp.astype(BF16)

        blocks(chan // 64, conv)
        whole = dot(br_n[...], dbp[:, here])
        for s in range(LINE):
            own[t, s] = whole[s * block : (s + 1) * block, :].astype(own.dtype)

    def finish(t, total):
        k = PARTS - 1 - t

        sums[k, z] = jnp.zeros(sums.shape[2:], F32)

        @pl.when(t == 0)
        def _():
            mix_part[...] = jnp.zeros(mix_part.shape, F32)

        def add(i):
            at = pl.ds(pl.multiple_of(i * 64, 64), 64)
            d = total(pl.multiple_of(i * 64, 64), 64)
            dn1[at, lanes(k)] = d
            w = d * x_own[at, lanes(k)].astype(F32)
            sums[k, z] += eight(w * gains[at, 8:9])
            w = w * scale_one[0:1, lanes(k)]
            mix_part[at, :] += fold(w)

        blocks(block // 64, add)
        for d in (1, 2, 3):
            share(k, d).start()

    def share(k, d):
        return remote(sums.at[k, z], sums.at[k, z], l_send.at[k, d - 1], l_recv.at[k, d - 1], at_line(z ^ d, core))

    def step(t, carry):
        gather.arrive(2, t)
        work(t)
        spread.serve(t, finish)
        return carry

    lax.fori_loop(0, PARTS, step, 0)
    load_n.wait()


    def cols_of(side):
        return pl.ds(pl.multiple_of(side * 2 * lru, 128), 2 * lru)

    def send_br():
        return remote(br_n.at[:, cols_of(1 - core)], g_got, d_send.at[0], d_recv.at[0], sibling)

    def grad_br(side):
        for low in range(0, width, 2 * block):
            piece = slice(low, low + 2 * block)
            br_n[piece, cols_of(side)] = dot_nt(tokens_of(n1, piece), dbp[rows_of(side, 2 * lru), :]).astype(BF16)

    def out_br(d):
        piece = br_n.at[rows_of(row ^ d, block), cols_of(core)]
        if d == 0:
            return pltpu.make_async_copy(piece, g_sum, d_own.at[0])
        return remote(piece, g_land.at[d - 1], q_send.at[0, d - 1], q_recv.at[0, d - 1], {"row": row ^ d})

    def out_m(d):
        piece = m_n.at[rows_of(core, lru), pl.ds(pl.multiple_of((row ^ d) * block, 128), block)]
        if d == 0:
            return pltpu.make_async_copy(piece, gm_sum, d_own.at[1])
        return remote(piece, gm_land.at[d - 1], q_send.at[1, d - 1], q_recv.at[1, d - 1], {"row": row ^ d})

    def drain(i, carry):
        t = PARTS + i

        @pl.when(i == 0)
        def _():
            grad_br(1 - core)
            send_br().start()
            send_m().wait_recv()

            def add(j):
                at = rows_of(j, 64)
                to = pl.ds(pl.multiple_of(core * lru + j * 64, 64), 64)
                m_n[to, :] = (m_n[to, :].astype(F32) + gm_got[at, :].astype(F32)).astype(BF16)

            blocks(lru // 64, add)
            for d in (3, 2, 1, 0):
                out_m(d).start()
            grad_br(core)

        @pl.when(i == 1)
        def _():
            send_br().wait_recv()

            def add(j):
                at = rows_of(j, 64)
                br_n[at, cols_of(core)] = (br_n[at, cols_of(core)].astype(F32) + g_got[at, :].astype(F32)).astype(BF16)

            blocks(width // 64, add)
            for d in (3, 2, 1, 0):
                out_br(d).start()
        spread.serve(t, finish)
        return carry

    lax.fori_loop(0, LINE - 1, drain, 0)
    mine = pl.ds(pl.multiple_of(core * seq, seq), seq)
    for side in (0, 1):
        for e in range(4):
            at = slice(e * 64, (e + 1) * 64)
            gd[side, at, 0:64] = gate_grad[side, at, e * 64 : (e + 1) * 64]
            gd[side, at, 64:128] = gate_grad[side, at, 256 + e * 64 : 256 + (e + 1) * 64]
    swap_gd = remote(gd.at[1 - core], gd_in, v_send.at[0], v_recv.at[0], sibling)
    swap_gd.start()
    lane = lax.broadcasted_iota(jnp.int32, (64, 128), 1)

    def columns(parts, at):
        total = jnp.zeros((64, 128), F32)
        for n, part in enumerate(parts):
            total = total + jnp.where(lane == n, jnp.sum(part(at), axis=1, keepdims=True), 0.0)
        return total

    vec[...] = jnp.zeros(vec.shape, F32)
    for j in range(chan // 64):
        at = slice(j * 64, (j + 1) * 64)
        v = columns([lambda at, n=n: small[n, at, :] for n in range(8)], at)
        vec[0, :, at] = v.T[0:8, :]

    for k in range(PARTS):
        for d in (1, 2, 3):
            share(k, d).wait_send()
            piece = sums.at[k, z ^ d]
            remote(piece, piece, l_send.at[k, d - 1], l_recv.at[k, d - 1], at_line(z ^ d, core)).wait_recv()
        total = jnp.sum(jnp.sum(sums[k], axis=0), axis=0, keepdims=True)
        at = slice(k * PART, (k + 1) * PART)
        s1 = scale_one[:, at]
        coef[:, at] = s1 * s1 * s1 * (total / width)

    def last(i):
        at = rows_of(i, 16)
        v = dy[at, :] + (
            scale_one[0:1, :] * (gains[at, 8:9] * dn1[at, :]) - x_own[at, :].astype(F32) * coef[0:1, :]
        )
        dy[at, :] = v

    blocks(block // 16, last)
    back = remote(dy.at[rows_of(1 - core, half), :], input_grad.at[:, mine], r_send, r_recv, sibling)
    back.start()
    keep_in = pltpu.make_async_copy(dy.at[rows_of(core, half), :], input_grad.at[:, mine], d_own.at[3])
    keep_in.start()
    for j in range(block // 64):
        at = slice(j * 64, (j + 1) * 64)
        v = columns([lambda at: mix_part[at, :], lambda at: feed_part[at, :]], at)
        vec[1, :, at] = v.T[0:8, :]
    swap_vec = remote(vec, vec_in, v_send.at[1], v_recv.at[1], sibling)
    swap_vec.start()
    swap_gd.wait()
    gd_all[0] = gd[core] + gd_in[...]
    rows_gd = [
        remote(gd_all.at[0], gd_all.at[d], n_send.at[0, d - 1], n_recv.at[0, d - 1], {"row": row ^ d}) for d in (1, 2, 3)
    ]
    for copy in rows_gd:
        copy.start()
    swap_vec.wait()
    vec_all[0] = vec[...] + vec_in[...]
    rows_vec = [
        remote(vec_all.at[0], vec_all.at[d], n_send.at[1, d - 1], n_recv.at[1, d - 1], {"row": row ^ d}) for d in (1, 2, 3)
    ]
    for copy in rows_vec:
        copy.start()
    spread.sent()
    gather.sent()
    for copy in rows_gd + rows_vec:
        copy.wait()
    for every, out in ((gd_all, tiny_g), (vec_all, tiny_v)):
        first, second = every[row % 2], every[1 - row % 2]
        third, fourth = every[2 + row % 2], every[3 - row % 2]
        out[...] = (first + second) + (third + fourth)
    for d in range(LINE):
        for out in f_out(d):
            out.wait()
    send_br().wait_send()
    send_m().wait_send()
    for d in (0, 1, 2, 3):
        out_br(d).wait()
        out_m(d).wait()
    for copy in (keep_in, back):
        copy.wait()


def last_kernel(
    f_sum, f_land, fd_sum, fd_land, g_sum, g_land, gm_sum, gm_land, result_in, grad_in, tiny_v, tiny_g, lambdas,
    s_b, s_r, s_m, s_g, s_u, s_d, result, input_grad, taps, offs, bias_r, bias_a, decay, mix, feed, retain, admit,
):
    lru, ff, half = s_b.shape[1], s_g.shape[0], mix.shape[1]

    def four(first, others):
        return first[...].astype(F32) + others[0].astype(F32) + (others[1].astype(F32) + others[2].astype(F32))

    v = four(f_sum, f_land)
    s_g[...] = v.T[:ff, :]
    s_u[...] = v.T[ff:, :]
    v = four(g_sum, g_land)
    s_b[...] = v[:, :lru]
    s_r[...] = v[:, lru:]
    s_d[...] = four(fd_sum, fd_land)
    result[...] = result_in[...]
    input_grad[...] = grad_in[...]

    @pl.when(pl.program_id(0) == 0)
    def _():
        core = place()[2]
        s_m[...] = four(gm_sum, gm_land)
        small = tiny_v[0, :, pl.ds(pl.multiple_of(core * lru, 128), lru)]
        taps[...] = small[0:4]
        offs[...] = small[4:5]
        bias_r[...] = small[5:6]
        bias_a[...] = small[6:7]
        decay[...] = small[7:8] * (8.0 * jax.nn.sigmoid(-lambdas[...]))
        gains = jnp.where(core == 0, tiny_v[1, :, 0:half], tiny_v[1, :, half : 2 * half])
        mix[...] = gains[0:1]
        feed[...] = gains[1:2]
        for e in range(retain.shape[0]):
            at = slice(e * 64, (e + 1) * 64)
            retain[e] = tiny_g[at, 0:64]
            admit[e] = tiny_g[at, 64:128]


ANY = pl.BlockSpec(memory_space=pl.ANY)
VM = pl.BlockSpec(memory_space=pltpu.VMEM)
DMA = pltpu.SemaphoreType.DMA
ROOM = 62 * 1024 * 1024


def shape(dims, kind):
    return jax.ShapeDtypeStruct(dims, kind)


def call(kernel, ins, outs, scratch, ident, name, flops):
    return pl.pallas_call(
        kernel,
        out_shape=[o[0] for o in outs],
        in_specs=ins,
        out_specs=[o[1] for o in outs],
        scratch_shapes=scratch,
        name=name,
        compiler_params=pltpu.CompilerParams(
            collective_id=ident, has_side_effects=True, vmem_limit_bytes=ROOM
        ),
        cost_estimate=pl.CostEstimate(flops=flops, bytes_accessed=40000000, transcendentals=0),
    )


def fast_body(
    inputs, segments, mix_gain, branch_weight, recur_weight, kernel, offsets, retain_weight, retain_bias,
    admit_weight, admit_bias, lambdas, merge_weight, feed_gain, gate_weight, up_weight, down_weight, cotangent,
):
    half, tokens = inputs.shape
    block, seq, width = 2 * half, tokens // 2, D
    lru, heads = branch_weight.shape[1], retain_weight.shape[0]
    chan = 2 * lru
    ff = gate_weight.shape[1]
    hid = 2 * ff
    rows = branch_weight.shape[0]
    cols = merge_weight.shape[1]
    gu_s = jnp.concatenate([gate_weight, up_weight], axis=1).T

    f_tok = lambda n, kind=F32: shape((n, seq), kind)
    padded = (shape((chan, 128 + seq), F32), ANY)
    state = [(f_tok(chan), ANY), padded, *[(f_tok(chan), ANY)] * 3, padded]
    line = [DMA((3,)), DMA((3,))]
    steps = [DMA((2, 3, PARTS)), DMA((2, 3, PARTS))]
    sums = [DMA((2, PARTS, LINE)), DMA((2, PARTS, LINE))]
    held = pltpu.VMEM((PARTS, LINE + 1, block, PART), BF16)
    own_low = pltpu.VMEM((PARTS, LINE, block, PART), BF16)
    tok = lambda n, kind=F32, lead=0: pltpu.VMEM((n, lead + seq), kind)
    one = lambda n, kind=F32, lead=0: pltpu.VMEM((n, lead + PART), kind)
    grad_gu, grad_d = (shape((width, 2 * ff), BF16), ANY), (shape((ff, width), BF16), ANY)
    low = lambda n, m: (shape((n, m), BF16), ANY)
    parted = lambda n: (shape((PARTS, n, PART), BF16), ANY)
    by_part = lambda n: pltpu.VMEM((PARTS, n, PART), BF16)

    (masks, par, gains, gates, coef, scale_one, scale_two, y, n1, q, x_own, g, b, p, u, r, i, h, result, dn2, _, _, f_own, f_got, fd_own, fd_got,
     br_n, m_n) = call(
        functools.partial(forward_kernel, width, EPS),
        [ANY] * 2 + [VM] * 13 + [ANY] * 2,
        [(shape((8, seq + 128), F32), VM), (shape((chan, 16), F32), VM), (shape((block, 16), F32), VM), (shape((2, lru, 2 * lru), BF16), VM),
         (f_tok(8), VM), (f_tok(8), VM), (f_tok(8), VM), (f_tok(block), ANY), parted(width), low(chan, seq), low(block, seq), parted(block)]
        + state + [low(half, tokens), (f_tok(block), ANY), low(2 * hid, seq), low(hid, seq), grad_gu, grad_gu, grad_d, grad_d,
                   low(width, 2 * chan), low(chan, width)],
        [pltpu.VMEM((LINE, 8, seq), F32), pltpu.VMEM((PARTS, LINE, 8, PART), F32), pltpu.VMEM((PARTS, LINE, 8, PART), F32),
         pltpu.VMEM((16, lru), F32), pltpu.VMEM((2 * lru, rows), BF16), pltpu.VMEM((rows, 2 * lru), BF16), pltpu.VMEM((cols, lru), BF16),
         pltpu.VMEM((2, 16, lru), F32), pltpu.VMEM((2, 2) + retain_weight.shape, F32), pltpu.VMEM((2, 2 * lru, lru), BF16),
         pltpu.VMEM((2, 2 * lru, lru), BF16), by_part(width), by_part(width),
         by_part(width), tok(block, BF16), tok(block), one(block), one(chan, BF16),
         one(chan, F32, 128), one(chan, F32, 128), one(max(5 * chan, 3 * hid)), one(chan, BF16), one(chan, BF16),
         own_low, held, held, held, pltpu.VMEM((2 * hid, width), BF16), pltpu.VMEM((width, 2 * hid), BF16),
         pltpu.VMEM((hid, width), BF16), pltpu.VMEM((width, hid), BF16), one(hid, BF16), one(2 * hid, BF16),
         DMA((5,)), DMA((5,)), DMA((5,)), DMA((PARTS,)), DMA((PARTS,)), DMA((PARTS,))] + line + [DMA((PARTS, 3)), DMA((PARTS, 3))] * 2 + steps * 3 + sums * 3
        + [DMA((7, 7)), DMA((7, 7)), DMA((7,)), DMA((7,)), DMA((7,)), DMA((4,)), DMA((4,)), DMA((4,))],
        0, "forward", 50 * 10**9,
    )(inputs, cotangent, segments[None, :], kernel, offsets[None, :], retain_bias[None, :], admit_bias[None, :],
      lambdas[None, :], mix_gain[None, :], feed_gain[None, :], retain_weight, admit_weight, branch_weight, recur_weight,
      merge_weight, gu_s, down_weight)

    late = seq // LATE
    pair = lambda lead=0: pltpu.VMEM((2, chan, lead + LATE), F32)
    one = lambda n, kind=F32, lead=0: pltpu.VMEM((n, lead + LATE), kind)
    steps = [DMA((2, 3, late)), DMA((2, 3, late))]
    sums = [DMA((2, late, LINE)), DMA((2, late, LINE))]
    held = pltpu.VMEM((late, LINE + 1, block, LATE), BF16)
    own_low = pltpu.VMEM((late, LINE, block, LATE), BF16)
    land = lambda n, m: ((shape((n, m), BF16), ANY), (shape((3, n, m), BF16), ANY))
    input_grad, tiny_v, tiny_g, *sums_of = call(
        functools.partial(back_kernel, width),
        [VM] + [ANY] * 2 + [VM] * 8 + [ANY] * 14,
        [(shape((half, tokens), F32), ANY), (shape((2, 8, chan), F32), VM),
         (shape((lru, 128), F32), VM), *land(cols, 2 * ff), *land(ff, cols), *land(cols, 2 * lru), *land(lru, cols)],
        [pltpu.VMEM((late, LINE, 8, LATE), F32), pltpu.VMEM((8, seq), F32),
         pltpu.VMEM((chan, width), BF16), pltpu.VMEM((width, 2 * chan), BF16),
         pair(), pair(128), pair(), pair(), pair(), pair(128), pltpu.VMEM((late, width, LATE), BF16), tok(2 * chan, BF16),
         tok(block), tok(block), one(chan), one(chan, F32, 128), one(2 * chan, BF16),
         one(chan), one(chan), pltpu.VMEM((chan, 128), F32), own_low, held,
         tok(chan, BF16), by_part(width), pltpu.VMEM((4, cols, 2 * ff), BF16), pltpu.VMEM((cols, 2 * ff), BF16),
         pltpu.VMEM((4, ff, cols), BF16), pltpu.VMEM((ff, cols), BF16),
         pltpu.VMEM((block, 128), F32), pltpu.VMEM((block, 128), F32), pltpu.VMEM((8, chan, 128), F32),
         pltpu.VMEM((2, lru, 2 * lru), F32), by_part(block), pltpu.VMEM((width, 2 * lru), BF16),
         pltpu.VMEM((lru, width), BF16), pltpu.VMEM((2, 8, chan), F32), pltpu.VMEM((2, 8, chan), F32),
         pltpu.VMEM((4, 2, 8, chan), F32), pltpu.VMEM((2, lru, 128), F32), pltpu.VMEM((lru, 128), F32),
         pltpu.VMEM((4, lru, 128), F32), DMA((7,)), DMA((6, 2))] + [DMA((late, 3)), DMA((late, 3))] + steps + sums
        + [DMA, DMA, DMA((2, 2)), DMA((2, LINE)), DMA((2, LINE)), DMA((2,)), DMA((2,)), DMA((4,))]
        + [DMA((2, 3)), DMA((2, 3)), DMA((2, 3)), DMA((2, 3)), DMA((2,)), DMA((2,))],
        2, "mix_backward", 10 * 10**9,
    )(y, dn2, g, x_own, scale_two, scale_one, coef, gains, masks, par, gates, m_n, br_n, b, p, u, r, i, h,
      q, n1, f_own, f_got, fd_own, fd_got)

    line_of = shape((1, lru), F32)
    cuts = 3
    rows_in = lambda *dims: pl.BlockSpec((dims[0] // cuts,) + dims[1:], lambda n: (n,) + (0,) * (len(dims) - 1))
    three = lambda *dims: pl.BlockSpec((3, dims[0] // cuts, dims[1]), lambda n: (0, n, 0))
    still = lambda *dims: pl.BlockSpec(dims, lambda n: (0,) * len(dims))
    sizes = ((cols, 2 * ff), (ff, cols), (cols, 2 * lru), (lru, cols))
    big = ((cols, lru), (cols, lru), (lru, cols), (ff, cols), (ff, cols), (ff, cols))
    across = pl.BlockSpec((ff, cols // cuts), lambda n: (0, n))
    flat = ((4, lru),) + ((1, lru),) * 4 + ((1, half),) * 2 + ((heads, 64, 64),) * 2
    s_b, s_r, s_m, s_g, s_u, s_d, result, input_grad, taps, offs, bias_r, bias_a, decay, mix, feed, retain, admit = pl.pallas_call(
        last_kernel,
        grid=(cuts,),
        out_shape=[shape(d, F32) for d in big] + [shape((half, tokens), BF16), shape((half, tokens), F32)]
        + [shape(d, F32) for d in flat],
        in_specs=[spec(*d) for d in sizes[:3] for spec in (rows_in, three)] + [still(lru, cols), still(3, lru, cols)]
        + [rows_in(half, tokens)] * 2
        + [still(2, 8, chan), still(lru, 128), still(1, lru)],
        out_specs=[rows_in(cols, lru)] * 2 + [still(lru, cols)] + [across] * 2 + [rows_in(ff, cols)] + [rows_in(half, tokens)] * 2 + [still(*d) for d in flat],
        name="last_sums",
        compiler_params=pltpu.CompilerParams(vmem_limit_bytes=ROOM),
    )(*sums_of, result, input_grad, tiny_v, tiny_g, lambdas[None, :])
    return (
        result,
        input_grad,
        mix[0],
        s_b,
        s_r,
        taps,
        offs[0],
        retain,
        bias_r[0],
        admit,
        bias_a[0],
        decay[0],
        s_m,
        feed[0],
        s_g.T,
        s_u.T,
        s_d,
    )


def suits(mesh, args):
    return (
        dict(mesh.shape) == {"row": 4, "col": 8}
        and args[0].shape == (D, 8 * SEQ)
        and args[3].shape == (D, 2048)
        and args[14].shape == (D, 4608)
        and args[7].shape == (32, 64, 64)
    )


def solution(mesh):
    in_specs = (
        P("col", "row"),
        P("row"),
        P("col"),
        P("row", "col"),
        P("row", "col"),
        P(None, "col"),
        P("col"),
        P("col", None, None),
        P("col"),
        P("col", None, None),
        P("col"),
        P("col"),
        P("col", "row"),
        P("col"),
        P("row", "col"),
        P("row", "col"),
        P("col", "row"),
        P("col", "row"),
    )
    out_specs = (
        P("col", "row"),
        P("col", "row"),
        P("col"),
        P("row", "col"),
        P("row", "col"),
        P(None, "col"),
        P("col"),
        P("col", None, None),
        P("col"),
        P("col", None, None),
        P("col"),
        P("col"),
        P("col", "row"),
        P("col"),
        P("row", "col"),
        P("row", "col"),
        P("col", "row"),
    )
    def run(*args):
        chosen = fast_body if suits(mesh, args) else body
        return jax.shard_map(
            chosen, mesh=mesh, in_specs=in_specs, out_specs=out_specs, check_vma=False
        )(*args)

    return run
```

```python
import functools

import jax
import jax.numpy as jnp
from jax import lax
from jax.experimental import pallas as pl
from jax.experimental.pallas import tpu as pltpu
from jax.sharding import PartitionSpec as P

D = 1536
SEQ = 1024
MICRO = 2


HIGH = lax.Precision.HIGHEST
EPS = 1e-06
POWER = 8.0
FLOOR = 0.01


def combine(earlier, later):
    first_a, first_b = earlier
    second_a, second_b = later
    return (first_a * second_a, second_a * first_b + second_b)


def mixer(
    branch_pre,
    lru_pre,
    segs,
    kernel,
    offsets,
    retain_weight,
    retain_bias,
    admit_weight,
    admit_bias,
    lambdas,
):
    length = lru_pre.shape[0]
    channels = lru_pre.shape[1]
    conv = offsets + kernel[0] * lru_pre
    for lag in range(1, kernel.shape[0]):
        shifted = jnp.concatenate(
            [jnp.zeros((lag, channels), lru_pre.dtype), lru_pre[:-lag]], axis=0
        )
        prior = jnp.concatenate([jnp.full((lag,), -1, jnp.int32), segs[:-lag]])
        keep = (prior == segs).astype(lru_pre.dtype)
        conv = conv + kernel[lag] * shifted * keep[:, None]
    heads = retain_weight.shape[0]
    blocks = conv.reshape(length, heads, channels // heads)
    retain = jax.nn.sigmoid(
        jnp.einsum("thi,hij->thj", blocks, retain_weight, precision=HIGH).reshape(length, channels)
        + retain_bias
    )
    admit = jax.nn.sigmoid(
        jnp.einsum("thi,hij->thj", blocks, admit_weight, precision=HIGH).reshape(length, channels)
        + admit_bias
    )
    decay = jnp.exp(-POWER * retain * jax.nn.softplus(-lambdas))
    factor = jnp.sqrt(1.0 - decay * decay + FLOOR)
    starts = jnp.concatenate([jnp.ones((1,), bool), segs[1:] != segs[:-1]])
    decay = jnp.where(starts[:, None], 0.0, decay)
    factor = jnp.where(starts[:, None], 1.0, factor)
    _, state = lax.associative_scan(combine, (decay, factor * admit * conv), axis=0)
    return jax.nn.gelu(branch_pre) * state


def geglu(gate, upper):
    return jax.nn.gelu(gate) * upper


def contract_rows(left, right):
    return lax.dot_general(
        left, right, (((0,), (0,)), ((), ())), preferred_element_type=jnp.float32
    )


def contract_cols(left, right):
    return lax.dot_general(
        left, right, (((1,), (1,)), ((), ())), preferred_element_type=jnp.float32
    )


def contract_cross(left, right):
    return lax.dot_general(
        left, right, (((0,), (1,)), ((), ())), preferred_element_type=jnp.float32
    )


def norm_forward(resid, gain):
    total = lax.psum(jnp.sum(resid * resid, axis=0), "col")
    scale = lax.rsqrt(total / D + EPS)[None, :]
    return (scale, (resid * scale * gain[:, None]).astype(jnp.bfloat16))


def norm_backward(resid, scale, gain, grad_normed):
    weighted = grad_normed * gain[:, None]
    total = lax.psum(jnp.sum(weighted * resid, axis=0), "col")
    grad_resid = scale * weighted - resid * (scale * scale * scale) * (total / D)[None, :]
    grad_gain = jnp.sum(grad_normed * resid * scale, axis=1)
    return (grad_resid, grad_gain)


def gather_features(normed):
    return lax.all_gather(normed, "col", axis=0, tiled=True)


def gather_cotangent(grad):
    return lax.all_gather(grad, "col", axis=0, tiled=True)


def spread_sum(term):
    return lax.psum_scatter(
        term.astype(jnp.bfloat16), "col", scatter_dimension=0, tiled=True
    ).astype(jnp.float32)


def back_sum(term):
    return spread_sum(term)


def merge_term(whole_merge, mixed_low):
    return spread_sum(contract_cross(whole_merge, mixed_low))


def weight_grads(normed, grad_joined):
    return jnp.dot(
        normed,
        grad_joined,
        preferred_element_type=jnp.float32,
    )


def row_sum(total, axis):
    return lax.psum_scatter(
        total.astype(jnp.bfloat16), "row", scatter_dimension=axis, tiled=True
    ).astype(jnp.float32)


def body(
    inputs,
    segments,
    mix_gain,
    branch_weight,
    recur_weight,
    kernel,
    offsets,
    retain_weight,
    retain_bias,
    admit_weight,
    admit_bias,
    lambdas,
    merge_weight,
    feed_gain,
    gate_weight,
    up_weight,
    down_weight,
    cotangent,
):
    lru_cols = branch_weight.shape[1]
    feed_cols = gate_weight.shape[1]
    mixer_params = (kernel, offsets, retain_weight, retain_bias, admit_weight, admit_bias, lambdas)
    acc_branch = jnp.zeros((D, lru_cols), jnp.float32)
    acc_recur = jnp.zeros((D, lru_cols), jnp.float32)
    acc_gate = jnp.zeros((D, feed_cols), jnp.float32)
    acc_up = jnp.zeros((D, feed_cols), jnp.float32)
    acc_merge = jnp.zeros((lru_cols, D), jnp.float32)
    acc_down = jnp.zeros((feed_cols, D), jnp.float32)
    acc_small = tuple((jnp.zeros_like(p) for p in mixer_params))
    acc_mix = jnp.zeros_like(mix_gain)
    acc_feed = jnp.zeros_like(feed_gain)
    outputs = []
    in_grads = []
    for batch in range(MICRO):
        lower = batch * SEQ
        resid_in = inputs[:, lower : lower + SEQ].astype(jnp.float32)
        grad_out = cotangent[:, lower : lower + SEQ].astype(jnp.float32)
        segs = segments[lower : lower + SEQ]
        whole_branch, whole_recur, whole_gate, whole_up = (
            lax.all_gather(branch_weight, "row", axis=0, tiled=True),
            lax.all_gather(recur_weight, "row", axis=0, tiled=True),
            lax.all_gather(gate_weight, "row", axis=0, tiled=True),
            lax.all_gather(up_weight, "row", axis=0, tiled=True),
        )
        whole_merge, whole_down = (
            lax.all_gather(merge_weight, "row", axis=1, tiled=True),
            lax.all_gather(down_weight, "row", axis=1, tiled=True),
        )
        scale_one, normed_one = norm_forward(resid_in, mix_gain)
        full_one = gather_features(normed_one)
        branch_pre = contract_rows(full_one, whole_branch)
        lru_pre = contract_rows(full_one, whole_recur)

        def local_mixer(bpre, lpre, kern, offs, rweight, rbias, aweight, abias, lams):
            return mixer(bpre, lpre, segs, kern, offs, rweight, rbias, aweight, abias, lams)

        mixed, mixer_pull = jax.vjp(local_mixer, branch_pre, lru_pre, *mixer_params)
        mixed_low = mixed.astype(jnp.bfloat16)
        resid_mid = resid_in + merge_term(whole_merge, mixed_low)
        scale_two, normed_two = norm_forward(resid_mid, feed_gain)
        full_two = gather_features(normed_two)
        gate = contract_rows(full_two, whole_gate)
        upper = contract_rows(full_two, whole_up)
        hidden, geglu_pull = jax.vjp(geglu, gate, upper)
        hidden_low = hidden.astype(jnp.bfloat16)
        result = resid_mid + spread_sum(contract_cross(whole_down, hidden_low))
        outputs.append(result.astype(jnp.bfloat16))
        grad_full = gather_cotangent(grad_out.astype(jnp.bfloat16))
        acc_down = acc_down + contract_cross(hidden_low, grad_full)
        grad_gate, grad_upper = geglu_pull(contract_cross(grad_full, whole_down))
        grad_gate = grad_gate.astype(jnp.bfloat16)
        grad_upper = grad_upper.astype(jnp.bfloat16)
        feed_joined = weight_grads(full_two, jnp.concatenate([grad_gate, grad_upper], axis=1))
        acc_gate = acc_gate + feed_joined[:, :feed_cols]
        acc_up = acc_up + feed_joined[:, feed_cols:]
        grad_normed_two = back_sum(
            contract_cols(whole_gate, grad_gate) + contract_cols(whole_up, grad_upper)
        )
        grad_mid_norm, feed_part = norm_backward(resid_mid, scale_two, feed_gain, grad_normed_two)
        acc_feed = acc_feed + feed_part
        grad_mid = grad_out + grad_mid_norm
        grad_mid_full = gather_cotangent(grad_mid.astype(jnp.bfloat16))
        acc_merge = acc_merge + contract_cross(mixed_low, grad_mid_full)
        pulled = mixer_pull(contract_cross(grad_mid_full, whole_merge))
        grad_branch = pulled[0].astype(jnp.bfloat16)
        grad_lru = pulled[1].astype(jnp.bfloat16)
        acc_small = tuple((total + part for total, part in zip(acc_small, pulled[2:])))
        branch_joined = weight_grads(full_one, jnp.concatenate([grad_branch, grad_lru], axis=1))
        acc_branch = acc_branch + branch_joined[:, :lru_cols]
        acc_recur = acc_recur + branch_joined[:, lru_cols:]
        grad_normed_one = back_sum(
            contract_cols(whole_branch, grad_branch) + contract_cols(whole_recur, grad_lru)
        )
        grad_in_norm, mix_part = norm_backward(resid_in, scale_one, mix_gain, grad_normed_one)
        acc_mix = acc_mix + mix_part
        in_grads.append(grad_mid + grad_in_norm)
    sum_branch, sum_recur, sum_gate, sum_up = (
        row_sum(acc_branch, 0),
        row_sum(acc_recur, 0),
        row_sum(acc_gate, 0),
        row_sum(acc_up, 0),
    )
    sum_merge, sum_down = (
        row_sum(acc_merge, 1),
        row_sum(acc_down, 1),
    )
    summed = lax.psum(
        (
            acc_mix,
            acc_feed,
            acc_small[0],
            acc_small[1],
            acc_small[2],
            acc_small[3],
            acc_small[4],
            acc_small[5],
            acc_small[6],
        ),
        "row",
    )
    result_all = jnp.concatenate(outputs, axis=1)
    input_grad = jnp.concatenate(in_grads, axis=1)
    return (
        result_all,
        input_grad,
        summed[0],
        sum_branch,
        sum_recur,
        summed[2],
        summed[3],
        summed[4],
        summed[5],
        summed[6],
        summed[7],
        summed[8],
        sum_merge,
        summed[1],
        sum_gate,
        sum_up,
        sum_down,
    )


MESH = pl.DeviceIdType.MESH
F32 = jnp.float32
BF16 = jnp.bfloat16
LINE = 4
PART = 128
PARTS = 8
LATE = 256
GELU_A = 0.7978845608028654
GELU_B = 0.044715


def place():
    row, col = lax.axis_index("row"), lax.axis_index("col")
    return row, col // 2, col % 2


def at_line(z, core):
    return {"col": 2 * z + core}


def lanes(part):
    return pl.ds(pl.multiple_of(part * PART, PART), PART)


def rows_of(index, size):
    return pl.ds(pl.multiple_of(index * size, 16), size)


def dot(a, b):
    return lax.dot_general(a, b, (((1,), (0,)), ((), ())), preferred_element_type=F32)


def dot_nt(a, b):
    return lax.dot_general(a, b, (((1,), (1,)), ((), ())), preferred_element_type=F32)


def greet(row, z, core, rows, line):
    barrier = pltpu.get_barrier_semaphore()
    peers = [{"col": 2 * z + (1 - core)}]
    if rows:
        peers += [{"row": row ^ d} for d in (1, 2, 3)]
    if line:
        peers += [at_line(z ^ d, core) for d in (1, 2, 3)]
    for peer in peers:
        pl.semaphore_signal(barrier, inc=1, device_id=peer, device_id_type=MESH)
    return functools.partial(pl.semaphore_wait, barrier, len(peers))


def remote(src, dst, send, recv, peer):
    return pltpu.make_async_remote_copy(
        src_ref=src, dst_ref=dst, send_sem=send, recv_sem=recv, device_id=peer, device_id_type=MESH
    )


class Gather:
    def __init__(self, ref, send, recv, z, core, block, back=False):
        self.parts = ref.shape[0]
        self.ref, self.sems, self.z, self.core = ref, (send, recv), z, core
        self.block, self.back = block, back

    def copy(self, way, hop, step, owner, incoming=False):
        part = self.parts - 1 - step if self.back else step
        piece = self.ref.at[part, rows_of(owner, self.block), :]
        peer = at_line(self.z + (1 if (way == 0) != incoming else -1), self.core)
        return remote(piece, piece, self.sems[0].at[way, hop, step], self.sems[1].at[way, hop, step], peer)

    def each(self, hop, act, incoming):
        z = self.z
        if incoming:
            cases = ((0, z - 1 - hop >= 0, z - 1 - hop), (1, z + 1 + hop < LINE, z + 1 + hop))
        else:
            cases = (
                (0, (z >= hop) & (z < LINE - 1), z - hop),
                (1, (z + hop < LINE) & (z >= 1), z + hop),
            )
        for way, here, owner in cases:
            pl.when(here)(functools.partial(act, way, owner))

    def send(self, hop, step):
        self.each(hop, lambda way, owner: self.copy(way, hop, step, owner).start(), False)

    def arrive(self, hop, step):
        self.each(hop, lambda way, owner: self.copy(way, hop, step, owner, True).wait_recv(), True)

    def forward(self, hop, step):
        self.arrive(hop - 1, step)
        self.send(hop, step)

    def sent(self):
        def one(step, carry):
            for hop in range(LINE - 1):
                self.each(hop, lambda way, owner: self.copy(way, hop, step, owner).wait_send(), False)
            return carry

        lax.fori_loop(0, self.parts, one, 0)

    def middle(self, step, ahead=1):
        for hop in (2, 1, 0):
            later = step + ahead + 2 - hop
            act = self.forward if hop else self.send
            pl.when(later < self.parts)(functools.partial(act, hop, later))


class Spread:
    def __init__(self, own, held, send, recv, z, core):
        self.parts = held.shape[0]
        self.own, self.held, self.sems, self.z, self.core = own, held, (send, recv), z, core

    def copy(self, way, step, hop):
        slot = hop if way == 0 else LINE - hop
        there = slot - 1 if way == 0 else slot + 1
        peer = at_line(self.z + (1 if way == 0 else -1), self.core)
        return remote(
            self.held.at[step, slot],
            self.held.at[step, there],
            self.sems[0].at[way, step, hop],
            self.sems[1].at[way, step, hop - 1],
            peer,
        )

    def landed(self, way, step, hop):
        slot = hop if way == 0 else LINE - hop
        piece = self.held.at[step, slot]
        peer = at_line(self.z + (-1 if way == 0 else 1), self.core)
        remote(piece, piece, self.sems[0].at[way, step, hop], self.sems[1].at[way, step, hop], peer).wait_recv()

    def push(self, way, step, first):
        z = self.z

        def one(i, carry):
            hop = LINE - 1 - i
            owner = z + hop if way == 0 else z - hop
            slot = hop if way == 0 else LINE - hop

            @pl.when((owner >= 0) & (owner < LINE))
            def _():
                @pl.when(first)
                def _():
                    self.held[step, slot] = self.own(step, owner)[...].astype(BF16)

                @pl.when(jnp.logical_not(first))
                def _():
                    self.landed(way, step, hop)
                    total = self.own(step, owner)[...].astype(F32) + self.held[step, slot].astype(F32)
                    self.held[step, slot] = total.astype(BF16)

                self.copy(way, step, hop).start()

            return carry

        lax.fori_loop(0, LINE - 1, one, 0)

    def serve(self, t, finish):
        z = self.z
        step = t - (LINE - 1)

        @pl.when((step >= 0) & (step < self.parts))
        def _():
            @pl.when(z == 0)
            def _():
                self.landed(1, step, 0)
                finish(step, lambda a, n: self.mine(step, a, n) + self.got(step, LINE, a, n))

            @pl.when(z == LINE - 1)
            def _():
                self.landed(0, step, 0)
                finish(step, lambda a, n: self.mine(step, a, n) + self.got(step, 0, a, n))

            @pl.when((z > 0) & (z < LINE - 1))
            def _():
                self.landed(0, step, 0)
                self.landed(1, step, 0)
                finish(
                    step,
                    lambda a, n: self.mine(step, a, n) + (self.got(step, 0, a, n) + self.got(step, LINE, a, n)),
                )

        for way, late, turn in ((1, LINE - 1 - z, z < 2), (0, z, z >= 0), (1, LINE - 1 - z, z >= 2)):
            step = t - late
            pl.when((step >= 0) & (step < self.parts) & turn)(functools.partial(self.push, way, step, late == 0))

    def mine(self, step, start, size):
        return self.own(step, self.z)[pl.ds(start, size), :].astype(F32)

    def got(self, step, slot, start, size):
        return self.held[step, slot, pl.ds(start, size)].astype(F32)

    def sent(self):
        z = self.z

        def one(step, carry):
            for way in (0, 1):
                for hop in range(1, LINE):
                    owner = z + hop if way == 0 else z - hop

                    @pl.when((owner >= 0) & (owner < LINE))
                    def _():
                        self.copy(way, step, hop).wait_send()

            return carry

        lax.fori_loop(0, self.parts, one, 0)


def share_line(ref, send, recv, z, core):
    copies = [
        remote(ref.at[z], ref.at[z], send.at[d - 1], recv.at[d - 1], at_line(z ^ d, core)) for d in (1, 2, 3)
    ]
    for copy in copies:
        copy.start()
    for d in (1, 2, 3):
        piece = ref.at[z ^ d]
        remote(piece, piece, send.at[d - 1], recv.at[d - 1], at_line(z ^ d, core)).wait_recv()
    for copy in copies:
        copy.wait_send()


class Weights:
    def __init__(self, src, dst, send, recv, own, row, z, core, turned, stride=0, start=0):
        self.src, self.dst, self.send, self.recv, self.own = src, dst, send, recv, own
        self.row, self.core, self.turned = row, core, turned
        self.stride, self.first = stride or src.shape[0], start
        self.sibling = {"col": 2 * z + (1 - core)}

    def spot(self, row, core):
        down, right = (row, core) if self.turned else (core, row)
        rows, cols = self.src.shape
        at = pl.ds(pl.multiple_of(down * self.stride + self.first, 16), rows)
        return self.dst.at[at, pl.ds(pl.multiple_of(right * cols, 128), cols)]

    def to_row(self, d):
        return remote(
            self.src, self.spot(self.row, self.core), self.send.at[d], self.recv.at[d], {"row": self.row ^ d}
        )

    def to_sibling(self, d):
        if d == 0:
            return remote(
                self.src, self.spot(self.row, self.core), self.send.at[0], self.recv.at[0], self.sibling
            )
        piece = self.spot(self.row ^ d, self.core)
        return remote(piece, piece, self.send.at[3 + d], self.recv.at[3 + d], self.sibling)

    def local(self):
        return pltpu.make_async_copy(self.src, self.spot(self.row, self.core), self.own)

    def start(self):
        for d in (1, 2, 3):
            self.to_row(d).start()
        self.to_sibling(0).start()
        self.local().start()

    def forward(self):
        for d in (1, 2, 3):
            piece = self.spot(self.row ^ d, self.core)
            remote(piece, piece, self.send.at[d], self.recv.at[d], {"row": self.row ^ d}).wait_recv()
            self.to_sibling(d).start()

    def finish(self):
        self.local().wait()
        for d in (0, 1, 2, 3):
            piece = self.spot(self.row ^ d, 1 - self.core)
            sem = 0 if d == 0 else 3 + d
            remote(piece, piece, self.send.at[sem], self.recv.at[sem], self.sibling).wait_recv()

    def sent(self):
        for d in (1, 2, 3):
            self.to_row(d).wait_send()
            self.to_sibling(d).wait_send()
        self.to_sibling(0).wait_send()


def gelu_parts(b):
    t = jnp.tanh(GELU_A * (b + GELU_B * (b * b * b)))
    half = 0.5 + 0.5 * t
    slope = half + (0.5 * b) * (1.0 - t * t) * (GELU_A + (3.0 * GELU_A * GELU_B) * (b * b))
    return b * half, slope


def eight(v):
    return jnp.sum(v.reshape(v.shape[0] // 8, 8, v.shape[1]), axis=0)


def fold(v):
    total = v[:, 0:128]
    for j in range(1, v.shape[1] // 128):
        total = total + v[:, j * 128 : (j + 1) * 128]
    return total


def tokens_of(ref, piece):
    return jnp.concatenate([ref[k, piece, :] for k in range(ref.shape[0])], axis=1)


def blocks(count, body):
    def one(i, carry):
        body(i)
        return carry

    lax.fori_loop(0, count, one, 0)


def scale_of(ref, eps, width):
    total = jnp.sum(jnp.sum(ref[...], axis=0), axis=0, keepdims=True)
    return lax.rsqrt(total / width + eps)


def forward_kernel(
    width, eps,
    x_in, g_in, segs, taps, offs, bias_r, bias_a, decay, mix, late, retain, admit, branch, recur, mn_s, gu_s, d_s,
    masks, par, gains, gates, coef, scale, scale_two, y_out, n1_out, q_out, x_out, g_out, b_out, p_out, u_out, r_out, i_out, h_out,
    result, dn2_out, dev_h, z_h, g_own, g_got, gd_own, gd_got, br_n, m_n,
    sums, sums2, sums3, vec, br_s, brn_s, m_s, vec_all, block_all, gates_hi, gates_lo, normed, normed2, go, x_own, y, dn2, q_c, p_s, h_s, room, uh, ul,
    own, held, held_n, held_o, gu, gun, down, dt, zs, dev,
    x_send, x_recv, x_loc, i_send, i_recv, i_loc, l_send, l_recv, n_send, n_recv, c_send, c_recv, g_send, g_recv, e_send, e_recv, f_send, f_recv,
    s_send, s_recv, t_send, t_recv, o_send, o_recv, w_send, w_recv, w_own, k_sem, v_sem, d_send, d_recv, d_own,
):
    row, z, core = place()
    block, seq = y.shape
    half = x_in.shape[0]
    chan = p_s.shape[0]
    hid = zs.shape[0]
    b_s, u_s, r_s, i_s, a_c = [room.at[n * chan : (n + 1) * chan, :] for n in range(5)]
    ev, dz = room.at[0 : 2 * hid, :], room.at[2 * hid : 3 * hid, :]
    hh = hid // 2
    hc = chan // 2
    sibling = {"col": 2 * z + (1 - core)}
    met = greet(row, z, core, True, True)
    br_s[0:hc, :] = branch[...].T
    br_s[hc:, :] = recur[...].T
    m_s[...] = mn_s[...].T
    br, mt = gun.at[0 : 2 * chan, 0:width], dt.at[:, 0:chan]
    wide = br_s.shape[0]
    recur_s, branch_s = br_s.at[wide // 2 :, :], br_s.at[0 : wide // 2, :]
    weights = [
        Weights(src, dst, w_send.at[n], w_recv.at[n], w_own.at[n], row, z, core, n in (2, 5), stride, start)
        for n, (src, dst, stride, start) in enumerate(
            (
                (recur_s, br, hc, 0),
                (branch_s, br, hc, chan),
                (m_s, mt, 0, 0),
                (gu_s, gu, 0, 0),
                (d_s, down, 0, 0),
                (brn_s, br_n, 0, 0),
                (mn_s, m_n, 0, 0),
            )
        )
    ]
    mine = pl.ds(pl.multiple_of(core * seq, seq), seq)
    other = pl.ds(pl.multiple_of((1 - core) * seq, seq), seq)
    inner = pl.ds(pl.multiple_of(z * block + core * half, 16), half)
    outer = rows_of(core, half)
    swaps = [
        remote(x_in.at[:, other], x_own.at[outer, :], x_send.at[0], x_recv.at[0], sibling),
        pltpu.make_async_copy(x_in.at[:, mine], x_own.at[outer, :], x_loc.at[0]),
    ]
    for k in range(PARTS):
        theirs, ours = [pl.ds(pl.multiple_of(c * seq + k * PART, 128), PART) for c in (1 - core, core)]
        swaps.append(remote(g_in.at[:, theirs], go.at[k, inner, :], i_send.at[k], i_recv.at[k], sibling))
        swaps.append(pltpu.make_async_copy(g_in.at[:, ours], go.at[k, inner, :], i_loc.at[k]))
    vec[...] = jnp.zeros(vec.shape, F32)
    vec[0:4, :] = taps[...]
    for n, one_row in enumerate((offs, bias_r, bias_a)):
        vec[4 + n : 5 + n, :] = one_row[...]
    rate = -decay[...]
    vec[7:8, :] = 8.0 * (jnp.maximum(rate, 0.0) + jnp.log1p(jnp.exp(-jnp.abs(rate))))
    vec[8:9, 0:half] = mix[...]
    vec[9:10, 0:half] = late[...]
    brn_s[:, 0:hc] = branch[...]
    brn_s[:, hc:] = recur[...]
    met()
    for w in weights[:3]:
        w.start()
    for swap in swaps:
        swap.start()
    trades = []
    for n, (src, dst) in enumerate(
        ((vec, vec_all.at[core]), (retain, block_all.at[core, 0]), (admit, block_all.at[core, 1]))
    ):
        trades.append(remote(src, dst, x_send.at[2 + n], x_recv.at[2 + n], sibling))
        trades.append(pltpu.make_async_copy(src, dst, x_loc.at[2 + n]))
    for trade in trades:
        trade.start()
    for swap in swaps + trades:
        swap.wait()
    flushes = [
        pltpu.make_async_copy(x_own, x_out, v_sem.at[0]),
        pltpu.make_async_copy(go.at[:, rows_of(z, block), :], g_out, v_sem.at[1]),
    ]
    for flush in flushes:
        flush.start()
    gather = Gather(normed, g_send, g_recv, z, core, block)
    gather_go = Gather(go, e_send, e_recv, z, core, block)
    gather_two = Gather(normed2, f_send, f_recv, z, core, block)
    shares = lambda k, s: own.at[k, s]
    shares_o = lambda k, s: normed.at[k, rows_of(s, block), :]
    spread = Spread(shares, held, s_send, s_recv, z, core)
    spread_n = Spread(shares, held_n, t_send, t_recv, z, core)
    spread_o = Spread(shares_o, held_o, o_send, o_recv, z, core)
    res = x_own
    gather_go.send(0, 0)
    gather_go.send(0, 1)
    for c in (0, 1):
        at = slice(c * hc, (c + 1) * hc)
        par[at, :] = vec_all[c].T
        gains[c * half : (c + 1) * half, :] = par[c * hc : c * hc + half, :]

    sums[z] = jnp.zeros(sums.shape[1:], F32)

    def squares(i):
        v = x_own[rows_of(i, 16), :].astype(F32)
        v = v * v
        sums[z] += v[:8] + v[8:]

    blocks(block // 16, squares)
    share_line(sums, l_send, l_recv, z, core)
    scale[...] = jnp.broadcast_to(scale_of(sums, eps, width), scale.shape)

    def norm(i):
        v = x_own[rows_of(i, 16), :].astype(F32) * scale[0:1, :] * gains[rows_of(i, 16), 8:9]
        v = v.astype(BF16)
        for k in range(PARTS):
            normed[k, pl.ds(pl.multiple_of(z * block + i * 16, 16), 16), :] = v[:, k * PART : (k + 1) * PART]

    blocks(block // 16, norm)
    gather.send(0, 0)
    p_s[:, PART:] = jnp.zeros((chan, 128), F32)
    h_s[:, PART:] = jnp.zeros((chan, 128), F32)
    pads = [
        pltpu.make_async_copy(src.at[:, PART:], out.at[:, 0:128], v_sem.at[2 + n])
        for n, (src, out) in enumerate(((p_s, p_out), (h_s, h_out)))
    ]
    for pad in pads:
        pad.start()
    gates[...] = jnp.zeros(gates.shape, BF16)
    gates_hi[...] = jnp.zeros(gates_hi.shape, BF16)
    gates_lo[...] = jnp.zeros(gates_lo.shape, BF16)
    per = retain.shape[0]
    tap = retain.shape[1]
    for c in (0, 1):
        for n in (0, 1):
            for e in range(per):
                w = block_all[c, n, e]
                at, far = slice(e * tap, (e + 1) * tap), slice(n * hc + e * tap, n * hc + (e + 1) * tap)
                gates[c, at, far] = w.astype(BF16)
                w = w.T
                high = w.astype(BF16)
                gates_hi[c, far, at] = high
                gates_lo[c, far, at] = (w - high.astype(F32)).astype(BF16)
    masks[...] = jnp.zeros(masks.shape, F32)
    here = jnp.broadcast_to(segs[:, mine], (8, seq))
    spot = lax.broadcasted_iota(jnp.int32, (8, seq), 1)
    for lag in (1, 2, 3):
        same = jnp.where((pltpu.roll(here, lag, 1) == here) & (spot >= lag), 1.0, 0.0)
        masks[lag : lag + 1, 0:seq] = same[0:1]
        if lag == 1:
            masks[0:1, 0:seq] = 1.0 - same[0:1]
    gather.forward(1, 0)
    gather.send(0, 1)
    weights[0].forward()
    gather.forward(2, 0)
    gather_go.forward(1, 0)
    gather.forward(1, 1)
    gather.send(0, 2)
    weights[1].forward()
    for w in weights[3:5]:
        w.start()
    gather_go.forward(1, 1)
    gather_go.forward(2, 0)
    weights[0].finish()
    for pad in pads:
        pad.wait()

    kept = (b_s, p_s, u_s, r_s, i_s, h_s, q_c)
    outs = (b_out, p_out, u_out, r_out, i_out, h_out, q_out)

    def keep(n, part):
        if n in (1, 5):
            at = pl.ds(pl.multiple_of(128 + part * PART, 128), PART)
            return pltpu.make_async_copy(kept[n].at[:, 128:], outs[n].at[:, at], k_sem.at[n])
        return pltpu.make_async_copy(kept[n], outs[n].at[:, lanes(part)], k_sem.at[n])

    def put_shares(k, whole):
        for s in range(LINE):
            own[k, s] = whole[s * block : (s + 1) * block, :].astype(own.dtype)

    def work(k):
        here = lanes(k)

        @pl.when(k > 0)
        def _():
            for n in range(len(kept)):
                keep(n, k - 1).wait()

        p_s[:, 0:128] = p_s[:, PART:]
        h_s[:, 0:128] = h_s[:, PART:]
        p_s[:, 128:] = dot(br[0:chan, :], normed[k])

        def conv(i):
            ch = rows_of(i, 64)
            window = p_s[ch, :]
            pr = par[ch, :]
            u = pr[:, 4:5] + pr[:, 0:1] * window[:, 128:]
            for lag in (1, 2, 3):
                u = u + pr[:, lag : lag + 1] * (pltpu.roll(window, lag, 1)[:, 128:] * masks[lag : lag + 1, here])
            u_s[ch, :] = u
            high = u.astype(BF16)
            uh[ch, :] = high
            ul[ch, :] = (u - high.astype(F32)).astype(BF16)

        blocks(chan // 64, conv)
        gather.middle(k)
        for g in range(chan // 256):
            at = slice(g * 256, (g + 1) * 256)
            pre = dot(gates_hi[g], uh[at, :]) + dot(gates_hi[g], ul[at, :]) + dot(gates_lo[g], uh[at, :])
            r_s[at, :] = pre[:256]
            i_s[at, :] = pre[256:]

        def gated(i):
            ch = rows_of(i, 64)
            pr = par[ch, :]
            start = masks[0:1, here] > 0.5
            r = jax.nn.sigmoid(r_s[ch, :] + pr[:, 5:6])
            gate = jax.nn.sigmoid(i_s[ch, :] + pr[:, 6:7])
            r_s[ch, :] = r
            i_s[ch, :] = gate
            a = jnp.exp(-(r * pr[:, 7:8]))
            m = jnp.where(start, 1.0, jnp.sqrt(1.0 - a * a + FLOOR))
            a_c[ch, :] = jnp.where(start, 0.0, a)
            h_s[ch, 128:] = m * gate * u_s[ch, :]

        blocks(chan // 64, gated)
        first = lax.broadcasted_iota(jnp.int32, (128, PART), 1) == 0

        def recur(i):
            ch = rows_of(i, 128)
            a, h = a_c[ch, :], h_s[ch, 128:]
            h = h + jnp.where(first, a * h_s[ch, 0:128][:, 127:128], 0.0)
            a = jnp.where(first, 0.0, a)
            shift = 1
            while shift < PART:
                h = h + a * pltpu.roll(h, shift, 1)
                if shift * 2 < PART:
                    a = a * pltpu.roll(a, shift, 1)
                shift *= 2
            h_s[ch, 128:] = h

        blocks(chan // 128, recur)

        @pl.when(k == 0)
        def _():
            weights[2].forward()
            weights[1].finish()

        b_s[...] = dot(br[chan : 2 * chan, :], normed[k])

        def mixed(i):
            ch = rows_of(i, 64)
            b = b_s[ch, :]
            t = jnp.tanh(GELU_A * (b + GELU_B * (b * b * b)))
            q_c[ch, :] = (b * (0.5 + 0.5 * t) * h_s[ch, 128:]).astype(BF16)

        blocks(chan // 64, mixed)
        pl.when(k == 0)(weights[2].finish)
        put_shares(k, dot(mt[...], q_c[...]))
        for n in range(len(kept)):
            keep(n, k).start()

    def finish(k, total):
        def add(i):
            at = pl.multiple_of(i * 64, 64)
            y[pl.ds(at, 64), lanes(k)] = x_own[pl.ds(at, 64), lanes(k)].astype(F32) + total(at, 64)

        blocks(block // 64, add)

    def square(k):
        sums2[k, z] = jnp.zeros(sums2.shape[2:], F32)

        def one(i):
            v = y[rows_of(i, 64), lanes(k)]
            sums2[k, z] += eight(v * v)

        blocks(block // 64, one)
        for d in (1, 2, 3):
            share(k, d).start()

    def share(k, d):
        return remote(
            sums2.at[k, z], sums2.at[k, z], n_send.at[k, d - 1], n_recv.at[k, d - 1], at_line(z ^ d, core)
        )

    def norm_two(k):
        for d in (1, 2, 3):
            piece = sums2.at[k, z ^ d]
            remote(piece, piece, n_send.at[k, d - 1], n_recv.at[k, d - 1], at_line(z ^ d, core)).wait_recv()
        s2 = scale_of(sums2.at[k], eps, width)
        scale_two[:, lanes(k)] = jnp.broadcast_to(s2, (8, PART))

        def one(i):
            at = rows_of(i, 64)
            v = y[at, lanes(k)] * scale_two[0:1, lanes(k)] * gains[at, 9:10]
            normed2[k, pl.ds(pl.multiple_of(z * block + i * 64, 64), 64), :] = v.astype(BF16)

        blocks(block // 64, one)

    def turn_down(i):
        at = pl.ds(pl.multiple_of(i * 128, 128), 128)
        dt[:, at] = down[at, :].T

    def turn_up(i):
        at = pl.ds(pl.multiple_of(i * 128, 128), 128)
        gun[:, at] = gu[at, :].T

    def step(t, carry):
        gather.arrive(2, t)
        work(t)
        spread.serve(t, finish)
        pl.when(t >= 3)(lambda: square(t - 3))
        pl.when(t >= 4)(lambda: norm_two(t - 4))
        pl.when((t >= 4) & (t < 7))(lambda: gather_two.send(0, t - 4))
        pl.when((t >= 6) & (t < 8))(lambda: gather_two.forward(1, t - 6))
        pl.when(t == 5)(weights[3].forward)
        return carry

    lax.fori_loop(0, PARTS, step, 0)
    for w in weights[:3]:
        w.sent()
    for w in weights[5:]:
        w.start()
    for n in range(len(kept)):
        keep(n, PARTS - 1).wait()
    flush_n = pltpu.make_async_copy(normed, n1_out, v_sem.at[4])
    flush_n.start()
    gather_go.forward(2, 1)
    gather_go.send(0, 2)
    gather_go.send(0, 3)
    spread.serve(PARTS, finish)
    square(PARTS - 3)
    norm_two(PARTS - 4)
    gather_two.forward(2, 0)
    weights[4].forward()
    spread.serve(PARTS + 1, finish)
    square(PARTS - 2)
    norm_two(PARTS - 3)
    gather_go.forward(1, 2)
    weights[4].finish()
    blocks(hid // 128, turn_down)
    spread.serve(PARTS + 2, finish)
    square(PARTS - 1)
    norm_two(PARTS - 2)
    gather.sent()
    for flush in flushes + [flush_n]:
        flush.wait()
    weights[3].finish()
    blocks(2 * hid // 128, turn_up)
    norm_two(PARTS - 1)
    flush_y = pltpu.make_async_copy(y, y_out, v_sem.at[2])
    flush_y.start()

    def keep_dev(k):
        return pltpu.make_async_copy(dev, dev_h.at[:, lanes(k)], v_sem.at[5])

    def keep_z(k):
        return pltpu.make_async_copy(zs, z_h.at[:, lanes(k)], v_sem.at[6])

    dev_all, z_all = gu.at[:, 0:seq], dt.at[0:hid, 0:seq]
    before, end = pl.ds(0, seq - PART), pl.ds(seq - PART, PART)
    loads = [
        pltpu.make_async_copy(dev_h.at[:, before], gu.at[:, before], v_sem.at[7]),
        pltpu.make_async_copy(z_h.at[:, before], dt.at[0:hid, before], v_sem.at[8]),
        pltpu.make_async_copy(dev, gu.at[:, end], v_sem.at[9]),
        pltpu.make_async_copy(zs, dt.at[0:hid, end], v_sem.at[10]),
    ]

    def feed(k):

        @pl.when(k > 0)
        def _():
            keep_dev(k - 1).wait()
            keep_z(k - 1).wait()

        ev[...] = dot(gu[...], normed2[k])

        @pl.when(k == PARTS - 1)
        def _():
            weights[3].sent()
            loads[0].start()

        gather_two.middle(k)
        gather_go.middle(k, 2)
        gather_go.arrive(2, k)
        dz[...] = dot(down[...], go[k])
        for c in range(2):

            def one(i):
                off = pl.multiple_of(i * 64, 64)
                e = ev[pl.ds(c * 2 * hh + off, 64), :]
                v = ev[pl.ds(c * 2 * hh + hh + off, 64), :]
                d = dz[pl.ds(c * hh + off, 64), :]
                act, slope = gelu_parts(e)
                zs[pl.ds(c * hh + off, 64), :] = (act * v).astype(BF16)
                dev[pl.ds(c * 2 * hh + off, 64), :] = (d * v * slope).astype(BF16)
                dev[pl.ds(c * 2 * hh + hh + off, 64), :] = (d * act).astype(BF16)

            blocks(hh // 64, one)
        put_shares(k, dot(gun[...], dev[...]))
        spread_n.serve(k, finish_n)
        normed[k] = dot(dt[...], zs[...]).astype(BF16)
        spread_o.serve(k, finish_o)
        keep_dev(k).start()
        keep_z(k).start()

    def finish_o(k, total):
        def add(i):
            at = pl.multiple_of(i * 64, 64)
            res[pl.ds(at, 64), lanes(k)] = (y[pl.ds(at, 64), lanes(k)] + total(at, 64)).astype(BF16)

        blocks(block // 64, add)

    def keep_n(k):
        return pltpu.make_async_copy(dn2, dn2_out.at[:, lanes(k)], v_sem.at[3])

    def finish_n(k, total):
        @pl.when(k > 0)
        def _():
            keep_n(k - 1).wait()

        sums3[k, z] = jnp.zeros(sums3.shape[2:], F32)

        def add(i):
            at = pl.multiple_of(i * 64, 64)
            d = total(at, 64)
            dn2[pl.ds(at, 64), :] = d
            sums3[k, z] += eight(d * y[pl.ds(at, 64), lanes(k)] * gains[pl.ds(at, 64), 9:10])

        blocks(block // 64, add)
        keep_n(k).start()
        for d in (1, 2, 3):
            share_c(k, d).start()

    def share_c(k, d):
        return remote(
            sums3.at[k, z], sums3.at[k, z], c_send.at[k, d - 1], c_recv.at[k, d - 1], at_line(z ^ d, core)
        )

    def feed_step(t, carry):
        gather_two.arrive(2, t)
        feed(t)
        pl.when(t == 4)(weights[5].forward)
        pl.when(t == 6)(weights[6].forward)
        return carry

    lax.fori_loop(0, PARTS, feed_step, 0)
    weights[4].sent()
    for load in loads[1:]:
        load.start()
    keep_dev(PARTS - 1).wait()
    keep_z(PARTS - 1).wait()
    loads[0].wait()
    loads[2].wait()

    def columns(start):
        return pl.ds(pl.multiple_of(start, 128), block)

    def place_up(j):
        side = jnp.where(j >= 3, core, 1 - core)
        return side * hid + (j % 3) * block, columns((j % 3) * block)

    def send_up(j):
        at, to = place_up(j)
        return remote(gun.at[:, columns(at)], g_got.at[:, to], d_send.at[j], d_recv.at[j], sibling)

    def keep_up(j):
        at, to = place_up(j)
        return pltpu.make_async_copy(gun.at[:, columns(at)], g_own.at[:, to], d_own.at[j - 3])

    def send_down():
        return remote(down.at[rows_of(1 - core, hh), :], gd_got, d_send.at[3], d_recv.at[3], sibling)

    def keep_down():
        return pltpu.make_async_copy(down.at[rows_of(core, hh), :], gd_own, d_own.at[3])

    def grad_up(j):
        at = place_up(j)[0]
        right = pl.ds(pl.multiple_of(at, 16), block)
        for low in (0, width // 2):
            piece = slice(low, low + width // 2)
            gun[piece, columns(at)] = dot_nt(tokens_of(normed2, piece), dev_all[right, :]).astype(BF16)

        @pl.when(j < 3)
        def _():
            send_up(j).start()

        @pl.when(j >= 3)
        def _():
            keep_up(j).start()

    def grad_down(side):
        at = rows_of(side, hh)
        for low in range(0, width, 2 * block):
            piece = slice(low, low + 2 * block)
            down[at, piece] = dot_nt(z_all[at, :], tokens_of(go, piece)).astype(BF16)

    def drain(i, carry):
        t = PARTS + i
        blocks(2, lambda j: grad_up(2 * i + j))
        spread_n.serve(t, finish_n)
        spread_o.serve(t, finish_o)

        @pl.when(i == 0)
        def _():
            loads[1].wait()
            loads[3].wait()

        @pl.when(i < 2)
        def _():
            grad_down(jnp.where(i == 0, 1 - core, core))

        pl.when(i == 0)(lambda: send_down().start())
        pl.when(i == 1)(lambda: keep_down().start())
        return carry

    lax.fori_loop(0, LINE - 1, drain, 0)
    last = [
        remote(res.at[rows_of(1 - core, half), :], result.at[:, mine], x_send.at[0], x_recv.at[0], sibling),
        pltpu.make_async_copy(res.at[rows_of(core, half), :], result.at[:, mine], x_loc.at[0]),
        keep_n(PARTS - 1),
        flush_y,
    ]
    for copy in last[:2]:
        copy.start()
    for w in weights[5:]:
        w.finish()
        w.sent()
    for one in (gather_go, gather_two, spread, spread_n, spread_o):
        one.sent()
    for k in range(PARTS):
        for d in (1, 2, 3):
            share(k, d).wait_send()
            share_c(k, d).wait_send()
            piece = sums3.at[k, z ^ d]
            remote(piece, piece, c_send.at[k, d - 1], c_recv.at[k, d - 1], at_line(z ^ d, core)).wait_recv()
        total = jnp.sum(jnp.sum(sums3[k], axis=0), axis=0, keepdims=True)
        at = slice(k * PART, (k + 1) * PART)
        s2 = scale_two[:, at]
        coef[:, at] = s2 * s2 * s2 * (total / width)
    for j in range(3):
        keep_up(j + 3).wait()
        send_up(j).wait()
    keep_down().wait()
    send_down().wait()
    for copy in last:
        copy.wait()


def back_kernel(
    width,
    y, dn2_h, g_h, x_own, scale_two, scale_one, coef_two, gains, masks, par, gates_t, m_h, br_h,
    b_h, p_h, u_h, r_h, i_h, h_h, q_h, n1_h, f_own, f_got, fd_own, fd_got,
    input_grad, tiny_v, tiny_g, f_sum, f_land, fd_sum, fd_land, g_sum, g_land, gm_sum, gm_land,
    sums, coef, m_n, br_n, b_s, p_s, u_s, r_s, i_s, h_s, dyf, dbp, dy, dn1, dq, du, dri, a_c, l_c, carry_s, own, held,
    qv, n1, f_a, f_b, fd_a, fd_b, feed_part, mix_part, small, gate_grad, g_s, g_got, gm_got,
    vec, vec_in, vec_all, gd, gd_in, gd_all,
    c_sem, k_sem, l_send, l_recv, g_send, g_recv, s_send, s_recv, r_send, r_recv,
    f_sem, f_send, f_recv, d_send, d_recv, d_own, q_send, q_recv, n_send, n_recv, v_send, v_recv,
):
    row, z, core = place()
    block, seq = y.shape
    PART, PARTS = LATE, seq // LATE

    def lanes(part):
        return pl.ds(pl.multiple_of(part * PART, PART), PART)

    half = block // 2
    chan = b_s.shape[1]
    hc = chan // 2
    sibling = {"col": 2 * z + (1 - core)}
    met = greet(row, z, core, True, True)
    load_g = pltpu.make_async_copy(g_h, g_s, c_sem.at[0])
    load_g.start()
    dn2 = dn1
    load_d = pltpu.make_async_copy(dn2_h, dn2, c_sem.at[5])
    load_d.start()
    load_m = pltpu.make_async_copy(m_h, m_n, c_sem.at[1])
    load_m.start()
    load_b = pltpu.make_async_copy(br_h, br_n, c_sem.at[2])
    load_b.start()
    load_q = pltpu.make_async_copy(q_h, qv, c_sem.at[3])
    load_n = pltpu.make_async_copy(n1_h, n1, c_sem.at[4])
    kept = (b_s, p_s, u_s, r_s, i_s, h_s)
    srcs = (b_h, p_h, u_h, r_h, i_h, h_h)

    def fetch(n, part):
        if kept[n] is p_s or kept[n] is h_s:
            at = pl.ds(pl.multiple_of(part * PART, 128), PART + 128)
        else:
            at = lanes(part)
        return pltpu.make_async_copy(srcs[n].at[:, at], kept[n].at[part % 2], k_sem.at[n, part % 2])

    def fetch_all(part):
        for n in range(len(kept)):
            fetch(n, part).start()

    fetch_all(PARTS - 1)
    load_q.start()
    load_n.start()
    du[:, 0:128] = jnp.zeros((chan, 128), F32)
    carry_s[...] = jnp.zeros(carry_s.shape, F32)
    small[...] = jnp.zeros(small.shape, F32)
    gate_grad[...] = jnp.zeros(gate_grad.shape, F32)

    load_d.wait()
    load_g.wait()
    gather = Gather(dyf, g_send, g_recv, z, core, block, back=True)

    def outer(part):
        here = slice(part * PART, (part + 1) * PART)

        def one(i):
            at = rows_of(i, 64)
            s2 = scale_two[0:1, here]
            d, v = dn2[at, here], y[at, here]
            w = fold(d * v * s2)
            feed_part[at, :] = w if part == PARTS - 1 else feed_part[at, :] + w
            few = PART // g_s.shape[2]
            g = jnp.concatenate([g_s[part * few + j, at, :] for j in range(few)], axis=1)
            v = g.astype(F32) + (s2 * (gains[at, 9:10] * d) - v * coef_two[0:1, here])
            dy[at, here] = v
            dyf[part, pl.ds(pl.multiple_of(z * block + i * 64, 64), 64), :] = v.astype(BF16)

        blocks(block // 64, one)

    outer(PARTS - 1)
    met()
    gather.send(0, 0)
    for part in range(PARTS - 2, -1, -1):
        outer(part)
    gather.forward(1, 0)
    gather.send(0, 1)
    gather.forward(2, 0)
    gather.forward(1, 1)
    gather.send(0, 2)
    spread = Spread(lambda k, s: own.at[k, s], held, s_send, s_recv, z, core)
    load_m.wait()
    load_b.wait()
    final = lax.broadcasted_iota(jnp.int32, (128, PART), 1) == PART - 1

    f_arrays = ((f_own, f_got, f_a, f_b, f_sum, f_land), (fd_own, fd_got, fd_a, fd_b, fd_sum, fd_land))

    def f_loads(d):
        pulls = []
        for n, (ours, theirs, a, b, _, _) in enumerate(f_arrays):
            if n == 0:
                piece = (rows_of(row ^ d, block), slice(None))
            else:
                piece = (slice(None), pl.ds(pl.multiple_of((row ^ d) * block, 128), block))
            pulls.append(pltpu.make_async_copy(ours.at[piece], a.at[d], f_sem.at[n, 0]))
            pulls.append(pltpu.make_async_copy(theirs.at[piece], b, f_sem.at[n, 1]))
        return pulls

    def f_out(d):
        outs = []
        for n, (_, _, a, _, kept_at, land) in enumerate(f_arrays):
            if d == 0:
                outs.append(pltpu.make_async_copy(a.at[0], kept_at, f_send.at[n, 0]))
            else:
                outs.append(
                    remote(a.at[d], land.at[d - 1], f_send.at[n, d], f_recv.at[n, d], {"row": row ^ d})
                )
        return outs

    def f_part(d):
        for pull in f_loads(d):
            pull.wait()
        for _, _, a, b, _, _ in f_arrays:

            def add(i):
                at = rows_of(i, 64)
                a[d, at, :] = (a[d, at, :].astype(F32) + b[at, :].astype(F32)).astype(BF16)

            blocks(b.shape[0] // 64, add)
        for out in f_out(d):
            out.start()
        if d > 0:
            for pull in f_loads(d - 1):
                pull.start()

    def f_step(t):
        for d in range(LINE):
            pl.when(t == LINE - 1 - d)(functools.partial(f_part, d))

    for pull in f_loads(LINE - 1):
        pull.start()

    lru = hc

    def send_m():
        return remote(m_n.at[rows_of(1 - core, lru), :], gm_got, d_send.at[1], d_recv.at[1], sibling)

    def work(t):
        k = PARTS - 1 - t
        here = lanes(k)
        wide = pl.ds(pl.multiple_of(k * PART, 128), PART + 128)
        slot = k % 2
        for n in range(len(kept)):
            fetch(n, k).wait()

        @pl.when(k > 0)
        def _():
            fetch_all(k - 1)

        dq[...] = dot(m_n[...], dyf[k])

        @pl.when(t == PARTS - 1)
        def _():
            load_q.wait()
            for low in range(0, width, 2 * block):
                piece = slice(low, low + 2 * block)
                m_n[:, piece] = dot_nt(qv[...], tokens_of(dyf, piece)).astype(BF16)
            send_m().start()

        def before(i):
            ch = rows_of(i, 64)
            c = i // (hc // 64)
            low = pl.ds(pl.multiple_of(c * hc + i * 64, 64), 64)
            pr = par[ch, :]
            d = dq[ch, :]
            act, slope = gelu_parts(b_s[slot, ch, :])
            dbp[low, here] = (d * h_s[slot, ch, :][:, 128:] * slope).astype(BF16)
            l_c[ch, :] = d * act
            a_c[ch, :] = jnp.exp(-(r_s[slot, ch, :] * pr[:, 7:8]))

        blocks(chan // 64, before)
        gather.middle(t)

        def recur(i):
            ch = rows_of(i, 128)
            start = masks[0:1, here] > 0.5
            a, lam = jnp.where(start, 0.0, a_c[ch, :]), l_c[ch, :]
            lam = lam + jnp.where(final, carry_s[ch, :][:, 0:1], 0.0)
            w = jnp.where(final, 0.0, pltpu.roll(a, PART - 1, 1))
            shift = 1
            while shift < PART:
                lam = lam + w * pltpu.roll(lam, PART - shift, 1)
                if shift * 2 < PART:
                    w = w * pltpu.roll(w, PART - shift, 1)
                shift *= 2
            carry_s[ch, :] = jnp.broadcast_to((a * lam)[:, 0:1], (128, 128))
            l_c[ch, :] = lam

        blocks(chan // 128, recur)
        f_step(t)

        def after(i):
            ch = rows_of(i, 64)
            du[ch, PART:] = du[ch, 0:128]
            pr = par[ch, :]
            start = masks[0:1, here] > 0.5
            lam, a0 = l_c[ch, :], a_c[ch, :]
            earlier = pltpu.roll(h_s[slot, ch, :], 1, 1)[:, 128:]
            r, gate, u = r_s[slot, ch, :], i_s[slot, ch, :], u_s[slot, ch, :]
            m0 = jnp.sqrt(1.0 - a0 * a0 + FLOOR)
            m = jnp.where(start, 1.0, m0)
            lm = lam * m
            lu = lam * u
            du[ch, 0:PART] = lm * gate
            da = jnp.where(start, 0.0, lam * earlier - (lu * gate) * (a0 / m0)) * a0
            dr = da * (-pr[:, 7:8]) * (r * (1.0 - r))
            di = lu * m * (gate * (1.0 - gate))
            g, o = i // 4, (i % 4) * 64
            dri[pl.ds(pl.multiple_of(g * 512 + o, 64), 64), :] = dr.astype(BF16)
            dri[pl.ds(pl.multiple_of(g * 512 + 256 + o, 64), 64), :] = di.astype(BF16)
            small[5, ch, :] += fold(dr)
            small[6, ch, :] += fold(di)
            small[7, ch, :] += fold(da * r)

        blocks(chan // 64, after)
        for g in range(chan // 256):
            at = slice(g * 256, (g + 1) * 256)
            dd = dri[g * 512 : (g + 1) * 512, :]
            du[at, 0:PART] += dot(gates_t[g], dd)
            gate_grad[g] += dot_nt(u_s[slot, at, :].astype(BF16), dd)

        def conv(i):
            ch = rows_of(i, 64)
            c = i // (hc // 64)
            low = pl.ds(pl.multiple_of((c + 1) * hc + i * 64, 64), 64)
            pr = par[ch, :]
            follow = du[ch, :]
            window = p_s[slot, ch, :]
            d = follow[:, :PART]
            dp = pr[:, 0:1] * d
            small[4, ch, :] += fold(d)
            small[0, ch, :] += fold(d * window[:, 128:])
            for lag in (1, 2, 3):
                kd = follow * masks[lag : lag + 1, wide]
                dp = dp + pr[:, lag : lag + 1] * pltpu.roll(kd, PART + 128 - lag, 1)[:, :PART]
                small[lag, ch, :] += fold(kd[:, :PART] * pltpu.roll(window, lag, 1)[:, 128:])
            dbp[low, here] = dp.astype(BF16)

        blocks(chan // 64, conv)
        whole = dot(br_n[...], dbp[:, here])
        for s in range(LINE):
            own[t, s] = whole[s * block : (s + 1) * block, :].astype(own.dtype)

    def finish(t, total):
        k = PARTS - 1 - t

        sums[k, z] = jnp.zeros(sums.shape[2:], F32)

        @pl.when(t == 0)
        def _():
            mix_part[...] = jnp.zeros(mix_part.shape, F32)

        def add(i):
            at = pl.ds(pl.multiple_of(i * 64, 64), 64)
            d = total(pl.multiple_of(i * 64, 64), 64)
            dn1[at, lanes(k)] = d
            w = d * x_own[at, lanes(k)].astype(F32)
            sums[k, z] += eight(w * gains[at, 8:9])
            w = w * scale_one[0:1, lanes(k)]
            mix_part[at, :] += fold(w)

        blocks(block // 64, add)
        for d in (1, 2, 3):
            share(k, d).start()

    def share(k, d):
        return remote(sums.at[k, z], sums.at[k, z], l_send.at[k, d - 1], l_recv.at[k, d - 1], at_line(z ^ d, core))

    def step(t, carry):
        gather.arrive(2, t)
        work(t)
        spread.serve(t, finish)
        return carry

    lax.fori_loop(0, PARTS, step, 0)
    load_n.wait()


    def cols_of(side):
        return pl.ds(pl.multiple_of(side * 2 * lru, 128), 2 * lru)

    def send_br():
        return remote(br_n.at[:, cols_of(1 - core)], g_got, d_send.at[0], d_recv.at[0], sibling)

    def grad_br(side):
        for low in range(0, width, 2 * block):
            piece = slice(low, low + 2 * block)
            br_n[piece, cols_of(side)] = dot_nt(tokens_of(n1, piece), dbp[rows_of(side, 2 * lru), :]).astype(BF16)

    def out_br(d):
        piece = br_n.at[rows_of(row ^ d, block), cols_of(core)]
        if d == 0:
            return pltpu.make_async_copy(piece, g_sum, d_own.at[0])
        return remote(piece, g_land.at[d - 1], q_send.at[0, d - 1], q_recv.at[0, d - 1], {"row": row ^ d})

    def out_m(d):
        piece = m_n.at[rows_of(core, lru), pl.ds(pl.multiple_of((row ^ d) * block, 128), block)]
        if d == 0:
            return pltpu.make_async_copy(piece, gm_sum, d_own.at[1])
        return remote(piece, gm_land.at[d - 1], q_send.at[1, d - 1], q_recv.at[1, d - 1], {"row": row ^ d})

    def drain(i, carry):
        t = PARTS + i

        @pl.when(i == 0)
        def _():
            grad_br(1 - core)
            send_br().start()
            send_m().wait_recv()

            def add(j):
                at = rows_of(j, 64)
                to = pl.ds(pl.multiple_of(core * lru + j * 64, 64), 64)
                m_n[to, :] = (m_n[to, :].astype(F32) + gm_got[at, :].astype(F32)).astype(BF16)

            blocks(lru // 64, add)
            for d in (3, 2, 1, 0):
                out_m(d).start()
            grad_br(core)

        @pl.when(i == 1)
        def _():
            send_br().wait_recv()

            def add(j):
                at = rows_of(j, 64)
                br_n[at, cols_of(core)] = (br_n[at, cols_of(core)].astype(F32) + g_got[at, :].astype(F32)).astype(BF16)

            blocks(width // 64, add)
            for d in (3, 2, 1, 0):
                out_br(d).start()
        spread.serve(t, finish)
        pl.when(i == 0)(tiny_open)
        pl.when(i == 1)(tiny_more)
        return carry

    mine = pl.ds(pl.multiple_of(core * seq, seq), seq)
    lane = lax.broadcasted_iota(jnp.int32, (64, 128), 1)
    swap_gd = remote(gd.at[1 - core], gd_in, v_send.at[0], v_recv.at[0], sibling)
    rows_gd = [
        remote(gd_all.at[0], gd_all.at[d], n_send.at[0, d - 1], n_recv.at[0, d - 1], {"row": row ^ d}) for d in (1, 2, 3)
    ]

    def tiny_open():
        for side in (0, 1):
            for e in range(4):
                at = slice(e * 64, (e + 1) * 64)
                gd[side, at, 0:64] = gate_grad[side, at, e * 64 : (e + 1) * 64]
                gd[side, at, 64:128] = gate_grad[side, at, 256 + e * 64 : 256 + (e + 1) * 64]
        swap_gd.start()

    def columns(parts, at):
        total = jnp.zeros((64, 128), F32)
        for n, part in enumerate(parts):
            total = total + jnp.where(lane == n, jnp.sum(part(at), axis=1, keepdims=True), 0.0)
        return total

    def tiny_more():
        swap_gd.wait()
        gd_all[0] = gd[core] + gd_in[...]
        for copy in rows_gd:
            copy.start()
        vec[...] = jnp.zeros(vec.shape, F32)
        for j in range(chan // 64):
            at = slice(j * 64, (j + 1) * 64)
            v = columns([lambda at, n=n: small[n, at, :] for n in range(8)], at)
            vec[0, :, at] = v.T[0:8, :]

    lax.fori_loop(0, LINE - 1, drain, 0)
    for j in range(block // 64):
        at = slice(j * 64, (j + 1) * 64)
        v = columns([lambda at: mix_part[at, :], lambda at: feed_part[at, :]], at)
        vec[1, :, at] = v.T[0:8, :]
    swap_vec = remote(vec, vec_in, v_send.at[1], v_recv.at[1], sibling)
    swap_vec.start()
    for k in range(PARTS):
        for d in (1, 2, 3):
            share(k, d).wait_send()
            piece = sums.at[k, z ^ d]
            remote(piece, piece, l_send.at[k, d - 1], l_recv.at[k, d - 1], at_line(z ^ d, core)).wait_recv()
        total = jnp.sum(jnp.sum(sums[k], axis=0), axis=0, keepdims=True)
        at = slice(k * PART, (k + 1) * PART)
        s1 = scale_one[:, at]
        coef[:, at] = s1 * s1 * s1 * (total / width)

    def last(i):
        at = rows_of(i, 16)
        v = dy[at, :] + (
            scale_one[0:1, :] * (gains[at, 8:9] * dn1[at, :]) - x_own[at, :].astype(F32) * coef[0:1, :]
        )
        dy[at, :] = v

    blocks(block // 16, last)
    back = remote(dy.at[rows_of(1 - core, half), :], input_grad.at[:, mine], r_send, r_recv, sibling)
    back.start()
    keep_in = pltpu.make_async_copy(dy.at[rows_of(core, half), :], input_grad.at[:, mine], d_own.at[3])
    keep_in.start()
    swap_vec.wait()
    vec_all[0] = vec[...] + vec_in[...]
    rows_vec = [
        remote(vec_all.at[0], vec_all.at[d], n_send.at[1, d - 1], n_recv.at[1, d - 1], {"row": row ^ d}) for d in (1, 2, 3)
    ]
    for copy in rows_vec:
        copy.start()
    spread.sent()
    gather.sent()
    for copy in rows_gd + rows_vec:
        copy.wait()
    for every, out in ((gd_all, tiny_g), (vec_all, tiny_v)):
        first, second = every[row % 2], every[1 - row % 2]
        third, fourth = every[2 + row % 2], every[3 - row % 2]
        out[...] = (first + second) + (third + fourth)
    for d in range(LINE):
        for out in f_out(d):
            out.wait()
    send_br().wait_send()
    send_m().wait_send()
    for d in (0, 1, 2, 3):
        out_br(d).wait()
        out_m(d).wait()
    for copy in (keep_in, back):
        copy.wait()


def last_kernel(
    f_sum, f_land, fd_sum, fd_land, g_sum, g_land, gm_sum, gm_land, result_in, grad_in, tiny_v, tiny_g, lambdas,
    s_b, s_r, s_m, s_g, s_u, s_d, result, input_grad, taps, offs, bias_r, bias_a, decay, mix, feed, retain, admit,
):
    lru, ff, half = s_b.shape[1], s_g.shape[0], mix.shape[1]

    def four(first, others):
        return first[...].astype(F32) + others[0].astype(F32) + (others[1].astype(F32) + others[2].astype(F32))

    v = four(f_sum, f_land)
    s_g[...] = v.T[:ff, :]
    s_u[...] = v.T[ff:, :]
    v = four(g_sum, g_land)
    s_b[...] = v[:, :lru]
    s_r[...] = v[:, lru:]
    s_d[...] = four(fd_sum, fd_land)
    result[...] = result_in[...]
    input_grad[...] = grad_in[...]

    @pl.when(pl.program_id(0) == 0)
    def _():
        core = place()[2]
        s_m[...] = four(gm_sum, gm_land)
        small = tiny_v[0, :, pl.ds(pl.multiple_of(core * lru, 128), lru)]
        taps[...] = small[0:4]
        offs[...] = small[4:5]
        bias_r[...] = small[5:6]
        bias_a[...] = small[6:7]
        decay[...] = small[7:8] * (8.0 * jax.nn.sigmoid(-lambdas[...]))
        gains = jnp.where(core == 0, tiny_v[1, :, 0:half], tiny_v[1, :, half : 2 * half])
        mix[...] = gains[0:1]
        feed[...] = gains[1:2]
        for e in range(retain.shape[0]):
            at = slice(e * 64, (e + 1) * 64)
            retain[e] = tiny_g[at, 0:64]
            admit[e] = tiny_g[at, 64:128]


ANY = pl.BlockSpec(memory_space=pl.ANY)
VM = pl.BlockSpec(memory_space=pltpu.VMEM)
DMA = pltpu.SemaphoreType.DMA
ROOM = 62 * 1024 * 1024


def shape(dims, kind):
    return jax.ShapeDtypeStruct(dims, kind)


def call(kernel, ins, outs, scratch, ident, name, flops):
    return pl.pallas_call(
        kernel,
        out_shape=[o[0] for o in outs],
        in_specs=ins,
        out_specs=[o[1] for o in outs],
        scratch_shapes=scratch,
        name=name,
        compiler_params=pltpu.CompilerParams(
            collective_id=ident, has_side_effects=True, vmem_limit_bytes=ROOM
        ),
        cost_estimate=pl.CostEstimate(flops=flops, bytes_accessed=40000000, transcendentals=0),
    )


def fast_body(
    inputs, segments, mix_gain, branch_weight, recur_weight, kernel, offsets, retain_weight, retain_bias,
    admit_weight, admit_bias, lambdas, merge_weight, feed_gain, gate_weight, up_weight, down_weight, cotangent,
):
    half, tokens = inputs.shape
    block, seq, width = 2 * half, tokens // 2, D
    lru, heads = branch_weight.shape[1], retain_weight.shape[0]
    chan = 2 * lru
    ff = gate_weight.shape[1]
    hid = 2 * ff
    rows = branch_weight.shape[0]
    cols = merge_weight.shape[1]
    gu_s = jnp.concatenate([gate_weight, up_weight], axis=1).T

    f_tok = lambda n, kind=F32: shape((n, seq), kind)
    padded = (shape((chan, 128 + seq), F32), ANY)
    state = [(f_tok(chan), ANY), padded, *[(f_tok(chan), ANY)] * 3, padded]
    line = [DMA((3,)), DMA((3,))]
    steps = [DMA((2, 3, PARTS)), DMA((2, 3, PARTS))]
    sums = [DMA((2, PARTS, LINE)), DMA((2, PARTS, LINE))]
    held = pltpu.VMEM((PARTS, LINE + 1, block, PART), BF16)
    own_low = pltpu.VMEM((PARTS, LINE, block, PART), BF16)
    tok = lambda n, kind=F32, lead=0: pltpu.VMEM((n, lead + seq), kind)
    one = lambda n, kind=F32, lead=0: pltpu.VMEM((n, lead + PART), kind)
    grad_gu, grad_d = (shape((width, 2 * ff), BF16), ANY), (shape((ff, width), BF16), ANY)
    low = lambda n, m: (shape((n, m), BF16), ANY)
    parted = lambda n: (shape((PARTS, n, PART), BF16), ANY)
    by_part = lambda n: pltpu.VMEM((PARTS, n, PART), BF16)

    (masks, par, gains, gates, coef, scale_one, scale_two, y, n1, q, x_own, g, b, p, u, r, i, h, result, dn2, _, _, f_own, f_got, fd_own, fd_got,
     br_n, m_n) = call(
        functools.partial(forward_kernel, width, EPS),
        [ANY] * 2 + [VM] * 13 + [ANY] * 2,
        [(shape((8, seq + 128), F32), VM), (shape((chan, 16), F32), VM), (shape((block, 16), F32), VM), (shape((2, lru, 2 * lru), BF16), VM),
         (f_tok(8), VM), (f_tok(8), VM), (f_tok(8), VM), (f_tok(block), ANY), parted(width), low(chan, seq), low(block, seq), parted(block)]
        + state + [low(half, tokens), (f_tok(block), ANY), low(2 * hid, seq), low(hid, seq), grad_gu, grad_gu, grad_d, grad_d,
                   low(width, 2 * chan), low(chan, width)],
        [pltpu.VMEM((LINE, 8, seq), F32), pltpu.VMEM((PARTS, LINE, 8, PART), F32), pltpu.VMEM((PARTS, LINE, 8, PART), F32),
         pltpu.VMEM((16, lru), F32), pltpu.VMEM((2 * lru, rows), BF16), pltpu.VMEM((rows, 2 * lru), BF16), pltpu.VMEM((cols, lru), BF16),
         pltpu.VMEM((2, 16, lru), F32), pltpu.VMEM((2, 2) + retain_weight.shape, F32), pltpu.VMEM((2, 2 * lru, lru), BF16),
         pltpu.VMEM((2, 2 * lru, lru), BF16), by_part(width), by_part(width),
         by_part(width), tok(block, BF16), tok(block), one(block), one(chan, BF16),
         one(chan, F32, 128), one(chan, F32, 128), one(max(5 * chan, 3 * hid)), one(chan, BF16), one(chan, BF16),
         own_low, held, held, held, pltpu.VMEM((2 * hid, width), BF16), pltpu.VMEM((width, 2 * hid), BF16),
         pltpu.VMEM((hid, width), BF16), pltpu.VMEM((width, hid), BF16), one(hid, BF16), one(2 * hid, BF16),
         DMA((5,)), DMA((5,)), DMA((5,)), DMA((PARTS,)), DMA((PARTS,)), DMA((PARTS,))] + line + [DMA((PARTS, 3)), DMA((PARTS, 3))] * 2 + steps * 3 + sums * 3
        + [DMA((7, 7)), DMA((7, 7)), DMA((7,)), DMA((7,)), DMA((11,)), DMA((4,)), DMA((4,)), DMA((4,))],
        0, "forward", 50 * 10**9,
    )(inputs, cotangent, segments[None, :], kernel, offsets[None, :], retain_bias[None, :], admit_bias[None, :],
      lambdas[None, :], mix_gain[None, :], feed_gain[None, :], retain_weight, admit_weight, branch_weight, recur_weight,
      merge_weight, gu_s, down_weight)

    late = seq // LATE
    pair = lambda lead=0: pltpu.VMEM((2, chan, lead + LATE), F32)
    one = lambda n, kind=F32, lead=0: pltpu.VMEM((n, lead + LATE), kind)
    steps = [DMA((2, 3, late)), DMA((2, 3, late))]
    sums = [DMA((2, late, LINE)), DMA((2, late, LINE))]
    held = pltpu.VMEM((late, LINE + 1, block, LATE), BF16)
    own_low = pltpu.VMEM((late, LINE, block, LATE), BF16)
    land = lambda n, m: ((shape((n, m), BF16), ANY), (shape((3, n, m), BF16), ANY))
    input_grad, tiny_v, tiny_g, *sums_of = call(
        functools.partial(back_kernel, width),
        [VM] + [ANY] * 2 + [VM] * 8 + [ANY] * 14,
        [(shape((half, tokens), F32), ANY), (shape((2, 8, chan), F32), VM),
         (shape((lru, 128), F32), VM), *land(cols, 2 * ff), *land(ff, cols), *land(cols, 2 * lru), *land(lru, cols)],
        [pltpu.VMEM((late, LINE, 8, LATE), F32), pltpu.VMEM((8, seq), F32),
         pltpu.VMEM((chan, width), BF16), pltpu.VMEM((width, 2 * chan), BF16),
         pair(), pair(128), pair(), pair(), pair(), pair(128), pltpu.VMEM((late, width, LATE), BF16), tok(2 * chan, BF16),
         tok(block), tok(block), one(chan), one(chan, F32, 128), one(2 * chan, BF16),
         one(chan), one(chan), pltpu.VMEM((chan, 128), F32), own_low, held,
         tok(chan, BF16), by_part(width), pltpu.VMEM((4, cols, 2 * ff), BF16), pltpu.VMEM((cols, 2 * ff), BF16),
         pltpu.VMEM((4, ff, cols), BF16), pltpu.VMEM((ff, cols), BF16),
         pltpu.VMEM((block, 128), F32), pltpu.VMEM((block, 128), F32), pltpu.VMEM((8, chan, 128), F32),
         pltpu.VMEM((2, lru, 2 * lru), F32), by_part(block), pltpu.VMEM((width, 2 * lru), BF16),
         pltpu.VMEM((lru, width), BF16), pltpu.VMEM((2, 8, chan), F32), pltpu.VMEM((2, 8, chan), F32),
         pltpu.VMEM((4, 2, 8, chan), F32), pltpu.VMEM((2, lru, 128), F32), pltpu.VMEM((lru, 128), F32),
         pltpu.VMEM((4, lru, 128), F32), DMA((7,)), DMA((6, 2))] + [DMA((late, 3)), DMA((late, 3))] + steps + sums
        + [DMA, DMA, DMA((2, 2)), DMA((2, LINE)), DMA((2, LINE)), DMA((2,)), DMA((2,)), DMA((4,))]
        + [DMA((2, 3)), DMA((2, 3)), DMA((2, 3)), DMA((2, 3)), DMA((2,)), DMA((2,))],
        2, "mix_backward", 10 * 10**9,
    )(y, dn2, g, x_own, scale_two, scale_one, coef, gains, masks, par, gates, m_n, br_n, b, p, u, r, i, h,
      q, n1, f_own, f_got, fd_own, fd_got)

    line_of = shape((1, lru), F32)
    cuts = 3
    rows_in = lambda *dims: pl.BlockSpec((dims[0] // cuts,) + dims[1:], lambda n: (n,) + (0,) * (len(dims) - 1))
    three = lambda *dims: pl.BlockSpec((3, dims[0] // cuts, dims[1]), lambda n: (0, n, 0))
    still = lambda *dims: pl.BlockSpec(dims, lambda n: (0,) * len(dims))
    sizes = ((cols, 2 * ff), (ff, cols), (cols, 2 * lru), (lru, cols))
    big = ((cols, lru), (cols, lru), (lru, cols), (ff, cols), (ff, cols), (ff, cols))
    across = pl.BlockSpec((ff, cols // cuts), lambda n: (0, n))
    flat = ((4, lru),) + ((1, lru),) * 4 + ((1, half),) * 2 + ((heads, 64, 64),) * 2
    s_b, s_r, s_m, s_g, s_u, s_d, result, input_grad, taps, offs, bias_r, bias_a, decay, mix, feed, retain, admit = pl.pallas_call(
        last_kernel,
        grid=(cuts,),
        out_shape=[shape(d, F32) for d in big] + [shape((half, tokens), BF16), shape((half, tokens), F32)]
        + [shape(d, F32) for d in flat],
        in_specs=[spec(*d) for d in sizes[:3] for spec in (rows_in, three)] + [still(lru, cols), still(3, lru, cols)]
        + [rows_in(half, tokens)] * 2
        + [still(2, 8, chan), still(lru, 128), still(1, lru)],
        out_specs=[rows_in(cols, lru)] * 2 + [still(lru, cols)] + [across] * 2 + [rows_in(ff, cols)] + [rows_in(half, tokens)] * 2 + [still(*d) for d in flat],
        name="last_sums",
        compiler_params=pltpu.CompilerParams(vmem_limit_bytes=ROOM),
    )(*sums_of, result, input_grad, tiny_v, tiny_g, lambdas[None, :])
    return (
        result,
        input_grad,
        mix[0],
        s_b,
        s_r,
        taps,
        offs[0],
        retain,
        bias_r[0],
        admit,
        bias_a[0],
        decay[0],
        s_m,
        feed[0],
        s_g.T,
        s_u.T,
        s_d,
    )


def suits(mesh, args):
    return (
        dict(mesh.shape) == {"row": 4, "col": 8}
        and args[0].shape == (D, 8 * SEQ)
        and args[3].shape == (D, 2048)
        and args[14].shape == (D, 4608)
        and args[7].shape == (32, 64, 64)
    )


def solution(mesh):
    in_specs = (
        P("col", "row"),
        P("row"),
        P("col"),
        P("row", "col"),
        P("row", "col"),
        P(None, "col"),
        P("col"),
        P("col", None, None),
        P("col"),
        P("col", None, None),
        P("col"),
        P("col"),
        P("col", "row"),
        P("col"),
        P("row", "col"),
        P("row", "col"),
        P("col", "row"),
        P("col", "row"),
    )
    out_specs = (
        P("col", "row"),
        P("col", "row"),
        P("col"),
        P("row", "col"),
        P("row", "col"),
        P(None, "col"),
        P("col"),
        P("col", None, None),
        P("col"),
        P("col", None, None),
        P("col"),
        P("col"),
        P("col", "row"),
        P("col"),
        P("row", "col"),
        P("row", "col"),
        P("col", "row"),
    )
    def run(*args):
        chosen = fast_body if suits(mesh, args) else body
        return jax.shard_map(
            chosen, mesh=mesh, in_specs=in_specs, out_specs=out_specs, check_vma=False
        )(*args)

    return run
```

```python
import functools

import jax
import jax.numpy as jnp
from jax import lax
from jax.experimental import pallas as pl
from jax.experimental.pallas import tpu as pltpu
from jax.sharding import PartitionSpec as P

D = 1536
SEQ = 1024
MICRO = 2


HIGH = lax.Precision.HIGHEST
EPS = 1e-06
POWER = 8.0
FLOOR = 0.01


def combine(earlier, later):
    first_a, first_b = earlier
    second_a, second_b = later
    return (first_a * second_a, second_a * first_b + second_b)


def mixer(
    branch_pre,
    lru_pre,
    segs,
    kernel,
    offsets,
    retain_weight,
    retain_bias,
    admit_weight,
    admit_bias,
    lambdas,
):
    length = lru_pre.shape[0]
    channels = lru_pre.shape[1]
    conv = offsets + kernel[0] * lru_pre
    for lag in range(1, kernel.shape[0]):
        shifted = jnp.concatenate(
            [jnp.zeros((lag, channels), lru_pre.dtype), lru_pre[:-lag]], axis=0
        )
        prior = jnp.concatenate([jnp.full((lag,), -1, jnp.int32), segs[:-lag]])
        keep = (prior == segs).astype(lru_pre.dtype)
        conv = conv + kernel[lag] * shifted * keep[:, None]
    heads = retain_weight.shape[0]
    blocks = conv.reshape(length, heads, channels // heads)
    retain = jax.nn.sigmoid(
        jnp.einsum("thi,hij->thj", blocks, retain_weight, precision=HIGH).reshape(length, channels)
        + retain_bias
    )
    admit = jax.nn.sigmoid(
        jnp.einsum("thi,hij->thj", blocks, admit_weight, precision=HIGH).reshape(length, channels)
        + admit_bias
    )
    decay = jnp.exp(-POWER * retain * jax.nn.softplus(-lambdas))
    factor = jnp.sqrt(1.0 - decay * decay + FLOOR)
    starts = jnp.concatenate([jnp.ones((1,), bool), segs[1:] != segs[:-1]])
    decay = jnp.where(starts[:, None], 0.0, decay)
    factor = jnp.where(starts[:, None], 1.0, factor)
    _, state = lax.associative_scan(combine, (decay, factor * admit * conv), axis=0)
    return jax.nn.gelu(branch_pre) * state


def geglu(gate, upper):
    return jax.nn.gelu(gate) * upper


def contract_rows(left, right):
    return lax.dot_general(
        left, right, (((0,), (0,)), ((), ())), preferred_element_type=jnp.float32
    )


def contract_cols(left, right):
    return lax.dot_general(
        left, right, (((1,), (1,)), ((), ())), preferred_element_type=jnp.float32
    )


def contract_cross(left, right):
    return lax.dot_general(
        left, right, (((0,), (1,)), ((), ())), preferred_element_type=jnp.float32
    )


def norm_forward(resid, gain):
    total = lax.psum(jnp.sum(resid * resid, axis=0), "col")
    scale = lax.rsqrt(total / D + EPS)[None, :]
    return (scale, (resid * scale * gain[:, None]).astype(jnp.bfloat16))


def norm_backward(resid, scale, gain, grad_normed):
    weighted = grad_normed * gain[:, None]
    total = lax.psum(jnp.sum(weighted * resid, axis=0), "col")
    grad_resid = scale * weighted - resid * (scale * scale * scale) * (total / D)[None, :]
    grad_gain = jnp.sum(grad_normed * resid * scale, axis=1)
    return (grad_resid, grad_gain)


def gather_features(normed):
    return lax.all_gather(normed, "col", axis=0, tiled=True)


def gather_cotangent(grad):
    return lax.all_gather(grad, "col", axis=0, tiled=True)


def spread_sum(term):
    return lax.psum_scatter(
        term.astype(jnp.bfloat16), "col", scatter_dimension=0, tiled=True
    ).astype(jnp.float32)


def back_sum(term):
    return spread_sum(term)


def merge_term(whole_merge, mixed_low):
    return spread_sum(contract_cross(whole_merge, mixed_low))


def weight_grads(normed, grad_joined):
    return jnp.dot(
        normed,
        grad_joined,
        preferred_element_type=jnp.float32,
    )


def row_sum(total, axis):
    return lax.psum_scatter(
        total.astype(jnp.bfloat16), "row", scatter_dimension=axis, tiled=True
    ).astype(jnp.float32)


def body(
    inputs,
    segments,
    mix_gain,
    branch_weight,
    recur_weight,
    kernel,
    offsets,
    retain_weight,
    retain_bias,
    admit_weight,
    admit_bias,
    lambdas,
    merge_weight,
    feed_gain,
    gate_weight,
    up_weight,
    down_weight,
    cotangent,
):
    lru_cols = branch_weight.shape[1]
    feed_cols = gate_weight.shape[1]
    mixer_params = (kernel, offsets, retain_weight, retain_bias, admit_weight, admit_bias, lambdas)
    acc_branch = jnp.zeros((D, lru_cols), jnp.float32)
    acc_recur = jnp.zeros((D, lru_cols), jnp.float32)
    acc_gate = jnp.zeros((D, feed_cols), jnp.float32)
    acc_up = jnp.zeros((D, feed_cols), jnp.float32)
    acc_merge = jnp.zeros((lru_cols, D), jnp.float32)
    acc_down = jnp.zeros((feed_cols, D), jnp.float32)
    acc_small = tuple((jnp.zeros_like(p) for p in mixer_params))
    acc_mix = jnp.zeros_like(mix_gain)
    acc_feed = jnp.zeros_like(feed_gain)
    outputs = []
    in_grads = []
    for batch in range(MICRO):
        lower = batch * SEQ
        resid_in = inputs[:, lower : lower + SEQ].astype(jnp.float32)
        grad_out = cotangent[:, lower : lower + SEQ].astype(jnp.float32)
        segs = segments[lower : lower + SEQ]
        whole_branch, whole_recur, whole_gate, whole_up = (
            lax.all_gather(branch_weight, "row", axis=0, tiled=True),
            lax.all_gather(recur_weight, "row", axis=0, tiled=True),
            lax.all_gather(gate_weight, "row", axis=0, tiled=True),
            lax.all_gather(up_weight, "row", axis=0, tiled=True),
        )
        whole_merge, whole_down = (
            lax.all_gather(merge_weight, "row", axis=1, tiled=True),
            lax.all_gather(down_weight, "row", axis=1, tiled=True),
        )
        scale_one, normed_one = norm_forward(resid_in, mix_gain)
        full_one = gather_features(normed_one)
        branch_pre = contract_rows(full_one, whole_branch)
        lru_pre = contract_rows(full_one, whole_recur)

        def local_mixer(bpre, lpre, kern, offs, rweight, rbias, aweight, abias, lams):
            return mixer(bpre, lpre, segs, kern, offs, rweight, rbias, aweight, abias, lams)

        mixed, mixer_pull = jax.vjp(local_mixer, branch_pre, lru_pre, *mixer_params)
        mixed_low = mixed.astype(jnp.bfloat16)
        resid_mid = resid_in + merge_term(whole_merge, mixed_low)
        scale_two, normed_two = norm_forward(resid_mid, feed_gain)
        full_two = gather_features(normed_two)
        gate = contract_rows(full_two, whole_gate)
        upper = contract_rows(full_two, whole_up)
        hidden, geglu_pull = jax.vjp(geglu, gate, upper)
        hidden_low = hidden.astype(jnp.bfloat16)
        result = resid_mid + spread_sum(contract_cross(whole_down, hidden_low))
        outputs.append(result.astype(jnp.bfloat16))
        grad_full = gather_cotangent(grad_out.astype(jnp.bfloat16))
        acc_down = acc_down + contract_cross(hidden_low, grad_full)
        grad_gate, grad_upper = geglu_pull(contract_cross(grad_full, whole_down))
        grad_gate = grad_gate.astype(jnp.bfloat16)
        grad_upper = grad_upper.astype(jnp.bfloat16)
        feed_joined = weight_grads(full_two, jnp.concatenate([grad_gate, grad_upper], axis=1))
        acc_gate = acc_gate + feed_joined[:, :feed_cols]
        acc_up = acc_up + feed_joined[:, feed_cols:]
        grad_normed_two = back_sum(
            contract_cols(whole_gate, grad_gate) + contract_cols(whole_up, grad_upper)
        )
        grad_mid_norm, feed_part = norm_backward(resid_mid, scale_two, feed_gain, grad_normed_two)
        acc_feed = acc_feed + feed_part
        grad_mid = grad_out + grad_mid_norm
        grad_mid_full = gather_cotangent(grad_mid.astype(jnp.bfloat16))
        acc_merge = acc_merge + contract_cross(mixed_low, grad_mid_full)
        pulled = mixer_pull(contract_cross(grad_mid_full, whole_merge))
        grad_branch = pulled[0].astype(jnp.bfloat16)
        grad_lru = pulled[1].astype(jnp.bfloat16)
        acc_small = tuple((total + part for total, part in zip(acc_small, pulled[2:])))
        branch_joined = weight_grads(full_one, jnp.concatenate([grad_branch, grad_lru], axis=1))
        acc_branch = acc_branch + branch_joined[:, :lru_cols]
        acc_recur = acc_recur + branch_joined[:, lru_cols:]
        grad_normed_one = back_sum(
            contract_cols(whole_branch, grad_branch) + contract_cols(whole_recur, grad_lru)
        )
        grad_in_norm, mix_part = norm_backward(resid_in, scale_one, mix_gain, grad_normed_one)
        acc_mix = acc_mix + mix_part
        in_grads.append(grad_mid + grad_in_norm)
    sum_branch, sum_recur, sum_gate, sum_up = (
        row_sum(acc_branch, 0),
        row_sum(acc_recur, 0),
        row_sum(acc_gate, 0),
        row_sum(acc_up, 0),
    )
    sum_merge, sum_down = (
        row_sum(acc_merge, 1),
        row_sum(acc_down, 1),
    )
    summed = lax.psum(
        (
            acc_mix,
            acc_feed,
            acc_small[0],
            acc_small[1],
            acc_small[2],
            acc_small[3],
            acc_small[4],
            acc_small[5],
            acc_small[6],
        ),
        "row",
    )
    result_all = jnp.concatenate(outputs, axis=1)
    input_grad = jnp.concatenate(in_grads, axis=1)
    return (
        result_all,
        input_grad,
        summed[0],
        sum_branch,
        sum_recur,
        summed[2],
        summed[3],
        summed[4],
        summed[5],
        summed[6],
        summed[7],
        summed[8],
        sum_merge,
        summed[1],
        sum_gate,
        sum_up,
        sum_down,
    )


MESH = pl.DeviceIdType.MESH
F32 = jnp.float32
BF16 = jnp.bfloat16
LINE = 4
PART = 128
PARTS = 8
LATE = 256
GELU_A = 0.7978845608028654
GELU_B = 0.044715


def place():
    row, col = lax.axis_index("row"), lax.axis_index("col")
    return row, col // 2, col % 2


def at_line(z, core):
    return {"col": 2 * z + core}


def lanes(part):
    return pl.ds(pl.multiple_of(part * PART, PART), PART)


def rows_of(index, size):
    return pl.ds(pl.multiple_of(index * size, 16), size)


def dot(a, b):
    return lax.dot_general(a, b, (((1,), (0,)), ((), ())), preferred_element_type=F32)


def dot_nt(a, b):
    return lax.dot_general(a, b, (((1,), (1,)), ((), ())), preferred_element_type=F32)


def greet(row, z, core, rows, line):
    barrier = pltpu.get_barrier_semaphore()
    peers = [{"col": 2 * z + (1 - core)}]
    if rows:
        peers += [{"row": row ^ d} for d in (1, 2, 3)]
    if line:
        peers += [at_line(z ^ d, core) for d in (1, 2, 3)]
    for peer in peers:
        pl.semaphore_signal(barrier, inc=1, device_id=peer, device_id_type=MESH)
    return functools.partial(pl.semaphore_wait, barrier, len(peers))


def remote(src, dst, send, recv, peer):
    return pltpu.make_async_remote_copy(
        src_ref=src, dst_ref=dst, send_sem=send, recv_sem=recv, device_id=peer, device_id_type=MESH
    )


class Gather:
    def __init__(self, ref, send, recv, z, core, block, back=False):
        self.parts = ref.shape[0]
        self.ref, self.sems, self.z, self.core = ref, (send, recv), z, core
        self.block, self.back = block, back

    def copy(self, way, hop, step, owner, incoming=False):
        part = self.parts - 1 - step if self.back else step
        piece = self.ref.at[part, rows_of(owner, self.block), :]
        peer = at_line(self.z + (1 if (way == 0) != incoming else -1), self.core)
        return remote(piece, piece, self.sems[0].at[way, hop, step], self.sems[1].at[way, hop, step], peer)

    def each(self, hop, act, incoming):
        z = self.z
        if incoming:
            cases = ((0, z - 1 - hop >= 0, z - 1 - hop), (1, z + 1 + hop < LINE, z + 1 + hop))
        else:
            cases = (
                (0, (z >= hop) & (z < LINE - 1), z - hop),
                (1, (z + hop < LINE) & (z >= 1), z + hop),
            )
        for way, here, owner in cases:
            pl.when(here)(functools.partial(act, way, owner))

    def send(self, hop, step):
        self.each(hop, lambda way, owner: self.copy(way, hop, step, owner).start(), False)

    def arrive(self, hop, step):
        self.each(hop, lambda way, owner: self.copy(way, hop, step, owner, True).wait_recv(), True)

    def forward(self, hop, step):
        self.arrive(hop - 1, step)
        self.send(hop, step)

    def sent(self):
        def one(step, carry):
            for hop in range(LINE - 1):
                self.each(hop, lambda way, owner: self.copy(way, hop, step, owner).wait_send(), False)
            return carry

        lax.fori_loop(0, self.parts, one, 0)

    def middle(self, step, ahead=1):
        for hop in (2, 1, 0):
            later = step + ahead + 2 - hop
            act = self.forward if hop else self.send
            pl.when(later < self.parts)(functools.partial(act, hop, later))


class Spread:
    def __init__(self, own, held, send, recv, z, core):
        self.parts = held.shape[0]
        self.own, self.held, self.sems, self.z, self.core = own, held, (send, recv), z, core

    def copy(self, way, step, hop):
        slot = hop if way == 0 else LINE - hop
        there = slot - 1 if way == 0 else slot + 1
        peer = at_line(self.z + (1 if way == 0 else -1), self.core)
        return remote(
            self.held.at[step, slot],
            self.held.at[step, there],
            self.sems[0].at[way, step, hop],
            self.sems[1].at[way, step, hop - 1],
            peer,
        )

    def landed(self, way, step, hop):
        slot = hop if way == 0 else LINE - hop
        piece = self.held.at[step, slot]
        peer = at_line(self.z + (-1 if way == 0 else 1), self.core)
        remote(piece, piece, self.sems[0].at[way, step, hop], self.sems[1].at[way, step, hop], peer).wait_recv()

    def push(self, way, step, first):
        z = self.z

        def one(i, carry):
            hop = LINE - 1 - i
            owner = z + hop if way == 0 else z - hop
            slot = hop if way == 0 else LINE - hop

            @pl.when((owner >= 0) & (owner < LINE))
            def _():
                @pl.when(first)
                def _():
                    self.held[step, slot] = self.own(step, owner)[...].astype(BF16)

                @pl.when(jnp.logical_not(first))
                def _():
                    self.landed(way, step, hop)
                    total = self.own(step, owner)[...].astype(F32) + self.held[step, slot].astype(F32)
                    self.held[step, slot] = total.astype(BF16)

                self.copy(way, step, hop).start()

            return carry

        lax.fori_loop(0, LINE - 1, one, 0)

    def serve(self, t, finish):
        z = self.z
        step = t - (LINE - 1)

        @pl.when((step >= 0) & (step < self.parts))
        def _():
            @pl.when(z == 0)
            def _():
                self.landed(1, step, 0)
                finish(step, lambda a, n: self.mine(step, a, n) + self.got(step, LINE, a, n))

            @pl.when(z == LINE - 1)
            def _():
                self.landed(0, step, 0)
                finish(step, lambda a, n: self.mine(step, a, n) + self.got(step, 0, a, n))

            @pl.when((z > 0) & (z < LINE - 1))
            def _():
                self.landed(0, step, 0)
                self.landed(1, step, 0)
                finish(
                    step,
                    lambda a, n: self.mine(step, a, n) + (self.got(step, 0, a, n) + self.got(step, LINE, a, n)),
                )

        for way, late, turn in ((1, LINE - 1 - z, z < 2), (0, z, z >= 0), (1, LINE - 1 - z, z >= 2)):
            step = t - late
            pl.when((step >= 0) & (step < self.parts) & turn)(functools.partial(self.push, way, step, late == 0))

    def mine(self, step, start, size):
        return self.own(step, self.z)[pl.ds(start, size), :].astype(F32)

    def got(self, step, slot, start, size):
        return self.held[step, slot, pl.ds(start, size)].astype(F32)

    def sent(self):
        z = self.z

        def one(step, carry):
            for way in (0, 1):
                for hop in range(1, LINE):
                    owner = z + hop if way == 0 else z - hop

                    @pl.when((owner >= 0) & (owner < LINE))
                    def _():
                        self.copy(way, step, hop).wait_send()

            return carry

        lax.fori_loop(0, self.parts, one, 0)


def share_line(ref, send, recv, z, core):
    copies = [
        remote(ref.at[z], ref.at[z], send.at[d - 1], recv.at[d - 1], at_line(z ^ d, core)) for d in (1, 2, 3)
    ]
    for copy in copies:
        copy.start()
    for d in (1, 2, 3):
        piece = ref.at[z ^ d]
        remote(piece, piece, send.at[d - 1], recv.at[d - 1], at_line(z ^ d, core)).wait_recv()
    for copy in copies:
        copy.wait_send()


class Weights:
    def __init__(self, src, dst, send, recv, own, row, z, core, turned, stride=0, start=0):
        self.src, self.dst, self.send, self.recv, self.own = src, dst, send, recv, own
        self.row, self.core, self.turned = row, core, turned
        self.stride, self.first = stride or src.shape[0], start
        self.sibling = {"col": 2 * z + (1 - core)}

    def spot(self, row, core):
        down, right = (row, core) if self.turned else (core, row)
        rows, cols = self.src.shape
        at = pl.ds(pl.multiple_of(down * self.stride + self.first, 16), rows)
        return self.dst.at[at, pl.ds(pl.multiple_of(right * cols, 128), cols)]

    def to_row(self, d):
        return remote(
            self.src, self.spot(self.row, self.core), self.send.at[d], self.recv.at[d], {"row": self.row ^ d}
        )

    def to_sibling(self, d):
        if d == 0:
            return remote(
                self.src, self.spot(self.row, self.core), self.send.at[0], self.recv.at[0], self.sibling
            )
        piece = self.spot(self.row ^ d, self.core)
        return remote(piece, piece, self.send.at[3 + d], self.recv.at[3 + d], self.sibling)

    def local(self):
        return pltpu.make_async_copy(self.src, self.spot(self.row, self.core), self.own)

    def start(self):
        for d in (1, 2, 3):
            self.to_row(d).start()
        self.to_sibling(0).start()
        self.local().start()

    def forward(self):
        for d in (1, 2, 3):
            piece = self.spot(self.row ^ d, self.core)
            remote(piece, piece, self.send.at[d], self.recv.at[d], {"row": self.row ^ d}).wait_recv()
            self.to_sibling(d).start()

    def finish(self):
        self.local().wait()
        for d in (0, 1, 2, 3):
            piece = self.spot(self.row ^ d, 1 - self.core)
            sem = 0 if d == 0 else 3 + d
            remote(piece, piece, self.send.at[sem], self.recv.at[sem], self.sibling).wait_recv()

    def sent(self):
        for d in (1, 2, 3):
            self.to_row(d).wait_send()
            self.to_sibling(d).wait_send()
        self.to_sibling(0).wait_send()


def gelu_parts(b):
    t = jnp.tanh(GELU_A * (b + GELU_B * (b * b * b)))
    half = 0.5 + 0.5 * t
    slope = half + (0.5 * b) * (1.0 - t * t) * (GELU_A + (3.0 * GELU_A * GELU_B) * (b * b))
    return b * half, slope


def eight(v):
    return jnp.sum(v.reshape(v.shape[0] // 8, 8, v.shape[1]), axis=0)


def fold(v):
    total = v[:, 0:128]
    for j in range(1, v.shape[1] // 128):
        total = total + v[:, j * 128 : (j + 1) * 128]
    return total


def tokens_of(ref, piece):
    return jnp.concatenate([ref[k, piece, :] for k in range(ref.shape[0])], axis=1)


def blocks(count, body):
    def one(i, carry):
        body(i)
        return carry

    lax.fori_loop(0, count, one, 0)


def scale_of(ref, eps, width):
    total = jnp.sum(jnp.sum(ref[...], axis=0), axis=0, keepdims=True)
    return lax.rsqrt(total / width + eps)


def forward_kernel(
    width, eps,
    x_in, g_in, segs, taps, offs, bias_r, bias_a, decay, mix, late, retain, admit, branch, recur, mn_s, gu_s, d_s,
    masks, par, gains, gates, coef, scale, scale_two, y_out, n1_out, q_out, x_out, g_out, b_out, p_out, u_out, r_out, i_out, h_out,
    result, dn2_out, dev_h, z_h, g_own, g_got, gd_own, gd_got, br_n, m_n,
    sums, sums2, sums3, vec, br_s, brn_s, m_s, vec_all, block_all, gates_hi, gates_lo, normed, normed2, go, x_own, y, dn2, q_c, p_s, h_s, room, uh, ul,
    own, held, held_n, held_o, gu, gun, down, dt, zs, dev,
    x_send, x_recv, x_loc, i_send, i_recv, i_loc, l_send, l_recv, n_send, n_recv, c_send, c_recv, g_send, g_recv, e_send, e_recv, f_send, f_recv,
    s_send, s_recv, t_send, t_recv, o_send, o_recv, w_send, w_recv, w_own, k_sem, v_sem, d_send, d_recv, d_own,
):
    row, z, core = place()
    block, seq = y.shape
    half = x_in.shape[0]
    chan = p_s.shape[0]
    hid = zs.shape[0]
    b_s, u_s, r_s, i_s, a_c = [room.at[n * chan : (n + 1) * chan, :] for n in range(5)]
    ev, dz = room.at[0 : 2 * hid, :], room.at[2 * hid : 3 * hid, :]
    hh = hid // 2
    hc = chan // 2
    sibling = {"col": 2 * z + (1 - core)}
    met = greet(row, z, core, True, True)
    br_s[0:hc, :] = branch[...].T
    br_s[hc:, :] = recur[...].T
    m_s[...] = mn_s[...].T
    br, mt = gun.at[0 : 2 * chan, 0:width], dt.at[:, 0:chan]
    wide = br_s.shape[0]
    recur_s, branch_s = br_s.at[wide // 2 :, :], br_s.at[0 : wide // 2, :]
    weights = [
        Weights(src, dst, w_send.at[n], w_recv.at[n], w_own.at[n], row, z, core, n in (2, 5), stride, start)
        for n, (src, dst, stride, start) in enumerate(
            (
                (recur_s, br, hc, 0),
                (branch_s, br, hc, chan),
                (m_s, mt, 0, 0),
                (gu_s, gu, 0, 0),
                (d_s, down, 0, 0),
                (brn_s, br_n, 0, 0),
                (mn_s, m_n, 0, 0),
            )
        )
    ]
    mine = pl.ds(pl.multiple_of(core * seq, seq), seq)
    other = pl.ds(pl.multiple_of((1 - core) * seq, seq), seq)
    inner = pl.ds(pl.multiple_of(z * block + core * half, 16), half)
    outer = rows_of(core, half)
    swaps = [
        remote(x_in.at[:, other], x_own.at[outer, :], x_send.at[0], x_recv.at[0], sibling),
        pltpu.make_async_copy(x_in.at[:, mine], x_own.at[outer, :], x_loc.at[0]),
    ]
    for k in range(PARTS):
        theirs, ours = [pl.ds(pl.multiple_of(c * seq + k * PART, 128), PART) for c in (1 - core, core)]
        swaps.append(remote(g_in.at[:, theirs], go.at[k, inner, :], i_send.at[k], i_recv.at[k], sibling))
        swaps.append(pltpu.make_async_copy(g_in.at[:, ours], go.at[k, inner, :], i_loc.at[k]))
    vec[...] = jnp.zeros(vec.shape, F32)
    vec[0:4, :] = taps[...]
    for n, one_row in enumerate((offs, bias_r, bias_a)):
        vec[4 + n : 5 + n, :] = one_row[...]
    rate = -decay[...]
    vec[7:8, :] = 8.0 * (jnp.maximum(rate, 0.0) + jnp.log1p(jnp.exp(-jnp.abs(rate))))
    vec[8:9, 0:half] = mix[...]
    vec[9:10, 0:half] = late[...]
    brn_s[:, 0:hc] = branch[...]
    brn_s[:, hc:] = recur[...]
    met()
    for w in weights[:3]:
        w.start()
    for swap in swaps:
        swap.start()
    trades = []
    for n, (src, dst) in enumerate(
        ((vec, vec_all.at[core]), (retain, block_all.at[core, 0]), (admit, block_all.at[core, 1]))
    ):
        trades.append(remote(src, dst, x_send.at[2 + n], x_recv.at[2 + n], sibling))
        trades.append(pltpu.make_async_copy(src, dst, x_loc.at[2 + n]))
    for trade in trades:
        trade.start()
    for swap in swaps + trades:
        swap.wait()
    flushes = [
        pltpu.make_async_copy(x_own, x_out, v_sem.at[0]),
        pltpu.make_async_copy(go.at[:, rows_of(z, block), :], g_out, v_sem.at[1]),
    ]
    for flush in flushes:
        flush.start()
    gather = Gather(normed, g_send, g_recv, z, core, block)
    gather_go = Gather(go, e_send, e_recv, z, core, block)
    gather_two = Gather(normed2, f_send, f_recv, z, core, block)
    shares = lambda k, s: own.at[k, s]
    shares_o = lambda k, s: normed.at[k, rows_of(s, block), :]
    spread = Spread(shares, held, s_send, s_recv, z, core)
    spread_n = Spread(shares, held_n, t_send, t_recv, z, core)
    spread_o = Spread(shares_o, held_o, o_send, o_recv, z, core)
    res = x_own
    gather_go.send(0, 0)
    gather_go.send(0, 1)
    for c in (0, 1):
        at = slice(c * hc, (c + 1) * hc)
        par[at, :] = vec_all[c].T
        gains[c * half : (c + 1) * half, :] = par[c * hc : c * hc + half, :]

    sums[z] = jnp.zeros(sums.shape[1:], F32)

    def squares(i):
        v = x_own[rows_of(i, 16), :].astype(F32)
        v = v * v
        sums[z] += v[:8] + v[8:]

    blocks(block // 16, squares)
    share_line(sums, l_send, l_recv, z, core)
    scale[...] = jnp.broadcast_to(scale_of(sums, eps, width), scale.shape)

    def norm(i):
        v = x_own[rows_of(i, 16), :].astype(F32) * scale[0:1, :] * gains[rows_of(i, 16), 8:9]
        v = v.astype(BF16)
        for k in range(PARTS):
            normed[k, pl.ds(pl.multiple_of(z * block + i * 16, 16), 16), :] = v[:, k * PART : (k + 1) * PART]

    blocks(block // 16, norm)
    gather.send(0, 0)
    p_s[:, PART:] = jnp.zeros((chan, 128), F32)
    h_s[:, PART:] = jnp.zeros((chan, 128), F32)
    pads = [
        pltpu.make_async_copy(src.at[:, PART:], out.at[:, 0:128], v_sem.at[2 + n])
        for n, (src, out) in enumerate(((p_s, p_out), (h_s, h_out)))
    ]
    for pad in pads:
        pad.start()
    gates[...] = jnp.zeros(gates.shape, BF16)
    gates_hi[...] = jnp.zeros(gates_hi.shape, BF16)
    gates_lo[...] = jnp.zeros(gates_lo.shape, BF16)
    per = retain.shape[0]
    tap = retain.shape[1]
    for c in (0, 1):
        for n in (0, 1):
            for e in range(per):
                w = block_all[c, n, e]
                at, far = slice(e * tap, (e + 1) * tap), slice(n * hc + e * tap, n * hc + (e + 1) * tap)
                gates[c, at, far] = w.astype(BF16)
                w = w.T
                high = w.astype(BF16)
                gates_hi[c, far, at] = high
                gates_lo[c, far, at] = (w - high.astype(F32)).astype(BF16)
    masks[...] = jnp.zeros(masks.shape, F32)
    here = jnp.broadcast_to(segs[:, mine], (8, seq))
    spot = lax.broadcasted_iota(jnp.int32, (8, seq), 1)
    for lag in (1, 2, 3):
        same = jnp.where((pltpu.roll(here, lag, 1) == here) & (spot >= lag), 1.0, 0.0)
        masks[lag : lag + 1, 0:seq] = same[0:1]
        if lag == 1:
            masks[0:1, 0:seq] = 1.0 - same[0:1]
    gather.forward(1, 0)
    gather.send(0, 1)
    weights[0].forward()
    gather.forward(2, 0)
    gather_go.forward(1, 0)
    gather.forward(1, 1)
    gather.send(0, 2)
    weights[1].forward()
    for w in weights[3:5]:
        w.start()
    gather_go.forward(1, 1)
    gather_go.forward(2, 0)
    weights[0].finish()
    for pad in pads:
        pad.wait()

    kept = (b_s, p_s, u_s, r_s, i_s, h_s, q_c)
    outs = (b_out, p_out, u_out, r_out, i_out, h_out, q_out)

    def keep(n, part):
        if n in (1, 5):
            at = pl.ds(pl.multiple_of(128 + part * PART, 128), PART)
            return pltpu.make_async_copy(kept[n].at[:, 128:], outs[n].at[:, at], k_sem.at[n])
        return pltpu.make_async_copy(kept[n], outs[n].at[:, lanes(part)], k_sem.at[n])

    def put_shares(k, whole):
        for s in range(LINE):
            own[k, s] = whole[s * block : (s + 1) * block, :].astype(own.dtype)

    def work(k):
        here = lanes(k)

        @pl.when(k > 0)
        def _():
            for n in range(len(kept)):
                keep(n, k - 1).wait()

        p_s[:, 0:128] = p_s[:, PART:]
        h_s[:, 0:128] = h_s[:, PART:]
        p_s[:, 128:] = dot(br[0:chan, :], normed[k])

        def conv(i):
            ch = rows_of(i, 64)
            window = p_s[ch, :]
            pr = par[ch, :]
            u = pr[:, 4:5] + pr[:, 0:1] * window[:, 128:]
            for lag in (1, 2, 3):
                u = u + pr[:, lag : lag + 1] * (pltpu.roll(window, lag, 1)[:, 128:] * masks[lag : lag + 1, here])
            u_s[ch, :] = u
            high = u.astype(BF16)
            uh[ch, :] = high
            ul[ch, :] = (u - high.astype(F32)).astype(BF16)

        blocks(chan // 64, conv)
        gather.middle(k)
        for g in range(chan // 256):
            at = slice(g * 256, (g + 1) * 256)
            pre = dot(gates_hi[g], uh[at, :]) + dot(gates_hi[g], ul[at, :]) + dot(gates_lo[g], uh[at, :])
            r_s[at, :] = pre[:256]
            i_s[at, :] = pre[256:]

        def gated(i):
            ch = rows_of(i, 64)
            pr = par[ch, :]
            start = masks[0:1, here] > 0.5
            r = jax.nn.sigmoid(r_s[ch, :] + pr[:, 5:6])
            gate = jax.nn.sigmoid(i_s[ch, :] + pr[:, 6:7])
            r_s[ch, :] = r
            i_s[ch, :] = gate
            a = jnp.exp(-(r * pr[:, 7:8]))
            m = jnp.where(start, 1.0, jnp.sqrt(1.0 - a * a + FLOOR))
            a_c[ch, :] = jnp.where(start, 0.0, a)
            h_s[ch, 128:] = m * gate * u_s[ch, :]

        blocks(chan // 64, gated)
        first = lax.broadcasted_iota(jnp.int32, (128, PART), 1) == 0

        def recur(i):
            ch = rows_of(i, 128)
            a, h = a_c[ch, :], h_s[ch, 128:]
            h = h + jnp.where(first, a * h_s[ch, 0:128][:, 127:128], 0.0)
            a = jnp.where(first, 0.0, a)
            shift = 1
            while shift < PART:
                h = h + a * pltpu.roll(h, shift, 1)
                if shift * 2 < PART:
                    a = a * pltpu.roll(a, shift, 1)
                shift *= 2
            h_s[ch, 128:] = h

        blocks(chan // 128, recur)

        @pl.when(k == 0)
        def _():
            weights[2].forward()
            weights[1].finish()

        b_s[...] = dot(br[chan : 2 * chan, :], normed[k])

        def mixed(i):
            ch = rows_of(i, 64)
            b = b_s[ch, :]
            t = jnp.tanh(GELU_A * (b + GELU_B * (b * b * b)))
            q_c[ch, :] = (b * (0.5 + 0.5 * t) * h_s[ch, 128:]).astype(BF16)

        blocks(chan // 64, mixed)
        pl.when(k == 0)(weights[2].finish)
        put_shares(k, dot(mt[...], q_c[...]))
        for n in range(len(kept)):
            keep(n, k).start()

    def finish(k, total):
        def add(i):
            at = pl.multiple_of(i * 64, 64)
            y[pl.ds(at, 64), lanes(k)] = x_own[pl.ds(at, 64), lanes(k)].astype(F32) + total(at, 64)

        blocks(block // 64, add)

    def square(k):
        sums2[k, z] = jnp.zeros(sums2.shape[2:], F32)

        def one(i):
            v = y[rows_of(i, 64), lanes(k)]
            sums2[k, z] += eight(v * v)

        blocks(block // 64, one)
        for d in (1, 2, 3):
            share(k, d).start()

    def share(k, d):
        return remote(
            sums2.at[k, z], sums2.at[k, z], n_send.at[k, d - 1], n_recv.at[k, d - 1], at_line(z ^ d, core)
        )

    def norm_two(k):
        for d in (1, 2, 3):
            piece = sums2.at[k, z ^ d]
            remote(piece, piece, n_send.at[k, d - 1], n_recv.at[k, d - 1], at_line(z ^ d, core)).wait_recv()
        s2 = scale_of(sums2.at[k], eps, width)
        scale_two[:, lanes(k)] = jnp.broadcast_to(s2, (8, PART))

        def one(i):
            at = rows_of(i, 64)
            v = y[at, lanes(k)] * scale_two[0:1, lanes(k)] * gains[at, 9:10]
            normed2[k, pl.ds(pl.multiple_of(z * block + i * 64, 64), 64), :] = v.astype(BF16)

        blocks(block // 64, one)

    def turn_down(i):
        at = pl.ds(pl.multiple_of(i * 128, 128), 128)
        dt[:, at] = down[at, :].T

    def turn_up(i):
        at = pl.ds(pl.multiple_of(i * 128, 128), 128)
        gun[:, at] = gu[at, :].T

    def step(t, carry):
        gather.arrive(2, t)
        work(t)
        spread.serve(t, finish)
        pl.when(t >= 3)(lambda: square(t - 3))
        pl.when(t >= 4)(lambda: norm_two(t - 4))
        pl.when((t >= 4) & (t < 7))(lambda: gather_two.send(0, t - 4))
        pl.when((t >= 6) & (t < 8))(lambda: gather_two.forward(1, t - 6))
        pl.when(t == 5)(weights[3].forward)
        return carry

    lax.fori_loop(0, PARTS, step, 0)
    for w in weights[:3]:
        w.sent()
    for w in weights[5:]:
        w.start()
    for n in range(len(kept)):
        keep(n, PARTS - 1).wait()
    flush_n = pltpu.make_async_copy(normed, n1_out, v_sem.at[4])
    flush_n.start()
    gather_go.forward(2, 1)
    gather_go.send(0, 2)
    gather_go.send(0, 3)
    spread.serve(PARTS, finish)
    square(PARTS - 3)
    norm_two(PARTS - 4)
    gather_two.forward(2, 0)
    weights[3].finish()
    blocks(2 * hid // 128, turn_up)
    weights[4].forward()
    spread.serve(PARTS + 1, finish)
    square(PARTS - 2)
    norm_two(PARTS - 3)
    gather_go.forward(1, 2)
    weights[4].finish()
    blocks(hid // 128, turn_down)
    gather.sent()
    for flush in flushes + [flush_n]:
        flush.wait()
    flush_y = pltpu.make_async_copy(y, y_out, v_sem.at[2])

    def keep_dev(k):
        return pltpu.make_async_copy(dev, dev_h.at[:, lanes(k)], v_sem.at[5])

    def keep_z(k):
        return pltpu.make_async_copy(zs, z_h.at[:, lanes(k)], v_sem.at[6])

    dev_all, z_all = gu.at[:, 0:seq], dt.at[0:hid, 0:seq]
    before, end = pl.ds(0, seq - PART), pl.ds(seq - PART, PART)
    loads = [
        pltpu.make_async_copy(dev_h.at[:, before], gu.at[:, before], v_sem.at[7]),
        pltpu.make_async_copy(z_h.at[:, before], dt.at[0:hid, before], v_sem.at[8]),
        pltpu.make_async_copy(dev, gu.at[:, end], v_sem.at[9]),
        pltpu.make_async_copy(zs, dt.at[0:hid, end], v_sem.at[10]),
    ]

    def feed(k):

        @pl.when(k > 0)
        def _():
            keep_dev(k - 1).wait()
            keep_z(k - 1).wait()

        ev[...] = dot(gu[...], normed2[k])

        @pl.when(k == PARTS - 1)
        def _():
            weights[3].sent()
            loads[0].start()

        gather_two.middle(k)
        gather_go.middle(k, 2)
        gather_go.arrive(2, k)
        dz[...] = dot(down[...], go[k])
        for c in range(2):

            def one(i):
                off = pl.multiple_of(i * 64, 64)
                e = ev[pl.ds(c * 2 * hh + off, 64), :]
                v = ev[pl.ds(c * 2 * hh + hh + off, 64), :]
                d = dz[pl.ds(c * hh + off, 64), :]
                act, slope = gelu_parts(e)
                zs[pl.ds(c * hh + off, 64), :] = (act * v).astype(BF16)
                dev[pl.ds(c * 2 * hh + off, 64), :] = (d * v * slope).astype(BF16)
                dev[pl.ds(c * 2 * hh + hh + off, 64), :] = (d * act).astype(BF16)

            blocks(hh // 64, one)
        put_shares(k, dot(gun[...], dev[...]))
        spread_n.serve(k, finish_n)
        normed[k] = dot(dt[...], zs[...]).astype(BF16)
        spread_o.serve(k, finish_o)
        keep_dev(k).start()
        keep_z(k).start()

        @pl.when(k == 0)
        def _():
            spread.serve(PARTS + 2, finish)
            square(PARTS - 1)
            norm_two(PARTS - 2)

        @pl.when(k == 1)
        def _():
            norm_two(PARTS - 1)
            flush_y.start()

    def finish_o(k, total):
        def add(i):
            at = pl.multiple_of(i * 64, 64)
            res[pl.ds(at, 64), lanes(k)] = (y[pl.ds(at, 64), lanes(k)] + total(at, 64)).astype(BF16)

        blocks(block // 64, add)

    def keep_n(k):
        return pltpu.make_async_copy(dn2, dn2_out.at[:, lanes(k)], v_sem.at[3])

    def finish_n(k, total):
        @pl.when(k > 0)
        def _():
            keep_n(k - 1).wait()

        sums3[k, z] = jnp.zeros(sums3.shape[2:], F32)

        def add(i):
            at = pl.multiple_of(i * 64, 64)
            d = total(at, 64)
            dn2[pl.ds(at, 64), :] = d
            sums3[k, z] += eight(d * y[pl.ds(at, 64), lanes(k)] * gains[pl.ds(at, 64), 9:10])

        blocks(block // 64, add)
        keep_n(k).start()
        for d in (1, 2, 3):
            share_c(k, d).start()

    def share_c(k, d):
        return remote(
            sums3.at[k, z], sums3.at[k, z], c_send.at[k, d - 1], c_recv.at[k, d - 1], at_line(z ^ d, core)
        )

    def feed_step(t, carry):
        gather_two.arrive(2, t)
        feed(t)
        pl.when(t == 4)(weights[5].forward)
        pl.when(t == 6)(weights[6].forward)
        return carry

    lax.fori_loop(0, PARTS, feed_step, 0)
    weights[4].sent()
    for load in loads[1:]:
        load.start()
    keep_dev(PARTS - 1).wait()
    keep_z(PARTS - 1).wait()
    loads[0].wait()
    loads[2].wait()

    def columns(start):
        return pl.ds(pl.multiple_of(start, 128), block)

    def place_up(j):
        side = jnp.where(j >= 3, core, 1 - core)
        return side * hid + (j % 3) * block, columns((j % 3) * block)

    def send_up(j):
        at, to = place_up(j)
        return remote(gun.at[:, columns(at)], g_got.at[:, to], d_send.at[j], d_recv.at[j], sibling)

    def keep_up(j):
        at, to = place_up(j)
        return pltpu.make_async_copy(gun.at[:, columns(at)], g_own.at[:, to], d_own.at[j - 3])

    def send_down():
        return remote(down.at[rows_of(1 - core, hh), :], gd_got, d_send.at[3], d_recv.at[3], sibling)

    def keep_down():
        return pltpu.make_async_copy(down.at[rows_of(core, hh), :], gd_own, d_own.at[3])

    def grad_up(j):
        at = place_up(j)[0]
        right = pl.ds(pl.multiple_of(at, 16), block)
        for low in (0, width // 2):
            piece = slice(low, low + width // 2)
            gun[piece, columns(at)] = dot_nt(tokens_of(normed2, piece), dev_all[right, :]).astype(BF16)

        @pl.when(j < 3)
        def _():
            send_up(j).start()

        @pl.when(j >= 3)
        def _():
            keep_up(j).start()

    def grad_down(side):
        at = rows_of(side, hh)
        for low in range(0, width, 2 * block):
            piece = slice(low, low + 2 * block)
            down[at, piece] = dot_nt(z_all[at, :], tokens_of(go, piece)).astype(BF16)

    def drain(i, carry):
        t = PARTS + i
        blocks(2, lambda j: grad_up(2 * i + j))
        spread_n.serve(t, finish_n)
        spread_o.serve(t, finish_o)

        @pl.when(i == 0)
        def _():
            loads[1].wait()
            loads[3].wait()

        @pl.when(i < 2)
        def _():
            grad_down(jnp.where(i == 0, 1 - core, core))

        pl.when(i == 0)(lambda: send_down().start())
        pl.when(i == 1)(lambda: keep_down().start())
        return carry

    lax.fori_loop(0, LINE - 1, drain, 0)
    last = [
        remote(res.at[rows_of(1 - core, half), :], result.at[:, mine], x_send.at[0], x_recv.at[0], sibling),
        pltpu.make_async_copy(res.at[rows_of(core, half), :], result.at[:, mine], x_loc.at[0]),
        keep_n(PARTS - 1),
        flush_y,
    ]
    for copy in last[:2]:
        copy.start()
    for w in weights[5:]:
        w.finish()
        w.sent()
    for one in (gather_go, gather_two, spread, spread_n, spread_o):
        one.sent()
    for k in range(PARTS):
        for d in (1, 2, 3):
            share(k, d).wait_send()
            share_c(k, d).wait_send()
            piece = sums3.at[k, z ^ d]
            remote(piece, piece, c_send.at[k, d - 1], c_recv.at[k, d - 1], at_line(z ^ d, core)).wait_recv()
        total = jnp.sum(jnp.sum(sums3[k], axis=0), axis=0, keepdims=True)
        at = slice(k * PART, (k + 1) * PART)
        s2 = scale_two[:, at]
        coef[:, at] = s2 * s2 * s2 * (total / width)
    for j in range(3):
        keep_up(j + 3).wait()
        send_up(j).wait()
    keep_down().wait()
    send_down().wait()
    for copy in last:
        copy.wait()


def back_kernel(
    width,
    y, dn2_h, g_h, x_own, scale_two, scale_one, coef_two, gains, masks, par, gates_t, m_h, br_h,
    b_h, p_h, u_h, r_h, i_h, h_h, q_h, n1_h, f_own, f_got, fd_own, fd_got,
    input_grad, tiny_v, tiny_g, f_sum, f_land, fd_sum, fd_land, g_sum, g_land, gm_sum, gm_land,
    sums, coef, m_n, br_n, b_s, p_s, u_s, r_s, i_s, h_s, dyf, dbp, dy, dn1, dq, du, dri, a_c, l_c, carry_s, own, held,
    qv, n1, f_a, f_b, fd_a, fd_b, feed_part, mix_part, small, gate_grad, g_s, g_got, gm_got,
    vec, vec_in, vec_all, gd, gd_in, gd_all,
    c_sem, k_sem, l_send, l_recv, g_send, g_recv, s_send, s_recv, r_send, r_recv,
    f_sem, f_send, f_recv, d_send, d_recv, d_own, q_send, q_recv, n_send, n_recv, v_send, v_recv,
):
    row, z, core = place()
    block, seq = y.shape
    PART, PARTS = LATE, seq // LATE

    def lanes(part):
        return pl.ds(pl.multiple_of(part * PART, PART), PART)

    half = block // 2
    chan = b_s.shape[1]
    hc = chan // 2
    sibling = {"col": 2 * z + (1 - core)}
    met = greet(row, z, core, True, True)
    load_g = pltpu.make_async_copy(g_h, g_s, c_sem.at[0])
    load_g.start()
    dn2 = dn1
    load_d = pltpu.make_async_copy(dn2_h, dn2, c_sem.at[5])
    load_d.start()
    load_m = pltpu.make_async_copy(m_h, m_n, c_sem.at[1])
    load_m.start()
    load_b = pltpu.make_async_copy(br_h, br_n, c_sem.at[2])
    load_b.start()
    load_q = pltpu.make_async_copy(q_h, qv, c_sem.at[3])
    load_n = pltpu.make_async_copy(n1_h, n1, c_sem.at[4])
    kept = (b_s, p_s, u_s, r_s, i_s, h_s)
    srcs = (b_h, p_h, u_h, r_h, i_h, h_h)

    def fetch(n, part):
        if kept[n] is p_s or kept[n] is h_s:
            at = pl.ds(pl.multiple_of(part * PART, 128), PART + 128)
        else:
            at = lanes(part)
        return pltpu.make_async_copy(srcs[n].at[:, at], kept[n].at[part % 2], k_sem.at[n, part % 2])

    def fetch_all(part):
        for n in range(len(kept)):
            fetch(n, part).start()

    fetch_all(PARTS - 1)
    load_q.start()
    load_n.start()
    du[:, 0:128] = jnp.zeros((chan, 128), F32)
    carry_s[...] = jnp.zeros(carry_s.shape, F32)
    small[...] = jnp.zeros(small.shape, F32)
    gate_grad[...] = jnp.zeros(gate_grad.shape, F32)

    load_d.wait()
    load_g.wait()
    gather = Gather(dyf, g_send, g_recv, z, core, block, back=True)

    def outer(part):
        here = slice(part * PART, (part + 1) * PART)

        def one(i):
            at = rows_of(i, 64)
            s2 = scale_two[0:1, here]
            d, v = dn2[at, here], y[at, here]
            w = fold(d * v * s2)
            feed_part[at, :] = w if part == PARTS - 1 else feed_part[at, :] + w
            few = PART // g_s.shape[2]
            g = jnp.concatenate([g_s[part * few + j, at, :] for j in range(few)], axis=1)
            v = g.astype(F32) + (s2 * (gains[at, 9:10] * d) - v * coef_two[0:1, here])
            dy[at, here] = v
            dyf[part, pl.ds(pl.multiple_of(z * block + i * 64, 64), 64), :] = v.astype(BF16)

        blocks(block // 64, one)

    outer(PARTS - 1)
    met()
    gather.send(0, 0)
    for part in range(PARTS - 2, -1, -1):
        outer(part)
    gather.forward(1, 0)
    gather.send(0, 1)
    gather.forward(2, 0)
    gather.forward(1, 1)
    gather.send(0, 2)
    spread = Spread(lambda k, s: own.at[k, s], held, s_send, s_recv, z, core)
    load_m.wait()
    load_b.wait()
    final = lax.broadcasted_iota(jnp.int32, (128, PART), 1) == PART - 1

    f_arrays = ((f_own, f_got, f_a, f_b, f_sum, f_land), (fd_own, fd_got, fd_a, fd_b, fd_sum, fd_land))

    def f_loads(d):
        pulls = []
        for n, (ours, theirs, a, b, _, _) in enumerate(f_arrays):
            if n == 0:
                piece = (rows_of(row ^ d, block), slice(None))
            else:
                piece = (slice(None), pl.ds(pl.multiple_of((row ^ d) * block, 128), block))
            pulls.append(pltpu.make_async_copy(ours.at[piece], a.at[d], f_sem.at[n, 0]))
            pulls.append(pltpu.make_async_copy(theirs.at[piece], b, f_sem.at[n, 1]))
        return pulls

    def f_out(d):
        outs = []
        for n, (_, _, a, _, kept_at, land) in enumerate(f_arrays):
            if d == 0:
                outs.append(pltpu.make_async_copy(a.at[0], kept_at, f_send.at[n, 0]))
            else:
                outs.append(
                    remote(a.at[d], land.at[d - 1], f_send.at[n, d], f_recv.at[n, d], {"row": row ^ d})
                )
        return outs

    def f_part(d):
        for pull in f_loads(d):
            pull.wait()
        for _, _, a, b, _, _ in f_arrays:

            def add(i):
                at = rows_of(i, 64)
                a[d, at, :] = (a[d, at, :].astype(F32) + b[at, :].astype(F32)).astype(BF16)

            blocks(b.shape[0] // 64, add)
        for out in f_out(d):
            out.start()
        if d > 0:
            for pull in f_loads(d - 1):
                pull.start()

    def f_step(t):
        for d in range(LINE):
            pl.when(t == LINE - 1 - d)(functools.partial(f_part, d))

    for pull in f_loads(LINE - 1):
        pull.start()

    lru = hc

    def send_m():
        return remote(m_n.at[rows_of(1 - core, lru), :], gm_got, d_send.at[1], d_recv.at[1], sibling)

    def work(t):
        k = PARTS - 1 - t
        here = lanes(k)
        wide = pl.ds(pl.multiple_of(k * PART, 128), PART + 128)
        slot = k % 2
        for n in range(len(kept)):
            fetch(n, k).wait()

        @pl.when(k > 0)
        def _():
            fetch_all(k - 1)

        dq[...] = dot(m_n[...], dyf[k])

        @pl.when(t == PARTS - 1)
        def _():
            load_q.wait()
            for low in range(0, width, 2 * block):
                piece = slice(low, low + 2 * block)
                m_n[:, piece] = dot_nt(qv[...], tokens_of(dyf, piece)).astype(BF16)
            send_m().start()

        def before(i):
            ch = rows_of(i, 64)
            c = i // (hc // 64)
            low = pl.ds(pl.multiple_of(c * hc + i * 64, 64), 64)
            pr = par[ch, :]
            d = dq[ch, :]
            act, slope = gelu_parts(b_s[slot, ch, :])
            dbp[low, here] = (d * h_s[slot, ch, :][:, 128:] * slope).astype(BF16)
            l_c[ch, :] = d * act
            a_c[ch, :] = jnp.exp(-(r_s[slot, ch, :] * pr[:, 7:8]))

        blocks(chan // 64, before)
        gather.middle(t)

        def recur(i):
            ch = rows_of(i, 128)
            start = masks[0:1, here] > 0.5
            a, lam = jnp.where(start, 0.0, a_c[ch, :]), l_c[ch, :]
            lam = lam + jnp.where(final, carry_s[ch, :][:, 0:1], 0.0)
            w = jnp.where(final, 0.0, pltpu.roll(a, PART - 1, 1))
            shift = 1
            while shift < PART:
                lam = lam + w * pltpu.roll(lam, PART - shift, 1)
                if shift * 2 < PART:
                    w = w * pltpu.roll(w, PART - shift, 1)
                shift *= 2
            carry_s[ch, :] = jnp.broadcast_to((a * lam)[:, 0:1], (128, 128))
            l_c[ch, :] = lam

        blocks(chan // 128, recur)
        f_step(t)

        def after(i):
            ch = rows_of(i, 64)
            du[ch, PART:] = du[ch, 0:128]
            pr = par[ch, :]
            start = masks[0:1, here] > 0.5
            lam, a0 = l_c[ch, :], a_c[ch, :]
            earlier = pltpu.roll(h_s[slot, ch, :], 1, 1)[:, 128:]
            r, gate, u = r_s[slot, ch, :], i_s[slot, ch, :], u_s[slot, ch, :]
            m0 = jnp.sqrt(1.0 - a0 * a0 + FLOOR)
            m = jnp.where(start, 1.0, m0)
            lm = lam * m
            lu = lam * u
            du[ch, 0:PART] = lm * gate
            da = jnp.where(start, 0.0, lam * earlier - (lu * gate) * (a0 / m0)) * a0
            dr = da * (-pr[:, 7:8]) * (r * (1.0 - r))
            di = lu * m * (gate * (1.0 - gate))
            g, o = i // 4, (i % 4) * 64
            dri[pl.ds(pl.multiple_of(g * 512 + o, 64), 64), :] = dr.astype(BF16)
            dri[pl.ds(pl.multiple_of(g * 512 + 256 + o, 64), 64), :] = di.astype(BF16)
            small[5, ch, :] += fold(dr)
            small[6, ch, :] += fold(di)
            small[7, ch, :] += fold(da * r)

        blocks(chan // 64, after)
        for g in range(chan // 256):
            at = slice(g * 256, (g + 1) * 256)
            dd = dri[g * 512 : (g + 1) * 512, :]
            du[at, 0:PART] += dot(gates_t[g], dd)
            gate_grad[g] += dot_nt(u_s[slot, at, :].astype(BF16), dd)

        def conv(i):
            ch = rows_of(i, 64)
            c = i // (hc // 64)
            low = pl.ds(pl.multiple_of((c + 1) * hc + i * 64, 64), 64)
            pr = par[ch, :]
            follow = du[ch, :]
            window = p_s[slot, ch, :]
            d = follow[:, :PART]
            dp = pr[:, 0:1] * d
            small[4, ch, :] += fold(d)
            small[0, ch, :] += fold(d * window[:, 128:])
            for lag in (1, 2, 3):
                kd = follow * masks[lag : lag + 1, wide]
                dp = dp + pr[:, lag : lag + 1] * pltpu.roll(kd, PART + 128 - lag, 1)[:, :PART]
                small[lag, ch, :] += fold(kd[:, :PART] * pltpu.roll(window, lag, 1)[:, 128:])
            dbp[low, here] = dp.astype(BF16)

        blocks(chan // 64, conv)
        whole = dot(br_n[...], dbp[:, here])
        for s in range(LINE):
            own[t, s] = whole[s * block : (s + 1) * block, :].astype(own.dtype)

    def finish(t, total):
        k = PARTS - 1 - t

        sums[k, z] = jnp.zeros(sums.shape[2:], F32)

        @pl.when(t == 0)
        def _():
            mix_part[...] = jnp.zeros(mix_part.shape, F32)

        def add(i):
            at = pl.ds(pl.multiple_of(i * 64, 64), 64)
            d = total(pl.multiple_of(i * 64, 64), 64)
            dn1[at, lanes(k)] = d
            w = d * x_own[at, lanes(k)].astype(F32)
            sums[k, z] += eight(w * gains[at, 8:9])
            w = w * scale_one[0:1, lanes(k)]
            mix_part[at, :] += fold(w)

        blocks(block // 64, add)
        for d in (1, 2, 3):
            share(k, d).start()

    def share(k, d):
        return remote(sums.at[k, z], sums.at[k, z], l_send.at[k, d - 1], l_recv.at[k, d - 1], at_line(z ^ d, core))

    def step(t, carry):
        gather.arrive(2, t)
        work(t)
        spread.serve(t, finish)
        return carry

    lax.fori_loop(0, PARTS, step, 0)
    load_n.wait()


    def cols_of(side):
        return pl.ds(pl.multiple_of(side * 2 * lru, 128), 2 * lru)

    def send_br():
        return remote(br_n.at[:, cols_of(1 - core)], g_got, d_send.at[0], d_recv.at[0], sibling)

    def grad_br(side):
        for low in range(0, width, 2 * block):
            piece = slice(low, low + 2 * block)
            br_n[piece, cols_of(side)] = dot_nt(tokens_of(n1, piece), dbp[rows_of(side, 2 * lru), :]).astype(BF16)

    def out_br(d):
        piece = br_n.at[rows_of(row ^ d, block), cols_of(core)]
        if d == 0:
            return pltpu.make_async_copy(piece, g_sum, d_own.at[0])
        return remote(piece, g_land.at[d - 1], q_send.at[0, d - 1], q_recv.at[0, d - 1], {"row": row ^ d})

    def out_m(d):
        piece = m_n.at[rows_of(core, lru), pl.ds(pl.multiple_of((row ^ d) * block, 128), block)]
        if d == 0:
            return pltpu.make_async_copy(piece, gm_sum, d_own.at[1])
        return remote(piece, gm_land.at[d - 1], q_send.at[1, d - 1], q_recv.at[1, d - 1], {"row": row ^ d})

    def drain(i, carry):
        t = PARTS + i

        @pl.when(i == 0)
        def _():
            grad_br(1 - core)
            send_br().start()
            send_m().wait_recv()

            def add(j):
                at = rows_of(j, 64)
                to = pl.ds(pl.multiple_of(core * lru + j * 64, 64), 64)
                m_n[to, :] = (m_n[to, :].astype(F32) + gm_got[at, :].astype(F32)).astype(BF16)

            blocks(lru // 64, add)
            for d in (3, 2, 1, 0):
                out_m(d).start()
            grad_br(core)

        @pl.when(i == 1)
        def _():
            send_br().wait_recv()

            def add(j):
                at = rows_of(j, 64)
                br_n[at, cols_of(core)] = (br_n[at, cols_of(core)].astype(F32) + g_got[at, :].astype(F32)).astype(BF16)

            blocks(width // 64, add)
            for d in (3, 2, 1, 0):
                out_br(d).start()
        spread.serve(t, finish)
        pl.when(i == 0)(tiny_open)
        pl.when(i == 1)(tiny_more)
        return carry

    mine = pl.ds(pl.multiple_of(core * seq, seq), seq)
    lane = lax.broadcasted_iota(jnp.int32, (64, 128), 1)
    swap_gd = remote(gd.at[1 - core], gd_in, v_send.at[0], v_recv.at[0], sibling)
    rows_gd = [
        remote(gd_all.at[0], gd_all.at[d], n_send.at[0, d - 1], n_recv.at[0, d - 1], {"row": row ^ d}) for d in (1, 2, 3)
    ]

    def tiny_open():
        for side in (0, 1):
            for e in range(4):
                at = slice(e * 64, (e + 1) * 64)
                gd[side, at, 0:64] = gate_grad[side, at, e * 64 : (e + 1) * 64]
                gd[side, at, 64:128] = gate_grad[side, at, 256 + e * 64 : 256 + (e + 1) * 64]
        swap_gd.start()

    def columns(parts, at):
        total = jnp.zeros((64, 128), F32)
        for n, part in enumerate(parts):
            total = total + jnp.where(lane == n, jnp.sum(part(at), axis=1, keepdims=True), 0.0)
        return total

    def tiny_more():
        swap_gd.wait()
        gd_all[0] = gd[core] + gd_in[...]
        for copy in rows_gd:
            copy.start()
        vec[...] = jnp.zeros(vec.shape, F32)
        for j in range(chan // 64):
            at = slice(j * 64, (j + 1) * 64)
            v = columns([lambda at, n=n: small[n, at, :] for n in range(8)], at)
            vec[0, :, at] = v.T[0:8, :]

    lax.fori_loop(0, LINE - 1, drain, 0)
    for j in range(block // 64):
        at = slice(j * 64, (j + 1) * 64)
        v = columns([lambda at: mix_part[at, :], lambda at: feed_part[at, :]], at)
        vec[1, :, at] = v.T[0:8, :]
    swap_vec = remote(vec, vec_in, v_send.at[1], v_recv.at[1], sibling)
    swap_vec.start()
    for k in range(PARTS):
        for d in (1, 2, 3):
            share(k, d).wait_send()
            piece = sums.at[k, z ^ d]
            remote(piece, piece, l_send.at[k, d - 1], l_recv.at[k, d - 1], at_line(z ^ d, core)).wait_recv()
        total = jnp.sum(jnp.sum(sums[k], axis=0), axis=0, keepdims=True)
        at = slice(k * PART, (k + 1) * PART)
        s1 = scale_one[:, at]
        coef[:, at] = s1 * s1 * s1 * (total / width)

    def last(i):
        at = rows_of(i, 16)
        v = dy[at, :] + (
            scale_one[0:1, :] * (gains[at, 8:9] * dn1[at, :]) - x_own[at, :].astype(F32) * coef[0:1, :]
        )
        dy[at, :] = v

    blocks(block // 16, last)
    back = remote(dy.at[rows_of(1 - core, half), :], input_grad.at[:, mine], r_send, r_recv, sibling)
    back.start()
    keep_in = pltpu.make_async_copy(dy.at[rows_of(core, half), :], input_grad.at[:, mine], d_own.at[3])
    keep_in.start()
    swap_vec.wait()
    vec_all[0] = vec[...] + vec_in[...]
    rows_vec = [
        remote(vec_all.at[0], vec_all.at[d], n_send.at[1, d - 1], n_recv.at[1, d - 1], {"row": row ^ d}) for d in (1, 2, 3)
    ]
    for copy in rows_vec:
        copy.start()
    spread.sent()
    gather.sent()
    for copy in rows_gd + rows_vec:
        copy.wait()
    for every, out in ((gd_all, tiny_g), (vec_all, tiny_v)):
        first, second = every[row % 2], every[1 - row % 2]
        third, fourth = every[2 + row % 2], every[3 - row % 2]
        out[...] = (first + second) + (third + fourth)
    for d in range(LINE):
        for out in f_out(d):
            out.wait()
    send_br().wait_send()
    send_m().wait_send()
    for d in (0, 1, 2, 3):
        out_br(d).wait()
        out_m(d).wait()
    for copy in (keep_in, back):
        copy.wait()


def last_kernel(
    f_sum, f_land, fd_sum, fd_land, g_sum, g_land, gm_sum, gm_land, result_in, grad_in, tiny_v, tiny_g, lambdas,
    s_b, s_r, s_m, s_g, s_u, s_d, result, input_grad, taps, offs, bias_r, bias_a, decay, mix, feed, retain, admit,
):
    lru, ff, half = s_b.shape[1], s_g.shape[0], mix.shape[1]

    def four(first, others):
        return first[...].astype(F32) + others[0].astype(F32) + (others[1].astype(F32) + others[2].astype(F32))

    v = four(f_sum, f_land)
    s_g[...] = v.T[:ff, :]
    s_u[...] = v.T[ff:, :]
    v = four(g_sum, g_land)
    s_b[...] = v[:, :lru]
    s_r[...] = v[:, lru:]
    s_d[...] = four(fd_sum, fd_land)
    result[...] = result_in[...]
    input_grad[...] = grad_in[...]

    @pl.when(pl.program_id(0) == 0)
    def _():
        core = place()[2]
        s_m[...] = four(gm_sum, gm_land)
        small = tiny_v[0, :, pl.ds(pl.multiple_of(core * lru, 128), lru)]
        taps[...] = small[0:4]
        offs[...] = small[4:5]
        bias_r[...] = small[5:6]
        bias_a[...] = small[6:7]
        decay[...] = small[7:8] * (8.0 * jax.nn.sigmoid(-lambdas[...]))
        gains = jnp.where(core == 0, tiny_v[1, :, 0:half], tiny_v[1, :, half : 2 * half])
        mix[...] = gains[0:1]
        feed[...] = gains[1:2]
        for e in range(retain.shape[0]):
            at = slice(e * 64, (e + 1) * 64)
            retain[e] = tiny_g[at, 0:64]
            admit[e] = tiny_g[at, 64:128]


ANY = pl.BlockSpec(memory_space=pl.ANY)
VM = pl.BlockSpec(memory_space=pltpu.VMEM)
DMA = pltpu.SemaphoreType.DMA
ROOM = 62 * 1024 * 1024


def shape(dims, kind):
    return jax.ShapeDtypeStruct(dims, kind)


def call(kernel, ins, outs, scratch, ident, name, flops):
    return pl.pallas_call(
        kernel,
        out_shape=[o[0] for o in outs],
        in_specs=ins,
        out_specs=[o[1] for o in outs],
        scratch_shapes=scratch,
        name=name,
        compiler_params=pltpu.CompilerParams(
            collective_id=ident, has_side_effects=True, vmem_limit_bytes=ROOM
        ),
        cost_estimate=pl.CostEstimate(flops=flops, bytes_accessed=40000000, transcendentals=0),
    )


def fast_body(
    inputs, segments, mix_gain, branch_weight, recur_weight, kernel, offsets, retain_weight, retain_bias,
    admit_weight, admit_bias, lambdas, merge_weight, feed_gain, gate_weight, up_weight, down_weight, cotangent,
):
    half, tokens = inputs.shape
    block, seq, width = 2 * half, tokens // 2, D
    lru, heads = branch_weight.shape[1], retain_weight.shape[0]
    chan = 2 * lru
    ff = gate_weight.shape[1]
    hid = 2 * ff
    rows = branch_weight.shape[0]
    cols = merge_weight.shape[1]
    gu_s = jnp.concatenate([gate_weight, up_weight], axis=1).T

    f_tok = lambda n, kind=F32: shape((n, seq), kind)
    padded = (shape((chan, 128 + seq), F32), ANY)
    state = [(f_tok(chan), ANY), padded, *[(f_tok(chan), ANY)] * 3, padded]
    line = [DMA((3,)), DMA((3,))]
    steps = [DMA((2, 3, PARTS)), DMA((2, 3, PARTS))]
    sums = [DMA((2, PARTS, LINE)), DMA((2, PARTS, LINE))]
    held = pltpu.VMEM((PARTS, LINE + 1, block, PART), BF16)
    own_low = pltpu.VMEM((PARTS, LINE, block, PART), BF16)
    tok = lambda n, kind=F32, lead=0: pltpu.VMEM((n, lead + seq), kind)
    one = lambda n, kind=F32, lead=0: pltpu.VMEM((n, lead + PART), kind)
    grad_gu, grad_d = (shape((width, 2 * ff), BF16), ANY), (shape((ff, width), BF16), ANY)
    low = lambda n, m: (shape((n, m), BF16), ANY)
    parted = lambda n: (shape((PARTS, n, PART), BF16), ANY)
    by_part = lambda n: pltpu.VMEM((PARTS, n, PART), BF16)

    (masks, par, gains, gates, coef, scale_one, scale_two, y, n1, q, x_own, g, b, p, u, r, i, h, result, dn2, _, _, f_own, f_got, fd_own, fd_got,
     br_n, m_n) = call(
        functools.partial(forward_kernel, width, EPS),
        [ANY] * 2 + [VM] * 13 + [ANY] * 2,
        [(shape((8, seq + 128), F32), VM), (shape((chan, 16), F32), VM), (shape((block, 16), F32), VM), (shape((2, lru, 2 * lru), BF16), VM),
         (f_tok(8), VM), (f_tok(8), VM), (f_tok(8), VM), (f_tok(block), ANY), parted(width), low(chan, seq), low(block, seq), parted(block)]
        + state + [low(half, tokens), (f_tok(block), ANY), low(2 * hid, seq), low(hid, seq), grad_gu, grad_gu, grad_d, grad_d,
                   low(width, 2 * chan), low(chan, width)],
        [pltpu.VMEM((LINE, 8, seq), F32), pltpu.VMEM((PARTS, LINE, 8, PART), F32), pltpu.VMEM((PARTS, LINE, 8, PART), F32),
         pltpu.VMEM((16, lru), F32), pltpu.VMEM((2 * lru, rows), BF16), pltpu.VMEM((rows, 2 * lru), BF16), pltpu.VMEM((cols, lru), BF16),
         pltpu.VMEM((2, 16, lru), F32), pltpu.VMEM((2, 2) + retain_weight.shape, F32), pltpu.VMEM((2, 2 * lru, lru), BF16),
         pltpu.VMEM((2, 2 * lru, lru), BF16), by_part(width), by_part(width),
         by_part(width), tok(block, BF16), tok(block), one(block), one(chan, BF16),
         one(chan, F32, 128), one(chan, F32, 128), one(max(5 * chan, 3 * hid)), one(chan, BF16), one(chan, BF16),
         own_low, held, held, held, pltpu.VMEM((2 * hid, width), BF16), pltpu.VMEM((width, 2 * hid), BF16),
         pltpu.VMEM((hid, width), BF16), pltpu.VMEM((width, hid), BF16), one(hid, BF16), one(2 * hid, BF16),
         DMA((5,)), DMA((5,)), DMA((5,)), DMA((PARTS,)), DMA((PARTS,)), DMA((PARTS,))] + line + [DMA((PARTS, 3)), DMA((PARTS, 3))] * 2 + steps * 3 + sums * 3
        + [DMA((7, 7)), DMA((7, 7)), DMA((7,)), DMA((7,)), DMA((11,)), DMA((4,)), DMA((4,)), DMA((4,))],
        0, "forward", 50 * 10**9,
    )(inputs, cotangent, segments[None, :], kernel, offsets[None, :], retain_bias[None, :], admit_bias[None, :],
      lambdas[None, :], mix_gain[None, :], feed_gain[None, :], retain_weight, admit_weight, branch_weight, recur_weight,
      merge_weight, gu_s, down_weight)

    late = seq // LATE
    pair = lambda lead=0: pltpu.VMEM((2, chan, lead + LATE), F32)
    one = lambda n, kind=F32, lead=0: pltpu.VMEM((n, lead + LATE), kind)
    steps = [DMA((2, 3, late)), DMA((2, 3, late))]
    sums = [DMA((2, late, LINE)), DMA((2, late, LINE))]
    held = pltpu.VMEM((late, LINE + 1, block, LATE), BF16)
    own_low = pltpu.VMEM((late, LINE, block, LATE), BF16)
    land = lambda n, m: ((shape((n, m), BF16), ANY), (shape((3, n, m), BF16), ANY))
    input_grad, tiny_v, tiny_g, *sums_of = call(
        functools.partial(back_kernel, width),
        [VM] + [ANY] * 2 + [VM] * 8 + [ANY] * 14,
        [(shape((half, tokens), F32), ANY), (shape((2, 8, chan), F32), VM),
         (shape((lru, 128), F32), VM), *land(cols, 2 * ff), *land(ff, cols), *land(cols, 2 * lru), *land(lru, cols)],
        [pltpu.VMEM((late, LINE, 8, LATE), F32), pltpu.VMEM((8, seq), F32),
         pltpu.VMEM((chan, width), BF16), pltpu.VMEM((width, 2 * chan), BF16),
         pair(), pair(128), pair(), pair(), pair(), pair(128), pltpu.VMEM((late, width, LATE), BF16), tok(2 * chan, BF16),
         tok(block), tok(block), one(chan), one(chan, F32, 128), one(2 * chan, BF16),
         one(chan), one(chan), pltpu.VMEM((chan, 128), F32), own_low, held,
         tok(chan, BF16), by_part(width), pltpu.VMEM((4, cols, 2 * ff), BF16), pltpu.VMEM((cols, 2 * ff), BF16),
         pltpu.VMEM((4, ff, cols), BF16), pltpu.VMEM((ff, cols), BF16),
         pltpu.VMEM((block, 128), F32), pltpu.VMEM((block, 128), F32), pltpu.VMEM((8, chan, 128), F32),
         pltpu.VMEM((2, lru, 2 * lru), F32), by_part(block), pltpu.VMEM((width, 2 * lru), BF16),
         pltpu.VMEM((lru, width), BF16), pltpu.VMEM((2, 8, chan), F32), pltpu.VMEM((2, 8, chan), F32),
         pltpu.VMEM((4, 2, 8, chan), F32), pltpu.VMEM((2, lru, 128), F32), pltpu.VMEM((lru, 128), F32),
         pltpu.VMEM((4, lru, 128), F32), DMA((7,)), DMA((6, 2))] + [DMA((late, 3)), DMA((late, 3))] + steps + sums
        + [DMA, DMA, DMA((2, 2)), DMA((2, LINE)), DMA((2, LINE)), DMA((2,)), DMA((2,)), DMA((4,))]
        + [DMA((2, 3)), DMA((2, 3)), DMA((2, 3)), DMA((2, 3)), DMA((2,)), DMA((2,))],
        2, "mix_backward", 10 * 10**9,
    )(y, dn2, g, x_own, scale_two, scale_one, coef, gains, masks, par, gates, m_n, br_n, b, p, u, r, i, h,
      q, n1, f_own, f_got, fd_own, fd_got)

    line_of = shape((1, lru), F32)
    cuts = 3
    rows_in = lambda *dims: pl.BlockSpec((dims[0] // cuts,) + dims[1:], lambda n: (n,) + (0,) * (len(dims) - 1))
    three = lambda *dims: pl.BlockSpec((3, dims[0] // cuts, dims[1]), lambda n: (0, n, 0))
    still = lambda *dims: pl.BlockSpec(dims, lambda n: (0,) * len(dims))
    sizes = ((cols, 2 * ff), (ff, cols), (cols, 2 * lru), (lru, cols))
    big = ((cols, lru), (cols, lru), (lru, cols), (ff, cols), (ff, cols), (ff, cols))
    across = pl.BlockSpec((ff, cols // cuts), lambda n: (0, n))
    flat = ((4, lru),) + ((1, lru),) * 4 + ((1, half),) * 2 + ((heads, 64, 64),) * 2
    s_b, s_r, s_m, s_g, s_u, s_d, result, input_grad, taps, offs, bias_r, bias_a, decay, mix, feed, retain, admit = pl.pallas_call(
        last_kernel,
        grid=(cuts,),
        out_shape=[shape(d, F32) for d in big] + [shape((half, tokens), BF16), shape((half, tokens), F32)]
        + [shape(d, F32) for d in flat],
        in_specs=[spec(*d) for d in sizes[:3] for spec in (rows_in, three)] + [still(lru, cols), still(3, lru, cols)]
        + [rows_in(half, tokens)] * 2
        + [still(2, 8, chan), still(lru, 128), still(1, lru)],
        out_specs=[rows_in(cols, lru)] * 2 + [still(lru, cols)] + [across] * 2 + [rows_in(ff, cols)] + [rows_in(half, tokens)] * 2 + [still(*d) for d in flat],
        name="last_sums",
        compiler_params=pltpu.CompilerParams(vmem_limit_bytes=ROOM),
    )(*sums_of, result, input_grad, tiny_v, tiny_g, lambdas[None, :])
    return (
        result,
        input_grad,
        mix[0],
        s_b,
        s_r,
        taps,
        offs[0],
        retain,
        bias_r[0],
        admit,
        bias_a[0],
        decay[0],
        s_m,
        feed[0],
        s_g.T,
        s_u.T,
        s_d,
    )


def suits(mesh, args):
    return (
        dict(mesh.shape) == {"row": 4, "col": 8}
        and args[0].shape == (D, 8 * SEQ)
        and args[3].shape == (D, 2048)
        and args[14].shape == (D, 4608)
        and args[7].shape == (32, 64, 64)
    )


def solution(mesh):
    in_specs = (
        P("col", "row"),
        P("row"),
        P("col"),
        P("row", "col"),
        P("row", "col"),
        P(None, "col"),
        P("col"),
        P("col", None, None),
        P("col"),
        P("col", None, None),
        P("col"),
        P("col"),
        P("col", "row"),
        P("col"),
        P("row", "col"),
        P("row", "col"),
        P("col", "row"),
        P("col", "row"),
    )
    out_specs = (
        P("col", "row"),
        P("col", "row"),
        P("col"),
        P("row", "col"),
        P("row", "col"),
        P(None, "col"),
        P("col"),
        P("col", None, None),
        P("col"),
        P("col", None, None),
        P("col"),
        P("col"),
        P("col", "row"),
        P("col"),
        P("row", "col"),
        P("row", "col"),
        P("col", "row"),
    )
    def run(*args):
        chosen = fast_body if suits(mesh, args) else body
        return jax.shard_map(
            chosen, mesh=mesh, in_specs=in_specs, out_specs=out_specs, check_vma=False
        )(*args)

    return run
```

```python
import functools

import jax
import jax.numpy as jnp
from jax import lax
from jax.experimental import pallas as pl
from jax.experimental.pallas import tpu as pltpu
from jax.sharding import PartitionSpec as P

D = 1536
SEQ = 1024
MICRO = 2


HIGH = lax.Precision.HIGHEST
EPS = 1e-06
POWER = 8.0
FLOOR = 0.01


def combine(earlier, later):
    first_a, first_b = earlier
    second_a, second_b = later
    return (first_a * second_a, second_a * first_b + second_b)


def mixer(
    branch_pre,
    lru_pre,
    segs,
    kernel,
    offsets,
    retain_weight,
    retain_bias,
    admit_weight,
    admit_bias,
    lambdas,
):
    length = lru_pre.shape[0]
    channels = lru_pre.shape[1]
    conv = offsets + kernel[0] * lru_pre
    for lag in range(1, kernel.shape[0]):
        shifted = jnp.concatenate(
            [jnp.zeros((lag, channels), lru_pre.dtype), lru_pre[:-lag]], axis=0
        )
        prior = jnp.concatenate([jnp.full((lag,), -1, jnp.int32), segs[:-lag]])
        keep = (prior == segs).astype(lru_pre.dtype)
        conv = conv + kernel[lag] * shifted * keep[:, None]
    heads = retain_weight.shape[0]
    blocks = conv.reshape(length, heads, channels // heads)
    retain = jax.nn.sigmoid(
        jnp.einsum("thi,hij->thj", blocks, retain_weight, precision=HIGH).reshape(length, channels)
        + retain_bias
    )
    admit = jax.nn.sigmoid(
        jnp.einsum("thi,hij->thj", blocks, admit_weight, precision=HIGH).reshape(length, channels)
        + admit_bias
    )
    decay = jnp.exp(-POWER * retain * jax.nn.softplus(-lambdas))
    factor = jnp.sqrt(1.0 - decay * decay + FLOOR)
    starts = jnp.concatenate([jnp.ones((1,), bool), segs[1:] != segs[:-1]])
    decay = jnp.where(starts[:, None], 0.0, decay)
    factor = jnp.where(starts[:, None], 1.0, factor)
    _, state = lax.associative_scan(combine, (decay, factor * admit * conv), axis=0)
    return jax.nn.gelu(branch_pre) * state


def geglu(gate, upper):
    return jax.nn.gelu(gate) * upper


def contract_rows(left, right):
    return lax.dot_general(
        left, right, (((0,), (0,)), ((), ())), preferred_element_type=jnp.float32
    )


def contract_cols(left, right):
    return lax.dot_general(
        left, right, (((1,), (1,)), ((), ())), preferred_element_type=jnp.float32
    )


def contract_cross(left, right):
    return lax.dot_general(
        left, right, (((0,), (1,)), ((), ())), preferred_element_type=jnp.float32
    )


def norm_forward(resid, gain):
    total = lax.psum(jnp.sum(resid * resid, axis=0), "col")
    scale = lax.rsqrt(total / D + EPS)[None, :]
    return (scale, (resid * scale * gain[:, None]).astype(jnp.bfloat16))


def norm_backward(resid, scale, gain, grad_normed):
    weighted = grad_normed * gain[:, None]
    total = lax.psum(jnp.sum(weighted * resid, axis=0), "col")
    grad_resid = scale * weighted - resid * (scale * scale * scale) * (total / D)[None, :]
    grad_gain = jnp.sum(grad_normed * resid * scale, axis=1)
    return (grad_resid, grad_gain)


def gather_features(normed):
    return lax.all_gather(normed, "col", axis=0, tiled=True)


def gather_cotangent(grad):
    return lax.all_gather(grad, "col", axis=0, tiled=True)


def spread_sum(term):
    return lax.psum_scatter(
        term.astype(jnp.bfloat16), "col", scatter_dimension=0, tiled=True
    ).astype(jnp.float32)


def back_sum(term):
    return spread_sum(term)


def merge_term(whole_merge, mixed_low):
    return spread_sum(contract_cross(whole_merge, mixed_low))


def weight_grads(normed, grad_joined):
    return jnp.dot(
        normed,
        grad_joined,
        preferred_element_type=jnp.float32,
    )


def row_sum(total, axis):
    return lax.psum_scatter(
        total.astype(jnp.bfloat16), "row", scatter_dimension=axis, tiled=True
    ).astype(jnp.float32)


def body(
    inputs,
    segments,
    mix_gain,
    branch_weight,
    recur_weight,
    kernel,
    offsets,
    retain_weight,
    retain_bias,
    admit_weight,
    admit_bias,
    lambdas,
    merge_weight,
    feed_gain,
    gate_weight,
    up_weight,
    down_weight,
    cotangent,
):
    lru_cols = branch_weight.shape[1]
    feed_cols = gate_weight.shape[1]
    mixer_params = (kernel, offsets, retain_weight, retain_bias, admit_weight, admit_bias, lambdas)
    acc_branch = jnp.zeros((D, lru_cols), jnp.float32)
    acc_recur = jnp.zeros((D, lru_cols), jnp.float32)
    acc_gate = jnp.zeros((D, feed_cols), jnp.float32)
    acc_up = jnp.zeros((D, feed_cols), jnp.float32)
    acc_merge = jnp.zeros((lru_cols, D), jnp.float32)
    acc_down = jnp.zeros((feed_cols, D), jnp.float32)
    acc_small = tuple((jnp.zeros_like(p) for p in mixer_params))
    acc_mix = jnp.zeros_like(mix_gain)
    acc_feed = jnp.zeros_like(feed_gain)
    outputs = []
    in_grads = []
    for batch in range(MICRO):
        lower = batch * SEQ
        resid_in = inputs[:, lower : lower + SEQ].astype(jnp.float32)
        grad_out = cotangent[:, lower : lower + SEQ].astype(jnp.float32)
        segs = segments[lower : lower + SEQ]
        whole_branch, whole_recur, whole_gate, whole_up = (
            lax.all_gather(branch_weight, "row", axis=0, tiled=True),
            lax.all_gather(recur_weight, "row", axis=0, tiled=True),
            lax.all_gather(gate_weight, "row", axis=0, tiled=True),
            lax.all_gather(up_weight, "row", axis=0, tiled=True),
        )
        whole_merge, whole_down = (
            lax.all_gather(merge_weight, "row", axis=1, tiled=True),
            lax.all_gather(down_weight, "row", axis=1, tiled=True),
        )
        scale_one, normed_one = norm_forward(resid_in, mix_gain)
        full_one = gather_features(normed_one)
        branch_pre = contract_rows(full_one, whole_branch)
        lru_pre = contract_rows(full_one, whole_recur)

        def local_mixer(bpre, lpre, kern, offs, rweight, rbias, aweight, abias, lams):
            return mixer(bpre, lpre, segs, kern, offs, rweight, rbias, aweight, abias, lams)

        mixed, mixer_pull = jax.vjp(local_mixer, branch_pre, lru_pre, *mixer_params)
        mixed_low = mixed.astype(jnp.bfloat16)
        resid_mid = resid_in + merge_term(whole_merge, mixed_low)
        scale_two, normed_two = norm_forward(resid_mid, feed_gain)
        full_two = gather_features(normed_two)
        gate = contract_rows(full_two, whole_gate)
        upper = contract_rows(full_two, whole_up)
        hidden, geglu_pull = jax.vjp(geglu, gate, upper)
        hidden_low = hidden.astype(jnp.bfloat16)
        result = resid_mid + spread_sum(contract_cross(whole_down, hidden_low))
        outputs.append(result.astype(jnp.bfloat16))
        grad_full = gather_cotangent(grad_out.astype(jnp.bfloat16))
        acc_down = acc_down + contract_cross(hidden_low, grad_full)
        grad_gate, grad_upper = geglu_pull(contract_cross(grad_full, whole_down))
        grad_gate = grad_gate.astype(jnp.bfloat16)
        grad_upper = grad_upper.astype(jnp.bfloat16)
        feed_joined = weight_grads(full_two, jnp.concatenate([grad_gate, grad_upper], axis=1))
        acc_gate = acc_gate + feed_joined[:, :feed_cols]
        acc_up = acc_up + feed_joined[:, feed_cols:]
        grad_normed_two = back_sum(
            contract_cols(whole_gate, grad_gate) + contract_cols(whole_up, grad_upper)
        )
        grad_mid_norm, feed_part = norm_backward(resid_mid, scale_two, feed_gain, grad_normed_two)
        acc_feed = acc_feed + feed_part
        grad_mid = grad_out + grad_mid_norm
        grad_mid_full = gather_cotangent(grad_mid.astype(jnp.bfloat16))
        acc_merge = acc_merge + contract_cross(mixed_low, grad_mid_full)
        pulled = mixer_pull(contract_cross(grad_mid_full, whole_merge))
        grad_branch = pulled[0].astype(jnp.bfloat16)
        grad_lru = pulled[1].astype(jnp.bfloat16)
        acc_small = tuple((total + part for total, part in zip(acc_small, pulled[2:])))
        branch_joined = weight_grads(full_one, jnp.concatenate([grad_branch, grad_lru], axis=1))
        acc_branch = acc_branch + branch_joined[:, :lru_cols]
        acc_recur = acc_recur + branch_joined[:, lru_cols:]
        grad_normed_one = back_sum(
            contract_cols(whole_branch, grad_branch) + contract_cols(whole_recur, grad_lru)
        )
        grad_in_norm, mix_part = norm_backward(resid_in, scale_one, mix_gain, grad_normed_one)
        acc_mix = acc_mix + mix_part
        in_grads.append(grad_mid + grad_in_norm)
    sum_branch, sum_recur, sum_gate, sum_up = (
        row_sum(acc_branch, 0),
        row_sum(acc_recur, 0),
        row_sum(acc_gate, 0),
        row_sum(acc_up, 0),
    )
    sum_merge, sum_down = (
        row_sum(acc_merge, 1),
        row_sum(acc_down, 1),
    )
    summed = lax.psum(
        (
            acc_mix,
            acc_feed,
            acc_small[0],
            acc_small[1],
            acc_small[2],
            acc_small[3],
            acc_small[4],
            acc_small[5],
            acc_small[6],
        ),
        "row",
    )
    result_all = jnp.concatenate(outputs, axis=1)
    input_grad = jnp.concatenate(in_grads, axis=1)
    return (
        result_all,
        input_grad,
        summed[0],
        sum_branch,
        sum_recur,
        summed[2],
        summed[3],
        summed[4],
        summed[5],
        summed[6],
        summed[7],
        summed[8],
        sum_merge,
        summed[1],
        sum_gate,
        sum_up,
        sum_down,
    )


MESH = pl.DeviceIdType.MESH
F32 = jnp.float32
BF16 = jnp.bfloat16
LINE = 4
PART = 128
PARTS = 8
LATE = 256
GELU_A = 0.7978845608028654
GELU_B = 0.044715


def place():
    row, col = lax.axis_index("row"), lax.axis_index("col")
    return row, col // 2, col % 2


def at_line(z, core):
    return {"col": 2 * z + core}


def lanes(part):
    return pl.ds(pl.multiple_of(part * PART, PART), PART)


def rows_of(index, size):
    return pl.ds(pl.multiple_of(index * size, 16), size)


def dot(a, b):
    return lax.dot_general(a, b, (((1,), (0,)), ((), ())), preferred_element_type=F32)


def dot_nt(a, b):
    return lax.dot_general(a, b, (((1,), (1,)), ((), ())), preferred_element_type=F32)


def greet(row, z, core, rows, line):
    barrier = pltpu.get_barrier_semaphore()
    peers = [{"col": 2 * z + (1 - core)}]
    if rows:
        peers += [{"row": row ^ d} for d in (1, 2, 3)]
    if line:
        peers += [at_line(z ^ d, core) for d in (1, 2, 3)]
    for peer in peers:
        pl.semaphore_signal(barrier, inc=1, device_id=peer, device_id_type=MESH)
    return functools.partial(pl.semaphore_wait, barrier, len(peers))


def remote(src, dst, send, recv, peer):
    return pltpu.make_async_remote_copy(
        src_ref=src, dst_ref=dst, send_sem=send, recv_sem=recv, device_id=peer, device_id_type=MESH
    )


class Gather:
    def __init__(self, ref, send, recv, z, core, block, back=False):
        self.parts = ref.shape[0]
        self.ref, self.sems, self.z, self.core = ref, (send, recv), z, core
        self.block, self.back = block, back

    def copy(self, way, hop, step, owner, incoming=False):
        part = self.parts - 1 - step if self.back else step
        piece = self.ref.at[part, rows_of(owner, self.block), :]
        peer = at_line(self.z + (1 if (way == 0) != incoming else -1), self.core)
        return remote(piece, piece, self.sems[0].at[way, hop, step], self.sems[1].at[way, hop, step], peer)

    def each(self, hop, act, incoming):
        z = self.z
        if incoming:
            cases = ((0, z - 1 - hop >= 0, z - 1 - hop), (1, z + 1 + hop < LINE, z + 1 + hop))
        else:
            cases = (
                (0, (z >= hop) & (z < LINE - 1), z - hop),
                (1, (z + hop < LINE) & (z >= 1), z + hop),
            )
        for way, here, owner in cases:
            pl.when(here)(functools.partial(act, way, owner))

    def send(self, hop, step):
        self.each(hop, lambda way, owner: self.copy(way, hop, step, owner).start(), False)

    def arrive(self, hop, step):
        self.each(hop, lambda way, owner: self.copy(way, hop, step, owner, True).wait_recv(), True)

    def forward(self, hop, step):
        self.arrive(hop - 1, step)
        self.send(hop, step)

    def sent(self):
        def one(step, carry):
            for hop in range(LINE - 1):
                self.each(hop, lambda way, owner: self.copy(way, hop, step, owner).wait_send(), False)
            return carry

        lax.fori_loop(0, self.parts, one, 0)

    def middle(self, step, ahead=1):
        for hop in (2, 1, 0):
            later = step + ahead + 2 - hop
            act = self.forward if hop else self.send
            pl.when(later < self.parts)(functools.partial(act, hop, later))


class Spread:
    def __init__(self, own, held, send, recv, z, core):
        self.parts = held.shape[0]
        self.own, self.held, self.sems, self.z, self.core = own, held, (send, recv), z, core

    def copy(self, way, step, hop):
        slot = hop if way == 0 else LINE - hop
        there = slot - 1 if way == 0 else slot + 1
        peer = at_line(self.z + (1 if way == 0 else -1), self.core)
        return remote(
            self.held.at[step, slot],
            self.held.at[step, there],
            self.sems[0].at[way, step, hop],
            self.sems[1].at[way, step, hop - 1],
            peer,
        )

    def landed(self, way, step, hop):
        slot = hop if way == 0 else LINE - hop
        piece = self.held.at[step, slot]
        peer = at_line(self.z + (-1 if way == 0 else 1), self.core)
        remote(piece, piece, self.sems[0].at[way, step, hop], self.sems[1].at[way, step, hop], peer).wait_recv()

    def push(self, way, step, first):
        z = self.z

        def one(i, carry):
            hop = LINE - 1 - i
            owner = z + hop if way == 0 else z - hop
            slot = hop if way == 0 else LINE - hop

            @pl.when((owner >= 0) & (owner < LINE))
            def _():
                @pl.when(first)
                def _():
                    self.held[step, slot] = self.own(step, owner)[...].astype(BF16)

                @pl.when(jnp.logical_not(first))
                def _():
                    self.landed(way, step, hop)
                    total = self.own(step, owner)[...].astype(F32) + self.held[step, slot].astype(F32)
                    self.held[step, slot] = total.astype(BF16)

                self.copy(way, step, hop).start()

            return carry

        lax.fori_loop(0, LINE - 1, one, 0)

    def serve(self, t, finish):
        z = self.z
        step = t - (LINE - 1)

        @pl.when((step >= 0) & (step < self.parts))
        def _():
            @pl.when(z == 0)
            def _():
                self.landed(1, step, 0)
                finish(step, lambda a, n: self.mine(step, a, n) + self.got(step, LINE, a, n))

            @pl.when(z == LINE - 1)
            def _():
                self.landed(0, step, 0)
                finish(step, lambda a, n: self.mine(step, a, n) + self.got(step, 0, a, n))

            @pl.when((z > 0) & (z < LINE - 1))
            def _():
                self.landed(0, step, 0)
                self.landed(1, step, 0)
                finish(
                    step,
                    lambda a, n: self.mine(step, a, n) + (self.got(step, 0, a, n) + self.got(step, LINE, a, n)),
                )

        for way, late, turn in ((1, LINE - 1 - z, z < 2), (0, z, z >= 0), (1, LINE - 1 - z, z >= 2)):
            step = t - late
            pl.when((step >= 0) & (step < self.parts) & turn)(functools.partial(self.push, way, step, late == 0))

    def mine(self, step, start, size):
        return self.own(step, self.z)[pl.ds(start, size), :].astype(F32)

    def got(self, step, slot, start, size):
        return self.held[step, slot, pl.ds(start, size)].astype(F32)

    def sent(self):
        z = self.z

        def one(step, carry):
            for way in (0, 1):
                for hop in range(1, LINE):
                    owner = z + hop if way == 0 else z - hop

                    @pl.when((owner >= 0) & (owner < LINE))
                    def _():
                        self.copy(way, step, hop).wait_send()

            return carry

        lax.fori_loop(0, self.parts, one, 0)


def share_line(ref, send, recv, z, core):
    copies = [
        remote(ref.at[z], ref.at[z], send.at[d - 1], recv.at[d - 1], at_line(z ^ d, core)) for d in (1, 2, 3)
    ]
    for copy in copies:
        copy.start()
    for d in (1, 2, 3):
        piece = ref.at[z ^ d]
        remote(piece, piece, send.at[d - 1], recv.at[d - 1], at_line(z ^ d, core)).wait_recv()
    for copy in copies:
        copy.wait_send()


class Weights:
    def __init__(self, src, dst, send, recv, own, row, z, core, turned, stride=0, start=0):
        self.src, self.dst, self.send, self.recv, self.own = src, dst, send, recv, own
        self.row, self.core, self.turned = row, core, turned
        self.stride, self.first = stride or src.shape[0], start
        self.sibling = {"col": 2 * z + (1 - core)}

    def spot(self, row, core):
        down, right = (row, core) if self.turned else (core, row)
        rows, cols = self.src.shape
        at = pl.ds(pl.multiple_of(down * self.stride + self.first, 16), rows)
        return self.dst.at[at, pl.ds(pl.multiple_of(right * cols, 128), cols)]

    def to_row(self, d):
        return remote(
            self.src, self.spot(self.row, self.core), self.send.at[d], self.recv.at[d], {"row": self.row ^ d}
        )

    def to_sibling(self, d):
        if d == 0:
            return remote(
                self.src, self.spot(self.row, self.core), self.send.at[0], self.recv.at[0], self.sibling
            )
        piece = self.spot(self.row ^ d, self.core)
        return remote(piece, piece, self.send.at[3 + d], self.recv.at[3 + d], self.sibling)

    def local(self):
        return pltpu.make_async_copy(self.src, self.spot(self.row, self.core), self.own)

    def start(self):
        for d in (1, 2, 3):
            self.to_row(d).start()
        self.to_sibling(0).start()
        self.local().start()

    def forward(self):
        for d in (1, 2, 3):
            piece = self.spot(self.row ^ d, self.core)
            remote(piece, piece, self.send.at[d], self.recv.at[d], {"row": self.row ^ d}).wait_recv()
            self.to_sibling(d).start()

    def finish(self):
        self.local().wait()
        for d in (0, 1, 2, 3):
            piece = self.spot(self.row ^ d, 1 - self.core)
            sem = 0 if d == 0 else 3 + d
            remote(piece, piece, self.send.at[sem], self.recv.at[sem], self.sibling).wait_recv()

    def sent(self):
        for d in (1, 2, 3):
            self.to_row(d).wait_send()
            self.to_sibling(d).wait_send()
        self.to_sibling(0).wait_send()


def gelu_parts(b):
    t = jnp.tanh(GELU_A * (b + GELU_B * (b * b * b)))
    half = 0.5 + 0.5 * t
    slope = half + (0.5 * b) * (1.0 - t * t) * (GELU_A + (3.0 * GELU_A * GELU_B) * (b * b))
    return b * half, slope


def eight(v):
    return jnp.sum(v.reshape(v.shape[0] // 8, 8, v.shape[1]), axis=0)


def fold(v):
    total = v[:, 0:128]
    for j in range(1, v.shape[1] // 128):
        total = total + v[:, j * 128 : (j + 1) * 128]
    return total


def tokens_of(ref, piece):
    return jnp.concatenate([ref[k, piece, :] for k in range(ref.shape[0])], axis=1)


def blocks(count, body):
    def one(i, carry):
        body(i)
        return carry

    lax.fori_loop(0, count, one, 0)


def scale_of(ref, eps, width):
    total = jnp.sum(jnp.sum(ref[...], axis=0), axis=0, keepdims=True)
    return lax.rsqrt(total / width + eps)


def forward_kernel(
    width, eps,
    x_in, g_in, segs, taps, offs, bias_r, bias_a, decay, mix, late, retain, admit, branch, recur, mn_s, gu_s, d_s,
    masks, par, gains, gates, coef, scale, scale_two, y_out, n1_out, q_out, x_out, g_out, b_out, p_out, u_out, r_out, i_out, h_out,
    result, dn2_out, dev_h, z_h, g_own, g_got, gd_own, gd_got, br_n, m_n,
    sums, sums2, sums3, vec, br_s, brn_s, m_s, vec_all, block_all, gates_hi, gates_lo, normed, normed2, go, x_own, y, dn2, q_c, p_s, h_s, room, uh, ul,
    own, held, held_n, held_o, gu, gun, down, dt, zs, dev,
    x_send, x_recv, x_loc, i_send, i_recv, i_loc, l_send, l_recv, n_send, n_recv, c_send, c_recv, g_send, g_recv, e_send, e_recv, f_send, f_recv,
    s_send, s_recv, t_send, t_recv, o_send, o_recv, w_send, w_recv, w_own, k_sem, v_sem, d_send, d_recv, d_own,
):
    row, z, core = place()
    block, seq = y.shape
    half = x_in.shape[0]
    chan = p_s.shape[0]
    hid = zs.shape[0]
    b_s, u_s, r_s, i_s, a_c = [room.at[n * chan : (n + 1) * chan, :] for n in range(5)]
    ev, dz = room.at[0 : 2 * hid, :], room.at[2 * hid : 3 * hid, :]
    hh = hid // 2
    hc = chan // 2
    sibling = {"col": 2 * z + (1 - core)}
    met = greet(row, z, core, True, True)
    br_s[0:hc, :] = branch[...].T
    br_s[hc:, :] = recur[...].T
    m_s[...] = mn_s[...].T
    br, mt = gun.at[0 : 2 * chan, 0:width], dt.at[:, 0:chan]
    wide = br_s.shape[0]
    recur_s, branch_s = br_s.at[wide // 2 :, :], br_s.at[0 : wide // 2, :]
    weights = [
        Weights(src, dst, w_send.at[n], w_recv.at[n], w_own.at[n], row, z, core, n in (2, 5), stride, start)
        for n, (src, dst, stride, start) in enumerate(
            (
                (recur_s, br, hc, 0),
                (branch_s, br, hc, chan),
                (m_s, mt, 0, 0),
                (gu_s, gu, 0, 0),
                (d_s, down, 0, 0),
                (brn_s, br_n, 0, 0),
                (mn_s, m_n, 0, 0),
            )
        )
    ]
    mine = pl.ds(pl.multiple_of(core * seq, seq), seq)
    other = pl.ds(pl.multiple_of((1 - core) * seq, seq), seq)
    inner = pl.ds(pl.multiple_of(z * block + core * half, 16), half)
    outer = rows_of(core, half)
    swaps = [
        remote(x_in.at[:, other], x_own.at[outer, :], x_send.at[0], x_recv.at[0], sibling),
        pltpu.make_async_copy(x_in.at[:, mine], x_own.at[outer, :], x_loc.at[0]),
    ]
    for k in range(PARTS):
        theirs, ours = [pl.ds(pl.multiple_of(c * seq + k * PART, 128), PART) for c in (1 - core, core)]
        swaps.append(remote(g_in.at[:, theirs], go.at[k, inner, :], i_send.at[k], i_recv.at[k], sibling))
        swaps.append(pltpu.make_async_copy(g_in.at[:, ours], go.at[k, inner, :], i_loc.at[k]))
    vec[...] = jnp.zeros(vec.shape, F32)
    vec[0:4, :] = taps[...]
    for n, one_row in enumerate((offs, bias_r, bias_a)):
        vec[4 + n : 5 + n, :] = one_row[...]
    rate = -decay[...]
    vec[7:8, :] = 8.0 * (jnp.maximum(rate, 0.0) + jnp.log1p(jnp.exp(-jnp.abs(rate))))
    vec[8:9, 0:half] = mix[...]
    vec[9:10, 0:half] = late[...]
    brn_s[:, 0:hc] = branch[...]
    brn_s[:, hc:] = recur[...]
    met()
    for w in weights[:3]:
        w.start()
    for swap in swaps:
        swap.start()
    trades = []
    for n, (src, dst) in enumerate(
        ((vec, vec_all.at[core]), (retain, block_all.at[core, 0]), (admit, block_all.at[core, 1]))
    ):
        trades.append(remote(src, dst, x_send.at[2 + n], x_recv.at[2 + n], sibling))
        trades.append(pltpu.make_async_copy(src, dst, x_loc.at[2 + n]))
    for trade in trades:
        trade.start()
    for swap in swaps + trades:
        swap.wait()
    flushes = [
        pltpu.make_async_copy(x_own, x_out, v_sem.at[0]),
        pltpu.make_async_copy(go.at[:, rows_of(z, block), :], g_out, v_sem.at[1]),
    ]
    for flush in flushes:
        flush.start()
    gather = Gather(normed, g_send, g_recv, z, core, block)
    gather_go = Gather(go, e_send, e_recv, z, core, block)
    gather_two = Gather(normed2, f_send, f_recv, z, core, block)
    shares = lambda k, s: own.at[k, s]
    shares_o = lambda k, s: normed.at[k, rows_of(s, block), :]
    spread = Spread(shares, held, s_send, s_recv, z, core)
    spread_n = Spread(shares, held_n, t_send, t_recv, z, core)
    spread_o = Spread(shares_o, held_o, o_send, o_recv, z, core)
    res = x_own
    gather_go.send(0, 0)
    gather_go.send(0, 1)
    for c in (0, 1):
        at = slice(c * hc, (c + 1) * hc)
        par[at, :] = vec_all[c].T
        gains[c * half : (c + 1) * half, :] = par[c * hc : c * hc + half, :]

    sums[z] = jnp.zeros(sums.shape[1:], F32)

    def squares(i):
        v = x_own[rows_of(i, 16), :].astype(F32)
        v = v * v
        sums[z] += v[:8] + v[8:]

    blocks(block // 16, squares)
    share_line(sums, l_send, l_recv, z, core)
    scale[...] = jnp.broadcast_to(scale_of(sums, eps, width), scale.shape)

    def norm(i):
        v = x_own[rows_of(i, 16), :].astype(F32) * scale[0:1, :] * gains[rows_of(i, 16), 8:9]
        v = v.astype(BF16)
        for k in range(PARTS):
            normed[k, pl.ds(pl.multiple_of(z * block + i * 16, 16), 16), :] = v[:, k * PART : (k + 1) * PART]

    blocks(block // 16, norm)
    gather.send(0, 0)
    p_s[:, PART:] = jnp.zeros((chan, 128), F32)
    h_s[:, PART:] = jnp.zeros((chan, 128), F32)
    pads = [
        pltpu.make_async_copy(src.at[:, PART:], out.at[:, 0:128], v_sem.at[2 + n])
        for n, (src, out) in enumerate(((p_s, p_out), (h_s, h_out)))
    ]
    for pad in pads:
        pad.start()
    gates[...] = jnp.zeros(gates.shape, BF16)
    gates_hi[...] = jnp.zeros(gates_hi.shape, BF16)
    gates_lo[...] = jnp.zeros(gates_lo.shape, BF16)
    per = retain.shape[0]
    tap = retain.shape[1]
    for c in (0, 1):
        for n in (0, 1):
            for e in range(per):
                w = block_all[c, n, e]
                at, far = slice(e * tap, (e + 1) * tap), slice(n * hc + e * tap, n * hc + (e + 1) * tap)
                gates[c, at, far] = w.astype(BF16)
                w = w.T
                high = w.astype(BF16)
                gates_hi[c, far, at] = high
                gates_lo[c, far, at] = (w - high.astype(F32)).astype(BF16)
    masks[...] = jnp.zeros(masks.shape, F32)
    here = jnp.broadcast_to(segs[:, mine], (8, seq))
    spot = lax.broadcasted_iota(jnp.int32, (8, seq), 1)
    for lag in (1, 2, 3):
        same = jnp.where((pltpu.roll(here, lag, 1) == here) & (spot >= lag), 1.0, 0.0)
        masks[lag : lag + 1, 0:seq] = same[0:1]
        if lag == 1:
            masks[0:1, 0:seq] = 1.0 - same[0:1]
    gather.forward(1, 0)
    gather.send(0, 1)
    weights[0].forward()
    gather.forward(2, 0)
    gather_go.forward(1, 0)
    gather.forward(1, 1)
    gather.send(0, 2)
    weights[1].forward()
    for w in weights[3:5]:
        w.start()
    gather_go.forward(1, 1)
    gather_go.forward(2, 0)
    weights[0].finish()
    for pad in pads:
        pad.wait()

    kept = (b_s, p_s, u_s, r_s, i_s, h_s, q_c)
    outs = (b_out, p_out, u_out, r_out, i_out, h_out, q_out)

    def keep(n, part):
        if n in (1, 5):
            at = pl.ds(pl.multiple_of(128 + part * PART, 128), PART)
            return pltpu.make_async_copy(kept[n].at[:, 128:], outs[n].at[:, at], k_sem.at[n])
        return pltpu.make_async_copy(kept[n], outs[n].at[:, lanes(part)], k_sem.at[n])

    def put_shares(k, whole):
        for s in range(LINE):
            own[k, s] = whole[s * block : (s + 1) * block, :].astype(own.dtype)

    def work(k):
        here = lanes(k)

        @pl.when(k > 0)
        def _():
            for n in range(len(kept)):
                keep(n, k - 1).wait()

        p_s[:, 0:128] = p_s[:, PART:]
        h_s[:, 0:128] = h_s[:, PART:]
        p_s[:, 128:] = dot(br[0:chan, :], normed[k])

        def conv(i):
            ch = rows_of(i, 64)
            window = p_s[ch, :]
            pr = par[ch, :]
            u = pr[:, 4:5] + pr[:, 0:1] * window[:, 128:]
            for lag in (1, 2, 3):
                u = u + pr[:, lag : lag + 1] * (pltpu.roll(window, lag, 1)[:, 128:] * masks[lag : lag + 1, here])
            u_s[ch, :] = u
            high = u.astype(BF16)
            uh[ch, :] = high
            ul[ch, :] = (u - high.astype(F32)).astype(BF16)

        blocks(chan // 64, conv)
        gather.middle(k)
        for g in range(chan // 256):
            at = slice(g * 256, (g + 1) * 256)
            pre = dot(gates_hi[g], uh[at, :]) + dot(gates_hi[g], ul[at, :]) + dot(gates_lo[g], uh[at, :])
            r_s[at, :] = pre[:256]
            i_s[at, :] = pre[256:]

        def gated(i):
            ch = rows_of(i, 64)
            pr = par[ch, :]
            start = masks[0:1, here] > 0.5
            r = jax.nn.sigmoid(r_s[ch, :] + pr[:, 5:6])
            gate = jax.nn.sigmoid(i_s[ch, :] + pr[:, 6:7])
            r_s[ch, :] = r
            i_s[ch, :] = gate
            a = jnp.exp(-(r * pr[:, 7:8]))
            m = jnp.where(start, 1.0, jnp.sqrt(1.0 - a * a + FLOOR))
            a_c[ch, :] = jnp.where(start, 0.0, a)
            h_s[ch, 128:] = m * gate * u_s[ch, :]

        blocks(chan // 64, gated)
        first = lax.broadcasted_iota(jnp.int32, (128, PART), 1) == 0

        def recur(i):
            ch = rows_of(i, 128)
            a, h = a_c[ch, :], h_s[ch, 128:]
            h = h + jnp.where(first, a * h_s[ch, 0:128][:, 127:128], 0.0)
            a = jnp.where(first, 0.0, a)
            shift = 1
            while shift < PART:
                h = h + a * pltpu.roll(h, shift, 1)
                if shift * 2 < PART:
                    a = a * pltpu.roll(a, shift, 1)
                shift *= 2
            h_s[ch, 128:] = h

        blocks(chan // 128, recur)

        @pl.when(k == 0)
        def _():
            weights[2].forward()
            weights[1].finish()

        b_s[...] = dot(br[chan : 2 * chan, :], normed[k])

        def mixed(i):
            ch = rows_of(i, 64)
            b = b_s[ch, :]
            t = jnp.tanh(GELU_A * (b + GELU_B * (b * b * b)))
            q_c[ch, :] = (b * (0.5 + 0.5 * t) * h_s[ch, 128:]).astype(BF16)

        blocks(chan // 64, mixed)
        pl.when(k == 0)(weights[2].finish)
        put_shares(k, dot(mt[...], q_c[...]))
        for n in range(len(kept)):
            keep(n, k).start()

    def finish(k, total):
        def add(i):
            at = pl.multiple_of(i * 64, 64)
            y[pl.ds(at, 64), lanes(k)] = x_own[pl.ds(at, 64), lanes(k)].astype(F32) + total(at, 64)

        blocks(block // 64, add)

    def square(k):
        sums2[k, z] = jnp.zeros(sums2.shape[2:], F32)

        def one(i):
            v = y[rows_of(i, 64), lanes(k)]
            sums2[k, z] += eight(v * v)

        blocks(block // 64, one)
        for d in (1, 2, 3):
            share(k, d).start()

    def share(k, d):
        return remote(
            sums2.at[k, z], sums2.at[k, z], n_send.at[k, d - 1], n_recv.at[k, d - 1], at_line(z ^ d, core)
        )

    def norm_two(k):
        for d in (1, 2, 3):
            piece = sums2.at[k, z ^ d]
            remote(piece, piece, n_send.at[k, d - 1], n_recv.at[k, d - 1], at_line(z ^ d, core)).wait_recv()
        s2 = scale_of(sums2.at[k], eps, width)
        scale_two[:, lanes(k)] = jnp.broadcast_to(s2, (8, PART))

        def one(i):
            at = rows_of(i, 64)
            v = y[at, lanes(k)] * scale_two[0:1, lanes(k)] * gains[at, 9:10]
            normed2[k, pl.ds(pl.multiple_of(z * block + i * 64, 64), 64), :] = v.astype(BF16)

        blocks(block // 64, one)

    def turn_down(i):
        at = pl.ds(pl.multiple_of(i * 128, 128), 128)
        dt[:, at] = down[at, :].T

    def turn_up(i):
        at = pl.ds(pl.multiple_of(i * 128, 128), 128)
        gun[:, at] = gu[at, :].T

    def step(t, carry):
        gather.arrive(2, t)
        work(t)
        spread.serve(t, finish)
        pl.when(t >= 3)(lambda: square(t - 3))
        pl.when(t >= 4)(lambda: norm_two(t - 4))
        pl.when((t >= 4) & (t < 7))(lambda: gather_two.send(0, t - 4))
        pl.when((t >= 6) & (t < 8))(lambda: gather_two.forward(1, t - 6))
        pl.when(t == 5)(weights[3].forward)
        return carry

    lax.fori_loop(0, PARTS, step, 0)
    for w in weights[:3]:
        w.sent()
    for w in weights[5:]:
        w.start()
    for n in range(len(kept)):
        keep(n, PARTS - 1).wait()
    flush_n = pltpu.make_async_copy(normed, n1_out, v_sem.at[4])
    flush_n.start()
    gather_go.forward(2, 1)
    gather_go.send(0, 2)
    gather_go.send(0, 3)
    spread.serve(PARTS, finish)
    square(PARTS - 3)
    norm_two(PARTS - 4)
    gather_two.forward(2, 0)
    weights[3].finish()
    blocks(2 * hid // 128, turn_up)
    weights[4].forward()
    spread.serve(PARTS + 1, finish)
    square(PARTS - 2)
    norm_two(PARTS - 3)
    gather_go.forward(1, 2)
    weights[4].finish()
    blocks(hid // 128, turn_down)
    gather.sent()
    for flush in flushes + [flush_n]:
        flush.wait()
    flush_y = pltpu.make_async_copy(y, y_out, v_sem.at[2])

    def keep_dev(k):
        return pltpu.make_async_copy(dev, dev_h.at[:, lanes(k)], v_sem.at[5])

    def keep_z(k):
        return pltpu.make_async_copy(zs, z_h.at[:, lanes(k)], v_sem.at[6])

    dev_all, z_all = gu.at[:, 0:seq], dt.at[0:hid, 0:seq]
    before, end = pl.ds(0, seq - PART), pl.ds(seq - PART, PART)
    loads = [
        pltpu.make_async_copy(dev_h.at[:, before], gu.at[:, before], v_sem.at[7]),
        pltpu.make_async_copy(z_h.at[:, before], dt.at[0:hid, before], v_sem.at[8]),
        pltpu.make_async_copy(dev, gu.at[:, end], v_sem.at[9]),
        pltpu.make_async_copy(zs, dt.at[0:hid, end], v_sem.at[10]),
    ]

    def feed(k):

        @pl.when(k > 0)
        def _():
            keep_dev(k - 1).wait()
            keep_z(k - 1).wait()

        ev[...] = dot(gu[...], normed2[k])

        @pl.when(k == PARTS - 1)
        def _():
            weights[3].sent()
            loads[0].start()

        gather_two.middle(k)
        gather_go.middle(k, 2)
        gather_go.arrive(2, k)
        dz[...] = dot(down[...], go[k])
        for c in range(2):

            def one(i):
                off = pl.multiple_of(i * 64, 64)
                e = ev[pl.ds(c * 2 * hh + off, 64), :]
                v = ev[pl.ds(c * 2 * hh + hh + off, 64), :]
                d = dz[pl.ds(c * hh + off, 64), :]
                act, slope = gelu_parts(e)
                zs[pl.ds(c * hh + off, 64), :] = (act * v).astype(BF16)
                dev[pl.ds(c * 2 * hh + off, 64), :] = (d * v * slope).astype(BF16)
                dev[pl.ds(c * 2 * hh + hh + off, 64), :] = (d * act).astype(BF16)

            blocks(hh // 64, one)
        put_shares(k, dot(gun[...], dev[...]))
        spread_n.serve(k, finish_n)
        normed[k] = dot(dt[...], zs[...]).astype(BF16)
        spread_o.serve(k, finish_o)
        keep_dev(k).start()
        keep_z(k).start()

        @pl.when(k == 0)
        def _():
            spread.serve(PARTS + 2, finish)
            square(PARTS - 1)
            norm_two(PARTS - 2)

        @pl.when(k == 1)
        def _():
            norm_two(PARTS - 1)
            flush_y.start()

    def finish_o(k, total):
        def add(i):
            at = pl.multiple_of(i * 64, 64)
            res[pl.ds(at, 64), lanes(k)] = (y[pl.ds(at, 64), lanes(k)] + total(at, 64)).astype(BF16)

        blocks(block // 64, add)

    def keep_n(k):
        return pltpu.make_async_copy(dn2, dn2_out.at[:, lanes(k)], v_sem.at[3])

    def finish_n(k, total):
        @pl.when(k > 0)
        def _():
            keep_n(k - 1).wait()

        sums3[k, z] = jnp.zeros(sums3.shape[2:], F32)

        def add(i):
            at = pl.multiple_of(i * 64, 64)
            d = total(at, 64)
            dn2[pl.ds(at, 64), :] = d
            sums3[k, z] += eight(d * y[pl.ds(at, 64), lanes(k)] * gains[pl.ds(at, 64), 9:10])

        blocks(block // 64, add)
        keep_n(k).start()
        for d in (1, 2, 3):
            share_c(k, d).start()

    def share_c(k, d):
        return remote(
            sums3.at[k, z], sums3.at[k, z], c_send.at[k, d - 1], c_recv.at[k, d - 1], at_line(z ^ d, core)
        )

    def feed_step(t, carry):
        gather_two.arrive(2, t)
        feed(t)
        pl.when(t == 4)(weights[5].forward)
        pl.when(t == 6)(weights[6].forward)
        return carry

    lax.fori_loop(0, PARTS, feed_step, 0)
    weights[4].sent()
    for load in loads[1:]:
        load.start()
    keep_dev(PARTS - 1).wait()
    keep_z(PARTS - 1).wait()
    loads[0].wait()
    loads[2].wait()

    def columns(start):
        return pl.ds(pl.multiple_of(start, 128), block)

    def place_up(j):
        side = jnp.where(j >= 3, core, 1 - core)
        return side * hid + (j % 3) * block, columns((j % 3) * block)

    def send_up(j):
        at, to = place_up(j)
        return remote(gun.at[:, columns(at)], g_got.at[:, to], d_send.at[j], d_recv.at[j], sibling)

    def keep_up(j):
        at, to = place_up(j)
        return pltpu.make_async_copy(gun.at[:, columns(at)], g_own.at[:, to], d_own.at[j - 3])

    def send_down():
        return remote(down.at[rows_of(1 - core, hh), :], gd_got, d_send.at[3], d_recv.at[3], sibling)

    def keep_down():
        return pltpu.make_async_copy(down.at[rows_of(core, hh), :], gd_own, d_own.at[3])

    def grad_up(j):
        at = place_up(j)[0]
        right = pl.ds(pl.multiple_of(at, 16), block)
        for low in (0, width // 2):
            piece = slice(low, low + width // 2)
            gun[piece, columns(at)] = dot_nt(tokens_of(normed2, piece), dev_all[right, :]).astype(BF16)

        @pl.when(j < 3)
        def _():
            send_up(j).start()

        @pl.when(j >= 3)
        def _():
            keep_up(j).start()

    def grad_down(side):
        at = rows_of(side, hh)
        for low in range(0, width, 2 * block):
            piece = slice(low, low + 2 * block)
            down[at, piece] = dot_nt(z_all[at, :], tokens_of(go, piece)).astype(BF16)

    def drain(i, carry):
        t = PARTS + i
        grad_up(2 * i)
        spread_n.serve(t, finish_n)
        spread_o.serve(t, finish_o)
        grad_up(2 * i + 1)

        @pl.when(i == 0)
        def _():
            loads[1].wait()
            loads[3].wait()

        @pl.when(i < 2)
        def _():
            grad_down(jnp.where(i == 0, 1 - core, core))

        pl.when(i == 0)(lambda: send_down().start())
        pl.when(i == 1)(lambda: keep_down().start())
        return carry

    lax.fori_loop(0, LINE - 1, drain, 0)
    last = [
        remote(res.at[rows_of(1 - core, half), :], result.at[:, mine], x_send.at[0], x_recv.at[0], sibling),
        pltpu.make_async_copy(res.at[rows_of(core, half), :], result.at[:, mine], x_loc.at[0]),
        keep_n(PARTS - 1),
        flush_y,
    ]
    for copy in last[:2]:
        copy.start()
    for w in weights[5:]:
        w.finish()
        w.sent()
    for one in (gather_go, gather_two, spread, spread_n, spread_o):
        one.sent()
    for k in range(PARTS):
        for d in (1, 2, 3):
            share(k, d).wait_send()
            share_c(k, d).wait_send()
            piece = sums3.at[k, z ^ d]
            remote(piece, piece, c_send.at[k, d - 1], c_recv.at[k, d - 1], at_line(z ^ d, core)).wait_recv()
        total = jnp.sum(jnp.sum(sums3[k], axis=0), axis=0, keepdims=True)
        at = slice(k * PART, (k + 1) * PART)
        s2 = scale_two[:, at]
        coef[:, at] = s2 * s2 * s2 * (total / width)
    for j in range(3):
        keep_up(j + 3).wait()
        send_up(j).wait()
    keep_down().wait()
    send_down().wait()
    for copy in last:
        copy.wait()


def back_kernel(
    width,
    y, dn2_h, g_h, x_own, scale_two, scale_one, coef_two, gains, masks, par, gates_t, m_h, br_h,
    b_h, p_h, u_h, r_h, i_h, h_h, q_h, n1_h, f_own, f_got, fd_own, fd_got,
    input_grad, tiny_v, tiny_g, f_sum, f_land, fd_sum, fd_land, g_sum, g_land, gm_sum, gm_land,
    sums, coef, m_n, br_n, b_s, p_s, u_s, r_s, i_s, h_s, dyf, dbp, dy, dn1, dq, du, dri, a_c, l_c, carry_s, own, held,
    qv, n1, f_a, f_b, fd_a, fd_b, feed_part, mix_part, small, gate_grad, g_s, g_got, gm_got,
    vec, vec_in, vec_all, gd, gd_in, gd_all,
    c_sem, k_sem, l_send, l_recv, g_send, g_recv, s_send, s_recv, r_send, r_recv,
    f_sem, f_send, f_recv, d_send, d_recv, d_own, q_send, q_recv, n_send, n_recv, v_send, v_recv,
):
    row, z, core = place()
    block, seq = y.shape
    PART, PARTS = LATE, seq // LATE

    def lanes(part):
        return pl.ds(pl.multiple_of(part * PART, PART), PART)

    half = block // 2
    chan = b_s.shape[1]
    hc = chan // 2
    sibling = {"col": 2 * z + (1 - core)}
    met = greet(row, z, core, True, True)
    load_g = pltpu.make_async_copy(g_h, g_s, c_sem.at[0])
    load_g.start()
    dn2 = dn1
    load_d = pltpu.make_async_copy(dn2_h, dn2, c_sem.at[5])
    load_d.start()
    load_m = pltpu.make_async_copy(m_h, m_n, c_sem.at[1])
    load_m.start()
    load_b = pltpu.make_async_copy(br_h, br_n, c_sem.at[2])
    load_b.start()
    load_q = pltpu.make_async_copy(q_h, qv, c_sem.at[3])
    load_n = pltpu.make_async_copy(n1_h, n1, c_sem.at[4])
    kept = (b_s, p_s, u_s, r_s, i_s, h_s)
    srcs = (b_h, p_h, u_h, r_h, i_h, h_h)

    def fetch(n, part):
        if kept[n] is p_s or kept[n] is h_s:
            at = pl.ds(pl.multiple_of(part * PART, 128), PART + 128)
        else:
            at = lanes(part)
        return pltpu.make_async_copy(srcs[n].at[:, at], kept[n].at[part % 2], k_sem.at[n, part % 2])

    def fetch_all(part):
        for n in range(len(kept)):
            fetch(n, part).start()

    fetch_all(PARTS - 1)
    load_q.start()
    load_n.start()
    du[:, 0:128] = jnp.zeros((chan, 128), F32)
    carry_s[...] = jnp.zeros(carry_s.shape, F32)
    small[...] = jnp.zeros(small.shape, F32)
    gate_grad[...] = jnp.zeros(gate_grad.shape, F32)

    load_d.wait()
    load_g.wait()
    gather = Gather(dyf, g_send, g_recv, z, core, block, back=True)

    def outer(part):
        here = slice(part * PART, (part + 1) * PART)

        def one(i):
            at = rows_of(i, 64)
            s2 = scale_two[0:1, here]
            d, v = dn2[at, here], y[at, here]
            w = fold(d * v * s2)
            feed_part[at, :] = w if part == PARTS - 1 else feed_part[at, :] + w
            few = PART // g_s.shape[2]
            g = jnp.concatenate([g_s[part * few + j, at, :] for j in range(few)], axis=1)
            v = g.astype(F32) + (s2 * (gains[at, 9:10] * d) - v * coef_two[0:1, here])
            dy[at, here] = v
            dyf[part, pl.ds(pl.multiple_of(z * block + i * 64, 64), 64), :] = v.astype(BF16)

        blocks(block // 64, one)

    outer(PARTS - 1)
    met()
    gather.send(0, 0)
    for part in range(PARTS - 2, -1, -1):
        outer(part)
    gather.forward(1, 0)
    gather.send(0, 1)
    gather.forward(2, 0)
    gather.forward(1, 1)
    gather.send(0, 2)
    spread = Spread(lambda k, s: own.at[k, s], held, s_send, s_recv, z, core)
    load_m.wait()
    load_b.wait()
    final = lax.broadcasted_iota(jnp.int32, (128, PART), 1) == PART - 1

    f_arrays = ((f_own, f_got, f_a, f_b, f_sum, f_land), (fd_own, fd_got, fd_a, fd_b, fd_sum, fd_land))

    def f_loads(d):
        pulls = []
        for n, (ours, theirs, a, b, _, _) in enumerate(f_arrays):
            if n == 0:
                piece = (rows_of(row ^ d, block), slice(None))
            else:
                piece = (slice(None), pl.ds(pl.multiple_of((row ^ d) * block, 128), block))
            pulls.append(pltpu.make_async_copy(ours.at[piece], a.at[d], f_sem.at[n, 0]))
            pulls.append(pltpu.make_async_copy(theirs.at[piece], b, f_sem.at[n, 1]))
        return pulls

    def f_out(d):
        outs = []
        for n, (_, _, a, _, kept_at, land) in enumerate(f_arrays):
            if d == 0:
                outs.append(pltpu.make_async_copy(a.at[0], kept_at, f_send.at[n, 0]))
            else:
                outs.append(
                    remote(a.at[d], land.at[d - 1], f_send.at[n, d], f_recv.at[n, d], {"row": row ^ d})
                )
        return outs

    def f_part(d):
        for pull in f_loads(d):
            pull.wait()
        for _, _, a, b, _, _ in f_arrays:

            def add(i):
                at = rows_of(i, 64)
                a[d, at, :] = (a[d, at, :].astype(F32) + b[at, :].astype(F32)).astype(BF16)

            blocks(b.shape[0] // 64, add)
        for out in f_out(d):
            out.start()
        if d > 0:
            for pull in f_loads(d - 1):
                pull.start()

    def f_step(t):
        for d in range(LINE):
            pl.when(t == LINE - 1 - d)(functools.partial(f_part, d))

    for pull in f_loads(LINE - 1):
        pull.start()

    lru = hc

    def send_m():
        return remote(m_n.at[rows_of(1 - core, lru), :], gm_got, d_send.at[1], d_recv.at[1], sibling)

    def work(t):
        k = PARTS - 1 - t
        here = lanes(k)
        wide = pl.ds(pl.multiple_of(k * PART, 128), PART + 128)
        slot = k % 2
        for n in range(len(kept)):
            fetch(n, k).wait()

        @pl.when(k > 0)
        def _():
            fetch_all(k - 1)

        dq[...] = dot(m_n[...], dyf[k])

        @pl.when(t == PARTS - 1)
        def _():
            load_q.wait()
            for low in range(0, width, 2 * block):
                piece = slice(low, low + 2 * block)
                m_n[:, piece] = dot_nt(qv[...], tokens_of(dyf, piece)).astype(BF16)
            send_m().start()

        def before(i):
            ch = rows_of(i, 64)
            c = i // (hc // 64)
            low = pl.ds(pl.multiple_of(c * hc + i * 64, 64), 64)
            pr = par[ch, :]
            d = dq[ch, :]
            act, slope = gelu_parts(b_s[slot, ch, :])
            dbp[low, here] = (d * h_s[slot, ch, :][:, 128:] * slope).astype(BF16)
            l_c[ch, :] = d * act
            a_c[ch, :] = jnp.exp(-(r_s[slot, ch, :] * pr[:, 7:8]))

        blocks(chan // 64, before)
        gather.middle(t)

        def recur(i):
            ch = rows_of(i, 128)
            start = masks[0:1, here] > 0.5
            a, lam = jnp.where(start, 0.0, a_c[ch, :]), l_c[ch, :]
            lam = lam + jnp.where(final, carry_s[ch, :][:, 0:1], 0.0)
            w = jnp.where(final, 0.0, pltpu.roll(a, PART - 1, 1))
            shift = 1
            while shift < PART:
                lam = lam + w * pltpu.roll(lam, PART - shift, 1)
                if shift * 2 < PART:
                    w = w * pltpu.roll(w, PART - shift, 1)
                shift *= 2
            carry_s[ch, :] = jnp.broadcast_to((a * lam)[:, 0:1], (128, 128))
            l_c[ch, :] = lam

        blocks(chan // 128, recur)
        f_step(t)

        def after(i):
            ch = rows_of(i, 64)
            du[ch, PART:] = du[ch, 0:128]
            pr = par[ch, :]
            start = masks[0:1, here] > 0.5
            lam, a0 = l_c[ch, :], a_c[ch, :]
            earlier = pltpu.roll(h_s[slot, ch, :], 1, 1)[:, 128:]
            r, gate, u = r_s[slot, ch, :], i_s[slot, ch, :], u_s[slot, ch, :]
            m0 = jnp.sqrt(1.0 - a0 * a0 + FLOOR)
            m = jnp.where(start, 1.0, m0)
            lm = lam * m
            lu = lam * u
            du[ch, 0:PART] = lm * gate
            da = jnp.where(start, 0.0, lam * earlier - (lu * gate) * (a0 / m0)) * a0
            dr = da * (-pr[:, 7:8]) * (r * (1.0 - r))
            di = lu * m * (gate * (1.0 - gate))
            g, o = i // 4, (i % 4) * 64
            dri[pl.ds(pl.multiple_of(g * 512 + o, 64), 64), :] = dr.astype(BF16)
            dri[pl.ds(pl.multiple_of(g * 512 + 256 + o, 64), 64), :] = di.astype(BF16)
            small[5, ch, :] += fold(dr)
            small[6, ch, :] += fold(di)
            small[7, ch, :] += fold(da * r)

        blocks(chan // 64, after)
        for g in range(chan // 256):
            at = slice(g * 256, (g + 1) * 256)
            dd = dri[g * 512 : (g + 1) * 512, :]
            du[at, 0:PART] += dot(gates_t[g], dd)
            gate_grad[g] += dot_nt(u_s[slot, at, :].astype(BF16), dd)

        def conv(i):
            ch = rows_of(i, 64)
            c = i // (hc // 64)
            low = pl.ds(pl.multiple_of((c + 1) * hc + i * 64, 64), 64)
            pr = par[ch, :]
            follow = du[ch, :]
            window = p_s[slot, ch, :]
            d = follow[:, :PART]
            dp = pr[:, 0:1] * d
            small[4, ch, :] += fold(d)
            small[0, ch, :] += fold(d * window[:, 128:])
            for lag in (1, 2, 3):
                kd = follow * masks[lag : lag + 1, wide]
                dp = dp + pr[:, lag : lag + 1] * pltpu.roll(kd, PART + 128 - lag, 1)[:, :PART]
                small[lag, ch, :] += fold(kd[:, :PART] * pltpu.roll(window, lag, 1)[:, 128:])
            dbp[low, here] = dp.astype(BF16)

        blocks(chan // 64, conv)
        whole = dot(br_n[...], dbp[:, here])
        for s in range(LINE):
            own[t, s] = whole[s * block : (s + 1) * block, :].astype(own.dtype)

    def finish(t, total):
        k = PARTS - 1 - t

        sums[k, z] = jnp.zeros(sums.shape[2:], F32)

        @pl.when(t == 0)
        def _():
            mix_part[...] = jnp.zeros(mix_part.shape, F32)

        def add(i):
            at = pl.ds(pl.multiple_of(i * 64, 64), 64)
            d = total(pl.multiple_of(i * 64, 64), 64)
            dn1[at, lanes(k)] = d
            w = d * x_own[at, lanes(k)].astype(F32)
            sums[k, z] += eight(w * gains[at, 8:9])
            w = w * scale_one[0:1, lanes(k)]
            mix_part[at, :] += fold(w)

        blocks(block // 64, add)
        for d in (1, 2, 3):
            share(k, d).start()

    def share(k, d):
        return remote(sums.at[k, z], sums.at[k, z], l_send.at[k, d - 1], l_recv.at[k, d - 1], at_line(z ^ d, core))

    def step(t, carry):
        gather.arrive(2, t)
        work(t)
        spread.serve(t, finish)
        return carry

    lax.fori_loop(0, PARTS, step, 0)
    load_n.wait()


    def cols_of(side):
        return pl.ds(pl.multiple_of(side * 2 * lru, 128), 2 * lru)

    def send_br():
        return remote(br_n.at[:, cols_of(1 - core)], g_got, d_send.at[0], d_recv.at[0], sibling)

    def grad_br(side):
        for low in range(0, width, 2 * block):
            piece = slice(low, low + 2 * block)
            br_n[piece, cols_of(side)] = dot_nt(tokens_of(n1, piece), dbp[rows_of(side, 2 * lru), :]).astype(BF16)

    def out_br(d):
        piece = br_n.at[rows_of(row ^ d, block), cols_of(core)]
        if d == 0:
            return pltpu.make_async_copy(piece, g_sum, d_own.at[0])
        return remote(piece, g_land.at[d - 1], q_send.at[0, d - 1], q_recv.at[0, d - 1], {"row": row ^ d})

    def out_m(d):
        piece = m_n.at[rows_of(core, lru), pl.ds(pl.multiple_of((row ^ d) * block, 128), block)]
        if d == 0:
            return pltpu.make_async_copy(piece, gm_sum, d_own.at[1])
        return remote(piece, gm_land.at[d - 1], q_send.at[1, d - 1], q_recv.at[1, d - 1], {"row": row ^ d})

    def drain(i, carry):
        t = PARTS + i

        @pl.when(i == 0)
        def _():
            grad_br(1 - core)
            send_br().start()
            send_m().wait_recv()

            def add(j):
                at = rows_of(j, 64)
                to = pl.ds(pl.multiple_of(core * lru + j * 64, 64), 64)
                m_n[to, :] = (m_n[to, :].astype(F32) + gm_got[at, :].astype(F32)).astype(BF16)

            blocks(lru // 64, add)
            for d in (3, 2, 1, 0):
                out_m(d).start()
            grad_br(core)

        @pl.when(i == 1)
        def _():
            send_br().wait_recv()

            def add(j):
                at = rows_of(j, 64)
                br_n[at, cols_of(core)] = (br_n[at, cols_of(core)].astype(F32) + g_got[at, :].astype(F32)).astype(BF16)

            blocks(width // 64, add)
            for d in (3, 2, 1, 0):
                out_br(d).start()
        spread.serve(t, finish)
        pl.when(i == 0)(tiny_open)
        pl.when(i == 1)(tiny_more)
        return carry

    mine = pl.ds(pl.multiple_of(core * seq, seq), seq)
    lane = lax.broadcasted_iota(jnp.int32, (64, 128), 1)
    swap_gd = remote(gd.at[1 - core], gd_in, v_send.at[0], v_recv.at[0], sibling)
    rows_gd = [
        remote(gd_all.at[0], gd_all.at[d], n_send.at[0, d - 1], n_recv.at[0, d - 1], {"row": row ^ d}) for d in (1, 2, 3)
    ]

    def tiny_open():
        for side in (0, 1):
            for e in range(4):
                at = slice(e * 64, (e + 1) * 64)
                gd[side, at, 0:64] = gate_grad[side, at, e * 64 : (e + 1) * 64]
                gd[side, at, 64:128] = gate_grad[side, at, 256 + e * 64 : 256 + (e + 1) * 64]
        swap_gd.start()

    def columns(parts, at):
        total = jnp.zeros((64, 128), F32)
        for n, part in enumerate(parts):
            total = total + jnp.where(lane == n, jnp.sum(part(at), axis=1, keepdims=True), 0.0)
        return total

    def tiny_more():
        swap_gd.wait()
        gd_all[0] = gd[core] + gd_in[...]
        for copy in rows_gd:
            copy.start()
        vec[...] = jnp.zeros(vec.shape, F32)
        for j in range(chan // 64):
            at = slice(j * 64, (j + 1) * 64)
            v = columns([lambda at, n=n: small[n, at, :] for n in range(8)], at)
            vec[0, :, at] = v.T[0:8, :]

    lax.fori_loop(0, LINE - 1, drain, 0)
    for j in range(block // 64):
        at = slice(j * 64, (j + 1) * 64)
        v = columns([lambda at: mix_part[at, :], lambda at: feed_part[at, :]], at)
        vec[1, :, at] = v.T[0:8, :]
    swap_vec = remote(vec, vec_in, v_send.at[1], v_recv.at[1], sibling)
    swap_vec.start()
    for k in range(PARTS):
        for d in (1, 2, 3):
            share(k, d).wait_send()
            piece = sums.at[k, z ^ d]
            remote(piece, piece, l_send.at[k, d - 1], l_recv.at[k, d - 1], at_line(z ^ d, core)).wait_recv()
        total = jnp.sum(jnp.sum(sums[k], axis=0), axis=0, keepdims=True)
        at = slice(k * PART, (k + 1) * PART)
        s1 = scale_one[:, at]
        coef[:, at] = s1 * s1 * s1 * (total / width)

    def last(i):
        at = rows_of(i, 16)
        v = dy[at, :] + (
            scale_one[0:1, :] * (gains[at, 8:9] * dn1[at, :]) - x_own[at, :].astype(F32) * coef[0:1, :]
        )
        dy[at, :] = v

    blocks(block // 16, last)
    back = remote(dy.at[rows_of(1 - core, half), :], input_grad.at[:, mine], r_send, r_recv, sibling)
    back.start()
    keep_in = pltpu.make_async_copy(dy.at[rows_of(core, half), :], input_grad.at[:, mine], d_own.at[3])
    keep_in.start()
    swap_vec.wait()
    vec_all[0] = vec[...] + vec_in[...]
    rows_vec = [
        remote(vec_all.at[0], vec_all.at[d], n_send.at[1, d - 1], n_recv.at[1, d - 1], {"row": row ^ d}) for d in (1, 2, 3)
    ]
    for copy in rows_vec:
        copy.start()
    spread.sent()
    gather.sent()
    for copy in rows_gd + rows_vec:
        copy.wait()
    for every, out in ((gd_all, tiny_g), (vec_all, tiny_v)):
        first, second = every[row % 2], every[1 - row % 2]
        third, fourth = every[2 + row % 2], every[3 - row % 2]
        out[...] = (first + second) + (third + fourth)
    for d in range(LINE):
        for out in f_out(d):
            out.wait()
    send_br().wait_send()
    send_m().wait_send()
    for d in (0, 1, 2, 3):
        out_br(d).wait()
        out_m(d).wait()
    for copy in (keep_in, back):
        copy.wait()


def last_kernel(
    f_sum, f_land, fd_sum, fd_land, g_sum, g_land, gm_sum, gm_land, result_in, grad_in, tiny_v, tiny_g, lambdas,
    s_b, s_r, s_m, s_g, s_u, s_d, result, input_grad, taps, offs, bias_r, bias_a, decay, mix, feed, retain, admit,
):
    lru, ff, half = s_b.shape[1], s_g.shape[0], mix.shape[1]

    def four(first, others):
        return first[...].astype(F32) + others[0].astype(F32) + (others[1].astype(F32) + others[2].astype(F32))

    v = four(f_sum, f_land)
    s_g[...] = v.T[:ff, :]
    s_u[...] = v.T[ff:, :]
    v = four(g_sum, g_land)
    s_b[...] = v[:, :lru]
    s_r[...] = v[:, lru:]
    s_d[...] = four(fd_sum, fd_land)
    result[...] = result_in[...]
    input_grad[...] = grad_in[...]

    @pl.when(pl.program_id(0) == 0)
    def _():
        core = place()[2]
        s_m[...] = four(gm_sum, gm_land)
        small = tiny_v[0, :, pl.ds(pl.multiple_of(core * lru, 128), lru)]
        taps[...] = small[0:4]
        offs[...] = small[4:5]
        bias_r[...] = small[5:6]
        bias_a[...] = small[6:7]
        decay[...] = small[7:8] * (8.0 * jax.nn.sigmoid(-lambdas[...]))
        gains = jnp.where(core == 0, tiny_v[1, :, 0:half], tiny_v[1, :, half : 2 * half])
        mix[...] = gains[0:1]
        feed[...] = gains[1:2]
        for e in range(retain.shape[0]):
            at = slice(e * 64, (e + 1) * 64)
            retain[e] = tiny_g[at, 0:64]
            admit[e] = tiny_g[at, 64:128]


ANY = pl.BlockSpec(memory_space=pl.ANY)
VM = pl.BlockSpec(memory_space=pltpu.VMEM)
DMA = pltpu.SemaphoreType.DMA
ROOM = 62 * 1024 * 1024


def shape(dims, kind):
    return jax.ShapeDtypeStruct(dims, kind)


def call(kernel, ins, outs, scratch, ident, name, flops):
    return pl.pallas_call(
        kernel,
        out_shape=[o[0] for o in outs],
        in_specs=ins,
        out_specs=[o[1] for o in outs],
        scratch_shapes=scratch,
        name=name,
        compiler_params=pltpu.CompilerParams(
            collective_id=ident, has_side_effects=True, vmem_limit_bytes=ROOM
        ),
        cost_estimate=pl.CostEstimate(flops=flops, bytes_accessed=40000000, transcendentals=0),
    )


def fast_body(
    inputs, segments, mix_gain, branch_weight, recur_weight, kernel, offsets, retain_weight, retain_bias,
    admit_weight, admit_bias, lambdas, merge_weight, feed_gain, gate_weight, up_weight, down_weight, cotangent,
):
    half, tokens = inputs.shape
    block, seq, width = 2 * half, tokens // 2, D
    lru, heads = branch_weight.shape[1], retain_weight.shape[0]
    chan = 2 * lru
    ff = gate_weight.shape[1]
    hid = 2 * ff
    rows = branch_weight.shape[0]
    cols = merge_weight.shape[1]
    gu_s = jnp.concatenate([gate_weight, up_weight], axis=1).T

    f_tok = lambda n, kind=F32: shape((n, seq), kind)
    padded = (shape((chan, 128 + seq), F32), ANY)
    state = [(f_tok(chan), ANY), padded, *[(f_tok(chan), ANY)] * 3, padded]
    line = [DMA((3,)), DMA((3,))]
    steps = [DMA((2, 3, PARTS)), DMA((2, 3, PARTS))]
    sums = [DMA((2, PARTS, LINE)), DMA((2, PARTS, LINE))]
    held = pltpu.VMEM((PARTS, LINE + 1, block, PART), BF16)
    own_low = pltpu.VMEM((PARTS, LINE, block, PART), BF16)
    tok = lambda n, kind=F32, lead=0: pltpu.VMEM((n, lead + seq), kind)
    one = lambda n, kind=F32, lead=0: pltpu.VMEM((n, lead + PART), kind)
    grad_gu, grad_d = (shape((width, 2 * ff), BF16), ANY), (shape((ff, width), BF16), ANY)
    low = lambda n, m: (shape((n, m), BF16), ANY)
    parted = lambda n: (shape((PARTS, n, PART), BF16), ANY)
    by_part = lambda n: pltpu.VMEM((PARTS, n, PART), BF16)

    (masks, par, gains, gates, coef, scale_one, scale_two, y, n1, q, x_own, g, b, p, u, r, i, h, result, dn2, _, _, f_own, f_got, fd_own, fd_got,
     br_n, m_n) = call(
        functools.partial(forward_kernel, width, EPS),
        [ANY] * 2 + [VM] * 13 + [ANY] * 2,
        [(shape((8, seq + 128), F32), VM), (shape((chan, 16), F32), VM), (shape((block, 16), F32), VM), (shape((2, lru, 2 * lru), BF16), VM),
         (f_tok(8), VM), (f_tok(8), VM), (f_tok(8), VM), (f_tok(block), ANY), parted(width), low(chan, seq), low(block, seq), parted(block)]
        + state + [low(half, tokens), (f_tok(block), ANY), low(2 * hid, seq), low(hid, seq), grad_gu, grad_gu, grad_d, grad_d,
                   low(width, 2 * chan), low(chan, width)],
        [pltpu.VMEM((LINE, 8, seq), F32), pltpu.VMEM((PARTS, LINE, 8, PART), F32), pltpu.VMEM((PARTS, LINE, 8, PART), F32),
         pltpu.VMEM((16, lru), F32), pltpu.VMEM((2 * lru, rows), BF16), pltpu.VMEM((rows, 2 * lru), BF16), pltpu.VMEM((cols, lru), BF16),
         pltpu.VMEM((2, 16, lru), F32), pltpu.VMEM((2, 2) + retain_weight.shape, F32), pltpu.VMEM((2, 2 * lru, lru), BF16),
         pltpu.VMEM((2, 2 * lru, lru), BF16), by_part(width), by_part(width),
         by_part(width), tok(block, BF16), tok(block), one(block), one(chan, BF16),
         one(chan, F32, 128), one(chan, F32, 128), one(max(5 * chan, 3 * hid)), one(chan, BF16), one(chan, BF16),
         own_low, held, held, held, pltpu.VMEM((2 * hid, width), BF16), pltpu.VMEM((width, 2 * hid), BF16),
         pltpu.VMEM((hid, width), BF16), pltpu.VMEM((width, hid), BF16), one(hid, BF16), one(2 * hid, BF16),
         DMA((5,)), DMA((5,)), DMA((5,)), DMA((PARTS,)), DMA((PARTS,)), DMA((PARTS,))] + line + [DMA((PARTS, 3)), DMA((PARTS, 3))] * 2 + steps * 3 + sums * 3
        + [DMA((7, 7)), DMA((7, 7)), DMA((7,)), DMA((7,)), DMA((11,)), DMA((4,)), DMA((4,)), DMA((4,))],
        0, "forward", 50 * 10**9,
    )(inputs, cotangent, segments[None, :], kernel, offsets[None, :], retain_bias[None, :], admit_bias[None, :],
      lambdas[None, :], mix_gain[None, :], feed_gain[None, :], retain_weight, admit_weight, branch_weight, recur_weight,
      merge_weight, gu_s, down_weight)

    late = seq // LATE
    pair = lambda lead=0: pltpu.VMEM((2, chan, lead + LATE), F32)
    one = lambda n, kind=F32, lead=0: pltpu.VMEM((n, lead + LATE), kind)
    steps = [DMA((2, 3, late)), DMA((2, 3, late))]
    sums = [DMA((2, late, LINE)), DMA((2, late, LINE))]
    held = pltpu.VMEM((late, LINE + 1, block, LATE), BF16)
    own_low = pltpu.VMEM((late, LINE, block, LATE), BF16)
    land = lambda n, m: ((shape((n, m), BF16), ANY), (shape((3, n, m), BF16), ANY))
    input_grad, tiny_v, tiny_g, *sums_of = call(
        functools.partial(back_kernel, width),
        [VM] + [ANY] * 2 + [VM] * 8 + [ANY] * 14,
        [(shape((half, tokens), F32), ANY), (shape((2, 8, chan), F32), VM),
         (shape((lru, 128), F32), VM), *land(cols, 2 * ff), *land(ff, cols), *land(cols, 2 * lru), *land(lru, cols)],
        [pltpu.VMEM((late, LINE, 8, LATE), F32), pltpu.VMEM((8, seq), F32),
         pltpu.VMEM((chan, width), BF16), pltpu.VMEM((width, 2 * chan), BF16),
         pair(), pair(128), pair(), pair(), pair(), pair(128), pltpu.VMEM((late, width, LATE), BF16), tok(2 * chan, BF16),
         tok(block), tok(block), one(chan), one(chan, F32, 128), one(2 * chan, BF16),
         one(chan), one(chan), pltpu.VMEM((chan, 128), F32), own_low, held,
         tok(chan, BF16), by_part(width), pltpu.VMEM((4, cols, 2 * ff), BF16), pltpu.VMEM((cols, 2 * ff), BF16),
         pltpu.VMEM((4, ff, cols), BF16), pltpu.VMEM((ff, cols), BF16),
         pltpu.VMEM((block, 128), F32), pltpu.VMEM((block, 128), F32), pltpu.VMEM((8, chan, 128), F32),
         pltpu.VMEM((2, lru, 2 * lru), F32), by_part(block), pltpu.VMEM((width, 2 * lru), BF16),
         pltpu.VMEM((lru, width), BF16), pltpu.VMEM((2, 8, chan), F32), pltpu.VMEM((2, 8, chan), F32),
         pltpu.VMEM((4, 2, 8, chan), F32), pltpu.VMEM((2, lru, 128), F32), pltpu.VMEM((lru, 128), F32),
         pltpu.VMEM((4, lru, 128), F32), DMA((7,)), DMA((6, 2))] + [DMA((late, 3)), DMA((late, 3))] + steps + sums
        + [DMA, DMA, DMA((2, 2)), DMA((2, LINE)), DMA((2, LINE)), DMA((2,)), DMA((2,)), DMA((4,))]
        + [DMA((2, 3)), DMA((2, 3)), DMA((2, 3)), DMA((2, 3)), DMA((2,)), DMA((2,))],
        2, "mix_backward", 10 * 10**9,
    )(y, dn2, g, x_own, scale_two, scale_one, coef, gains, masks, par, gates, m_n, br_n, b, p, u, r, i, h,
      q, n1, f_own, f_got, fd_own, fd_got)

    line_of = shape((1, lru), F32)
    cuts = 3
    rows_in = lambda *dims: pl.BlockSpec((dims[0] // cuts,) + dims[1:], lambda n: (n,) + (0,) * (len(dims) - 1))
    three = lambda *dims: pl.BlockSpec((3, dims[0] // cuts, dims[1]), lambda n: (0, n, 0))
    still = lambda *dims: pl.BlockSpec(dims, lambda n: (0,) * len(dims))
    sizes = ((cols, 2 * ff), (ff, cols), (cols, 2 * lru), (lru, cols))
    big = ((cols, lru), (cols, lru), (lru, cols), (ff, cols), (ff, cols), (ff, cols))
    across = pl.BlockSpec((ff, cols // cuts), lambda n: (0, n))
    flat = ((4, lru),) + ((1, lru),) * 4 + ((1, half),) * 2 + ((heads, 64, 64),) * 2
    s_b, s_r, s_m, s_g, s_u, s_d, result, input_grad, taps, offs, bias_r, bias_a, decay, mix, feed, retain, admit = pl.pallas_call(
        last_kernel,
        grid=(cuts,),
        out_shape=[shape(d, F32) for d in big] + [shape((half, tokens), BF16), shape((half, tokens), F32)]
        + [shape(d, F32) for d in flat],
        in_specs=[spec(*d) for d in sizes[:3] for spec in (rows_in, three)] + [still(lru, cols), still(3, lru, cols)]
        + [rows_in(half, tokens)] * 2
        + [still(2, 8, chan), still(lru, 128), still(1, lru)],
        out_specs=[rows_in(cols, lru)] * 2 + [still(lru, cols)] + [across] * 2 + [rows_in(ff, cols)] + [rows_in(half, tokens)] * 2 + [still(*d) for d in flat],
        name="last_sums",
        compiler_params=pltpu.CompilerParams(vmem_limit_bytes=ROOM),
    )(*sums_of, result, input_grad, tiny_v, tiny_g, lambdas[None, :])
    return (
        result,
        input_grad,
        mix[0],
        s_b,
        s_r,
        taps,
        offs[0],
        retain,
        bias_r[0],
        admit,
        bias_a[0],
        decay[0],
        s_m,
        feed[0],
        s_g.T,
        s_u.T,
        s_d,
    )


def suits(mesh, args):
    return (
        dict(mesh.shape) == {"row": 4, "col": 8}
        and args[0].shape == (D, 8 * SEQ)
        and args[3].shape == (D, 2048)
        and args[14].shape == (D, 4608)
        and args[7].shape == (32, 64, 64)
    )


def solution(mesh):
    in_specs = (
        P("col", "row"),
        P("row"),
        P("col"),
        P("row", "col"),
        P("row", "col"),
        P(None, "col"),
        P("col"),
        P("col", None, None),
        P("col"),
        P("col", None, None),
        P("col"),
        P("col"),
        P("col", "row"),
        P("col"),
        P("row", "col"),
        P("row", "col"),
        P("col", "row"),
        P("col", "row"),
    )
    out_specs = (
        P("col", "row"),
        P("col", "row"),
        P("col"),
        P("row", "col"),
        P("row", "col"),
        P(None, "col"),
        P("col"),
        P("col", None, None),
        P("col"),
        P("col", None, None),
        P("col"),
        P("col"),
        P("col", "row"),
        P("col"),
        P("row", "col"),
        P("row", "col"),
        P("col", "row"),
    )
    def run(*args):
        chosen = fast_body if suits(mesh, args) else body
        return jax.shard_map(
            chosen, mesh=mesh, in_specs=in_specs, out_specs=out_specs, check_vma=False
        )(*args)

    return run
```

```python
import functools

import jax
import jax.numpy as jnp
from jax import lax
from jax.experimental import pallas as pl
from jax.experimental.pallas import tpu as pltpu
from jax.sharding import PartitionSpec as P

D = 1536
SEQ = 1024
MICRO = 2


HIGH = lax.Precision.HIGHEST
EPS = 1e-06
POWER = 8.0
FLOOR = 0.01


def combine(earlier, later):
    first_a, first_b = earlier
    second_a, second_b = later
    return (first_a * second_a, second_a * first_b + second_b)


def mixer(
    branch_pre,
    lru_pre,
    segs,
    kernel,
    offsets,
    retain_weight,
    retain_bias,
    admit_weight,
    admit_bias,
    lambdas,
):
    length = lru_pre.shape[0]
    channels = lru_pre.shape[1]
    conv = offsets + kernel[0] * lru_pre
    for lag in range(1, kernel.shape[0]):
        shifted = jnp.concatenate(
            [jnp.zeros((lag, channels), lru_pre.dtype), lru_pre[:-lag]], axis=0
        )
        prior = jnp.concatenate([jnp.full((lag,), -1, jnp.int32), segs[:-lag]])
        keep = (prior == segs).astype(lru_pre.dtype)
        conv = conv + kernel[lag] * shifted * keep[:, None]
    heads = retain_weight.shape[0]
    blocks = conv.reshape(length, heads, channels // heads)
    retain = jax.nn.sigmoid(
        jnp.einsum("thi,hij->thj", blocks, retain_weight, precision=HIGH).reshape(length, channels)
        + retain_bias
    )
    admit = jax.nn.sigmoid(
        jnp.einsum("thi,hij->thj", blocks, admit_weight, precision=HIGH).reshape(length, channels)
        + admit_bias
    )
    decay = jnp.exp(-POWER * retain * jax.nn.softplus(-lambdas))
    factor = jnp.sqrt(1.0 - decay * decay + FLOOR)
    starts = jnp.concatenate([jnp.ones((1,), bool), segs[1:] != segs[:-1]])
    decay = jnp.where(starts[:, None], 0.0, decay)
    factor = jnp.where(starts[:, None], 1.0, factor)
    _, state = lax.associative_scan(combine, (decay, factor * admit * conv), axis=0)
    return jax.nn.gelu(branch_pre) * state


def geglu(gate, upper):
    return jax.nn.gelu(gate) * upper


def contract_rows(left, right):
    return lax.dot_general(
        left, right, (((0,), (0,)), ((), ())), preferred_element_type=jnp.float32
    )


def contract_cols(left, right):
    return lax.dot_general(
        left, right, (((1,), (1,)), ((), ())), preferred_element_type=jnp.float32
    )


def contract_cross(left, right):
    return lax.dot_general(
        left, right, (((0,), (1,)), ((), ())), preferred_element_type=jnp.float32
    )


def norm_forward(resid, gain):
    total = lax.psum(jnp.sum(resid * resid, axis=0), "col")
    scale = lax.rsqrt(total / D + EPS)[None, :]
    return (scale, (resid * scale * gain[:, None]).astype(jnp.bfloat16))


def norm_backward(resid, scale, gain, grad_normed):
    weighted = grad_normed * gain[:, None]
    total = lax.psum(jnp.sum(weighted * resid, axis=0), "col")
    grad_resid = scale * weighted - resid * (scale * scale * scale) * (total / D)[None, :]
    grad_gain = jnp.sum(grad_normed * resid * scale, axis=1)
    return (grad_resid, grad_gain)


def gather_features(normed):
    return lax.all_gather(normed, "col", axis=0, tiled=True)


def gather_cotangent(grad):
    return lax.all_gather(grad, "col", axis=0, tiled=True)


def spread_sum(term):
    return lax.psum_scatter(
        term.astype(jnp.bfloat16), "col", scatter_dimension=0, tiled=True
    ).astype(jnp.float32)


def back_sum(term):
    return spread_sum(term)


def merge_term(whole_merge, mixed_low):
    return spread_sum(contract_cross(whole_merge, mixed_low))


def weight_grads(normed, grad_joined):
    return jnp.dot(
        normed,
        grad_joined,
        preferred_element_type=jnp.float32,
    )


def row_sum(total, axis):
    return lax.psum_scatter(
        total.astype(jnp.bfloat16), "row", scatter_dimension=axis, tiled=True
    ).astype(jnp.float32)


def body(
    inputs,
    segments,
    mix_gain,
    branch_weight,
    recur_weight,
    kernel,
    offsets,
    retain_weight,
    retain_bias,
    admit_weight,
    admit_bias,
    lambdas,
    merge_weight,
    feed_gain,
    gate_weight,
    up_weight,
    down_weight,
    cotangent,
):
    lru_cols = branch_weight.shape[1]
    feed_cols = gate_weight.shape[1]
    mixer_params = (kernel, offsets, retain_weight, retain_bias, admit_weight, admit_bias, lambdas)
    acc_branch = jnp.zeros((D, lru_cols), jnp.float32)
    acc_recur = jnp.zeros((D, lru_cols), jnp.float32)
    acc_gate = jnp.zeros((D, feed_cols), jnp.float32)
    acc_up = jnp.zeros((D, feed_cols), jnp.float32)
    acc_merge = jnp.zeros((lru_cols, D), jnp.float32)
    acc_down = jnp.zeros((feed_cols, D), jnp.float32)
    acc_small = tuple((jnp.zeros_like(p) for p in mixer_params))
    acc_mix = jnp.zeros_like(mix_gain)
    acc_feed = jnp.zeros_like(feed_gain)
    outputs = []
    in_grads = []
    for batch in range(MICRO):
        lower = batch * SEQ
        resid_in = inputs[:, lower : lower + SEQ].astype(jnp.float32)
        grad_out = cotangent[:, lower : lower + SEQ].astype(jnp.float32)
        segs = segments[lower : lower + SEQ]
        whole_branch, whole_recur, whole_gate, whole_up = (
            lax.all_gather(branch_weight, "row", axis=0, tiled=True),
            lax.all_gather(recur_weight, "row", axis=0, tiled=True),
            lax.all_gather(gate_weight, "row", axis=0, tiled=True),
            lax.all_gather(up_weight, "row", axis=0, tiled=True),
        )
        whole_merge, whole_down = (
            lax.all_gather(merge_weight, "row", axis=1, tiled=True),
            lax.all_gather(down_weight, "row", axis=1, tiled=True),
        )
        scale_one, normed_one = norm_forward(resid_in, mix_gain)
        full_one = gather_features(normed_one)
        branch_pre = contract_rows(full_one, whole_branch)
        lru_pre = contract_rows(full_one, whole_recur)

        def local_mixer(bpre, lpre, kern, offs, rweight, rbias, aweight, abias, lams):
            return mixer(bpre, lpre, segs, kern, offs, rweight, rbias, aweight, abias, lams)

        mixed, mixer_pull = jax.vjp(local_mixer, branch_pre, lru_pre, *mixer_params)
        mixed_low = mixed.astype(jnp.bfloat16)
        resid_mid = resid_in + merge_term(whole_merge, mixed_low)
        scale_two, normed_two = norm_forward(resid_mid, feed_gain)
        full_two = gather_features(normed_two)
        gate = contract_rows(full_two, whole_gate)
        upper = contract_rows(full_two, whole_up)
        hidden, geglu_pull = jax.vjp(geglu, gate, upper)
        hidden_low = hidden.astype(jnp.bfloat16)
        result = resid_mid + spread_sum(contract_cross(whole_down, hidden_low))
        outputs.append(result.astype(jnp.bfloat16))
        grad_full = gather_cotangent(grad_out.astype(jnp.bfloat16))
        acc_down = acc_down + contract_cross(hidden_low, grad_full)
        grad_gate, grad_upper = geglu_pull(contract_cross(grad_full, whole_down))
        grad_gate = grad_gate.astype(jnp.bfloat16)
        grad_upper = grad_upper.astype(jnp.bfloat16)
        feed_joined = weight_grads(full_two, jnp.concatenate([grad_gate, grad_upper], axis=1))
        acc_gate = acc_gate + feed_joined[:, :feed_cols]
        acc_up = acc_up + feed_joined[:, feed_cols:]
        grad_normed_two = back_sum(
            contract_cols(whole_gate, grad_gate) + contract_cols(whole_up, grad_upper)
        )
        grad_mid_norm, feed_part = norm_backward(resid_mid, scale_two, feed_gain, grad_normed_two)
        acc_feed = acc_feed + feed_part
        grad_mid = grad_out + grad_mid_norm
        grad_mid_full = gather_cotangent(grad_mid.astype(jnp.bfloat16))
        acc_merge = acc_merge + contract_cross(mixed_low, grad_mid_full)
        pulled = mixer_pull(contract_cross(grad_mid_full, whole_merge))
        grad_branch = pulled[0].astype(jnp.bfloat16)
        grad_lru = pulled[1].astype(jnp.bfloat16)
        acc_small = tuple((total + part for total, part in zip(acc_small, pulled[2:])))
        branch_joined = weight_grads(full_one, jnp.concatenate([grad_branch, grad_lru], axis=1))
        acc_branch = acc_branch + branch_joined[:, :lru_cols]
        acc_recur = acc_recur + branch_joined[:, lru_cols:]
        grad_normed_one = back_sum(
            contract_cols(whole_branch, grad_branch) + contract_cols(whole_recur, grad_lru)
        )
        grad_in_norm, mix_part = norm_backward(resid_in, scale_one, mix_gain, grad_normed_one)
        acc_mix = acc_mix + mix_part
        in_grads.append(grad_mid + grad_in_norm)
    sum_branch, sum_recur, sum_gate, sum_up = (
        row_sum(acc_branch, 0),
        row_sum(acc_recur, 0),
        row_sum(acc_gate, 0),
        row_sum(acc_up, 0),
    )
    sum_merge, sum_down = (
        row_sum(acc_merge, 1),
        row_sum(acc_down, 1),
    )
    summed = lax.psum(
        (
            acc_mix,
            acc_feed,
            acc_small[0],
            acc_small[1],
            acc_small[2],
            acc_small[3],
            acc_small[4],
            acc_small[5],
            acc_small[6],
        ),
        "row",
    )
    result_all = jnp.concatenate(outputs, axis=1)
    input_grad = jnp.concatenate(in_grads, axis=1)
    return (
        result_all,
        input_grad,
        summed[0],
        sum_branch,
        sum_recur,
        summed[2],
        summed[3],
        summed[4],
        summed[5],
        summed[6],
        summed[7],
        summed[8],
        sum_merge,
        summed[1],
        sum_gate,
        sum_up,
        sum_down,
    )


MESH = pl.DeviceIdType.MESH
F32 = jnp.float32
BF16 = jnp.bfloat16
LINE = 4
PART = 128
PARTS = 8
LATE = 256
GELU_A = 0.7978845608028654
GELU_B = 0.044715


def place():
    row, col = lax.axis_index("row"), lax.axis_index("col")
    return row, col // 2, col % 2


def at_line(z, core):
    return {"col": 2 * z + core}


def lanes(part):
    return pl.ds(pl.multiple_of(part * PART, PART), PART)


def rows_of(index, size):
    return pl.ds(pl.multiple_of(index * size, 16), size)


def dot(a, b):
    return lax.dot_general(a, b, (((1,), (0,)), ((), ())), preferred_element_type=F32)


def dot_nt(a, b):
    return lax.dot_general(a, b, (((1,), (1,)), ((), ())), preferred_element_type=F32)


def greet(row, z, core, rows, line):
    barrier = pltpu.get_barrier_semaphore()
    peers = [{"col": 2 * z + (1 - core)}]
    if rows:
        peers += [{"row": row ^ d} for d in (1, 2, 3)]
    if line:
        peers += [at_line(z ^ d, core) for d in (1, 2, 3)]
    for peer in peers:
        pl.semaphore_signal(barrier, inc=1, device_id=peer, device_id_type=MESH)
    return functools.partial(pl.semaphore_wait, barrier, len(peers))


def remote(src, dst, send, recv, peer):
    return pltpu.make_async_remote_copy(
        src_ref=src, dst_ref=dst, send_sem=send, recv_sem=recv, device_id=peer, device_id_type=MESH
    )


class Gather:
    def __init__(self, ref, send, recv, z, core, block, back=False):
        self.parts = ref.shape[0]
        self.ref, self.sems, self.z, self.core = ref, (send, recv), z, core
        self.block, self.back = block, back

    def copy(self, way, hop, step, owner, incoming=False):
        part = self.parts - 1 - step if self.back else step
        piece = self.ref.at[part, rows_of(owner, self.block), :]
        peer = at_line(self.z + (1 if (way == 0) != incoming else -1), self.core)
        return remote(piece, piece, self.sems[0].at[way, hop, step], self.sems[1].at[way, hop, step], peer)

    def each(self, hop, act, incoming):
        z = self.z
        if incoming:
            cases = ((0, z - 1 - hop >= 0, z - 1 - hop), (1, z + 1 + hop < LINE, z + 1 + hop))
        else:
            cases = (
                (0, (z >= hop) & (z < LINE - 1), z - hop),
                (1, (z + hop < LINE) & (z >= 1), z + hop),
            )
        for way, here, owner in cases:
            pl.when(here)(functools.partial(act, way, owner))

    def send(self, hop, step):
        self.each(hop, lambda way, owner: self.copy(way, hop, step, owner).start(), False)

    def arrive(self, hop, step):
        self.each(hop, lambda way, owner: self.copy(way, hop, step, owner, True).wait_recv(), True)

    def forward(self, hop, step):
        self.arrive(hop - 1, step)
        self.send(hop, step)

    def sent(self):
        def one(step, carry):
            for hop in range(LINE - 1):
                self.each(hop, lambda way, owner: self.copy(way, hop, step, owner).wait_send(), False)
            return carry

        lax.fori_loop(0, self.parts, one, 0)

    def middle(self, step, ahead=1):
        for hop in (2, 1, 0):
            later = step + ahead + 2 - hop
            act = self.forward if hop else self.send
            pl.when(later < self.parts)(functools.partial(act, hop, later))


class Spread:
    def __init__(self, own, held, send, recv, z, core):
        self.parts = held.shape[0]
        self.own, self.held, self.sems, self.z, self.core = own, held, (send, recv), z, core

    def copy(self, way, step, hop):
        slot = hop if way == 0 else LINE - hop
        there = slot - 1 if way == 0 else slot + 1
        peer = at_line(self.z + (1 if way == 0 else -1), self.core)
        return remote(
            self.held.at[step, slot],
            self.held.at[step, there],
            self.sems[0].at[way, step, hop],
            self.sems[1].at[way, step, hop - 1],
            peer,
        )

    def landed(self, way, step, hop):
        slot = hop if way == 0 else LINE - hop
        piece = self.held.at[step, slot]
        peer = at_line(self.z + (-1 if way == 0 else 1), self.core)
        remote(piece, piece, self.sems[0].at[way, step, hop], self.sems[1].at[way, step, hop], peer).wait_recv()

    def push(self, way, step, first):
        z = self.z

        def one(i, carry):
            hop = LINE - 1 - i
            owner = z + hop if way == 0 else z - hop
            slot = hop if way == 0 else LINE - hop

            @pl.when((owner >= 0) & (owner < LINE))
            def _():
                @pl.when(first)
                def _():
                    self.held[step, slot] = self.own(step, owner)[...].astype(BF16)

                @pl.when(jnp.logical_not(first))
                def _():
                    self.landed(way, step, hop)
                    total = self.own(step, owner)[...].astype(F32) + self.held[step, slot].astype(F32)
                    self.held[step, slot] = total.astype(BF16)

                self.copy(way, step, hop).start()

            return carry

        lax.fori_loop(0, LINE - 1, one, 0)

    def serve(self, t, finish):
        z = self.z
        step = t - (LINE - 1)

        @pl.when((step >= 0) & (step < self.parts))
        def _():
            @pl.when(z == 0)
            def _():
                self.landed(1, step, 0)
                finish(step, lambda a, n: self.mine(step, a, n) + self.got(step, LINE, a, n))

            @pl.when(z == LINE - 1)
            def _():
                self.landed(0, step, 0)
                finish(step, lambda a, n: self.mine(step, a, n) + self.got(step, 0, a, n))

            @pl.when((z > 0) & (z < LINE - 1))
            def _():
                self.landed(0, step, 0)
                self.landed(1, step, 0)
                finish(
                    step,
                    lambda a, n: self.mine(step, a, n) + (self.got(step, 0, a, n) + self.got(step, LINE, a, n)),
                )

        for way, late, turn in ((1, LINE - 1 - z, z < 2), (0, z, z >= 0), (1, LINE - 1 - z, z >= 2)):
            step = t - late
            pl.when((step >= 0) & (step < self.parts) & turn)(functools.partial(self.push, way, step, late == 0))

    def mine(self, step, start, size):
        return self.own(step, self.z)[pl.ds(start, size), :].astype(F32)

    def got(self, step, slot, start, size):
        return self.held[step, slot, pl.ds(start, size)].astype(F32)

    def sent(self):
        z = self.z

        def one(step, carry):
            for way in (0, 1):
                for hop in range(1, LINE):
                    owner = z + hop if way == 0 else z - hop

                    @pl.when((owner >= 0) & (owner < LINE))
                    def _():
                        self.copy(way, step, hop).wait_send()

            return carry

        lax.fori_loop(0, self.parts, one, 0)


def share_line(ref, send, recv, z, core):
    copies = [
        remote(ref.at[z], ref.at[z], send.at[d - 1], recv.at[d - 1], at_line(z ^ d, core)) for d in (1, 2, 3)
    ]
    for copy in copies:
        copy.start()
    for d in (1, 2, 3):
        piece = ref.at[z ^ d]
        remote(piece, piece, send.at[d - 1], recv.at[d - 1], at_line(z ^ d, core)).wait_recv()
    for copy in copies:
        copy.wait_send()


class Weights:
    def __init__(self, src, dst, send, recv, own, row, z, core, turned, stride=0, start=0):
        self.src, self.dst, self.send, self.recv, self.own = src, dst, send, recv, own
        self.row, self.core, self.turned = row, core, turned
        self.stride, self.first = stride or src.shape[0], start
        self.sibling = {"col": 2 * z + (1 - core)}

    def spot(self, row, core):
        down, right = (row, core) if self.turned else (core, row)
        rows, cols = self.src.shape
        at = pl.ds(pl.multiple_of(down * self.stride + self.first, 16), rows)
        return self.dst.at[at, pl.ds(pl.multiple_of(right * cols, 128), cols)]

    def to_row(self, d):
        return remote(
            self.src, self.spot(self.row, self.core), self.send.at[d], self.recv.at[d], {"row": self.row ^ d}
        )

    def to_sibling(self, d):
        if d == 0:
            return remote(
                self.src, self.spot(self.row, self.core), self.send.at[0], self.recv.at[0], self.sibling
            )
        piece = self.spot(self.row ^ d, self.core)
        return remote(piece, piece, self.send.at[3 + d], self.recv.at[3 + d], self.sibling)

    def local(self):
        return pltpu.make_async_copy(self.src, self.spot(self.row, self.core), self.own)

    def start(self):
        for d in (1, 2, 3):
            self.to_row(d).start()
        self.to_sibling(0).start()
        self.local().start()

    def forward(self):
        for d in (1, 2, 3):
            piece = self.spot(self.row ^ d, self.core)
            remote(piece, piece, self.send.at[d], self.recv.at[d], {"row": self.row ^ d}).wait_recv()
            self.to_sibling(d).start()

    def finish(self):
        self.local().wait()
        for d in (0, 1, 2, 3):
            piece = self.spot(self.row ^ d, 1 - self.core)
            sem = 0 if d == 0 else 3 + d
            remote(piece, piece, self.send.at[sem], self.recv.at[sem], self.sibling).wait_recv()

    def sent(self):
        for d in (1, 2, 3):
            self.to_row(d).wait_send()
            self.to_sibling(d).wait_send()
        self.to_sibling(0).wait_send()


def gelu_parts(b):
    t = jnp.tanh(GELU_A * (b + GELU_B * (b * b * b)))
    half = 0.5 + 0.5 * t
    slope = half + (0.5 * b) * (1.0 - t * t) * (GELU_A + (3.0 * GELU_A * GELU_B) * (b * b))
    return b * half, slope


def eight(v):
    return jnp.sum(v.reshape(v.shape[0] // 8, 8, v.shape[1]), axis=0)


def fold(v):
    total = v[:, 0:128]
    for j in range(1, v.shape[1] // 128):
        total = total + v[:, j * 128 : (j + 1) * 128]
    return total


def tokens_of(ref, piece):
    return jnp.concatenate([ref[k, piece, :] for k in range(ref.shape[0])], axis=1)


def blocks(count, body):
    def one(i, carry):
        body(i)
        return carry

    lax.fori_loop(0, count, one, 0)


def scale_of(ref, eps, width):
    total = jnp.sum(jnp.sum(ref[...], axis=0), axis=0, keepdims=True)
    return lax.rsqrt(total / width + eps)


def forward_kernel(
    width, eps,
    x_in, g_in, segs, taps, offs, bias_r, bias_a, decay, mix, late, retain, admit, branch, recur, mn_s, gu_s, d_s,
    masks, par, gains, gates, coef, scale, scale_two, y_out, n1_out, q_out, x_out, g_out, b_out, p_out, u_out, r_out, i_out, h_out,
    result, dn2_out, dev_h, z_h, g_own, g_got, gd_own, gd_got, br_n, m_n,
    sums, sums2, sums3, vec, br_s, brn_s, m_s, vec_all, block_all, gates_hi, gates_lo, normed, normed2, go, x_own, y, dn2, q_c, p_s, h_s, room, uh, ul,
    own, held, held_n, held_o, gu, gun, down, dt, zs, dev,
    x_send, x_recv, x_loc, i_send, i_recv, i_loc, l_send, l_recv, n_send, n_recv, c_send, c_recv, g_send, g_recv, e_send, e_recv, f_send, f_recv,
    s_send, s_recv, t_send, t_recv, o_send, o_recv, w_send, w_recv, w_own, k_sem, v_sem, d_send, d_recv, d_own,
):
    row, z, core = place()
    block, seq = y.shape
    half = x_in.shape[0]
    chan = p_s.shape[0]
    hid = zs.shape[0]
    b_s, u_s, r_s, i_s, a_c = [room.at[n * chan : (n + 1) * chan, :] for n in range(5)]
    ev, dz = room.at[0 : 2 * hid, :], room.at[2 * hid : 3 * hid, :]
    hh = hid // 2
    hc = chan // 2
    sibling = {"col": 2 * z + (1 - core)}
    met = greet(row, z, core, True, True)
    br_s[0:hc, :] = branch[...].T
    br_s[hc:, :] = recur[...].T
    m_s[...] = mn_s[...].T
    br, mt = gun.at[0 : 2 * chan, 0:width], dt.at[:, 0:chan]
    wide = br_s.shape[0]
    recur_s, branch_s = br_s.at[wide // 2 :, :], br_s.at[0 : wide // 2, :]
    weights = [
        Weights(src, dst, w_send.at[n], w_recv.at[n], w_own.at[n], row, z, core, n in (2, 5), stride, start)
        for n, (src, dst, stride, start) in enumerate(
            (
                (recur_s, br, hc, 0),
                (branch_s, br, hc, chan),
                (m_s, mt, 0, 0),
                (gu_s, gu, 0, 0),
                (d_s, down, 0, 0),
                (brn_s, br_n, 0, 0),
                (mn_s, m_n, 0, 0),
            )
        )
    ]
    mine = pl.ds(pl.multiple_of(core * seq, seq), seq)
    other = pl.ds(pl.multiple_of((1 - core) * seq, seq), seq)
    inner = pl.ds(pl.multiple_of(z * block + core * half, 16), half)
    outer = rows_of(core, half)
    swaps = [
        remote(x_in.at[:, other], x_own.at[outer, :], x_send.at[0], x_recv.at[0], sibling),
        pltpu.make_async_copy(x_in.at[:, mine], x_own.at[outer, :], x_loc.at[0]),
    ]
    for k in range(PARTS):
        theirs, ours = [pl.ds(pl.multiple_of(c * seq + k * PART, 128), PART) for c in (1 - core, core)]
        swaps.append(remote(g_in.at[:, theirs], go.at[k, inner, :], i_send.at[k], i_recv.at[k], sibling))
        swaps.append(pltpu.make_async_copy(g_in.at[:, ours], go.at[k, inner, :], i_loc.at[k]))
    vec[...] = jnp.zeros(vec.shape, F32)
    vec[0:4, :] = taps[...]
    for n, one_row in enumerate((offs, bias_r, bias_a)):
        vec[4 + n : 5 + n, :] = one_row[...]
    rate = -decay[...]
    vec[7:8, :] = 8.0 * (jnp.maximum(rate, 0.0) + jnp.log1p(jnp.exp(-jnp.abs(rate))))
    vec[8:9, 0:half] = mix[...]
    vec[9:10, 0:half] = late[...]
    brn_s[:, 0:hc] = branch[...]
    brn_s[:, hc:] = recur[...]
    met()
    for w in weights[:3]:
        w.start()
    for swap in swaps:
        swap.start()
    trades = []
    for n, (src, dst) in enumerate(
        ((vec, vec_all.at[core]), (retain, block_all.at[core, 0]), (admit, block_all.at[core, 1]))
    ):
        trades.append(remote(src, dst, x_send.at[2 + n], x_recv.at[2 + n], sibling))
        trades.append(pltpu.make_async_copy(src, dst, x_loc.at[2 + n]))
    for trade in trades:
        trade.start()
    for swap in swaps + trades:
        swap.wait()
    flushes = [
        pltpu.make_async_copy(x_own, x_out, v_sem.at[0]),
        pltpu.make_async_copy(go.at[:, rows_of(z, block), :], g_out, v_sem.at[1]),
    ]
    for flush in flushes:
        flush.start()
    gather = Gather(normed, g_send, g_recv, z, core, block)
    gather_go = Gather(go, e_send, e_recv, z, core, block)
    gather_two = Gather(normed2, f_send, f_recv, z, core, block)
    shares = lambda k, s: own.at[k, s]
    shares_o = lambda k, s: normed.at[k, rows_of(s, block), :]
    spread = Spread(shares, held, s_send, s_recv, z, core)
    spread_n = Spread(shares, held_n, t_send, t_recv, z, core)
    spread_o = Spread(shares_o, held_o, o_send, o_recv, z, core)
    res = x_own
    gather_go.send(0, 0)
    gather_go.send(0, 1)
    for c in (0, 1):
        at = slice(c * hc, (c + 1) * hc)
        par[at, :] = vec_all[c].T
        gains[c * half : (c + 1) * half, :] = par[c * hc : c * hc + half, :]

    sums[z] = jnp.zeros(sums.shape[1:], F32)

    def squares(i):
        v = x_own[rows_of(i, 16), :].astype(F32)
        v = v * v
        sums[z] += v[:8] + v[8:]

    blocks(block // 16, squares)
    share_line(sums, l_send, l_recv, z, core)
    scale[...] = jnp.broadcast_to(scale_of(sums, eps, width), scale.shape)

    def norm(i):
        v = x_own[rows_of(i, 16), :].astype(F32) * scale[0:1, :] * gains[rows_of(i, 16), 8:9]
        v = v.astype(BF16)
        for k in range(PARTS):
            normed[k, pl.ds(pl.multiple_of(z * block + i * 16, 16), 16), :] = v[:, k * PART : (k + 1) * PART]

    blocks(block // 16, norm)
    gather.send(0, 0)
    p_s[:, PART:] = jnp.zeros((chan, 128), F32)
    h_s[:, PART:] = jnp.zeros((chan, 128), F32)
    pads = [
        pltpu.make_async_copy(src.at[:, PART:], out.at[:, 0:128], v_sem.at[2 + n])
        for n, (src, out) in enumerate(((p_s, p_out), (h_s, h_out)))
    ]
    for pad in pads:
        pad.start()
    gates[...] = jnp.zeros(gates.shape, BF16)
    gates_hi[...] = jnp.zeros(gates_hi.shape, BF16)
    gates_lo[...] = jnp.zeros(gates_lo.shape, BF16)
    per = retain.shape[0]
    tap = retain.shape[1]
    for c in (0, 1):
        for n in (0, 1):
            for e in range(per):
                w = block_all[c, n, e]
                at, far = slice(e * tap, (e + 1) * tap), slice(n * hc + e * tap, n * hc + (e + 1) * tap)
                gates[c, at, far] = w.astype(BF16)
                w = w.T
                high = w.astype(BF16)
                gates_hi[c, far, at] = high
                gates_lo[c, far, at] = (w - high.astype(F32)).astype(BF16)
    masks[...] = jnp.zeros(masks.shape, F32)
    here = jnp.broadcast_to(segs[:, mine], (8, seq))
    spot = lax.broadcasted_iota(jnp.int32, (8, seq), 1)
    for lag in (1, 2, 3):
        same = jnp.where((pltpu.roll(here, lag, 1) == here) & (spot >= lag), 1.0, 0.0)
        masks[lag : lag + 1, 0:seq] = same[0:1]
        if lag == 1:
            masks[0:1, 0:seq] = 1.0 - same[0:1]
    gather.forward(1, 0)
    gather.send(0, 1)
    weights[0].forward()
    gather.forward(2, 0)
    gather_go.forward(1, 0)
    gather.forward(1, 1)
    gather.send(0, 2)
    weights[1].forward()
    for w in weights[3:5]:
        w.start()
    gather_go.forward(1, 1)
    gather_go.forward(2, 0)
    weights[0].finish()
    for pad in pads:
        pad.wait()

    kept = (b_s, p_s, u_s, r_s, i_s, h_s, q_c)
    outs = (b_out, p_out, u_out, r_out, i_out, h_out, q_out)

    def keep(n, part):
        if n in (1, 5):
            at = pl.ds(pl.multiple_of(128 + part * PART, 128), PART)
            return pltpu.make_async_copy(kept[n].at[:, 128:], outs[n].at[:, at], k_sem.at[n])
        return pltpu.make_async_copy(kept[n], outs[n].at[:, lanes(part)], k_sem.at[n])

    def put_shares(k, whole):
        for s in range(LINE):
            own[k, s] = whole[s * block : (s + 1) * block, :].astype(own.dtype)

    def work(k):
        here = lanes(k)

        @pl.when(k > 0)
        def _():
            for n in range(len(kept)):
                keep(n, k - 1).wait()

        gather.middle(k)
        p_s[:, 0:128] = p_s[:, PART:]
        h_s[:, 0:128] = h_s[:, PART:]
        p_s[:, 128:] = dot(br[0:chan, :], normed[k])

        def conv(i):
            ch = rows_of(i, 64)
            window = p_s[ch, :]
            pr = par[ch, :]
            u = pr[:, 4:5] + pr[:, 0:1] * window[:, 128:]
            for lag in (1, 2, 3):
                u = u + pr[:, lag : lag + 1] * (pltpu.roll(window, lag, 1)[:, 128:] * masks[lag : lag + 1, here])
            u_s[ch, :] = u
            high = u.astype(BF16)
            uh[ch, :] = high
            ul[ch, :] = (u - high.astype(F32)).astype(BF16)

        blocks(chan // 64, conv)
        for g in range(chan // 256):
            at = slice(g * 256, (g + 1) * 256)
            pre = dot(gates_hi[g], uh[at, :]) + dot(gates_hi[g], ul[at, :]) + dot(gates_lo[g], uh[at, :])
            r_s[at, :] = pre[:256]
            i_s[at, :] = pre[256:]

        def gated(i):
            ch = rows_of(i, 64)
            pr = par[ch, :]
            start = masks[0:1, here] > 0.5
            r = jax.nn.sigmoid(r_s[ch, :] + pr[:, 5:6])
            gate = jax.nn.sigmoid(i_s[ch, :] + pr[:, 6:7])
            r_s[ch, :] = r
            i_s[ch, :] = gate
            a = jnp.exp(-(r * pr[:, 7:8]))
            m = jnp.where(start, 1.0, jnp.sqrt(1.0 - a * a + FLOOR))
            a_c[ch, :] = jnp.where(start, 0.0, a)
            h_s[ch, 128:] = m * gate * u_s[ch, :]

        blocks(chan // 64, gated)
        first = lax.broadcasted_iota(jnp.int32, (128, PART), 1) == 0

        def recur(i):
            ch = rows_of(i, 128)
            a, h = a_c[ch, :], h_s[ch, 128:]
            h = h + jnp.where(first, a * h_s[ch, 0:128][:, 127:128], 0.0)
            a = jnp.where(first, 0.0, a)
            shift = 1
            while shift < PART:
                h = h + a * pltpu.roll(h, shift, 1)
                if shift * 2 < PART:
                    a = a * pltpu.roll(a, shift, 1)
                shift *= 2
            h_s[ch, 128:] = h

        blocks(chan // 128, recur)

        @pl.when(k == 0)
        def _():
            weights[2].forward()
            weights[1].finish()

        b_s[...] = dot(br[chan : 2 * chan, :], normed[k])

        def mixed(i):
            ch = rows_of(i, 64)
            b = b_s[ch, :]
            t = jnp.tanh(GELU_A * (b + GELU_B * (b * b * b)))
            q_c[ch, :] = (b * (0.5 + 0.5 * t) * h_s[ch, 128:]).astype(BF16)

        blocks(chan // 64, mixed)
        pl.when(k == 0)(weights[2].finish)
        put_shares(k, dot(mt[...], q_c[...]))
        for n in range(len(kept)):
            keep(n, k).start()

    def finish(k, total):
        def add(i):
            at = pl.multiple_of(i * 64, 64)
            y[pl.ds(at, 64), lanes(k)] = x_own[pl.ds(at, 64), lanes(k)].astype(F32) + total(at, 64)

        blocks(block // 64, add)

    def square(k):
        sums2[k, z] = jnp.zeros(sums2.shape[2:], F32)

        def one(i):
            v = y[rows_of(i, 64), lanes(k)]
            sums2[k, z] += eight(v * v)

        blocks(block // 64, one)
        for d in (1, 2, 3):
            share(k, d).start()

    def share(k, d):
        return remote(
            sums2.at[k, z], sums2.at[k, z], n_send.at[k, d - 1], n_recv.at[k, d - 1], at_line(z ^ d, core)
        )

    def norm_two(k):
        for d in (1, 2, 3):
            piece = sums2.at[k, z ^ d]
            remote(piece, piece, n_send.at[k, d - 1], n_recv.at[k, d - 1], at_line(z ^ d, core)).wait_recv()
        s2 = scale_of(sums2.at[k], eps, width)
        scale_two[:, lanes(k)] = jnp.broadcast_to(s2, (8, PART))

        def one(i):
            at = rows_of(i, 64)
            v = y[at, lanes(k)] * scale_two[0:1, lanes(k)] * gains[at, 9:10]
            normed2[k, pl.ds(pl.multiple_of(z * block + i * 64, 64), 64), :] = v.astype(BF16)

        blocks(block // 64, one)

    def turn_down(i):
        at = pl.ds(pl.multiple_of(i * 128, 128), 128)
        dt[:, at] = down[at, :].T

    def turn_up(i):
        at = pl.ds(pl.multiple_of(i * 128, 128), 128)
        gun[:, at] = gu[at, :].T

    def step(t, carry):
        gather.arrive(2, t)
        work(t)
        spread.serve(t, finish)
        pl.when(t >= 3)(lambda: square(t - 3))
        pl.when(t >= 4)(lambda: norm_two(t - 4))
        pl.when((t >= 4) & (t < 7))(lambda: gather_two.send(0, t - 4))
        pl.when((t >= 6) & (t < 8))(lambda: gather_two.forward(1, t - 6))
        pl.when(t == 5)(weights[3].forward)
        return carry

    lax.fori_loop(0, PARTS, step, 0)
    for w in weights[:3]:
        w.sent()
    for w in weights[5:]:
        w.start()
    for n in range(len(kept)):
        keep(n, PARTS - 1).wait()
    flush_n = pltpu.make_async_copy(normed, n1_out, v_sem.at[4])
    flush_n.start()
    gather_go.forward(2, 1)
    gather_go.send(0, 2)
    gather_go.send(0, 3)
    spread.serve(PARTS, finish)
    square(PARTS - 3)
    norm_two(PARTS - 4)
    gather_two.forward(2, 0)
    weights[3].finish()
    blocks(2 * hid // 128, turn_up)
    weights[4].forward()
    spread.serve(PARTS + 1, finish)
    square(PARTS - 2)
    norm_two(PARTS - 3)
    gather_go.forward(1, 2)
    weights[4].finish()
    blocks(hid // 128, turn_down)
    gather.sent()
    for flush in flushes + [flush_n]:
        flush.wait()
    flush_y = pltpu.make_async_copy(y, y_out, v_sem.at[2])

    def keep_dev(k):
        return pltpu.make_async_copy(dev, dev_h.at[:, lanes(k)], v_sem.at[5])

    def keep_z(k):
        return pltpu.make_async_copy(zs, z_h.at[:, lanes(k)], v_sem.at[6])

    dev_all, z_all = gu.at[:, 0:seq], dt.at[0:hid, 0:seq]
    before, end = pl.ds(0, seq - PART), pl.ds(seq - PART, PART)
    loads = [
        pltpu.make_async_copy(dev_h.at[:, before], gu.at[:, before], v_sem.at[7]),
        pltpu.make_async_copy(z_h.at[:, before], dt.at[0:hid, before], v_sem.at[8]),
        pltpu.make_async_copy(dev, gu.at[:, end], v_sem.at[9]),
        pltpu.make_async_copy(zs, dt.at[0:hid, end], v_sem.at[10]),
    ]

    def feed(k):

        @pl.when(k > 0)
        def _():
            keep_dev(k - 1).wait()
            keep_z(k - 1).wait()

        gather_two.middle(k)
        gather_go.middle(k, 2)
        ev[...] = dot(gu[...], normed2[k])

        @pl.when(k == PARTS - 1)
        def _():
            weights[3].sent()
            loads[0].start()

        gather_go.arrive(2, k)
        dz[...] = dot(down[...], go[k])
        for c in range(2):

            def one(i):
                off = pl.multiple_of(i * 64, 64)
                e = ev[pl.ds(c * 2 * hh + off, 64), :]
                v = ev[pl.ds(c * 2 * hh + hh + off, 64), :]
                d = dz[pl.ds(c * hh + off, 64), :]
                act, slope = gelu_parts(e)
                zs[pl.ds(c * hh + off, 64), :] = (act * v).astype(BF16)
                dev[pl.ds(c * 2 * hh + off, 64), :] = (d * v * slope).astype(BF16)
                dev[pl.ds(c * 2 * hh + hh + off, 64), :] = (d * act).astype(BF16)

            blocks(hh // 64, one)
        put_shares(k, dot(gun[...], dev[...]))
        spread_n.serve(k, finish_n)
        normed[k] = dot(dt[...], zs[...]).astype(BF16)
        spread_o.serve(k, finish_o)
        keep_dev(k).start()
        keep_z(k).start()

        @pl.when(k == 0)
        def _():
            spread.serve(PARTS + 2, finish)
            square(PARTS - 1)
            norm_two(PARTS - 2)

        @pl.when(k == 1)
        def _():
            norm_two(PARTS - 1)
            flush_y.start()

    def finish_o(k, total):
        def add(i):
            at = pl.multiple_of(i * 64, 64)
            res[pl.ds(at, 64), lanes(k)] = (y[pl.ds(at, 64), lanes(k)] + total(at, 64)).astype(BF16)

        blocks(block // 64, add)

    def keep_n(k):
        return pltpu.make_async_copy(dn2, dn2_out.at[:, lanes(k)], v_sem.at[3])

    def finish_n(k, total):
        @pl.when(k > 0)
        def _():
            keep_n(k - 1).wait()

        sums3[k, z] = jnp.zeros(sums3.shape[2:], F32)

        def add(i):
            at = pl.multiple_of(i * 64, 64)
            d = total(at, 64)
            dn2[pl.ds(at, 64), :] = d
            sums3[k, z] += eight(d * y[pl.ds(at, 64), lanes(k)] * gains[pl.ds(at, 64), 9:10])

        blocks(block // 64, add)
        keep_n(k).start()
        for d in (1, 2, 3):
            share_c(k, d).start()

    def share_c(k, d):
        return remote(
            sums3.at[k, z], sums3.at[k, z], c_send.at[k, d - 1], c_recv.at[k, d - 1], at_line(z ^ d, core)
        )

    def feed_step(t, carry):
        gather_two.arrive(2, t)
        feed(t)
        pl.when(t == 4)(weights[5].forward)
        pl.when(t == 6)(weights[6].forward)
        return carry

    lax.fori_loop(0, PARTS, feed_step, 0)
    weights[4].sent()
    for load in loads[1:]:
        load.start()
    keep_dev(PARTS - 1).wait()
    keep_z(PARTS - 1).wait()
    loads[0].wait()
    loads[2].wait()

    def columns(start):
        return pl.ds(pl.multiple_of(start, 128), block)

    def place_up(j):
        side = jnp.where(j >= 3, core, 1 - core)
        return side * hid + (j % 3) * block, columns((j % 3) * block)

    def send_up(j):
        at, to = place_up(j)
        return remote(gun.at[:, columns(at)], g_got.at[:, to], d_send.at[j], d_recv.at[j], sibling)

    def keep_up(j):
        at, to = place_up(j)
        return pltpu.make_async_copy(gun.at[:, columns(at)], g_own.at[:, to], d_own.at[j - 3])

    def send_down():
        return remote(down.at[rows_of(1 - core, hh), :], gd_got, d_send.at[3], d_recv.at[3], sibling)

    def keep_down():
        return pltpu.make_async_copy(down.at[rows_of(core, hh), :], gd_own, d_own.at[3])

    def grad_up(j):
        at = place_up(j)[0]
        right = pl.ds(pl.multiple_of(at, 16), block)
        for low in (0, width // 2):
            piece = slice(low, low + width // 2)
            gun[piece, columns(at)] = dot_nt(tokens_of(normed2, piece), dev_all[right, :]).astype(BF16)

        @pl.when(j < 3)
        def _():
            send_up(j).start()

        @pl.when(j >= 3)
        def _():
            keep_up(j).start()

    def grad_down(side):
        at = rows_of(side, hh)
        for low in range(0, width, 2 * block):
            piece = slice(low, low + 2 * block)
            down[at, piece] = dot_nt(z_all[at, :], tokens_of(go, piece)).astype(BF16)

    def drain(i, carry):
        t = PARTS + i
        blocks(2, lambda j: grad_up(2 * i + j))
        spread_n.serve(t, finish_n)
        spread_o.serve(t, finish_o)

        @pl.when(i == 0)
        def _():
            loads[1].wait()
            loads[3].wait()

        @pl.when(i < 2)
        def _():
            grad_down(jnp.where(i == 0, 1 - core, core))

        pl.when(i == 0)(lambda: send_down().start())
        pl.when(i == 1)(lambda: keep_down().start())
        return carry

    lax.fori_loop(0, LINE - 1, drain, 0)
    last = [
        remote(res.at[rows_of(1 - core, half), :], result.at[:, mine], x_send.at[0], x_recv.at[0], sibling),
        pltpu.make_async_copy(res.at[rows_of(core, half), :], result.at[:, mine], x_loc.at[0]),
        keep_n(PARTS - 1),
        flush_y,
    ]
    for copy in last[:2]:
        copy.start()
    for w in weights[5:]:
        w.finish()
        w.sent()
    for one in (gather_go, gather_two, spread, spread_n, spread_o):
        one.sent()
    for k in range(PARTS):
        for d in (1, 2, 3):
            share(k, d).wait_send()
            share_c(k, d).wait_send()
            piece = sums3.at[k, z ^ d]
            remote(piece, piece, c_send.at[k, d - 1], c_recv.at[k, d - 1], at_line(z ^ d, core)).wait_recv()
        total = jnp.sum(jnp.sum(sums3[k], axis=0), axis=0, keepdims=True)
        at = slice(k * PART, (k + 1) * PART)
        s2 = scale_two[:, at]
        coef[:, at] = s2 * s2 * s2 * (total / width)
    for j in range(3):
        keep_up(j + 3).wait()
        send_up(j).wait()
    keep_down().wait()
    send_down().wait()
    for copy in last:
        copy.wait()


def back_kernel(
    width,
    y, dn2_h, g_h, x_own, scale_two, scale_one, coef_two, gains, masks, par, gates_t, m_h, br_h,
    b_h, p_h, u_h, r_h, i_h, h_h, q_h, n1_h, f_own, f_got, fd_own, fd_got,
    input_grad, tiny_v, tiny_g, f_sum, f_land, fd_sum, fd_land, g_sum, g_land, gm_sum, gm_land,
    sums, coef, m_n, br_n, b_s, p_s, u_s, r_s, i_s, h_s, dyf, dbp, dy, dn1, dq, du, dri, a_c, l_c, carry_s, own, held,
    qv, n1, f_a, f_b, fd_a, fd_b, feed_part, mix_part, small, gate_grad, g_s, g_got, gm_got,
    vec, vec_in, vec_all, gd, gd_in, gd_all,
    c_sem, k_sem, l_send, l_recv, g_send, g_recv, s_send, s_recv, r_send, r_recv,
    f_sem, f_send, f_recv, d_send, d_recv, d_own, q_send, q_recv, n_send, n_recv, v_send, v_recv,
):
    row, z, core = place()
    block, seq = y.shape
    PART, PARTS = LATE, seq // LATE

    def lanes(part):
        return pl.ds(pl.multiple_of(part * PART, PART), PART)

    half = block // 2
    chan = b_s.shape[1]
    hc = chan // 2
    sibling = {"col": 2 * z + (1 - core)}
    met = greet(row, z, core, True, True)
    load_g = pltpu.make_async_copy(g_h, g_s, c_sem.at[0])
    load_g.start()
    dn2 = dn1
    load_d = pltpu.make_async_copy(dn2_h, dn2, c_sem.at[5])
    load_d.start()
    load_m = pltpu.make_async_copy(m_h, m_n, c_sem.at[1])
    load_m.start()
    load_b = pltpu.make_async_copy(br_h, br_n, c_sem.at[2])
    load_b.start()
    load_q = pltpu.make_async_copy(q_h, qv, c_sem.at[3])
    load_n = pltpu.make_async_copy(n1_h, n1, c_sem.at[4])
    kept = (b_s, p_s, u_s, r_s, i_s, h_s)
    srcs = (b_h, p_h, u_h, r_h, i_h, h_h)

    def fetch(n, part):
        if kept[n] is p_s or kept[n] is h_s:
            at = pl.ds(pl.multiple_of(part * PART, 128), PART + 128)
        else:
            at = lanes(part)
        return pltpu.make_async_copy(srcs[n].at[:, at], kept[n].at[part % 2], k_sem.at[n, part % 2])

    def fetch_all(part):
        for n in range(len(kept)):
            fetch(n, part).start()

    fetch_all(PARTS - 1)
    load_q.start()
    load_n.start()
    du[:, 0:128] = jnp.zeros((chan, 128), F32)
    carry_s[...] = jnp.zeros(carry_s.shape, F32)
    small[...] = jnp.zeros(small.shape, F32)
    gate_grad[...] = jnp.zeros(gate_grad.shape, F32)

    load_d.wait()
    load_g.wait()
    gather = Gather(dyf, g_send, g_recv, z, core, block, back=True)

    def outer(part):
        here = slice(part * PART, (part + 1) * PART)

        def one(i):
            at = rows_of(i, 64)
            s2 = scale_two[0:1, here]
            d, v = dn2[at, here], y[at, here]
            w = fold(d * v * s2)
            feed_part[at, :] = w if part == PARTS - 1 else feed_part[at, :] + w
            few = PART // g_s.shape[2]
            g = jnp.concatenate([g_s[part * few + j, at, :] for j in range(few)], axis=1)
            v = g.astype(F32) + (s2 * (gains[at, 9:10] * d) - v * coef_two[0:1, here])
            dy[at, here] = v
            dyf[part, pl.ds(pl.multiple_of(z * block + i * 64, 64), 64), :] = v.astype(BF16)

        blocks(block // 64, one)

    outer(PARTS - 1)
    met()
    gather.send(0, 0)
    for part in range(PARTS - 2, -1, -1):
        outer(part)
    gather.forward(1, 0)
    gather.send(0, 1)
    gather.forward(2, 0)
    gather.forward(1, 1)
    gather.send(0, 2)
    spread = Spread(lambda k, s: own.at[k, s], held, s_send, s_recv, z, core)
    load_m.wait()
    load_b.wait()
    final = lax.broadcasted_iota(jnp.int32, (128, PART), 1) == PART - 1

    f_arrays = ((f_own, f_got, f_a, f_b, f_sum, f_land), (fd_own, fd_got, fd_a, fd_b, fd_sum, fd_land))

    def f_loads(d):
        pulls = []
        for n, (ours, theirs, a, b, _, _) in enumerate(f_arrays):
            if n == 0:
                piece = (rows_of(row ^ d, block), slice(None))
            else:
                piece = (slice(None), pl.ds(pl.multiple_of((row ^ d) * block, 128), block))
            pulls.append(pltpu.make_async_copy(ours.at[piece], a.at[d], f_sem.at[n, 0]))
            pulls.append(pltpu.make_async_copy(theirs.at[piece], b, f_sem.at[n, 1]))
        return pulls

    def f_out(d):
        outs = []
        for n, (_, _, a, _, kept_at, land) in enumerate(f_arrays):
            if d == 0:
                outs.append(pltpu.make_async_copy(a.at[0], kept_at, f_send.at[n, 0]))
            else:
                outs.append(
                    remote(a.at[d], land.at[d - 1], f_send.at[n, d], f_recv.at[n, d], {"row": row ^ d})
                )
        return outs

    def f_part(d):
        for pull in f_loads(d):
            pull.wait()
        for _, _, a, b, _, _ in f_arrays:

            def add(i):
                at = rows_of(i, 64)
                a[d, at, :] = (a[d, at, :].astype(F32) + b[at, :].astype(F32)).astype(BF16)

            blocks(b.shape[0] // 64, add)
        for out in f_out(d):
            out.start()
        if d > 0:
            for pull in f_loads(d - 1):
                pull.start()

    def f_step(t):
        for d in range(LINE):
            pl.when(t == LINE - 1 - d)(functools.partial(f_part, d))

    for pull in f_loads(LINE - 1):
        pull.start()

    lru = hc

    def send_m():
        return remote(m_n.at[rows_of(1 - core, lru), :], gm_got, d_send.at[1], d_recv.at[1], sibling)

    def work(t):
        k = PARTS - 1 - t
        here = lanes(k)
        wide = pl.ds(pl.multiple_of(k * PART, 128), PART + 128)
        slot = k % 2
        for n in range(len(kept)):
            fetch(n, k).wait()

        @pl.when(k > 0)
        def _():
            fetch_all(k - 1)

        gather.middle(t)
        dq[...] = dot(m_n[...], dyf[k])

        @pl.when(t == PARTS - 1)
        def _():
            load_q.wait()
            for low in range(0, width, 2 * block):
                piece = slice(low, low + 2 * block)
                m_n[:, piece] = dot_nt(qv[...], tokens_of(dyf, piece)).astype(BF16)
            send_m().start()

        def before(i):
            ch = rows_of(i, 64)
            c = i // (hc // 64)
            low = pl.ds(pl.multiple_of(c * hc + i * 64, 64), 64)
            pr = par[ch, :]
            d = dq[ch, :]
            act, slope = gelu_parts(b_s[slot, ch, :])
            dbp[low, here] = (d * h_s[slot, ch, :][:, 128:] * slope).astype(BF16)
            l_c[ch, :] = d * act
            a_c[ch, :] = jnp.exp(-(r_s[slot, ch, :] * pr[:, 7:8]))

        blocks(chan // 64, before)

        def recur(i):
            ch = rows_of(i, 128)
            start = masks[0:1, here] > 0.5
            a, lam = jnp.where(start, 0.0, a_c[ch, :]), l_c[ch, :]
            lam = lam + jnp.where(final, carry_s[ch, :][:, 0:1], 0.0)
            w = jnp.where(final, 0.0, pltpu.roll(a, PART - 1, 1))
            shift = 1
            while shift < PART:
                lam = lam + w * pltpu.roll(lam, PART - shift, 1)
                if shift * 2 < PART:
                    w = w * pltpu.roll(w, PART - shift, 1)
                shift *= 2
            carry_s[ch, :] = jnp.broadcast_to((a * lam)[:, 0:1], (128, 128))
            l_c[ch, :] = lam

        blocks(chan // 128, recur)
        f_step(t)

        def after(i):
            ch = rows_of(i, 64)
            du[ch, PART:] = du[ch, 0:128]
            pr = par[ch, :]
            start = masks[0:1, here] > 0.5
            lam, a0 = l_c[ch, :], a_c[ch, :]
            earlier = pltpu.roll(h_s[slot, ch, :], 1, 1)[:, 128:]
            r, gate, u = r_s[slot, ch, :], i_s[slot, ch, :], u_s[slot, ch, :]
            m0 = jnp.sqrt(1.0 - a0 * a0 + FLOOR)
            m = jnp.where(start, 1.0, m0)
            lm = lam * m
            lu = lam * u
            du[ch, 0:PART] = lm * gate
            da = jnp.where(start, 0.0, lam * earlier - (lu * gate) * (a0 / m0)) * a0
            dr = da * (-pr[:, 7:8]) * (r * (1.0 - r))
            di = lu * m * (gate * (1.0 - gate))
            g, o = i // 4, (i % 4) * 64
            dri[pl.ds(pl.multiple_of(g * 512 + o, 64), 64), :] = dr.astype(BF16)
            dri[pl.ds(pl.multiple_of(g * 512 + 256 + o, 64), 64), :] = di.astype(BF16)
            small[5, ch, :] += fold(dr)
            small[6, ch, :] += fold(di)
            small[7, ch, :] += fold(da * r)

        blocks(chan // 64, after)
        for g in range(chan // 256):
            at = slice(g * 256, (g + 1) * 256)
            dd = dri[g * 512 : (g + 1) * 512, :]
            du[at, 0:PART] += dot(gates_t[g], dd)
            gate_grad[g] += dot_nt(u_s[slot, at, :].astype(BF16), dd)

        def conv(i):
            ch = rows_of(i, 64)
            c = i // (hc // 64)
            low = pl.ds(pl.multiple_of((c + 1) * hc + i * 64, 64), 64)
            pr = par[ch, :]
            follow = du[ch, :]
            window = p_s[slot, ch, :]
            d = follow[:, :PART]
            dp = pr[:, 0:1] * d
            small[4, ch, :] += fold(d)
            small[0, ch, :] += fold(d * window[:, 128:])
            for lag in (1, 2, 3):
                kd = follow * masks[lag : lag + 1, wide]
                dp = dp + pr[:, lag : lag + 1] * pltpu.roll(kd, PART + 128 - lag, 1)[:, :PART]
                small[lag, ch, :] += fold(kd[:, :PART] * pltpu.roll(window, lag, 1)[:, 128:])
            dbp[low, here] = dp.astype(BF16)

        blocks(chan // 64, conv)
        whole = dot(br_n[...], dbp[:, here])
        for s in range(LINE):
            own[t, s] = whole[s * block : (s + 1) * block, :].astype(own.dtype)

    def finish(t, total):
        k = PARTS - 1 - t

        sums[k, z] = jnp.zeros(sums.shape[2:], F32)

        @pl.when(t == 0)
        def _():
            mix_part[...] = jnp.zeros(mix_part.shape, F32)

        def add(i):
            at = pl.ds(pl.multiple_of(i * 64, 64), 64)
            d = total(pl.multiple_of(i * 64, 64), 64)
            dn1[at, lanes(k)] = d
            w = d * x_own[at, lanes(k)].astype(F32)
            sums[k, z] += eight(w * gains[at, 8:9])
            w = w * scale_one[0:1, lanes(k)]
            mix_part[at, :] += fold(w)

        blocks(block // 64, add)
        for d in (1, 2, 3):
            share(k, d).start()

    def share(k, d):
        return remote(sums.at[k, z], sums.at[k, z], l_send.at[k, d - 1], l_recv.at[k, d - 1], at_line(z ^ d, core))

    def step(t, carry):
        gather.arrive(2, t)
        work(t)
        spread.serve(t, finish)
        return carry

    lax.fori_loop(0, PARTS, step, 0)
    load_n.wait()


    def cols_of(side):
        return pl.ds(pl.multiple_of(side * 2 * lru, 128), 2 * lru)

    def send_br():
        return remote(br_n.at[:, cols_of(1 - core)], g_got, d_send.at[0], d_recv.at[0], sibling)

    def grad_br(side):
        for low in range(0, width, 2 * block):
            piece = slice(low, low + 2 * block)
            br_n[piece, cols_of(side)] = dot_nt(tokens_of(n1, piece), dbp[rows_of(side, 2 * lru), :]).astype(BF16)

    def out_br(d):
        piece = br_n.at[rows_of(row ^ d, block), cols_of(core)]
        if d == 0:
            return pltpu.make_async_copy(piece, g_sum, d_own.at[0])
        return remote(piece, g_land.at[d - 1], q_send.at[0, d - 1], q_recv.at[0, d - 1], {"row": row ^ d})

    def out_m(d):
        piece = m_n.at[rows_of(core, lru), pl.ds(pl.multiple_of((row ^ d) * block, 128), block)]
        if d == 0:
            return pltpu.make_async_copy(piece, gm_sum, d_own.at[1])
        return remote(piece, gm_land.at[d - 1], q_send.at[1, d - 1], q_recv.at[1, d - 1], {"row": row ^ d})

    def drain(i, carry):
        t = PARTS + i

        @pl.when(i == 0)
        def _():
            grad_br(1 - core)
            send_br().start()
            send_m().wait_recv()

            def add(j):
                at = rows_of(j, 64)
                to = pl.ds(pl.multiple_of(core * lru + j * 64, 64), 64)
                m_n[to, :] = (m_n[to, :].astype(F32) + gm_got[at, :].astype(F32)).astype(BF16)

            blocks(lru // 64, add)
            for d in (3, 2, 1, 0):
                out_m(d).start()
            grad_br(core)

        @pl.when(i == 1)
        def _():
            send_br().wait_recv()

            def add(j):
                at = rows_of(j, 64)
                br_n[at, cols_of(core)] = (br_n[at, cols_of(core)].astype(F32) + g_got[at, :].astype(F32)).astype(BF16)

            blocks(width // 64, add)
            for d in (3, 2, 1, 0):
                out_br(d).start()
        spread.serve(t, finish)
        pl.when(i == 0)(tiny_open)
        pl.when(i == 1)(tiny_more)
        return carry

    mine = pl.ds(pl.multiple_of(core * seq, seq), seq)
    lane = lax.broadcasted_iota(jnp.int32, (64, 128), 1)
    swap_gd = remote(gd.at[1 - core], gd_in, v_send.at[0], v_recv.at[0], sibling)
    rows_gd = [
        remote(gd_all.at[0], gd_all.at[d], n_send.at[0, d - 1], n_recv.at[0, d - 1], {"row": row ^ d}) for d in (1, 2, 3)
    ]

    def tiny_open():
        for side in (0, 1):
            for e in range(4):
                at = slice(e * 64, (e + 1) * 64)
                gd[side, at, 0:64] = gate_grad[side, at, e * 64 : (e + 1) * 64]
                gd[side, at, 64:128] = gate_grad[side, at, 256 + e * 64 : 256 + (e + 1) * 64]
        swap_gd.start()

    def columns(parts, at):
        total = jnp.zeros((64, 128), F32)
        for n, part in enumerate(parts):
            total = total + jnp.where(lane == n, jnp.sum(part(at), axis=1, keepdims=True), 0.0)
        return total

    def tiny_more():
        swap_gd.wait()
        gd_all[0] = gd[core] + gd_in[...]
        for copy in rows_gd:
            copy.start()
        vec[...] = jnp.zeros(vec.shape, F32)
        for j in range(chan // 64):
            at = slice(j * 64, (j + 1) * 64)
            v = columns([lambda at, n=n: small[n, at, :] for n in range(8)], at)
            vec[0, :, at] = v.T[0:8, :]

    lax.fori_loop(0, LINE - 1, drain, 0)
    for j in range(block // 64):
        at = slice(j * 64, (j + 1) * 64)
        v = columns([lambda at: mix_part[at, :], lambda at: feed_part[at, :]], at)
        vec[1, :, at] = v.T[0:8, :]
    swap_vec = remote(vec, vec_in, v_send.at[1], v_recv.at[1], sibling)
    swap_vec.start()
    for k in range(PARTS):
        for d in (1, 2, 3):
            share(k, d).wait_send()
            piece = sums.at[k, z ^ d]
            remote(piece, piece, l_send.at[k, d - 1], l_recv.at[k, d - 1], at_line(z ^ d, core)).wait_recv()
        total = jnp.sum(jnp.sum(sums[k], axis=0), axis=0, keepdims=True)
        at = slice(k * PART, (k + 1) * PART)
        s1 = scale_one[:, at]
        coef[:, at] = s1 * s1 * s1 * (total / width)

    def last(i):
        at = rows_of(i, 16)
        v = dy[at, :] + (
            scale_one[0:1, :] * (gains[at, 8:9] * dn1[at, :]) - x_own[at, :].astype(F32) * coef[0:1, :]
        )
        dy[at, :] = v

    blocks(block // 16, last)
    back = remote(dy.at[rows_of(1 - core, half), :], input_grad.at[:, mine], r_send, r_recv, sibling)
    back.start()
    keep_in = pltpu.make_async_copy(dy.at[rows_of(core, half), :], input_grad.at[:, mine], d_own.at[3])
    keep_in.start()
    swap_vec.wait()
    vec_all[0] = vec[...] + vec_in[...]
    rows_vec = [
        remote(vec_all.at[0], vec_all.at[d], n_send.at[1, d - 1], n_recv.at[1, d - 1], {"row": row ^ d}) for d in (1, 2, 3)
    ]
    for copy in rows_vec:
        copy.start()
    spread.sent()
    gather.sent()
    for copy in rows_gd + rows_vec:
        copy.wait()
    for every, out in ((gd_all, tiny_g), (vec_all, tiny_v)):
        first, second = every[row % 2], every[1 - row % 2]
        third, fourth = every[2 + row % 2], every[3 - row % 2]
        out[...] = (first + second) + (third + fourth)
    for d in range(LINE):
        for out in f_out(d):
            out.wait()
    send_br().wait_send()
    send_m().wait_send()
    for d in (0, 1, 2, 3):
        out_br(d).wait()
        out_m(d).wait()
    for copy in (keep_in, back):
        copy.wait()


def last_kernel(
    f_sum, f_land, fd_sum, fd_land, g_sum, g_land, gm_sum, gm_land, result_in, grad_in, tiny_v, tiny_g, lambdas,
    s_b, s_r, s_m, s_g, s_u, s_d, result, input_grad, taps, offs, bias_r, bias_a, decay, mix, feed, retain, admit,
):
    lru, ff, half = s_b.shape[1], s_g.shape[0], mix.shape[1]

    def four(first, others):
        return first[...].astype(F32) + others[0].astype(F32) + (others[1].astype(F32) + others[2].astype(F32))

    v = four(f_sum, f_land)
    s_g[...] = v.T[:ff, :]
    s_u[...] = v.T[ff:, :]
    v = four(g_sum, g_land)
    s_b[...] = v[:, :lru]
    s_r[...] = v[:, lru:]
    s_d[...] = four(fd_sum, fd_land)
    result[...] = result_in[...]
    input_grad[...] = grad_in[...]

    @pl.when(pl.program_id(0) == 0)
    def _():
        core = place()[2]
        s_m[...] = four(gm_sum, gm_land)
        small = tiny_v[0, :, pl.ds(pl.multiple_of(core * lru, 128), lru)]
        taps[...] = small[0:4]
        offs[...] = small[4:5]
        bias_r[...] = small[5:6]
        bias_a[...] = small[6:7]
        decay[...] = small[7:8] * (8.0 * jax.nn.sigmoid(-lambdas[...]))
        gains = jnp.where(core == 0, tiny_v[1, :, 0:half], tiny_v[1, :, half : 2 * half])
        mix[...] = gains[0:1]
        feed[...] = gains[1:2]
        for e in range(retain.shape[0]):
            at = slice(e * 64, (e + 1) * 64)
            retain[e] = tiny_g[at, 0:64]
            admit[e] = tiny_g[at, 64:128]


ANY = pl.BlockSpec(memory_space=pl.ANY)
VM = pl.BlockSpec(memory_space=pltpu.VMEM)
DMA = pltpu.SemaphoreType.DMA
ROOM = 62 * 1024 * 1024


def shape(dims, kind):
    return jax.ShapeDtypeStruct(dims, kind)


def call(kernel, ins, outs, scratch, ident, name, flops):
    return pl.pallas_call(
        kernel,
        out_shape=[o[0] for o in outs],
        in_specs=ins,
        out_specs=[o[1] for o in outs],
        scratch_shapes=scratch,
        name=name,
        compiler_params=pltpu.CompilerParams(
            collective_id=ident, has_side_effects=True, vmem_limit_bytes=ROOM
        ),
        cost_estimate=pl.CostEstimate(flops=flops, bytes_accessed=40000000, transcendentals=0),
    )


def fast_body(
    inputs, segments, mix_gain, branch_weight, recur_weight, kernel, offsets, retain_weight, retain_bias,
    admit_weight, admit_bias, lambdas, merge_weight, feed_gain, gate_weight, up_weight, down_weight, cotangent,
):
    half, tokens = inputs.shape
    block, seq, width = 2 * half, tokens // 2, D
    lru, heads = branch_weight.shape[1], retain_weight.shape[0]
    chan = 2 * lru
    ff = gate_weight.shape[1]
    hid = 2 * ff
    rows = branch_weight.shape[0]
    cols = merge_weight.shape[1]
    gu_s = jnp.concatenate([gate_weight, up_weight], axis=1).T

    f_tok = lambda n, kind=F32: shape((n, seq), kind)
    padded = (shape((chan, 128 + seq), F32), ANY)
    state = [(f_tok(chan), ANY), padded, *[(f_tok(chan), ANY)] * 3, padded]
    line = [DMA((3,)), DMA((3,))]
    steps = [DMA((2, 3, PARTS)), DMA((2, 3, PARTS))]
    sums = [DMA((2, PARTS, LINE)), DMA((2, PARTS, LINE))]
    held = pltpu.VMEM((PARTS, LINE + 1, block, PART), BF16)
    own_low = pltpu.VMEM((PARTS, LINE, block, PART), BF16)
    tok = lambda n, kind=F32, lead=0: pltpu.VMEM((n, lead + seq), kind)
    one = lambda n, kind=F32, lead=0: pltpu.VMEM((n, lead + PART), kind)
    grad_gu, grad_d = (shape((width, 2 * ff), BF16), ANY), (shape((ff, width), BF16), ANY)
    low = lambda n, m: (shape((n, m), BF16), ANY)
    parted = lambda n: (shape((PARTS, n, PART), BF16), ANY)
    by_part = lambda n: pltpu.VMEM((PARTS, n, PART), BF16)

    (masks, par, gains, gates, coef, scale_one, scale_two, y, n1, q, x_own, g, b, p, u, r, i, h, result, dn2, _, _, f_own, f_got, fd_own, fd_got,
     br_n, m_n) = call(
        functools.partial(forward_kernel, width, EPS),
        [ANY] * 2 + [VM] * 13 + [ANY] * 2,
        [(shape((8, seq + 128), F32), VM), (shape((chan, 16), F32), VM), (shape((block, 16), F32), VM), (shape((2, lru, 2 * lru), BF16), VM),
         (f_tok(8), VM), (f_tok(8), VM), (f_tok(8), VM), (f_tok(block), ANY), parted(width), low(chan, seq), low(block, seq), parted(block)]
        + state + [low(half, tokens), (f_tok(block), ANY), low(2 * hid, seq), low(hid, seq), grad_gu, grad_gu, grad_d, grad_d,
                   low(width, 2 * chan), low(chan, width)],
        [pltpu.VMEM((LINE, 8, seq), F32), pltpu.VMEM((PARTS, LINE, 8, PART), F32), pltpu.VMEM((PARTS, LINE, 8, PART), F32),
         pltpu.VMEM((16, lru), F32), pltpu.VMEM((2 * lru, rows), BF16), pltpu.VMEM((rows, 2 * lru), BF16), pltpu.VMEM((cols, lru), BF16),
         pltpu.VMEM((2, 16, lru), F32), pltpu.VMEM((2, 2) + retain_weight.shape, F32), pltpu.VMEM((2, 2 * lru, lru), BF16),
         pltpu.VMEM((2, 2 * lru, lru), BF16), by_part(width), by_part(width),
         by_part(width), tok(block, BF16), tok(block), one(block), one(chan, BF16),
         one(chan, F32, 128), one(chan, F32, 128), one(max(5 * chan, 3 * hid)), one(chan, BF16), one(chan, BF16),
         own_low, held, held, held, pltpu.VMEM((2 * hid, width), BF16), pltpu.VMEM((width, 2 * hid), BF16),
         pltpu.VMEM((hid, width), BF16), pltpu.VMEM((width, hid), BF16), one(hid, BF16), one(2 * hid, BF16),
         DMA((5,)), DMA((5,)), DMA((5,)), DMA((PARTS,)), DMA((PARTS,)), DMA((PARTS,))] + line + [DMA((PARTS, 3)), DMA((PARTS, 3))] * 2 + steps * 3 + sums * 3
        + [DMA((7, 7)), DMA((7, 7)), DMA((7,)), DMA((7,)), DMA((11,)), DMA((4,)), DMA((4,)), DMA((4,))],
        0, "forward", 50 * 10**9,
    )(inputs, cotangent, segments[None, :], kernel, offsets[None, :], retain_bias[None, :], admit_bias[None, :],
      lambdas[None, :], mix_gain[None, :], feed_gain[None, :], retain_weight, admit_weight, branch_weight, recur_weight,
      merge_weight, gu_s, down_weight)

    late = seq // LATE
    pair = lambda lead=0: pltpu.VMEM((2, chan, lead + LATE), F32)
    one = lambda n, kind=F32, lead=0: pltpu.VMEM((n, lead + LATE), kind)
    steps = [DMA((2, 3, late)), DMA((2, 3, late))]
    sums = [DMA((2, late, LINE)), DMA((2, late, LINE))]
    held = pltpu.VMEM((late, LINE + 1, block, LATE), BF16)
    own_low = pltpu.VMEM((late, LINE, block, LATE), BF16)
    land = lambda n, m: ((shape((n, m), BF16), ANY), (shape((3, n, m), BF16), ANY))
    input_grad, tiny_v, tiny_g, *sums_of = call(
        functools.partial(back_kernel, width),
        [VM] + [ANY] * 2 + [VM] * 8 + [ANY] * 14,
        [(shape((half, tokens), F32), ANY), (shape((2, 8, chan), F32), VM),
         (shape((lru, 128), F32), VM), *land(cols, 2 * ff), *land(ff, cols), *land(cols, 2 * lru), *land(lru, cols)],
        [pltpu.VMEM((late, LINE, 8, LATE), F32), pltpu.VMEM((8, seq), F32),
         pltpu.VMEM((chan, width), BF16), pltpu.VMEM((width, 2 * chan), BF16),
         pair(), pair(128), pair(), pair(), pair(), pair(128), pltpu.VMEM((late, width, LATE), BF16), tok(2 * chan, BF16),
         tok(block), tok(block), one(chan), one(chan, F32, 128), one(2 * chan, BF16),
         one(chan), one(chan), pltpu.VMEM((chan, 128), F32), own_low, held,
         tok(chan, BF16), by_part(width), pltpu.VMEM((4, cols, 2 * ff), BF16), pltpu.VMEM((cols, 2 * ff), BF16),
         pltpu.VMEM((4, ff, cols), BF16), pltpu.VMEM((ff, cols), BF16),
         pltpu.VMEM((block, 128), F32), pltpu.VMEM((block, 128), F32), pltpu.VMEM((8, chan, 128), F32),
         pltpu.VMEM((2, lru, 2 * lru), F32), by_part(block), pltpu.VMEM((width, 2 * lru), BF16),
         pltpu.VMEM((lru, width), BF16), pltpu.VMEM((2, 8, chan), F32), pltpu.VMEM((2, 8, chan), F32),
         pltpu.VMEM((4, 2, 8, chan), F32), pltpu.VMEM((2, lru, 128), F32), pltpu.VMEM((lru, 128), F32),
         pltpu.VMEM((4, lru, 128), F32), DMA((7,)), DMA((6, 2))] + [DMA((late, 3)), DMA((late, 3))] + steps + sums
        + [DMA, DMA, DMA((2, 2)), DMA((2, LINE)), DMA((2, LINE)), DMA((2,)), DMA((2,)), DMA((4,))]
        + [DMA((2, 3)), DMA((2, 3)), DMA((2, 3)), DMA((2, 3)), DMA((2,)), DMA((2,))],
        2, "mix_backward", 10 * 10**9,
    )(y, dn2, g, x_own, scale_two, scale_one, coef, gains, masks, par, gates, m_n, br_n, b, p, u, r, i, h,
      q, n1, f_own, f_got, fd_own, fd_got)

    line_of = shape((1, lru), F32)
    cuts = 3
    rows_in = lambda *dims: pl.BlockSpec((dims[0] // cuts,) + dims[1:], lambda n: (n,) + (0,) * (len(dims) - 1))
    three = lambda *dims: pl.BlockSpec((3, dims[0] // cuts, dims[1]), lambda n: (0, n, 0))
    still = lambda *dims: pl.BlockSpec(dims, lambda n: (0,) * len(dims))
    sizes = ((cols, 2 * ff), (ff, cols), (cols, 2 * lru), (lru, cols))
    big = ((cols, lru), (cols, lru), (lru, cols), (ff, cols), (ff, cols), (ff, cols))
    across = pl.BlockSpec((ff, cols // cuts), lambda n: (0, n))
    flat = ((4, lru),) + ((1, lru),) * 4 + ((1, half),) * 2 + ((heads, 64, 64),) * 2
    s_b, s_r, s_m, s_g, s_u, s_d, result, input_grad, taps, offs, bias_r, bias_a, decay, mix, feed, retain, admit = pl.pallas_call(
        last_kernel,
        grid=(cuts,),
        out_shape=[shape(d, F32) for d in big] + [shape((half, tokens), BF16), shape((half, tokens), F32)]
        + [shape(d, F32) for d in flat],
        in_specs=[spec(*d) for d in sizes[:3] for spec in (rows_in, three)] + [still(lru, cols), still(3, lru, cols)]
        + [rows_in(half, tokens)] * 2
        + [still(2, 8, chan), still(lru, 128), still(1, lru)],
        out_specs=[rows_in(cols, lru)] * 2 + [still(lru, cols)] + [across] * 2 + [rows_in(ff, cols)] + [rows_in(half, tokens)] * 2 + [still(*d) for d in flat],
        name="last_sums",
        compiler_params=pltpu.CompilerParams(vmem_limit_bytes=ROOM),
    )(*sums_of, result, input_grad, tiny_v, tiny_g, lambdas[None, :])
    return (
        result,
        input_grad,
        mix[0],
        s_b,
        s_r,
        taps,
        offs[0],
        retain,
        bias_r[0],
        admit,
        bias_a[0],
        decay[0],
        s_m,
        feed[0],
        s_g.T,
        s_u.T,
        s_d,
    )


def suits(mesh, args):
    return (
        dict(mesh.shape) == {"row": 4, "col": 8}
        and args[0].shape == (D, 8 * SEQ)
        and args[3].shape == (D, 2048)
        and args[14].shape == (D, 4608)
        and args[7].shape == (32, 64, 64)
    )


def solution(mesh):
    in_specs = (
        P("col", "row"),
        P("row"),
        P("col"),
        P("row", "col"),
        P("row", "col"),
        P(None, "col"),
        P("col"),
        P("col", None, None),
        P("col"),
        P("col", None, None),
        P("col"),
        P("col"),
        P("col", "row"),
        P("col"),
        P("row", "col"),
        P("row", "col"),
        P("col", "row"),
        P("col", "row"),
    )
    out_specs = (
        P("col", "row"),
        P("col", "row"),
        P("col"),
        P("row", "col"),
        P("row", "col"),
        P(None, "col"),
        P("col"),
        P("col", None, None),
        P("col"),
        P("col", None, None),
        P("col"),
        P("col"),
        P("col", "row"),
        P("col"),
        P("row", "col"),
        P("row", "col"),
        P("col", "row"),
    )
    def run(*args):
        chosen = fast_body if suits(mesh, args) else body
        return jax.shard_map(
            chosen, mesh=mesh, in_specs=in_specs, out_specs=out_specs, check_vma=False
        )(*args)

    return run
```
